32 devices in a mesh: section: 2 (over y), dp: 4 (over z), tensor: 4 (over x, core).
Axes of the slice: x: 2, y: 2, z: 4, core: 2. Of those that a mesh axis runs over, the one named last changes fastest.
Arguments:
- text_input: bfloat16 [2, 8, 512, 768], P('section', 'dp', 'tensor'), may hold values from -6 to 6
- layout_input: bfloat16 [2, 8, 512, 192], P('section', 'dp', 'tensor'), may hold values from -6 to 6
- text_cotangent: bfloat16 [2, 8, 512, 768], P('section', 'dp', 'tensor'), may hold values from -6 to 6
- layout_cotangent: bfloat16 [2, 8, 512, 192], P('section', 'dp', 'tensor'), may hold values from -6 to 6
- page_counts: int32 [2, 8], P(None, 'dp'), may hold values from 64 to 512, as said below
- pad_mask: int32 [2, 8, 512], P(None, 'dp'), may hold values 0 or 1
- lang_ids: int32 [2, 8], P(None, 'dp'), may hold values from 0 to 7
- lang_table: float32 [8, 768], replicated, may hold values from -3 to 3
- text_project: bfloat16 [2, 768, 3, 768], P('section', None, None, 'tensor'), may hold values from -0.21875 to 0.21875
- text_outward: bfloat16 [2, 768, 768], P('section', 'tensor'), may hold values from -0.875 to 0.875
- text_upward: bfloat16 [2, 768, 3072], P('section', None, 'tensor'), may hold values from -0.21875 to 0.21875
- text_downward: bfloat16 [2, 3072, 768], P('section', 'tensor'), may hold values from -0.109375 to 0.109375
- text_gains: float32 [2, 2, 768], P('section'), may hold values from 0.25 to 1.75
- text_biases: float32 [2, 2, 768], P('section'), may hold values from -1.8 to 1.8
- layout_project: bfloat16 [2, 192, 3, 192], P('section', None, None, 'tensor'), may hold values from -0.4375 to 0.4375
- layout_outward: bfloat16 [2, 192, 192], P('section', 'tensor'), may hold values from -1.75 to 1.75
- layout_upward: bfloat16 [2, 192, 768], P('section', None, 'tensor'), may hold values from -0.4375 to 0.4375
- layout_downward: bfloat16 [2, 768, 192], P('section', 'tensor'), may hold values from -0.21875 to 0.21875
- layout_gains: float32 [2, 2, 192], P('section'), may hold values from 0.25 to 1.75
- layout_biases: float32 [2, 2, 192], P('section'), may hold values from -1.8 to 1.8
Outputs:
- text_output: bfloat16 [2, 8, 512, 768], P('section', 'dp', 'tensor')
- layout_output: bfloat16 [2, 8, 512, 192], P('section', 'dp', 'tensor')
- text_input_gradient: bfloat16 [2, 8, 512, 768], P('section', 'dp', 'tensor')
- layout_input_gradient: bfloat16 [2, 8, 512, 192], P('section', 'dp', 'tensor')
- lang_table_gradient: float32 [8, 768], replicated
- text_project_gradient: float32 [2, 768, 3, 768], P('section', None, None, 'tensor')
- text_outward_gradient: float32 [2, 768, 768], P('section', 'tensor')
- text_upward_gradient: float32 [2, 768, 3072], P('section', None, 'tensor')
- text_downward_gradient: float32 [2, 3072, 768], P('section', 'tensor')
- text_gains_gradient: float32 [2, 2, 768], P('section')
- text_biases_gradient: float32 [2, 2, 768], P('section')
- layout_project_gradient: float32 [2, 192, 3, 192], P('section', None, None, 'tensor')
- layout_outward_gradient: float32 [2, 192, 192], P('section', 'tensor')
- layout_upward_gradient: float32 [2, 192, 768], P('section', None, 'tensor')
- layout_downward_gradient: float32 [2, 768, 192], P('section', 'tensor')
- layout_gains_gradient: float32 [2, 2, 192], P('section')
- layout_biases_gradient: float32 [2, 2, 192], P('section')
The draws below stay inside these ranges and needn't reach their ends.
Inputs may be any that keep to these rules, and one draw needn't show every extreme that they name: `page_counts`: in every draw one page holds all 512 tokens; position 0 of a page always counts as a key.
All inputs are finite; a program needn't handle non-finite values. No bound on the sum of `pad_mask` on one device may be relied on, other than what follows from the above.
Results may differ from the reference program's by a relative error of at most 0.035.
Values may be sent and summed in bfloat16 or wider, within the bound.
A program may use at most 192 MiB of HBM per device.

```python
import math
import jax
import jax.numpy as jnp
from jax import lax

D = 768
HEADS = 12
FF = 3072
DL = 192
FF_LAYOUT = 768
HEAD_TEXT = 64
HEAD_LAYOUT = 16
LENGTH = 512
LANGS = 8
MB = 2
PAGES = 8


def draw_page_counts(key, part):
    key = jax.random.fold_in(key, 11)
    count_key, pick_key = jax.random.split(key)
    counts = jax.random.randint(count_key, (MB, PAGES), LENGTH // 8, LENGTH + 1, dtype=jnp.int32)
    chosen = jax.random.randint(pick_key, (), 0, MB * PAGES, dtype=jnp.int32)
    flat_index = jnp.arange(MB * PAGES, dtype=jnp.int32).reshape(MB, PAGES)
    return jnp.where(flat_index == chosen, LENGTH, counts).astype(jnp.int32)


def set_ends(values, stream_key, least, high):
    place = [jax.random.randint(jax.random.fold_in(stream_key, axis), (), 0, length) for axis, length in enumerate(values.shape)]
    widest = values.shape.index(max(values.shape))
    next_to = place[:widest] + [(place[widest] + 1) % values.shape[widest]] + place[widest + 1:]
    return values.at[tuple(place)].set(least).at[tuple(next_to)].set(high)


def levels(own_key, dims, pieces, smallest, largest):
    level = 1.0
    for axis_at, shards_of in pieces:
        heights = jax.random.uniform(jax.random.fold_in(jax.random.fold_in(own_key, 6), axis_at), (shards_of,), jnp.float32, smallest / len(pieces), largest / len(pieces))
        level = level * jnp.repeat(jnp.exp(heights), dims[axis_at] // shards_of).reshape((-1,) + (1,) * (len(dims) - 1 - axis_at))
    return level


def centred(stream_key, dims, scale, most, shards=(), held_as=jnp.bfloat16):
    level = levels(stream_key, dims, shards, -0.22, 0.18) if shards else 1.0
    values = jax.random.normal(stream_key, dims, jnp.float32) * scale * level
    return jnp.minimum(jnp.maximum(values, -most), most).astype(held_as)


def setup_inputs(seed: int = 0) -> dict:
    keys = jax.random.split(jax.random.key(seed), 21)
    text_input = centred(keys[0], (MB, PAGES, LENGTH, D), 1.0, 6.0, ((0, 2), (1, 4), (2, 4)))
    layout_input = centred(keys[1], (MB, PAGES, LENGTH, DL), 1.0, 6.0, ((0, 2), (1, 4), (2, 4)))
    text_cotangent = centred(keys[2], (MB, PAGES, LENGTH, D), 1.0, 6.0, ((0, 2), (1, 4), (2, 4)))
    layout_cotangent = centred(keys[3], (MB, PAGES, LENGTH, DL), 1.0, 6.0, ((0, 2), (1, 4), (2, 4)))
    page_counts = draw_page_counts(jax.random.fold_in(keys[20], 71), 0)
    pad_mask = set_ends((jax.random.randint(keys[5], (MB, PAGES, LENGTH), 0, 8) < 7).astype(jnp.int32), jax.random.fold_in(keys[5], 1), 0, 1)
    lang_ids = set_ends(jax.random.randint(keys[6], (MB, PAGES), 0, LANGS), jax.random.fold_in(keys[6], 1), 0, LANGS - 1).astype(jnp.int32)
    lang_table = centred(keys[7], (LANGS, D), 0.5, 3.0, (), jnp.float32)
    text_project = centred(keys[8], (2, D, 3, D), D ** -0.5, 0.21875, ((0, 2), (3, 4)))
    text_outward = centred(keys[9], (2, D, D), (D // 16) ** -0.5, 0.875, ((0, 2), (1, 4)))
    text_upward = centred(keys[10], (2, D, FF), D ** -0.5, 0.21875, ((0, 2), (2, 4)))
    text_downward = centred(keys[11], (2, FF, D), FF ** -0.5, 0.109375, ((0, 2), (1, 4)))
    text_gains = jnp.clip(1.0 + 0.15 * jax.random.normal(keys[12], (2, 2, D), jnp.float32), 0.25, 1.75)
    text_biases = centred(keys[13], (2, 2, D), 0.3, 1.8, ((0, 2),), jnp.float32)
    layout_project = centred(keys[14], (2, DL, 3, DL), DL ** -0.5, 0.4375, ((0, 2), (3, 4)))
    layout_outward = centred(keys[15], (2, DL, DL), (DL // 16) ** -0.5, 1.75, ((0, 2), (1, 4)))
    layout_upward = centred(keys[16], (2, DL, FF_LAYOUT), DL ** -0.5, 0.4375, ((0, 2), (2, 4)))
    layout_downward = centred(keys[17], (2, FF_LAYOUT, DL), FF_LAYOUT ** -0.5, 0.21875, ((0, 2), (1, 4)))
    layout_gains = jnp.clip(1.0 + 0.15 * jax.random.normal(keys[18], (2, 2, DL), jnp.float32), 0.25, 1.75)
    layout_biases = centred(keys[19], (2, 2, DL), 0.3, 1.8, ((0, 2),), jnp.float32)
    return {"text_input": text_input, "layout_input": layout_input, "text_cotangent": text_cotangent, "layout_cotangent": layout_cotangent, "page_counts": page_counts, "pad_mask": pad_mask, "lang_ids": lang_ids, "lang_table": lang_table, "text_project": text_project, "text_outward": text_outward, "text_upward": text_upward, "text_downward": text_downward, "text_gains": text_gains, "text_biases": text_biases, "layout_project": layout_project, "layout_outward": layout_outward, "layout_upward": layout_upward, "layout_downward": layout_downward, "layout_gains": layout_gains, "layout_biases": layout_biases}


@jax.custom_vjp
def low(v):
    return lax.optimization_barrier(v.astype(jnp.bfloat16)).astype(jnp.float32)

@jax.custom_vjp
def low_back(v):
    return v

def low_keep(v):
    return (low(v), None)

def low_pass(kept, grad):
    return (grad,)

def back_keep(v):
    return (v, None)

def back_low(kept, grad):
    return (low(grad),)
low.defvjp(low_keep, low_pass)
low_back.defvjp(back_keep, back_low)
EPSILON = 1e-05
NEGATIVE = -1e+30
HIGH = lax.Precision.HIGHEST

def layer_norm(summed, gain, offset):
    center = summed - lax.optimization_barrier(jnp.mean(summed, axis=-1, keepdims=True))
    inverse = lax.rsqrt(lax.optimization_barrier(jnp.mean(center * center, axis=-1, keepdims=True)) + EPSILON)
    return center * inverse * gain + offset

def project_heads(rows, weight, head_size):
    projected = jnp.einsum('gld,dcn->glcn', rows, weight, precision=HIGH)
    projected = low(low_back(projected))
    return projected.reshape(rows.shape[0], rows.shape[1], 3, HEADS, head_size)

def attend_and_feed(rows, head_set, probs, outward, upward, downward, gains, biases):
    context = jnp.einsum('ghqk,gkhd->gqhd', probs, head_set[:, :, 2], precision=HIGH)
    context = low(low_back(context)).reshape(rows.shape[0], rows.shape[1], -1)
    attended = low_back(jnp.einsum('gln,nd->gld', context, outward, precision=HIGH))
    hidden = layer_norm(rows + attended, gains[0], biases[0])
    pre_act = low_back(jnp.einsum('gld,dn->gln', low(hidden), upward, precision=HIGH))
    active = low(jax.nn.gelu(pre_act, approximate=False))
    fed = low_back(jnp.einsum('gln,nd->gld', active, downward, precision=HIGH))
    return layer_norm(hidden + fed, gains[1], biases[1])

def pair_scores(query, key, head_size):
    return jnp.einsum('gqhd,gkhd->ghqk', query, key, precision=HIGH) * (1.0 / math.sqrt(head_size))

def coupled_layer(text_rows, layout_rows, params, key_valid, held_heads):
    project_text, outward_text, upward_text, downward_text, gains_text, biases_text, project_layout, outward_layout, upward_layout, downward_layout, gains_layout, biases_layout = params
    text_heads = project_heads(text_rows, project_text, HEAD_TEXT)
    layout_heads = project_heads(layout_rows, project_layout, HEAD_LAYOUT)
    text_part = pair_scores(text_heads[:, :, 0], text_heads[:, :, 1], HEAD_TEXT)
    layout_part = pair_scores(layout_heads[:, :, 0], layout_heads[:, :, 1], HEAD_LAYOUT)
    if held_heads is None:
        held_part = layout_part
    else:
        held_part = pair_scores(held_heads[:, :, 0], held_heads[:, :, 1], HEAD_LAYOUT)
    valid = key_valid[:, None, None, :]
    text_scores = jnp.where(valid, low_back(text_part + held_part), NEGATIVE)
    layout_scores = jnp.where(valid, low_back(layout_part + text_part), NEGATIVE)
    text_probs = low(jax.nn.softmax(text_scores, axis=-1))
    layout_probs = low(jax.nn.softmax(layout_scores, axis=-1))
    text_next = attend_and_feed(text_rows, text_heads, text_probs, outward_text, upward_text, downward_text, gains_text, biases_text)
    layout_next = attend_and_feed(layout_rows, layout_heads, layout_probs, outward_layout, upward_layout, downward_layout, gains_layout, biases_layout)
    return (text_next, layout_next, layout_heads[:, :, :2])

def two_layers(text_piece, layout_piece, valid_piece, onehot_piece, table, weight_set, held_set):
    embedded = text_piece + jnp.einsum('gs,sd->gd', onehot_piece, table, precision=HIGH)[:, None, :]
    text_rows = low(low_back(embedded))
    layout_rows = low(low_back(layout_piece))
    kept_heads = []
    for layer in range(2):
        params = tuple((member[layer] for member in weight_set))
        held_heads = None if held_set is None else held_set[layer]
        text_rows, layout_rows, own_heads = coupled_layer(text_rows, layout_rows, params, valid_piece, held_heads)
        kept_heads.append(own_heads)
        if layer == 0:
            text_rows = low(low_back(text_rows))
            layout_rows = low(low_back(layout_rows))
    return (text_rows, layout_rows, jnp.stack(kept_heads))

def reference(text_input, layout_input, text_cotangent, layout_cotangent, page_counts, pad_mask, lang_ids, lang_table, text_project, text_outward, text_upward, text_downward, text_gains, text_biases, layout_project, layout_outward, layout_upward, layout_downward, layout_gains, layout_biases):
    total_pages = MB * PAGES
    group = math.gcd(total_pages, 8)
    steps_count = total_pages // group
    positions = jnp.arange(LENGTH, dtype=jnp.int32)
    key_valid = (positions[None, None, :] < page_counts[:, :, None]) & ((pad_mask == 1) | (positions[None, None, :] == 0))
    onehot = (lang_ids[:, :, None] == jnp.arange(LANGS, dtype=jnp.int32)[None, None, :]).astype(jnp.float32)

    def regroup(array):
        return array.reshape((steps_count, group) + array.shape[2:])
    valid_groups = regroup(key_valid)
    onehot_groups = regroup(onehot)
    weight_set = tuple((member.astype(jnp.float32) for member in (text_project, text_outward, text_upward, text_downward, text_gains, text_biases, layout_project, layout_outward, layout_upward, layout_downward, layout_gains, layout_biases)))
    text_float = text_input.astype(jnp.float32)
    layout_float = layout_input.astype(jnp.float32)

    def plain_group(carry, items):
        text_piece, layout_piece, valid_piece, onehot_piece = items
        unused_text, unused_layout, kept = two_layers(text_piece, layout_piece, valid_piece, onehot_piece, lang_table, weight_set, None)
        return (carry, kept)
    carry_zero = jnp.zeros((), jnp.float32)
    unused, held_groups = lax.scan(plain_group, carry_zero, (regroup(text_float), regroup(layout_float), valid_groups, onehot_groups))
    checked = jax.checkpoint(two_layers)

    def forward(text_rows, layout_rows, table, weights_now):

        def one_group(carry, items):
            text_piece, layout_piece, valid_piece, onehot_piece, held_piece = items
            text_out, layout_out, unused_heads = checked(text_piece, layout_piece, valid_piece, onehot_piece, table, weights_now, held_piece)
            return (carry, (text_out, layout_out))
        unused_carry, (text_all, layout_all) = lax.scan(one_group, carry_zero, (regroup(text_rows), regroup(layout_rows), valid_groups, onehot_groups, held_groups))
        return (text_all.reshape(text_rows.shape), layout_all.reshape(layout_rows.shape))
    (text_out, layout_out), pullback = jax.vjp(forward, text_float, layout_float, lang_table, weight_set)
    text_grad, layout_grad, table_grad, weight_grads = pullback((text_cotangent.astype(jnp.float32), layout_cotangent.astype(jnp.float32)))
    return (text_out.astype(jnp.bfloat16), layout_out.astype(jnp.bfloat16), text_grad.astype(jnp.bfloat16), layout_grad.astype(jnp.bfloat16), table_grad, weight_grads[0], weight_grads[1], weight_grads[2], weight_grads[3], weight_grads[4], weight_grads[5], weight_grads[6], weight_grads[7], weight_grads[8], weight_grads[9], weight_grads[10], weight_grads[11])
```

```python
import functools
import math

import jax
import jax.numpy as jnp
from jax import lax
from jax.experimental import pallas as pl
from jax.experimental.pallas import tpu as pltpu
from jax.sharding import PartitionSpec as P

HEAD_TEXT = 64
HEAD_LAYOUT = 16
EPSILON = 1e-05
NEGATIVE = -1e30
HIGH = lax.Precision.HIGHEST
MESH = pl.DeviceIdType.MESH
BF = jnp.bfloat16
F32 = jnp.float32
ANY = pl.BlockSpec(memory_space=pl.ANY)


def remote(src, dst, send, recv, device):
    return pltpu.make_async_remote_copy(
        src_ref=src, dst_ref=dst, send_sem=send, recv_sem=recv, device_id=device, device_id_type=MESH
    )


def greet(section, tensor, sections, tensors, extra=()):
    barrier = pltpu.get_barrier_semaphore()
    for g in range(sections):
        for q in range(tensors):

            @pl.when((section != g) | (tensor != q))
            def _():
                pl.semaphore_signal(
                    barrier, inc=1, device_id={"section": g, "tensor": q}, device_id_type=MESH
                )

    for device in extra:
        pl.semaphore_signal(barrier, inc=1, device_id=device, device_id_type=MESH)
    pl.semaphore_wait(barrier, sections * tensors - 1 + len(extra))


def fetch_kernel(sections, tensors, dp, shared, *refs):
    n_weights = len(shared)
    sources = (refs[0:2], refs[2:4])
    weights = refs[4 : 4 + n_weights]
    pages = refs[4 + n_weights : 6 + n_weights]
    full = refs[6 + n_weights : 6 + 2 * n_weights]
    page_send, page_recv, w_send, w_recv, own_sem = refs[6 + 2 * n_weights :]
    section, d, t = lax.axis_index("section"), lax.axis_index("dp"), lax.axis_index("tensor")
    sibling = t + 1 - 2 * (t % 2)
    partner = (t + tensors // 2) % tensors
    mate = d + 1 - 2 * (d % 2)
    half = d % 2
    length = sources[0][0].shape[1]
    greet(section, t, sections, tensors, ({"dp": mate},))

    def rows(ref, i, which):
        count = ref.shape[1] // 2
        if not shared[i]:
            return ref
        return ref.at[:, pl.ds(pl.multiple_of(which * count, 16), count)]

    def part(ref, i, slot, which):
        if not shared[i]:
            return ref.at[slot]
        count = ref.shape[1] // 2
        return ref.at[slot, pl.ds(pl.multiple_of(which * count, 16), count)]

    def own_part(i):
        if not shared[i]:
            return weights[i]
        count = weights[i].shape[0] // 2
        return weights[i].at[pl.ds(pl.multiple_of(half * count, 16), count)]

    def token_slot(a, index):
        start = pl.multiple_of(index * length, length)
        return pages[a].at[pl.ds(start, length)] if a == 0 else pages[a].at[:, pl.ds(start, length)]

    def over_pages(act):
        for g in range(sections):
            for j in range(2):
                target = 2 * j + section
                here = (section == g) & (t == target)
                for a in range(2):
                    act(g, j, a, target, here)

    def page_start(g, j, a, target, here):
        src, dst = sources[g][a].at[j], token_slot(a, t)

        @pl.when(here)
        def _():
            pltpu.make_async_copy(src, dst, page_recv.at[a, t]).start()

        @pl.when(jnp.logical_not(here))
        def _():
            remote(
                src, dst, page_send.at[g, j, a], page_recv.at[a, t], {"section": g, "tensor": target}
            ).start()

    def page_sent(g, j, a, target, here):
        @pl.when(jnp.logical_not(here))
        def _():
            remote(
                sources[g][a].at[j], token_slot(a, t), page_send.at[g, j, a], page_recv.at[a, t],
                {"section": g, "tensor": target},
            ).wait_send()

    over_pages(page_start)

    def to_partner(i):
        return remote(
            own_part(i), part(full[i], i, t, half), w_send.at[0, i], w_recv.at[0, i], {"tensor": partner}
        )

    def to_sibling(i):
        return remote(
            weights[i], full[i].at[t], w_send.at[1, i], w_recv.at[1, i], {"tensor": sibling}
        )

    def to_mate(i):
        ref = part(full[i], i, partner, half)
        return remote(ref, ref, w_send.at[2, i], w_recv.at[2, i], {"dp": mate})

    def on_first(i):
        ref = part(full[i], i, partner, half)
        return remote(ref, ref, w_send.at[3, i], w_recv.at[3, i], {"tensor": sibling})

    def on_second(i):
        ref = part(full[i], i, partner, 1 - half)
        return remote(ref, ref, w_send.at[4, i], w_recv.at[4, i], {"tensor": sibling})

    def keep(i):
        return pltpu.make_async_copy(weights[i], full[i].at[t], own_sem.at[i])

    for i in range(n_weights):
        to_partner(i).start()
        to_sibling(i).start()
        keep(i).start()
    for i in range(n_weights):
        to_partner(i).wait_recv()
        on_first(i).start()
        if shared[i]:
            to_mate(i).start()
    for i in range(n_weights):
        if shared[i]:
            to_mate(i).wait_recv()
            on_second(i).start()
    for i in range(n_weights):
        keep(i).wait()
        to_sibling(i).wait()
        to_partner(i).wait_send()
        on_first(i).wait()
        if shared[i]:
            to_mate(i).wait_send()
            on_second(i).wait()
    over_pages(page_sent)
    for a in range(2):
        for q in range(tensors):
            slot = token_slot(a, q)
            remote(slot, slot, page_send.at[0, 0, a], page_recv.at[a, q], {"tensor": sibling}).wait_recv()


def fetch(mesh, text_in, layout_in, text_cot, layout_cot, weights):
    sections, dp, tensors = mesh.shape["section"], mesh.shape["dp"], mesh.shape["tensor"]
    length = text_in.shape[1] * tensors
    shared = tuple(dp % 2 == 0 and w.shape[0] >= 512 for w in weights)
    n = len(weights)
    shapes = (
        jax.ShapeDtypeStruct((length, text_in.shape[2]), BF),
        jax.ShapeDtypeStruct((layout_in.shape[1], length), BF),
    ) + tuple(jax.ShapeDtypeStruct((tensors,) + w.shape, BF) for w in weights)
    outs = pl.pallas_call(
        functools.partial(fetch_kernel, sections, tensors, dp, shared),
        out_shape=shapes,
        in_specs=[ANY] * (4 + n),
        out_specs=[ANY] * len(shapes),
        scratch_shapes=[
            pltpu.SemaphoreType.DMA((sections, 2, 2)),
            pltpu.SemaphoreType.DMA((2, tensors)),
            pltpu.SemaphoreType.DMA((5, n)),
            pltpu.SemaphoreType.DMA((5, n)),
            pltpu.SemaphoreType.DMA((n,)),
        ],
        compiler_params=pltpu.CompilerParams(collective_id=0, has_side_effects=True),
        name="fetch",
    )(text_in, layout_in, text_cot, layout_cot, *weights)
    return outs[0], outs[1], outs[2:]


def return_kernel(sections, tensors, text, layout, text_out, layout_out, grad_out, layout_grad_out, send, recv):
    section, t = lax.axis_index("section"), lax.axis_index("tensor")
    length = text_out.shape[1]
    greet(section, t, sections, tensors)
    micro, page = t % 2, t // 2
    kinds = ((grad_out, layout_grad_out), (text_out, layout_out))

    def source(a, q):
        start = q * length
        return text.at[pl.ds(start, length)] if a == 0 else layout.at[:, pl.ds(start, length)]

    def each(act):
        for g in range(sections):
            for q in range(tensors):
                for a in range(2):
                    @pl.when(section == g)
                    def _():
                        act(g, q, a, (micro == g) & (t == q))

    def start(g, q, a, here):
        src, dst = source(a, q), kinds[g][a].at[page]

        @pl.when(here)
        def _():
            pltpu.make_async_copy(src, dst, recv.at[g, a, page]).start()

        @pl.when(jnp.logical_not(here))
        def _():
            remote(src, dst, send.at[q, a], recv.at[g, a, page], {"section": micro, "tensor": q}).start()

    def sent(g, q, a, here):
        @pl.when(jnp.logical_not(here))
        def _():
            remote(
                source(a, q), kinds[g][a].at[page], send.at[q, a], recv.at[g, a, page],
                {"section": micro, "tensor": q},
            ).wait_send()

    each(start)
    each(sent)
    for g in range(sections):
        for a in range(2):
            for j in range(2):
                dst = kinds[g][a].at[j]
                remote(dst, dst, send.at[0, a], recv.at[g, a, j], {"tensor": (t + 1) % tensors}).wait_recv()


def give_back(mesh, text, layout):
    sections, tensors = mesh.shape["section"], mesh.shape["tensor"]
    length = text.shape[0] // tensors
    text_shape = jax.ShapeDtypeStruct((2, length, text.shape[1]), BF)
    layout_shape = jax.ShapeDtypeStruct((2, layout.shape[0], length), BF)
    return pl.pallas_call(
        functools.partial(return_kernel, sections, tensors),
        out_shape=(text_shape, layout_shape, text_shape, layout_shape),
        in_specs=[ANY] * 2,
        out_specs=[ANY] * 4,
        scratch_shapes=[
            pltpu.SemaphoreType.DMA((tensors, 2)),
            pltpu.SemaphoreType.DMA((sections, 2, 2)),
        ],
        compiler_params=pltpu.CompilerParams(collective_id=1, has_side_effects=True),
        name="give_back",
    )(text, layout)


def norm_forward(summed, gain, offset):
    center = summed - jnp.mean(summed, axis=-1, keepdims=True)
    inverse = lax.rsqrt(jnp.mean(center * center, axis=-1, keepdims=True) + EPSILON)
    normed = center * inverse
    return (normed * gain + offset, normed, inverse)


def norm_backward(upstream, normed, inverse, gain):
    scaled = upstream * gain
    mean_scaled = jnp.mean(scaled, axis=-1, keepdims=True)
    mean_product = jnp.mean(scaled * normed, axis=-1, keepdims=True)
    downstream = inverse * (scaled - mean_scaled - normed * mean_product)
    return (downstream, jnp.sum(upstream * normed, axis=0), jnp.sum(upstream, axis=0))


def activation(values):
    return jax.nn.gelu(values, approximate=False)


def mm(spec, a, b):
    return jnp.einsum(spec, a, b, preferred_element_type=F32)


def layer_forward(rows, weights, norms, valid):
    heads = []
    for b in range(2):
        qkv = mm("ld,tnd->ltn", rows[b], weights[b][0]).astype(BF)
        heads.append(qkv.reshape(qkv.shape[0], qkv.shape[1], 3, -1, (HEAD_TEXT, HEAD_LAYOUT)[b]))
    scores = mm("qthd,kthd->thqk", heads[0][:, :, 0], heads[0][:, :, 1]) * (1.0 / math.sqrt(HEAD_TEXT))
    scores = scores + mm("qthd,kthd->thqk", heads[1][:, :, 0], heads[1][:, :, 1]) * (
        1.0 / math.sqrt(HEAD_LAYOUT)
    )
    scores = jnp.where(valid[None, None, None, :], scores, NEGATIVE)
    highest = jnp.max(scores, axis=-1, keepdims=True)
    raised = jnp.exp(scores - highest)
    probs = (raised / jnp.sum(raised, axis=-1, keepdims=True)).astype(BF)
    outs, kept = [], []
    for b in range(2):
        gains, biases = norms[b]
        context = mm("thqk,kthd->qthd", probs, heads[b][:, :, 2]).astype(BF)
        context = context.reshape(context.shape[0], context.shape[1], -1)
        attended = mm("ltn,tnd->ld", context, weights[b][1])
        hidden, n1, r1 = norm_forward(rows[b].astype(F32) + attended, gains[0], biases[0])
        low = hidden.astype(BF)
        pre = mm("ld,tdn->ltn", low, weights[b][2])
        active = activation(pre).astype(BF)
        fed = mm("ltn,tnd->ld", active, weights[b][3])
        out, n2, r2 = norm_forward(hidden + fed, gains[1], biases[1])
        outs.append(out.astype(BF))
        kept.append((context, n1, r1, low, pre, active, n2, r2))
    return tuple(outs), (tuple(heads), probs, tuple(kept))


def layer_backward(saved, grads, weights, norms):
    heads, probs, kept = saved
    probs_f = probs.astype(F32)
    norm_grads, operands, dz_ones, score_grads, context_grads = [], [], [], [], []
    for b in range(2):
        gains, biases = norms[b]
        context, n1, r1, low, pre, active, n2, r2 = kept[b]
        dz_two, g2, b2 = norm_backward(grads[b].astype(F32), n2, r2, gains[1])
        gf = dz_two.astype(BF)
        d_active = mm("ld,tnd->ltn", gf, weights[b][3])
        d_pre = jax.vjp(activation, pre)[1](d_active)[0].astype(BF)
        d_hidden = dz_two + mm("ltn,tdn->ld", d_pre, weights[b][2])
        dz_one, g1, b1 = norm_backward(d_hidden, n1, r1, gains[0])
        ga = dz_one.astype(BF)
        d_context = mm("ld,tnd->ltn", ga, weights[b][1]).astype(BF)
        d_context = d_context.reshape(heads[b][:, :, 2].shape)
        d_probs = mm("qthd,kthd->thqk", d_context, heads[b][:, :, 2])
        inner = jnp.sum(probs_f * d_probs, axis=-1, keepdims=True)
        score_grads.append((probs_f * (d_probs - inner)).astype(BF))
        context_grads.append(d_context)
        dz_ones.append(dz_one)
        norm_grads.append((jnp.stack([g1, g2]), jnp.stack([b1, b2])))
        operands.append([gf, d_pre, ga])
    total = (score_grads[0].astype(F32) + score_grads[1].astype(F32)).astype(BF)
    reaching = (total, score_grads[1])
    downs, out_operands = [], []
    for b in range(2):
        scale = 1.0 / math.sqrt((HEAD_TEXT, HEAD_LAYOUT)[b])
        dq = (mm("thqk,kthd->qthd", reaching[b], heads[b][:, :, 1]) * scale).astype(BF)
        dk = (mm("thqk,qthd->kthd", reaching[b], heads[b][:, :, 0]) * scale).astype(BF)
        dv = mm("thqk,qthd->kthd", probs, context_grads[b]).astype(BF)
        stacked = jnp.stack([dq, dk, dv], axis=2)
        stacked = stacked.reshape(stacked.shape[0], stacked.shape[1], -1)
        down = dz_ones[b] + mm("ltn,tnd->ld", stacked, weights[b][0])
        downs.append(down.astype(BF))
        out_operands.append((stacked, *operands[b]))
    return tuple(downs), tuple(out_operands), tuple(norm_grads)


def zeros_like_tree(shapes):
    return jax.tree.map(lambda s: jnp.zeros(s.shape, s.dtype), shapes)


def reduce_shard(grad, t, tensors):
    sibling = [(i, i + 1 - 2 * (i % 2)) for i in range(tensors)]
    partner = [(i, (i + tensors // 2) % tensors) for i in range(tensors)]
    pairs = grad.reshape((2, tensors // 2) + grad.shape[1:])
    core, chip = t % 2, t // 2
    theirs = lax.dynamic_index_in_dim(pairs, 1 - core, 1, keepdims=False)
    mine = lax.dynamic_index_in_dim(pairs, core, 1, keepdims=False)
    summed = (mine.astype(F32) + lax.ppermute(theirs, "tensor", sibling).astype(F32)).astype(BF)
    theirs = lax.dynamic_index_in_dim(summed, 1 - chip, 0, keepdims=False)
    mine = lax.dynamic_index_in_dim(summed, chip, 0, keepdims=False)
    summed = (mine.astype(F32) + lax.ppermute(theirs, "tensor", partner).astype(F32)).astype(BF)
    return lax.psum(summed, "dp").astype(F32)


def per_device(
    mesh,
    text_input,
    layout_input,
    text_cotangent,
    layout_cotangent,
    page_counts,
    pad_mask,
    lang_ids,
    lang_table,
    text_project,
    text_outward,
    text_upward,
    text_downward,
    text_gains,
    text_biases,
    layout_project,
    layout_outward,
    layout_upward,
    layout_downward,
    layout_gains,
    layout_biases,
):
    section, t = lax.axis_index("section"), lax.axis_index("tensor")
    tensors = mesh.shape["tensor"]
    micro, page = t % 2, t // 2

    def flat(project):
        return jnp.transpose(project[0], (1, 2, 0)).reshape(-1, project.shape[1])

    own_ids = lax.dynamic_index_in_dim(lang_ids, section, 0, keepdims=False)
    groups = jnp.arange(lang_table.shape[0], dtype=jnp.int32)
    onehot = (own_ids[:, None] == groups[None, :]).astype(F32)
    lang_rows = jnp.dot(onehot, lang_table, precision=HIGH)
    embedded = (text_input[0].astype(F32) + lang_rows[:, None, :]).astype(BF)
    flipped = lambda block: jnp.transpose(block[0], (0, 2, 1))
    shards = (
        flat(text_project), text_outward[0], text_upward[0], text_downward[0],
        flat(layout_project), layout_outward[0], layout_upward[0], layout_downward[0],
    )
    text_page, layout_page, full = fetch(
        mesh, embedded, flipped(layout_input), text_cotangent[0], flipped(layout_cotangent), shards
    )
    weights = (full[0:4], full[4:8])
    norms = ((text_gains[0], text_biases[0]), (layout_gains[0], layout_biases[0]))
    counts = page_counts[micro, page]
    positions = jnp.arange(pad_mask.shape[2], dtype=jnp.int32)
    valid = (positions < counts) & ((pad_mask[micro, page] == 1) | (positions == 0))
    arrived = (text_page, layout_page.T)

    def run(rows):
        return (rows,) + layer_forward(rows, weights, norms, valid)

    shapes = jax.eval_shape(run, arrived)
    kept = lax.cond(section == 0, run, lambda rows: zeros_like_tree(shapes), arrived)
    hopped = tuple(lax.ppermute(block, "section", [(0, 1)]) for block in kept[1])
    rows, outs, saved = lax.cond(section == 1, lambda old, got: run(got), lambda old, got: old, kept, hopped)

    def back(grads):
        return layer_backward(saved, grads, weights, norms)

    back_shapes = jax.eval_shape(back, arrived)
    first = lax.cond(section == 1, back, lambda grads: zeros_like_tree(back_shapes), arrived)
    hopped = tuple(lax.ppermute(block, "section", [(1, 0)]) for block in first[0])
    downs, operands, norm_grads = lax.cond(
        section == 0, lambda old, got: back(got), lambda old, got: old, first, hopped
    )
    _, _, kept = saved
    grads = []
    for b in range(2):
        stacked, gf, d_pre, ga = operands[b]
        context, n1, r1, low, pre, active, n2, r2 = kept[b]
        grads.append((
            mm("ltn,ld->tnd", stacked, rows[b]).astype(BF),
            mm("ltn,ld->tnd", context, ga).astype(BF),
            mm("ld,ltn->tdn", low, d_pre).astype(BF),
            mm("ltn,ld->tnd", active, gf).astype(BF),
        ))
    final = tuple(jnp.where(section == 0, d, o) for d, o in zip(downs, outs))
    text_out, layout_out, text_grad, layout_grad = give_back(mesh, final[0], final[1].T)
    summed = [[reduce_shard(g, t, tensors) for g in per_stream] for per_stream in grads]

    own_group = lax.dynamic_index_in_dim(lang_ids[:, page], micro, 0, keepdims=False)
    page_sum = jnp.where(section == 0, jnp.sum(downs[0].astype(F32), axis=0), 0.0)
    lang_grad = (groups == own_group).astype(F32)[:, None] * page_sum[None, :]
    pick = (jnp.arange(2, dtype=jnp.int32) == section).astype(F32)[:, None, None]
    small = lax.psum(
        tuple(pick * member[None] for pair in norm_grads for member in pair) + (lang_grad,),
        ("section", "dp", "tensor"),
    )

    def own_row(stacked):
        return lax.dynamic_slice_in_dim(stacked, section, 1, 0)

    def unflat(grad, like):
        return jnp.transpose(grad.reshape(like.shape[2], like.shape[3], like.shape[1]), (2, 0, 1))[None]

    unflip = lambda block: jnp.transpose(block, (0, 2, 1))[None]
    return (
        text_out[None], unflip(layout_out), text_grad[None], unflip(layout_grad), small[4],
        unflat(summed[0][0], text_project), summed[0][1][None], summed[0][2][None], summed[0][3][None],
        own_row(small[0]), own_row(small[1]),
        unflat(summed[1][0], layout_project), summed[1][1][None], summed[1][2][None], summed[1][3][None],
        own_row(small[2]), own_row(small[3]),
    )


def solution(mesh):
    tokens = P("section", "dp", "tensor", None)
    weight_specs = (
        P("section", None, None, "tensor"), P("section", "tensor", None), P("section", None, "tensor"),
        P("section", "tensor", None), P("section", None, None), P("section", None, None),
    )
    in_specs = (tokens,) * 4 + (P(None, "dp"), P(None, "dp", None), P(None, "dp"), P()) + weight_specs * 2
    out_specs = (tokens,) * 4 + (P(),) + weight_specs * 2
    return jax.shard_map(
        functools.partial(per_device, mesh), mesh=mesh, in_specs=in_specs, out_specs=out_specs, check_vma=False
    )
```

```python
import functools
import math
import typing

import jax
import jax.numpy as jnp
from jax import lax
from jax.experimental import pallas as pl
from jax.experimental.pallas import tpu as pltpu
from jax.sharding import PartitionSpec as P

HEAD_TEXT = 64
HEAD_LAYOUT = 16
EPSILON = 1e-05
NEGATIVE = -1e30
HIGH = lax.Precision.HIGHEST
MESH = pl.DeviceIdType.MESH
BF = jnp.bfloat16
F32 = jnp.float32
ANY = pl.BlockSpec(memory_space=pl.ANY)


def remote(src, dst, send, recv, device):
    return pltpu.make_async_remote_copy(
        src_ref=src, dst_ref=dst, send_sem=send, recv_sem=recv, device_id=device, device_id_type=MESH
    )


def greet(section, tensor, sections, tensors, extra=()):
    barrier = pltpu.get_barrier_semaphore()
    for g in range(sections):
        for q in range(tensors):

            @pl.when((section != g) | (tensor != q))
            def _():
                pl.semaphore_signal(
                    barrier, inc=1, device_id={"section": g, "tensor": q}, device_id_type=MESH
                )

    for device in extra:
        pl.semaphore_signal(barrier, inc=1, device_id=device, device_id_type=MESH)
    pl.semaphore_wait(barrier, sections * tensors - 1 + len(extra))


def fetch_kernel(sections, tensors, dp, shared, *refs):
    n_weights = len(shared)
    sources = (refs[0:2], refs[2:4])
    weights = refs[4 : 4 + n_weights]
    pages = refs[4 + n_weights : 6 + n_weights]
    full = refs[6 + n_weights : 6 + 2 * n_weights]
    page_send, page_recv, w_send, w_recv, own_sem = refs[6 + 2 * n_weights :]
    section, d, t = lax.axis_index("section"), lax.axis_index("dp"), lax.axis_index("tensor")
    sibling = t + 1 - 2 * (t % 2)
    partner = (t + tensors // 2) % tensors
    mate = d + 1 - 2 * (d % 2)
    half = d % 2
    length = sources[0][0].shape[1]
    greet(section, t, sections, tensors, ({"dp": mate},))

    def part(ref, i, slot, which):
        if not shared[i]:
            return ref.at[slot]
        count = ref.shape[1] // 2
        return ref.at[slot, pl.ds(pl.multiple_of(which * count, 16), count)]

    def own_part(i):
        if not shared[i]:
            return weights[i]
        count = weights[i].shape[0] // 2
        return weights[i].at[pl.ds(pl.multiple_of(half * count, 16), count)]

    def token_slot(a, index):
        start = pl.multiple_of(index * length, length)
        return pages[a].at[pl.ds(start, length)] if a == 0 else pages[a].at[:, pl.ds(start, length)]

    def over_pages(g, act):
        for j in range(2):
            target = 2 * j + section
            here = (section == g) & (t == target)
            for a in range(2):
                act(g, j, a, target, here)

    def page_start(g, j, a, target, here):
        src, dst = sources[g][a].at[j], token_slot(a, t)

        @pl.when(here)
        def _():
            pltpu.make_async_copy(src, dst, page_recv.at[a, t]).start()

        @pl.when(jnp.logical_not(here))
        def _():
            remote(
                src, dst, page_send.at[g, j, a], page_recv.at[a, t], {"section": g, "tensor": target}
            ).start()

    def page_sent(g, j, a, target, here):
        @pl.when(jnp.logical_not(here))
        def _():
            remote(
                sources[g][a].at[j], token_slot(a, t), page_send.at[g, j, a], page_recv.at[a, t],
                {"section": g, "tensor": target},
            ).wait_send()

    over_pages(0, page_start)

    def to_partner(i):
        return remote(
            own_part(i), part(full[i], i, t, half), w_send.at[0, i], w_recv.at[0, i], {"tensor": partner}
        )

    def to_sibling(i):
        return remote(
            weights[i], full[i].at[t], w_send.at[1, i], w_recv.at[1, i], {"tensor": sibling}
        )

    def to_mate(i):
        ref = part(full[i], i, partner, half)
        return remote(ref, ref, w_send.at[2, i], w_recv.at[2, i], {"dp": mate})

    def on_first(i):
        ref = part(full[i], i, partner, half)
        return remote(ref, ref, w_send.at[3, i], w_recv.at[3, i], {"tensor": sibling})

    def on_second(i):
        ref = part(full[i], i, partner, 1 - half)
        return remote(ref, ref, w_send.at[4, i], w_recv.at[4, i], {"tensor": sibling})

    def keep(i):
        return pltpu.make_async_copy(weights[i], full[i].at[t], own_sem.at[i])

    to_partner(0).start()
    to_partner(1).start()
    for i in range(n_weights):
        to_sibling(i).start()
        keep(i).start()
    for i in range(n_weights):
        to_partner(i).wait()
        if i + 2 < n_weights:
            to_partner(i + 2).start()
        if shared[i]:
            to_mate(i).start()
        on_first(i).start()
    over_pages(1, page_start)
    for i in range(n_weights):
        if shared[i]:
            to_mate(i).wait_recv()
            on_second(i).start()
    for i in range(n_weights):
        keep(i).wait()
        to_sibling(i).wait()
        on_first(i).wait()
        if shared[i]:
            to_mate(i).wait_send()
            on_second(i).wait()
    for g in range(sections):
        over_pages(g, page_sent)
    for a in range(2):
        for q in range(tensors):
            slot = token_slot(a, q)
            remote(slot, slot, page_send.at[0, 0, a], page_recv.at[a, q], {"tensor": sibling}).wait_recv()


def fetch(mesh, text_in, layout_in, text_cot, layout_cot, weights):
    sections, dp, tensors = mesh.shape["section"], mesh.shape["dp"], mesh.shape["tensor"]
    length = text_in.shape[1] * tensors
    shared = tuple(dp % 2 == 0 and w.shape[0] >= 512 for w in weights)
    n = len(weights)
    shapes = (
        jax.ShapeDtypeStruct((length, text_in.shape[2]), BF),
        jax.ShapeDtypeStruct((layout_in.shape[1], length), BF),
    ) + tuple(jax.ShapeDtypeStruct((tensors,) + w.shape, BF) for w in weights)
    outs = pl.pallas_call(
        functools.partial(fetch_kernel, sections, tensors, dp, shared),
        out_shape=shapes,
        in_specs=[ANY] * (4 + n),
        out_specs=[ANY] * len(shapes),
        scratch_shapes=[
            pltpu.SemaphoreType.DMA((sections, 2, 2)),
            pltpu.SemaphoreType.DMA((2, tensors)),
            pltpu.SemaphoreType.DMA((5, n)),
            pltpu.SemaphoreType.DMA((5, n)),
            pltpu.SemaphoreType.DMA((n,)),
        ],
        compiler_params=pltpu.CompilerParams(collective_id=0, has_side_effects=True),
        name="fetch",
    )(text_in, layout_in, text_cot, layout_cot, *weights)
    return outs[0], outs[1], outs[2:]


def return_kernel(sections, tensors, text, layout, text_out, layout_out, grad_out, layout_grad_out, send, recv):
    section, t = lax.axis_index("section"), lax.axis_index("tensor")
    length = text_out.shape[1]
    greet(section, t, sections, tensors)
    micro, page = t % 2, t // 2
    kinds = ((grad_out, layout_grad_out), (text_out, layout_out))

    def source(a, q):
        start = q * length
        return text.at[pl.ds(start, length)] if a == 0 else layout.at[:, pl.ds(start, length)]

    def each(act):
        for g in range(sections):
            for q in range(tensors):
                for a in range(2):
                    @pl.when(section == g)
                    def _():
                        act(g, q, a, (micro == g) & (t == q))

    def start(g, q, a, here):
        src, dst = source(a, q), kinds[g][a].at[page]

        @pl.when(here)
        def _():
            pltpu.make_async_copy(src, dst, recv.at[g, a, page]).start()

        @pl.when(jnp.logical_not(here))
        def _():
            remote(src, dst, send.at[q, a], recv.at[g, a, page], {"section": micro, "tensor": q}).start()

    def sent(g, q, a, here):
        @pl.when(jnp.logical_not(here))
        def _():
            remote(
                source(a, q), kinds[g][a].at[page], send.at[q, a], recv.at[g, a, page],
                {"section": micro, "tensor": q},
            ).wait_send()

    each(start)
    each(sent)
    for g in range(sections):
        for a in range(2):
            for j in range(2):
                dst = kinds[g][a].at[j]
                remote(dst, dst, send.at[0, a], recv.at[g, a, j], {"tensor": (t + 1) % tensors}).wait_recv()


def give_back(mesh, text, layout):
    sections, tensors = mesh.shape["section"], mesh.shape["tensor"]
    length = text.shape[0] // tensors
    text_shape = jax.ShapeDtypeStruct((2, length, text.shape[1]), BF)
    layout_shape = jax.ShapeDtypeStruct((2, layout.shape[0], length), BF)
    return pl.pallas_call(
        functools.partial(return_kernel, sections, tensors),
        out_shape=(text_shape, layout_shape, text_shape, layout_shape),
        in_specs=[ANY] * 2,
        out_specs=[ANY] * 4,
        scratch_shapes=[
            pltpu.SemaphoreType.DMA((tensors, 2)),
            pltpu.SemaphoreType.DMA((sections, 2, 2)),
        ],
        compiler_params=pltpu.CompilerParams(collective_id=1, has_side_effects=True),
        name="give_back",
    )(text, layout)


GELU_P = 0.3275911
GELU_A = (0.254829592, -0.284496736, 1.421413741, -1.453152027, 1.061405429)
NN = (((1,), (0,)), ((), ()))
NT = (((1,), (1,)), ((), ()))
SCALES = (1.0 / math.sqrt(HEAD_TEXT), 1.0 / math.sqrt(HEAD_LAYOUT))
SIZES = (HEAD_TEXT, HEAD_LAYOUT)
ROWS = 128


class Weights(typing.NamedTuple):
    project: typing.Any
    outward: typing.Any
    upward: typing.Any
    downward: typing.Any


class Kept(typing.NamedTuple):
    qkv: typing.Any
    ctx: typing.Any
    n1: typing.Any
    r1: typing.Any
    low: typing.Any
    act: typing.Any
    slope: typing.Any
    n2: typing.Any
    r2: typing.Any


class Needed(typing.NamedTuple):
    g: typing.Any
    n2: typing.Any
    r2: typing.Any
    downward: typing.Any
    slope: typing.Any
    upward: typing.Any
    n1: typing.Any
    r1: typing.Any
    outward: typing.Any
    qkv: typing.Any
    project: typing.Any


class Back(typing.NamedTuple):
    dx: typing.Any
    dqkv: typing.Any
    gf: typing.Any
    dpre: typing.Any
    ga: typing.Any


def dot(a, b, dims=NN):
    return lax.dot_general(a, b, dims, preferred_element_type=F32)


def gelu_pair(u):
    t = 1.0 / (1.0 + (GELU_P / math.sqrt(2.0)) * jnp.abs(u))
    e = jnp.exp(-0.5 * (u * u))
    a1, a2, a3, a4, a5 = (0.5 * a for a in GELU_A)
    tail = ((((a5 * t + a4) * t + a3) * t + a2) * t + a1) * t * e
    cdf = jnp.where(u >= 0, 1.0 - tail, tail)
    return u * cdf, cdf + u * e * (1.0 / math.sqrt(2.0 * math.pi))


def norm_rows(z, gain, offset):
    center = z - jnp.mean(z, axis=-1, keepdims=True)
    inverse = lax.rsqrt(jnp.mean(center * center, axis=-1, keepdims=True) + EPSILON)
    normed = center * inverse
    return normed * gain + offset, normed, inverse


def norm_rows_back(g, n, r, gain):
    t = g * gain
    return r * (t - jnp.mean(t, axis=-1, keepdims=True) - n * jnp.mean(t * n, axis=-1, keepdims=True))


class Staged:
    def __init__(self, tree, hbm, vmem, sem, inward):
        self.tree, self.vmem = tree, list(vmem)
        pairs = zip(hbm, vmem) if inward else zip(vmem, hbm)
        self.copies = [pltpu.make_async_copy(a, b, sem.at[i]) for i, (a, b) in enumerate(pairs)]

    def refs(self):
        return jax.tree.unflatten(self.tree, self.vmem)

    def parts(self):
        return jax.tree.unflatten(self.tree, self.copies)

    def start(self):
        for copy in self.copies:
            copy.start()

    def wait(self):
        for copy in self.copies:
            copy.wait()


def start(*copies):
    for copy in copies:
        copy.start()


def wait(*copies):
    for copy in copies:
        copy.wait()


def head_rows(stacks, slot, kind, local, scales=None):
    rows = []
    for b in range(2):
        first = kind * (stacks[b].shape[1] // 3) + local * SIZES[b]
        piece = stacks[b][slot, first : first + SIZES[b], :]
        rows.append(piece if scales is None else piece * BF(scales[b]))
    rows.append(jnp.zeros((128 - sum(SIZES), rows[0].shape[1]), BF))
    return jnp.concatenate(rows, axis=0)


def put_head(stacks, slot, kind, local, b, value):
    first = kind * (stacks[b].shape[1] // 3) + local * SIZES[b]
    stacks[b][slot, first : first + SIZES[b], :] = value.astype(BF)


def forward_kernel(in_tree, out_tree, *refs):
    n_in, n_out = in_tree.num_leaves, out_tree.num_leaves
    hbm_in, (valid, *norms) = refs[:n_in], refs[n_in : n_in + 5]
    hbm_out = refs[n_in + 5 : n_in + 5 + n_out]
    rest = refs[n_in + 5 + n_out :]
    (*nats, total_t, total_l, in_sem, out_sem) = rest[n_in + n_out :]
    incoming = Staged(in_tree, hbm_in, rest[:n_in], in_sem, True)
    outgoing = Staged(out_tree, hbm_out, rest[n_in : n_in + n_out], out_sem, False)
    x, weights = incoming.refs()
    x_in, weights_in = incoming.parts()
    y, probs_out, kept = outgoing.refs()
    y_out, probs_copy, kept_out = outgoing.parts()
    slots, length = weights[0].project.shape[0], x[0].shape[0]
    local_heads = weights[0].project.shape[1] // (3 * HEAD_TEXT)
    incoming.start()
    wait(*x_in, weights_in[0].project, weights_in[1].project)
    qkv = (kept[0].qkv, kept[1].qkv)

    @pl.loop(0, slots)
    def _(t):
        for b in range(2):
            qkv[b][t] = dot(weights[b].project[t], x[b][...], NT).astype(BF)

    start(kept_out[0].qkv, kept_out[1].qkv)
    key_mask = valid[...] > 0

    @pl.loop(0, slots)
    def _(t):
        for local in range(local_heads):
            q = head_rows(qkv, t, 0, local, SCALES).T
            scores = jnp.where(key_mask, dot(q, head_rows(qkv, t, 1, local)), NEGATIVE)
            raised = jnp.exp(scores - jnp.max(scores, axis=-1, keepdims=True))
            probs = (raised * (1.0 / jnp.sum(raised, axis=-1, keepdims=True))).astype(BF)
            probs_out[t, local] = probs
            ctx = dot(head_rows(qkv, t, 2, local), probs, NT).astype(BF)
            kept[0].ctx[t, local * HEAD_TEXT : (local + 1) * HEAD_TEXT, :] = ctx[:HEAD_TEXT]
            kept[1].ctx[t, local * HEAD_LAYOUT : (local + 1) * HEAD_LAYOUT, :] = ctx[
                HEAD_TEXT : HEAD_TEXT + HEAD_LAYOUT
            ]

    start(probs_copy, kept_out[0].ctx, kept_out[1].ctx)
    for b, total in enumerate((total_t, total_l)):
        gains, biases = norms[2 * b : 2 * b + 2]
        width = x[b].shape[1]
        hidden, fed = total.at[0], total.at[1]
        own, own_out, nat = kept[b], kept_out[b], nats[b]
        nat[...] = own.ctx[...].reshape(width, length).T
        wait(weights_in[b].outward)
        wide = weights[b].outward[...].reshape(width, width)
        for c in range(0, length, ROWS):
            rows = slice(c, c + ROWS)
            h, n, r = norm_rows(x[b][rows].astype(F32) + dot(nat[rows], wide), gains[0:1], biases[0:1])
            hidden[rows] = h
            own.n1[rows] = n
            own.r1[rows] = r
            own.low[rows] = h.astype(BF)
        start(own_out.n1, own_out.r1, own_out.low)
        wait(weights_in[b].upward, weights_in[b].downward)
        fed[...] = jnp.zeros((length, width), F32)

        @pl.loop(0, slots)
        def _(t):
            for c in range(0, length, 2 * ROWS):
                rows = slice(c, c + 2 * ROWS)
                act, slope = gelu_pair(dot(own.low[rows], weights[b].upward[t]))
                act = act.astype(BF)
                own.act[t, rows] = act
                own.slope[t, rows] = slope.astype(BF)
                fed[rows] += dot(act, weights[b].downward[t])

        start(own_out.act, own_out.slope)
        for c in range(0, length, ROWS):
            rows = slice(c, c + ROWS)
            out, n, r = norm_rows(hidden[rows] + fed[rows], gains[1:2], biases[1:2])
            y[b][rows] = out.astype(BF)
            own.n2[rows] = n
            own.r2[rows] = r
        start(y_out[b], own_out.n2, own_out.r2)
    outgoing.wait()


def vmem_like(tree):
    return [pltpu.VMEM(s.shape, s.dtype) for s in jax.tree.leaves(tree)]


VMEM = pl.BlockSpec(memory_space=pltpu.VMEM)
BIG = pltpu.CompilerParams(vmem_limit_bytes=60 << 20)


def shape(dims, dtype=BF):
    return jax.ShapeDtypeStruct(tuple(dims), dtype)


def layer_forward(rows, weights, norms, valid):
    length = rows[0].shape[0]
    slots, local_heads = weights[0].project.shape[0], weights[0].project.shape[1] // (3 * HEAD_TEXT)
    kept = []
    for x, w in zip(rows, weights):
        units, column = shape((slots, length, w.upward.shape[2])), shape((length, 1), F32)
        kept.append(Kept(
            qkv=shape((slots, w.project.shape[1], length)), ctx=shape((slots, w.outward.shape[1], length)),
            n1=shape(x.shape, F32), r1=column, low=shape(x.shape), act=units, slope=units,
            n2=shape(x.shape, F32), r2=column,
        ))
    outs = (tuple(shape(x.shape) for x in rows), shape((slots, local_heads, length, length)), tuple(kept))
    flat_out, out_tree = jax.tree.flatten(outs)
    flat_in, in_tree = jax.tree.flatten((rows, weights))
    small = (valid.astype(F32)[None], *norms[0], *norms[1])
    results = pl.pallas_call(
        functools.partial(forward_kernel, in_tree, out_tree),
        out_shape=flat_out,
        in_specs=[ANY] * len(flat_in) + [VMEM] * len(small),
        out_specs=[ANY] * len(flat_out),
        scratch_shapes=vmem_like(flat_in) + vmem_like(flat_out)
        + [pltpu.VMEM(x.shape, BF) for x in rows]
        + [pltpu.VMEM((2,) + x.shape, F32) for x in rows]
        + [pltpu.SemaphoreType.DMA((len(flat_in),)), pltpu.SemaphoreType.DMA((len(flat_out),))],
        compiler_params=BIG,
        name="layer_forward",
    )(*flat_in, *small)
    ys, probs, kept = jax.tree.unflatten(out_tree, results)
    return ys, (probs, kept)


def backward_kernel(in_tree, out_tree, *refs):
    n_in, n_out = in_tree.num_leaves, out_tree.num_leaves
    hbm_in, gains = refs[:n_in], refs[n_in : n_in + 2]
    hbm_out = refs[n_in + 2 : n_in + 2 + n_out]
    norm_sums = refs[n_in + 2 + n_out : n_in + 4 + n_out]
    rest = refs[n_in + 4 + n_out :]
    dctx, dz, (in_sem, out_sem) = rest[n_in + n_out :][0:2], rest[n_in + n_out :][2:4], rest[n_in + n_out :][4:]
    incoming = Staged(in_tree, hbm_in, rest[:n_in], in_sem, True)
    outgoing = Staged(out_tree, hbm_out, rest[n_in : n_in + n_out], out_sem, False)
    needed, probs_in = incoming.refs()
    needed_in, probs_copy = incoming.parts()
    back, back_out = outgoing.refs(), outgoing.parts()
    slots, length = needed[0].project.shape[0], needed[0].g.shape[0]
    local_heads = needed[0].project.shape[1] // (3 * HEAD_TEXT)
    incoming.start()
    for b in range(2):
        own, own_in, res, res_out, gain, sums = needed[b], needed_in[b], back[b], back_out[b], gains[b], norm_sums[b]
        wait(own_in.g, own_in.n2, own_in.r2)
        sums[...] = jnp.zeros(sums.shape, F32)
        for c in range(0, length, ROWS):
            rows = slice(c, c + ROWS)
            g, n = own.g[rows].astype(F32), own.n2[rows]
            low = norm_rows_back(g, n, own.r2[rows], gain[1:2])
            dz[b][rows] = low
            res.gf[rows] = low.astype(BF)
            sums[1:2] += jnp.sum(g * n, axis=0, keepdims=True)
            sums[3:4] += jnp.sum(g, axis=0, keepdims=True)
        start(res_out.gf)
        wait(own_in.downward, own_in.slope, own_in.upward)

        @pl.loop(0, slots)
        def _(t):
            for c in range(0, length, 2 * ROWS):
                rows = slice(c, c + 2 * ROWS)
                d_act = dot(res.gf[rows], own.downward[t], NT)
                d_pre = (d_act * own.slope[t, rows].astype(F32)).astype(BF)
                res.dpre[t, rows] = d_pre
                dz[b][rows] += dot(d_pre, own.upward[t], NT)

        start(res_out.dpre)
        wait(own_in.n1, own_in.r1)
        for c in range(0, length, ROWS):
            rows = slice(c, c + ROWS)
            g, n = dz[b][rows], own.n1[rows]
            low = norm_rows_back(g, n, own.r1[rows], gain[0:1])
            dz[b][rows] = low
            res.ga[rows] = low.astype(BF)
            sums[0:1] += jnp.sum(g * n, axis=0, keepdims=True)
            sums[2:3] += jnp.sum(g, axis=0, keepdims=True)
        start(res_out.ga)
        wait(own_in.outward)
        for t in range(slots):
            dctx[b][t] = dot(own.outward[t], res.ga[...], NT).astype(BF)
    wait(needed_in[0].qkv, needed_in[1].qkv, probs_copy)
    qkv, dqkv = (needed[0].qkv, needed[1].qkv), (back[0].dqkv, back[1].dqkv)
    text_rows, layout_rows = slice(0, HEAD_TEXT), slice(HEAD_TEXT, HEAD_TEXT + HEAD_LAYOUT)

    @pl.loop(0, slots)
    def _(t):
        for local in range(local_heads):
            dcT = jnp.concatenate(
                [dctx[b][t, local * SIZES[b] : (local + 1) * SIZES[b], :] for b in range(2)]
                + [jnp.zeros((128 - sum(SIZES), length), BF)], axis=0,
            )
            dc = dcT.T
            lane = lax.broadcasted_iota(jnp.int32, dc.shape, 1)
            dc_layout = jnp.where(lane >= HEAD_TEXT, dc, jnp.zeros_like(dc))
            qT, kT, vT = (head_rows(qkv, t, kind, local, SCALES if kind == 0 else None) for kind in range(3))
            low = probs_in[t, local]
            probs = low.astype(F32)
            both = dot(dc, vT)
            ds_both = (probs * (both - jnp.sum(probs * both, axis=-1, keepdims=True))).astype(BF)
            single = dot(dc_layout, vT)
            ds_layout = (probs * (single - jnp.sum(probs * single, axis=-1, keepdims=True))).astype(BF)
            dvT = dot(dcT, low)
            put_head(dqkv, t, 2, local, 0, dvT[text_rows])
            put_head(dqkv, t, 2, local, 1, dvT[layout_rows])
            put_head(dqkv, t, 0, local, 0, dot(kT[text_rows], ds_both, NT) * SCALES[0])
            put_head(dqkv, t, 1, local, 0, dot(qT[text_rows], ds_both))
            put_head(dqkv, t, 0, local, 1, dot(kT[layout_rows], ds_layout, NT) * SCALES[1])
            put_head(dqkv, t, 1, local, 1, dot(qT[layout_rows], ds_layout))

    start(back_out[0].dqkv, back_out[1].dqkv)
    for b in range(2):
        wait(needed_in[b].project)
        for t in range(slots):
            dz[b][...] += dot(dqkv[b][t].T, needed[b].project[t])
        back[b].dx[...] = dz[b][...].astype(BF)
        start(back_out[b].dx)
    outgoing.wait()


def layer_backward(saved, grads, weights, norms):
    probs, kept = saved
    needed, back = [], []
    for g, k, w in zip(grads, kept, weights):
        needed.append(Needed(
            g=g, n2=k.n2, r2=k.r2, downward=w.downward, slope=k.slope, upward=w.upward, n1=k.n1, r1=k.r1,
            outward=w.outward, qkv=k.qkv, project=w.project,
        ))
        rows = shape(g.shape)
        back.append(Back(dx=rows, dqkv=shape(k.qkv.shape), gf=rows, dpre=shape(k.slope.shape), ga=rows))
    flat_in, in_tree = jax.tree.flatten((tuple(needed), probs))
    flat_out, out_tree = jax.tree.flatten(tuple(back))
    results = pl.pallas_call(
        functools.partial(backward_kernel, in_tree, out_tree),
        out_shape=flat_out + [shape((4, g.shape[1]), F32) for g in grads],
        in_specs=[ANY] * len(flat_in) + [VMEM] * 2,
        out_specs=[ANY] * len(flat_out) + [VMEM] * 2,
        scratch_shapes=vmem_like(flat_in) + vmem_like(flat_out)
        + [pltpu.VMEM(k.ctx.shape, BF) for k in kept]
        + [pltpu.VMEM(g.shape, F32) for g in grads]
        + [pltpu.SemaphoreType.DMA((len(flat_in),)), pltpu.SemaphoreType.DMA((len(flat_out),))],
        compiler_params=BIG,
        name="layer_backward",
    )(*flat_in, norms[0][0], norms[1][0])
    return jax.tree.unflatten(out_tree, results[:-2]), tuple(results[-2:])


def mm(spec, a, b):
    return jnp.einsum(spec, a, b, preferred_element_type=F32)


def zeros_like_tree(shapes):
    return jax.tree.map(lambda s: jnp.zeros(s.shape, s.dtype), shapes)


def reduce_shard(grad, t, tensors):
    sibling = [(i, i + 1 - 2 * (i % 2)) for i in range(tensors)]
    partner = [(i, (i + tensors // 2) % tensors) for i in range(tensors)]
    pairs = grad.reshape((2, tensors // 2) + grad.shape[1:])
    core, chip = t % 2, t // 2
    theirs = lax.dynamic_index_in_dim(pairs, 1 - core, 1, keepdims=False)
    mine = lax.dynamic_index_in_dim(pairs, core, 1, keepdims=False)
    summed = (mine.astype(F32) + lax.ppermute(theirs, "tensor", sibling).astype(F32)).astype(BF)
    theirs = lax.dynamic_index_in_dim(summed, 1 - chip, 0, keepdims=False)
    mine = lax.dynamic_index_in_dim(summed, chip, 0, keepdims=False)
    summed = (mine.astype(F32) + lax.ppermute(theirs, "tensor", partner).astype(F32)).astype(BF)
    return lax.psum(summed, "dp").astype(F32)


def per_device(
    mesh,
    text_input,
    layout_input,
    text_cotangent,
    layout_cotangent,
    page_counts,
    pad_mask,
    lang_ids,
    lang_table,
    text_project,
    text_outward,
    text_upward,
    text_downward,
    text_gains,
    text_biases,
    layout_project,
    layout_outward,
    layout_upward,
    layout_downward,
    layout_gains,
    layout_biases,
):
    section, t = lax.axis_index("section"), lax.axis_index("tensor")
    tensors = mesh.shape["tensor"]
    micro, page = t % 2, t // 2

    def flat(project):
        return jnp.transpose(project[0], (1, 2, 0)).reshape(-1, project.shape[1])

    own_ids = lax.dynamic_index_in_dim(lang_ids, section, 0, keepdims=False)
    groups = jnp.arange(lang_table.shape[0], dtype=jnp.int32)
    onehot = (own_ids[:, None] == groups[None, :]).astype(F32)
    lang_rows = jnp.dot(onehot, lang_table, precision=HIGH)
    embedded = (text_input[0].astype(F32) + lang_rows[:, None, :]).astype(BF)
    flipped = lambda block: jnp.transpose(block[0], (0, 2, 1))
    shards = (
        flat(text_project), text_outward[0], text_upward[0], text_downward[0],
        flat(layout_project), layout_outward[0], layout_upward[0], layout_downward[0],
    )
    text_page, layout_page, full = fetch(
        mesh, embedded, flipped(layout_input), text_cotangent[0], flipped(layout_cotangent), shards
    )
    weights = (Weights(*full[0:4]), Weights(*full[4:8]))
    norms = ((text_gains[0], text_biases[0]), (layout_gains[0], layout_biases[0]))
    counts = page_counts[micro, page]
    positions = jnp.arange(pad_mask.shape[2], dtype=jnp.int32)
    valid = (positions < counts) & ((pad_mask[micro, page] == 1) | (positions == 0))
    arrived = (text_page, layout_page.T)

    def run(rows):
        return (rows,) + layer_forward(rows, weights, norms, valid)

    shapes = jax.eval_shape(run, arrived)
    kept = lax.cond(section == 0, run, lambda rows: zeros_like_tree(shapes), arrived)
    hopped = tuple(lax.ppermute(block, "section", [(0, 1)]) for block in kept[1])
    rows, outs, saved = lax.cond(section == 1, lambda old, got: run(got), lambda old, got: old, kept, hopped)

    def back(grads):
        return layer_backward(saved, grads, weights, norms)

    back_shapes = jax.eval_shape(back, arrived)
    first = lax.cond(section == 1, back, lambda grads: zeros_like_tree(back_shapes), arrived)
    hopped = tuple(lax.ppermute(res.dx, "section", [(1, 0)]) for res in first[0])
    back_results, norm_grads = lax.cond(
        section == 0, lambda old, got: back(got), lambda old, got: old, first, hopped
    )
    downs = tuple(res.dx for res in back_results)
    grads = [
        (
            mm("tnl,ld->tnd", res.dqkv, rows[b]).astype(BF),
            mm("tnl,ld->tnd", saved[1][b].ctx, res.ga).astype(BF),
            mm("ld,tln->tdn", saved[1][b].low, res.dpre).astype(BF),
            mm("tln,ld->tnd", saved[1][b].act, res.gf).astype(BF),
        )
        for b, res in enumerate(back_results)
    ]
    final = tuple(jnp.where(section == 0, d, o) for d, o in zip(downs, outs))
    text_out, layout_out, text_grad, layout_grad = give_back(mesh, final[0], final[1].T)
    summed = [[reduce_shard(g, t, tensors) for g in per_stream] for per_stream in grads]

    own_group = lax.dynamic_index_in_dim(lang_ids[:, page], micro, 0, keepdims=False)
    page_sum = jnp.where(section == 0, jnp.sum(downs[0].astype(F32), axis=0), 0.0)
    lang_grad = (groups == own_group).astype(F32)[:, None] * page_sum[None, :]
    pick = (jnp.arange(2, dtype=jnp.int32) == section).astype(F32)[:, None, None]
    small = lax.psum(
        tuple(pick * member[None] for sums in norm_grads for member in (sums[0:2], sums[2:4])) + (lang_grad,),
        ("section", "dp", "tensor"),
    )

    def own_row(stacked):
        return lax.dynamic_slice_in_dim(stacked, section, 1, 0)

    def unflat(grad, like):
        return jnp.transpose(grad.reshape(like.shape[2], like.shape[3], like.shape[1]), (2, 0, 1))[None]

    unflip = lambda block: jnp.transpose(block, (0, 2, 1))[None]
    return (
        text_out[None], unflip(layout_out), text_grad[None], unflip(layout_grad), small[4],
        unflat(summed[0][0], text_project), summed[0][1][None], summed[0][2][None], summed[0][3][None],
        own_row(small[0]), own_row(small[1]),
        unflat(summed[1][0], layout_project), summed[1][1][None], summed[1][2][None], summed[1][3][None],
        own_row(small[2]), own_row(small[3]),
    )


def solution(mesh):
    tokens = P("section", "dp", "tensor", None)
    weight_specs = (
        P("section", None, None, "tensor"), P("section", "tensor", None), P("section", None, "tensor"),
        P("section", "tensor", None), P("section", None, None), P("section", None, None),
    )
    in_specs = (tokens,) * 4 + (P(None, "dp"), P(None, "dp", None), P(None, "dp"), P()) + weight_specs * 2
    out_specs = (tokens,) * 4 + (P(),) + weight_specs * 2
    return jax.shard_map(
        functools.partial(per_device, mesh), mesh=mesh, in_specs=in_specs, out_specs=out_specs, check_vma=False
    )
```

```python
import functools
import math
import typing

import jax
import jax.numpy as jnp
from jax import lax
from jax.experimental import pallas as pl
from jax.experimental.pallas import tpu as pltpu
from jax.sharding import PartitionSpec as P

HEAD_TEXT = 64
HEAD_LAYOUT = 16
EPSILON = 1e-05
NEGATIVE = -1e30
HIGH = lax.Precision.HIGHEST
MESH = pl.DeviceIdType.MESH
BF = jnp.bfloat16
F32 = jnp.float32
ANY = pl.BlockSpec(memory_space=pl.ANY)


def remote(src, dst, send, recv, device):
    return pltpu.make_async_remote_copy(
        src_ref=src, dst_ref=dst, send_sem=send, recv_sem=recv, device_id=device, device_id_type=MESH
    )


def greet(section, tensor, sections, tensors, extra=()):
    barrier = pltpu.get_barrier_semaphore()
    for g in range(sections):
        for q in range(tensors):

            @pl.when((section != g) | (tensor != q))
            def _():
                pl.semaphore_signal(
                    barrier, inc=1, device_id={"section": g, "tensor": q}, device_id_type=MESH
                )

    for device in extra:
        pl.semaphore_signal(barrier, inc=1, device_id=device, device_id_type=MESH)
    pl.semaphore_wait(barrier, sections * tensors - 1 + len(extra))


def fetch_kernel(sections, tensors, dp, shared, *refs):
    n_weights = len(shared)
    sources = (refs[0:2], refs[2:4])
    weights = refs[4 : 4 + n_weights]
    pages = refs[4 + n_weights : 6 + n_weights]
    full = refs[6 + n_weights : 6 + 2 * n_weights]
    page_send, page_recv, w_send, w_recv, own_sem = refs[6 + 2 * n_weights :]
    section, d, t = lax.axis_index("section"), lax.axis_index("dp"), lax.axis_index("tensor")
    sibling = t + 1 - 2 * (t % 2)
    partner = (t + tensors // 2) % tensors
    mate = d + 1 - 2 * (d % 2)
    half = d % 2
    length = sources[0][0].shape[1]
    greet(section, t, sections, tensors, ({"dp": mate},))

    def part(ref, i, slot, which):
        if not shared[i]:
            return ref.at[slot]
        count = ref.shape[1] // 2
        return ref.at[slot, pl.ds(pl.multiple_of(which * count, 16), count)]

    def own_part(i):
        if not shared[i]:
            return weights[i]
        count = weights[i].shape[0] // 2
        return weights[i].at[pl.ds(pl.multiple_of(half * count, 16), count)]

    def token_slot(a, index):
        start = pl.multiple_of(index * length, length)
        return pages[a].at[pl.ds(start, length)] if a == 0 else pages[a].at[:, pl.ds(start, length)]

    def over_pages(g, act):
        for j in range(2):
            target = 2 * j + section
            here = (section == g) & (t == target)
            for a in range(2):
                act(g, j, a, target, here)

    def page_start(g, j, a, target, here):
        src, dst = sources[g][a].at[j], token_slot(a, t)

        @pl.when(here)
        def _():
            pltpu.make_async_copy(src, dst, page_recv.at[a, t]).start()

        @pl.when(jnp.logical_not(here))
        def _():
            remote(
                src, dst, page_send.at[g, j, a], page_recv.at[a, t], {"section": g, "tensor": target}
            ).start()

    def page_sent(g, j, a, target, here):
        @pl.when(jnp.logical_not(here))
        def _():
            remote(
                sources[g][a].at[j], token_slot(a, t), page_send.at[g, j, a], page_recv.at[a, t],
                {"section": g, "tensor": target},
            ).wait_send()

    over_pages(0, page_start)

    def to_partner(i):
        return remote(
            own_part(i), part(full[i], i, t, half), w_send.at[0, i], w_recv.at[0, i], {"tensor": partner}
        )

    def to_sibling(i):
        return remote(
            weights[i], full[i].at[t], w_send.at[1, i], w_recv.at[1, i], {"tensor": sibling}
        )

    def to_mate(i):
        ref = part(full[i], i, partner, half)
        return remote(ref, ref, w_send.at[2, i], w_recv.at[2, i], {"dp": mate})

    def on_first(i):
        ref = part(full[i], i, partner, half)
        return remote(ref, ref, w_send.at[3, i], w_recv.at[3, i], {"tensor": sibling})

    def on_second(i):
        ref = part(full[i], i, partner, 1 - half)
        return remote(ref, ref, w_send.at[4, i], w_recv.at[4, i], {"tensor": sibling})

    def keep(i):
        return pltpu.make_async_copy(weights[i], full[i].at[t], own_sem.at[i])

    to_partner(0).start()
    to_partner(1).start()
    for i in range(n_weights):
        to_sibling(i).start()
        keep(i).start()
    for i in range(n_weights):
        to_partner(i).wait()
        if i + 2 < n_weights:
            to_partner(i + 2).start()
        if shared[i]:
            to_mate(i).start()
        on_first(i).start()
    over_pages(1, page_start)
    for i in range(n_weights):
        if shared[i]:
            to_mate(i).wait_recv()
            on_second(i).start()
    for i in range(n_weights):
        keep(i).wait()
        to_sibling(i).wait()
        on_first(i).wait()
        if shared[i]:
            to_mate(i).wait_send()
            on_second(i).wait()
    for g in range(sections):
        over_pages(g, page_sent)
    for a in range(2):
        for q in range(tensors):
            slot = token_slot(a, q)
            remote(slot, slot, page_send.at[0, 0, a], page_recv.at[a, q], {"tensor": sibling}).wait_recv()


def fetch(mesh, text_in, layout_in, text_cot, layout_cot, weights):
    sections, dp, tensors = mesh.shape["section"], mesh.shape["dp"], mesh.shape["tensor"]
    length = text_in.shape[1] * tensors
    shared = tuple(dp % 2 == 0 and w.shape[0] >= 512 for w in weights)
    n = len(weights)
    shapes = (
        jax.ShapeDtypeStruct((length, text_in.shape[2]), BF),
        jax.ShapeDtypeStruct((layout_in.shape[1], length), BF),
    ) + tuple(jax.ShapeDtypeStruct((tensors,) + w.shape, BF) for w in weights)
    outs = pl.pallas_call(
        functools.partial(fetch_kernel, sections, tensors, dp, shared),
        out_shape=shapes,
        in_specs=[ANY] * (4 + n),
        out_specs=[ANY] * len(shapes),
        scratch_shapes=[
            pltpu.SemaphoreType.DMA((sections, 2, 2)),
            pltpu.SemaphoreType.DMA((2, tensors)),
            pltpu.SemaphoreType.DMA((5, n)),
            pltpu.SemaphoreType.DMA((5, n)),
            pltpu.SemaphoreType.DMA((n,)),
        ],
        compiler_params=pltpu.CompilerParams(collective_id=0, has_side_effects=True),
        name="fetch",
    )(text_in, layout_in, text_cot, layout_cot, *weights)
    return outs[0], outs[1], outs[2:]


GELU_P = 0.3275911
GELU_A = (0.254829592, -0.284496736, 1.421413741, -1.453152027, 1.061405429)
NN = (((1,), (0,)), ((), ()))
NT = (((1,), (1,)), ((), ()))
SCALES = (1.0 / math.sqrt(HEAD_TEXT), 1.0 / math.sqrt(HEAD_LAYOUT))
SIZES = (HEAD_TEXT, HEAD_LAYOUT)
ROWS = 128


class Weights(typing.NamedTuple):
    project: typing.Any
    outward: typing.Any
    upward: typing.Any
    downward: typing.Any


class Kept(typing.NamedTuple):
    qkv: typing.Any
    ctx: typing.Any
    n1: typing.Any
    r1: typing.Any
    low: typing.Any
    act: typing.Any
    slope: typing.Any
    n2: typing.Any
    r2: typing.Any


class Needed(typing.NamedTuple):
    g: typing.Any
    n2: typing.Any
    r2: typing.Any
    downward: typing.Any
    slope: typing.Any
    upward: typing.Any
    n1: typing.Any
    r1: typing.Any
    outward: typing.Any
    qkv: typing.Any
    project: typing.Any


class Back(typing.NamedTuple):
    dx: typing.Any
    dqkv: typing.Any
    gf: typing.Any
    dpre: typing.Any
    ga: typing.Any


def dot(a, b, dims=NN):
    return lax.dot_general(a, b, dims, preferred_element_type=F32)


def gelu_pair(u):
    t = 1.0 / (1.0 + (GELU_P / math.sqrt(2.0)) * jnp.abs(u))
    e = jnp.exp(-0.5 * (u * u))
    a1, a2, a3, a4, a5 = (0.5 * a for a in GELU_A)
    tail = ((((a5 * t + a4) * t + a3) * t + a2) * t + a1) * t * e
    cdf = jnp.where(u >= 0, 1.0 - tail, tail)
    return u * cdf, cdf + u * e * (1.0 / math.sqrt(2.0 * math.pi))


def norm_rows(z, gain, offset):
    center = z - jnp.mean(z, axis=-1, keepdims=True)
    inverse = lax.rsqrt(jnp.mean(center * center, axis=-1, keepdims=True) + EPSILON)
    normed = center * inverse
    return normed * gain + offset, normed, inverse


def norm_rows_back(g, n, r, gain):
    t = g * gain
    return r * (t - jnp.mean(t, axis=-1, keepdims=True) - n * jnp.mean(t * n, axis=-1, keepdims=True))


class Staged:
    def __init__(self, tree, hbm, vmem, sem, inward):
        self.tree, self.vmem = tree, list(vmem)
        pairs = zip(hbm, vmem) if inward else zip(vmem, hbm)
        self.copies = [pltpu.make_async_copy(a, b, sem.at[i]) for i, (a, b) in enumerate(pairs)]

    def refs(self):
        return jax.tree.unflatten(self.tree, self.vmem)

    def parts(self):
        return jax.tree.unflatten(self.tree, self.copies)

    def start(self):
        for copy in self.copies:
            copy.start()

    def wait(self):
        for copy in self.copies:
            copy.wait()


def start(*copies):
    for copy in copies:
        copy.start()


def wait(*copies):
    for copy in copies:
        copy.wait()


def head_rows(stacks, slot, kind, local, scales=None):
    rows = []
    for b in range(2):
        first = kind * (stacks[b].shape[1] // 3) + local * SIZES[b]
        piece = stacks[b][slot, first : first + SIZES[b], :]
        rows.append(piece if scales is None else piece * BF(scales[b]))
    rows.append(jnp.zeros((128 - sum(SIZES), rows[0].shape[1]), BF))
    return jnp.concatenate(rows, axis=0)


def put_head(stacks, slot, kind, local, b, value):
    first = kind * (stacks[b].shape[1] // 3) + local * SIZES[b]
    stacks[b][slot, first : first + SIZES[b], :] = value.astype(BF)


def forward_kernel(in_tree, out_tree, *refs):
    n_in, n_out = in_tree.num_leaves, out_tree.num_leaves
    hbm_in, (valid, *norms) = refs[:n_in], refs[n_in : n_in + 5]
    hbm_out = refs[n_in + 5 : n_in + 5 + n_out]
    rest = refs[n_in + 5 + n_out :]
    (*nats, total_t, total_l, in_sem, out_sem) = rest[n_in + n_out :]
    incoming = Staged(in_tree, hbm_in, rest[:n_in], in_sem, True)
    outgoing = Staged(out_tree, hbm_out, rest[n_in : n_in + n_out], out_sem, False)
    x, weights = incoming.refs()
    x_in, weights_in = incoming.parts()
    y, probs_out, kept = outgoing.refs()
    y_out, probs_copy, kept_out = outgoing.parts()
    slots, length = weights[0].project.shape[0], x[0].shape[0]
    local_heads = weights[0].project.shape[1] // (3 * HEAD_TEXT)
    incoming.start()
    wait(*x_in, weights_in[0].project, weights_in[1].project)
    qkv = (kept[0].qkv, kept[1].qkv)

    @pl.loop(0, slots)
    def _(t):
        for b in range(2):
            qkv[b][t] = dot(weights[b].project[t], x[b][...], NT).astype(BF)

    start(kept_out[0].qkv, kept_out[1].qkv)
    key_mask = valid[...] > 0

    @pl.loop(0, slots)
    def _(t):
        for local in range(local_heads):
            q = head_rows(qkv, t, 0, local, SCALES).T
            scores = jnp.where(key_mask, dot(q, head_rows(qkv, t, 1, local)), NEGATIVE)
            raised = jnp.exp(scores - jnp.max(scores, axis=-1, keepdims=True))
            probs = (raised * (1.0 / jnp.sum(raised, axis=-1, keepdims=True))).astype(BF)
            probs_out[t, local] = probs
            ctx = dot(head_rows(qkv, t, 2, local), probs, NT).astype(BF)
            kept[0].ctx[t, local * HEAD_TEXT : (local + 1) * HEAD_TEXT, :] = ctx[:HEAD_TEXT]
            kept[1].ctx[t, local * HEAD_LAYOUT : (local + 1) * HEAD_LAYOUT, :] = ctx[
                HEAD_TEXT : HEAD_TEXT + HEAD_LAYOUT
            ]

    start(probs_copy, kept_out[0].ctx, kept_out[1].ctx)
    for b, total in enumerate((total_t, total_l)):
        gains, biases = norms[2 * b : 2 * b + 2]
        width = x[b].shape[1]
        hidden, fed = total.at[0], total.at[1]
        own, own_out, nat = kept[b], kept_out[b], nats[b]
        nat[...] = own.ctx[...].reshape(width, length).T
        wait(weights_in[b].outward)
        wide = weights[b].outward[...].reshape(width, width)
        for c in range(0, length, ROWS):
            rows = slice(c, c + ROWS)
            h, n, r = norm_rows(x[b][rows].astype(F32) + dot(nat[rows], wide), gains[0:1], biases[0:1])
            hidden[rows] = h
            own.n1[rows] = n
            own.r1[rows] = r
            own.low[rows] = h.astype(BF)
        start(own_out.n1, own_out.r1, own_out.low)
        wait(weights_in[b].upward, weights_in[b].downward)
        fed[...] = jnp.zeros((length, width), F32)

        @pl.loop(0, slots)
        def _(t):
            for c in range(0, length, 2 * ROWS):
                rows = slice(c, c + 2 * ROWS)
                act, slope = gelu_pair(dot(own.low[rows], weights[b].upward[t]))
                act = act.astype(BF)
                own.act[t, rows] = act
                own.slope[t, rows] = slope.astype(BF)
                fed[rows] += dot(act, weights[b].downward[t])

        start(own_out.act, own_out.slope)
        for c in range(0, length, ROWS):
            rows = slice(c, c + ROWS)
            out, n, r = norm_rows(hidden[rows] + fed[rows], gains[1:2], biases[1:2])
            y[b][rows] = out.astype(BF)
            own.n2[rows] = n
            own.r2[rows] = r
        start(y_out[b], own_out.n2, own_out.r2)
    outgoing.wait()


def vmem_like(tree):
    return [pltpu.VMEM(s.shape, s.dtype) for s in jax.tree.leaves(tree)]


VMEM = pl.BlockSpec(memory_space=pltpu.VMEM)
BIG = pltpu.CompilerParams(vmem_limit_bytes=60 << 20)


def shape(dims, dtype=BF):
    return jax.ShapeDtypeStruct(tuple(dims), dtype)


def layer_forward(rows, weights, norms, valid):
    length = rows[0].shape[0]
    slots, local_heads = weights[0].project.shape[0], weights[0].project.shape[1] // (3 * HEAD_TEXT)
    kept = []
    for x, w in zip(rows, weights):
        units, column = shape((slots, length, w.upward.shape[2])), shape((length, 1), F32)
        kept.append(Kept(
            qkv=shape((slots, w.project.shape[1], length)), ctx=shape((slots, w.outward.shape[1], length)),
            n1=shape(x.shape, F32), r1=column, low=shape(x.shape), act=units, slope=units,
            n2=shape(x.shape, F32), r2=column,
        ))
    outs = (tuple(shape(x.shape) for x in rows), shape((slots, local_heads, length, length)), tuple(kept))
    flat_out, out_tree = jax.tree.flatten(outs)
    flat_in, in_tree = jax.tree.flatten((rows, weights))
    small = (valid.astype(F32)[None], *norms[0], *norms[1])
    results = pl.pallas_call(
        functools.partial(forward_kernel, in_tree, out_tree),
        out_shape=flat_out,
        in_specs=[ANY] * len(flat_in) + [VMEM] * len(small),
        out_specs=[ANY] * len(flat_out),
        scratch_shapes=vmem_like(flat_in) + vmem_like(flat_out)
        + [pltpu.VMEM(x.shape, BF) for x in rows]
        + [pltpu.VMEM((2,) + x.shape, F32) for x in rows]
        + [pltpu.SemaphoreType.DMA((len(flat_in),)), pltpu.SemaphoreType.DMA((len(flat_out),))],
        compiler_params=BIG,
        name="layer_forward",
    )(*flat_in, *small)
    ys, probs, kept = jax.tree.unflatten(out_tree, results)
    return ys, (probs, kept)


def backward_kernel(in_tree, out_tree, *refs):
    n_in, n_out = in_tree.num_leaves, out_tree.num_leaves
    hbm_in, gains = refs[:n_in], refs[n_in : n_in + 2]
    hbm_out = refs[n_in + 2 : n_in + 2 + n_out]
    norm_sums = refs[n_in + 2 + n_out : n_in + 4 + n_out]
    rest = refs[n_in + 4 + n_out :]
    dctx, dz, (in_sem, out_sem) = rest[n_in + n_out :][0:2], rest[n_in + n_out :][2:4], rest[n_in + n_out :][4:]
    incoming = Staged(in_tree, hbm_in, rest[:n_in], in_sem, True)
    outgoing = Staged(out_tree, hbm_out, rest[n_in : n_in + n_out], out_sem, False)
    needed, probs_in = incoming.refs()
    needed_in, probs_copy = incoming.parts()
    back, back_out = outgoing.refs(), outgoing.parts()
    slots, length = needed[0].project.shape[0], needed[0].g.shape[0]
    local_heads = needed[0].project.shape[1] // (3 * HEAD_TEXT)
    incoming.start()
    for b in range(2):
        own, own_in, res, res_out, gain, sums = needed[b], needed_in[b], back[b], back_out[b], gains[b], norm_sums[b]
        wait(own_in.g, own_in.n2, own_in.r2)
        sums[...] = jnp.zeros(sums.shape, F32)
        for c in range(0, length, ROWS):
            rows = slice(c, c + ROWS)
            g, n = own.g[rows].astype(F32), own.n2[rows]
            low = norm_rows_back(g, n, own.r2[rows], gain[1:2])
            dz[b][rows] = low
            res.gf[rows] = low.astype(BF)
            sums[1:2] += jnp.sum(g * n, axis=0, keepdims=True)
            sums[3:4] += jnp.sum(g, axis=0, keepdims=True)
        start(res_out.gf)
        wait(own_in.downward, own_in.slope, own_in.upward)

        @pl.loop(0, slots)
        def _(t):
            for c in range(0, length, 2 * ROWS):
                rows = slice(c, c + 2 * ROWS)
                d_act = dot(res.gf[rows], own.downward[t], NT)
                d_pre = (d_act * own.slope[t, rows].astype(F32)).astype(BF)
                res.dpre[t, rows] = d_pre
                dz[b][rows] += dot(d_pre, own.upward[t], NT)

        start(res_out.dpre)
        wait(own_in.n1, own_in.r1)
        for c in range(0, length, ROWS):
            rows = slice(c, c + ROWS)
            g, n = dz[b][rows], own.n1[rows]
            low = norm_rows_back(g, n, own.r1[rows], gain[0:1])
            dz[b][rows] = low
            res.ga[rows] = low.astype(BF)
            sums[0:1] += jnp.sum(g * n, axis=0, keepdims=True)
            sums[2:3] += jnp.sum(g, axis=0, keepdims=True)
        start(res_out.ga)
        wait(own_in.outward)
        for t in range(slots):
            dctx[b][t] = dot(own.outward[t], res.ga[...], NT).astype(BF)
    wait(needed_in[0].qkv, needed_in[1].qkv, probs_copy)
    qkv, dqkv = (needed[0].qkv, needed[1].qkv), (back[0].dqkv, back[1].dqkv)
    text_rows, layout_rows = slice(0, HEAD_TEXT), slice(HEAD_TEXT, HEAD_TEXT + HEAD_LAYOUT)

    @pl.loop(0, slots)
    def _(t):
        for local in range(local_heads):
            dcT = jnp.concatenate(
                [dctx[b][t, local * SIZES[b] : (local + 1) * SIZES[b], :] for b in range(2)]
                + [jnp.zeros((128 - sum(SIZES), length), BF)], axis=0,
            )
            dc = dcT.T
            lane = lax.broadcasted_iota(jnp.int32, dc.shape, 1)
            dc_layout = jnp.where(lane >= HEAD_TEXT, dc, jnp.zeros_like(dc))
            qT, kT, vT = (head_rows(qkv, t, kind, local, SCALES if kind == 0 else None) for kind in range(3))
            low = probs_in[t, local]
            probs = low.astype(F32)
            both = dot(dc, vT)
            ds_both = (probs * (both - jnp.sum(probs * both, axis=-1, keepdims=True))).astype(BF)
            single = dot(dc_layout, vT)
            ds_layout = (probs * (single - jnp.sum(probs * single, axis=-1, keepdims=True))).astype(BF)
            dvT = dot(dcT, low)
            put_head(dqkv, t, 2, local, 0, dvT[text_rows])
            put_head(dqkv, t, 2, local, 1, dvT[layout_rows])
            put_head(dqkv, t, 0, local, 0, dot(kT[text_rows], ds_both, NT) * SCALES[0])
            put_head(dqkv, t, 1, local, 0, dot(qT[text_rows], ds_both))
            put_head(dqkv, t, 0, local, 1, dot(kT[layout_rows], ds_layout, NT) * SCALES[1])
            put_head(dqkv, t, 1, local, 1, dot(qT[layout_rows], ds_layout))

    start(back_out[0].dqkv, back_out[1].dqkv)
    for b in range(2):
        wait(needed_in[b].project)
        for t in range(slots):
            dz[b][...] += dot(dqkv[b][t].T, needed[b].project[t])
        back[b].dx[...] = dz[b][...].astype(BF)
        start(back_out[b].dx)
    outgoing.wait()


def layer_backward(saved, grads, weights, norms):
    probs, kept = saved
    needed, back = [], []
    for g, k, w in zip(grads, kept, weights):
        needed.append(Needed(
            g=g, n2=k.n2, r2=k.r2, downward=w.downward, slope=k.slope, upward=w.upward, n1=k.n1, r1=k.r1,
            outward=w.outward, qkv=k.qkv, project=w.project,
        ))
        rows = shape(g.shape)
        back.append(Back(dx=rows, dqkv=shape(k.qkv.shape), gf=rows, dpre=shape(k.slope.shape), ga=rows))
    flat_in, in_tree = jax.tree.flatten((tuple(needed), probs))
    flat_out, out_tree = jax.tree.flatten(tuple(back))
    results = pl.pallas_call(
        functools.partial(backward_kernel, in_tree, out_tree),
        out_shape=flat_out + [shape((4, g.shape[1]), F32) for g in grads],
        in_specs=[ANY] * len(flat_in) + [VMEM] * 2,
        out_specs=[ANY] * len(flat_out) + [VMEM] * 2,
        scratch_shapes=vmem_like(flat_in) + vmem_like(flat_out)
        + [pltpu.VMEM(k.ctx.shape, BF) for k in kept]
        + [pltpu.VMEM(g.shape, F32) for g in grads]
        + [pltpu.SemaphoreType.DMA((len(flat_in),)), pltpu.SemaphoreType.DMA((len(flat_out),))],
        compiler_params=BIG,
        name="layer_backward",
    )(*flat_in, norms[0][0], norms[1][0])
    return jax.tree.unflatten(out_tree, results[:-2]), tuple(results[-2:])


def zeros_like_tree(shapes):
    return jax.tree.map(lambda s: jnp.zeros(s.shape, s.dtype), shapes)


class Operands(typing.NamedTuple):
    act: typing.Any
    gf: typing.Any
    low: typing.Any
    dpre: typing.Any
    x: typing.Any
    dqkv: typing.Any
    ctx: typing.Any
    ga: typing.Any


def gradient_rows(own):
    return own.dqkv.shape[1], own.ctx.shape[1], own.low.shape[1], own.act.shape[2]


def gradient_block(own, lowT, slot, which, first, rows):
    if which == 0:
        return dot(own.dqkv[slot, first : first + rows, :], own.x[...])
    if which == 1:
        return dot(own.ctx[slot, first : first + rows, :], own.ga[...])
    if which == 2:
        return dot(lowT[first : first + rows, :], own.dpre[slot])
    return dot(own.act[slot, :, first : first + rows].T, own.gf[...])


def chunks_of(own, step):
    sizes = gradient_rows(own)
    starts = [sum(sizes[:i]) for i in range(4)]
    chunks = []
    for which in (3, 2, 0, 1):
        size = sizes[which]
        piece = next(p for p in (step, 192, size) if size % p == 0)
        chunks += [(starts[which] + f, piece, ((which, f, piece),)) for f in range(0, size, piece)]
    return chunks


def whole_chunk(own):
    sizes = gradient_rows(own)
    return (0, sum(sizes), tuple((which, 0, sizes[which]) for which in range(4)))


def reduce_kernel(sections, tensors, chain, in_tree, *refs):
    n_in = in_tree.num_leaves
    hbm_in = refs[:n_in]
    dx_t, dx_l, y_t, y_l, small_in = refs[n_in : n_in + 5]
    results = refs[n_in + 5 : n_in + 7]
    small_out, text_out, layout_out, grad_out, layout_grad_out = refs[n_in + 7 : n_in + 12]
    rest = refs[n_in + 12 :]
    operands = Staged(in_tree, hbm_in, rest[:n_in], rest[n_in], True)
    lowT, raw, from_sibling, from_partner, near_in, cross_in, total = (
        rest[n_in + 1 + 2 * i : n_in + 3 + 2 * i] for i in range(7)
    )
    small_got, small_sum, send, recv, out_sem, small_send, small_recv, page_send, page_recv = rest[n_in + 15 :]
    section, d, t = lax.axis_index("section"), lax.axis_index("dp"), lax.axis_index("tensor")
    core, chip = t % 2, t // 2
    sibling = {"tensor": t + 1 - 2 * core}
    partner = {"tensor": (t + tensors // 2) % tensors}
    near, cross = {"dp": d + 1 - 2 * (d % 2)}, {"dp": 3 - d}
    outer = (d == 0) | (d == 3)
    operands.start()
    greet(section, t, sections, tensors, (near, cross) if chain else ())

    length = text_out.shape[1]
    micro, page = t % 2, t // 2
    kinds = ((grad_out, layout_grad_out), (text_out, layout_out))
    pages = ((dx_t, dx_l), (y_t, y_l))

    def page_part(g, q, a):
        return pages[g][a].at[pl.ds(q * length, length)] if a == 0 else pages[g][a].at[:, pl.ds(q * length, length)]

    def each_page(act):
        for g in range(sections):
            for q in range(tensors):
                for a in range(2):
                    here = (micro == g) & (t == q)

                    @pl.when((section == g) & here)
                    def _():
                        act(g, q, a, True)

                    @pl.when((section == g) & jnp.logical_not(here))
                    def _():
                        act(g, q, a, False)

    def page_copy(g, q, a):
        return remote(
            page_part(g, q, a), kinds[g][a].at[page], page_send.at[q, a], page_recv.at[g, a, page],
            {"section": micro, "tensor": q},
        )

    def page_start(g, q, a, here):
        if here:
            pltpu.make_async_copy(page_part(g, q, a), kinds[g][a].at[page], page_recv.at[g, a, page]).start()
        else:
            page_copy(g, q, a).start()

    def page_sent(g, q, a, here):
        if not here:
            page_copy(g, q, a).wait_send()

    each_page(page_start)

    def small_copy(i, device):
        return remote(small_sum.at[i], small_got.at[i], small_send.at[i], small_recv.at[i], device)

    small_sum[0] = small_in[...]
    if chain:
        small_copy(0, sibling).start()

    own, own_in = operands.refs(), operands.parts()
    work = [(1,) + whole_chunk(own[1])] + [(0,) + c for c in chunks_of(own[0], 256)]
    for b in range(2):
        wait(own_in[b].low)
        lowT[b][...] = own[b].low[...].T
    for b in (1, 0):
        wait(*(part for part in own_in[b] if part is not own_in[b].low))

    def span(ref, k):
        return ref.at[pl.ds(work[k][1], work[k][2])]

    def spans(ref, k):
        return ref.at[:, pl.ds(work[k][1], work[k][2])]

    def to_sibling(k):
        b = work[k][0]
        return remote(
            spans(raw[b].at[1 - core], k), spans(from_sibling[b], k), send.at[0, k], recv.at[0, k], sibling
        )

    def to_partner(k):
        b = work[k][0]
        return remote(
            span(raw[b].at[core, 1 - chip], k), span(from_partner[b], k), send.at[1, k], recv.at[1, k], partner
        )

    def to_near(k):
        b = work[k][0]
        return remote(span(raw[b].at[core, chip], k), span(near_in[b], k), send.at[2, k], recv.at[2, k], near)

    def total_to_near(k):
        b = work[k][0]
        return remote(span(total[b], k), span(near_in[b], k), send.at[2, k], recv.at[2, k], near)

    def to_cross(k):
        b = work[k][0]
        return remote(span(raw[b].at[core, chip], k), span(cross_in[b], k), send.at[3, k], recv.at[3, k], cross)

    def out_copy(k, source):
        b = work[k][0]
        return pltpu.make_async_copy(span(source, k), span(results[b], k), out_sem.at[k])

    def added(target, *sources):
        target[...] = sum(s[...].astype(F32) for s in sources).astype(BF)

    def stage_product(k):
        b, first, rows, pieces = work[k]
        for slot in range(tensors):
            at = first
            for which, begin, count in pieces:
                raw[b][slot % 2, slot // 2, at : at + count, :] = gradient_block(
                    own[b], lowT[b], slot, which, begin, count
                ).astype(BF)
                at += count
        to_sibling(k).start()

    def stage_sibling(k):
        b = work[k][0]
        to_sibling(k).wait_recv()
        mine = raw[b].at[core, 1 - chip]
        added(span(mine, k), span(mine, k), span(from_sibling[b].at[1 - chip], k))
        to_partner(k).start()
        mine = raw[b].at[core, chip]
        added(span(mine, k), span(mine, k), span(from_sibling[b].at[chip], k))

    def stage_partner(k):
        b = work[k][0]
        to_partner(k).wait_recv()
        mine = span(raw[b].at[core, chip], k)
        added(mine, mine, span(from_partner[b], k))
        if not chain:
            out_copy(k, raw[b].at[core, chip]).start()
            return

        @pl.when(outer)
        def _():
            to_near(k).start()

    def stage_near(k):
        b = work[k][0]

        @pl.when(jnp.logical_not(outer))
        def _():
            to_near(k).wait_recv()
            mine = span(raw[b].at[core, chip], k)
            added(mine, mine, span(near_in[b], k))
            to_cross(k).start()

    def stage_cross(k):
        b = work[k][0]

        @pl.when(jnp.logical_not(outer))
        def _():
            to_cross(k).wait_recv()
            added(span(total[b], k), span(raw[b].at[core, chip], k), span(cross_in[b], k))
            total_to_near(k).start()
            out_copy(k, total[b]).start()

    def stage_total(k):
        b = work[k][0]

        @pl.when(outer)
        def _():
            to_near(k).wait_recv()
            out_copy(k, near_in[b]).start()

    stages = [stage_product, stage_sibling, stage_partner]
    if chain:
        stages += [stage_near, stage_cross, stage_total]
    for step in range(len(work) + len(stages) - 1):
        for lag, stage in enumerate(stages):
            if 0 <= step - lag < len(work):
                stage(step - lag)
        if not chain:
            continue
        if step == 0:
            small_copy(0, sibling).wait_recv()
            small_sum[1] = small_sum[0] + small_got[0]
            small_copy(1, partner).start()
        if step == 1:
            small_copy(1, partner).wait_recv()
            small_sum[2] = small_sum[1] + small_got[1]
            small_copy(2, near).start()
        if step == 2:
            small_copy(2, near).wait_recv()
            small_sum[3] = small_sum[2] + small_got[2]

            @pl.when(jnp.logical_not(outer))
            def _():
                small_copy(3, cross).start()

        if step == 4:
            @pl.when(jnp.logical_not(outer))
            def _():
                small_copy(3, cross).wait_recv()
                small_sum[4] = small_sum[3] + small_got[3]
                small_copy(4, near).start()

        if step == 6:
            @pl.when(outer)
            def _():
                small_copy(4, near).wait_recv()
                small_sum[4] = small_got[4]

            small_sum[5] = small_sum[4]
            small_copy(5, {"section": 1 - section}).start()
        if step == 8:
            small_copy(5, {"section": 1 - section}).wait_recv()
            small_out[0] = small_sum[5]
            small_out[1] = small_got[5]

    if chain:
        for i, device in enumerate((sibling, partner, near)):
            small_copy(i, device).wait_send()

        @pl.when(jnp.logical_not(outer))
        def _():
            small_copy(3, cross).wait_send()
            small_copy(4, near).wait_send()

        small_copy(5, {"section": 1 - section}).wait_send()
    else:
        small_out[0] = small_in[...]
        small_out[1] = small_in[...]
    for k in range(len(work)):
        to_sibling(k).wait_send()
        to_partner(k).wait_send()
        b = work[k][0]
        if chain:
            to_near(k).wait_send()

            @pl.when(jnp.logical_not(outer))
            def _():
                to_cross(k).wait_send()

        out_copy(k, total[b]).wait()
    each_page(page_sent)
    for g in range(sections):
        for a in range(2):
            for j in range(2):
                dst = kinds[g][a].at[j]
                remote(dst, dst, page_send.at[0, a], page_recv.at[g, a, j], partner).wait_recv()


def reduce_all(mesh, operands, dx, y, small):
    sections, dp, tensors = mesh.shape["section"], mesh.shape["dp"], mesh.shape["tensor"]
    chain = dp == 4
    flat_in, in_tree = jax.tree.flatten(operands)
    length = dx[0].shape[0] // tensors
    rows = [sum(gradient_rows(own)) for own in operands]
    widths = [own.x.shape[1] for own in operands]
    n_chunks = 1 + len(chunks_of(operands[0], 256))
    text_shape, layout_shape = shape((2, length, widths[0])), shape((2, widths[1], length))
    big = [pltpu.VMEM((r, w), BF) for r, w in zip(rows, widths)]
    scratch = [pltpu.VMEM(x.shape, x.dtype) for x in flat_in] + [pltpu.SemaphoreType.DMA((len(flat_in),))]
    scratch += [pltpu.VMEM((own.low.shape[1], own.low.shape[0]), BF) for own in operands]
    scratch += [pltpu.VMEM((2, tensors // 2, r, w), BF) for r, w in zip(rows, widths)]
    scratch += [pltpu.VMEM((tensors // 2, r, w), BF) for r, w in zip(rows, widths)]
    scratch += big * 4
    scratch += [pltpu.VMEM((6,) + small.shape, F32)] * 2
    scratch += [pltpu.SemaphoreType.DMA((4, n_chunks))] * 2 + [pltpu.SemaphoreType.DMA((n_chunks,))]
    scratch += [pltpu.SemaphoreType.DMA((6,))] * 2
    scratch += [pltpu.SemaphoreType.DMA((tensors, 2)), pltpu.SemaphoreType.DMA((sections, 2, 2))]
    total_t, total_l, small, *pages = pl.pallas_call(
        functools.partial(reduce_kernel, sections, tensors, chain, in_tree),
        out_shape=[shape((r, w)) for r, w in zip(rows, widths)]
        + [shape((2,) + small.shape, F32), text_shape, layout_shape, text_shape, layout_shape],
        in_specs=[ANY] * (len(flat_in) + 4) + [VMEM],
        out_specs=[ANY] * 2 + [VMEM] + [ANY] * 4,
        scratch_shapes=scratch,
        compiler_params=pltpu.CompilerParams(
            collective_id=1, has_side_effects=True, vmem_limit_bytes=62 << 20
        ),
        name="reduce_all",
    )(*flat_in, dx[0], dx[1].T, y[0], y[1].T, small)
    if not chain:
        total_t, total_l = lax.psum((total_t, total_l), "dp")
        both = lax.psum(small[0], ("dp", "tensor"))
        small = jnp.stack([both, lax.ppermute(both, "section", [(0, 1), (1, 0)])])
    return (total_t, total_l), small, pages


def per_device(
    mesh,
    text_input,
    layout_input,
    text_cotangent,
    layout_cotangent,
    page_counts,
    pad_mask,
    lang_ids,
    lang_table,
    text_project,
    text_outward,
    text_upward,
    text_downward,
    text_gains,
    text_biases,
    layout_project,
    layout_outward,
    layout_upward,
    layout_downward,
    layout_gains,
    layout_biases,
):
    section, t = lax.axis_index("section"), lax.axis_index("tensor")
    tensors = mesh.shape["tensor"]
    micro, page = t % 2, t // 2

    def flat(project):
        return jnp.transpose(project[0], (1, 2, 0)).reshape(-1, project.shape[1])

    own_ids = lax.dynamic_index_in_dim(lang_ids, section, 0, keepdims=False)
    groups = jnp.arange(lang_table.shape[0], dtype=jnp.int32)
    onehot = (own_ids[:, None] == groups[None, :]).astype(F32)
    lang_rows = jnp.dot(onehot, lang_table, precision=HIGH)
    embedded = (text_input[0].astype(F32) + lang_rows[:, None, :]).astype(BF)
    flipped = lambda block: jnp.transpose(block[0], (0, 2, 1))
    shards = (
        flat(text_project), text_outward[0], text_upward[0], text_downward[0],
        flat(layout_project), layout_outward[0], layout_upward[0], layout_downward[0],
    )
    text_page, layout_page, full = fetch(
        mesh, embedded, flipped(layout_input), text_cotangent[0], flipped(layout_cotangent), shards
    )
    weights = (Weights(*full[0:4]), Weights(*full[4:8]))
    norms = ((text_gains[0], text_biases[0]), (layout_gains[0], layout_biases[0]))
    counts = page_counts[micro, page]
    positions = jnp.arange(pad_mask.shape[2], dtype=jnp.int32)
    valid = (positions < counts) & ((pad_mask[micro, page] == 1) | (positions == 0))
    arrived = (text_page, layout_page.T)

    def run(rows):
        return (rows,) + layer_forward(rows, weights, norms, valid)

    shapes = jax.eval_shape(run, arrived)
    kept = lax.cond(section == 0, run, lambda rows: zeros_like_tree(shapes), arrived)
    hopped = tuple(lax.ppermute(block, "section", [(0, 1)]) for block in kept[1])
    rows, outs, saved = lax.cond(section == 1, lambda old, got: run(got), lambda old, got: old, kept, hopped)

    def back(grads):
        return layer_backward(saved, grads, weights, norms)

    back_shapes = jax.eval_shape(back, arrived)
    first = lax.cond(section == 1, back, lambda grads: zeros_like_tree(back_shapes), arrived)
    hopped = tuple(lax.ppermute(res.dx, "section", [(1, 0)]) for res in first[0])
    back_results, norm_grads = lax.cond(
        section == 0, lambda old, got: back(got), lambda old, got: old, first, hopped
    )
    downs = tuple(res.dx for res in back_results)
    operands = tuple(
        Operands(act=k.act, gf=res.gf, low=k.low, dpre=res.dpre, x=x, dqkv=res.dqkv, ctx=k.ctx, ga=res.ga)
        for x, k, res in zip(rows, saved[1], back_results)
    )
    own_group = lax.dynamic_index_in_dim(lang_ids[:, page], micro, 0, keepdims=False)
    page_sum = jnp.where(section == 0, jnp.sum(downs[0].astype(F32), axis=0), 0.0)
    lang_grad = (groups == own_group).astype(F32)[:, None] * page_sum[None, :]
    wide = text_gains.shape[-1]
    small = jnp.concatenate(
        [lang_grad, norm_grads[0], jnp.pad(norm_grads[1], ((0, 0), (0, wide - norm_grads[1].shape[1])))]
    )
    totals, small, (text_out, layout_out, text_grad, layout_grad) = reduce_all(mesh, operands, downs, outs, small)
    n_lang = lang_table.shape[0]
    lang_sum = jnp.where(section == 0, small[0, :n_lang], small[1, :n_lang])
    norm_sums = (small[0, n_lang : n_lang + 4], small[0, n_lang + 4 : n_lang + 8, : layout_gains.shape[-1]])
    summed = []
    for total, own in zip(totals, operands):
        sizes = gradient_rows(own)
        starts = [sum(sizes[:i]) for i in range(4)]
        summed.append([total[s : s + n].astype(F32) for s, n in zip(starts, sizes)])

    def unflat(grad, like):
        return jnp.transpose(grad.reshape(like.shape[2], like.shape[3], like.shape[1]), (2, 0, 1))[None]

    unflip = lambda block: jnp.transpose(block, (0, 2, 1))[None]
    return (
        text_out[None], unflip(layout_out), text_grad[None], unflip(layout_grad), lang_sum,
        unflat(summed[0][0], text_project), summed[0][1][None], summed[0][2][None], summed[0][3][None],
        norm_sums[0][None, 0:2], norm_sums[0][None, 2:4],
        unflat(summed[1][0], layout_project), summed[1][1][None], summed[1][2][None], summed[1][3][None],
        norm_sums[1][None, 0:2], norm_sums[1][None, 2:4],
    )


def solution(mesh):
    tokens = P("section", "dp", "tensor", None)
    weight_specs = (
        P("section", None, None, "tensor"), P("section", "tensor", None), P("section", None, "tensor"),
        P("section", "tensor", None), P("section", None, None), P("section", None, None),
    )
    in_specs = (tokens,) * 4 + (P(None, "dp"), P(None, "dp", None), P(None, "dp"), P()) + weight_specs * 2
    out_specs = (tokens,) * 4 + (P(),) + weight_specs * 2
    return jax.shard_map(
        functools.partial(per_device, mesh), mesh=mesh, in_specs=in_specs, out_specs=out_specs, check_vma=False
    )
```

```python
import functools
import math
import typing

import jax
import jax.numpy as jnp
from jax import lax
from jax.experimental import pallas as pl
from jax.experimental.pallas import tpu as pltpu
from jax.sharding import PartitionSpec as P

HEAD_TEXT = 64
HEAD_LAYOUT = 16
EPSILON = 1e-05
NEGATIVE = -1e30
HIGH = lax.Precision.HIGHEST
MESH = pl.DeviceIdType.MESH
BF = jnp.bfloat16
F32 = jnp.float32
ANY = pl.BlockSpec(memory_space=pl.ANY)


def remote(src, dst, send, recv, device):
    return pltpu.make_async_remote_copy(
        src_ref=src, dst_ref=dst, send_sem=send, recv_sem=recv, device_id=device, device_id_type=MESH
    )


def greet(section, tensor, sections, tensors, extra=()):
    barrier = pltpu.get_barrier_semaphore()
    for g in range(sections):
        for q in range(tensors):

            @pl.when((section != g) | (tensor != q))
            def _():
                pl.semaphore_signal(
                    barrier, inc=1, device_id={"section": g, "tensor": q}, device_id_type=MESH
                )

    for device in extra:
        pl.semaphore_signal(barrier, inc=1, device_id=device, device_id_type=MESH)
    pl.semaphore_wait(barrier, sections * tensors - 1 + len(extra))


GELU_P = 0.3275911
GELU_A = (0.254829592, -0.284496736, 1.421413741, -1.453152027, 1.061405429)
NN = (((1,), (0,)), ((), ()))
NT = (((1,), (1,)), ((), ()))
SCALES = (1.0 / math.sqrt(HEAD_TEXT), 1.0 / math.sqrt(HEAD_LAYOUT))
SIZES = (HEAD_TEXT, HEAD_LAYOUT)
ROWS = 128


class Weights(typing.NamedTuple):
    project: typing.Any
    outward: typing.Any
    upward: typing.Any
    downward: typing.Any


class Kept(typing.NamedTuple):
    qkv: typing.Any
    ctx: typing.Any
    n1: typing.Any
    r1: typing.Any
    low: typing.Any
    act: typing.Any
    slope: typing.Any
    n2: typing.Any
    r2: typing.Any


class Needed(typing.NamedTuple):
    n2: typing.Any
    r2: typing.Any
    downward: typing.Any
    slope: typing.Any
    upward: typing.Any
    n1: typing.Any
    r1: typing.Any
    outward: typing.Any
    qkv: typing.Any
    project: typing.Any


class Back(typing.NamedTuple):
    dx: typing.Any
    dqkv: typing.Any
    gf: typing.Any
    dpre: typing.Any
    ga: typing.Any


def dot(a, b, dims=NN):
    return lax.dot_general(a, b, dims, preferred_element_type=F32)


def gelu_pair(u):
    t = 1.0 / (1.0 + (GELU_P / math.sqrt(2.0)) * jnp.abs(u))
    e = jnp.exp(-0.5 * (u * u))
    a1, a2, a3, a4, a5 = (0.5 * a for a in GELU_A)
    tail = ((((a5 * t + a4) * t + a3) * t + a2) * t + a1) * t * e
    cdf = jnp.where(u >= 0, 1.0 - tail, tail)
    return u * cdf, cdf + u * e * (1.0 / math.sqrt(2.0 * math.pi))


def norm_rows(z, gain, offset):
    center = z - jnp.mean(z, axis=-1, keepdims=True)
    inverse = lax.rsqrt(jnp.mean(center * center, axis=-1, keepdims=True) + EPSILON)
    normed = center * inverse
    return normed * gain + offset, normed, inverse


def norm_rows_back(g, n, r, gain):
    t = g * gain
    return r * (t - jnp.mean(t, axis=-1, keepdims=True) - n * jnp.mean(t * n, axis=-1, keepdims=True))


class Staged:
    def __init__(self, tree, hbm, vmem, sem, inward):
        self.tree, self.vmem = tree, list(vmem)
        pairs = zip(hbm, vmem) if inward else zip(vmem, hbm)
        self.copies = [pltpu.make_async_copy(a, b, sem.at[i]) for i, (a, b) in enumerate(pairs)]

    def refs(self):
        return jax.tree.unflatten(self.tree, self.vmem)

    def parts(self):
        return jax.tree.unflatten(self.tree, self.copies)

    def start(self):
        for copy in self.copies:
            copy.start()

    def wait(self):
        for copy in self.copies:
            copy.wait()


def start(*copies):
    for copy in copies:
        copy.start()


def wait(*copies):
    for copy in copies:
        copy.wait()


def head_rows(stacks, slot, kind, local, scales=None):
    rows = []
    for b in range(2):
        first = kind * (stacks[b].shape[1] // 3) + local * SIZES[b]
        piece = stacks[b][slot, first : first + SIZES[b], :]
        rows.append(piece if scales is None else piece * BF(scales[b]))
    rows.append(jnp.zeros((128 - sum(SIZES), rows[0].shape[1]), BF))
    return jnp.concatenate(rows, axis=0)


def put_head(stacks, slot, kind, local, b, value):
    first = kind * (stacks[b].shape[1] // 3) + local * SIZES[b]
    stacks[b][slot, first : first + SIZES[b], :] = value.astype(BF)


def slot_of(u, core, chip):
    return ((chip + u // 2) % 2) * 2 + (core + u % 2) % 2


def forward_kernel(sections, tensors, shared, in_tree, out_tree, *refs):
    n_w, n_out = len(shared), out_tree.num_leaves
    sources = (refs[0:2], refs[2:4])
    shards = refs[4 : 4 + n_w]
    pad_mask, counts, lang_ids, lang_table, *norms = refs[4 + n_w : 12 + n_w]
    rest = refs[12 + n_w :]
    hbm_out, cots, rest = rest[:n_out], rest[n_out : n_out + 2], rest[n_out + 2 :]
    outgoing = Staged(out_tree, hbm_out, rest[:n_out], rest[n_out], False)
    rest = rest[n_out + 1 :]
    flipped, raw_x, *rest = rest
    nats, totals, rest = rest[0:2], rest[2:4], rest[4:]
    page_send, page_recv, w_send, w_recv, own_sem, hop_send, hop_recv = rest
    x, y, probs_out, kept, weights = outgoing.refs()
    x_out, y_out, probs_copy, kept_out, weights_out = outgoing.parts()
    section, d, t = lax.axis_index("section"), lax.axis_index("dp"), lax.axis_index("tensor")
    core, chip, half_index = t % 2, t // 2, d % 2
    sibling, partner = t + 1 - 2 * core, (t + tensors // 2) % tensors
    mate = d + 1 - 2 * half_index
    micro, page = core, chip
    part_length = sources[0][0].shape[1]
    length = x[0].shape[0]
    blocks = [slice(c, c + 2 * ROWS) for c in range(0, length, 2 * ROWS)]
    full = (
        weights[0].project, weights[1].project, weights[0].outward, weights[0].upward,
        weights[0].downward, weights[1].outward, weights[1].upward, weights[1].downward,
    )
    greet(section, t, sections, tensors, ({"dp": mate},) if any(shared) else ())

    def half_of(ref, i, which):
        count = shards[i].shape[0] // 2
        return ref.at[pl.ds(pl.multiple_of(which * count, 16), count)] if shared[i] else ref

    def to_partner(i):
        return remote(
            half_of(shards[i], i, half_index), half_of(full[i].at[t], i, half_index),
            w_send.at[0, i], w_recv.at[0, i], {"tensor": partner},
        )

    def to_sibling(i):
        return remote(shards[i], full[i].at[t], w_send.at[1, i], w_recv.at[1, i], {"tensor": sibling})

    def to_mate(i):
        ref = half_of(full[i].at[partner], i, half_index)
        return remote(ref, ref, w_send.at[2, i], w_recv.at[2, i], {"dp": mate})

    def on_first(i):
        ref = half_of(full[i].at[partner], i, half_index)
        return remote(ref, ref, w_send.at[3, i], w_recv.at[3, i], {"tensor": sibling})

    def on_second(i):
        ref = half_of(full[i].at[partner], i, 1 - half_index)
        return remote(ref, ref, w_send.at[4, i], w_recv.at[4, i], {"tensor": sibling})

    def keep(i):
        return pltpu.make_async_copy(shards[i], full[i].at[t], own_sem.at[i])

    def relay(*which):
        for i in which:
            to_partner(i).wait_recv()
            if shared[i]:
                to_mate(i).start()
            on_first(i).start()

    def relay_second(*which):
        for i in which:
            if shared[i]:
                to_mate(i).wait_recv()
                on_second(i).start()

    def early(*which):
        for i in which:
            keep(i).wait()
            to_sibling(i).wait_recv()

    def late(*which):
        for i in which:
            on_first(i).wait_recv()
            if shared[i]:
                on_second(i).wait_recv()

    def token_slot(g, a, index):
        start_at = pl.multiple_of(index * part_length, part_length)
        target = ((raw_x, flipped), cots)[g][a]
        return target.at[pl.ds(start_at, part_length)] if a == 0 else target.at[:, pl.ds(start_at, part_length)]

    def over_pages(g, act):
        for j in range(2):
            target = 2 * j + section
            here = (section == g) & (t == target)
            for a in range(2):
                act(g, j, a, target, here)

    def page_copy(g, j, a, target):
        return remote(
            sources[g][a].at[j], token_slot(g, a, t), page_send.at[g, j, a], page_recv.at[a, t],
            {"section": g, "tensor": target},
        )

    def page_start(g, j, a, target, here):
        @pl.when(here)
        def _():
            pltpu.make_async_copy(sources[g][a].at[j], token_slot(g, a, t), page_recv.at[a, t]).start()

        @pl.when(jnp.logical_not(here))
        def _():
            page_copy(g, j, a, target).start()

    def page_sent(g, j, a, target, here):
        @pl.when(jnp.logical_not(here))
        def _():
            page_copy(g, j, a, target).wait_send()

    def pages_arrived(g):
        for a in range(2):
            for q in range(tensors):
                slot = token_slot(g, a, q)
                remote(slot, slot, page_send.at[0, 0, a], page_recv.at[a, q], {"tensor": sibling}).wait_recv()

    def hop(b, n):
        return remote(
            y[b].at[blocks[n]], x[b].at[blocks[n]], hop_send.at[b, n], hop_recv.at[b, n], {"section": 1 - section}
        )

    over_pages(0, page_start)
    for i in range(n_w):
        to_partner(i).start()
        keep(i).start()
    for i in range(n_w):
        to_sibling(i).start()
    over_pages(1, page_start)

    at_page = (lax.broadcasted_iota(jnp.int32, counts.shape, 0) == micro) & (
        lax.broadcasted_iota(jnp.int32, counts.shape, 1) == page
    )

    def own_entry(ref):
        return jnp.sum(jnp.where(at_page, ref[...], 0), axis=(0, 1), keepdims=True)

    positions = lax.broadcasted_iota(jnp.int32, (1, length), 1)
    mask_row = pad_mask[micro, pl.ds(page, 1), :]
    key_mask = (positions < own_entry(counts)) & ((mask_row == 1) | (positions == 0))
    groups = lax.broadcasted_iota(jnp.int32, (lang_table.shape[0], 1), 0)
    lang_row = jnp.sum(jnp.where(groups == own_entry(lang_ids), lang_table[...], 0.0), axis=0, keepdims=True)
    local_heads = weights[0].project.shape[1] // (3 * HEAD_TEXT)
    qkv = (kept[0].qkv, kept[1].qkv)

    @pl.when(section == 0)
    def _():
        pages_arrived(0)
        x[0][...] = (raw_x[...].astype(F32) + lang_row).astype(BF)
        x[1][...] = flipped[...].T
        early(0, 1)

    @pl.when(section == 1)
    def _():
        relay(*range(n_w))
        relay_second(*range(n_w))
        early(*range(n_w))
        late(*range(n_w))
        start(*weights_out[0], *weights_out[1])

    @pl.loop(0, 2)
    def _(half):
        @pl.when((half == 1) & (section == 0))
        def _():
            relay(0, 1)
            relay_second(0)
            late(0, 1)

        for n, block in enumerate(blocks):
            @pl.when((half == 0) & (section == 1))
            def _():
                for b in range(2):
                    hop(b, n).wait_recv()

            @pl.loop(0, 2)
            def _(u):
                slot = slot_of(2 * half + u, core, chip)
                for b in range(2):
                    qkv[b][slot, :, block] = dot(weights[b].project[slot], x[b][block], NT).astype(BF)

        @pl.loop(0, 2)
        def _(u):
            slot = slot_of(2 * half + u, core, chip)
            for local in range(local_heads):
                q = head_rows(qkv, slot, 0, local, SCALES).T
                scores = jnp.where(key_mask, dot(q, head_rows(qkv, slot, 1, local)), NEGATIVE)
                raised = jnp.exp(scores - jnp.max(scores, axis=-1, keepdims=True))
                probs = (raised * (1.0 / jnp.sum(raised, axis=-1, keepdims=True))).astype(BF)
                probs_out[slot, local] = probs
                ctx = dot(head_rows(qkv, slot, 2, local), probs, NT).astype(BF)
                kept[0].ctx[slot, local * HEAD_TEXT : (local + 1) * HEAD_TEXT, :] = ctx[:HEAD_TEXT]
                kept[1].ctx[slot, local * HEAD_LAYOUT : (local + 1) * HEAD_LAYOUT, :] = ctx[
                    HEAD_TEXT : HEAD_TEXT + HEAD_LAYOUT
                ]

    start(probs_copy, *x_out, *(k.qkv for k in kept_out), *(k.ctx for k in kept_out))

    def attend(b):
        gains, biases = norms[2 * b : 2 * b + 2]
        width = x[b].shape[1]
        nats[b][...] = kept[b].ctx[...].reshape(width, length).T
        wide = weights[b].outward[...].reshape(width, width)
        for block in blocks:
            h, n, r = norm_rows(x[b][block].astype(F32) + dot(nats[b][block], wide), gains[0:1], biases[0:1])
            totals[b][0, block] = h
            totals[b][1, block] = jnp.zeros(h.shape, F32)
            kept[b].n1[block] = n
            kept[b].r1[block] = r
            kept[b].low[block] = h.astype(BF)
        start(kept_out[b].n1, kept_out[b].r1, kept_out[b].low)

    def feed(b, first, which):
        @pl.loop(first, first + 2)
        def _(u):
            slot = slot_of(u, core, chip)
            for block in which:
                act, slope = gelu_pair(dot(kept[b].low[block], weights[b].upward[slot]))
                act = act.astype(BF)
                kept[b].act[slot, block] = act
                kept[b].slope[slot, block] = slope.astype(BF)
                totals[b][1, block] += dot(act, weights[b].downward[slot])

    def finish(b):
        gains, biases = norms[2 * b : 2 * b + 2]
        for n, block in enumerate(blocks):
            feed(b, 2, [block])
            out, normed, r = norm_rows(totals[b][0, block] + totals[b][1, block], gains[1:2], biases[1:2])
            y[b][block] = out.astype(BF)
            kept[b].n2[block] = normed
            kept[b].r2[block] = r

            @pl.when(section == 0)
            def _():
                hop(b, n).start()

        start(y_out[b], kept_out[b].act, kept_out[b].slope, kept_out[b].n2, kept_out[b].r2)

    @pl.when(section == 0)
    def _():
        relay(2, 3)
        early(2)
        late(2)

    attend(0)

    @pl.when(section == 0)
    def _():
        early(3, 4)

    feed(0, 0, blocks)

    @pl.when(section == 0)
    def _():
        relay(4, 5, 6, 7)
        relay_second(3)
        early(5, 6, 7)
        late(5, 6, 7)

    attend(1)
    feed(1, 0, blocks)
    finish(1)

    @pl.when(section == 0)
    def _():
        relay_second(4)
        late(3, 4)

    finish(0)

    @pl.when(section == 0)
    def _():
        start(*weights_out[0], *weights_out[1])
        for b in range(2):
            for n in range(len(blocks)):
                hop(b, n).wait_send()

    for i in range(n_w):
        to_partner(i).wait_send()
        to_sibling(i).wait_send()
        on_first(i).wait_send()
        if shared[i]:
            to_mate(i).wait_send()
            on_second(i).wait_send()
    for g in range(sections):
        over_pages(g, page_sent)

    @pl.when(section == 1)
    def _():
        pages_arrived(1)

    outgoing.wait()


def vmem_like(tree):
    return [pltpu.VMEM(s.shape, s.dtype) for s in jax.tree.leaves(tree)]


VMEM = pl.BlockSpec(memory_space=pltpu.VMEM)


def shape(dims, dtype=BF):
    return jax.ShapeDtypeStruct(tuple(dims), dtype)


def layer_forward(mesh, text_in, layout_in, text_cot, layout_cot, shards, norms, marks):
    sections, dp, tensors = mesh.shape["section"], mesh.shape["dp"], mesh.shape["tensor"]
    length = text_in.shape[1] * tensors
    rows = (shape((length, text_in.shape[2])), shape((length, layout_in.shape[1])))
    local_heads = shards[0].project.shape[0] // (3 * HEAD_TEXT)
    kept = []
    for x, w in zip(rows, shards):
        units, column = shape((tensors, length, w.upward.shape[1])), shape((length, 1), F32)
        kept.append(Kept(
            qkv=shape((tensors, w.project.shape[0], length)), ctx=shape((tensors, w.outward.shape[0], length)),
            n1=shape(x.shape, F32), r1=column, low=shape(x.shape), act=units, slope=units,
            n2=shape(x.shape, F32), r2=column,
        ))
    weights = tuple(Weights(*(shape((tensors,) + m.shape) for m in w)) for w in shards)
    outs = (rows, rows, shape((tensors, local_heads, length, length)), tuple(kept), weights)
    flat_out, out_tree = jax.tree.flatten(outs)
    (a, b) = shards
    ordered = (a.project, b.project, a.outward, a.upward, a.downward, b.outward, b.upward, b.downward)
    shared = tuple(dp % 2 == 0 and w.shape[0] >= 512 for w in ordered)
    n_w = len(ordered)
    cots = [rows[0], shape((rows[1].shape[1], length))]
    small = (*marks, *norms[0], *norms[1])
    results = pl.pallas_call(
        functools.partial(forward_kernel, sections, tensors, shared, None, out_tree),
        out_shape=flat_out + cots,
        in_specs=[ANY] * (4 + n_w) + [VMEM] * len(small),
        out_specs=[ANY] * (len(flat_out) + 2),
        scratch_shapes=vmem_like(flat_out) + [pltpu.SemaphoreType.DMA((len(flat_out),))]
        + [pltpu.VMEM(cots[1].shape, BF), pltpu.VMEM(cots[0].shape, BF)]
        + [pltpu.VMEM(x.shape, BF) for x in rows]
        + [pltpu.VMEM((2,) + x.shape, F32) for x in rows]
        + [
            pltpu.SemaphoreType.DMA((sections, 2, 2)), pltpu.SemaphoreType.DMA((2, tensors)),
            pltpu.SemaphoreType.DMA((5, n_w)), pltpu.SemaphoreType.DMA((5, n_w)), pltpu.SemaphoreType.DMA((n_w,)),
            pltpu.SemaphoreType.DMA((2, length // (2 * ROWS))), pltpu.SemaphoreType.DMA((2, length // (2 * ROWS))),
        ],
        compiler_params=pltpu.CompilerParams(
            collective_id=0, has_side_effects=True, vmem_limit_bytes=62 << 20
        ),
        name="layer_forward",
    )(text_in, layout_in, text_cot, layout_cot, *ordered, *small)
    return jax.tree.unflatten(out_tree, results[:-2]), tuple(results[-2:])


def backward_kernel(in_tree, out_tree, *refs):
    n_in, n_out = in_tree.num_leaves, out_tree.num_leaves
    hbm_in, cots, lang_ids, gains = refs[:n_in], refs[n_in : n_in + 2], refs[n_in + 2], refs[n_in + 3 : n_in + 5]
    rest = refs[n_in + 5 :]
    hbm_out, small, rest = rest[:n_out], rest[n_out], rest[n_out + 1 :]
    incoming = Staged(in_tree, hbm_in, rest[:n_in], rest[n_in], True)
    rest = rest[n_in + 1 :]
    outgoing = Staged(out_tree, hbm_out, rest[:n_out], rest[n_out], False)
    rest = rest[n_out + 1 :]
    g_in, flipped, dctx, dz, sums, rest = rest[0:2], rest[2], rest[3:5], rest[5:7], rest[7:9], rest[9:]
    cot_sem, hop_send, hop_recv = rest
    needed, probs_in = incoming.refs()
    needed_in, probs_copy = incoming.parts()
    back, back_out = outgoing.refs(), outgoing.parts()
    section, t = lax.axis_index("section"), lax.axis_index("tensor")
    slots, length = needed[0].project.shape[0], g_in[0].shape[0]
    local_heads = needed[0].project.shape[1] // (3 * HEAD_TEXT)
    blocks = [slice(c, c + 2 * ROWS) for c in range(0, length, 2 * ROWS)]
    other = {"section": 1 - section}
    barrier = pltpu.get_barrier_semaphore()
    pl.semaphore_signal(barrier, inc=1, device_id=other, device_id_type=MESH)
    cot_copies = (
        pltpu.make_async_copy(cots[0], g_in[0], cot_sem.at[0]), pltpu.make_async_copy(cots[1], flipped, cot_sem.at[1])
    )

    @pl.when(section == 1)
    def _():
        start(*cot_copies)

    incoming.start()
    pl.semaphore_wait(barrier, 1)

    def hop(b, n):
        return remote(back[b].dx.at[blocks[n]], g_in[b].at[blocks[n]], hop_send.at[b, n], hop_recv.at[b, n], other)

    @pl.when(section == 1)
    def _():
        wait(*cot_copies)
        g_in[1][...] = flipped[...].T

    for b in range(2):
        sums[b][...] = jnp.zeros(sums[b].shape, F32)
        own_in = needed_in[b]
        wait(own_in.n2, own_in.r2, own_in.downward, own_in.slope, own_in.upward, own_in.n1, own_in.r1, own_in.outward)
    for n, block in enumerate(blocks):
        for b in (1, 0):
            own, res, gain = needed[b], back[b], gains[b]

            @pl.when(section == 0)
            def _():
                hop(b, n).wait_recv()

            g, normed = g_in[b][block].astype(F32), own.n2[block]
            low = norm_rows_back(g, normed, own.r2[block], gain[1:2])
            dz[b][block] = low
            res.gf[block] = low.astype(BF)
            sums[b][1:2] += jnp.sum(g * normed, axis=0, keepdims=True)
            sums[b][3:4] += jnp.sum(g, axis=0, keepdims=True)

            @pl.loop(0, slots)
            def _(q):
                d_act = dot(res.gf[block], own.downward[q], NT)
                d_pre = (d_act * own.slope[q, block].astype(F32)).astype(BF)
                res.dpre[q, block] = d_pre
                dz[b][block] += dot(d_pre, own.upward[q], NT)

            g, normed = dz[b][block], own.n1[block]
            low = norm_rows_back(g, normed, own.r1[block], gain[0:1])
            dz[b][block] = low
            res.ga[block] = low.astype(BF)
            sums[b][0:1] += jnp.sum(g * normed, axis=0, keepdims=True)
            sums[b][2:3] += jnp.sum(g, axis=0, keepdims=True)
            for q in range(slots):
                dctx[b][q, :, block] = dot(own.outward[q], res.ga[block], NT).astype(BF)

    for res_out in back_out:
        start(res_out.gf, res_out.dpre, res_out.ga)
    wait(needed_in[0].qkv, needed_in[1].qkv, probs_copy)
    qkv, dqkv = (needed[0].qkv, needed[1].qkv), (back[0].dqkv, back[1].dqkv)
    text_rows, layout_rows = slice(0, HEAD_TEXT), slice(HEAD_TEXT, HEAD_TEXT + HEAD_LAYOUT)

    @pl.loop(0, slots)
    def _(q):
        for local in range(local_heads):
            dcT = jnp.concatenate(
                [dctx[b][q, local * SIZES[b] : (local + 1) * SIZES[b], :] for b in range(2)]
                + [jnp.zeros((128 - sum(SIZES), length), BF)], axis=0,
            )
            dc = dcT.T
            lane = lax.broadcasted_iota(jnp.int32, dc.shape, 1)
            dc_layout = jnp.where(lane >= HEAD_TEXT, dc, jnp.zeros_like(dc))
            qT, kT, vT = (head_rows(qkv, q, kind, local, SCALES if kind == 0 else None) for kind in range(3))
            low = probs_in[q, local]
            probs = low.astype(F32)
            both = dot(dc, vT)
            ds_both = (probs * (both - jnp.sum(probs * both, axis=-1, keepdims=True))).astype(BF)
            single = dot(dc_layout, vT)
            ds_layout = (probs * (single - jnp.sum(probs * single, axis=-1, keepdims=True))).astype(BF)
            dvT = dot(dcT, low)
            put_head(dqkv, q, 2, local, 0, dvT[text_rows])
            put_head(dqkv, q, 2, local, 1, dvT[layout_rows])
            put_head(dqkv, q, 0, local, 0, dot(kT[text_rows], ds_both, NT) * SCALES[0])
            put_head(dqkv, q, 1, local, 0, dot(qT[text_rows], ds_both))
            put_head(dqkv, q, 0, local, 1, dot(kT[layout_rows], ds_layout, NT) * SCALES[1])
            put_head(dqkv, q, 1, local, 1, dot(qT[layout_rows], ds_layout))

    start(back_out[0].dqkv, back_out[1].dqkv)
    wait(needed_in[0].project, needed_in[1].project)
    page_sum = jnp.zeros((1, dz[0].shape[1]), F32)
    for n, block in enumerate(blocks):
        for b in (1, 0):
            down = dz[b][block]
            for q in range(slots):
                down += dot(dqkv[b][q, :, block].T, needed[b].project[q])
            down = down.astype(BF)
            back[b].dx[block] = down
            if b == 0:
                page_sum += jnp.sum(down.astype(F32), axis=0, keepdims=True)

            @pl.when(section == 1)
            def _():
                hop(b, n).start()

    start(back_out[0].dx, back_out[1].dx)
    at_page = (lax.broadcasted_iota(jnp.int32, lang_ids.shape, 0) == t % 2) & (
        lax.broadcasted_iota(jnp.int32, lang_ids.shape, 1) == t // 2
    )
    group = jnp.sum(jnp.where(at_page, lang_ids[...], 0), axis=(0, 1), keepdims=True)
    n_lang = small.shape[0] - 8
    chosen = (lax.broadcasted_iota(jnp.int32, (n_lang, 1), 0) == group) & (section == 0)
    small[0:n_lang] = jnp.where(chosen, page_sum, 0.0)
    small[n_lang : n_lang + 4] = sums[0][...]
    small[n_lang + 4 : n_lang + 8] = jnp.zeros((4, small.shape[1]), F32)
    small[n_lang + 4 : n_lang + 8, : sums[1].shape[1]] = sums[1][...]

    @pl.when(section == 1)
    def _():
        for b in range(2):
            for n in range(len(blocks)):
                hop(b, n).wait_send()

    outgoing.wait()


def layer_backward(saved, weights, cots, norms, lang_ids, n_lang):
    probs, kept = saved
    needed, back = [], []
    for k, w in zip(kept, weights):
        rows = shape(k.low.shape)
        needed.append(Needed(
            n2=k.n2, r2=k.r2, downward=w.downward, slope=k.slope, upward=w.upward, n1=k.n1, r1=k.r1,
            outward=w.outward, qkv=k.qkv, project=w.project,
        ))
        back.append(Back(dx=rows, dqkv=shape(k.qkv.shape), gf=rows, dpre=shape(k.slope.shape), ga=rows))
    flat_in, in_tree = jax.tree.flatten((tuple(needed), probs))
    flat_out, out_tree = jax.tree.flatten(tuple(back))
    widths = [k.low.shape[1] for k in kept]
    n_blocks = kept[0].low.shape[0] // (2 * ROWS)
    results = pl.pallas_call(
        functools.partial(backward_kernel, in_tree, out_tree),
        out_shape=flat_out + [shape((n_lang + 8, widths[0]), F32)],
        in_specs=[ANY] * (len(flat_in) + 2) + [VMEM] * 3,
        out_specs=[ANY] * len(flat_out) + [VMEM],
        scratch_shapes=vmem_like(flat_in) + [pltpu.SemaphoreType.DMA((len(flat_in),))]
        + vmem_like(flat_out) + [pltpu.SemaphoreType.DMA((len(flat_out),))]
        + [pltpu.VMEM(k.low.shape, BF) for k in kept] + [pltpu.VMEM(cots[1].shape, BF)]
        + [pltpu.VMEM(k.ctx.shape, BF) for k in kept]
        + [pltpu.VMEM(k.low.shape, F32) for k in kept]
        + [pltpu.VMEM((4, w), F32) for w in widths]
        + [pltpu.SemaphoreType.DMA((2,))] + [pltpu.SemaphoreType.DMA((2, n_blocks))] * 2,
        compiler_params=pltpu.CompilerParams(
            collective_id=2, has_side_effects=True, vmem_limit_bytes=62 << 20
        ),
        name="layer_backward",
    )(*flat_in, *cots, lang_ids, norms[0][0], norms[1][0])
    return jax.tree.unflatten(out_tree, results[:-1]), results[-1]


def widen_kernel(*refs):
    n = (len(refs) - 2) // 2
    for b in range(2):
        at = 0
        for out in refs[2 + b * n : 2 + (b + 1) * n]:
            for c in range(0, out.shape[0], 48):
                out[c : c + 48] = refs[b][at + c : at + c + 48].astype(F32)
            at += out.shape[0]


def widen(totals, operands):
    outs = [shape((rows, total.shape[1]), F32) for total, own in zip(totals, operands) for rows in gradient_rows(own)]
    results = pl.pallas_call(
        widen_kernel, out_shape=outs, in_specs=[VMEM] * 2, out_specs=[VMEM] * len(outs),
        compiler_params=pltpu.CompilerParams(vmem_limit_bytes=40 << 20), name="widen",
    )(*totals)
    return results[:4], results[4:]


class Operands(typing.NamedTuple):
    act: typing.Any
    gf: typing.Any
    low: typing.Any
    dpre: typing.Any
    x: typing.Any
    dqkv: typing.Any
    ctx: typing.Any
    ga: typing.Any


def gradient_rows(own):
    return own.dqkv.shape[1], own.ctx.shape[1], own.low.shape[1], own.act.shape[2]


def gradient_block(own, lowT, slot, which, first, rows):
    if which == 0:
        return dot(own.dqkv[slot, first : first + rows, :], own.x[...])
    if which == 1:
        return dot(own.ctx[slot, first : first + rows, :], own.ga[...])
    if which == 2:
        return dot(lowT[first : first + rows, :], own.dpre[slot])
    return dot(own.act[slot, :, first : first + rows].T, own.gf[...])


def chunks_of(own, step):
    sizes = gradient_rows(own)
    starts = [sum(sizes[:i]) for i in range(4)]
    chunks = []
    for which in (3, 2, 0, 1):
        size = sizes[which]
        piece = next(p for p in (step, 192, size) if size % p == 0)
        chunks += [(starts[which] + f, piece, ((which, f, piece),)) for f in range(0, size, piece)]
    return chunks


def whole_chunk(own):
    sizes = gradient_rows(own)
    return (0, sum(sizes), tuple((which, 0, sizes[which]) for which in range(4)))


def reduce_kernel(sections, tensors, chain, in_tree, *refs):
    n_in = in_tree.num_leaves
    hbm_in = refs[:n_in]
    dx_t, dx_l, y_t, y_l, small_in = refs[n_in : n_in + 5]
    results = refs[n_in + 5 : n_in + 7]
    small_out, text_out, layout_out, grad_out, layout_grad_out = refs[n_in + 7 : n_in + 12]
    rest = refs[n_in + 12 :]
    operands = Staged(in_tree, hbm_in, rest[:n_in], rest[n_in], True)
    lowT, raw, from_sibling, from_partner, near_in, cross_in, total = (
        rest[n_in + 1 + 2 * i : n_in + 3 + 2 * i] for i in range(7)
    )
    small_got, small_sum, send, recv, out_sem, small_send, small_recv, page_send, page_recv = rest[n_in + 15 :]
    section, d, t = lax.axis_index("section"), lax.axis_index("dp"), lax.axis_index("tensor")
    core, chip = t % 2, t // 2
    sibling = {"tensor": t + 1 - 2 * core}
    partner = {"tensor": (t + tensors // 2) % tensors}
    near, cross = {"dp": d + 1 - 2 * (d % 2)}, {"dp": 3 - d}
    outer = (d == 0) | (d == 3)
    operands.start()
    greet(section, t, sections, tensors, (near, cross) if chain else ())

    length = text_out.shape[1]
    micro, page = t % 2, t // 2
    kinds = ((grad_out, layout_grad_out), (text_out, layout_out))
    pages = ((dx_t, dx_l), (y_t, y_l))

    def page_part(g, q, a):
        return pages[g][a].at[pl.ds(q * length, length)] if a == 0 else pages[g][a].at[:, pl.ds(q * length, length)]

    def each_page(act):
        for g in range(sections):
            for q in range(tensors):
                for a in range(2):
                    here = (micro == g) & (t == q)

                    @pl.when((section == g) & here)
                    def _():
                        act(g, q, a, True)

                    @pl.when((section == g) & jnp.logical_not(here))
                    def _():
                        act(g, q, a, False)

    def page_copy(g, q, a):
        return remote(
            page_part(g, q, a), kinds[g][a].at[page], page_send.at[q, a], page_recv.at[g, a, page],
            {"section": micro, "tensor": q},
        )

    def page_start(g, q, a, here):
        if here:
            pltpu.make_async_copy(page_part(g, q, a), kinds[g][a].at[page], page_recv.at[g, a, page]).start()
        else:
            page_copy(g, q, a).start()

    def page_sent(g, q, a, here):
        if not here:
            page_copy(g, q, a).wait_send()

    each_page(page_start)

    def small_copy(i, device):
        return remote(small_sum.at[i], small_got.at[i], small_send.at[i], small_recv.at[i], device)

    small_sum[0] = small_in[...]
    if chain:
        small_copy(0, sibling).start()

    own, own_in = operands.refs(), operands.parts()
    work = [(1,) + whole_chunk(own[1])] + [(0,) + c for c in chunks_of(own[0], 256)]
    for b in range(2):
        wait(own_in[b].low)
        lowT[b][...] = own[b].low[...].T
    for b in (1, 0):
        wait(*(part for part in own_in[b] if part is not own_in[b].low))

    def span(ref, k):
        return ref.at[pl.ds(work[k][1], work[k][2])]

    def spans(ref, k):
        return ref.at[:, pl.ds(work[k][1], work[k][2])]

    def to_sibling(k):
        b = work[k][0]
        return remote(
            spans(raw[b].at[1 - core], k), spans(from_sibling[b], k), send.at[0, k], recv.at[0, k], sibling
        )

    def to_partner(k):
        b = work[k][0]
        return remote(
            span(raw[b].at[core, 1 - chip], k), span(from_partner[b], k), send.at[1, k], recv.at[1, k], partner
        )

    def to_near(k):
        b = work[k][0]
        return remote(span(raw[b].at[core, chip], k), span(near_in[b], k), send.at[2, k], recv.at[2, k], near)

    def total_to_near(k):
        b = work[k][0]
        return remote(span(total[b], k), span(near_in[b], k), send.at[2, k], recv.at[2, k], near)

    def to_cross(k):
        b = work[k][0]
        return remote(span(raw[b].at[core, chip], k), span(cross_in[b], k), send.at[3, k], recv.at[3, k], cross)

    def out_copy(k, source):
        b = work[k][0]
        return pltpu.make_async_copy(span(source, k), span(results[b], k), out_sem.at[k])

    def added(target, *sources):
        target[...] = sum(s[...].astype(F32) for s in sources).astype(BF)

    def stage_product(k):
        b, first, rows, pieces = work[k]
        for slot in range(tensors):
            at = first
            for which, begin, count in pieces:
                raw[b][slot % 2, slot // 2, at : at + count, :] = gradient_block(
                    own[b], lowT[b], slot, which, begin, count
                ).astype(BF)
                at += count
        to_sibling(k).start()

    def stage_sibling(k):
        b = work[k][0]
        to_sibling(k).wait_recv()
        mine = raw[b].at[core, 1 - chip]
        added(span(mine, k), span(mine, k), span(from_sibling[b].at[1 - chip], k))
        to_partner(k).start()
        mine = raw[b].at[core, chip]
        added(span(mine, k), span(mine, k), span(from_sibling[b].at[chip], k))

    def stage_partner(k):
        b = work[k][0]
        to_partner(k).wait_recv()
        mine = span(raw[b].at[core, chip], k)
        added(mine, mine, span(from_partner[b], k))
        if not chain:
            out_copy(k, raw[b].at[core, chip]).start()
            return

        @pl.when(outer)
        def _():
            to_near(k).start()

    def stage_near(k):
        b = work[k][0]

        @pl.when(jnp.logical_not(outer))
        def _():
            to_near(k).wait_recv()
            mine = span(raw[b].at[core, chip], k)
            added(mine, mine, span(near_in[b], k))
            to_cross(k).start()

    def stage_cross(k):
        b = work[k][0]

        @pl.when(jnp.logical_not(outer))
        def _():
            to_cross(k).wait_recv()
            added(span(total[b], k), span(raw[b].at[core, chip], k), span(cross_in[b], k))
            total_to_near(k).start()
            out_copy(k, total[b]).start()

    def stage_total(k):
        b = work[k][0]

        @pl.when(outer)
        def _():
            to_near(k).wait_recv()
            out_copy(k, near_in[b]).start()

    stages = [stage_product, stage_sibling, stage_partner]
    if chain:
        stages += [stage_near, stage_cross, stage_total]
    for step in range(len(work) + len(stages) - 1):
        for lag, stage in enumerate(stages):
            if 0 <= step - lag < len(work):
                stage(step - lag)
        if not chain:
            continue
        if step == 0:
            small_copy(0, sibling).wait_recv()
            small_sum[1] = small_sum[0] + small_got[0]
            small_copy(1, partner).start()
        if step == 1:
            small_copy(1, partner).wait_recv()
            small_sum[2] = small_sum[1] + small_got[1]
            small_copy(2, near).start()
        if step == 2:
            small_copy(2, near).wait_recv()
            small_sum[3] = small_sum[2] + small_got[2]

            @pl.when(jnp.logical_not(outer))
            def _():
                small_copy(3, cross).start()

        if step == 4:
            @pl.when(jnp.logical_not(outer))
            def _():
                small_copy(3, cross).wait_recv()
                small_sum[4] = small_sum[3] + small_got[3]
                small_copy(4, near).start()

        if step == 6:
            @pl.when(outer)
            def _():
                small_copy(4, near).wait_recv()
                small_sum[4] = small_got[4]

            small_sum[5] = small_sum[4]
            small_copy(5, {"section": 1 - section}).start()
        if step == 8:
            small_copy(5, {"section": 1 - section}).wait_recv()
            small_out[0] = small_sum[5]
            small_out[1] = small_got[5]

    if chain:
        for i, device in enumerate((sibling, partner, near)):
            small_copy(i, device).wait_send()

        @pl.when(jnp.logical_not(outer))
        def _():
            small_copy(3, cross).wait_send()
            small_copy(4, near).wait_send()

        small_copy(5, {"section": 1 - section}).wait_send()
    else:
        small_out[0] = small_in[...]
        small_out[1] = small_in[...]
    for k in range(len(work)):
        to_sibling(k).wait_send()
        to_partner(k).wait_send()
        b = work[k][0]
        if chain:
            to_near(k).wait_send()

            @pl.when(jnp.logical_not(outer))
            def _():
                to_cross(k).wait_send()

        out_copy(k, total[b]).wait()
    each_page(page_sent)
    for g in range(sections):
        for a in range(2):
            for j in range(2):
                dst = kinds[g][a].at[j]
                remote(dst, dst, page_send.at[0, a], page_recv.at[g, a, j], partner).wait_recv()


def reduce_all(mesh, operands, dx, y, small):
    sections, dp, tensors = mesh.shape["section"], mesh.shape["dp"], mesh.shape["tensor"]
    chain = dp == 4
    flat_in, in_tree = jax.tree.flatten(operands)
    length = dx[0].shape[0] // tensors
    rows = [sum(gradient_rows(own)) for own in operands]
    widths = [own.x.shape[1] for own in operands]
    n_chunks = 1 + len(chunks_of(operands[0], 256))
    text_shape, layout_shape = shape((2, length, widths[0])), shape((2, widths[1], length))
    big = [pltpu.VMEM((r, w), BF) for r, w in zip(rows, widths)]
    scratch = [pltpu.VMEM(x.shape, x.dtype) for x in flat_in] + [pltpu.SemaphoreType.DMA((len(flat_in),))]
    scratch += [pltpu.VMEM((own.low.shape[1], own.low.shape[0]), BF) for own in operands]
    scratch += [pltpu.VMEM((2, tensors // 2, r, w), BF) for r, w in zip(rows, widths)]
    scratch += [pltpu.VMEM((tensors // 2, r, w), BF) for r, w in zip(rows, widths)]
    scratch += big * 4
    scratch += [pltpu.VMEM((6,) + small.shape, F32)] * 2
    scratch += [pltpu.SemaphoreType.DMA((4, n_chunks))] * 2 + [pltpu.SemaphoreType.DMA((n_chunks,))]
    scratch += [pltpu.SemaphoreType.DMA((6,))] * 2
    scratch += [pltpu.SemaphoreType.DMA((tensors, 2)), pltpu.SemaphoreType.DMA((sections, 2, 2))]
    total_t, total_l, small, *pages = pl.pallas_call(
        functools.partial(reduce_kernel, sections, tensors, chain, in_tree),
        out_shape=[shape((r, w)) for r, w in zip(rows, widths)]
        + [shape((2,) + small.shape, F32), text_shape, layout_shape, text_shape, layout_shape],
        in_specs=[ANY] * (len(flat_in) + 4) + [VMEM],
        out_specs=[ANY] * 2 + [VMEM] + [ANY] * 4,
        scratch_shapes=scratch,
        compiler_params=pltpu.CompilerParams(
            collective_id=1, has_side_effects=True, vmem_limit_bytes=62 << 20
        ),
        name="reduce_all",
    )(*flat_in, dx[0], dx[1].T, y[0], y[1].T, small)
    if not chain:
        total_t, total_l = lax.psum((total_t, total_l), "dp")
        both = lax.psum(small[0], ("dp", "tensor"))
        small = jnp.stack([both, lax.ppermute(both, "section", [(0, 1), (1, 0)])])
    return (total_t, total_l), small, pages


def per_device(
    mesh,
    text_input,
    layout_input,
    text_cotangent,
    layout_cotangent,
    page_counts,
    pad_mask,
    lang_ids,
    lang_table,
    text_project,
    text_outward,
    text_upward,
    text_downward,
    text_gains,
    text_biases,
    layout_project,
    layout_outward,
    layout_upward,
    layout_downward,
    layout_gains,
    layout_biases,
):
    section = lax.axis_index("section")

    def flat(project):
        return jnp.transpose(project[0], (1, 2, 0)).reshape(-1, project.shape[1])

    def flipped(block):
        return jnp.transpose(block[0], (0, 2, 1))

    shards = (
        Weights(flat(text_project), text_outward[0], text_upward[0], text_downward[0]),
        Weights(flat(layout_project), layout_outward[0], layout_upward[0], layout_downward[0]),
    )
    norms = ((text_gains[0], text_biases[0]), (layout_gains[0], layout_biases[0]))
    marks = (pad_mask, page_counts, lang_ids, lang_table)
    (x, y, probs, kept, weights), cots = layer_forward(
        mesh, text_input[0], flipped(layout_input), text_cotangent[0], flipped(layout_cotangent), shards, norms, marks
    )
    n_lang = lang_table.shape[0]
    back, small = layer_backward((probs, kept), weights, cots, norms, lang_ids, n_lang)
    operands = tuple(
        Operands(act=k.act, gf=res.gf, low=k.low, dpre=res.dpre, x=rows, dqkv=res.dqkv, ctx=k.ctx, ga=res.ga)
        for rows, k, res in zip(x, kept, back)
    )
    downs = tuple(res.dx for res in back)
    totals, small, (text_out, layout_out, text_grad, layout_grad) = reduce_all(mesh, operands, downs, y, small)
    lang_sum = jnp.where(section == 0, small[0, :n_lang], small[1, :n_lang])
    norm_sums = (small[0, n_lang : n_lang + 4], small[0, n_lang + 4 : n_lang + 8, : layout_gains.shape[-1]])
    summed = widen(totals, operands)

    def unflat(grad, like):
        return jnp.transpose(grad.reshape(like.shape[2], like.shape[3], like.shape[1]), (2, 0, 1))[None]

    unflip = lambda block: jnp.transpose(block, (0, 2, 1))[None]
    return (
        text_out[None], unflip(layout_out), text_grad[None], unflip(layout_grad), lang_sum,
        unflat(summed[0][0], text_project), summed[0][1][None], summed[0][2][None], summed[0][3][None],
        norm_sums[0][None, 0:2], norm_sums[0][None, 2:4],
        unflat(summed[1][0], layout_project), summed[1][1][None], summed[1][2][None], summed[1][3][None],
        norm_sums[1][None, 0:2], norm_sums[1][None, 2:4],
    )


def solution(mesh):
    tokens = P("section", "dp", "tensor", None)
    weight_specs = (
        P("section", None, None, "tensor"), P("section", "tensor", None), P("section", None, "tensor"),
        P("section", "tensor", None), P("section", None, None), P("section", None, None),
    )
    in_specs = (tokens,) * 4 + (P(None, "dp"), P(None, "dp", None), P(None, "dp"), P()) + weight_specs * 2
    out_specs = (tokens,) * 4 + (P(),) + weight_specs * 2
    return jax.shard_map(
        functools.partial(per_device, mesh), mesh=mesh, in_specs=in_specs, out_specs=out_specs, check_vma=False
    )
```

```python
import functools
import math
import typing

import jax
import jax.numpy as jnp
from jax import lax
from jax.experimental import pallas as pl
from jax.experimental.pallas import tpu as pltpu
from jax.sharding import PartitionSpec as P

HEAD_TEXT = 64
HEAD_LAYOUT = 16
EPSILON = 1e-05
NEGATIVE = -1e30
HIGH = lax.Precision.HIGHEST
MESH = pl.DeviceIdType.MESH
BF = jnp.bfloat16
F32 = jnp.float32
ANY = pl.BlockSpec(memory_space=pl.ANY)


def remote(src, dst, send, recv, device):
    return pltpu.make_async_remote_copy(
        src_ref=src, dst_ref=dst, send_sem=send, recv_sem=recv, device_id=device, device_id_type=MESH
    )


def greet(section, tensor, sections, tensors, extra=()):
    barrier = pltpu.get_barrier_semaphore()
    for g in range(sections):
        for q in range(tensors):

            @pl.when((section != g) | (tensor != q))
            def _():
                pl.semaphore_signal(
                    barrier, inc=1, device_id={"section": g, "tensor": q}, device_id_type=MESH
                )

    for device in extra:
        pl.semaphore_signal(barrier, inc=1, device_id=device, device_id_type=MESH)
    pl.semaphore_wait(barrier, sections * tensors - 1 + len(extra))


GELU_P = 0.3275911
GELU_A = (0.254829592, -0.284496736, 1.421413741, -1.453152027, 1.061405429)
NN = (((1,), (0,)), ((), ()))
NT = (((1,), (1,)), ((), ()))
SCALES = (1.0 / math.sqrt(HEAD_TEXT), 1.0 / math.sqrt(HEAD_LAYOUT))
SIZES = (HEAD_TEXT, HEAD_LAYOUT)
ROWS = 128


class Weights(typing.NamedTuple):
    project: typing.Any
    outward: typing.Any
    upward: typing.Any
    downward: typing.Any


class Kept(typing.NamedTuple):
    qkv: typing.Any
    ctx: typing.Any
    n1: typing.Any
    r1: typing.Any
    low: typing.Any
    act: typing.Any
    slope: typing.Any
    n2: typing.Any
    r2: typing.Any


def dot(a, b, dims=NN):
    return lax.dot_general(a, b, dims, preferred_element_type=F32)


def gelu_pair(u):
    t = 1.0 / (1.0 + (GELU_P / math.sqrt(2.0)) * jnp.abs(u))
    e = jnp.exp(-0.5 * (u * u))
    a1, a2, a3, a4, a5 = (0.5 * a for a in GELU_A)
    tail = ((((a5 * t + a4) * t + a3) * t + a2) * t + a1) * t * e
    cdf = jnp.where(u >= 0, 1.0 - tail, tail)
    return u * cdf, cdf + u * e * (1.0 / math.sqrt(2.0 * math.pi))


def norm_rows(z, gain, offset):
    center = z - jnp.mean(z, axis=-1, keepdims=True)
    inverse = lax.rsqrt(jnp.mean(center * center, axis=-1, keepdims=True) + EPSILON)
    normed = center * inverse
    return normed * gain + offset, normed, inverse


def norm_rows_back(g, n, r, gain):
    t = g * gain
    return r * (t - jnp.mean(t, axis=-1, keepdims=True) - n * jnp.mean(t * n, axis=-1, keepdims=True))


class Staged:
    def __init__(self, tree, hbm, vmem, sem, inward):
        self.tree, self.vmem = tree, list(vmem)
        pairs = zip(hbm, vmem) if inward else zip(vmem, hbm)
        self.copies = [pltpu.make_async_copy(a, b, sem.at[i]) for i, (a, b) in enumerate(pairs)]

    def refs(self):
        return jax.tree.unflatten(self.tree, self.vmem)

    def parts(self):
        return jax.tree.unflatten(self.tree, self.copies)

    def start(self):
        for copy in self.copies:
            copy.start()

    def wait(self):
        for copy in self.copies:
            copy.wait()


def start(*copies):
    for copy in copies:
        copy.start()


def wait(*copies):
    for copy in copies:
        copy.wait()


def head_rows(stacks, slot, kind, local, scales=None):
    rows = []
    for b in range(2):
        first = kind * (stacks[b].shape[1] // 3) + local * SIZES[b]
        piece = stacks[b][slot, first : first + SIZES[b], :]
        rows.append(piece if scales is None else piece * BF(scales[b]))
    rows.append(jnp.zeros((128 - sum(SIZES), rows[0].shape[1]), BF))
    return jnp.concatenate(rows, axis=0)


def put_head(stacks, slot, kind, local, b, value):
    first = kind * (stacks[b].shape[1] // 3) + local * SIZES[b]
    stacks[b][slot, first : first + SIZES[b], :] = value.astype(BF)


def slot_of(u, core, chip):
    return ((chip + u // 2) % 2) * 2 + (core + u % 2) % 2


def forward_kernel(sections, tensors, shared, in_tree, out_tree, *refs):
    n_w, n_out = len(shared), out_tree.num_leaves
    sources = (refs[0:2], refs[2:4])
    shards = refs[4 : 4 + n_w]
    pad_mask, counts, lang_ids, lang_table, *norms = refs[4 + n_w : 12 + n_w]
    rest = refs[12 + n_w :]
    hbm_out, cots, rest = rest[:n_out], rest[n_out : n_out + 2], rest[n_out + 2 :]
    outgoing = Staged(out_tree, hbm_out, rest[:n_out], rest[n_out], False)
    rest = rest[n_out + 1 :]
    flipped, raw_x, y_narrow, *rest = rest
    nats, totals, rest = rest[0:2], rest[2:4], rest[4:]
    page_send, page_recv, w_send, w_recv, own_sem, hop_send, hop_recv = rest
    x, y_pages, probs_out, kept, weights = outgoing.refs()
    y = (y_pages[0], y_narrow)
    x_out, y_out, probs_copy, kept_out, weights_out = outgoing.parts()
    section, d, t = lax.axis_index("section"), lax.axis_index("dp"), lax.axis_index("tensor")
    core, chip, half_index = t % 2, t // 2, d % 2
    sibling, partner = t + 1 - 2 * core, (t + tensors // 2) % tensors
    mate = d + 1 - 2 * half_index
    micro, page = core, chip
    part_length = sources[0][0].shape[1]
    length = x[0].shape[0]
    blocks = [slice(c, c + 2 * ROWS) for c in range(0, length, 2 * ROWS)]
    full = (
        weights[0].project, weights[1].project, weights[0].outward, weights[0].upward,
        weights[0].downward, weights[1].outward, weights[1].upward, weights[1].downward,
    )
    greet(section, t, sections, tensors, ({"dp": mate},) if any(shared) else ())

    def half_of(ref, i, which):
        count = shards[i].shape[0] // 2
        return ref.at[pl.ds(pl.multiple_of(which * count, 16), count)] if shared[i] else ref

    def to_partner(i):
        return remote(
            half_of(shards[i], i, half_index), half_of(full[i].at[t], i, half_index),
            w_send.at[0, i], w_recv.at[0, i], {"tensor": partner},
        )

    def to_sibling(i):
        return remote(shards[i], full[i].at[t], w_send.at[1, i], w_recv.at[1, i], {"tensor": sibling})

    def to_mate(i):
        ref = half_of(full[i].at[partner], i, half_index)
        return remote(ref, ref, w_send.at[2, i], w_recv.at[2, i], {"dp": mate})

    def on_first(i):
        ref = half_of(full[i].at[partner], i, half_index)
        return remote(ref, ref, w_send.at[3, i], w_recv.at[3, i], {"tensor": sibling})

    def on_second(i):
        ref = half_of(full[i].at[partner], i, 1 - half_index)
        return remote(ref, ref, w_send.at[4, i], w_recv.at[4, i], {"tensor": sibling})

    def keep(i):
        return pltpu.make_async_copy(shards[i], full[i].at[t], own_sem.at[i])

    def relay(*which):
        for i in which:
            to_partner(i).wait_recv()
            if shared[i]:
                to_mate(i).start()
            on_first(i).start()

    def relay_second(*which):
        for i in which:
            if shared[i]:
                to_mate(i).wait_recv()
                on_second(i).start()

    def early(*which):
        for i in which:
            keep(i).wait()
            to_sibling(i).wait_recv()

    def late(*which):
        for i in which:
            on_first(i).wait_recv()
            if shared[i]:
                on_second(i).wait_recv()

    def token_slot(g, a, index):
        start_at = pl.multiple_of(index * part_length, part_length)
        target = ((raw_x, flipped), cots)[g][a]
        return target.at[pl.ds(start_at, part_length)] if a == 0 else target.at[:, pl.ds(start_at, part_length)]

    def over_pages(g, act):
        for j in range(2):
            target = 2 * j + section
            here = (section == g) & (t == target)
            for a in range(2):
                act(g, j, a, target, here)

    def page_copy(g, j, a, target):
        return remote(
            sources[g][a].at[j], token_slot(g, a, t), page_send.at[g, j, a], page_recv.at[a, t],
            {"section": g, "tensor": target},
        )

    def page_start(g, j, a, target, here):
        @pl.when(here)
        def _():
            pltpu.make_async_copy(sources[g][a].at[j], token_slot(g, a, t), page_recv.at[a, t]).start()

        @pl.when(jnp.logical_not(here))
        def _():
            page_copy(g, j, a, target).start()

    def page_sent(g, j, a, target, here):
        @pl.when(jnp.logical_not(here))
        def _():
            page_copy(g, j, a, target).wait_send()

    def pages_arrived(g):
        for a in range(2):
            for q in range(tensors):
                slot = token_slot(g, a, q)
                remote(slot, slot, page_send.at[0, 0, a], page_recv.at[a, q], {"tensor": sibling}).wait_recv()

    def hop(b, n):
        return remote(
            y[b].at[blocks[n]], x[b].at[blocks[n]], hop_send.at[b, n], hop_recv.at[b, n], {"section": 1 - section}
        )

    over_pages(0, page_start)
    for i in range(n_w):
        to_partner(i).start()
        keep(i).start()
    for i in range(n_w):
        to_sibling(i).start()
    over_pages(1, page_start)

    at_page = (lax.broadcasted_iota(jnp.int32, counts.shape, 0) == micro) & (
        lax.broadcasted_iota(jnp.int32, counts.shape, 1) == page
    )

    def own_entry(ref):
        return jnp.sum(jnp.where(at_page, ref[...], 0), axis=(0, 1), keepdims=True)

    positions = lax.broadcasted_iota(jnp.int32, (1, length), 1)
    mask_row = pad_mask[micro, pl.ds(page, 1), :]
    key_mask = (positions < own_entry(counts)) & ((mask_row == 1) | (positions == 0))
    groups = lax.broadcasted_iota(jnp.int32, (lang_table.shape[0], 1), 0)
    lang_row = jnp.sum(jnp.where(groups == own_entry(lang_ids), lang_table[...], 0.0), axis=0, keepdims=True)
    local_heads = weights[0].project.shape[1] // (3 * HEAD_TEXT)
    qkv = (kept[0].qkv, kept[1].qkv)

    @pl.when(section == 0)
    def _():
        pages_arrived(0)
        x[0][...] = (raw_x[...].astype(F32) + lang_row).astype(BF)
        x[1][...] = flipped[...].T
        early(0, 1)

    @pl.when(section == 1)
    def _():
        relay(*range(n_w))
        relay_second(*range(n_w))
        early(*range(n_w))
        late(*range(n_w))
        start(*weights_out[0], *weights_out[1])

    @pl.loop(0, 2)
    def _(half):
        @pl.when((half == 1) & (section == 0))
        def _():
            relay(0, 1)
            relay_second(0)
            late(0, 1)

        for n, block in enumerate(blocks):
            @pl.when((half == 0) & (section == 1))
            def _():
                for b in range(2):
                    hop(b, n).wait_recv()

            @pl.loop(0, 2)
            def _(u):
                slot = slot_of(2 * half + u, core, chip)
                for b in range(2):
                    qkv[b][slot, :, block] = dot(weights[b].project[slot], x[b][block], NT).astype(BF)

        @pl.loop(0, 2)
        def _(u):
            slot = slot_of(2 * half + u, core, chip)
            for local in range(local_heads):
                q = head_rows(qkv, slot, 0, local, SCALES).T
                scores = jnp.where(key_mask, dot(q, head_rows(qkv, slot, 1, local)), NEGATIVE)
                raised = jnp.exp(scores - jnp.max(scores, axis=-1, keepdims=True))
                probs = (raised * (1.0 / jnp.sum(raised, axis=-1, keepdims=True))).astype(BF)
                probs_out[slot, local] = probs
                ctx = dot(head_rows(qkv, slot, 2, local), probs, NT).astype(BF)
                kept[0].ctx[slot, local * HEAD_TEXT : (local + 1) * HEAD_TEXT, :] = ctx[:HEAD_TEXT]
                kept[1].ctx[slot, local * HEAD_LAYOUT : (local + 1) * HEAD_LAYOUT, :] = ctx[
                    HEAD_TEXT : HEAD_TEXT + HEAD_LAYOUT
                ]

    start(probs_copy, *x_out, *(k.qkv for k in kept_out), *(k.ctx for k in kept_out))

    def attend(b):
        gains, biases = norms[2 * b : 2 * b + 2]
        width = x[b].shape[1]
        nats[b][...] = kept[b].ctx[...].reshape(width, length).T
        wide = weights[b].outward[...].reshape(width, width)
        for block in blocks:
            h, n, r = norm_rows(x[b][block].astype(F32) + dot(nats[b][block], wide), gains[0:1], biases[0:1])
            totals[b][0, block] = h
            totals[b][1, block] = jnp.zeros(h.shape, F32)
            kept[b].n1[block] = n.astype(BF)
            kept[b].r1[block] = r
            kept[b].low[block] = h.astype(BF)
        start(kept_out[b].n1, kept_out[b].r1, kept_out[b].low)

    def feed(b, first, which):
        @pl.loop(first, first + 2)
        def _(u):
            slot = slot_of(u, core, chip)
            for block in which:
                act, slope = gelu_pair(dot(kept[b].low[block], weights[b].upward[slot]))
                act = act.astype(BF)
                kept[b].act[slot, block] = act
                kept[b].slope[slot, block] = slope.astype(BF)
                totals[b][1, block] += dot(act, weights[b].downward[slot])

    def finish(b):
        gains, biases = norms[2 * b : 2 * b + 2]
        for n, block in enumerate(blocks):
            feed(b, 2, [block])
            out, normed, r = norm_rows(totals[b][0, block] + totals[b][1, block], gains[1:2], biases[1:2])
            y[b][block] = out.astype(BF)
            kept[b].n2[block] = normed.astype(BF)
            kept[b].r2[block] = r

            @pl.when(section == 0)
            def _():
                hop(b, n).start()

        if b == 1:
            y_pages[1][...] = y_narrow[...].T
        start(y_out[b], kept_out[b].act, kept_out[b].slope, kept_out[b].n2, kept_out[b].r2)

    @pl.when(section == 0)
    def _():
        relay(2, 3)
        early(2)
        late(2)

    attend(0)

    @pl.when(section == 0)
    def _():
        early(3, 4)

    feed(0, 0, blocks)

    @pl.when(section == 0)
    def _():
        relay(4, 5, 6, 7)
        relay_second(3)
        early(5, 6, 7)
        late(5, 6, 7)

    attend(1)
    feed(1, 0, blocks)
    finish(1)

    @pl.when(section == 0)
    def _():
        relay_second(4)
        late(3, 4)

    finish(0)

    @pl.when(section == 0)
    def _():
        start(*weights_out[0], *weights_out[1])
        for b in range(2):
            for n in range(len(blocks)):
                hop(b, n).wait_send()

    for i in range(n_w):
        to_partner(i).wait_send()
        to_sibling(i).wait_send()
        on_first(i).wait_send()
        if shared[i]:
            to_mate(i).wait_send()
            on_second(i).wait_send()
    for g in range(sections):
        over_pages(g, page_sent)

    @pl.when(section == 1)
    def _():
        pages_arrived(1)

    outgoing.wait()


def vmem_like(tree):
    return [pltpu.VMEM(s.shape, s.dtype) for s in jax.tree.leaves(tree)]


VMEM = pl.BlockSpec(memory_space=pltpu.VMEM)


def shape(dims, dtype=BF):
    return jax.ShapeDtypeStruct(tuple(dims), dtype)


def layer_forward(mesh, text_in, layout_in, text_cot, layout_cot, shards, norms, marks):
    sections, dp, tensors = mesh.shape["section"], mesh.shape["dp"], mesh.shape["tensor"]
    length = text_in.shape[1] * tensors
    rows = (shape((length, text_in.shape[2])), shape((length, layout_in.shape[1])))
    local_heads = shards[0].project.shape[0] // (3 * HEAD_TEXT)
    kept = []
    for x, w in zip(rows, shards):
        units, column = shape((tensors, length, w.upward.shape[1])), shape((length, 1), F32)
        kept.append(Kept(
            qkv=shape((tensors, w.project.shape[0], length)), ctx=shape((tensors, w.outward.shape[0], length)),
            n1=shape(x.shape), r1=column, low=shape(x.shape), act=units, slope=units,
            n2=shape(x.shape), r2=column,
        ))
    weights = tuple(Weights(*(shape((tensors,) + m.shape) for m in w)) for w in shards)
    pages_out = (rows[0], shape((rows[1].shape[1], length)))
    outs = (rows, pages_out, shape((tensors, local_heads, length, length)), tuple(kept), weights)
    flat_out, out_tree = jax.tree.flatten(outs)
    (a, b) = shards
    ordered = (a.project, b.project, a.outward, a.upward, a.downward, b.outward, b.upward, b.downward)
    shared = tuple(dp % 2 == 0 and w.shape[0] >= 512 for w in ordered)
    n_w = len(ordered)
    cots = [rows[0], shape((rows[1].shape[1], length))]
    small = (*marks, *norms[0], *norms[1])
    results = pl.pallas_call(
        functools.partial(forward_kernel, sections, tensors, shared, None, out_tree),
        out_shape=flat_out + cots,
        in_specs=[ANY] * (4 + n_w) + [VMEM] * len(small),
        out_specs=[ANY] * (len(flat_out) + 2),
        scratch_shapes=vmem_like(flat_out) + [pltpu.SemaphoreType.DMA((len(flat_out),))]
        + [pltpu.VMEM(cots[1].shape, BF), pltpu.VMEM(cots[0].shape, BF), pltpu.VMEM(rows[1].shape, BF)]
        + [pltpu.VMEM(x.shape, BF) for x in rows]
        + [pltpu.VMEM((2,) + x.shape, F32) for x in rows]
        + [
            pltpu.SemaphoreType.DMA((sections, 2, 2)), pltpu.SemaphoreType.DMA((2, tensors)),
            pltpu.SemaphoreType.DMA((5, n_w)), pltpu.SemaphoreType.DMA((5, n_w)), pltpu.SemaphoreType.DMA((n_w,)),
            pltpu.SemaphoreType.DMA((2, length // (2 * ROWS))), pltpu.SemaphoreType.DMA((2, length // (2 * ROWS))),
        ],
        compiler_params=pltpu.CompilerParams(
            collective_id=0, has_side_effects=True, vmem_limit_bytes=62 << 20
        ),
        name="layer_forward",
    )(text_in, layout_in, text_cot, layout_cot, *ordered, *small)
    return jax.tree.unflatten(out_tree, results[:-2]), tuple(results[-2:])


class Needed(typing.NamedTuple):
    n2: typing.Any
    r2: typing.Any
    downward: typing.Any
    slope: typing.Any
    upward: typing.Any
    n1: typing.Any
    r1: typing.Any
    outward: typing.Any
    low: typing.Any
    act: typing.Any
    qkv: typing.Any
    ctx: typing.Any
    project: typing.Any
    x: typing.Any


class Work(typing.NamedTuple):
    g: typing.Any
    gf: typing.Any
    ga: typing.Any
    dz: typing.Any
    dctx: typing.Any
    sums: typing.Any
    lowT: typing.Any
    raw: typing.Any
    from_sibling: typing.Any
    from_partner: typing.Any
    stage: typing.Any


class Chunk(typing.NamedTuple):
    b: typing.Any
    index: typing.Any
    first: typing.Any
    rows: typing.Any


MATRICES = 4


def matrix_rows(own):
    return own.project.shape[1], own.outward.shape[1], own.upward.shape[1], own.downward.shape[1]


def matrix_starts(own):
    sizes = matrix_rows(own)
    return [sum(sizes[:i]) for i in range(MATRICES + 1)]


def pieces_of(size, step):
    return [(f, step) for f in range(0, size, step)]


def backward_kernel(sections, tensors, chain, in_tree, *refs):
    n_in = in_tree.num_leaves
    hbm_in, refs = refs[:n_in], refs[n_in:]
    (cots, ys, lang_ids, gains), refs = (refs[0:2], refs[2:4], refs[4], refs[5:7]), refs[7:]
    (results, small_out, text_out, layout_out, grad_out, layout_grad_out, near_hbm, cross_hbm), refs = (
        (refs[0:2], *refs[2:7], refs[7:9], refs[9:11]), refs[11:]
    )
    n_work = len(Work._fields)
    work, refs = (Work(*refs[:n_work]), Work(*refs[n_work : 2 * n_work])), refs[2 * n_work :]
    plain, refs = refs[: n_in - 2 * MATRICES], refs[n_in - 2 * MATRICES :]
    flipped, small_got, small_sum, refs = refs[0], refs[1], refs[2], refs[3:]
    in_sem, cot_sem, hop_send, hop_recv, sib_send, sib_recv, send, recv, stage_sem, out_sem, *refs = refs
    small_send, small_recv, page_send, page_recv = refs
    section, d, t = lax.axis_index("section"), lax.axis_index("dp"), lax.axis_index("tensor")
    core, chip = t % 2, t // 2
    sibling = {"tensor": t + 1 - 2 * core}
    partner = {"tensor": (t + tensors // 2) % tensors}
    near, cross = {"dp": d + 1 - 2 * (d % 2)}, {"dp": 3 - d}
    outer = (d == 0) | (d == 3)
    other = {"section": 1 - section}
    hbm, probs_hbm = jax.tree.unflatten(in_tree, hbm_in)
    starts = [matrix_starts(own) for own in hbm]

    plain = list(plain)
    views = []
    for b in range(2):
        fields = {}
        for name, value in hbm[b]._asdict().items():
            if name in Weights._fields:
                i = Weights._fields.index(name)
                fields[name] = work[b].raw.at[:, pl.ds(starts[b][i], starts[b][i + 1] - starts[b][i])]
            else:
                fields[name] = plain.pop(0)
        views.append(Needed(**fields))
    probs_in = plain.pop(0)
    flat_views = jax.tree.leaves((tuple(views), probs_in))
    flat_copies = [pltpu.make_async_copy(a, v, in_sem.at[i]) for i, (a, v) in enumerate(zip(hbm_in, flat_views))]
    loads, probs_copy = jax.tree.unflatten(in_tree, flat_copies)
    length = work[0].gf.shape[0]
    local_heads = probs_in.shape[1]
    blocks = [slice(c, c + 2 * ROWS) for c in range(0, length, 2 * ROWS)]
    cot_copies = (
        pltpu.make_async_copy(cots[0], work[0].g, cot_sem.at[0]),
        pltpu.make_async_copy(cots[1], flipped, cot_sem.at[1]),
    )

    @pl.when(section == 1)
    def _():
        start(*cot_copies)

    start(*flat_copies)
    greet(section, t, sections, tensors, (near, cross) if chain else ())

    part_length = text_out.shape[1]
    micro, page = core, chip
    kinds = ((grad_out, layout_grad_out), (text_out, layout_out))
    pages = ((work[0].g, flipped), ys)

    def page_part(g, q, a):
        span = pl.ds(q * part_length, part_length)
        return pages[g][a].at[span] if a == 0 else pages[g][a].at[:, span]

    def each_page(g, act):
        for q in range(tensors):
            for a in range(2):
                here = (micro == g) & (t == q)

                @pl.when((section == g) & here)
                def _():
                    act(g, q, a, True)

                @pl.when((section == g) & jnp.logical_not(here))
                def _():
                    act(g, q, a, False)

    def page_copy(g, q, a):
        return remote(
            page_part(g, q, a), kinds[g][a].at[page], page_send.at[q, a], page_recv.at[g, a, page],
            {"section": micro, "tensor": q},
        )

    def page_start(g, q, a, here):
        if here:
            pltpu.make_async_copy(page_part(g, q, a), kinds[g][a].at[page], page_recv.at[g, a, page]).start()
        else:
            page_copy(g, q, a).start()

    def page_sent(g, q, a, here):
        if not here:
            page_copy(g, q, a).wait_send()

    each_page(1, page_start)

    def hop(b, n):
        part = work[b].g.at[blocks[n]]
        return remote(part, part, hop_send.at[b, n], hop_recv.at[b, n], other)

    step = 2 * ROWS
    up_first, down_first = starts[0][2], starts[0][3]
    up_count, down_count = (starts[0][3] - up_first) // step, (starts[0][4] - down_first) // step
    n_feed = up_count + down_count
    chunks = [Chunk(0, k, up_first + k * step, step) for k in range(n_feed)]
    later = [(1, 0, starts[1][MATRICES])]
    later += [(0, f, n) for f, n in pieces_of(starts[0][1], 192)]
    later += [(0, starts[0][1] + f, n) for f, n in pieces_of(starts[0][2] - starts[0][1], 64)]
    chunks += [Chunk(b, n_feed + i, f, n) for i, (b, f, n) in enumerate(later)]

    def feed_chunk(k):
        return Chunk(0, k, pl.multiple_of(up_first + k * step, 16), step)

    def span(ref, c):
        return ref.at[pl.ds(c.first, c.rows)]

    def to_sibling(c, j):
        w = work[c.b]
        return remote(
            span(w.raw.at[2 * j + 1 - core], c), span(w.from_sibling.at[j], c),
            sib_send.at[c.index, j], sib_recv.at[c.index, j], sibling,
        )

    def mine(c):
        return span(work[c.b].raw.at[t], c)

    def theirs(c):
        return span(work[c.b].raw.at[2 * (1 - chip) + core], c)

    def to_partner(c):
        return remote(
            theirs(c), span(work[c.b].from_partner, c), send.at[0, c.index], recv.at[0, c.index], partner
        )

    def to_near(c):
        return remote(mine(c), span(near_hbm[c.b], c), send.at[1, c.index], recv.at[1, c.index], near)

    def to_cross(c):
        return remote(mine(c), span(cross_hbm[c.b], c), send.at[2, c.index], recv.at[2, c.index], cross)

    def total_to_near(c):
        return remote(
            span(work[c.b].from_partner, c), span(results[c.b], c), send.at[3, c.index], recv.at[3, c.index], near
        )

    def out_copy(c, source):
        return pltpu.make_async_copy(span(source, c), span(results[c.b], c), out_sem.at[c.index])

    def added(target, *sources):
        target[...] = sum(s[...].astype(F32) for s in sources).astype(BF)

    def staged(c, source):
        target = work[c.b].stage.at[pl.ds(0, c.rows)]
        copy = pltpu.make_async_copy(span(source, c), target, stage_sem.at[0])
        copy.start()
        copy.wait()
        return target

    def send_to_sibling(c):
        for j in range(tensors // 2):
            to_sibling(c, j).start()

    def stage_sibling(c):
        w = work[c.b]
        for j in range(tensors // 2):
            to_sibling(c, j).wait_recv()
        added(theirs(c), theirs(c), span(w.from_sibling.at[1 - chip], c))
        to_partner(c).start()
        added(mine(c), mine(c), span(w.from_sibling.at[chip], c))

    def stage_partner(c):
        to_partner(c).wait_recv()
        added(mine(c), mine(c), span(work[c.b].from_partner, c))
        if not chain:
            out_copy(c, work[c.b].raw.at[t]).start()
            return

        @pl.when(outer)
        def _():
            to_near(c).start()

    def stage_near(c):
        @pl.when(jnp.logical_not(outer))
        def _():
            to_near(c).wait_recv()
            added(mine(c), mine(c), staged(c, near_hbm[c.b]))
            to_cross(c).start()

    def stage_cross(c):
        @pl.when(jnp.logical_not(outer))
        def _():
            to_cross(c).wait_recv()
            total = work[c.b].from_partner
            added(span(total, c), mine(c), staged(c, cross_hbm[c.b]))
            total_to_near(c).start()
            out_copy(c, total).start()

    def feed_products():
        own, w = views[0], work[0]
        w.lowT[...] = own.low[...].T

        @pl.loop(0, up_count)
        def _(k):
            rows = pl.ds(pl.multiple_of(k * step, step), step)
            for q in range(tensors):
                w.raw[q, pl.ds(pl.multiple_of(up_first + k * step, 16), step), :] = dot(
                    w.lowT[rows, :], own.slope[q]
                ).astype(BF)
            send_to_sibling(feed_chunk(k))

        @pl.loop(0, down_count)
        def _(k):
            lanes = pl.ds(pl.multiple_of(k * step, step), step)
            for q in range(tensors):
                w.raw[q, pl.ds(pl.multiple_of(down_first + k * step, 16), step), :] = dot(
                    own.act[q, :, lanes].T, w.gf[...]
                ).astype(BF)
            send_to_sibling(feed_chunk(up_count + k))

    def later_product(c):
        own, w = views[c.b], work[c.b]
        for q in range(tensors):
            for i in range(MATRICES):
                first = max(c.first, starts[c.b][i])
                last = min(c.first + c.rows, starts[c.b][i + 1])
                if first >= last:
                    continue
                rows = slice(first - starts[c.b][i], last - starts[c.b][i])
                if i == 0:
                    value = dot(own.qkv[q, rows, :], own.x[...])
                elif i == 1:
                    value = dot(own.ctx[q, rows, :], w.ga[...])
                elif i == 2:
                    value = dot(w.lowT[rows, :], own.slope[q])
                else:
                    value = dot(own.act[q, :, rows].T, w.gf[...])
                w.raw[q, first:last, :] = value.astype(BF)
        send_to_sibling(c)

    @pl.when(section == 1)
    def _():
        wait(*cot_copies)
        work[1].g[...] = flipped[...].T

    for b in range(2):
        work[b].sums[...] = jnp.zeros(work[b].sums.shape, F32)
    for b in (1, 0):
        own_in = loads[b]
        wait(own_in.n2, own_in.r2, own_in.downward, own_in.slope, own_in.upward, own_in.n1, own_in.r1, own_in.outward)
    for n, block in enumerate(blocks):
        for b in (1, 0):
            own, w, gain = views[b], work[b], gains[b]

            @pl.when(section == 0)
            def _():
                hop(b, n).wait_recv()

            g, normed = w.g[block].astype(F32), own.n2[block].astype(F32)
            low = norm_rows_back(g, normed, own.r2[block], gain[1:2])
            w.dz[block] = low
            w.gf[block] = low.astype(BF)
            w.sums[1:2] += jnp.sum(g * normed, axis=0, keepdims=True)
            w.sums[3:4] += jnp.sum(g, axis=0, keepdims=True)

            @pl.loop(0, tensors)
            def _(q):
                d_act = dot(w.gf[block], own.downward[q], NT)
                d_pre = (d_act * own.slope[q, block].astype(F32)).astype(BF)
                own.slope[q, block] = d_pre
                w.dz[block] += dot(d_pre, own.upward[q], NT)

            g, normed = w.dz[block], own.n1[block].astype(F32)
            low = norm_rows_back(g, normed, own.r1[block], gain[0:1])
            w.dz[block] = low
            w.ga[block] = low.astype(BF)
            w.sums[0:1] += jnp.sum(g * normed, axis=0, keepdims=True)
            w.sums[2:3] += jnp.sum(g, axis=0, keepdims=True)
            for q in range(tensors):
                w.dctx[q, :, block] = dot(own.outward[q], w.ga[block], NT).astype(BF)

    wait(loads[0].low, loads[0].act)

    @pl.when(section == 0)
    def _():
        feed_products()

    wait(loads[0].qkv, loads[1].qkv, probs_copy)
    qkv = (views[0].qkv, views[1].qkv)
    text_rows, layout_rows = slice(0, HEAD_TEXT), slice(HEAD_TEXT, HEAD_TEXT + HEAD_LAYOUT)

    @pl.loop(0, tensors)
    def _(q):
        @pl.when((section == 0) & (q < n_feed // 2))
        def _():
            stage_sibling(feed_chunk(2 * q))
            stage_sibling(feed_chunk(2 * q + 1))

        @pl.when((section == 0) & (q >= 2))
        def _():
            stage_partner(feed_chunk(q - 2))

        for local in range(local_heads):
            dcT = jnp.concatenate(
                [work[b].dctx[q, local * SIZES[b] : (local + 1) * SIZES[b], :] for b in range(2)]
                + [jnp.zeros((128 - sum(SIZES), length), BF)], axis=0,
            )
            dc = dcT.T
            lane = lax.broadcasted_iota(jnp.int32, dc.shape, 1)
            dc_layout = jnp.where(lane >= HEAD_TEXT, dc, jnp.zeros_like(dc))
            qT, kT, vT = (head_rows(qkv, q, kind, local, SCALES if kind == 0 else None) for kind in range(3))
            low = probs_in[q, local]
            probs = low.astype(F32)
            both = dot(dc, vT)
            ds_both = (probs * (both - jnp.sum(probs * both, axis=-1, keepdims=True))).astype(BF)
            single = dot(dc_layout, vT)
            ds_layout = (probs * (single - jnp.sum(probs * single, axis=-1, keepdims=True))).astype(BF)
            dvT = dot(dcT, low)
            put_head(qkv, q, 2, local, 0, dvT[text_rows])
            put_head(qkv, q, 2, local, 1, dvT[layout_rows])
            put_head(qkv, q, 0, local, 0, dot(kT[text_rows], ds_both, NT) * SCALES[0])
            put_head(qkv, q, 1, local, 0, dot(qT[text_rows], ds_both))
            put_head(qkv, q, 0, local, 1, dot(kT[layout_rows], ds_layout, NT) * SCALES[1])
            put_head(qkv, q, 1, local, 1, dot(qT[layout_rows], ds_layout))

    wait(loads[0].project, loads[1].project)
    page_sum = jnp.zeros((1, work[0].dz.shape[1]), F32)
    for n, block in enumerate(blocks):
        for b in (1, 0):
            down = work[b].dz[block]
            for q in range(tensors):
                down += dot(qkv[b][q, :, block].T, views[b].project[q])
            down = down.astype(BF)
            work[b].g[block] = down
            if b == 0:
                page_sum += jnp.sum(down.astype(F32), axis=0, keepdims=True)

            @pl.when(section == 1)
            def _():
                hop(b, n).start()

    wait(loads[1].low, loads[1].act)
    work[1].lowT[...] = views[1].low[...].T
    for own_in in loads:
        wait(own_in.ctx, own_in.x)
    for c in chunks[n_feed:]:
        later_product(c)

    @pl.when(section == 1)
    def _():
        feed_products()

        @pl.loop(0, n_feed)
        def _(k):
            stage_sibling(feed_chunk(k))

    for c in chunks[n_feed:]:
        stage_sibling(c)

    @pl.when(section == 0)
    def _():
        flipped[...] = work[1].g[...].T
        each_page(0, page_start)

    at_page = (lax.broadcasted_iota(jnp.int32, lang_ids.shape, 0) == t % 2) & (
        lax.broadcasted_iota(jnp.int32, lang_ids.shape, 1) == t // 2
    )
    group = jnp.sum(jnp.where(at_page, lang_ids[...], 0), axis=(0, 1), keepdims=True)
    n_lang = small_out.shape[1] - 8
    chosen = (lax.broadcasted_iota(jnp.int32, (n_lang, 1), 0) == group) & (section == 0)
    small_sum[0, 0:n_lang] = jnp.where(chosen, page_sum, 0.0)
    small_sum[0, n_lang : n_lang + 4] = work[0].sums[...]
    small_sum[0, n_lang + 4 : n_lang + 8] = jnp.zeros((4, small_out.shape[2]), F32)
    small_sum[0, n_lang + 4 : n_lang + 8, : work[1].sums.shape[1]] = work[1].sums[...]

    def small_copy(i, device):
        return remote(small_sum.at[i], small_got.at[i], small_send.at[i], small_recv.at[i], device)

    if chain:
        small_copy(0, sibling).start()
    stages = [stage_partner] + ([stage_near, stage_cross] if chain else [])
    for turn in range(len(chunks) + len(stages) - 1):
        for lag, stage in enumerate(stages):
            k = turn - lag
            if not 0 <= k < len(chunks):
                continue
            if stage is stage_partner and k < 2:

                @pl.when(section == 1)
                def _():
                    stage_partner(chunks[k])
            else:
                stage(chunks[k])
        if not chain:
            continue
        if turn == 0:
            small_copy(0, sibling).wait_recv()
            small_sum[1] = small_sum[0] + small_got[0]
            small_copy(1, partner).start()
        if turn == 1:
            small_copy(1, partner).wait_recv()
            small_sum[2] = small_sum[1] + small_got[1]
            small_copy(2, near).start()
        if turn == 2:
            small_copy(2, near).wait_recv()
            small_sum[3] = small_sum[2] + small_got[2]

            @pl.when(jnp.logical_not(outer))
            def _():
                small_copy(3, cross).start()

        if turn == 4:
            @pl.when(jnp.logical_not(outer))
            def _():
                small_copy(3, cross).wait_recv()
                small_sum[4] = small_sum[3] + small_got[3]
                small_copy(4, near).start()

        if turn == 6:
            @pl.when(outer)
            def _():
                small_copy(4, near).wait_recv()
                small_sum[4] = small_got[4]

            small_sum[5] = small_sum[4]
            small_copy(5, other).start()
        if turn == 8:
            small_copy(5, other).wait_recv()
            small_out[0] = small_sum[5]
            small_out[1] = small_got[5]

    if chain:
        for i, device in enumerate((sibling, partner, near)):
            small_copy(i, device).wait_send()

        @pl.when(jnp.logical_not(outer))
        def _():
            small_copy(3, cross).wait_send()
            small_copy(4, near).wait_send()

        small_copy(5, other).wait_send()
    else:
        small_out[0] = small_sum[0]
        small_out[1] = small_sum[0]

    @pl.when(section == 1)
    def _():
        for b in range(2):
            for n in range(len(blocks)):
                hop(b, n).wait_send()

    for c in chunks:
        for j in range(tensors // 2):
            to_sibling(c, j).wait_send()
        to_partner(c).wait_send()
        if not chain:
            out_copy(c, work[c.b].from_partner).wait()
            continue

        @pl.when(outer)
        def _():
            to_near(c).wait_send()
            total_to_near(c).wait_recv()

        @pl.when(jnp.logical_not(outer))
        def _():
            to_cross(c).wait_send()
            total_to_near(c).wait_send()
            out_copy(c, work[c.b].from_partner).wait()

    for g in range(sections):
        each_page(g, page_sent)
        for a in range(2):
            for j in range(2):
                dst = kinds[g][a].at[j]
                remote(dst, dst, page_send.at[0, a], page_recv.at[g, a, j], partner).wait_recv()


def layer_backward(mesh, x, y, probs, kept, weights, cots, norms, lang_ids, n_lang):
    sections, dp, tensors = mesh.shape["section"], mesh.shape["dp"], mesh.shape["tensor"]
    chain = dp == 4
    needed = tuple(
        Needed(
            n2=k.n2, r2=k.r2, downward=w.downward, slope=k.slope, upward=w.upward, n1=k.n1, r1=k.r1,
            outward=w.outward, low=k.low, act=k.act, qkv=k.qkv, ctx=k.ctx, project=w.project, x=rows,
        )
        for k, w, rows in zip(kept, weights, x)
    )
    flat_in, in_tree = jax.tree.flatten((needed, probs))
    plain = [v for own in needed for name, v in own._asdict().items() if name not in Weights._fields] + [probs]
    stacks = [(matrix_starts(own)[MATRICES], rows.shape[1]) for own, rows in zip(needed, x)]
    length = x[0].shape[0]
    work = []
    for own, rows, (count, width), staging in zip(needed, x, stacks, (2 * ROWS, stacks[1][0])):
        work += Work(
            g=shape(rows.shape), gf=shape(rows.shape), ga=shape(rows.shape), dz=shape(rows.shape, F32),
            dctx=shape(own.ctx.shape), sums=shape((4, width), F32), lowT=shape((width, length)),
            raw=shape((tensors, count, width)), from_sibling=shape((tensors // 2, count, width)),
            from_partner=shape((count, width)), stage=shape((staging, width)),
        )
    small = shape((2, n_lang + 8, x[0].shape[1]), F32)
    text_page = shape((2, length // tensors, x[0].shape[1]))
    layout_page = shape((2, x[1].shape[1], length // tensors))
    summed = [shape(s) for s in stacks]
    own = needed[0]
    n_feed = (own.upward.shape[1] + own.downward.shape[1]) // (2 * ROWS)
    n_chunks = n_feed + 1 + own.project.shape[1] // 192 + own.outward.shape[1] // 64
    n_blocks = length // (2 * ROWS)
    dma = pltpu.SemaphoreType.DMA
    results = pl.pallas_call(
        functools.partial(backward_kernel, sections, tensors, chain, in_tree),
        out_shape=summed + [small, text_page, layout_page, text_page, layout_page] + summed * 2,
        in_specs=[ANY] * (len(flat_in) + 4) + [VMEM] * 3,
        out_specs=[ANY] * 2 + [VMEM] + [ANY] * 8,
        scratch_shapes=vmem_like(work) + vmem_like(plain)
        + [pltpu.VMEM(cots[1].shape, BF)] + [pltpu.VMEM((6,) + small.shape[1:], F32)] * 2
        + [dma((len(flat_in),)), dma((2,)), dma((2, n_blocks)), dma((2, n_blocks))]
        + [dma((n_chunks, tensors // 2))] * 2 + [dma((4, n_chunks))] * 2 + [dma((1,)), dma((n_chunks,))]
        + [dma((6,))] * 2 + [dma((tensors, 2)), dma((sections, 2, 2))],
        compiler_params=pltpu.CompilerParams(
            collective_id=1, has_side_effects=True, vmem_limit_bytes=64 << 20
        ),
        name="layer_backward",
    )(*flat_in, *cots, *y, lang_ids, norms[0][0], norms[1][0])
    totals, small, pages = results[:2], results[2], results[3:7]
    if not chain:
        totals = lax.psum(tuple(totals), "dp")
        both = lax.psum(small[0], ("dp", "tensor"))
        small = jnp.stack([both, lax.ppermute(both, "section", [(0, 1), (1, 0)])])
    return totals, small, pages


def widen_kernel(section_rows, n_pages, *refs):
    totals, small, pages, refs = refs[0:2], refs[2], refs[3 : 3 + n_pages], refs[3 + n_pages :]
    (lang, *norm_outs), page_outs, outs = refs[0:5], refs[5 : 5 + n_pages], refs[5 + n_pages :]
    n = len(outs) // 2
    for b in range(2):
        at = 0
        for out in outs[b * n : (b + 1) * n]:
            for c in range(0, out.shape[0], 48):
                out[c : c + 48] = totals[b][at + c : at + c + 48].astype(F32)
            at += out.shape[0]
    n_lang = lang.shape[0]
    lang[...] = jnp.where(lax.axis_index("section") == 0, small[0, :n_lang], small[1, :n_lang])
    for i, out in enumerate(norm_outs):
        first = n_lang + 2 * i
        out[...] = small[0, first : first + 2, : out.shape[1]]
    for source, out in zip(pages, page_outs):
        out[...] = source[...]


def widen(totals, small, pages, shards, n_lang):
    widths = [total.shape[1] for total in totals]
    outs = [shape((n_lang, widths[0]), F32)] + [shape((2, w), F32) for w in widths for _ in range(2)]
    outs += [shape(page.shape) for page in pages]
    outs += [shape(m.shape, F32) for own in shards for m in own]
    results = pl.pallas_call(
        functools.partial(widen_kernel, 2, len(pages)), out_shape=outs,
        in_specs=[VMEM] * (3 + len(pages)), out_specs=[VMEM] * len(outs),
        compiler_params=pltpu.CompilerParams(vmem_limit_bytes=48 << 20), name="widen",
    )(*totals, small, *pages)
    return results[0], results[1:5], results[5:9], results[9:13], results[13:17]


def per_device(
    mesh,
    text_input,
    layout_input,
    text_cotangent,
    layout_cotangent,
    page_counts,
    pad_mask,
    lang_ids,
    lang_table,
    text_project,
    text_outward,
    text_upward,
    text_downward,
    text_gains,
    text_biases,
    layout_project,
    layout_outward,
    layout_upward,
    layout_downward,
    layout_gains,
    layout_biases,
):
    def flat(project):
        return jnp.transpose(project[0], (1, 2, 0)).reshape(-1, project.shape[1])

    def flipped(block):
        return jnp.transpose(block[0], (0, 2, 1))

    shards = (
        Weights(flat(text_project), text_outward[0], text_upward[0], text_downward[0]),
        Weights(flat(layout_project), layout_outward[0], layout_upward[0], layout_downward[0]),
    )
    norms = ((text_gains[0], text_biases[0]), (layout_gains[0], layout_biases[0]))
    marks = (pad_mask, page_counts, lang_ids, lang_table)
    (x, y, probs, kept, weights), cots = layer_forward(
        mesh, text_input[0], flipped(layout_input), text_cotangent[0], flipped(layout_cotangent), shards, norms, marks
    )
    n_lang = lang_table.shape[0]
    totals, small, pages = layer_backward(mesh, x, y, probs, kept, weights, cots, norms, lang_ids, n_lang)
    lang_sum, norm_sums, pages, text_sums, layout_sums = widen(totals, small, pages, shards, n_lang)
    text_out, layout_out, text_grad, layout_grad = pages

    def unflat(grad, like):
        return jnp.transpose(grad.reshape(like.shape[2], like.shape[3], like.shape[1]), (2, 0, 1))[None]

    unflip = lambda block: jnp.transpose(block, (0, 2, 1))[None]
    return (
        text_out[None], unflip(layout_out), text_grad[None], unflip(layout_grad), lang_sum,
        unflat(text_sums[0], text_project), *(s[None] for s in text_sums[1:]), norm_sums[0][None], norm_sums[1][None],
        unflat(layout_sums[0], layout_project), *(s[None] for s in layout_sums[1:]),
        norm_sums[2][None], norm_sums[3][None],
    )


def solution(mesh):
    tokens = P("section", "dp", "tensor", None)
    weight_specs = (
        P("section", None, None, "tensor"), P("section", "tensor", None), P("section", None, "tensor"),
        P("section", "tensor", None), P("section", None, None), P("section", None, None),
    )
    in_specs = (tokens,) * 4 + (P(None, "dp"), P(None, "dp", None), P(None, "dp"), P()) + weight_specs * 2
    out_specs = (tokens,) * 4 + (P(),) + weight_specs * 2
    return jax.shard_map(
        functools.partial(per_device, mesh), mesh=mesh, in_specs=in_specs, out_specs=out_specs, check_vma=False
    )
```

```python
import functools
import math
import typing

import jax
import jax.numpy as jnp
from jax import lax
from jax.experimental import pallas as pl
from jax.experimental.pallas import tpu as pltpu
from jax.sharding import PartitionSpec as P

HEAD_TEXT = 64
HEAD_LAYOUT = 16
EPSILON = 1e-05
NEGATIVE = -1e30
HIGH = lax.Precision.HIGHEST
MESH = pl.DeviceIdType.MESH
BF = jnp.bfloat16
F32 = jnp.float32
ANY = pl.BlockSpec(memory_space=pl.ANY)


def remote(src, dst, send, recv, device):
    return pltpu.make_async_remote_copy(
        src_ref=src, dst_ref=dst, send_sem=send, recv_sem=recv, device_id=device, device_id_type=MESH
    )


def greet(section, tensor, sections, tensors, extra=()):
    barrier = pltpu.get_barrier_semaphore()
    for g in range(sections):
        for q in range(tensors):

            @pl.when((section != g) | (tensor != q))
            def _():
                pl.semaphore_signal(
                    barrier, inc=1, device_id={"section": g, "tensor": q}, device_id_type=MESH
                )

    for device in extra:
        pl.semaphore_signal(barrier, inc=1, device_id=device, device_id_type=MESH)
    pl.semaphore_wait(barrier, sections * tensors - 1 + len(extra))


GELU_P = 0.3275911
GELU_A = (0.254829592, -0.284496736, 1.421413741, -1.453152027, 1.061405429)
NN = (((1,), (0,)), ((), ()))
NT = (((1,), (1,)), ((), ()))
SCALES = (1.0 / math.sqrt(HEAD_TEXT), 1.0 / math.sqrt(HEAD_LAYOUT))
SIZES = (HEAD_TEXT, HEAD_LAYOUT)
ROWS = 128


class Weights(typing.NamedTuple):
    project: typing.Any
    outward: typing.Any
    upward: typing.Any
    downward: typing.Any


class Kept(typing.NamedTuple):
    qkv: typing.Any
    ctx: typing.Any
    n1: typing.Any
    r1: typing.Any
    low: typing.Any
    act: typing.Any
    slope: typing.Any
    n2: typing.Any
    r2: typing.Any


def dot(a, b, dims=NN):
    return lax.dot_general(a, b, dims, preferred_element_type=F32)


def gelu_pair(u):
    t = 1.0 / (1.0 + (GELU_P / math.sqrt(2.0)) * jnp.abs(u))
    e = jnp.exp(-0.5 * (u * u))
    a1, a2, a3, a4, a5 = (0.5 * a for a in GELU_A)
    tail = ((((a5 * t + a4) * t + a3) * t + a2) * t + a1) * t * e
    cdf = jnp.where(u >= 0, 1.0 - tail, tail)
    return u * cdf, cdf + u * e * (1.0 / math.sqrt(2.0 * math.pi))


def norm_rows(z, gain, offset):
    center = z - jnp.mean(z, axis=-1, keepdims=True)
    inverse = lax.rsqrt(jnp.mean(center * center, axis=-1, keepdims=True) + EPSILON)
    normed = center * inverse
    return normed * gain + offset, normed, inverse


def norm_rows_back(g, n, r, gain):
    t = g * gain
    return r * (t - jnp.mean(t, axis=-1, keepdims=True) - n * jnp.mean(t * n, axis=-1, keepdims=True))


class Staged:
    def __init__(self, tree, hbm, vmem, sem, inward):
        self.tree, self.vmem = tree, list(vmem)
        pairs = zip(hbm, vmem) if inward else zip(vmem, hbm)
        self.copies = [pltpu.make_async_copy(a, b, sem.at[i]) for i, (a, b) in enumerate(pairs)]

    def refs(self):
        return jax.tree.unflatten(self.tree, self.vmem)

    def parts(self):
        return jax.tree.unflatten(self.tree, self.copies)

    def start(self):
        for copy in self.copies:
            copy.start()

    def wait(self):
        for copy in self.copies:
            copy.wait()


def start(*copies):
    for copy in copies:
        copy.start()


def wait(*copies):
    for copy in copies:
        copy.wait()


def head_rows(stacks, slot, kind, local, scales=None):
    rows = []
    for b in range(2):
        first = kind * (stacks[b].shape[1] // 3) + local * SIZES[b]
        piece = stacks[b][slot, first : first + SIZES[b], :]
        rows.append(piece if scales is None else piece * BF(scales[b]))
    rows.append(jnp.zeros((128 - sum(SIZES), rows[0].shape[1]), BF))
    return jnp.concatenate(rows, axis=0)


def put_head(stacks, slot, kind, local, b, value):
    first = kind * (stacks[b].shape[1] // 3) + local * SIZES[b]
    stacks[b][slot, first : first + SIZES[b], :] = value.astype(BF)


def slot_of(u, core, chip):
    return ((chip + u // 2) % 2) * 2 + (core + u % 2) % 2


def forward_kernel(sections, tensors, shared, in_tree, out_tree, *refs):
    n_w, n_out = len(shared), out_tree.num_leaves
    sources = (refs[0:2], refs[2:4])
    shards = refs[4 : 4 + n_w]
    pad_mask, counts, lang_ids, lang_table, *norms = refs[4 + n_w : 12 + n_w]
    rest = refs[12 + n_w :]
    hbm_out, cots_out, rest = rest[:n_out], rest[n_out : n_out + 2], rest[n_out + 2 :]
    outgoing = Staged(out_tree, hbm_out, rest[:n_out], rest[n_out], False)
    rest = rest[n_out + 1 :]
    flipped, raw_x, y_narrow, *rest = rest
    nats, totals, rest = rest[0:2], rest[2:4], rest[4:]
    page_send, page_recv, w_send, w_recv, own_sem, hop_send, hop_recv, cot_sem = rest
    x, y_pages, probs_out, kept, weights = outgoing.refs()
    y = (y_pages[0], y_narrow)
    x_out, y_out, probs_copy, kept_out, weights_out = outgoing.parts()
    section, d, t = lax.axis_index("section"), lax.axis_index("dp"), lax.axis_index("tensor")
    core, chip, half_index = t % 2, t // 2, d % 2
    sibling, partner = t + 1 - 2 * core, (t + tensors // 2) % tensors
    mate = d + 1 - 2 * half_index
    micro, page = core, chip
    part_length = sources[0][0].shape[1]
    length = x[0].shape[0]
    blocks = [slice(c, c + 2 * ROWS) for c in range(0, length, 2 * ROWS)]
    full = (
        weights[0].project, weights[1].project, weights[0].outward, weights[0].upward,
        weights[0].downward, weights[1].outward, weights[1].upward, weights[1].downward,
    )
    greet(section, t, sections, tensors, ({"dp": mate},) if any(shared) else ())

    def half_of(ref, i, which):
        count = shards[i].shape[0] // 2
        return ref.at[pl.ds(pl.multiple_of(which * count, 16), count)] if shared[i] else ref

    def to_partner(i):
        return remote(
            half_of(shards[i], i, half_index), half_of(full[i].at[t], i, half_index),
            w_send.at[0, i], w_recv.at[0, i], {"tensor": partner},
        )

    def to_sibling(i):
        return remote(shards[i], full[i].at[t], w_send.at[1, i], w_recv.at[1, i], {"tensor": sibling})

    def to_mate(i):
        ref = half_of(full[i].at[partner], i, half_index)
        return remote(ref, ref, w_send.at[2, i], w_recv.at[2, i], {"dp": mate})

    def on_first(i):
        ref = half_of(full[i].at[partner], i, half_index)
        return remote(ref, ref, w_send.at[3, i], w_recv.at[3, i], {"tensor": sibling})

    def on_second(i):
        ref = half_of(full[i].at[partner], i, 1 - half_index)
        return remote(ref, ref, w_send.at[4, i], w_recv.at[4, i], {"tensor": sibling})

    def keep(i):
        return pltpu.make_async_copy(shards[i], full[i].at[t], own_sem.at[i])

    def relay(*which):
        for i in which:
            to_partner(i).wait_recv()
            if shared[i]:
                to_mate(i).start()
            on_first(i).start()

    def relay_second(*which):
        for i in which:
            if shared[i]:
                to_mate(i).wait_recv()
                on_second(i).start()

    def early(*which):
        for i in which:
            keep(i).wait()
            to_sibling(i).wait_recv()

    def late(*which):
        for i in which:
            on_first(i).wait_recv()
            if shared[i]:
                on_second(i).wait_recv()

    def token_slot(g, a, index):
        start_at = pl.multiple_of(index * part_length, part_length)
        target = (raw_x, flipped)[a]
        return target.at[pl.ds(start_at, part_length)] if a == 0 else target.at[:, pl.ds(start_at, part_length)]

    def over_pages(g, act):
        for j in range(2):
            target = 2 * j + section
            here = (section == g) & (t == target)
            for a in range(2):
                act(g, j, a, target, here)

    def page_copy(g, j, a, target):
        return remote(
            sources[g][a].at[j], token_slot(g, a, t), page_send.at[g, j, a], page_recv.at[a, t],
            {"section": g, "tensor": target},
        )

    def page_start(g, j, a, target, here):
        @pl.when(here)
        def _():
            pltpu.make_async_copy(sources[g][a].at[j], token_slot(g, a, t), page_recv.at[a, t]).start()

        @pl.when(jnp.logical_not(here))
        def _():
            page_copy(g, j, a, target).start()

    def page_sent(g, j, a, target, here):
        @pl.when(jnp.logical_not(here))
        def _():
            page_copy(g, j, a, target).wait_send()

    def pages_arrived(g):
        for a in range(2):
            for q in range(tensors):
                slot = token_slot(g, a, q)
                remote(slot, slot, page_send.at[0, 0, a], page_recv.at[a, q], {"tensor": sibling}).wait_recv()

    def hop(b, n):
        return remote(
            y[b].at[blocks[n]], x[b].at[blocks[n]], hop_send.at[b, n], hop_recv.at[b, n], {"section": 1 - section}
        )

    over_pages(0, page_start)
    for i in range(n_w):
        to_partner(i).start()
        keep(i).start()
    for i in range(n_w):
        to_sibling(i).start()
    over_pages(1, page_start)

    at_page = (lax.broadcasted_iota(jnp.int32, counts.shape, 0) == micro) & (
        lax.broadcasted_iota(jnp.int32, counts.shape, 1) == page
    )

    def own_entry(ref):
        return jnp.sum(jnp.where(at_page, ref[...], 0), axis=(0, 1), keepdims=True)

    positions = lax.broadcasted_iota(jnp.int32, (1, length), 1)
    mask_row = pad_mask[micro, pl.ds(page, 1), :]
    key_mask = (positions < own_entry(counts)) & ((mask_row == 1) | (positions == 0))
    groups = lax.broadcasted_iota(jnp.int32, (lang_table.shape[0], 1), 0)
    lang_row = jnp.sum(jnp.where(groups == own_entry(lang_ids), lang_table[...], 0.0), axis=0, keepdims=True)
    local_heads = weights[0].project.shape[1] // (3 * HEAD_TEXT)
    qkv = (kept[0].qkv, kept[1].qkv)

    @pl.when(section == 0)
    def _():
        pages_arrived(0)
        x[0][...] = (raw_x[...].astype(F32) + lang_row).astype(BF)
        x[1][...] = flipped[...].T
        early(0, 1)

    @pl.when(section == 1)
    def _():
        relay(*range(n_w))
        relay_second(*range(n_w))
        early(*range(n_w))
        late(*range(n_w))
        start(*weights_out[0], *weights_out[1])

    @pl.loop(0, 2)
    def _(half):
        @pl.when((half == 1) & (section == 0))
        def _():
            relay(0, 1)
            relay_second(0)
            late(0, 1)

        for n, block in enumerate(blocks):
            @pl.when((half == 0) & (section == 1))
            def _():
                for b in range(2):
                    hop(b, n).wait_recv()

            @pl.loop(0, 2)
            def _(u):
                slot = slot_of(2 * half + u, core, chip)
                for b in range(2):
                    qkv[b][slot, :, block] = dot(weights[b].project[slot], x[b][block], NT).astype(BF)

        @pl.loop(0, 2)
        def _(u):
            slot = slot_of(2 * half + u, core, chip)
            for local in range(local_heads):
                q = head_rows(qkv, slot, 0, local, SCALES).T
                scores = jnp.where(key_mask, dot(q, head_rows(qkv, slot, 1, local)), NEGATIVE)
                raised = jnp.exp(scores - jnp.max(scores, axis=-1, keepdims=True))
                probs = (raised * (1.0 / jnp.sum(raised, axis=-1, keepdims=True))).astype(BF)
                probs_out[slot, local] = probs
                ctx = dot(head_rows(qkv, slot, 2, local), probs, NT).astype(BF)
                kept[0].ctx[slot, local * HEAD_TEXT : (local + 1) * HEAD_TEXT, :] = ctx[:HEAD_TEXT]
                kept[1].ctx[slot, local * HEAD_LAYOUT : (local + 1) * HEAD_LAYOUT, :] = ctx[
                    HEAD_TEXT : HEAD_TEXT + HEAD_LAYOUT
                ]

    start(probs_copy, *x_out, *(k.qkv for k in kept_out), *(k.ctx for k in kept_out))

    def attend(b):
        gains, biases = norms[2 * b : 2 * b + 2]
        width = x[b].shape[1]
        nats[b][...] = kept[b].ctx[...].reshape(width, length).T
        wide = weights[b].outward[...].reshape(width, width)
        for block in blocks:
            h, n, r = norm_rows(x[b][block].astype(F32) + dot(nats[b][block], wide), gains[0:1], biases[0:1])
            totals[b][0, block] = h
            totals[b][1, block] = jnp.zeros(h.shape, F32)
            kept[b].n1[block] = n.astype(BF)
            kept[b].r1[block] = r
            kept[b].low[block] = h.astype(BF)
        start(kept_out[b].n1, kept_out[b].r1, kept_out[b].low)

    def feed(b, first, which):
        @pl.loop(first, first + 2)
        def _(u):
            slot = slot_of(u, core, chip)
            for block in which:
                act, slope = gelu_pair(dot(kept[b].low[block], weights[b].upward[slot]))
                act = act.astype(BF)
                kept[b].act[slot, block] = act
                kept[b].slope[slot, block] = slope.astype(BF)
                totals[b][1, block] += dot(act, weights[b].downward[slot])

    def finish(b):
        gains, biases = norms[2 * b : 2 * b + 2]
        for n, block in enumerate(blocks):
            feed(b, 2, [block])
            out, normed, r = norm_rows(totals[b][0, block] + totals[b][1, block], gains[1:2], biases[1:2])
            y[b][block] = out.astype(BF)
            kept[b].n2[block] = normed.astype(BF)
            kept[b].r2[block] = r

            @pl.when(section == 0)
            def _():
                hop(b, n).start()

        if b == 1:
            y_pages[1][...] = y_narrow[...].T
        start(y_out[b], kept_out[b].act, kept_out[b].slope, kept_out[b].n2, kept_out[b].r2)

    @pl.when(section == 0)
    def _():
        relay(2, 3)
        early(2)
        late(2)

    attend(0)

    @pl.when(section == 0)
    def _():
        early(3, 4)

    feed(0, 0, blocks)

    @pl.when(section == 0)
    def _():
        relay(4, 5, 6, 7)
        relay_second(3)
        early(5, 6, 7)
        late(5, 6, 7)

    attend(1)
    feed(1, 0, blocks)
    finish(1)

    @pl.when(section == 0)
    def _():
        relay_second(4)
        late(3, 4)

    finish(0)

    @pl.when(section == 0)
    def _():
        start(*weights_out[0], *weights_out[1])
        for b in range(2):
            for n in range(len(blocks)):
                hop(b, n).wait_send()

    for i in range(n_w):
        to_partner(i).wait_send()
        to_sibling(i).wait_send()
        on_first(i).wait_send()
        if shared[i]:
            to_mate(i).wait_send()
            on_second(i).wait_send()
    for g in range(sections):
        over_pages(g, page_sent)

    @pl.when(section == 1)
    def _():
        pages_arrived(1)
        copies = [pltpu.make_async_copy(v, h, cot_sem.at[i]) for i, (v, h) in enumerate(zip((raw_x, flipped), cots_out))]
        start(*copies)
        wait(*copies)

    outgoing.wait()


def vmem_like(tree):
    return [pltpu.VMEM(s.shape, s.dtype) for s in jax.tree.leaves(tree)]


VMEM = pl.BlockSpec(memory_space=pltpu.VMEM)


def shape(dims, dtype=BF):
    return jax.ShapeDtypeStruct(tuple(dims), dtype)


def layer_forward(mesh, text_in, layout_in, text_cot, layout_cot, shards, norms, marks):
    sections, dp, tensors = mesh.shape["section"], mesh.shape["dp"], mesh.shape["tensor"]
    length = text_in.shape[1] * tensors
    rows = (shape((length, text_in.shape[2])), shape((length, layout_in.shape[1])))
    local_heads = shards[0].project.shape[0] // (3 * HEAD_TEXT)
    kept = []
    for x, w in zip(rows, shards):
        units, column = shape((tensors, length, w.upward.shape[1])), shape((length, 1), F32)
        kept.append(Kept(
            qkv=shape((tensors, w.project.shape[0], length)), ctx=shape((tensors, w.outward.shape[0], length)),
            n1=shape(x.shape), r1=column, low=shape(x.shape), act=units, slope=units,
            n2=shape(x.shape), r2=column,
        ))
    weights = tuple(Weights(*(shape((tensors,) + m.shape) for m in w)) for w in shards)
    pages_out = (rows[0], shape((rows[1].shape[1], length)))
    outs = (rows, pages_out, shape((tensors, local_heads, length, length)), tuple(kept), weights)
    flat_out, out_tree = jax.tree.flatten(outs)
    (a, b) = shards
    ordered = (a.project, b.project, a.outward, a.upward, a.downward, b.outward, b.upward, b.downward)
    shared = tuple(dp % 2 == 0 and w.shape[0] >= 512 for w in ordered)
    n_w = len(ordered)
    cots = [rows[0], shape((rows[1].shape[1], length))]
    small = (*marks, *norms[0], *norms[1])
    results = pl.pallas_call(
        functools.partial(forward_kernel, sections, tensors, shared, None, out_tree),
        out_shape=flat_out + cots,
        in_specs=[ANY] * (4 + n_w) + [VMEM] * len(small),
        out_specs=[ANY] * (len(flat_out) + 2),
        scratch_shapes=vmem_like(flat_out) + [pltpu.SemaphoreType.DMA((len(flat_out),))]
        + [pltpu.VMEM(cots[1].shape, BF), pltpu.VMEM(cots[0].shape, BF), pltpu.VMEM(rows[1].shape, BF)]
        + [pltpu.VMEM(x.shape, BF) for x in rows]
        + [pltpu.VMEM((2,) + x.shape, F32) for x in rows]
        + [
            pltpu.SemaphoreType.DMA((sections, 2, 2)), pltpu.SemaphoreType.DMA((2, tensors)),
            pltpu.SemaphoreType.DMA((5, n_w)), pltpu.SemaphoreType.DMA((5, n_w)), pltpu.SemaphoreType.DMA((n_w,)),
            pltpu.SemaphoreType.DMA((2, length // (2 * ROWS))), pltpu.SemaphoreType.DMA((2, length // (2 * ROWS))),
            pltpu.SemaphoreType.DMA((2,)),
        ],
        compiler_params=pltpu.CompilerParams(
            collective_id=0, has_side_effects=True, vmem_limit_bytes=62 << 20
        ),
        name="layer_forward",
    )(text_in, layout_in, text_cot, layout_cot, *ordered, *small)
    return jax.tree.unflatten(out_tree, results[:-2]), tuple(results[-2:])


class Needed(typing.NamedTuple):
    n2: typing.Any
    r2: typing.Any
    downward: typing.Any
    slope: typing.Any
    upward: typing.Any
    n1: typing.Any
    r1: typing.Any
    outward: typing.Any
    low: typing.Any
    act: typing.Any
    qkv: typing.Any
    ctx: typing.Any
    project: typing.Any
    x: typing.Any


class Work(typing.NamedTuple):
    g: typing.Any
    gf: typing.Any
    ga: typing.Any
    dz: typing.Any
    dctx: typing.Any
    sums: typing.Any
    lowT: typing.Any
    raw: typing.Any
    from_sibling: typing.Any
    from_partner: typing.Any


class Chunk(typing.NamedTuple):
    b: typing.Any
    index: typing.Any
    first: typing.Any
    rows: typing.Any


MATRICES = 4


def matrix_rows(own):
    return own.project.shape[1], own.outward.shape[1], own.upward.shape[1], own.downward.shape[1]


def matrix_starts(own):
    sizes = matrix_rows(own)
    return [sum(sizes[:i]) for i in range(MATRICES + 1)]


def pieces_of(size, step):
    return [(f, step) for f in range(0, size, step)]


def backward_kernel(sections, tensors, chain, in_tree, *refs):
    n_in = in_tree.num_leaves
    hbm_in, refs = refs[:n_in], refs[n_in:]
    (cots, ys, lang_ids, gains), refs = (refs[0:2], refs[2:4], refs[4], refs[5:7]), refs[7:]
    results, small_out, page_outs, refs = refs[0:2], refs[2], refs[3:7], refs[7:]
    n_work = len(Work._fields)
    work, refs = (Work(*refs[:n_work]), Work(*refs[n_work : 2 * n_work])), refs[2 * n_work :]
    plain, refs = refs[: n_in - 2 * MATRICES], refs[n_in - 2 * MATRICES :]
    flipped, small_got, small_sum, refs = refs[0], refs[1], refs[2], refs[3:]
    text_out, layout_out, grad_out, layout_grad_out, *refs = refs
    in_sem, cot_sem, hop_send, hop_recv, sib_send, sib_recv, send, recv, credit, out_sem, *refs = refs
    small_send, small_recv, page_send, page_recv, page_out_sem = refs
    section, d, t = lax.axis_index("section"), lax.axis_index("dp"), lax.axis_index("tensor")
    core, chip = t % 2, t // 2
    sibling = {"tensor": t + 1 - 2 * core}
    partner = {"tensor": (t + tensors // 2) % tensors}
    near, cross = {"dp": d + 1 - 2 * (d % 2)}, {"dp": 3 - d}
    outer = (d == 0) | (d == 3)
    other = {"section": 1 - section}
    hbm, probs_hbm = jax.tree.unflatten(in_tree, hbm_in)
    starts = [matrix_starts(own) for own in hbm]

    plain = list(plain)
    views = []
    for b in range(2):
        fields = {}
        for name, value in hbm[b]._asdict().items():
            if name in Weights._fields:
                i = Weights._fields.index(name)
                fields[name] = work[b].raw.at[:, pl.ds(starts[b][i], starts[b][i + 1] - starts[b][i])]
            else:
                fields[name] = plain.pop(0)
        views.append(Needed(**fields))
    probs_in = plain.pop(0)
    flat_views = jax.tree.leaves((tuple(views), probs_in))
    flat_copies = [pltpu.make_async_copy(a, v, in_sem.at[i]) for i, (a, v) in enumerate(zip(hbm_in, flat_views))]
    loads, probs_copy = jax.tree.unflatten(in_tree, flat_copies)
    length = work[0].gf.shape[0]
    local_heads = probs_in.shape[1]
    blocks = [slice(c, c + 2 * ROWS) for c in range(0, length, 2 * ROWS)]
    cot_copies = (
        pltpu.make_async_copy(cots[0], work[0].g, cot_sem.at[0]),
        pltpu.make_async_copy(cots[1], flipped, cot_sem.at[1]),
    )

    @pl.when(section == 1)
    def _():
        start(*cot_copies)

    start(*flat_copies)
    greet(section, t, sections, tensors, (near, cross) if chain else ())

    part_length = text_out.shape[1]
    micro, page = core, chip
    kinds = ((grad_out, layout_grad_out), (text_out, layout_out))
    pages = ((work[0].g, flipped), ys)

    def page_part(g, q, a):
        span = pl.ds(q * part_length, part_length)
        return pages[g][a].at[span] if a == 0 else pages[g][a].at[:, span]

    def each_page(g, act):
        for q in range(tensors):
            for a in range(2):
                here = (micro == g) & (t == q)

                @pl.when((section == g) & here)
                def _():
                    act(g, q, a, True)

                @pl.when((section == g) & jnp.logical_not(here))
                def _():
                    act(g, q, a, False)

    def page_copy(g, q, a):
        return remote(
            page_part(g, q, a), kinds[g][a].at[page], page_send.at[q, a], page_recv.at[g, a, page],
            {"section": micro, "tensor": q},
        )

    def page_start(g, q, a, here):
        if here:
            pltpu.make_async_copy(page_part(g, q, a), kinds[g][a].at[page], page_recv.at[g, a, page]).start()
        else:
            page_copy(g, q, a).start()

    def page_sent(g, q, a, here):
        if not here:
            page_copy(g, q, a).wait_send()

    each_page(1, page_start)

    def hop(b, n):
        part = work[b].g.at[blocks[n]]
        return remote(part, part, hop_send.at[b, n], hop_recv.at[b, n], other)

    step = 2 * ROWS
    up_first, down_first = starts[0][2], starts[0][3]
    up_count, down_count = (starts[0][3] - up_first) // step, (starts[0][4] - down_first) // step
    n_feed = up_count + down_count
    chunks = [Chunk(0, k, up_first + k * step, step) for k in range(n_feed)]
    later = [(1, 0, starts[1][MATRICES])]
    later += [(0, f, n) for f, n in pieces_of(starts[0][1], 192)]
    later += [(0, starts[0][1] + f, n) for f, n in pieces_of(starts[0][2] - starts[0][1], 64)]
    chunks += [Chunk(b, n_feed + i, f, n) for i, (b, f, n) in enumerate(later)]

    def feed_chunk(k):
        return Chunk(0, k, pl.multiple_of(up_first + k * step, 16), step)

    def span(ref, c):
        return ref.at[pl.ds(c.first, c.rows)]

    def to_sibling(c, j):
        w = work[c.b]
        return remote(
            span(w.raw.at[2 * j + 1 - core], c), span(w.from_sibling.at[j], c),
            sib_send.at[c.index, j], sib_recv.at[c.index, j], sibling,
        )

    def mine(c):
        return span(work[c.b].raw.at[t], c)

    def theirs(c):
        return span(work[c.b].raw.at[2 * (1 - chip) + core], c)

    def to_partner(c):
        return remote(
            theirs(c), span(work[c.b].from_partner, c), send.at[0, c.index], recv.at[0, c.index], partner
        )

    def from_near(c):
        return span(work[c.b].from_sibling.at[0], c)

    def from_cross(c):
        return span(work[c.b].from_sibling.at[1], c)

    def to_near(c):
        return remote(mine(c), from_near(c), send.at[1, c.index], recv.at[1, c.index], near)

    def to_cross(c):
        return remote(mine(c), from_cross(c), send.at[2, c.index], recv.at[2, c.index], cross)

    def total_to_near(c):
        return remote(
            span(work[c.b].from_partner, c), from_near(c), send.at[3, c.index], recv.at[3, c.index], near
        )

    def out_copy(c, source):
        return pltpu.make_async_copy(span(source, c), span(results[c.b], c), out_sem.at[c.index])

    def added(target, *sources):
        target[...] = sum(s[...].astype(F32) for s in sources).astype(BF)

    def send_to_sibling(c):
        for j in range(tensors // 2):
            to_sibling(c, j).start()

    def stage_sibling(c):
        w = work[c.b]
        for j in range(tensors // 2):
            to_sibling(c, j).wait_recv()
        added(theirs(c), theirs(c), span(w.from_sibling.at[1 - chip], c))
        to_partner(c).start()
        added(mine(c), mine(c), span(w.from_sibling.at[chip], c))
        if chain:
            @pl.when(jnp.logical_not(outer))
            def _():
                for device in (near, cross):
                    pl.semaphore_signal(credit, inc=1, device_id=device, device_id_type=MESH)

    def stage_partner(c):
        to_partner(c).wait_recv()
        added(mine(c), mine(c), span(work[c.b].from_partner, c))
        if not chain:
            out_copy(c, work[c.b].raw.at[t]).start()
            return

        @pl.when(outer)
        def _():
            pl.semaphore_wait(credit, 1)
            to_near(c).start()

    def stage_near(c):
        @pl.when(jnp.logical_not(outer))
        def _():
            to_near(c).wait_recv()
            added(mine(c), mine(c), from_near(c))
            pl.semaphore_wait(credit, 1)
            to_cross(c).start()

    def stage_cross(c):
        @pl.when(jnp.logical_not(outer))
        def _():
            to_cross(c).wait_recv()
            total = work[c.b].from_partner
            added(span(total, c), mine(c), from_cross(c))
            total_to_near(c).start()
            out_copy(c, total).start()

    def stage_total(c):
        @pl.when(outer)
        def _():
            total_to_near(c).wait_recv()
            out_copy(c, work[c.b].from_sibling.at[0]).start()

    def feed_products():
        own, w = views[0], work[0]
        w.lowT[...] = own.low[...].T

        @pl.loop(0, up_count)
        def _(k):
            rows = pl.ds(pl.multiple_of(k * step, step), step)
            for q in range(tensors):
                w.raw[q, pl.ds(pl.multiple_of(up_first + k * step, 16), step), :] = dot(
                    w.lowT[rows, :], own.slope[q]
                ).astype(BF)
            send_to_sibling(feed_chunk(k))

        @pl.loop(0, down_count)
        def _(k):
            lanes = pl.ds(pl.multiple_of(k * step, step), step)
            for q in range(tensors):
                w.raw[q, pl.ds(pl.multiple_of(down_first + k * step, 16), step), :] = dot(
                    own.act[q, :, lanes].T, w.gf[...]
                ).astype(BF)
            send_to_sibling(feed_chunk(up_count + k))

    def later_product(c):
        own, w = views[c.b], work[c.b]
        for q in range(tensors):
            for i in range(MATRICES):
                first = max(c.first, starts[c.b][i])
                last = min(c.first + c.rows, starts[c.b][i + 1])
                if first >= last:
                    continue
                rows = slice(first - starts[c.b][i], last - starts[c.b][i])
                if i == 0:
                    value = dot(own.qkv[q, rows, :], own.x[...])
                elif i == 1:
                    value = dot(own.ctx[q, rows, :], w.ga[...])
                elif i == 2:
                    value = dot(w.lowT[rows, :], own.slope[q])
                else:
                    value = dot(own.act[q, :, rows].T, w.gf[...])
                w.raw[q, first:last, :] = value.astype(BF)
        send_to_sibling(c)

    @pl.when(section == 1)
    def _():
        wait(*cot_copies)
        work[1].g[...] = flipped[...].T

    for b in range(2):
        work[b].sums[...] = jnp.zeros(work[b].sums.shape, F32)
    for b in (1, 0):
        own_in = loads[b]
        wait(own_in.n2, own_in.r2, own_in.downward, own_in.slope, own_in.upward, own_in.n1, own_in.r1, own_in.outward)
    for n, block in enumerate(blocks):
        for b in (1, 0):
            own, w, gain = views[b], work[b], gains[b]

            @pl.when(section == 0)
            def _():
                hop(b, n).wait_recv()

            g, normed = w.g[block].astype(F32), own.n2[block].astype(F32)
            low = norm_rows_back(g, normed, own.r2[block], gain[1:2])
            w.dz[block] = low
            w.gf[block] = low.astype(BF)
            w.sums[1:2] += jnp.sum(g * normed, axis=0, keepdims=True)
            w.sums[3:4] += jnp.sum(g, axis=0, keepdims=True)

            @pl.loop(0, tensors)
            def _(q):
                d_act = dot(w.gf[block], own.downward[q], NT)
                d_pre = (d_act * own.slope[q, block].astype(F32)).astype(BF)
                own.slope[q, block] = d_pre
                w.dz[block] += dot(d_pre, own.upward[q], NT)

            g, normed = w.dz[block], own.n1[block].astype(F32)
            low = norm_rows_back(g, normed, own.r1[block], gain[0:1])
            w.dz[block] = low
            w.ga[block] = low.astype(BF)
            w.sums[0:1] += jnp.sum(g * normed, axis=0, keepdims=True)
            w.sums[2:3] += jnp.sum(g, axis=0, keepdims=True)
            for q in range(tensors):
                w.dctx[q, :, block] = dot(own.outward[q], w.ga[block], NT).astype(BF)

    wait(loads[0].low, loads[0].act)

    @pl.when(section == 0)
    def _():
        feed_products()

    wait(loads[0].qkv, loads[1].qkv, probs_copy)
    qkv = (views[0].qkv, views[1].qkv)
    text_rows, layout_rows = slice(0, HEAD_TEXT), slice(HEAD_TEXT, HEAD_TEXT + HEAD_LAYOUT)

    @pl.loop(0, tensors)
    def _(q):
        @pl.when((section == 0) & (q < n_feed // 2))
        def _():
            stage_sibling(feed_chunk(2 * q))
            stage_sibling(feed_chunk(2 * q + 1))

        @pl.when((section == 0) & (q >= 2))
        def _():
            stage_partner(feed_chunk(q - 2))

        for local in range(local_heads):
            dcT = jnp.concatenate(
                [work[b].dctx[q, local * SIZES[b] : (local + 1) * SIZES[b], :] for b in range(2)]
                + [jnp.zeros((128 - sum(SIZES), length), BF)], axis=0,
            )
            dc = dcT.T
            lane = lax.broadcasted_iota(jnp.int32, dc.shape, 1)
            dc_layout = jnp.where(lane >= HEAD_TEXT, dc, jnp.zeros_like(dc))
            qT, kT, vT = (head_rows(qkv, q, kind, local, SCALES if kind == 0 else None) for kind in range(3))
            low = probs_in[q, local]
            probs = low.astype(F32)
            both = dot(dc, vT)
            ds_both = (probs * (both - jnp.sum(probs * both, axis=-1, keepdims=True))).astype(BF)
            single = dot(dc_layout, vT)
            ds_layout = (probs * (single - jnp.sum(probs * single, axis=-1, keepdims=True))).astype(BF)
            dvT = dot(dcT, low)
            put_head(qkv, q, 2, local, 0, dvT[text_rows])
            put_head(qkv, q, 2, local, 1, dvT[layout_rows])
            put_head(qkv, q, 0, local, 0, dot(kT[text_rows], ds_both, NT) * SCALES[0])
            put_head(qkv, q, 1, local, 0, dot(qT[text_rows], ds_both))
            put_head(qkv, q, 0, local, 1, dot(kT[layout_rows], ds_layout, NT) * SCALES[1])
            put_head(qkv, q, 1, local, 1, dot(qT[layout_rows], ds_layout))

    wait(loads[0].project, loads[1].project)
    page_sum = jnp.zeros((1, work[0].dz.shape[1]), F32)
    for n, block in enumerate(blocks):
        for b in (1, 0):
            down = work[b].dz[block]
            for q in range(tensors):
                down += dot(qkv[b][q, :, block].T, views[b].project[q])
            down = down.astype(BF)
            work[b].g[block] = down
            if b == 0:
                page_sum += jnp.sum(down.astype(F32), axis=0, keepdims=True)

            @pl.when(section == 1)
            def _():
                hop(b, n).start()

    wait(loads[1].low, loads[1].act)
    work[1].lowT[...] = views[1].low[...].T
    for own_in in loads:
        wait(own_in.ctx, own_in.x)
    for c in chunks[n_feed:]:
        later_product(c)

    @pl.when(section == 1)
    def _():
        feed_products()

        @pl.loop(0, n_feed)
        def _(k):
            stage_sibling(feed_chunk(k))

    for c in chunks[n_feed:]:
        stage_sibling(c)

    @pl.when(section == 0)
    def _():
        flipped[...] = work[1].g[...].T
        each_page(0, page_start)

    at_page = (lax.broadcasted_iota(jnp.int32, lang_ids.shape, 0) == t % 2) & (
        lax.broadcasted_iota(jnp.int32, lang_ids.shape, 1) == t // 2
    )
    group = jnp.sum(jnp.where(at_page, lang_ids[...], 0), axis=(0, 1), keepdims=True)
    n_lang = small_out.shape[1] - 8
    chosen = (lax.broadcasted_iota(jnp.int32, (n_lang, 1), 0) == group) & (section == 0)
    small_sum[0, 0:n_lang] = jnp.where(chosen, page_sum, 0.0)
    small_sum[0, n_lang : n_lang + 4] = work[0].sums[...]
    small_sum[0, n_lang + 4 : n_lang + 8] = jnp.zeros((4, small_out.shape[2]), F32)
    small_sum[0, n_lang + 4 : n_lang + 8, : work[1].sums.shape[1]] = work[1].sums[...]

    def small_copy(i, device):
        return remote(small_sum.at[i], small_got.at[i], small_send.at[i], small_recv.at[i], device)

    if chain:
        small_copy(0, sibling).start()
    stages = [(0, stage_partner)] + ([(2, stage_near), (4, stage_cross), (6, stage_total)] if chain else [])
    for turn in range(len(chunks) + stages[-1][0]):
        for lag, stage in stages:
            k = turn - lag
            if not 0 <= k < len(chunks):
                continue
            if stage is stage_partner and k < 2:

                @pl.when(section == 1)
                def _():
                    stage_partner(chunks[k])
            else:
                stage(chunks[k])
        if not chain:
            continue
        if turn == 0:
            small_copy(0, sibling).wait_recv()
            small_sum[1] = small_sum[0] + small_got[0]
            small_copy(1, partner).start()
        if turn == 1:
            small_copy(1, partner).wait_recv()
            small_sum[2] = small_sum[1] + small_got[1]
            small_copy(2, near).start()
        if turn == 2:
            small_copy(2, near).wait_recv()
            small_sum[3] = small_sum[2] + small_got[2]

            @pl.when(jnp.logical_not(outer))
            def _():
                small_copy(3, cross).start()

        if turn == 4:
            @pl.when(jnp.logical_not(outer))
            def _():
                small_copy(3, cross).wait_recv()
                small_sum[4] = small_sum[3] + small_got[3]
                small_copy(4, near).start()

        if turn == 6:
            @pl.when(outer)
            def _():
                small_copy(4, near).wait_recv()
                small_sum[4] = small_got[4]

            small_sum[5] = small_sum[4]
            small_copy(5, other).start()
        if turn == 8:
            small_copy(5, other).wait_recv()
            small_out[0] = small_sum[5]
            small_out[1] = small_got[5]

    if chain:
        for i, device in enumerate((sibling, partner, near)):
            small_copy(i, device).wait_send()

        @pl.when(jnp.logical_not(outer))
        def _():
            small_copy(3, cross).wait_send()
            small_copy(4, near).wait_send()

        small_copy(5, other).wait_send()
    else:
        small_out[0] = small_sum[0]
        small_out[1] = small_sum[0]

    @pl.when(section == 1)
    def _():
        for b in range(2):
            for n in range(len(blocks)):
                hop(b, n).wait_send()

    for c in chunks:
        for j in range(tensors // 2):
            to_sibling(c, j).wait_send()
        to_partner(c).wait_send()
        if not chain:
            out_copy(c, work[c.b].from_partner).wait()
            continue

        @pl.when(outer)
        def _():
            to_near(c).wait_send()

        @pl.when(jnp.logical_not(outer))
        def _():
            to_cross(c).wait_send()
            total_to_near(c).wait_send()

        out_copy(c, work[c.b].from_partner).wait()

    for g in range(sections):
        each_page(g, page_sent)
        for a in range(2):
            for j in range(2):
                dst = kinds[g][a].at[j]
                remote(dst, dst, page_send.at[0, a], page_recv.at[g, a, j], partner).wait_recv()
    landed = (text_out, layout_out, grad_out, layout_grad_out)
    copies = [pltpu.make_async_copy(v, h, page_out_sem.at[i]) for i, (v, h) in enumerate(zip(landed, page_outs))]
    start(*copies)
    wait(*copies)


def layer_backward(mesh, x, y, probs, kept, weights, cots, norms, lang_ids, n_lang):
    sections, dp, tensors = mesh.shape["section"], mesh.shape["dp"], mesh.shape["tensor"]
    chain = dp == 4
    needed = tuple(
        Needed(
            n2=k.n2, r2=k.r2, downward=w.downward, slope=k.slope, upward=w.upward, n1=k.n1, r1=k.r1,
            outward=w.outward, low=k.low, act=k.act, qkv=k.qkv, ctx=k.ctx, project=w.project, x=rows,
        )
        for k, w, rows in zip(kept, weights, x)
    )
    flat_in, in_tree = jax.tree.flatten((needed, probs))
    plain = [v for own in needed for name, v in own._asdict().items() if name not in Weights._fields] + [probs]
    stacks = [(matrix_starts(own)[MATRICES], rows.shape[1]) for own, rows in zip(needed, x)]
    length = x[0].shape[0]
    work = []
    for own, rows, (count, width) in zip(needed, x, stacks):
        work += Work(
            g=shape(rows.shape), gf=shape(rows.shape), ga=shape(rows.shape), dz=shape(rows.shape, F32),
            dctx=shape(own.ctx.shape), sums=shape((4, width), F32), lowT=shape((width, length)),
            raw=shape((tensors, count, width)), from_sibling=shape((tensors // 2, count, width)),
            from_partner=shape((count, width)),
        )
    small = shape((2, n_lang + 8, x[0].shape[1]), F32)
    text_page = shape((2, length // tensors, x[0].shape[1]))
    layout_page = shape((2, x[1].shape[1], length // tensors))
    summed = [shape(s) for s in stacks]
    own = needed[0]
    n_feed = (own.upward.shape[1] + own.downward.shape[1]) // (2 * ROWS)
    n_chunks = n_feed + 1 + own.project.shape[1] // 192 + own.outward.shape[1] // 64
    n_blocks = length // (2 * ROWS)
    dma = pltpu.SemaphoreType.DMA
    results = pl.pallas_call(
        functools.partial(backward_kernel, sections, tensors, chain, in_tree),
        out_shape=summed + [small, text_page, layout_page, text_page, layout_page],
        in_specs=[ANY] * (len(flat_in) + 4) + [VMEM] * 3,
        out_specs=[ANY] * 2 + [VMEM] + [ANY] * 4,
        scratch_shapes=vmem_like(work) + vmem_like(plain)
        + [pltpu.VMEM(cots[1].shape, BF)] + [pltpu.VMEM((6,) + small.shape[1:], F32)] * 2
        + vmem_like([text_page, layout_page] * 2)
        + [dma((len(flat_in),)), dma((2,)), dma((2, n_blocks)), dma((2, n_blocks))]
        + [dma((n_chunks, tensors // 2))] * 2 + [dma((4, n_chunks))] * 2
        + [pltpu.SemaphoreType.REGULAR, dma((n_chunks,))]
        + [dma((6,))] * 2 + [dma((tensors, 2)), dma((sections, 2, 2)), dma((4,))],
        compiler_params=pltpu.CompilerParams(
            collective_id=1, has_side_effects=True, vmem_limit_bytes=64 << 20
        ),
        name="layer_backward",
    )(*flat_in, *cots, *y, lang_ids, norms[0][0], norms[1][0])
    totals, small, pages = results[:2], results[2], results[3:7]
    if not chain:
        totals = lax.psum(tuple(totals), "dp")
        both = lax.psum(small[0], ("dp", "tensor"))
        small = jnp.stack([both, lax.ppermute(both, "section", [(0, 1), (1, 0)])])
    return totals, small, pages


def widen_kernel(n_in, n_pages, *refs):
    n_out = 5 + n_pages + 2 * MATRICES
    hbm_in, hbm_out = refs[:n_in], refs[n_in : n_in + n_out]
    vmem_in, vmem_out = refs[n_in + n_out : 2 * n_in + n_out], refs[2 * n_in + n_out : -2]
    in_sem, out_sem = refs[-2:]
    loads = [pltpu.make_async_copy(h, v, in_sem.at[i]) for i, (h, v) in enumerate(zip(hbm_in, vmem_in))]
    sources = vmem_out[:5] + vmem_in[3:] + vmem_out[5:]
    stores = [pltpu.make_async_copy(v, h, out_sem.at[i]) for i, (v, h) in enumerate(zip(sources, hbm_out))]
    start(*loads)
    totals, small = vmem_in[0:2], vmem_in[2]
    for b in range(2):
        wait(loads[b])
        at = 0
        for i in range(b * MATRICES, (b + 1) * MATRICES):
            out = vmem_out[5 + i]
            for c in range(0, out.shape[0], 48):
                out[c : c + 48] = totals[b][at + c : at + c + 48].astype(F32)
            at += out.shape[0]
            stores[5 + n_pages + i].start()
    for i in range(n_pages):
        loads[3 + i].wait()
        stores[5 + i].start()
    loads[2].wait()
    n_lang = vmem_out[0].shape[0]
    vmem_out[0][...] = jnp.where(lax.axis_index("section") == 0, small[0, :n_lang], small[1, :n_lang])
    for i, out in enumerate(vmem_out[1:5]):
        first = n_lang + 2 * i
        out[...] = small[0, first : first + 2, : out.shape[1]]
    start(*stores[:5])
    wait(*stores)


def widen(totals, small, pages, shards, n_lang):
    widths = [total.shape[1] for total in totals]
    sums = [shape((n_lang, widths[0]), F32)] + [shape((2, w), F32) for w in widths for _ in range(2)]
    grads = [shape(m.shape, F32) for own in shards for m in own]
    inputs = (*totals, small, *pages)
    outs = sums + [shape(page.shape) for page in pages] + grads
    results = pl.pallas_call(
        functools.partial(widen_kernel, len(inputs), len(pages)), out_shape=outs,
        in_specs=[ANY] * len(inputs), out_specs=[ANY] * len(outs),
        scratch_shapes=vmem_like(inputs) + vmem_like(sums + grads)
        + [pltpu.SemaphoreType.DMA((len(inputs),)), pltpu.SemaphoreType.DMA((len(outs),))],
        compiler_params=pltpu.CompilerParams(vmem_limit_bytes=62 << 20), name="widen",
    )(*inputs)
    return results[0], results[1:5], results[5:9], results[9:13], results[13:17]


def per_device(
    mesh,
    text_input,
    layout_input,
    text_cotangent,
    layout_cotangent,
    page_counts,
    pad_mask,
    lang_ids,
    lang_table,
    text_project,
    text_outward,
    text_upward,
    text_downward,
    text_gains,
    text_biases,
    layout_project,
    layout_outward,
    layout_upward,
    layout_downward,
    layout_gains,
    layout_biases,
):
    def flat(project):
        return jnp.transpose(project[0], (1, 2, 0)).reshape(-1, project.shape[1])

    def flipped(block):
        return jnp.transpose(block[0], (0, 2, 1))

    shards = (
        Weights(flat(text_project), text_outward[0], text_upward[0], text_downward[0]),
        Weights(flat(layout_project), layout_outward[0], layout_upward[0], layout_downward[0]),
    )
    norms = ((text_gains[0], text_biases[0]), (layout_gains[0], layout_biases[0]))
    marks = (pad_mask, page_counts, lang_ids, lang_table)
    (x, y, probs, kept, weights), cots = layer_forward(
        mesh, text_input[0], flipped(layout_input), text_cotangent[0], flipped(layout_cotangent), shards, norms, marks
    )
    n_lang = lang_table.shape[0]
    totals, small, pages = layer_backward(mesh, x, y, probs, kept, weights, cots, norms, lang_ids, n_lang)
    lang_sum, norm_sums, pages, text_sums, layout_sums = widen(totals, small, pages, shards, n_lang)
    text_out, layout_out, text_grad, layout_grad = pages

    def unflat(grad, like):
        return jnp.transpose(grad.reshape(like.shape[2], like.shape[3], like.shape[1]), (2, 0, 1))[None]

    unflip = lambda block: jnp.transpose(block, (0, 2, 1))[None]
    return (
        text_out[None], unflip(layout_out), text_grad[None], unflip(layout_grad), lang_sum,
        unflat(text_sums[0], text_project), *(s[None] for s in text_sums[1:]), norm_sums[0][None], norm_sums[1][None],
        unflat(layout_sums[0], layout_project), *(s[None] for s in layout_sums[1:]),
        norm_sums[2][None], norm_sums[3][None],
    )


def solution(mesh):
    tokens = P("section", "dp", "tensor", None)
    weight_specs = (
        P("section", None, None, "tensor"), P("section", "tensor", None), P("section", None, "tensor"),
        P("section", "tensor", None), P("section", None, None), P("section", None, None),
    )
    in_specs = (tokens,) * 4 + (P(None, "dp"), P(None, "dp", None), P(None, "dp"), P()) + weight_specs * 2
    out_specs = (tokens,) * 4 + (P(),) + weight_specs * 2
    return jax.shard_map(
        functools.partial(per_device, mesh), mesh=mesh, in_specs=in_specs, out_specs=out_specs, check_vma=False
    )
```

```python
import functools
import math
import typing

import jax
import jax.numpy as jnp
from jax import lax
from jax.experimental import pallas as pl
from jax.experimental.pallas import tpu as pltpu
from jax.sharding import PartitionSpec as P

HEAD_TEXT = 64
HEAD_LAYOUT = 16
EPSILON = 1e-05
NEGATIVE = -1e30
HIGH = lax.Precision.HIGHEST
MESH = pl.DeviceIdType.MESH
BF = jnp.bfloat16
F32 = jnp.float32
ANY = pl.BlockSpec(memory_space=pl.ANY)


def remote(src, dst, send, recv, device):
    return pltpu.make_async_remote_copy(
        src_ref=src, dst_ref=dst, send_sem=send, recv_sem=recv, device_id=device, device_id_type=MESH
    )


def greet(section, tensor, sections, tensors, extra=()):
    barrier = pltpu.get_barrier_semaphore()
    for g in range(sections):
        for q in range(tensors):

            @pl.when((section != g) | (tensor != q))
            def _():
                pl.semaphore_signal(
                    barrier, inc=1, device_id={"section": g, "tensor": q}, device_id_type=MESH
                )

    for device in extra:
        pl.semaphore_signal(barrier, inc=1, device_id=device, device_id_type=MESH)
    pl.semaphore_wait(barrier, sections * tensors - 1 + len(extra))


GELU_P = 0.3275911
GELU_A = (0.254829592, -0.284496736, 1.421413741, -1.453152027, 1.061405429)
NN = (((1,), (0,)), ((), ()))
NT = (((1,), (1,)), ((), ()))
SCALES = (1.0 / math.sqrt(HEAD_TEXT), 1.0 / math.sqrt(HEAD_LAYOUT))
SIZES = (HEAD_TEXT, HEAD_LAYOUT)
ROWS = 128


class Weights(typing.NamedTuple):
    project: typing.Any
    outward: typing.Any
    upward: typing.Any
    downward: typing.Any


class Kept(typing.NamedTuple):
    qkv: typing.Any
    ctx: typing.Any
    n1: typing.Any
    r1: typing.Any
    low: typing.Any
    act: typing.Any
    slope: typing.Any
    n2: typing.Any
    r2: typing.Any


def dot(a, b, dims=NN):
    return lax.dot_general(a, b, dims, preferred_element_type=F32)


def gelu_pair(u):
    t = 1.0 / (1.0 + (GELU_P / math.sqrt(2.0)) * jnp.abs(u))
    e = jnp.exp(-0.5 * (u * u))
    a1, a2, a3, a4, a5 = (0.5 * a for a in GELU_A)
    tail = ((((a5 * t + a4) * t + a3) * t + a2) * t + a1) * t * e
    cdf = jnp.where(u >= 0, 1.0 - tail, tail)
    return u * cdf, cdf + u * e * (1.0 / math.sqrt(2.0 * math.pi))


def norm_rows(z, gain, offset):
    center = z - jnp.mean(z, axis=-1, keepdims=True)
    inverse = lax.rsqrt(jnp.mean(center * center, axis=-1, keepdims=True) + EPSILON)
    normed = center * inverse
    return normed * gain + offset, normed, inverse


def norm_rows_back(g, n, r, gain):
    t = g * gain
    return r * (t - jnp.mean(t, axis=-1, keepdims=True) - n * jnp.mean(t * n, axis=-1, keepdims=True))


class Staged:
    def __init__(self, tree, hbm, vmem, sem, inward):
        self.tree, self.vmem = tree, list(vmem)
        pairs = zip(hbm, vmem) if inward else zip(vmem, hbm)
        self.copies = [pltpu.make_async_copy(a, b, sem.at[i]) for i, (a, b) in enumerate(pairs)]

    def refs(self):
        return jax.tree.unflatten(self.tree, self.vmem)

    def parts(self):
        return jax.tree.unflatten(self.tree, self.copies)

    def start(self):
        for copy in self.copies:
            copy.start()

    def wait(self):
        for copy in self.copies:
            copy.wait()


def start(*copies):
    for copy in copies:
        copy.start()


def wait(*copies):
    for copy in copies:
        copy.wait()


def head_rows(stacks, slot, kind, local, scales=None):
    rows = []
    for b in range(2):
        first = kind * (stacks[b].shape[1] // 3) + local * SIZES[b]
        piece = stacks[b][slot, first : first + SIZES[b], :]
        rows.append(piece if scales is None else piece * BF(scales[b]))
    rows.append(jnp.zeros((128 - sum(SIZES), rows[0].shape[1]), BF))
    return jnp.concatenate(rows, axis=0)


def put_head(stacks, slot, kind, local, b, value):
    first = kind * (stacks[b].shape[1] // 3) + local * SIZES[b]
    stacks[b][slot, first : first + SIZES[b], :] = value.astype(BF)


def slot_of(u, core, chip):
    return ((chip + u // 2) % 2) * 2 + (core + u % 2) % 2


def forward_kernel(sections, tensors, shared, in_tree, out_tree, *refs):
    n_w, n_out = len(shared), out_tree.num_leaves
    sources = (refs[0:2], refs[2:4])
    shards = refs[4 : 4 + n_w]
    pad_mask, counts, lang_ids, lang_table, *norms = refs[4 + n_w : 12 + n_w]
    rest = refs[12 + n_w :]
    hbm_out, cots_out, rest = rest[:n_out], rest[n_out : n_out + 2], rest[n_out + 2 :]
    outgoing = Staged(out_tree, hbm_out, rest[:n_out], rest[n_out], False)
    rest = rest[n_out + 1 :]
    flipped, raw_x, y_narrow, *rest = rest
    nats, totals, rest = rest[0:2], rest[2:4], rest[4:]
    page_send, page_recv, w_send, w_recv, own_sem, hop_send, hop_recv, cot_sem = rest
    x, y_pages, probs_out, kept, weights = outgoing.refs()
    y = (y_pages[0], y_narrow)
    x_out, y_out, probs_copy, kept_out, weights_out = outgoing.parts()
    section, d, t = lax.axis_index("section"), lax.axis_index("dp"), lax.axis_index("tensor")
    core, chip, half_index = t % 2, t // 2, d % 2
    sibling, partner = t + 1 - 2 * core, (t + tensors // 2) % tensors
    mate = d + 1 - 2 * half_index
    micro, page = core, chip
    part_length = sources[0][0].shape[1]
    length = x[0].shape[0]
    blocks = [slice(c, c + 2 * ROWS) for c in range(0, length, 2 * ROWS)]
    full = (
        weights[0].project, weights[1].project, weights[0].outward, weights[0].upward,
        weights[0].downward, weights[1].outward, weights[1].upward, weights[1].downward,
    )
    greet(section, t, sections, tensors, ({"dp": mate},) if any(shared) else ())

    def half_of(ref, i, which):
        count = shards[i].shape[0] // 2
        return ref.at[pl.ds(pl.multiple_of(which * count, 16), count)] if shared[i] else ref

    def to_partner(i):
        return remote(
            half_of(shards[i], i, half_index), half_of(full[i].at[t], i, half_index),
            w_send.at[0, i], w_recv.at[0, i], {"tensor": partner},
        )

    def to_sibling(i):
        return remote(shards[i], full[i].at[t], w_send.at[1, i], w_recv.at[1, i], {"tensor": sibling})

    def to_mate(i):
        ref = half_of(full[i].at[partner], i, half_index)
        return remote(ref, ref, w_send.at[2, i], w_recv.at[2, i], {"dp": mate})

    def on_first(i):
        ref = half_of(full[i].at[partner], i, half_index)
        return remote(ref, ref, w_send.at[3, i], w_recv.at[3, i], {"tensor": sibling})

    def on_second(i):
        ref = half_of(full[i].at[partner], i, 1 - half_index)
        return remote(ref, ref, w_send.at[4, i], w_recv.at[4, i], {"tensor": sibling})

    def keep(i):
        return pltpu.make_async_copy(shards[i], full[i].at[t], own_sem.at[i])

    def relay(*which):
        for i in which:
            to_partner(i).wait_recv()
            if shared[i]:
                to_mate(i).start()
            on_first(i).start()

    def relay_second(*which):
        for i in which:
            if shared[i]:
                to_mate(i).wait_recv()
                on_second(i).start()

    def early(*which):
        for i in which:
            keep(i).wait()
            to_sibling(i).wait_recv()

    def late(*which):
        for i in which:
            on_first(i).wait_recv()
            if shared[i]:
                on_second(i).wait_recv()

    def token_slot(g, a, index):
        start_at = pl.multiple_of(index * part_length, part_length)
        target = (raw_x, flipped)[a]
        return target.at[pl.ds(start_at, part_length)] if a == 0 else target.at[:, pl.ds(start_at, part_length)]

    def over_pages(g, act):
        for j in range(2):
            target = 2 * j + section
            here = (section == g) & (t == target)
            for a in range(2):
                act(g, j, a, target, here)

    def page_copy(g, j, a, target):
        return remote(
            sources[g][a].at[j], token_slot(g, a, t), page_send.at[g, j, a], page_recv.at[a, t],
            {"section": g, "tensor": target},
        )

    def page_start(g, j, a, target, here):
        @pl.when(here)
        def _():
            pltpu.make_async_copy(sources[g][a].at[j], token_slot(g, a, t), page_recv.at[a, t]).start()

        @pl.when(jnp.logical_not(here))
        def _():
            page_copy(g, j, a, target).start()

    def page_sent(g, j, a, target, here):
        @pl.when(jnp.logical_not(here))
        def _():
            page_copy(g, j, a, target).wait_send()

    def pages_arrived(g):
        for a in range(2):
            for q in range(tensors):
                slot = token_slot(g, a, q)
                remote(slot, slot, page_send.at[0, 0, a], page_recv.at[a, q], {"tensor": sibling}).wait_recv()

    def hop(b, n):
        return remote(
            y[b].at[blocks[n]], x[b].at[blocks[n]], hop_send.at[b, n], hop_recv.at[b, n], {"section": 1 - section}
        )

    over_pages(0, page_start)
    for i in range(n_w):
        to_partner(i).start()
        keep(i).start()
    for i in range(n_w):
        to_sibling(i).start()
    over_pages(1, page_start)

    at_page = (lax.broadcasted_iota(jnp.int32, counts.shape, 0) == micro) & (
        lax.broadcasted_iota(jnp.int32, counts.shape, 1) == page
    )

    def own_entry(ref):
        return jnp.sum(jnp.where(at_page, ref[...], 0), axis=(0, 1), keepdims=True)

    positions = lax.broadcasted_iota(jnp.int32, (1, length), 1)
    mask_row = pad_mask[micro, pl.ds(page, 1), :]
    key_mask = (positions < own_entry(counts)) & ((mask_row == 1) | (positions == 0))
    groups = lax.broadcasted_iota(jnp.int32, (lang_table.shape[0], 1), 0)
    lang_row = jnp.sum(jnp.where(groups == own_entry(lang_ids), lang_table[...], 0.0), axis=0, keepdims=True)
    local_heads = weights[0].project.shape[1] // (3 * HEAD_TEXT)
    qkv = (kept[0].qkv, kept[1].qkv)

    @pl.when(section == 0)
    def _():
        pages_arrived(0)
        x[0][...] = (raw_x[...].astype(F32) + lang_row).astype(BF)
        x[1][...] = flipped[...].T
        early(0, 1)

    @pl.when(section == 1)
    def _():
        relay(*range(n_w))
        relay_second(*range(n_w))
        early(*range(n_w))
        late(*range(n_w))
        start(*weights_out[0], *weights_out[1])

    @pl.loop(0, 2)
    def _(half):
        @pl.when((half == 1) & (section == 0))
        def _():
            relay(0, 1)
            relay_second(0)
            late(0, 1)

        for n, block in enumerate(blocks):
            @pl.when((half == 0) & (section == 1))
            def _():
                for b in range(2):
                    hop(b, n).wait_recv()

            @pl.loop(0, 2)
            def _(u):
                slot = slot_of(2 * half + u, core, chip)
                for b in range(2):
                    qkv[b][slot, :, block] = dot(weights[b].project[slot], x[b][block], NT).astype(BF)

        @pl.loop(0, 2)
        def _(u):
            slot = slot_of(2 * half + u, core, chip)
            for local in range(local_heads):
                q = head_rows(qkv, slot, 0, local, SCALES).T
                scores = jnp.where(key_mask, dot(q, head_rows(qkv, slot, 1, local)), NEGATIVE)
                raised = jnp.exp(scores - jnp.max(scores, axis=-1, keepdims=True))
                probs = (raised * (1.0 / jnp.sum(raised, axis=-1, keepdims=True))).astype(BF)
                probs_out[slot, local] = probs
                ctx = dot(head_rows(qkv, slot, 2, local), probs, NT).astype(BF)
                kept[0].ctx[slot, local * HEAD_TEXT : (local + 1) * HEAD_TEXT, :] = ctx[:HEAD_TEXT]
                kept[1].ctx[slot, local * HEAD_LAYOUT : (local + 1) * HEAD_LAYOUT, :] = ctx[
                    HEAD_TEXT : HEAD_TEXT + HEAD_LAYOUT
                ]

    start(probs_copy, *x_out, *(k.qkv for k in kept_out), *(k.ctx for k in kept_out))

    def attend(b):
        gains, biases = norms[2 * b : 2 * b + 2]
        width = x[b].shape[1]
        nats[b][...] = kept[b].ctx[...].reshape(width, length).T
        wide = weights[b].outward[...].reshape(width, width)
        for block in blocks:
            h, n, r = norm_rows(x[b][block].astype(F32) + dot(nats[b][block], wide), gains[0:1], biases[0:1])
            totals[b][0, block] = h
            totals[b][1, block] = jnp.zeros(h.shape, F32)
            kept[b].n1[block] = n.astype(BF)
            kept[b].r1[block] = r
            kept[b].low[block] = h.astype(BF)
        start(kept_out[b].n1, kept_out[b].r1, kept_out[b].low)

    def feed(b, first, which):
        @pl.loop(first, first + 2)
        def _(u):
            slot = slot_of(u, core, chip)
            for block in which:
                act, slope = gelu_pair(dot(kept[b].low[block], weights[b].upward[slot]))
                act = act.astype(BF)
                kept[b].act[slot, block] = act
                kept[b].slope[slot, block] = slope.astype(BF)
                totals[b][1, block] += dot(act, weights[b].downward[slot])

    def finish(b):
        gains, biases = norms[2 * b : 2 * b + 2]
        for n, block in enumerate(blocks):
            feed(b, 2, [block])
            out, normed, r = norm_rows(totals[b][0, block] + totals[b][1, block], gains[1:2], biases[1:2])
            y[b][block] = out.astype(BF)
            kept[b].n2[block] = normed.astype(BF)
            kept[b].r2[block] = r

            @pl.when(section == 0)
            def _():
                hop(b, n).start()

        if b == 1:
            y_pages[1][...] = y_narrow[...].T
        start(y_out[b], kept_out[b].act, kept_out[b].slope, kept_out[b].n2, kept_out[b].r2)

    @pl.when(section == 0)
    def _():
        relay(2, 3)
        early(2)
        late(2)

    attend(0)

    @pl.when(section == 0)
    def _():
        early(3, 4)

    feed(0, 0, blocks)

    @pl.when(section == 0)
    def _():
        relay(4, 5, 6, 7)
        relay_second(3)
        early(5, 6, 7)
        late(5, 6, 7)

    attend(1)
    feed(1, 0, blocks)
    finish(1)

    @pl.when(section == 0)
    def _():
        relay_second(4)
        late(3, 4)

    finish(0)

    @pl.when(section == 0)
    def _():
        start(*weights_out[0], *weights_out[1])
        for b in range(2):
            for n in range(len(blocks)):
                hop(b, n).wait_send()

    for i in range(n_w):
        to_partner(i).wait_send()
        to_sibling(i).wait_send()
        on_first(i).wait_send()
        if shared[i]:
            to_mate(i).wait_send()
            on_second(i).wait_send()
    for g in range(sections):
        over_pages(g, page_sent)

    @pl.when(section == 1)
    def _():
        pages_arrived(1)
        copies = [pltpu.make_async_copy(v, h, cot_sem.at[i]) for i, (v, h) in enumerate(zip((raw_x, flipped), cots_out))]
        start(*copies)
        wait(*copies)

    outgoing.wait()


def vmem_like(tree):
    return [pltpu.VMEM(s.shape, s.dtype) for s in jax.tree.leaves(tree)]


VMEM = pl.BlockSpec(memory_space=pltpu.VMEM)


def shape(dims, dtype=BF):
    return jax.ShapeDtypeStruct(tuple(dims), dtype)


def layer_forward(mesh, text_in, layout_in, text_cot, layout_cot, shards, norms, marks):
    sections, dp, tensors = mesh.shape["section"], mesh.shape["dp"], mesh.shape["tensor"]
    length = text_in.shape[1] * tensors
    rows = (shape((length, text_in.shape[2])), shape((length, layout_in.shape[1])))
    local_heads = shards[0].project.shape[0] // (3 * HEAD_TEXT)
    kept = []
    for x, w in zip(rows, shards):
        units, column = shape((tensors, length, w.upward.shape[1])), shape((length, 1), F32)
        kept.append(Kept(
            qkv=shape((tensors, w.project.shape[0], length)), ctx=shape((tensors, w.outward.shape[0], length)),
            n1=shape(x.shape), r1=column, low=shape(x.shape), act=units, slope=units,
            n2=shape(x.shape), r2=column,
        ))
    weights = tuple(Weights(*(shape((tensors,) + m.shape) for m in w)) for w in shards)
    pages_out = (rows[0], shape((rows[1].shape[1], length)))
    outs = (rows, pages_out, shape((tensors, local_heads, length, length)), tuple(kept), weights)
    flat_out, out_tree = jax.tree.flatten(outs)
    (a, b) = shards
    ordered = (a.project, b.project, a.outward, a.upward, a.downward, b.outward, b.upward, b.downward)
    shared = tuple(dp % 2 == 0 and w.shape[0] >= 512 for w in ordered)
    n_w = len(ordered)
    cots = [rows[0], shape((rows[1].shape[1], length))]
    small = (*marks, *norms[0], *norms[1])
    results = pl.pallas_call(
        functools.partial(forward_kernel, sections, tensors, shared, None, out_tree),
        out_shape=flat_out + cots,
        in_specs=[ANY] * (4 + n_w) + [VMEM] * len(small),
        out_specs=[ANY] * (len(flat_out) + 2),
        scratch_shapes=vmem_like(flat_out) + [pltpu.SemaphoreType.DMA((len(flat_out),))]
        + [pltpu.VMEM(cots[1].shape, BF), pltpu.VMEM(cots[0].shape, BF), pltpu.VMEM(rows[1].shape, BF)]
        + [pltpu.VMEM(x.shape, BF) for x in rows]
        + [pltpu.VMEM((2,) + x.shape, F32) for x in rows]
        + [
            pltpu.SemaphoreType.DMA((sections, 2, 2)), pltpu.SemaphoreType.DMA((2, tensors)),
            pltpu.SemaphoreType.DMA((5, n_w)), pltpu.SemaphoreType.DMA((5, n_w)), pltpu.SemaphoreType.DMA((n_w,)),
            pltpu.SemaphoreType.DMA((2, length // (2 * ROWS))), pltpu.SemaphoreType.DMA((2, length // (2 * ROWS))),
            pltpu.SemaphoreType.DMA((2,)),
        ],
        compiler_params=pltpu.CompilerParams(
            collective_id=0, has_side_effects=True, vmem_limit_bytes=62 << 20
        ),
        name="layer_forward",
    )(text_in, layout_in, text_cot, layout_cot, *ordered, *small)
    return jax.tree.unflatten(out_tree, results[:-2]), tuple(results[-2:])


class Needed(typing.NamedTuple):
    n2: typing.Any
    r2: typing.Any
    downward: typing.Any
    slope: typing.Any
    upward: typing.Any
    n1: typing.Any
    r1: typing.Any
    outward: typing.Any
    low: typing.Any
    act: typing.Any
    qkv: typing.Any
    ctx: typing.Any
    project: typing.Any
    x: typing.Any


class Work(typing.NamedTuple):
    g: typing.Any
    gf: typing.Any
    ga: typing.Any
    dz: typing.Any
    dctx: typing.Any
    sums: typing.Any
    lowT: typing.Any
    raw: typing.Any
    from_sibling: typing.Any
    from_partner: typing.Any


class Chunk(typing.NamedTuple):
    b: typing.Any
    index: typing.Any
    first: typing.Any
    rows: typing.Any


MATRICES = 4


def matrix_rows(own):
    return own.project.shape[1], own.outward.shape[1], own.upward.shape[1], own.downward.shape[1]


def matrix_starts(own):
    sizes = matrix_rows(own)
    return [sum(sizes[:i]) for i in range(MATRICES + 1)]


def pieces_of(size, step):
    return [(f, step) for f in range(0, size, step)]


def backward_kernel(sections, tensors, chain, in_tree, *refs):
    n_in = in_tree.num_leaves
    hbm_in, refs = refs[:n_in], refs[n_in:]
    (cots, ys, lang_ids, gains), refs = (refs[0:2], refs[2:4], refs[4], refs[5:7]), refs[7:]
    results, small_out, page_outs, refs = refs[0:2], refs[2], refs[3:7], refs[7:]
    n_work = len(Work._fields)
    work, refs = (Work(*refs[:n_work]), Work(*refs[n_work : 2 * n_work])), refs[2 * n_work :]
    plain, refs = refs[: n_in - 2 * MATRICES], refs[n_in - 2 * MATRICES :]
    flipped, small_got, small_sum, refs = refs[0], refs[1], refs[2], refs[3:]
    text_out, layout_out, grad_out, layout_grad_out, *refs = refs
    in_sem, cot_sem, hop_send, hop_recv, sib_send, sib_recv, send, recv, credit, out_sem, *refs = refs
    small_send, small_recv, page_send, page_recv, page_out_sem = refs
    section, d, t = lax.axis_index("section"), lax.axis_index("dp"), lax.axis_index("tensor")
    core, chip = t % 2, t // 2
    sibling = {"tensor": t + 1 - 2 * core}
    partner = {"tensor": (t + tensors // 2) % tensors}
    near, cross = {"dp": d + 1 - 2 * (d % 2)}, {"dp": 3 - d}
    outer = (d == 0) | (d == 3)
    other = {"section": 1 - section}
    hbm, probs_hbm = jax.tree.unflatten(in_tree, hbm_in)
    starts = [matrix_starts(own) for own in hbm]

    plain = list(plain)
    views = []
    for b in range(2):
        fields = {}
        for name, value in hbm[b]._asdict().items():
            if name in Weights._fields:
                i = Weights._fields.index(name)
                fields[name] = work[b].raw.at[:, pl.ds(starts[b][i], starts[b][i + 1] - starts[b][i])]
            else:
                fields[name] = plain.pop(0)
        views.append(Needed(**fields))
    probs_in = plain.pop(0)
    flat_views = jax.tree.leaves((tuple(views), probs_in))
    flat_copies = [pltpu.make_async_copy(a, v, in_sem.at[i]) for i, (a, v) in enumerate(zip(hbm_in, flat_views))]
    loads, probs_copy = jax.tree.unflatten(in_tree, flat_copies)
    length = work[0].gf.shape[0]
    local_heads = probs_in.shape[1]
    blocks = [slice(c, c + 2 * ROWS) for c in range(0, length, 2 * ROWS)]
    cot_copies = (
        pltpu.make_async_copy(cots[0], work[0].g, cot_sem.at[0]),
        pltpu.make_async_copy(cots[1], flipped, cot_sem.at[1]),
    )

    @pl.when(section == 1)
    def _():
        start(*cot_copies)

    start(*flat_copies)
    greet(section, t, sections, tensors, (near, cross) if chain else ())

    part_length = text_out.shape[1]
    micro, page = core, chip
    kinds = ((grad_out, layout_grad_out), (text_out, layout_out))
    pages = ((work[0].g, flipped), ys)

    def page_part(g, q, a):
        span = pl.ds(q * part_length, part_length)
        return pages[g][a].at[span] if a == 0 else pages[g][a].at[:, span]

    def each_page(g, act):
        for q in range(tensors):
            for a in range(2):
                here = (micro == g) & (t == q)

                @pl.when((section == g) & here)
                def _():
                    act(g, q, a, True)

                @pl.when((section == g) & jnp.logical_not(here))
                def _():
                    act(g, q, a, False)

    def page_copy(g, q, a):
        return remote(
            page_part(g, q, a), kinds[g][a].at[page], page_send.at[q, a], page_recv.at[g, a, page],
            {"section": micro, "tensor": q},
        )

    def page_start(g, q, a, here):
        if here:
            pltpu.make_async_copy(page_part(g, q, a), kinds[g][a].at[page], page_recv.at[g, a, page]).start()
        else:
            page_copy(g, q, a).start()

    def page_sent(g, q, a, here):
        if not here:
            page_copy(g, q, a).wait_send()

    each_page(1, page_start)

    def hop(b, n):
        part = work[b].g.at[blocks[n]]
        return remote(part, part, hop_send.at[b, n], hop_recv.at[b, n], other)

    step = 2 * ROWS
    up_first, down_first = starts[0][2], starts[0][3]
    up_count, down_count = (starts[0][3] - up_first) // step, (starts[0][4] - down_first) // step
    n_feed = up_count + down_count
    chunks = [Chunk(0, k, up_first + k * step, step) for k in range(n_feed)]
    later = [(1, 0, starts[1][MATRICES])]
    later += [(0, f, n) for f, n in pieces_of(starts[0][1], 192)]
    later += [(0, starts[0][1] + f, n) for f, n in pieces_of(starts[0][2] - starts[0][1], 64)]
    chunks += [Chunk(b, n_feed + i, f, n) for i, (b, f, n) in enumerate(later)]

    def feed_chunk(k):
        return Chunk(0, k, pl.multiple_of(up_first + k * step, 16), step)

    def span(ref, c):
        return ref.at[pl.ds(c.first, c.rows)]

    def to_sibling(c, j):
        w = work[c.b]
        return remote(
            span(w.raw.at[2 * j + 1 - core], c), span(w.from_sibling.at[j], c),
            sib_send.at[c.index, j], sib_recv.at[c.index, j], sibling,
        )

    def mine(c):
        return span(work[c.b].raw.at[t], c)

    def theirs(c):
        return span(work[c.b].raw.at[2 * (1 - chip) + core], c)

    def to_partner(c):
        return remote(
            theirs(c), span(work[c.b].from_partner, c), send.at[0, c.index], recv.at[0, c.index], partner
        )

    def from_near(c):
        return span(work[c.b].from_sibling.at[0], c)

    def from_cross(c):
        return span(work[c.b].from_sibling.at[1], c)

    def to_near(c):
        return remote(mine(c), from_near(c), send.at[1, c.index], recv.at[1, c.index], near)

    def to_cross(c):
        return remote(mine(c), from_cross(c), send.at[2, c.index], recv.at[2, c.index], cross)

    def total_to_near(c):
        return remote(
            span(work[c.b].from_partner, c), from_near(c), send.at[3, c.index], recv.at[3, c.index], near
        )

    def out_copy(c, source):
        return pltpu.make_async_copy(span(source, c), span(results[c.b], c), out_sem.at[c.index])

    def added(target, *sources):
        target[...] = sum(s[...].astype(F32) for s in sources).astype(BF)

    def send_to_sibling(c):
        for j in range(tensors // 2):
            to_sibling(c, j).start()

    def stage_sibling(c):
        w = work[c.b]
        for j in range(tensors // 2):
            to_sibling(c, j).wait_recv()
        added(theirs(c), theirs(c), span(w.from_sibling.at[1 - chip], c))
        added(mine(c), mine(c), span(w.from_sibling.at[chip], c))
        if chain:
            @pl.when(jnp.logical_not(outer))
            def _():
                for device in (near, cross):
                    pl.semaphore_signal(credit, inc=1, device_id=device, device_id_type=MESH)

    def stage_partner(c):
        to_partner(c).wait_recv()
        added(mine(c), mine(c), span(work[c.b].from_partner, c))
        if not chain:
            out_copy(c, work[c.b].raw.at[t]).start()
            return

        @pl.when(outer)
        def _():
            pl.semaphore_wait(credit, 1)
            to_near(c).start()

    def stage_near(c):
        @pl.when(jnp.logical_not(outer))
        def _():
            to_near(c).wait_recv()
            added(mine(c), mine(c), from_near(c))
            pl.semaphore_wait(credit, 1)
            to_cross(c).start()

    def stage_cross(c):
        @pl.when(jnp.logical_not(outer))
        def _():
            to_cross(c).wait_recv()
            total = work[c.b].from_partner
            added(span(total, c), mine(c), from_cross(c))
            total_to_near(c).start()
            out_copy(c, total).start()

    def stage_total(c):
        @pl.when(outer)
        def _():
            total_to_near(c).wait_recv()
            out_copy(c, work[c.b].from_sibling.at[0]).start()

    def feed_products():
        own, w = views[0], work[0]
        w.lowT[...] = own.low[...].T

        @pl.loop(0, up_count)
        def _(k):
            rows = pl.ds(pl.multiple_of(k * step, step), step)
            for q in range(tensors):
                w.raw[q, pl.ds(pl.multiple_of(up_first + k * step, 16), step), :] = dot(
                    w.lowT[rows, :], own.slope[q]
                ).astype(BF)
            send_to_sibling(feed_chunk(k))

        @pl.loop(0, down_count)
        def _(k):
            lanes = pl.ds(pl.multiple_of(k * step, step), step)
            for q in range(tensors):
                w.raw[q, pl.ds(pl.multiple_of(down_first + k * step, 16), step), :] = dot(
                    own.act[q, :, lanes].T, w.gf[...]
                ).astype(BF)
            send_to_sibling(feed_chunk(up_count + k))

    def later_product(c):
        own, w = views[c.b], work[c.b]
        for q in range(tensors):
            for i in range(MATRICES):
                first = max(c.first, starts[c.b][i])
                last = min(c.first + c.rows, starts[c.b][i + 1])
                if first >= last:
                    continue
                rows = slice(first - starts[c.b][i], last - starts[c.b][i])
                if i == 0:
                    value = dot(own.qkv[q, rows, :], own.x[...])
                elif i == 1:
                    value = dot(own.ctx[q, rows, :], w.ga[...])
                elif i == 2:
                    value = dot(w.lowT[rows, :], own.slope[q])
                else:
                    value = dot(own.act[q, :, rows].T, w.gf[...])
                w.raw[q, first:last, :] = value.astype(BF)
        send_to_sibling(c)

    @pl.when(section == 1)
    def _():
        wait(*cot_copies)
        work[1].g[...] = flipped[...].T

    for b in range(2):
        work[b].sums[...] = jnp.zeros(work[b].sums.shape, F32)
    for b in (1, 0):
        own_in = loads[b]
        wait(own_in.n2, own_in.r2, own_in.downward, own_in.slope, own_in.upward, own_in.n1, own_in.r1, own_in.outward)
    for n, block in enumerate(blocks):
        for b in (1, 0):
            own, w, gain = views[b], work[b], gains[b]

            @pl.when(section == 0)
            def _():
                hop(b, n).wait_recv()

            g, normed = w.g[block].astype(F32), own.n2[block].astype(F32)
            low = norm_rows_back(g, normed, own.r2[block], gain[1:2])
            w.dz[block] = low
            w.gf[block] = low.astype(BF)
            w.sums[1:2] += jnp.sum(g * normed, axis=0, keepdims=True)
            w.sums[3:4] += jnp.sum(g, axis=0, keepdims=True)

            @pl.loop(0, tensors)
            def _(q):
                d_act = dot(w.gf[block], own.downward[q], NT)
                d_pre = (d_act * own.slope[q, block].astype(F32)).astype(BF)
                own.slope[q, block] = d_pre
                w.dz[block] += dot(d_pre, own.upward[q], NT)

            g, normed = w.dz[block], own.n1[block].astype(F32)
            low = norm_rows_back(g, normed, own.r1[block], gain[0:1])
            w.dz[block] = low
            w.ga[block] = low.astype(BF)
            w.sums[0:1] += jnp.sum(g * normed, axis=0, keepdims=True)
            w.sums[2:3] += jnp.sum(g, axis=0, keepdims=True)
            for q in range(tensors):
                w.dctx[q, :, block] = dot(own.outward[q], w.ga[block], NT).astype(BF)

    wait(loads[0].low, loads[0].act)

    @pl.when(section == 0)
    def _():
        feed_products()

    wait(loads[0].qkv, loads[1].qkv, probs_copy)
    qkv = (views[0].qkv, views[1].qkv)
    text_rows, layout_rows = slice(0, HEAD_TEXT), slice(HEAD_TEXT, HEAD_TEXT + HEAD_LAYOUT)

    @pl.loop(0, tensors)
    def _(q):
        @pl.when((section == 0) & (q < n_feed // 2))
        def _():
            stage_sibling(feed_chunk(2 * q))
            stage_sibling(feed_chunk(2 * q + 1))

        @pl.when((section == 0) & (q == 0))
        def _():
            to_partner(chunks[0]).start()
            to_partner(chunks[1]).start()

        @pl.when((section == 0) & (q >= 2))
        def _():
            stage_partner(feed_chunk(q - 2))
            to_partner(feed_chunk(q)).start()

        for local in range(local_heads):
            dcT = jnp.concatenate(
                [work[b].dctx[q, local * SIZES[b] : (local + 1) * SIZES[b], :] for b in range(2)]
                + [jnp.zeros((128 - sum(SIZES), length), BF)], axis=0,
            )
            dc = dcT.T
            lane = lax.broadcasted_iota(jnp.int32, dc.shape, 1)
            dc_layout = jnp.where(lane >= HEAD_TEXT, dc, jnp.zeros_like(dc))
            qT, kT, vT = (head_rows(qkv, q, kind, local, SCALES if kind == 0 else None) for kind in range(3))
            low = probs_in[q, local]
            probs = low.astype(F32)
            both = dot(dc, vT)
            ds_both = (probs * (both - jnp.sum(probs * both, axis=-1, keepdims=True))).astype(BF)
            single = dot(dc_layout, vT)
            ds_layout = (probs * (single - jnp.sum(probs * single, axis=-1, keepdims=True))).astype(BF)
            dvT = dot(dcT, low)
            put_head(qkv, q, 2, local, 0, dvT[text_rows])
            put_head(qkv, q, 2, local, 1, dvT[layout_rows])
            put_head(qkv, q, 0, local, 0, dot(kT[text_rows], ds_both, NT) * SCALES[0])
            put_head(qkv, q, 1, local, 0, dot(qT[text_rows], ds_both))
            put_head(qkv, q, 0, local, 1, dot(kT[layout_rows], ds_layout, NT) * SCALES[1])
            put_head(qkv, q, 1, local, 1, dot(qT[layout_rows], ds_layout))

    wait(loads[0].project, loads[1].project)
    page_sum = jnp.zeros((1, work[0].dz.shape[1]), F32)
    for n, block in enumerate(blocks):
        for b in (1, 0):
            down = work[b].dz[block]
            for q in range(tensors):
                down += dot(qkv[b][q, :, block].T, views[b].project[q])
            down = down.astype(BF)
            work[b].g[block] = down
            if b == 0:
                page_sum += jnp.sum(down.astype(F32), axis=0, keepdims=True)

            @pl.when(section == 1)
            def _():
                hop(b, n).start()

    wait(loads[1].low, loads[1].act)
    work[1].lowT[...] = views[1].low[...].T
    for own_in in loads:
        wait(own_in.ctx, own_in.x)
    @pl.when(section == 1)
    def _():
        feed_products()
        for c in chunks[:2]:
            stage_sibling(c)
            to_partner(c).start()

        @pl.loop(2, n_feed)
        def _(k):
            stage_sibling(feed_chunk(k))

    for c in chunks[n_feed:]:
        later_product(c)
    for c in chunks[n_feed:]:
        stage_sibling(c)

    @pl.when(section == 0)
    def _():
        flipped[...] = work[1].g[...].T
        each_page(0, page_start)

    at_page = (lax.broadcasted_iota(jnp.int32, lang_ids.shape, 0) == t % 2) & (
        lax.broadcasted_iota(jnp.int32, lang_ids.shape, 1) == t // 2
    )
    group = jnp.sum(jnp.where(at_page, lang_ids[...], 0), axis=(0, 1), keepdims=True)
    n_lang = small_out.shape[1] - 8
    chosen = (lax.broadcasted_iota(jnp.int32, (n_lang, 1), 0) == group) & (section == 0)
    small_sum[0, 0:n_lang] = jnp.where(chosen, page_sum, 0.0)
    small_sum[0, n_lang : n_lang + 4] = work[0].sums[...]
    small_sum[0, n_lang + 4 : n_lang + 8] = jnp.zeros((4, small_out.shape[2]), F32)
    small_sum[0, n_lang + 4 : n_lang + 8, : work[1].sums.shape[1]] = work[1].sums[...]

    def small_copy(i, device):
        return remote(small_sum.at[i], small_got.at[i], small_send.at[i], small_recv.at[i], device)

    if chain:
        small_copy(0, sibling).start()
    stages = [(0, stage_partner)] + ([(2, stage_near), (4, stage_cross), (6, stage_total)] if chain else [])
    for turn in range(len(chunks) + stages[-1][0]):
        for lag, stage in stages:
            k = turn - lag
            if not 0 <= k < len(chunks):
                continue
            if stage is not stage_partner:
                stage(chunks[k])
            elif k < 2:

                @pl.when(section == 1)
                def _():
                    stage_partner(chunks[k])
                    to_partner(chunks[k + 2]).start()
            else:
                stage_partner(chunks[k])
                if k + 2 < len(chunks):
                    to_partner(chunks[k + 2]).start()
        if not chain:
            continue
        if turn == 0:
            small_copy(0, sibling).wait_recv()
            small_sum[1] = small_sum[0] + small_got[0]
            small_copy(1, partner).start()
        if turn == 1:
            small_copy(1, partner).wait_recv()
            small_sum[2] = small_sum[1] + small_got[1]
            small_copy(2, near).start()
        if turn == 2:
            small_copy(2, near).wait_recv()
            small_sum[3] = small_sum[2] + small_got[2]

            @pl.when(jnp.logical_not(outer))
            def _():
                small_copy(3, cross).start()

        if turn == 4:
            @pl.when(jnp.logical_not(outer))
            def _():
                small_copy(3, cross).wait_recv()
                small_sum[4] = small_sum[3] + small_got[3]
                small_copy(4, near).start()

        if turn == 6:
            @pl.when(outer)
            def _():
                small_copy(4, near).wait_recv()
                small_sum[4] = small_got[4]

            small_sum[5] = small_sum[4]
            small_copy(5, other).start()
        if turn == 8:
            small_copy(5, other).wait_recv()
            small_out[0] = small_sum[5]
            small_out[1] = small_got[5]

    if chain:
        for i, device in enumerate((sibling, partner, near)):
            small_copy(i, device).wait_send()

        @pl.when(jnp.logical_not(outer))
        def _():
            small_copy(3, cross).wait_send()
            small_copy(4, near).wait_send()

        small_copy(5, other).wait_send()
    else:
        small_out[0] = small_sum[0]
        small_out[1] = small_sum[0]

    @pl.when(section == 1)
    def _():
        for b in range(2):
            for n in range(len(blocks)):
                hop(b, n).wait_send()

    for c in chunks:
        for j in range(tensors // 2):
            to_sibling(c, j).wait_send()
        to_partner(c).wait_send()
        if not chain:
            out_copy(c, work[c.b].from_partner).wait()
            continue

        @pl.when(outer)
        def _():
            to_near(c).wait_send()

        @pl.when(jnp.logical_not(outer))
        def _():
            to_cross(c).wait_send()
            total_to_near(c).wait_send()

        out_copy(c, work[c.b].from_partner).wait()

    for g in range(sections):
        each_page(g, page_sent)
        for a in range(2):
            for j in range(2):
                dst = kinds[g][a].at[j]
                remote(dst, dst, page_send.at[0, a], page_recv.at[g, a, j], partner).wait_recv()
    landed = (text_out, layout_out, grad_out, layout_grad_out)
    copies = [pltpu.make_async_copy(v, h, page_out_sem.at[i]) for i, (v, h) in enumerate(zip(landed, page_outs))]
    start(*copies)
    wait(*copies)


def layer_backward(mesh, x, y, probs, kept, weights, cots, norms, lang_ids, n_lang):
    sections, dp, tensors = mesh.shape["section"], mesh.shape["dp"], mesh.shape["tensor"]
    chain = dp == 4
    needed = tuple(
        Needed(
            n2=k.n2, r2=k.r2, downward=w.downward, slope=k.slope, upward=w.upward, n1=k.n1, r1=k.r1,
            outward=w.outward, low=k.low, act=k.act, qkv=k.qkv, ctx=k.ctx, project=w.project, x=rows,
        )
        for k, w, rows in zip(kept, weights, x)
    )
    flat_in, in_tree = jax.tree.flatten((needed, probs))
    plain = [v for own in needed for name, v in own._asdict().items() if name not in Weights._fields] + [probs]
    stacks = [(matrix_starts(own)[MATRICES], rows.shape[1]) for own, rows in zip(needed, x)]
    length = x[0].shape[0]
    work = []
    for own, rows, (count, width) in zip(needed, x, stacks):
        work += Work(
            g=shape(rows.shape), gf=shape(rows.shape), ga=shape(rows.shape), dz=shape(rows.shape, F32),
            dctx=shape(own.ctx.shape), sums=shape((4, width), F32), lowT=shape((width, length)),
            raw=shape((tensors, count, width)), from_sibling=shape((tensors // 2, count, width)),
            from_partner=shape((count, width)),
        )
    small = shape((2, n_lang + 8, x[0].shape[1]), F32)
    text_page = shape((2, length // tensors, x[0].shape[1]))
    layout_page = shape((2, x[1].shape[1], length // tensors))
    summed = [shape(s) for s in stacks]
    own = needed[0]
    n_feed = (own.upward.shape[1] + own.downward.shape[1]) // (2 * ROWS)
    n_chunks = n_feed + 1 + own.project.shape[1] // 192 + own.outward.shape[1] // 64
    n_blocks = length // (2 * ROWS)
    dma = pltpu.SemaphoreType.DMA
    results = pl.pallas_call(
        functools.partial(backward_kernel, sections, tensors, chain, in_tree),
        out_shape=summed + [small, text_page, layout_page, text_page, layout_page],
        in_specs=[ANY] * (len(flat_in) + 4) + [VMEM] * 3,
        out_specs=[ANY] * 2 + [VMEM] + [ANY] * 4,
        scratch_shapes=vmem_like(work) + vmem_like(plain)
        + [pltpu.VMEM(cots[1].shape, BF)] + [pltpu.VMEM((6,) + small.shape[1:], F32)] * 2
        + vmem_like([text_page, layout_page] * 2)
        + [dma((len(flat_in),)), dma((2,)), dma((2, n_blocks)), dma((2, n_blocks))]
        + [dma((n_chunks, tensors // 2))] * 2 + [dma((4, n_chunks))] * 2
        + [pltpu.SemaphoreType.REGULAR, dma((n_chunks,))]
        + [dma((6,))] * 2 + [dma((tensors, 2)), dma((sections, 2, 2)), dma((4,))],
        compiler_params=pltpu.CompilerParams(
            collective_id=1, has_side_effects=True, vmem_limit_bytes=64 << 20
        ),
        name="layer_backward",
    )(*flat_in, *cots, *y, lang_ids, norms[0][0], norms[1][0])
    totals, small, pages = results[:2], results[2], results[3:7]
    if not chain:
        totals = lax.psum(tuple(totals), "dp")
        both = lax.psum(small[0], ("dp", "tensor"))
        small = jnp.stack([both, lax.ppermute(both, "section", [(0, 1), (1, 0)])])
    return totals, small, pages


def widen_kernel(n_in, n_pages, *refs):
    n_out = 5 + n_pages + 2 * MATRICES
    hbm_in, hbm_out = refs[:n_in], refs[n_in : n_in + n_out]
    vmem_in, vmem_out = refs[n_in + n_out : 2 * n_in + n_out], refs[2 * n_in + n_out : -2]
    in_sem, out_sem = refs[-2:]
    loads = [pltpu.make_async_copy(h, v, in_sem.at[i]) for i, (h, v) in enumerate(zip(hbm_in, vmem_in))]
    sources = vmem_out[:5] + vmem_in[3:] + vmem_out[5:]
    stores = [pltpu.make_async_copy(v, h, out_sem.at[i]) for i, (v, h) in enumerate(zip(sources, hbm_out))]
    start(*loads)
    totals, small = vmem_in[0:2], vmem_in[2]
    for b in range(2):
        wait(loads[b])
        at = 0
        for i in range(b * MATRICES, (b + 1) * MATRICES):
            out = vmem_out[5 + i]
            for c in range(0, out.shape[0], 48):
                out[c : c + 48] = totals[b][at + c : at + c + 48].astype(F32)
            at += out.shape[0]
            stores[5 + n_pages + i].start()
    for i in range(n_pages):
        loads[3 + i].wait()
        stores[5 + i].start()
    loads[2].wait()
    n_lang = vmem_out[0].shape[0]
    vmem_out[0][...] = jnp.where(lax.axis_index("section") == 0, small[0, :n_lang], small[1, :n_lang])
    for i, out in enumerate(vmem_out[1:5]):
        first = n_lang + 2 * i
        out[...] = small[0, first : first + 2, : out.shape[1]]
    start(*stores[:5])
    wait(*stores)


def widen(totals, small, pages, shards, n_lang):
    widths = [total.shape[1] for total in totals]
    sums = [shape((n_lang, widths[0]), F32)] + [shape((2, w), F32) for w in widths for _ in range(2)]
    grads = [shape(m.shape, F32) for own in shards for m in own]
    inputs = (*totals, small, *pages)
    outs = sums + [shape(page.shape) for page in pages] + grads
    results = pl.pallas_call(
        functools.partial(widen_kernel, len(inputs), len(pages)), out_shape=outs,
        in_specs=[ANY] * len(inputs), out_specs=[ANY] * len(outs),
        scratch_shapes=vmem_like(inputs) + vmem_like(sums + grads)
        + [pltpu.SemaphoreType.DMA((len(inputs),)), pltpu.SemaphoreType.DMA((len(outs),))],
        compiler_params=pltpu.CompilerParams(vmem_limit_bytes=62 << 20), name="widen",
    )(*inputs)
    return results[0], results[1:5], results[5:9], results[9:13], results[13:17]


def per_device(
    mesh,
    text_input,
    layout_input,
    text_cotangent,
    layout_cotangent,
    page_counts,
    pad_mask,
    lang_ids,
    lang_table,
    text_project,
    text_outward,
    text_upward,
    text_downward,
    text_gains,
    text_biases,
    layout_project,
    layout_outward,
    layout_upward,
    layout_downward,
    layout_gains,
    layout_biases,
):
    def flat(project):
        return jnp.transpose(project[0], (1, 2, 0)).reshape(-1, project.shape[1])

    def flipped(block):
        return jnp.transpose(block[0], (0, 2, 1))

    shards = (
        Weights(flat(text_project), text_outward[0], text_upward[0], text_downward[0]),
        Weights(flat(layout_project), layout_outward[0], layout_upward[0], layout_downward[0]),
    )
    norms = ((text_gains[0], text_biases[0]), (layout_gains[0], layout_biases[0]))
    marks = (pad_mask, page_counts, lang_ids, lang_table)
    (x, y, probs, kept, weights), cots = layer_forward(
        mesh, text_input[0], flipped(layout_input), text_cotangent[0], flipped(layout_cotangent), shards, norms, marks
    )
    n_lang = lang_table.shape[0]
    totals, small, pages = layer_backward(mesh, x, y, probs, kept, weights, cots, norms, lang_ids, n_lang)
    lang_sum, norm_sums, pages, text_sums, layout_sums = widen(totals, small, pages, shards, n_lang)
    text_out, layout_out, text_grad, layout_grad = pages

    def unflat(grad, like):
        return jnp.transpose(grad.reshape(like.shape[2], like.shape[3], like.shape[1]), (2, 0, 1))[None]

    unflip = lambda block: jnp.transpose(block, (0, 2, 1))[None]
    return (
        text_out[None], unflip(layout_out), text_grad[None], unflip(layout_grad), lang_sum,
        unflat(text_sums[0], text_project), *(s[None] for s in text_sums[1:]), norm_sums[0][None], norm_sums[1][None],
        unflat(layout_sums[0], layout_project), *(s[None] for s in layout_sums[1:]),
        norm_sums[2][None], norm_sums[3][None],
    )


def solution(mesh):
    tokens = P("section", "dp", "tensor", None)
    weight_specs = (
        P("section", None, None, "tensor"), P("section", "tensor", None), P("section", None, "tensor"),
        P("section", "tensor", None), P("section", None, None), P("section", None, None),
    )
    in_specs = (tokens,) * 4 + (P(None, "dp"), P(None, "dp", None), P(None, "dp"), P()) + weight_specs * 2
    out_specs = (tokens,) * 4 + (P(),) + weight_specs * 2
    return jax.shard_map(
        functools.partial(per_device, mesh), mesh=mesh, in_specs=in_specs, out_specs=out_specs, check_vma=False
    )
```

```python
import functools
import math
import typing

import jax
import jax.numpy as jnp
from jax import lax
from jax.experimental import pallas as pl
from jax.experimental.pallas import tpu as pltpu
from jax.sharding import PartitionSpec as P

HEAD_TEXT = 64
HEAD_LAYOUT = 16
EPSILON = 1e-05
NEGATIVE = -1e30
HIGH = lax.Precision.HIGHEST
MESH = pl.DeviceIdType.MESH
BF = jnp.bfloat16
F32 = jnp.float32
ANY = pl.BlockSpec(memory_space=pl.ANY)


def remote(src, dst, send, recv, device):
    return pltpu.make_async_remote_copy(
        src_ref=src, dst_ref=dst, send_sem=send, recv_sem=recv, device_id=device, device_id_type=MESH
    )


def greet(section, tensor, sections, tensors, extra=()):
    barrier = pltpu.get_barrier_semaphore()
    for g in range(sections):
        for q in range(tensors):

            @pl.when((section != g) | (tensor != q))
            def _():
                pl.semaphore_signal(
                    barrier, inc=1, device_id={"section": g, "tensor": q}, device_id_type=MESH
                )

    for device in extra:
        pl.semaphore_signal(barrier, inc=1, device_id=device, device_id_type=MESH)
    pl.semaphore_wait(barrier, sections * tensors - 1 + len(extra))


GELU_P = 0.3275911
GELU_A = (0.254829592, -0.284496736, 1.421413741, -1.453152027, 1.061405429)
NN = (((1,), (0,)), ((), ()))
NT = (((1,), (1,)), ((), ()))
SCALES = (1.0 / math.sqrt(HEAD_TEXT), 1.0 / math.sqrt(HEAD_LAYOUT))
SIZES = (HEAD_TEXT, HEAD_LAYOUT)
ROWS = 128


class Weights(typing.NamedTuple):
    project: typing.Any
    outward: typing.Any
    upward: typing.Any
    downward: typing.Any


class Kept(typing.NamedTuple):
    qkv: typing.Any
    ctx: typing.Any
    n1: typing.Any
    r1: typing.Any
    low: typing.Any
    act: typing.Any
    slope: typing.Any
    n2: typing.Any
    r2: typing.Any


def dot(a, b, dims=NN):
    return lax.dot_general(a, b, dims, preferred_element_type=F32)


def gelu_pair(u):
    t = 1.0 / (1.0 + (GELU_P / math.sqrt(2.0)) * jnp.abs(u))
    e = jnp.exp(-0.5 * (u * u))
    a1, a2, a3, a4, a5 = (0.5 * a for a in GELU_A)
    tail = ((((a5 * t + a4) * t + a3) * t + a2) * t + a1) * t * e
    cdf = jnp.where(u >= 0, 1.0 - tail, tail)
    return u * cdf, cdf + u * e * (1.0 / math.sqrt(2.0 * math.pi))


def norm_rows(z, gain, offset):
    center = z - jnp.mean(z, axis=-1, keepdims=True)
    inverse = lax.rsqrt(jnp.mean(center * center, axis=-1, keepdims=True) + EPSILON)
    normed = center * inverse
    return normed * gain + offset, normed, inverse


def norm_rows_back(g, n, r, gain):
    t = g * gain
    return r * (t - jnp.mean(t, axis=-1, keepdims=True) - n * jnp.mean(t * n, axis=-1, keepdims=True))


class Staged:
    def __init__(self, tree, hbm, vmem, sem, inward):
        self.tree, self.vmem = tree, list(vmem)
        pairs = zip(hbm, vmem) if inward else zip(vmem, hbm)
        self.copies = [pltpu.make_async_copy(a, b, sem.at[i]) for i, (a, b) in enumerate(pairs)]

    def refs(self):
        return jax.tree.unflatten(self.tree, self.vmem)

    def parts(self):
        return jax.tree.unflatten(self.tree, self.copies)

    def start(self):
        for copy in self.copies:
            copy.start()

    def wait(self):
        for copy in self.copies:
            copy.wait()


def start(*copies):
    for copy in copies:
        copy.start()


def wait(*copies):
    for copy in copies:
        copy.wait()


def head_rows(stacks, slot, kind, local, scales=None):
    rows = []
    for b in range(2):
        first = kind * (stacks[b].shape[1] // 3) + local * SIZES[b]
        piece = stacks[b][slot, first : first + SIZES[b], :]
        rows.append(piece if scales is None else piece * BF(scales[b]))
    rows.append(jnp.zeros((128 - sum(SIZES), rows[0].shape[1]), BF))
    return jnp.concatenate(rows, axis=0)


def put_head(stacks, slot, kind, local, b, value):
    first = kind * (stacks[b].shape[1] // 3) + local * SIZES[b]
    stacks[b][slot, first : first + SIZES[b], :] = value.astype(BF)


def slot_of(u, core, chip):
    return ((chip + u // 2) % 2) * 2 + (core + u % 2) % 2


def forward_kernel(sections, tensors, shared, in_tree, out_tree, *refs):
    n_w, n_out = len(shared), out_tree.num_leaves
    sources = (refs[0:2], refs[2:4])
    shards = refs[4 : 4 + n_w]
    pad_mask, counts, lang_ids, lang_table, *norms = refs[4 + n_w : 12 + n_w]
    rest = refs[12 + n_w :]
    hbm_out, cots_out, rest = rest[:n_out], rest[n_out : n_out + 2], rest[n_out + 2 :]
    outgoing = Staged(out_tree, hbm_out, rest[:n_out], rest[n_out], False)
    rest = rest[n_out + 1 :]
    flipped, raw_x, y_narrow, *rest = rest
    nats, totals, rest = rest[0:2], rest[2:4], rest[4:]
    page_send, page_recv, w_send, w_recv, own_sem, hop_send, hop_recv, cot_sem = rest
    x, y_pages, probs_out, kept, weights = outgoing.refs()
    y = (y_pages[0], y_narrow)
    x_out, y_out, probs_copy, kept_out, weights_out = outgoing.parts()
    section, d, t = lax.axis_index("section"), lax.axis_index("dp"), lax.axis_index("tensor")
    core, chip, half_index = t % 2, t // 2, d % 2
    sibling, partner = t + 1 - 2 * core, (t + tensors // 2) % tensors
    mate = d + 1 - 2 * half_index
    micro, page = core, chip
    part_length = sources[0][0].shape[1]
    length = x[0].shape[0]
    blocks = [slice(c, c + 2 * ROWS) for c in range(0, length, 2 * ROWS)]
    full = (
        weights[0].project, weights[1].project, weights[0].outward, weights[0].upward,
        weights[0].downward, weights[1].outward, weights[1].upward, weights[1].downward,
    )
    greet(section, t, sections, tensors, ({"dp": mate},) if any(shared) else ())

    def half_of(ref, i, which):
        count = shards[i].shape[0] // 2
        return ref.at[pl.ds(pl.multiple_of(which * count, 16), count)] if shared[i] else ref

    def to_partner(i):
        return remote(
            half_of(shards[i], i, half_index), half_of(full[i].at[t], i, half_index),
            w_send.at[0, i], w_recv.at[0, i], {"tensor": partner},
        )

    def to_sibling(i):
        return remote(full[i].at[t], full[i].at[t], w_send.at[1, i], w_recv.at[1, i], {"tensor": sibling})

    def to_mate(i):
        ref = half_of(full[i].at[partner], i, half_index)
        return remote(ref, ref, w_send.at[2, i], w_recv.at[2, i], {"dp": mate})

    def on_first(i):
        ref = half_of(full[i].at[partner], i, half_index)
        return remote(ref, ref, w_send.at[3, i], w_recv.at[3, i], {"tensor": sibling})

    def on_second(i):
        ref = half_of(full[i].at[partner], i, 1 - half_index)
        return remote(ref, ref, w_send.at[4, i], w_recv.at[4, i], {"tensor": sibling})

    def keep(i):
        return pltpu.make_async_copy(shards[i], full[i].at[t], own_sem.at[i])

    def relay(*which):
        for i in which:
            to_partner(i).wait_recv()
            if shared[i]:
                to_mate(i).start()
            on_first(i).start()

    def relay_second(*which):
        for i in which:
            if shared[i]:
                to_mate(i).wait_recv()
                on_second(i).start()

    def early(*which):
        for i in which:
            to_sibling(i).wait_recv()

    def late(*which):
        for i in which:
            on_first(i).wait_recv()
            if shared[i]:
                on_second(i).wait_recv()

    def token_slot(g, a, index):
        start_at = pl.multiple_of(index * part_length, part_length)
        target = (raw_x, flipped)[a]
        return target.at[pl.ds(start_at, part_length)] if a == 0 else target.at[:, pl.ds(start_at, part_length)]

    def over_pages(g, act):
        for j in range(2):
            target = 2 * j + section
            here = (section == g) & (t == target)
            for a in range(2):
                act(g, j, a, target, here)

    def page_copy(g, j, a, target):
        return remote(
            sources[g][a].at[j], token_slot(g, a, t), page_send.at[g, j, a], page_recv.at[a, t],
            {"section": g, "tensor": target},
        )

    def page_start(g, j, a, target, here):
        @pl.when(here)
        def _():
            pltpu.make_async_copy(sources[g][a].at[j], token_slot(g, a, t), page_recv.at[a, t]).start()

        @pl.when(jnp.logical_not(here))
        def _():
            page_copy(g, j, a, target).start()

    def page_sent(g, j, a, target, here):
        @pl.when(jnp.logical_not(here))
        def _():
            page_copy(g, j, a, target).wait_send()

    def pages_arrived(g):
        for a in range(2):
            for q in range(tensors):
                slot = token_slot(g, a, q)
                remote(slot, slot, page_send.at[0, 0, a], page_recv.at[a, q], {"tensor": sibling}).wait_recv()

    def hop(b, n):
        return remote(
            y[b].at[blocks[n]], x[b].at[blocks[n]], hop_send.at[b, n], hop_recv.at[b, n], {"section": 1 - section}
        )

    over_pages(0, page_start)
    for i in range(n_w):
        keep(i).start()
    for i in range(n_w):
        to_partner(i).start()
    over_pages(1, page_start)
    for i in range(n_w):
        keep(i).wait()
        to_sibling(i).start()

    at_page = (lax.broadcasted_iota(jnp.int32, counts.shape, 0) == micro) & (
        lax.broadcasted_iota(jnp.int32, counts.shape, 1) == page
    )

    def own_entry(ref):
        return jnp.sum(jnp.where(at_page, ref[...], 0), axis=(0, 1), keepdims=True)

    positions = lax.broadcasted_iota(jnp.int32, (1, length), 1)
    mask_row = pad_mask[micro, pl.ds(page, 1), :]
    key_mask = (positions < own_entry(counts)) & ((mask_row == 1) | (positions == 0))
    groups = lax.broadcasted_iota(jnp.int32, (lang_table.shape[0], 1), 0)
    lang_row = jnp.sum(jnp.where(groups == own_entry(lang_ids), lang_table[...], 0.0), axis=0, keepdims=True)
    local_heads = weights[0].project.shape[1] // (3 * HEAD_TEXT)
    qkv = (kept[0].qkv, kept[1].qkv)

    @pl.when(section == 0)
    def _():
        pages_arrived(0)
        x[0][...] = (raw_x[...].astype(F32) + lang_row).astype(BF)
        x[1][...] = flipped[...].T
        early(0, 1)

    @pl.when(section == 1)
    def _():
        relay(*range(n_w))
        relay_second(*range(n_w))
        early(*range(n_w))
        late(*range(n_w))
        start(*weights_out[0], *weights_out[1])

    @pl.loop(0, 2)
    def _(half):
        @pl.when((half == 1) & (section == 0))
        def _():
            relay(0, 1)
            relay_second(0)
            late(0, 1)

        for n, block in enumerate(blocks):
            @pl.when((half == 0) & (section == 1))
            def _():
                for b in range(2):
                    hop(b, n).wait_recv()

            @pl.loop(0, 2)
            def _(u):
                slot = slot_of(2 * half + u, core, chip)
                for b in range(2):
                    qkv[b][slot, :, block] = dot(weights[b].project[slot], x[b][block], NT).astype(BF)

        @pl.loop(0, 2)
        def _(u):
            slot = slot_of(2 * half + u, core, chip)
            for local in range(local_heads):
                q = head_rows(qkv, slot, 0, local, SCALES).T
                scores = jnp.where(key_mask, dot(q, head_rows(qkv, slot, 1, local)), NEGATIVE)
                raised = jnp.exp(scores - jnp.max(scores, axis=-1, keepdims=True))
                probs = (raised * (1.0 / jnp.sum(raised, axis=-1, keepdims=True))).astype(BF)
                probs_out[slot, local] = probs
                ctx = dot(head_rows(qkv, slot, 2, local), probs, NT).astype(BF)
                kept[0].ctx[slot, local * HEAD_TEXT : (local + 1) * HEAD_TEXT, :] = ctx[:HEAD_TEXT]
                kept[1].ctx[slot, local * HEAD_LAYOUT : (local + 1) * HEAD_LAYOUT, :] = ctx[
                    HEAD_TEXT : HEAD_TEXT + HEAD_LAYOUT
                ]

    start(probs_copy, *x_out, *(k.qkv for k in kept_out), *(k.ctx for k in kept_out))

    def attend(b):
        gains, biases = norms[2 * b : 2 * b + 2]
        width = x[b].shape[1]
        nats[b][...] = kept[b].ctx[...].reshape(width, length).T
        wide = weights[b].outward[...].reshape(width, width)
        for block in blocks:
            h, n, r = norm_rows(x[b][block].astype(F32) + dot(nats[b][block], wide), gains[0:1], biases[0:1])
            totals[b][0, block] = h
            totals[b][1, block] = jnp.zeros(h.shape, F32)
            kept[b].n1[block] = n.astype(BF)
            kept[b].r1[block] = r
            kept[b].low[block] = h.astype(BF)
        start(kept_out[b].n1, kept_out[b].r1, kept_out[b].low)

    def feed(b, first, which):
        @pl.loop(first, first + 2)
        def _(u):
            slot = slot_of(u, core, chip)
            for block in which:
                act, slope = gelu_pair(dot(kept[b].low[block], weights[b].upward[slot]))
                act = act.astype(BF)
                kept[b].act[slot, block] = act
                kept[b].slope[slot, block] = slope.astype(BF)
                totals[b][1, block] += dot(act, weights[b].downward[slot])

    def finish(b):
        gains, biases = norms[2 * b : 2 * b + 2]
        for n, block in enumerate(blocks):
            feed(b, 2, [block])
            out, normed, r = norm_rows(totals[b][0, block] + totals[b][1, block], gains[1:2], biases[1:2])
            y[b][block] = out.astype(BF)
            kept[b].n2[block] = normed.astype(BF)
            kept[b].r2[block] = r

            @pl.when(section == 0)
            def _():
                hop(b, n).start()

        if b == 1:
            y_pages[1][...] = y_narrow[...].T
        start(y_out[b], kept_out[b].act, kept_out[b].slope, kept_out[b].n2, kept_out[b].r2)

    @pl.when(section == 0)
    def _():
        relay(2, 3)
        early(2)
        late(2)

    attend(0)

    @pl.when(section == 0)
    def _():
        early(3, 4)

    feed(0, 0, blocks)

    @pl.when(section == 0)
    def _():
        relay(4, 5, 6, 7)
        relay_second(3)
        early(5, 6, 7)
        late(5, 6, 7)

    attend(1)
    feed(1, 0, blocks)
    finish(1)

    @pl.when(section == 0)
    def _():
        relay_second(4)
        late(3, 4)

    finish(0)

    @pl.when(section == 0)
    def _():
        start(*weights_out[0], *weights_out[1])
        for b in range(2):
            for n in range(len(blocks)):
                hop(b, n).wait_send()

    for i in range(n_w):
        to_partner(i).wait_send()
        to_sibling(i).wait_send()
        on_first(i).wait_send()
        if shared[i]:
            to_mate(i).wait_send()
            on_second(i).wait_send()
    for g in range(sections):
        over_pages(g, page_sent)

    @pl.when(section == 1)
    def _():
        pages_arrived(1)
        copies = [pltpu.make_async_copy(v, h, cot_sem.at[i]) for i, (v, h) in enumerate(zip((raw_x, flipped), cots_out))]
        start(*copies)
        wait(*copies)

    outgoing.wait()


def vmem_like(tree):
    return [pltpu.VMEM(s.shape, s.dtype) for s in jax.tree.leaves(tree)]


VMEM = pl.BlockSpec(memory_space=pltpu.VMEM)


def shape(dims, dtype=BF):
    return jax.ShapeDtypeStruct(tuple(dims), dtype)


def layer_forward(mesh, text_in, layout_in, text_cot, layout_cot, shards, norms, marks):
    sections, dp, tensors = mesh.shape["section"], mesh.shape["dp"], mesh.shape["tensor"]
    length = text_in.shape[1] * tensors
    rows = (shape((length, text_in.shape[2])), shape((length, layout_in.shape[1])))
    local_heads = shards[0].project.shape[0] // (3 * HEAD_TEXT)
    kept = []
    for x, w in zip(rows, shards):
        units, column = shape((tensors, length, w.upward.shape[1])), shape((length, 1), F32)
        kept.append(Kept(
            qkv=shape((tensors, w.project.shape[0], length)), ctx=shape((tensors, w.outward.shape[0], length)),
            n1=shape(x.shape), r1=column, low=shape(x.shape), act=units, slope=units,
            n2=shape(x.shape), r2=column,
        ))
    weights = tuple(Weights(*(shape((tensors,) + m.shape) for m in w)) for w in shards)
    pages_out = (rows[0], shape((rows[1].shape[1], length)))
    outs = (rows, pages_out, shape((tensors, local_heads, length, length)), tuple(kept), weights)
    flat_out, out_tree = jax.tree.flatten(outs)
    (a, b) = shards
    ordered = (a.project, b.project, a.outward, a.upward, a.downward, b.outward, b.upward, b.downward)
    shared = tuple(dp % 2 == 0 and w.shape[0] >= 512 for w in ordered)
    n_w = len(ordered)
    cots = [rows[0], shape((rows[1].shape[1], length))]
    small = (*marks, *norms[0], *norms[1])
    results = pl.pallas_call(
        functools.partial(forward_kernel, sections, tensors, shared, None, out_tree),
        out_shape=flat_out + cots,
        in_specs=[ANY] * (4 + n_w) + [VMEM] * len(small),
        out_specs=[ANY] * (len(flat_out) + 2),
        scratch_shapes=vmem_like(flat_out) + [pltpu.SemaphoreType.DMA((len(flat_out),))]
        + [pltpu.VMEM(cots[1].shape, BF), pltpu.VMEM(cots[0].shape, BF), pltpu.VMEM(rows[1].shape, BF)]
        + [pltpu.VMEM(x.shape, BF) for x in rows]
        + [pltpu.VMEM((2,) + x.shape, F32) for x in rows]
        + [
            pltpu.SemaphoreType.DMA((sections, 2, 2)), pltpu.SemaphoreType.DMA((2, tensors)),
            pltpu.SemaphoreType.DMA((5, n_w)), pltpu.SemaphoreType.DMA((5, n_w)), pltpu.SemaphoreType.DMA((n_w,)),
            pltpu.SemaphoreType.DMA((2, length // (2 * ROWS))), pltpu.SemaphoreType.DMA((2, length // (2 * ROWS))),
            pltpu.SemaphoreType.DMA((2,)),
        ],
        compiler_params=pltpu.CompilerParams(
            collective_id=0, has_side_effects=True, vmem_limit_bytes=62 << 20
        ),
        name="layer_forward",
    )(text_in, layout_in, text_cot, layout_cot, *ordered, *small)
    return jax.tree.unflatten(out_tree, results[:-2]), tuple(results[-2:])


class Needed(typing.NamedTuple):
    n2: typing.Any
    r2: typing.Any
    downward: typing.Any
    slope: typing.Any
    upward: typing.Any
    n1: typing.Any
    r1: typing.Any
    outward: typing.Any
    low: typing.Any
    act: typing.Any
    qkv: typing.Any
    ctx: typing.Any
    project: typing.Any
    x: typing.Any


class Work(typing.NamedTuple):
    g: typing.Any
    gf: typing.Any
    ga: typing.Any
    dz: typing.Any
    dctx: typing.Any
    sums: typing.Any
    lowT: typing.Any
    raw: typing.Any
    from_sibling: typing.Any
    from_partner: typing.Any


class Chunk(typing.NamedTuple):
    b: typing.Any
    index: typing.Any
    first: typing.Any
    rows: typing.Any


MATRICES = 4


def matrix_rows(own):
    return own.project.shape[1], own.outward.shape[1], own.upward.shape[1], own.downward.shape[1]


def matrix_starts(own):
    sizes = matrix_rows(own)
    return [sum(sizes[:i]) for i in range(MATRICES + 1)]


def pieces_of(size, step):
    return [(f, step) for f in range(0, size, step)]


def backward_kernel(sections, tensors, chain, in_tree, *refs):
    n_in = in_tree.num_leaves
    hbm_in, refs = refs[:n_in], refs[n_in:]
    (cots, ys, lang_ids, gains), refs = (refs[0:2], refs[2:4], refs[4], refs[5:7]), refs[7:]
    results, small_out, page_outs, parked, refs = refs[0:2], refs[2], refs[3:7], refs[7:9], refs[9:]
    n_work = len(Work._fields)
    work, refs = (Work(*refs[:n_work]), Work(*refs[n_work : 2 * n_work])), refs[2 * n_work :]
    plain, refs = refs[: n_in - 2 * MATRICES], refs[n_in - 2 * MATRICES :]
    flipped, small_got, small_sum, refs = refs[0], refs[1], refs[2], refs[3:]
    text_out, layout_out, grad_out, layout_grad_out, *refs = refs
    in_sem, cot_sem, hop_send, hop_recv, sib_send, sib_recv, send, recv, credit, out_sem, park_sem, *refs = refs
    small_send, small_recv, page_send, page_recv, page_out_sem = refs
    section, d, t = lax.axis_index("section"), lax.axis_index("dp"), lax.axis_index("tensor")
    core, chip = t % 2, t // 2
    sibling = {"tensor": t + 1 - 2 * core}
    partner = {"tensor": (t + tensors // 2) % tensors}
    near, cross = {"dp": d + 1 - 2 * (d % 2)}, {"dp": 3 - d}
    outer = (d == 0) | (d == 3)
    other = {"section": 1 - section}
    hbm, probs_hbm = jax.tree.unflatten(in_tree, hbm_in)
    starts = [matrix_starts(own) for own in hbm]

    plain = list(plain)
    views = []
    for b in range(2):
        fields = {}
        for name, value in hbm[b]._asdict().items():
            if name in Weights._fields:
                i = Weights._fields.index(name)
                fields[name] = work[b].raw.at[:, pl.ds(starts[b][i], starts[b][i + 1] - starts[b][i])]
            else:
                fields[name] = plain.pop(0)
        views.append(Needed(**fields))
    probs_in = plain.pop(0)
    flat_views = jax.tree.leaves((tuple(views), probs_in))
    flat_copies = [pltpu.make_async_copy(a, v, in_sem.at[i]) for i, (a, v) in enumerate(zip(hbm_in, flat_views))]
    loads, probs_copy = jax.tree.unflatten(in_tree, flat_copies)
    length = work[0].gf.shape[0]
    local_heads = probs_in.shape[1]
    blocks = [slice(c, c + 2 * ROWS) for c in range(0, length, 2 * ROWS)]
    cot_copies = (
        pltpu.make_async_copy(cots[0], work[0].g, cot_sem.at[0]),
        pltpu.make_async_copy(cots[1], flipped, cot_sem.at[1]),
    )

    @pl.when(section == 1)
    def _():
        start(*cot_copies)

    start(*flat_copies)
    greet(section, t, sections, tensors, (near, cross) if chain else ())

    part_length = text_out.shape[1]
    micro, page = core, chip
    kinds = ((grad_out, layout_grad_out), (text_out, layout_out))
    pages = ((work[0].g, flipped), ys)

    def page_part(g, q, a):
        span = pl.ds(q * part_length, part_length)
        return pages[g][a].at[span] if a == 0 else pages[g][a].at[:, span]

    def each_page(g, act):
        for q in range(tensors):
            for a in range(2):
                here = (micro == g) & (t == q)

                @pl.when((section == g) & here)
                def _():
                    act(g, q, a, True)

                @pl.when((section == g) & jnp.logical_not(here))
                def _():
                    act(g, q, a, False)

    def page_copy(g, q, a):
        return remote(
            page_part(g, q, a), kinds[g][a].at[page], page_send.at[q, a], page_recv.at[g, a, page],
            {"section": micro, "tensor": q},
        )

    def page_start(g, q, a, here):
        if here:
            pltpu.make_async_copy(page_part(g, q, a), kinds[g][a].at[page], page_recv.at[g, a, page]).start()
        else:
            page_copy(g, q, a).start()

    def page_sent(g, q, a, here):
        if not here:
            page_copy(g, q, a).wait_send()

    each_page(1, page_start)

    def hop(b, n):
        part = work[b].g.at[blocks[n]]
        return remote(part, part, hop_send.at[b, n], hop_recv.at[b, n], other)

    step = 2 * ROWS
    up_first, down_first = starts[0][2], starts[0][3]
    up_count, down_count = (starts[0][3] - up_first) // step, (starts[0][4] - down_first) // step
    n_feed = up_count + down_count
    chunks = [Chunk(0, k, up_first + k * step, step) for k in range(n_feed)]
    later = [(1, 0, starts[1][MATRICES])]
    later += [(0, f, n) for f, n in pieces_of(starts[0][1], 192)]
    later += [(0, starts[0][1] + f, n) for f, n in pieces_of(starts[0][2] - starts[0][1], 64)]
    chunks += [Chunk(b, n_feed + i, f, n) for i, (b, f, n) in enumerate(later)]

    def feed_chunk(k):
        return Chunk(0, k, pl.multiple_of(up_first + k * step, 16), step)

    def span(ref, c):
        return ref.at[pl.ds(c.first, c.rows)]

    def to_sibling(c, j):
        w = work[c.b]
        return remote(
            span(w.raw.at[2 * j + 1 - core], c), span(w.from_sibling.at[j], c),
            sib_send.at[c.index, j], sib_recv.at[c.index, j], sibling,
        )

    def mine(c):
        return span(work[c.b].raw.at[t], c)

    def theirs(c):
        return span(work[c.b].raw.at[2 * (1 - chip) + core], c)

    def park(c):
        return pltpu.make_async_copy(theirs(c), span(parked[c.b], c), park_sem.at[c.index])

    def to_partner(c):
        return remote(
            span(parked[c.b], c), span(work[c.b].from_partner, c), send.at[0, c.index], recv.at[0, c.index], partner
        )

    def from_near(c):
        return span(work[c.b].from_sibling.at[0], c)

    def from_cross(c):
        return span(work[c.b].from_sibling.at[1], c)

    def to_near(c):
        return remote(mine(c), from_near(c), send.at[1, c.index], recv.at[1, c.index], near)

    def to_cross(c):
        return remote(mine(c), from_cross(c), send.at[2, c.index], recv.at[2, c.index], cross)

    def total_to_near(c):
        return remote(span(results[c.b], c), from_near(c), send.at[3, c.index], recv.at[3, c.index], near)

    def out_copy(c, source):
        return pltpu.make_async_copy(span(source, c), span(results[c.b], c), out_sem.at[c.index])

    def added(target, *sources):
        target[...] = sum(s[...].astype(F32) for s in sources).astype(BF)

    def send_to_partner(c):
        park(c).wait()
        to_partner(c).start()

    def send_to_sibling(c):
        for j in range(tensors // 2):
            to_sibling(c, j).start()

    def stage_sibling(c):
        w = work[c.b]
        for j in range(tensors // 2):
            to_sibling(c, j).wait_recv()
        added(theirs(c), theirs(c), span(w.from_sibling.at[1 - chip], c))
        park(c).start()
        added(mine(c), mine(c), span(w.from_sibling.at[chip], c))
        if chain:
            @pl.when(jnp.logical_not(outer))
            def _():
                for device in (near, cross):
                    pl.semaphore_signal(credit, inc=1, device_id=device, device_id_type=MESH)

    def stage_partner(c):
        to_partner(c).wait_recv()
        added(mine(c), mine(c), span(work[c.b].from_partner, c))
        if not chain:
            out_copy(c, work[c.b].raw.at[t]).start()
            return

        @pl.when(outer)
        def _():
            pl.semaphore_wait(credit, 1)
            to_near(c).start()

    def stage_near(c):
        @pl.when(jnp.logical_not(outer))
        def _():
            to_near(c).wait_recv()
            added(mine(c), mine(c), from_near(c))
            pl.semaphore_wait(credit, 1)
            to_cross(c).start()

    def stage_cross(c):
        @pl.when(jnp.logical_not(outer))
        def _():
            to_cross(c).wait_recv()
            total = work[c.b].from_partner
            added(span(total, c), mine(c), from_cross(c))
            out_copy(c, total).start()
            out_copy(c, total).wait()
            total_to_near(c).start()

    def stage_total(c):
        @pl.when(outer)
        def _():
            total_to_near(c).wait_recv()
            out_copy(c, work[c.b].from_sibling.at[0]).start()

    def feed_products():
        own, w = views[0], work[0]
        w.lowT[...] = own.low[...].T

        @pl.loop(0, up_count)
        def _(k):
            rows = pl.ds(pl.multiple_of(k * step, step), step)
            for q in range(tensors):
                w.raw[q, pl.ds(pl.multiple_of(up_first + k * step, 16), step), :] = dot(
                    w.lowT[rows, :], own.slope[q]
                ).astype(BF)
            send_to_sibling(feed_chunk(k))

        @pl.loop(0, down_count)
        def _(k):
            lanes = pl.ds(pl.multiple_of(k * step, step), step)
            for q in range(tensors):
                w.raw[q, pl.ds(pl.multiple_of(down_first + k * step, 16), step), :] = dot(
                    own.act[q, :, lanes].T, w.gf[...]
                ).astype(BF)
            send_to_sibling(feed_chunk(up_count + k))

    def later_product(c):
        own, w = views[c.b], work[c.b]
        for q in range(tensors):
            for i in range(MATRICES):
                first = max(c.first, starts[c.b][i])
                last = min(c.first + c.rows, starts[c.b][i + 1])
                if first >= last:
                    continue
                rows = slice(first - starts[c.b][i], last - starts[c.b][i])
                if i == 0:
                    value = dot(own.qkv[q, rows, :], own.x[...])
                elif i == 1:
                    value = dot(own.ctx[q, rows, :], w.ga[...])
                elif i == 2:
                    value = dot(w.lowT[rows, :], own.slope[q])
                else:
                    value = dot(own.act[q, :, rows].T, w.gf[...])
                w.raw[q, first:last, :] = value.astype(BF)
        send_to_sibling(c)

    @pl.when(section == 1)
    def _():
        wait(*cot_copies)
        work[1].g[...] = flipped[...].T

    for b in range(2):
        work[b].sums[...] = jnp.zeros(work[b].sums.shape, F32)
    for b in (1, 0):
        own_in = loads[b]
        wait(own_in.n2, own_in.r2, own_in.downward, own_in.slope, own_in.upward, own_in.n1, own_in.r1, own_in.outward)
    for n, block in enumerate(blocks):
        for b in (1, 0):
            own, w, gain = views[b], work[b], gains[b]

            @pl.when(section == 0)
            def _():
                hop(b, n).wait_recv()

            g, normed = w.g[block].astype(F32), own.n2[block].astype(F32)
            low = norm_rows_back(g, normed, own.r2[block], gain[1:2])
            w.dz[block] = low
            w.gf[block] = low.astype(BF)
            w.sums[1:2] += jnp.sum(g * normed, axis=0, keepdims=True)
            w.sums[3:4] += jnp.sum(g, axis=0, keepdims=True)

            @pl.loop(0, tensors)
            def _(q):
                d_act = dot(w.gf[block], own.downward[q], NT)
                d_pre = (d_act * own.slope[q, block].astype(F32)).astype(BF)
                own.slope[q, block] = d_pre
                w.dz[block] += dot(d_pre, own.upward[q], NT)

            g, normed = w.dz[block], own.n1[block].astype(F32)
            low = norm_rows_back(g, normed, own.r1[block], gain[0:1])
            w.dz[block] = low
            w.ga[block] = low.astype(BF)
            w.sums[0:1] += jnp.sum(g * normed, axis=0, keepdims=True)
            w.sums[2:3] += jnp.sum(g, axis=0, keepdims=True)
            for q in range(tensors):
                w.dctx[q, :, block] = dot(own.outward[q], w.ga[block], NT).astype(BF)

    wait(loads[0].low, loads[0].act)

    @pl.when(section == 0)
    def _():
        feed_products()

    wait(loads[0].qkv, loads[1].qkv, probs_copy)
    qkv = (views[0].qkv, views[1].qkv)
    text_rows, layout_rows = slice(0, HEAD_TEXT), slice(HEAD_TEXT, HEAD_TEXT + HEAD_LAYOUT)

    @pl.loop(0, tensors)
    def _(q):
        @pl.when((section == 0) & (q < n_feed // 2))
        def _():
            stage_sibling(feed_chunk(2 * q))
            stage_sibling(feed_chunk(2 * q + 1))

        @pl.when((section == 0) & (q == 0))
        def _():
            send_to_partner(chunks[0])
            send_to_partner(chunks[1])

        @pl.when((section == 0) & (q >= 2))
        def _():
            stage_partner(feed_chunk(q - 2))
            send_to_partner(feed_chunk(q))

        for local in range(local_heads):
            dcT = jnp.concatenate(
                [work[b].dctx[q, local * SIZES[b] : (local + 1) * SIZES[b], :] for b in range(2)]
                + [jnp.zeros((128 - sum(SIZES), length), BF)], axis=0,
            )
            dc = dcT.T
            lane = lax.broadcasted_iota(jnp.int32, dc.shape, 1)
            dc_layout = jnp.where(lane >= HEAD_TEXT, dc, jnp.zeros_like(dc))
            qT, kT, vT = (head_rows(qkv, q, kind, local, SCALES if kind == 0 else None) for kind in range(3))
            low = probs_in[q, local]
            probs = low.astype(F32)
            both = dot(dc, vT)
            ds_both = (probs * (both - jnp.sum(probs * both, axis=-1, keepdims=True))).astype(BF)
            single = dot(dc_layout, vT)
            ds_layout = (probs * (single - jnp.sum(probs * single, axis=-1, keepdims=True))).astype(BF)
            dvT = dot(dcT, low)
            put_head(qkv, q, 2, local, 0, dvT[text_rows])
            put_head(qkv, q, 2, local, 1, dvT[layout_rows])
            put_head(qkv, q, 0, local, 0, dot(kT[text_rows], ds_both, NT) * SCALES[0])
            put_head(qkv, q, 1, local, 0, dot(qT[text_rows], ds_both))
            put_head(qkv, q, 0, local, 1, dot(kT[layout_rows], ds_layout, NT) * SCALES[1])
            put_head(qkv, q, 1, local, 1, dot(qT[layout_rows], ds_layout))

    wait(loads[0].project, loads[1].project)
    page_sum = jnp.zeros((1, work[0].dz.shape[1]), F32)
    for n, block in enumerate(blocks):
        for b in (1, 0):
            down = work[b].dz[block]
            for q in range(tensors):
                down += dot(qkv[b][q, :, block].T, views[b].project[q])
            down = down.astype(BF)
            work[b].g[block] = down
            if b == 0:
                page_sum += jnp.sum(down.astype(F32), axis=0, keepdims=True)

            @pl.when(section == 1)
            def _():
                hop(b, n).start()

    wait(loads[1].low, loads[1].act)
    work[1].lowT[...] = views[1].low[...].T
    for own_in in loads:
        wait(own_in.ctx, own_in.x)
    @pl.when(section == 1)
    def _():
        feed_products()
        for c in chunks[:2]:
            stage_sibling(c)
            send_to_partner(c)

        @pl.loop(2, n_feed)
        def _(k):
            stage_sibling(feed_chunk(k))

    for c in chunks[n_feed:]:
        later_product(c)
    for c in chunks[n_feed:]:
        stage_sibling(c)

    @pl.when(section == 0)
    def _():
        flipped[...] = work[1].g[...].T
        each_page(0, page_start)

    at_page = (lax.broadcasted_iota(jnp.int32, lang_ids.shape, 0) == t % 2) & (
        lax.broadcasted_iota(jnp.int32, lang_ids.shape, 1) == t // 2
    )
    group = jnp.sum(jnp.where(at_page, lang_ids[...], 0), axis=(0, 1), keepdims=True)
    n_lang = small_out.shape[1] - 8
    chosen = (lax.broadcasted_iota(jnp.int32, (n_lang, 1), 0) == group) & (section == 0)
    small_sum[0, 0:n_lang] = jnp.where(chosen, page_sum, 0.0)
    small_sum[0, n_lang : n_lang + 4] = work[0].sums[...]
    small_sum[0, n_lang + 4 : n_lang + 8] = jnp.zeros((4, small_out.shape[2]), F32)
    small_sum[0, n_lang + 4 : n_lang + 8, : work[1].sums.shape[1]] = work[1].sums[...]

    def small_copy(i, device):
        return remote(small_sum.at[i], small_got.at[i], small_send.at[i], small_recv.at[i], device)

    if chain:
        small_copy(0, sibling).start()
    stages = [(0, stage_partner)] + ([(2, stage_near), (4, stage_cross), (6, stage_total)] if chain else [])
    for turn in range(len(chunks) + stages[-1][0]):

        def send_next(on_core):
            if turn + 2 < len(chunks):
                @pl.when((core == on_core) & ((section == 1) | (turn >= 2)))
                def _():
                    send_to_partner(chunks[turn + 2])

        for lag, stage in stages:
            k = turn - lag
            if not 0 <= k < len(chunks):
                continue
            if stage is stage_partner and k < 2:

                @pl.when(section == 1)
                def _():
                    stage_partner(chunks[k])
            else:
                stage(chunks[k])
            if stage is stage_partner:
                send_next(0)
        send_next(1)
        if not chain:
            continue
        if turn == 0:
            small_copy(0, sibling).wait_recv()
            small_sum[1] = small_sum[0] + small_got[0]
            small_copy(1, partner).start()
        if turn == 1:
            small_copy(1, partner).wait_recv()
            small_sum[2] = small_sum[1] + small_got[1]
            small_copy(2, near).start()
        if turn == 2:
            small_copy(2, near).wait_recv()
            small_sum[3] = small_sum[2] + small_got[2]

            @pl.when(jnp.logical_not(outer))
            def _():
                small_copy(3, cross).start()

        if turn == 4:
            @pl.when(jnp.logical_not(outer))
            def _():
                small_copy(3, cross).wait_recv()
                small_sum[4] = small_sum[3] + small_got[3]
                small_copy(4, near).start()

        if turn == 6:
            @pl.when(outer)
            def _():
                small_copy(4, near).wait_recv()
                small_sum[4] = small_got[4]

            small_sum[5] = small_sum[4]
            small_copy(5, other).start()
        if turn == 8:
            small_copy(5, other).wait_recv()
            small_out[0] = small_sum[5]
            small_out[1] = small_got[5]

    if chain:
        for i, device in enumerate((sibling, partner, near)):
            small_copy(i, device).wait_send()

        @pl.when(jnp.logical_not(outer))
        def _():
            small_copy(3, cross).wait_send()
            small_copy(4, near).wait_send()

        small_copy(5, other).wait_send()
    else:
        small_out[0] = small_sum[0]
        small_out[1] = small_sum[0]

    @pl.when(section == 1)
    def _():
        for b in range(2):
            for n in range(len(blocks)):
                hop(b, n).wait_send()

    for c in chunks:
        for j in range(tensors // 2):
            to_sibling(c, j).wait_send()
        to_partner(c).wait_send()
        if not chain:
            out_copy(c, work[c.b].from_partner).wait()
            continue

        @pl.when(outer)
        def _():
            to_near(c).wait_send()

        @pl.when(jnp.logical_not(outer))
        def _():
            to_cross(c).wait_send()
            total_to_near(c).wait_send()

        @pl.when(outer)
        def _():
            out_copy(c, work[c.b].from_partner).wait()

    for g in range(sections):
        each_page(g, page_sent)
        for a in range(2):
            for j in range(2):
                dst = kinds[g][a].at[j]
                remote(dst, dst, page_send.at[0, a], page_recv.at[g, a, j], partner).wait_recv()
    landed = (text_out, layout_out, grad_out, layout_grad_out)
    copies = [pltpu.make_async_copy(v, h, page_out_sem.at[i]) for i, (v, h) in enumerate(zip(landed, page_outs))]
    start(*copies)
    wait(*copies)


def layer_backward(mesh, x, y, probs, kept, weights, cots, norms, lang_ids, n_lang):
    sections, dp, tensors = mesh.shape["section"], mesh.shape["dp"], mesh.shape["tensor"]
    chain = dp == 4
    needed = tuple(
        Needed(
            n2=k.n2, r2=k.r2, downward=w.downward, slope=k.slope, upward=w.upward, n1=k.n1, r1=k.r1,
            outward=w.outward, low=k.low, act=k.act, qkv=k.qkv, ctx=k.ctx, project=w.project, x=rows,
        )
        for k, w, rows in zip(kept, weights, x)
    )
    flat_in, in_tree = jax.tree.flatten((needed, probs))
    plain = [v for own in needed for name, v in own._asdict().items() if name not in Weights._fields] + [probs]
    stacks = [(matrix_starts(own)[MATRICES], rows.shape[1]) for own, rows in zip(needed, x)]
    length = x[0].shape[0]
    work = []
    for own, rows, (count, width) in zip(needed, x, stacks):
        work += Work(
            g=shape(rows.shape), gf=shape(rows.shape), ga=shape(rows.shape), dz=shape(rows.shape, F32),
            dctx=shape(own.ctx.shape), sums=shape((4, width), F32), lowT=shape((width, length)),
            raw=shape((tensors, count, width)), from_sibling=shape((tensors // 2, count, width)),
            from_partner=shape((count, width)),
        )
    small = shape((2, n_lang + 8, x[0].shape[1]), F32)
    text_page = shape((2, length // tensors, x[0].shape[1]))
    layout_page = shape((2, x[1].shape[1], length // tensors))
    summed = [shape(s) for s in stacks]
    own = needed[0]
    n_feed = (own.upward.shape[1] + own.downward.shape[1]) // (2 * ROWS)
    n_chunks = n_feed + 1 + own.project.shape[1] // 192 + own.outward.shape[1] // 64
    n_blocks = length // (2 * ROWS)
    dma = pltpu.SemaphoreType.DMA
    results = pl.pallas_call(
        functools.partial(backward_kernel, sections, tensors, chain, in_tree),
        out_shape=summed + [small, text_page, layout_page, text_page, layout_page] + summed,
        in_specs=[ANY] * (len(flat_in) + 4) + [VMEM] * 3,
        out_specs=[ANY] * 2 + [VMEM] + [ANY] * 6,
        scratch_shapes=vmem_like(work) + vmem_like(plain)
        + [pltpu.VMEM(cots[1].shape, BF)] + [pltpu.VMEM((6,) + small.shape[1:], F32)] * 2
        + vmem_like([text_page, layout_page] * 2)
        + [dma((len(flat_in),)), dma((2,)), dma((2, n_blocks)), dma((2, n_blocks))]
        + [dma((n_chunks, tensors // 2))] * 2 + [dma((4, n_chunks))] * 2
        + [pltpu.SemaphoreType.REGULAR, dma((n_chunks,)), dma((n_chunks,))]
        + [dma((6,))] * 2 + [dma((tensors, 2)), dma((sections, 2, 2)), dma((4,))],
        compiler_params=pltpu.CompilerParams(
            collective_id=1, has_side_effects=True, vmem_limit_bytes=64 << 20
        ),
        name="layer_backward",
    )(*flat_in, *cots, *y, lang_ids, norms[0][0], norms[1][0])
    totals, small, pages = results[:2], results[2], results[3:7]
    if not chain:
        totals = lax.psum(tuple(totals), "dp")
        both = lax.psum(small[0], ("dp", "tensor"))
        small = jnp.stack([both, lax.ppermute(both, "section", [(0, 1), (1, 0)])])
    return totals, small, pages


def widen_kernel(n_in, n_pages, *refs):
    n_out = 5 + n_pages + 2 * MATRICES
    hbm_in, hbm_out = refs[:n_in], refs[n_in : n_in + n_out]
    vmem_in, vmem_out = refs[n_in + n_out : 2 * n_in + n_out], refs[2 * n_in + n_out : -2]
    in_sem, out_sem = refs[-2:]
    loads = [pltpu.make_async_copy(h, v, in_sem.at[i]) for i, (h, v) in enumerate(zip(hbm_in, vmem_in))]
    sources = vmem_out[:5] + vmem_in[3:] + vmem_out[5:]
    stores = [pltpu.make_async_copy(v, h, out_sem.at[i]) for i, (v, h) in enumerate(zip(sources, hbm_out))]
    start(*loads)
    totals, small = vmem_in[0:2], vmem_in[2]
    for b in range(2):
        wait(loads[b])
        at = 0
        for i in range(b * MATRICES, (b + 1) * MATRICES):
            out = vmem_out[5 + i]
            for c in range(0, out.shape[0], 48):
                out[c : c + 48] = totals[b][at + c : at + c + 48].astype(F32)
            at += out.shape[0]
            stores[5 + n_pages + i].start()
    for i in range(n_pages):
        loads[3 + i].wait()
        stores[5 + i].start()
    loads[2].wait()
    n_lang = vmem_out[0].shape[0]
    vmem_out[0][...] = jnp.where(lax.axis_index("section") == 0, small[0, :n_lang], small[1, :n_lang])
    for i, out in enumerate(vmem_out[1:5]):
        first = n_lang + 2 * i
        out[...] = small[0, first : first + 2, : out.shape[1]]
    start(*stores[:5])
    wait(*stores)


def widen(totals, small, pages, shards, n_lang):
    widths = [total.shape[1] for total in totals]
    sums = [shape((n_lang, widths[0]), F32)] + [shape((2, w), F32) for w in widths for _ in range(2)]
    grads = [shape(m.shape, F32) for own in shards for m in own]
    inputs = (*totals, small, *pages)
    outs = sums + [shape(page.shape) for page in pages] + grads
    results = pl.pallas_call(
        functools.partial(widen_kernel, len(inputs), len(pages)), out_shape=outs,
        in_specs=[ANY] * len(inputs), out_specs=[ANY] * len(outs),
        scratch_shapes=vmem_like(inputs) + vmem_like(sums + grads)
        + [pltpu.SemaphoreType.DMA((len(inputs),)), pltpu.SemaphoreType.DMA((len(outs),))],
        compiler_params=pltpu.CompilerParams(vmem_limit_bytes=62 << 20), name="widen",
    )(*inputs)
    return results[0], results[1:5], results[5:9], results[9:13], results[13:17]


def per_device(
    mesh,
    text_input,
    layout_input,
    text_cotangent,
    layout_cotangent,
    page_counts,
    pad_mask,
    lang_ids,
    lang_table,
    text_project,
    text_outward,
    text_upward,
    text_downward,
    text_gains,
    text_biases,
    layout_project,
    layout_outward,
    layout_upward,
    layout_downward,
    layout_gains,
    layout_biases,
):
    def flat(project):
        return jnp.transpose(project[0], (1, 2, 0)).reshape(-1, project.shape[1])

    def flipped(block):
        return jnp.transpose(block[0], (0, 2, 1))

    shards = (
        Weights(flat(text_project), text_outward[0], text_upward[0], text_downward[0]),
        Weights(flat(layout_project), layout_outward[0], layout_upward[0], layout_downward[0]),
    )
    norms = ((text_gains[0], text_biases[0]), (layout_gains[0], layout_biases[0]))
    marks = (pad_mask, page_counts, lang_ids, lang_table)
    (x, y, probs, kept, weights), cots = layer_forward(
        mesh, text_input[0], flipped(layout_input), text_cotangent[0], flipped(layout_cotangent), shards, norms, marks
    )
    n_lang = lang_table.shape[0]
    totals, small, pages = layer_backward(mesh, x, y, probs, kept, weights, cots, norms, lang_ids, n_lang)
    lang_sum, norm_sums, pages, text_sums, layout_sums = widen(totals, small, pages, shards, n_lang)
    text_out, layout_out, text_grad, layout_grad = pages

    def unflat(grad, like):
        return jnp.transpose(grad.reshape(like.shape[2], like.shape[3], like.shape[1]), (2, 0, 1))[None]

    unflip = lambda block: jnp.transpose(block, (0, 2, 1))[None]
    return (
        text_out[None], unflip(layout_out), text_grad[None], unflip(layout_grad), lang_sum,
        unflat(text_sums[0], text_project), *(s[None] for s in text_sums[1:]), norm_sums[0][None], norm_sums[1][None],
        unflat(layout_sums[0], layout_project), *(s[None] for s in layout_sums[1:]),
        norm_sums[2][None], norm_sums[3][None],
    )


def solution(mesh):
    tokens = P("section", "dp", "tensor", None)
    weight_specs = (
        P("section", None, None, "tensor"), P("section", "tensor", None), P("section", None, "tensor"),
        P("section", "tensor", None), P("section", None, None), P("section", None, None),
    )
    in_specs = (tokens,) * 4 + (P(None, "dp"), P(None, "dp", None), P(None, "dp"), P()) + weight_specs * 2
    out_specs = (tokens,) * 4 + (P(),) + weight_specs * 2
    return jax.shard_map(
        functools.partial(per_device, mesh), mesh=mesh, in_specs=in_specs, out_specs=out_specs, check_vma=False
    )
```

```python
import functools
import math
import typing

import jax
import jax.numpy as jnp
from jax import lax
from jax.experimental import pallas as pl
from jax.experimental.pallas import tpu as pltpu
from jax.sharding import PartitionSpec as P

HEAD_TEXT = 64
HEAD_LAYOUT = 16
EPSILON = 1e-05
NEGATIVE = -1e30
HIGH = lax.Precision.HIGHEST
MESH = pl.DeviceIdType.MESH
BF = jnp.bfloat16
F32 = jnp.float32
ANY = pl.BlockSpec(memory_space=pl.ANY)


def remote(src, dst, send, recv, device):
    return pltpu.make_async_remote_copy(
        src_ref=src, dst_ref=dst, send_sem=send, recv_sem=recv, device_id=device, device_id_type=MESH
    )


def greet(section, tensor, sections, tensors, extra=()):
    barrier = pltpu.get_barrier_semaphore()
    for g in range(sections):
        for q in range(tensors):

            @pl.when((section != g) | (tensor != q))
            def _():
                pl.semaphore_signal(
                    barrier, inc=1, device_id={"section": g, "tensor": q}, device_id_type=MESH
                )

    for device in extra:
        pl.semaphore_signal(barrier, inc=1, device_id=device, device_id_type=MESH)
    pl.semaphore_wait(barrier, sections * tensors - 1 + len(extra))


GELU_P = 0.3275911
GELU_A = (0.254829592, -0.284496736, 1.421413741, -1.453152027, 1.061405429)
NN = (((1,), (0,)), ((), ()))
NT = (((1,), (1,)), ((), ()))
SCALES = (1.0 / math.sqrt(HEAD_TEXT), 1.0 / math.sqrt(HEAD_LAYOUT))
SIZES = (HEAD_TEXT, HEAD_LAYOUT)
ROWS = 128


class Weights(typing.NamedTuple):
    project: typing.Any
    outward: typing.Any
    upward: typing.Any
    downward: typing.Any


class Kept(typing.NamedTuple):
    qkv: typing.Any
    ctx: typing.Any
    n1: typing.Any
    r1: typing.Any
    low: typing.Any
    act: typing.Any
    slope: typing.Any
    n2: typing.Any
    r2: typing.Any


def dot(a, b, dims=NN):
    return lax.dot_general(a, b, dims, preferred_element_type=F32)


def gelu_pair(u):
    t = 1.0 / (1.0 + (GELU_P / math.sqrt(2.0)) * jnp.abs(u))
    e = jnp.exp(-0.5 * (u * u))
    a1, a2, a3, a4, a5 = (0.5 * a for a in GELU_A)
    tail = ((((a5 * t + a4) * t + a3) * t + a2) * t + a1) * t * e
    cdf = jnp.where(u >= 0, 1.0 - tail, tail)
    return u * cdf, cdf + u * e * (1.0 / math.sqrt(2.0 * math.pi))


def norm_rows(z, gain, offset):
    center = z - jnp.mean(z, axis=-1, keepdims=True)
    inverse = lax.rsqrt(jnp.mean(center * center, axis=-1, keepdims=True) + EPSILON)
    normed = center * inverse
    return normed * gain + offset, normed, inverse


def norm_rows_back(g, n, r, gain):
    t = g * gain
    return r * (t - jnp.mean(t, axis=-1, keepdims=True) - n * jnp.mean(t * n, axis=-1, keepdims=True))


class Staged:
    def __init__(self, tree, hbm, vmem, sem, inward):
        self.tree, self.vmem = tree, list(vmem)
        pairs = zip(hbm, vmem) if inward else zip(vmem, hbm)
        self.copies = [pltpu.make_async_copy(a, b, sem.at[i]) for i, (a, b) in enumerate(pairs)]

    def refs(self):
        return jax.tree.unflatten(self.tree, self.vmem)

    def parts(self):
        return jax.tree.unflatten(self.tree, self.copies)

    def start(self):
        for copy in self.copies:
            copy.start()

    def wait(self):
        for copy in self.copies:
            copy.wait()


def start(*copies):
    for copy in copies:
        copy.start()


def wait(*copies):
    for copy in copies:
        copy.wait()


def head_rows(stacks, slot, kind, local, scales=None):
    rows = []
    for b in range(2):
        first = kind * (stacks[b].shape[1] // 3) + local * SIZES[b]
        piece = stacks[b][slot, first : first + SIZES[b], :]
        rows.append(piece if scales is None else piece * BF(scales[b]))
    rows.append(jnp.zeros((128 - sum(SIZES), rows[0].shape[1]), BF))
    return jnp.concatenate(rows, axis=0)


def put_head(stacks, slot, kind, local, b, value):
    first = kind * (stacks[b].shape[1] // 3) + local * SIZES[b]
    stacks[b][slot, first : first + SIZES[b], :] = value.astype(BF)


def hop_blocks(length):
    ends = [0, length // 2, length * 3 // 4, length]
    return [slice(a, b) for a, b in zip(ends, ends[1:])]


def slot_of(u, core, chip):
    return ((chip + u // 2) % 2) * 2 + (core + u % 2) % 2


def forward_kernel(sections, tensors, shared, in_tree, out_tree, *refs):
    n_w, n_out = len(shared), out_tree.num_leaves
    sources = (refs[0:2], refs[2:4])
    shards = refs[4 : 4 + n_w]
    pad_mask, counts, lang_ids, lang_table, *norms = refs[4 + n_w : 12 + n_w]
    rest = refs[12 + n_w :]
    hbm_out, cots_out, rest = rest[:n_out], rest[n_out : n_out + 2], rest[n_out + 2 :]
    outgoing = Staged(out_tree, hbm_out, rest[:n_out], rest[n_out], False)
    rest = rest[n_out + 1 :]
    flipped, raw_x, y_narrow, *rest = rest
    nats, totals, rest = rest[0:2], rest[2:4], rest[4:]
    page_send, page_recv, w_send, w_recv, own_sem, hop_send, hop_recv, cot_sem = rest
    x, y_pages, probs_out, kept, weights = outgoing.refs()
    y = (y_pages[0], y_narrow)
    x_out, y_out, probs_copy, kept_out, weights_out = outgoing.parts()
    section, d, t = lax.axis_index("section"), lax.axis_index("dp"), lax.axis_index("tensor")
    core, chip, half_index = t % 2, t // 2, d % 2
    sibling, partner = t + 1 - 2 * core, (t + tensors // 2) % tensors
    mate = d + 1 - 2 * half_index
    micro, page = core, chip
    part_length = sources[0][0].shape[1]
    length = x[0].shape[0]
    blocks = [slice(c, c + 2 * ROWS) for c in range(0, length, 2 * ROWS)]
    parts = hop_blocks(length)
    full = (
        weights[0].project, weights[1].project, weights[0].outward, weights[0].upward,
        weights[0].downward, weights[1].outward, weights[1].upward, weights[1].downward,
    )
    greet(section, t, sections, tensors, ({"dp": mate},) if any(shared) else ())

    def half_of(ref, i, which):
        count = shards[i].shape[0] // 2
        return ref.at[pl.ds(pl.multiple_of(which * count, 16), count)] if shared[i] else ref

    def to_partner(i):
        return remote(
            half_of(shards[i], i, half_index), half_of(full[i].at[t], i, half_index),
            w_send.at[0, i], w_recv.at[0, i], {"tensor": partner},
        )

    def to_sibling(i):
        return remote(full[i].at[t], full[i].at[t], w_send.at[1, i], w_recv.at[1, i], {"tensor": sibling})

    def to_mate(i):
        ref = half_of(full[i].at[partner], i, half_index)
        return remote(ref, ref, w_send.at[2, i], w_recv.at[2, i], {"dp": mate})

    def on_first(i):
        ref = half_of(full[i].at[partner], i, half_index)
        return remote(ref, ref, w_send.at[3, i], w_recv.at[3, i], {"tensor": sibling})

    def on_second(i):
        ref = half_of(full[i].at[partner], i, 1 - half_index)
        return remote(ref, ref, w_send.at[4, i], w_recv.at[4, i], {"tensor": sibling})

    def keep(i):
        return pltpu.make_async_copy(shards[i], full[i].at[t], own_sem.at[i])

    def relay(*which):
        for i in which:
            to_partner(i).wait_recv()
            if shared[i]:
                to_mate(i).start()
            on_first(i).start()

    def relay_second(*which):
        for i in which:
            if shared[i]:
                to_mate(i).wait_recv()
                on_second(i).start()

    def early(*which):
        for i in which:
            to_sibling(i).wait_recv()

    def late(*which):
        for i in which:
            on_first(i).wait_recv()
            if shared[i]:
                on_second(i).wait_recv()

    def token_slot(g, a, index):
        start_at = pl.multiple_of(index * part_length, part_length)
        target = (raw_x, flipped)[a]
        return target.at[pl.ds(start_at, part_length)] if a == 0 else target.at[:, pl.ds(start_at, part_length)]

    def over_pages(g, act):
        for j in range(2):
            target = 2 * j + section
            here = (section == g) & (t == target)
            for a in range(2):
                act(g, j, a, target, here)

    def page_copy(g, j, a, target):
        return remote(
            sources[g][a].at[j], token_slot(g, a, t), page_send.at[g, j, a], page_recv.at[a, t],
            {"section": g, "tensor": target},
        )

    def page_start(g, j, a, target, here):
        @pl.when(here)
        def _():
            pltpu.make_async_copy(sources[g][a].at[j], token_slot(g, a, t), page_recv.at[a, t]).start()

        @pl.when(jnp.logical_not(here))
        def _():
            page_copy(g, j, a, target).start()

    def page_sent(g, j, a, target, here):
        @pl.when(jnp.logical_not(here))
        def _():
            page_copy(g, j, a, target).wait_send()

    def pages_arrived(g):
        for a in range(2):
            for q in range(tensors):
                slot = token_slot(g, a, q)
                remote(slot, slot, page_send.at[0, 0, a], page_recv.at[a, q], {"tensor": sibling}).wait_recv()

    def hop(b, n):
        return remote(
            y[b].at[parts[n]], x[b].at[parts[n]], hop_send.at[b, n], hop_recv.at[b, n], {"section": 1 - section}
        )

    over_pages(0, page_start)
    for i in range(n_w):
        keep(i).start()
    for i in range(n_w):
        to_partner(i).start()
    over_pages(1, page_start)
    for i in range(n_w):
        keep(i).wait()
        to_sibling(i).start()

    at_page = (lax.broadcasted_iota(jnp.int32, counts.shape, 0) == micro) & (
        lax.broadcasted_iota(jnp.int32, counts.shape, 1) == page
    )

    def own_entry(ref):
        return jnp.sum(jnp.where(at_page, ref[...], 0), axis=(0, 1), keepdims=True)

    positions = lax.broadcasted_iota(jnp.int32, (1, length), 1)
    mask_row = pad_mask[micro, pl.ds(page, 1), :]
    key_mask = (positions < own_entry(counts)) & ((mask_row == 1) | (positions == 0))
    groups = lax.broadcasted_iota(jnp.int32, (lang_table.shape[0], 1), 0)
    lang_row = jnp.sum(jnp.where(groups == own_entry(lang_ids), lang_table[...], 0.0), axis=0, keepdims=True)
    local_heads = weights[0].project.shape[1] // (3 * HEAD_TEXT)
    qkv = (kept[0].qkv, kept[1].qkv)

    @pl.when(section == 0)
    def _():
        pages_arrived(0)
        x[0][...] = (raw_x[...].astype(F32) + lang_row).astype(BF)
        x[1][...] = flipped[...].T
        early(0, 1)

    @pl.when(section == 1)
    def _():
        relay(*range(n_w))
        relay_second(*range(n_w))
        early(*range(n_w))
        late(*range(n_w))
        start(*weights_out[0], *weights_out[1])

    @pl.loop(0, 2)
    def _(half):
        @pl.when((half == 1) & (section == 0))
        def _():
            relay(0, 1)
            relay_second(0)
            late(0, 1)

        for n, block in enumerate(parts):
            @pl.when((half == 0) & (section == 1))
            def _():
                for b in range(2):
                    hop(b, n).wait_recv()

            @pl.loop(0, 2)
            def _(u):
                slot = slot_of(2 * half + u, core, chip)
                for b in range(2):
                    qkv[b][slot, :, block] = dot(weights[b].project[slot], x[b][block], NT).astype(BF)

        @pl.loop(0, 2)
        def _(u):
            slot = slot_of(2 * half + u, core, chip)
            for local in range(local_heads):
                q = head_rows(qkv, slot, 0, local, SCALES).T
                scores = jnp.where(key_mask, dot(q, head_rows(qkv, slot, 1, local)), NEGATIVE)
                raised = jnp.exp(scores - jnp.max(scores, axis=-1, keepdims=True))
                probs = (raised * (1.0 / jnp.sum(raised, axis=-1, keepdims=True))).astype(BF)
                probs_out[slot, local] = probs
                ctx = dot(head_rows(qkv, slot, 2, local), probs, NT).astype(BF)
                kept[0].ctx[slot, local * HEAD_TEXT : (local + 1) * HEAD_TEXT, :] = ctx[:HEAD_TEXT]
                kept[1].ctx[slot, local * HEAD_LAYOUT : (local + 1) * HEAD_LAYOUT, :] = ctx[
                    HEAD_TEXT : HEAD_TEXT + HEAD_LAYOUT
                ]

    start(probs_copy, *x_out, *(k.qkv for k in kept_out), *(k.ctx for k in kept_out))

    def attend(b):
        gains, biases = norms[2 * b : 2 * b + 2]
        width = x[b].shape[1]
        nats[b][...] = kept[b].ctx[...].reshape(width, length).T
        wide = weights[b].outward[...].reshape(width, width)
        for block in blocks:
            h, n, r = norm_rows(x[b][block].astype(F32) + dot(nats[b][block], wide), gains[0:1], biases[0:1])
            totals[b][0, block] = h
            totals[b][1, block] = jnp.zeros(h.shape, F32)
            kept[b].n1[block] = n.astype(BF)
            kept[b].r1[block] = r
            kept[b].low[block] = h.astype(BF)
        start(kept_out[b].n1, kept_out[b].r1, kept_out[b].low)

    def feed(b, first, which):
        @pl.loop(first, first + 2)
        def _(u):
            slot = slot_of(u, core, chip)
            for block in which:
                act, slope = gelu_pair(dot(kept[b].low[block], weights[b].upward[slot]))
                act = act.astype(BF)
                kept[b].act[slot, block] = act
                kept[b].slope[slot, block] = slope.astype(BF)
                totals[b][1, block] += dot(act, weights[b].downward[slot])

    def finish(b):
        gains, biases = norms[2 * b : 2 * b + 2]
        for n, block in enumerate(parts):
            feed(b, 2, [block])
            out, normed, r = norm_rows(totals[b][0, block] + totals[b][1, block], gains[1:2], biases[1:2])
            y[b][block] = out.astype(BF)
            kept[b].n2[block] = normed.astype(BF)
            kept[b].r2[block] = r

            @pl.when(section == 0)
            def _():
                hop(b, n).start()

        if b == 1:
            y_pages[1][...] = y_narrow[...].T
        start(y_out[b], kept_out[b].act, kept_out[b].slope, kept_out[b].n2, kept_out[b].r2)

    @pl.when(section == 0)
    def _():
        relay(2, 3)
        early(2)
        late(2)

    attend(0)

    @pl.when(section == 0)
    def _():
        early(3, 4)

    feed(0, 0, blocks)

    @pl.when(section == 0)
    def _():
        relay(4, 5, 6, 7)
        relay_second(3)
        early(5, 6, 7)
        late(5, 6, 7)

    attend(1)
    feed(1, 0, blocks)
    finish(1)

    @pl.when(section == 0)
    def _():
        relay_second(4)
        late(3, 4)

    finish(0)

    @pl.when(section == 0)
    def _():
        start(*weights_out[0], *weights_out[1])
        for b in range(2):
            for n in range(len(parts)):
                hop(b, n).wait_send()

    for i in range(n_w):
        to_partner(i).wait_send()
        to_sibling(i).wait_send()
        on_first(i).wait_send()
        if shared[i]:
            to_mate(i).wait_send()
            on_second(i).wait_send()
    for g in range(sections):
        over_pages(g, page_sent)

    @pl.when(section == 1)
    def _():
        pages_arrived(1)
        copies = [pltpu.make_async_copy(v, h, cot_sem.at[i]) for i, (v, h) in enumerate(zip((raw_x, flipped), cots_out))]
        start(*copies)
        wait(*copies)

    outgoing.wait()


def vmem_like(tree):
    return [pltpu.VMEM(s.shape, s.dtype) for s in jax.tree.leaves(tree)]


VMEM = pl.BlockSpec(memory_space=pltpu.VMEM)


def shape(dims, dtype=BF):
    return jax.ShapeDtypeStruct(tuple(dims), dtype)


def layer_forward(mesh, text_in, layout_in, text_cot, layout_cot, shards, norms, marks):
    sections, dp, tensors = mesh.shape["section"], mesh.shape["dp"], mesh.shape["tensor"]
    length = text_in.shape[1] * tensors
    rows = (shape((length, text_in.shape[2])), shape((length, layout_in.shape[1])))
    local_heads = shards[0].project.shape[0] // (3 * HEAD_TEXT)
    kept = []
    for x, w in zip(rows, shards):
        units, column = shape((tensors, length, w.upward.shape[1])), shape((length, 1), F32)
        kept.append(Kept(
            qkv=shape((tensors, w.project.shape[0], length)), ctx=shape((tensors, w.outward.shape[0], length)),
            n1=shape(x.shape), r1=column, low=shape(x.shape), act=units, slope=units,
            n2=shape(x.shape), r2=column,
        ))
    weights = tuple(Weights(*(shape((tensors,) + m.shape) for m in w)) for w in shards)
    pages_out = (rows[0], shape((rows[1].shape[1], length)))
    outs = (rows, pages_out, shape((tensors, local_heads, length, length)), tuple(kept), weights)
    flat_out, out_tree = jax.tree.flatten(outs)
    (a, b) = shards
    ordered = (a.project, b.project, a.outward, a.upward, a.downward, b.outward, b.upward, b.downward)
    shared = tuple(dp % 2 == 0 and w.shape[0] >= 512 for w in ordered)
    n_w = len(ordered)
    cots = [rows[0], shape((rows[1].shape[1], length))]
    small = (*marks, *norms[0], *norms[1])
    results = pl.pallas_call(
        functools.partial(forward_kernel, sections, tensors, shared, None, out_tree),
        out_shape=flat_out + cots,
        in_specs=[ANY] * (4 + n_w) + [VMEM] * len(small),
        out_specs=[ANY] * (len(flat_out) + 2),
        scratch_shapes=vmem_like(flat_out) + [pltpu.SemaphoreType.DMA((len(flat_out),))]
        + [pltpu.VMEM(cots[1].shape, BF), pltpu.VMEM(cots[0].shape, BF), pltpu.VMEM(rows[1].shape, BF)]
        + [pltpu.VMEM(x.shape, BF) for x in rows]
        + [pltpu.VMEM((2,) + x.shape, F32) for x in rows]
        + [
            pltpu.SemaphoreType.DMA((sections, 2, 2)), pltpu.SemaphoreType.DMA((2, tensors)),
            pltpu.SemaphoreType.DMA((5, n_w)), pltpu.SemaphoreType.DMA((5, n_w)), pltpu.SemaphoreType.DMA((n_w,)),
            pltpu.SemaphoreType.DMA((2, len(hop_blocks(length)))), pltpu.SemaphoreType.DMA((2, len(hop_blocks(length)))),
            pltpu.SemaphoreType.DMA((2,)),
        ],
        compiler_params=pltpu.CompilerParams(
            collective_id=0, has_side_effects=True, vmem_limit_bytes=62 << 20
        ),
        name="layer_forward",
    )(text_in, layout_in, text_cot, layout_cot, *ordered, *small)
    return jax.tree.unflatten(out_tree, results[:-2]), tuple(results[-2:])


class Needed(typing.NamedTuple):
    n2: typing.Any
    r2: typing.Any
    downward: typing.Any
    slope: typing.Any
    upward: typing.Any
    n1: typing.Any
    r1: typing.Any
    outward: typing.Any
    low: typing.Any
    act: typing.Any
    qkv: typing.Any
    ctx: typing.Any
    project: typing.Any
    x: typing.Any


class Work(typing.NamedTuple):
    g: typing.Any
    gf: typing.Any
    ga: typing.Any
    dz: typing.Any
    dctx: typing.Any
    sums: typing.Any
    lowT: typing.Any
    raw: typing.Any
    from_sibling: typing.Any
    from_partner: typing.Any


class Chunk(typing.NamedTuple):
    b: typing.Any
    index: typing.Any
    first: typing.Any
    rows: typing.Any


MATRICES = 4


def matrix_rows(own):
    return own.project.shape[1], own.outward.shape[1], own.upward.shape[1], own.downward.shape[1]


def matrix_starts(own):
    sizes = matrix_rows(own)
    return [sum(sizes[:i]) for i in range(MATRICES + 1)]


def pieces_of(size, step):
    return [(f, step) for f in range(0, size, step)]


def backward_kernel(sections, tensors, chain, in_tree, *refs):
    n_in = in_tree.num_leaves
    hbm_in, refs = refs[:n_in], refs[n_in:]
    (cots, ys, lang_ids, gains), refs = (refs[0:2], refs[2:4], refs[4], refs[5:7]), refs[7:]
    results, small_out, page_outs, refs = refs[0:2], refs[2], refs[3:7], refs[7:]
    n_work = len(Work._fields)
    work, refs = (Work(*refs[:n_work]), Work(*refs[n_work : 2 * n_work])), refs[2 * n_work :]
    plain, refs = refs[: n_in - 2 * MATRICES], refs[n_in - 2 * MATRICES :]
    flipped, small_got, small_sum, refs = refs[0], refs[1], refs[2], refs[3:]
    text_out, layout_out, grad_out, layout_grad_out, *refs = refs
    in_sem, cot_sem, hop_send, hop_recv, sib_send, sib_recv, send, recv, credit, out_sem, *refs = refs
    small_send, small_recv, page_send, page_recv, page_out_sem = refs
    section, d, t = lax.axis_index("section"), lax.axis_index("dp"), lax.axis_index("tensor")
    core, chip = t % 2, t // 2
    sibling = {"tensor": t + 1 - 2 * core}
    partner = {"tensor": (t + tensors // 2) % tensors}
    near, cross = {"dp": d + 1 - 2 * (d % 2)}, {"dp": 3 - d}
    outer = (d == 0) | (d == 3)
    other = {"section": 1 - section}
    hbm, probs_hbm = jax.tree.unflatten(in_tree, hbm_in)
    starts = [matrix_starts(own) for own in hbm]

    plain = list(plain)
    views = []
    for b in range(2):
        fields = {}
        for name, value in hbm[b]._asdict().items():
            if name in Weights._fields:
                i = Weights._fields.index(name)
                fields[name] = work[b].raw.at[:, pl.ds(starts[b][i], starts[b][i + 1] - starts[b][i])]
            else:
                fields[name] = plain.pop(0)
        views.append(Needed(**fields))
    probs_in = plain.pop(0)
    flat_views = jax.tree.leaves((tuple(views), probs_in))
    flat_copies = [pltpu.make_async_copy(a, v, in_sem.at[i]) for i, (a, v) in enumerate(zip(hbm_in, flat_views))]
    loads, probs_copy = jax.tree.unflatten(in_tree, flat_copies)
    length = work[0].gf.shape[0]
    local_heads = probs_in.shape[1]
    blocks = hop_blocks(length)
    cot_copies = (
        pltpu.make_async_copy(cots[0], work[0].g, cot_sem.at[0]),
        pltpu.make_async_copy(cots[1], flipped, cot_sem.at[1]),
    )

    @pl.when(section == 1)
    def _():
        start(*cot_copies)

    for field in zip(loads[1], loads[0]):
        start(*field)
    probs_copy.start()
    greet(section, t, sections, tensors, (near, cross) if chain else ())

    part_length = text_out.shape[1]
    micro, page = core, chip
    kinds = ((grad_out, layout_grad_out), (text_out, layout_out))
    pages = ((work[0].g, flipped), ys)

    def page_part(g, q, a):
        span = pl.ds(q * part_length, part_length)
        return pages[g][a].at[span] if a == 0 else pages[g][a].at[:, span]

    def each_page(g, act):
        for q in range(tensors):
            for a in range(2):
                here = (micro == g) & (t == q)

                @pl.when((section == g) & here)
                def _():
                    act(g, q, a, True)

                @pl.when((section == g) & jnp.logical_not(here))
                def _():
                    act(g, q, a, False)

    def page_copy(g, q, a):
        return remote(
            page_part(g, q, a), kinds[g][a].at[page], page_send.at[q, a], page_recv.at[g, a, page],
            {"section": micro, "tensor": q},
        )

    def page_start(g, q, a, here):
        if here:
            pltpu.make_async_copy(page_part(g, q, a), kinds[g][a].at[page], page_recv.at[g, a, page]).start()
        else:
            page_copy(g, q, a).start()

    def page_sent(g, q, a, here):
        if not here:
            page_copy(g, q, a).wait_send()

    each_page(1, page_start)

    def hop(b, n):
        part = work[b].g.at[blocks[n]]
        return remote(part, part, hop_send.at[b, n], hop_recv.at[b, n], other)

    step = ROWS
    up_first, down_first = starts[0][2], starts[0][3]
    up_count, down_count = (starts[0][3] - up_first) // step, (starts[0][4] - down_first) // step
    n_feed = up_count + down_count
    chunks = [Chunk(0, k, up_first + k * step, step) for k in range(n_feed)]
    later = [(1, 0, starts[1][MATRICES])]
    later += [(0, f, n) for f, n in pieces_of(starts[0][1], 192)]
    later += [(0, starts[0][1] + f, n) for f, n in pieces_of(starts[0][2] - starts[0][1], 64)]
    chunks += [Chunk(b, n_feed + i, f, n) for i, (b, f, n) in enumerate(later)]

    def feed_chunk(k):
        return Chunk(0, k, pl.multiple_of(up_first + k * step, 16), step)

    def span(ref, c):
        return ref.at[pl.ds(c.first, c.rows)]

    def to_sibling(c, j):
        w = work[c.b]
        return remote(
            span(w.raw.at[2 * j + 1 - core], c), span(w.from_sibling.at[j], c),
            sib_send.at[c.index, j], sib_recv.at[c.index, j], sibling,
        )

    def mine(c):
        return span(work[c.b].raw.at[t], c)

    def theirs(c):
        return span(work[c.b].raw.at[2 * (1 - chip) + core], c)

    def to_partner(c):
        return remote(
            theirs(c), span(work[c.b].from_partner, c), send.at[0, c.index], recv.at[0, c.index], partner
        )

    def from_near(c):
        return span(work[c.b].from_sibling.at[0], c)

    def from_cross(c):
        return span(work[c.b].from_sibling.at[1], c)

    def to_near(c):
        return remote(mine(c), from_near(c), send.at[1, c.index], recv.at[1, c.index], near)

    def to_cross(c):
        return remote(mine(c), from_cross(c), send.at[2, c.index], recv.at[2, c.index], cross)

    def total_to_near(c):
        return remote(
            span(work[c.b].from_partner, c), from_near(c), send.at[3, c.index], recv.at[3, c.index], near
        )

    def out_copy(c, source):
        return pltpu.make_async_copy(span(source, c), span(results[c.b], c), out_sem.at[c.index])

    def added(target, *sources):
        target[...] = sum(s[...].astype(F32) for s in sources).astype(BF)

    def send_to_sibling(c):
        for j in range(tensors // 2):
            to_sibling(c, j).start()

    def stage_sibling(c):
        w = work[c.b]
        for j in range(tensors // 2):
            to_sibling(c, j).wait_recv()
        added(theirs(c), theirs(c), span(w.from_sibling.at[1 - chip], c))
        added(mine(c), mine(c), span(w.from_sibling.at[chip], c))
        if chain:
            @pl.when(jnp.logical_not(outer))
            def _():
                for device in (near, cross):
                    pl.semaphore_signal(credit, inc=1, device_id=device, device_id_type=MESH)

    def stage_partner(c):
        to_partner(c).wait_recv()
        added(mine(c), mine(c), span(work[c.b].from_partner, c))
        if not chain:
            out_copy(c, work[c.b].raw.at[t]).start()
            return

        @pl.when(outer)
        def _():
            pl.semaphore_wait(credit, 1)
            to_near(c).start()

    def stage_near(c):
        @pl.when(jnp.logical_not(outer))
        def _():
            to_near(c).wait_recv()
            added(mine(c), mine(c), from_near(c))
            pl.semaphore_wait(credit, 1)
            to_cross(c).start()

    def stage_cross(c):
        @pl.when(jnp.logical_not(outer))
        def _():
            to_cross(c).wait_recv()
            total = work[c.b].from_partner
            added(span(total, c), mine(c), from_cross(c))
            total_to_near(c).start()
            out_copy(c, total).start()

    def stage_total(c):
        @pl.when(outer)
        def _():
            total_to_near(c).wait_recv()
            out_copy(c, work[c.b].from_sibling.at[0]).start()

    def feed_products():
        own, w = views[0], work[0]
        w.lowT[...] = own.low[...].T

        @pl.loop(0, up_count)
        def _(k):
            rows = pl.ds(pl.multiple_of(k * step, step), step)
            for q in range(tensors):
                w.raw[q, pl.ds(pl.multiple_of(up_first + k * step, 16), step), :] = dot(
                    w.lowT[rows, :], own.slope[q]
                ).astype(BF)
            send_to_sibling(feed_chunk(k))

        @pl.loop(0, down_count)
        def _(k):
            lanes = pl.ds(pl.multiple_of(k * step, step), step)
            for q in range(tensors):
                w.raw[q, pl.ds(pl.multiple_of(down_first + k * step, 16), step), :] = dot(
                    own.act[q, :, lanes].T, w.gf[...]
                ).astype(BF)
            send_to_sibling(feed_chunk(up_count + k))

    def later_product(c):
        own, w = views[c.b], work[c.b]
        for q in range(tensors):
            for i in range(MATRICES):
                first = max(c.first, starts[c.b][i])
                last = min(c.first + c.rows, starts[c.b][i + 1])
                if first >= last:
                    continue
                rows = slice(first - starts[c.b][i], last - starts[c.b][i])
                if i == 0:
                    value = dot(own.qkv[q, rows, :], own.x[...])
                elif i == 1:
                    value = dot(own.ctx[q, rows, :], w.ga[...])
                elif i == 2:
                    value = dot(w.lowT[rows, :], own.slope[q])
                else:
                    value = dot(own.act[q, :, rows].T, w.gf[...])
                w.raw[q, first:last, :] = value.astype(BF)
        send_to_sibling(c)

    @pl.when(section == 1)
    def _():
        wait(*cot_copies)
        work[1].g[...] = flipped[...].T

    for b in range(2):
        work[b].sums[...] = jnp.zeros(work[b].sums.shape, F32)
    for n, block in enumerate(blocks):
        for b in (1, 0):
            own, own_in, w, gain = views[b], loads[b], work[b], gains[b]
            if n == 0:
                wait(own_in.n2, own_in.r2)

            @pl.when(section == 0)
            def _():
                hop(b, n).wait_recv()

            g, normed = w.g[block].astype(F32), own.n2[block].astype(F32)
            low = norm_rows_back(g, normed, own.r2[block], gain[1:2])
            w.dz[block] = low
            w.gf[block] = low.astype(BF)
            w.sums[1:2] += jnp.sum(g * normed, axis=0, keepdims=True)
            w.sums[3:4] += jnp.sum(g, axis=0, keepdims=True)

            if n == 0:
                wait(own_in.downward, own_in.slope, own_in.upward)

            @pl.loop(0, tensors)
            def _(q):
                d_act = dot(w.gf[block], own.downward[q], NT)
                d_pre = (d_act * own.slope[q, block].astype(F32)).astype(BF)
                own.slope[q, block] = d_pre
                w.dz[block] += dot(d_pre, own.upward[q], NT)

            if n == 0:
                wait(own_in.n1, own_in.r1, own_in.outward)
            g, normed = w.dz[block], own.n1[block].astype(F32)
            low = norm_rows_back(g, normed, own.r1[block], gain[0:1])
            w.dz[block] = low
            w.ga[block] = low.astype(BF)
            w.sums[0:1] += jnp.sum(g * normed, axis=0, keepdims=True)
            w.sums[2:3] += jnp.sum(g, axis=0, keepdims=True)
            for q in range(tensors):
                w.dctx[q, :, block] = dot(own.outward[q], w.ga[block], NT).astype(BF)

    wait(loads[0].low, loads[0].act)

    @pl.when(section == 0)
    def _():
        feed_products()

    wait(loads[0].qkv, loads[1].qkv, probs_copy)
    qkv = (views[0].qkv, views[1].qkv)
    text_rows, layout_rows = slice(0, HEAD_TEXT), slice(HEAD_TEXT, HEAD_TEXT + HEAD_LAYOUT)

    ahead = 3

    def turn(k, n_known):
        fixed = isinstance(k, int)

        def at(i, stage):
            if not fixed:
                pl.when((i >= 0) & (i < n_feed))(lambda: stage(feed_chunk(i)))
            elif 0 <= i < n_known:
                stage(chunks[i])

        def sibling_and_send(c):
            stage_sibling(c)
            to_partner(c).start()

        at(k + ahead, sibling_and_send)
        at(k, stage_partner)
        if chain:
            at(k - 2, stage_near)
            at(k - 4, stage_cross)
            at(k - 6, stage_total)

    def first_copies():
        for c in chunks[:ahead]:
            stage_sibling(c)
            to_partner(c).start()

    early_turns = 6

    @pl.when(section == 0)
    def _():
        first_copies()

    @pl.loop(0, tensors)
    def _(q):
        for local in range(local_heads):
            head = q * local_heads + local

            @pl.when((section == 0) & (head % 2 == 0) & (head < 2 * early_turns))
            def _():
                turn(head // 2, n_feed)

            dcT = jnp.concatenate(
                [work[b].dctx[q, local * SIZES[b] : (local + 1) * SIZES[b], :] for b in range(2)]
                + [jnp.zeros((128 - sum(SIZES), length), BF)], axis=0,
            )
            dc = dcT.T
            lane = lax.broadcasted_iota(jnp.int32, dc.shape, 1)
            dc_layout = jnp.where(lane >= HEAD_TEXT, dc, jnp.zeros_like(dc))
            qT, kT, vT = (head_rows(qkv, q, kind, local, SCALES if kind == 0 else None) for kind in range(3))
            low = probs_in[q, local]
            probs = low.astype(F32)
            both = dot(dc, vT)
            ds_both = (probs * (both - jnp.sum(probs * both, axis=-1, keepdims=True))).astype(BF)
            single = dot(dc_layout, vT)
            ds_layout = (probs * (single - jnp.sum(probs * single, axis=-1, keepdims=True))).astype(BF)
            dvT = dot(dcT, low)
            put_head(qkv, q, 2, local, 0, dvT[text_rows])
            put_head(qkv, q, 2, local, 1, dvT[layout_rows])
            put_head(qkv, q, 0, local, 0, dot(kT[text_rows], ds_both, NT) * SCALES[0])
            put_head(qkv, q, 1, local, 0, dot(qT[text_rows], ds_both))
            put_head(qkv, q, 0, local, 1, dot(kT[layout_rows], ds_layout, NT) * SCALES[1])
            put_head(qkv, q, 1, local, 1, dot(qT[layout_rows], ds_layout))

    wait(loads[0].project, loads[1].project)
    page_sum = jnp.zeros((1, work[0].dz.shape[1]), F32)
    for n, block in enumerate(blocks):
        for b in (1, 0):
            down = work[b].dz[block]
            for q in range(tensors):
                down += dot(qkv[b][q, :, block].T, views[b].project[q])
            down = down.astype(BF)
            work[b].g[block] = down
            if b == 0:
                page_sum += jnp.sum(down.astype(F32), axis=0, keepdims=True)

            @pl.when(section == 1)
            def _():
                hop(b, n).start()

    wait(loads[1].low, loads[1].act)
    work[1].lowT[...] = views[1].low[...].T
    for own_in in loads:
        wait(own_in.ctx, own_in.x)
    @pl.when(section == 1)
    def _():
        feed_products()
        first_copies()

    for c in chunks[n_feed:]:
        later_product(c)

    @pl.when(section == 0)
    def _():
        flipped[...] = work[1].g[...].T
        each_page(0, page_start)

    at_page = (lax.broadcasted_iota(jnp.int32, lang_ids.shape, 0) == t % 2) & (
        lax.broadcasted_iota(jnp.int32, lang_ids.shape, 1) == t // 2
    )
    group = jnp.sum(jnp.where(at_page, lang_ids[...], 0), axis=(0, 1), keepdims=True)
    n_lang = small_out.shape[1] - 8
    chosen = (lax.broadcasted_iota(jnp.int32, (n_lang, 1), 0) == group) & (section == 0)
    small_sum[0, 0:n_lang] = jnp.where(chosen, page_sum, 0.0)
    small_sum[0, n_lang : n_lang + 4] = work[0].sums[...]
    small_sum[0, n_lang + 4 : n_lang + 8] = jnp.zeros((4, small_out.shape[2]), F32)
    small_sum[0, n_lang + 4 : n_lang + 8, : work[1].sums.shape[1]] = work[1].sums[...]

    def small_copy(i, device):
        return remote(small_sum.at[i], small_got.at[i], small_send.at[i], small_recv.at[i], device)

    if chain:
        small_copy(0, sibling).start()
    @pl.when(section == 1)
    def _():
        @pl.loop(0, early_turns)
        def _(k):
            turn(k, n_feed)

    for k in range(early_turns, len(chunks) + (6 if chain else 0)):
        turn(k, len(chunks))
        if not chain:
            continue
        if k == early_turns:
            small_copy(0, sibling).wait_recv()
            small_sum[1] = small_sum[0] + small_got[0]
            small_copy(1, partner).start()
        if k == early_turns + 1:
            small_copy(1, partner).wait_recv()
            small_sum[2] = small_sum[1] + small_got[1]
            small_copy(2, near).start()
        if k == early_turns + 2:
            small_copy(2, near).wait_recv()
            small_sum[3] = small_sum[2] + small_got[2]

            @pl.when(jnp.logical_not(outer))
            def _():
                small_copy(3, cross).start()

        if k == early_turns + 4:
            @pl.when(jnp.logical_not(outer))
            def _():
                small_copy(3, cross).wait_recv()
                small_sum[4] = small_sum[3] + small_got[3]
                small_copy(4, near).start()

        if k == early_turns + 6:
            @pl.when(outer)
            def _():
                small_copy(4, near).wait_recv()
                small_sum[4] = small_got[4]

            small_sum[5] = small_sum[4]
            small_copy(5, other).start()

    if chain:
        for i, device in enumerate((sibling, partner, near)):
            small_copy(i, device).wait_send()

        @pl.when(jnp.logical_not(outer))
        def _():
            small_copy(3, cross).wait_send()
            small_copy(4, near).wait_send()

        small_copy(5, other).wait()
        small_out[0] = small_sum[5]
        small_out[1] = small_got[5]
    else:
        small_out[0] = small_sum[0]
        small_out[1] = small_sum[0]

    @pl.when(section == 1)
    def _():
        for b in range(2):
            for n in range(len(blocks)):
                hop(b, n).wait_send()

    for c in chunks:
        for j in range(tensors // 2):
            to_sibling(c, j).wait_send()
        to_partner(c).wait_send()
        if not chain:
            out_copy(c, work[c.b].from_partner).wait()
            continue

        @pl.when(outer)
        def _():
            to_near(c).wait_send()

        @pl.when(jnp.logical_not(outer))
        def _():
            to_cross(c).wait_send()
            total_to_near(c).wait_send()

        out_copy(c, work[c.b].from_partner).wait()

    for g in range(sections):
        each_page(g, page_sent)
        for a in range(2):
            for j in range(2):
                dst = kinds[g][a].at[j]
                remote(dst, dst, page_send.at[0, a], page_recv.at[g, a, j], partner).wait_recv()
    landed = (text_out, layout_out, grad_out, layout_grad_out)
    copies = [pltpu.make_async_copy(v, h, page_out_sem.at[i]) for i, (v, h) in enumerate(zip(landed, page_outs))]
    start(*copies)
    wait(*copies)


def layer_backward(mesh, x, y, probs, kept, weights, cots, norms, lang_ids, n_lang):
    sections, dp, tensors = mesh.shape["section"], mesh.shape["dp"], mesh.shape["tensor"]
    chain = dp == 4
    needed = tuple(
        Needed(
            n2=k.n2, r2=k.r2, downward=w.downward, slope=k.slope, upward=w.upward, n1=k.n1, r1=k.r1,
            outward=w.outward, low=k.low, act=k.act, qkv=k.qkv, ctx=k.ctx, project=w.project, x=rows,
        )
        for k, w, rows in zip(kept, weights, x)
    )
    flat_in, in_tree = jax.tree.flatten((needed, probs))
    plain = [v for own in needed for name, v in own._asdict().items() if name not in Weights._fields] + [probs]
    stacks = [(matrix_starts(own)[MATRICES], rows.shape[1]) for own, rows in zip(needed, x)]
    length = x[0].shape[0]
    work = []
    for own, rows, (count, width) in zip(needed, x, stacks):
        work += Work(
            g=shape(rows.shape), gf=shape(rows.shape), ga=shape(rows.shape), dz=shape(rows.shape, F32),
            dctx=shape(own.ctx.shape), sums=shape((4, width), F32), lowT=shape((width, length)),
            raw=shape((tensors, count, width)), from_sibling=shape((tensors // 2, count, width)),
            from_partner=shape((count, width)),
        )
    small = shape((2, n_lang + 8, x[0].shape[1]), F32)
    text_page = shape((2, length // tensors, x[0].shape[1]))
    layout_page = shape((2, x[1].shape[1], length // tensors))
    summed = [shape(s) for s in stacks]
    own = needed[0]
    n_feed = (own.upward.shape[1] + own.downward.shape[1]) // ROWS
    n_chunks = n_feed + 1 + own.project.shape[1] // 192 + own.outward.shape[1] // 64
    n_blocks = len(hop_blocks(length))
    dma = pltpu.SemaphoreType.DMA
    results = pl.pallas_call(
        functools.partial(backward_kernel, sections, tensors, chain, in_tree),
        out_shape=summed + [small, text_page, layout_page, text_page, layout_page],
        in_specs=[ANY] * (len(flat_in) + 4) + [VMEM] * 3,
        out_specs=[ANY] * 2 + [VMEM] + [ANY] * 4,
        scratch_shapes=vmem_like(work) + vmem_like(plain)
        + [pltpu.VMEM(cots[1].shape, BF)] + [pltpu.VMEM((6,) + small.shape[1:], F32)] * 2
        + vmem_like([text_page, layout_page] * 2)
        + [dma((len(flat_in),)), dma((2,)), dma((2, n_blocks)), dma((2, n_blocks))]
        + [dma((n_chunks, tensors // 2))] * 2 + [dma((4, n_chunks))] * 2
        + [pltpu.SemaphoreType.REGULAR, dma((n_chunks,))]
        + [dma((6,))] * 2 + [dma((tensors, 2)), dma((sections, 2, 2)), dma((4,))],
        compiler_params=pltpu.CompilerParams(
            collective_id=1, has_side_effects=True, vmem_limit_bytes=64 << 20
        ),
        name="layer_backward",
    )(*flat_in, *cots, *y, lang_ids, norms[0][0], norms[1][0])
    totals, small, pages = results[:2], results[2], results[3:7]
    if not chain:
        totals = lax.psum(tuple(totals), "dp")
        both = lax.psum(small[0], ("dp", "tensor"))
        small = jnp.stack([both, lax.ppermute(both, "section", [(0, 1), (1, 0)])])
    return totals, small, pages


def widen_kernel(n_in, n_pages, *refs):
    n_out = 5 + n_pages + 2 * MATRICES
    hbm_in, hbm_out = refs[:n_in], refs[n_in : n_in + n_out]
    vmem_in, vmem_out = refs[n_in + n_out : 2 * n_in + n_out], refs[2 * n_in + n_out : -2]
    in_sem, out_sem = refs[-2:]
    loads = [pltpu.make_async_copy(h, v, in_sem.at[i]) for i, (h, v) in enumerate(zip(hbm_in, vmem_in))]
    sources = vmem_out[:5] + vmem_in[3:] + vmem_out[5:]
    stores = [pltpu.make_async_copy(v, h, out_sem.at[i]) for i, (v, h) in enumerate(zip(sources, hbm_out))]
    start(*loads)
    totals, small = vmem_in[0:2], vmem_in[2]
    for b in range(2):
        wait(loads[b])
        at = 0
        for i in range(b * MATRICES, (b + 1) * MATRICES):
            out = vmem_out[5 + i]
            for c in range(0, out.shape[0], 48):
                out[c : c + 48] = totals[b][at + c : at + c + 48].astype(F32)
            at += out.shape[0]
            stores[5 + n_pages + i].start()
    for i in range(n_pages):
        loads[3 + i].wait()
        stores[5 + i].start()
    loads[2].wait()
    n_lang = vmem_out[0].shape[0]
    vmem_out[0][...] = jnp.where(lax.axis_index("section") == 0, small[0, :n_lang], small[1, :n_lang])
    for i, out in enumerate(vmem_out[1:5]):
        first = n_lang + 2 * i
        out[...] = small[0, first : first + 2, : out.shape[1]]
    start(*stores[:5])
    wait(*stores)


def widen(totals, small, pages, shards, n_lang):
    widths = [total.shape[1] for total in totals]
    sums = [shape((n_lang, widths[0]), F32)] + [shape((2, w), F32) for w in widths for _ in range(2)]
    grads = [shape(m.shape, F32) for own in shards for m in own]
    inputs = (*totals, small, *pages)
    outs = sums + [shape(page.shape) for page in pages] + grads
    results = pl.pallas_call(
        functools.partial(widen_kernel, len(inputs), len(pages)), out_shape=outs,
        in_specs=[ANY] * len(inputs), out_specs=[ANY] * len(outs),
        scratch_shapes=vmem_like(inputs) + vmem_like(sums + grads)
        + [pltpu.SemaphoreType.DMA((len(inputs),)), pltpu.SemaphoreType.DMA((len(outs),))],
        compiler_params=pltpu.CompilerParams(vmem_limit_bytes=62 << 20), name="widen",
    )(*inputs)
    return results[0], results[1:5], results[5:9], results[9:13], results[13:17]


def per_device(
    mesh,
    text_input,
    layout_input,
    text_cotangent,
    layout_cotangent,
    page_counts,
    pad_mask,
    lang_ids,
    lang_table,
    text_project,
    text_outward,
    text_upward,
    text_downward,
    text_gains,
    text_biases,
    layout_project,
    layout_outward,
    layout_upward,
    layout_downward,
    layout_gains,
    layout_biases,
):
    def flat(project):
        return jnp.transpose(project[0], (1, 2, 0)).reshape(-1, project.shape[1])

    def flipped(block):
        return jnp.transpose(block[0], (0, 2, 1))

    shards = (
        Weights(flat(text_project), text_outward[0], text_upward[0], text_downward[0]),
        Weights(flat(layout_project), layout_outward[0], layout_upward[0], layout_downward[0]),
    )
    norms = ((text_gains[0], text_biases[0]), (layout_gains[0], layout_biases[0]))
    marks = (pad_mask, page_counts, lang_ids, lang_table)
    (x, y, probs, kept, weights), cots = layer_forward(
        mesh, text_input[0], flipped(layout_input), text_cotangent[0], flipped(layout_cotangent), shards, norms, marks
    )
    n_lang = lang_table.shape[0]
    totals, small, pages = layer_backward(mesh, x, y, probs, kept, weights, cots, norms, lang_ids, n_lang)
    lang_sum, norm_sums, pages, text_sums, layout_sums = widen(totals, small, pages, shards, n_lang)
    text_out, layout_out, text_grad, layout_grad = pages

    def unflat(grad, like):
        return jnp.transpose(grad.reshape(like.shape[2], like.shape[3], like.shape[1]), (2, 0, 1))[None]

    unflip = lambda block: jnp.transpose(block, (0, 2, 1))[None]
    return (
        text_out[None], unflip(layout_out), text_grad[None], unflip(layout_grad), lang_sum,
        unflat(text_sums[0], text_project), *(s[None] for s in text_sums[1:]), norm_sums[0][None], norm_sums[1][None],
        unflat(layout_sums[0], layout_project), *(s[None] for s in layout_sums[1:]),
        norm_sums[2][None], norm_sums[3][None],
    )


def solution(mesh):
    tokens = P("section", "dp", "tensor", None)
    weight_specs = (
        P("section", None, None, "tensor"), P("section", "tensor", None), P("section", None, "tensor"),
        P("section", "tensor", None), P("section", None, None), P("section", None, None),
    )
    in_specs = (tokens,) * 4 + (P(None, "dp"), P(None, "dp", None), P(None, "dp"), P()) + weight_specs * 2
    out_specs = (tokens,) * 4 + (P(),) + weight_specs * 2
    return jax.shard_map(
        functools.partial(per_device, mesh), mesh=mesh, in_specs=in_specs, out_specs=out_specs, check_vma=False
    )
```

```python
import functools
import math
import typing

import jax
import jax.numpy as jnp
from jax import lax
from jax.experimental import pallas as pl
from jax.experimental.pallas import tpu as pltpu
from jax.sharding import PartitionSpec as P

HEAD_TEXT = 64
HEAD_LAYOUT = 16
EPSILON = 1e-05
NEGATIVE = -1e30
HIGH = lax.Precision.HIGHEST
MESH = pl.DeviceIdType.MESH
BF = jnp.bfloat16
F32 = jnp.float32
ANY = pl.BlockSpec(memory_space=pl.ANY)


def remote(src, dst, send, recv, device):
    return pltpu.make_async_remote_copy(
        src_ref=src, dst_ref=dst, send_sem=send, recv_sem=recv, device_id=device, device_id_type=MESH
    )


def greet(section, tensor, sections, tensors, extra=()):
    barrier = pltpu.get_barrier_semaphore()
    for g in range(sections):
        for q in range(tensors):

            @pl.when((section != g) | (tensor != q))
            def _():
                pl.semaphore_signal(
                    barrier, inc=1, device_id={"section": g, "tensor": q}, device_id_type=MESH
                )

    for device in extra:
        pl.semaphore_signal(barrier, inc=1, device_id=device, device_id_type=MESH)
    pl.semaphore_wait(barrier, sections * tensors - 1 + len(extra))


GELU_P = 0.3275911
GELU_A = (0.254829592, -0.284496736, 1.421413741, -1.453152027, 1.061405429)
NN = (((1,), (0,)), ((), ()))
NT = (((1,), (1,)), ((), ()))
SCALES = (1.0 / math.sqrt(HEAD_TEXT), 1.0 / math.sqrt(HEAD_LAYOUT))
SIZES = (HEAD_TEXT, HEAD_LAYOUT)
ROWS = 128


class Weights(typing.NamedTuple):
    project: typing.Any
    outward: typing.Any
    upward: typing.Any
    downward: typing.Any


class Kept(typing.NamedTuple):
    qkv: typing.Any
    ctx: typing.Any
    inv: typing.Any
    n1: typing.Any
    r1: typing.Any
    low: typing.Any
    act: typing.Any
    slope: typing.Any
    n2: typing.Any
    r2: typing.Any


def dot(a, b, dims=NN):
    return lax.dot_general(a, b, dims, preferred_element_type=F32)


def gelu_pair(u):
    t = 1.0 / (1.0 + (GELU_P / math.sqrt(2.0)) * jnp.abs(u))
    e = jnp.exp(-0.5 * (u * u))
    a1, a2, a3, a4, a5 = (0.5 * a for a in GELU_A)
    tail = ((((a5 * t + a4) * t + a3) * t + a2) * t + a1) * t * e
    cdf = jnp.where(u >= 0, 1.0 - tail, tail)
    return u * cdf, cdf + u * e * (1.0 / math.sqrt(2.0 * math.pi))


def norm_rows(z, gain, offset):
    center = z - jnp.mean(z, axis=-1, keepdims=True)
    inverse = lax.rsqrt(jnp.mean(center * center, axis=-1, keepdims=True) + EPSILON)
    normed = center * inverse
    return normed * gain + offset, normed, inverse


def norm_rows_back(g, n, r, gain):
    t = g * gain
    return r * (t - jnp.mean(t, axis=-1, keepdims=True) - n * jnp.mean(t * n, axis=-1, keepdims=True))


class Staged:
    def __init__(self, tree, hbm, vmem, sem, inward):
        self.tree, self.vmem = tree, list(vmem)
        pairs = zip(hbm, vmem) if inward else zip(vmem, hbm)
        self.copies = [pltpu.make_async_copy(a, b, sem.at[i]) for i, (a, b) in enumerate(pairs)]

    def refs(self):
        return jax.tree.unflatten(self.tree, self.vmem)

    def parts(self):
        return jax.tree.unflatten(self.tree, self.copies)

    def start(self):
        for copy in self.copies:
            copy.start()

    def wait(self):
        for copy in self.copies:
            copy.wait()


def start(*copies):
    for copy in copies:
        copy.start()


def wait(*copies):
    for copy in copies:
        copy.wait()


def head_rows(stacks, slot, kind, local, scales=None, extra=None):
    rows = []
    for b in range(2):
        piece = head_part(stacks, slot, kind, local, b)
        rows.append(piece if scales is None else piece * BF(scales[b]))
    length = rows[0].shape[1]
    rows.append(jnp.zeros((16, length), BF) if extra is None else extra)
    rows.append(jnp.zeros((128 - sum(SIZES) - 16, length), BF))
    return jnp.concatenate(rows, axis=0)


def head_part(stacks, slot, kind, local, b):
    first = kind * (stacks[b].shape[1] // 3) + local * SIZES[b]
    return stacks[b][slot, first : first + SIZES[b], :]


def small_blocks(block, step=64):
    return [slice(c, c + step) for c in range(block.start, block.stop, step)]


def put_head(stacks, slot, kind, local, b, value):
    first = kind * (stacks[b].shape[1] // 3) + local * SIZES[b]
    stacks[b][slot, first : first + SIZES[b], :] = value.astype(BF)


def hop_blocks(length):
    ends = [0, length // 2, length * 3 // 4, length]
    return [slice(a, b) for a, b in zip(ends, ends[1:])]


def slot_of(u, core, chip):
    return ((chip + u // 2) % 2) * 2 + (core + u % 2) % 2


def forward_kernel(sections, tensors, shared, in_tree, out_tree, *refs):
    n_w, n_out = len(shared), out_tree.num_leaves
    sources = (refs[0:2], refs[2:4])
    shards = refs[4 : 4 + n_w]
    pad_mask, counts, lang_ids, lang_table, *norms = refs[4 + n_w : 12 + n_w]
    rest = refs[12 + n_w :]
    hbm_out, cots_out, rest = rest[:n_out], rest[n_out : n_out + 2], rest[n_out + 2 :]
    outgoing = Staged(out_tree, hbm_out, rest[:n_out], rest[n_out], False)
    rest = rest[n_out + 1 :]
    flipped, raw_x, y_narrow, *rest = rest
    nats, totals, pre, rest = rest[0:2], rest[2:4], rest[4:6], rest[6:]
    page_send, page_recv, w_send, w_recv, own_sem, hop_send, hop_recv, cot_sem = rest
    x, y_pages, probs_out, kept, weights = outgoing.refs()
    y = (y_pages[0], y_narrow)
    x_out, y_out, probs_copy, kept_out, weights_out = outgoing.parts()
    section, d, t = lax.axis_index("section"), lax.axis_index("dp"), lax.axis_index("tensor")
    core, chip, half_index = t % 2, t // 2, d % 2
    sibling, partner = t + 1 - 2 * core, (t + tensors // 2) % tensors
    mate = d + 1 - 2 * half_index
    micro, page = core, chip
    part_length = sources[0][0].shape[1]
    length = x[0].shape[0]
    blocks = [slice(c, c + 2 * ROWS) for c in range(0, length, 2 * ROWS)]
    parts = hop_blocks(length)
    full = (
        weights[0].project, weights[1].project, weights[0].outward, weights[0].upward,
        weights[0].downward, weights[1].outward, weights[1].upward, weights[1].downward,
    )
    greet(section, t, sections, tensors, ({"dp": mate},) if any(shared) else ())

    def half_of(ref, i, which):
        count = shards[i].shape[0] // 2
        return ref.at[pl.ds(pl.multiple_of(which * count, 16), count)] if shared[i] else ref

    def to_partner(i):
        return remote(
            half_of(shards[i], i, half_index), half_of(full[i].at[t], i, half_index),
            w_send.at[0, i], w_recv.at[0, i], {"tensor": partner},
        )

    def to_sibling(i):
        return remote(full[i].at[t], full[i].at[t], w_send.at[1, i], w_recv.at[1, i], {"tensor": sibling})

    def to_mate(i):
        ref = half_of(full[i].at[partner], i, half_index)
        return remote(ref, ref, w_send.at[2, i], w_recv.at[2, i], {"dp": mate})

    def on_first(i):
        ref = half_of(full[i].at[partner], i, half_index)
        return remote(ref, ref, w_send.at[3, i], w_recv.at[3, i], {"tensor": sibling})

    def on_second(i):
        ref = half_of(full[i].at[partner], i, 1 - half_index)
        return remote(ref, ref, w_send.at[4, i], w_recv.at[4, i], {"tensor": sibling})

    def keep(i):
        return pltpu.make_async_copy(shards[i], full[i].at[t], own_sem.at[i])

    def relay(*which):
        for i in which:
            to_partner(i).wait_recv()
            if shared[i]:
                to_mate(i).start()
            on_first(i).start()

    def relay_second(*which):
        for i in which:
            if shared[i]:
                to_mate(i).wait_recv()
                on_second(i).start()

    def early(*which):
        for i in which:
            to_sibling(i).wait_recv()

    def late(*which):
        for i in which:
            on_first(i).wait_recv()
            if shared[i]:
                on_second(i).wait_recv()

    def token_slot(g, a, index):
        start_at = pl.multiple_of(index * part_length, part_length)
        target = (raw_x, flipped)[a]
        return target.at[pl.ds(start_at, part_length)] if a == 0 else target.at[:, pl.ds(start_at, part_length)]

    def over_pages(g, act):
        for j in range(2):
            target = 2 * j + section
            here = (section == g) & (t == target)
            for a in range(2):
                act(g, j, a, target, here)

    def page_copy(g, j, a, target):
        return remote(
            sources[g][a].at[j], token_slot(g, a, t), page_send.at[g, j, a], page_recv.at[a, t],
            {"section": g, "tensor": target},
        )

    def page_start(g, j, a, target, here):
        @pl.when(here)
        def _():
            pltpu.make_async_copy(sources[g][a].at[j], token_slot(g, a, t), page_recv.at[a, t]).start()

        @pl.when(jnp.logical_not(here))
        def _():
            page_copy(g, j, a, target).start()

    def page_sent(g, j, a, target, here):
        @pl.when(jnp.logical_not(here))
        def _():
            page_copy(g, j, a, target).wait_send()

    def pages_arrived(g):
        for a in range(2):
            for q in range(tensors):
                slot = token_slot(g, a, q)
                remote(slot, slot, page_send.at[0, 0, a], page_recv.at[a, q], {"tensor": sibling}).wait_recv()

    def hop(b, n):
        return remote(
            y[b].at[parts[n]], x[b].at[parts[n]], hop_send.at[b, n], hop_recv.at[b, n], {"section": 1 - section}
        )

    over_pages(0, page_start)
    for i in range(n_w):
        keep(i).start()
    for i in range(n_w):
        to_partner(i).start()
    over_pages(1, page_start)
    for i in range(n_w):
        keep(i).wait()
        to_sibling(i).start()

    at_page = (lax.broadcasted_iota(jnp.int32, counts.shape, 0) == micro) & (
        lax.broadcasted_iota(jnp.int32, counts.shape, 1) == page
    )

    def own_entry(ref):
        return jnp.sum(jnp.where(at_page, ref[...], 0), axis=(0, 1), keepdims=True)

    positions = lax.broadcasted_iota(jnp.int32, (1, length), 1)
    mask_row = pad_mask[micro, pl.ds(page, 1), :]
    key_mask = (positions < own_entry(counts)) & ((mask_row == 1) | (positions == 0))
    first_row = (lax.broadcasted_iota(jnp.int32, (16, length), 0) == 0).astype(F32)
    mask_row16 = (first_row * jnp.where(key_mask, 0.0, NEGATIVE)).astype(BF)
    groups = lax.broadcasted_iota(jnp.int32, (lang_table.shape[0], 1), 0)
    lang_row = jnp.sum(jnp.where(groups == own_entry(lang_ids), lang_table[...], 0.0), axis=0, keepdims=True)
    local_heads = weights[0].project.shape[1] // (3 * HEAD_TEXT)
    qkv = (kept[0].qkv, kept[1].qkv)

    @pl.when(section == 0)
    def _():
        pages_arrived(0)
        x[0][...] = (raw_x[...].astype(F32) + lang_row).astype(BF)
        x[1][...] = flipped[...].T
        early(0, 1)

    @pl.when(section == 1)
    def _():
        relay(*range(n_w))
        relay_second(*range(n_w))
        early(*range(n_w))
        late(*range(n_w))
        start(*weights_out[0], *weights_out[1])

    @pl.loop(0, 2)
    def _(half):
        @pl.when((half == 1) & (section == 0))
        def _():
            relay(0, 1)
            relay_second(0)
            late(0, 1)

        for n, block in enumerate(parts):
            @pl.when((half == 0) & (section == 1))
            def _():
                for b in range(2):
                    hop(b, n).wait_recv()

            @pl.loop(0, 2)
            def _(u):
                slot = slot_of(2 * half + u, core, chip)
                for b in range(2):
                    qkv[b][slot, :, block] = dot(weights[b].project[slot], x[b][block], NT).astype(BF)

        @pl.loop(0, 2)
        def _(u):
            slot = slot_of(2 * half + u, core, chip)
            for local in range(local_heads):
                q = head_rows(qkv, slot, 0, local, SCALES, first_row.astype(BF)).T
                kT = head_rows(qkv, slot, 1, local, None, mask_row16)
                for rows in small_blocks(slice(0, length)):
                    scores = dot(q[rows], kT)
                    raised = jnp.exp(scores - jnp.max(scores, axis=-1, keepdims=True))
                    probs_out[slot, local, rows, :] = raised.astype(BF)
                vT = head_rows(qkv, slot, 2, local, None, first_row.astype(BF))
                ctx = dot(vT, probs_out[slot, local], NT)
                inv = 1.0 / ctx[sum(SIZES) : sum(SIZES) + 1]
                ctx = (ctx * inv).astype(BF)
                kept[0].inv[slot, local : local + 1, :] = inv
                kept[0].ctx[slot, local * HEAD_TEXT : (local + 1) * HEAD_TEXT, :] = ctx[:HEAD_TEXT]
                kept[1].ctx[slot, local * HEAD_LAYOUT : (local + 1) * HEAD_LAYOUT, :] = ctx[
                    HEAD_TEXT : HEAD_TEXT + HEAD_LAYOUT
                ]

    kept[1].inv[...] = jnp.zeros(kept[1].inv.shape, F32)
    start(probs_copy, *x_out, *(c for k in kept_out for c in (k.qkv, k.ctx, k.inv)))

    def attend(b):
        gains, biases = norms[2 * b : 2 * b + 2]
        width = x[b].shape[1]
        nats[b][...] = kept[b].ctx[...].reshape(width, length).T
        wide = weights[b].outward[...].reshape(width, width)
        for block in blocks:
            totals[b][1, block] = dot(nats[b][block], wide)
            for rows in small_blocks(block):
                h, n, r = norm_rows(x[b][rows].astype(F32) + totals[b][1, rows], gains[0:1], biases[0:1])
                totals[b][0, rows] = h
                totals[b][1, rows] = jnp.zeros(h.shape, F32)
                kept[b].n1[rows] = n.astype(BF)
                kept[b].r1[rows] = r
                kept[b].low[rows] = h.astype(BF)
        start(kept_out[b].n1, kept_out[b].r1, kept_out[b].low)

    def feed(b, first, which):
        @pl.loop(first, first + 2)
        def _(u):
            slot = slot_of(u, core, chip)
            for block in which:
                pre[b][block] = dot(kept[b].low[block], weights[b].upward[slot])
                for rows in small_blocks(block, 16):
                    act, slope = gelu_pair(pre[b][rows])
                    kept[b].act[slot, rows] = act.astype(BF)
                    kept[b].slope[slot, rows] = slope.astype(BF)
                totals[b][1, block] += dot(kept[b].act[slot, block], weights[b].downward[slot])

    def finish(b):
        gains, biases = norms[2 * b : 2 * b + 2]
        for n, block in enumerate(parts):
            feed(b, 2, [block])
            for rows in small_blocks(block):
                out, normed, r = norm_rows(totals[b][0, rows] + totals[b][1, rows], gains[1:2], biases[1:2])
                y[b][rows] = out.astype(BF)
                kept[b].n2[rows] = normed.astype(BF)
                kept[b].r2[rows] = r

            @pl.when(section == 0)
            def _():
                hop(b, n).start()

        if b == 1:
            y_pages[1][...] = y_narrow[...].T
        start(y_out[b], kept_out[b].act, kept_out[b].slope, kept_out[b].n2, kept_out[b].r2)

    @pl.when(section == 0)
    def _():
        relay(2, 3)
        early(2)
        late(2)

    attend(0)

    @pl.when(section == 0)
    def _():
        early(3, 4)

    feed(0, 0, blocks)

    @pl.when(section == 0)
    def _():
        relay(4, 5, 6, 7)
        relay_second(3)
        early(5, 6, 7)
        late(5, 6, 7)

    attend(1)
    feed(1, 0, blocks)
    finish(1)

    @pl.when(section == 0)
    def _():
        relay_second(4)
        late(3, 4)

    finish(0)

    @pl.when(section == 0)
    def _():
        start(*weights_out[0], *weights_out[1])
        for b in range(2):
            for n in range(len(parts)):
                hop(b, n).wait_send()

    for i in range(n_w):
        to_partner(i).wait_send()
        to_sibling(i).wait_send()
        on_first(i).wait_send()
        if shared[i]:
            to_mate(i).wait_send()
            on_second(i).wait_send()
    for g in range(sections):
        over_pages(g, page_sent)

    @pl.when(section == 1)
    def _():
        pages_arrived(1)
        copies = [pltpu.make_async_copy(v, h, cot_sem.at[i]) for i, (v, h) in enumerate(zip((raw_x, flipped), cots_out))]
        start(*copies)
        wait(*copies)

    outgoing.wait()


def vmem_like(tree):
    return [pltpu.VMEM(s.shape, s.dtype) for s in jax.tree.leaves(tree)]


VMEM = pl.BlockSpec(memory_space=pltpu.VMEM)


def shape(dims, dtype=BF):
    return jax.ShapeDtypeStruct(tuple(dims), dtype)


def layer_forward(mesh, text_in, layout_in, text_cot, layout_cot, shards, norms, marks):
    sections, dp, tensors = mesh.shape["section"], mesh.shape["dp"], mesh.shape["tensor"]
    length = text_in.shape[1] * tensors
    rows = (shape((length, text_in.shape[2])), shape((length, layout_in.shape[1])))
    local_heads = shards[0].project.shape[0] // (3 * HEAD_TEXT)
    kept = []
    for x, w in zip(rows, shards):
        units, column = shape((tensors, length, w.upward.shape[1])), shape((length, 1), F32)
        kept.append(Kept(
            qkv=shape((tensors, w.project.shape[0], length)), ctx=shape((tensors, w.outward.shape[0], length)),
            inv=shape((tensors, local_heads, length), F32),
            n1=shape(x.shape), r1=column, low=shape(x.shape), act=units, slope=units,
            n2=shape(x.shape), r2=column,
        ))
    weights = tuple(Weights(*(shape((tensors,) + m.shape) for m in w)) for w in shards)
    pages_out = (rows[0], shape((rows[1].shape[1], length)))
    outs = (rows, pages_out, shape((tensors, local_heads, length, length)), tuple(kept), weights)
    flat_out, out_tree = jax.tree.flatten(outs)
    (a, b) = shards
    ordered = (a.project, b.project, a.outward, a.upward, a.downward, b.outward, b.upward, b.downward)
    shared = tuple(dp % 2 == 0 and w.shape[0] >= 512 for w in ordered)
    n_w = len(ordered)
    cots = [rows[0], shape((rows[1].shape[1], length))]
    small = (*marks, *norms[0], *norms[1])
    results = pl.pallas_call(
        functools.partial(forward_kernel, sections, tensors, shared, None, out_tree),
        out_shape=flat_out + cots,
        in_specs=[ANY] * (4 + n_w) + [VMEM] * len(small),
        out_specs=[ANY] * (len(flat_out) + 2),
        scratch_shapes=vmem_like(flat_out) + [pltpu.SemaphoreType.DMA((len(flat_out),))]
        + [pltpu.VMEM(cots[1].shape, BF), pltpu.VMEM(cots[0].shape, BF), pltpu.VMEM(rows[1].shape, BF)]
        + [pltpu.VMEM(x.shape, BF) for x in rows]
        + [pltpu.VMEM((2,) + x.shape, F32) for x in rows]
        + [pltpu.VMEM((length, w.upward.shape[1]), F32) for w in shards]
        + [
            pltpu.SemaphoreType.DMA((sections, 2, 2)), pltpu.SemaphoreType.DMA((2, tensors)),
            pltpu.SemaphoreType.DMA((5, n_w)), pltpu.SemaphoreType.DMA((5, n_w)), pltpu.SemaphoreType.DMA((n_w,)),
            pltpu.SemaphoreType.DMA((2, len(hop_blocks(length)))), pltpu.SemaphoreType.DMA((2, len(hop_blocks(length)))),
            pltpu.SemaphoreType.DMA((2,)),
        ],
        compiler_params=pltpu.CompilerParams(
            collective_id=0, has_side_effects=True, vmem_limit_bytes=62 << 20
        ),
        name="layer_forward",
    )(text_in, layout_in, text_cot, layout_cot, *ordered, *small)
    return jax.tree.unflatten(out_tree, results[:-2]), tuple(results[-2:])


class Needed(typing.NamedTuple):
    n2: typing.Any
    r2: typing.Any
    downward: typing.Any
    slope: typing.Any
    upward: typing.Any
    n1: typing.Any
    r1: typing.Any
    outward: typing.Any
    low: typing.Any
    act: typing.Any
    qkv: typing.Any
    ctx: typing.Any
    inv: typing.Any
    project: typing.Any
    x: typing.Any


class Work(typing.NamedTuple):
    g: typing.Any
    gf: typing.Any
    ga: typing.Any
    dz: typing.Any
    dctx: typing.Any
    sums: typing.Any
    lowT: typing.Any
    raw: typing.Any
    from_sibling: typing.Any
    from_partner: typing.Any


class Chunk(typing.NamedTuple):
    b: typing.Any
    index: typing.Any
    first: typing.Any
    rows: typing.Any


MATRICES = 4


def matrix_rows(own):
    return own.project.shape[1], own.outward.shape[1], own.upward.shape[1], own.downward.shape[1]


def matrix_starts(own):
    sizes = matrix_rows(own)
    return [sum(sizes[:i]) for i in range(MATRICES + 1)]


def pieces_of(size, step):
    return [(f, step) for f in range(0, size, step)]


def backward_kernel(sections, tensors, chain, in_tree, *refs):
    n_in = in_tree.num_leaves
    hbm_in, refs = refs[:n_in], refs[n_in:]
    (cots, ys, lang_ids, gains), refs = (refs[0:2], refs[2:4], refs[4], refs[5:7]), refs[7:]
    results, small_out, page_outs, refs = refs[0:2], refs[2], refs[3:7], refs[7:]
    n_work = len(Work._fields)
    work, refs = (Work(*refs[:n_work]), Work(*refs[n_work : 2 * n_work])), refs[2 * n_work :]
    plain, refs = refs[: n_in - 2 * MATRICES], refs[n_in - 2 * MATRICES :]
    flipped, small_got, small_sum, refs = refs[0], refs[1], refs[2], refs[3:]
    text_out, layout_out, grad_out, layout_grad_out, *refs = refs
    in_sem, cot_sem, hop_send, hop_recv, sib_send, sib_recv, send, recv, credit, out_sem, *refs = refs
    small_send, small_recv, page_send, page_recv, page_out_sem = refs
    section, d, t = lax.axis_index("section"), lax.axis_index("dp"), lax.axis_index("tensor")
    core, chip = t % 2, t // 2
    sibling = {"tensor": t + 1 - 2 * core}
    partner = {"tensor": (t + tensors // 2) % tensors}
    near, cross = {"dp": d + 1 - 2 * (d % 2)}, {"dp": 3 - d}
    outer = (d == 0) | (d == 3)
    other = {"section": 1 - section}
    hbm, probs_hbm = jax.tree.unflatten(in_tree, hbm_in)
    starts = [matrix_starts(own) for own in hbm]

    plain = list(plain)
    views = []
    for b in range(2):
        fields = {}
        for name, value in hbm[b]._asdict().items():
            if name in Weights._fields:
                i = Weights._fields.index(name)
                fields[name] = work[b].raw.at[:, pl.ds(starts[b][i], starts[b][i + 1] - starts[b][i])]
            else:
                fields[name] = plain.pop(0)
        views.append(Needed(**fields))
    probs_in = plain.pop(0)
    flat_views = jax.tree.leaves((tuple(views), probs_in))
    flat_copies = [pltpu.make_async_copy(a, v, in_sem.at[i]) for i, (a, v) in enumerate(zip(hbm_in, flat_views))]
    loads, probs_copy = jax.tree.unflatten(in_tree, flat_copies)
    length = work[0].gf.shape[0]
    local_heads = probs_in.shape[1]
    blocks = hop_blocks(length)
    cot_copies = (
        pltpu.make_async_copy(cots[0], work[0].g, cot_sem.at[0]),
        pltpu.make_async_copy(cots[1], flipped, cot_sem.at[1]),
    )

    @pl.when(section == 1)
    def _():
        start(*cot_copies)

    for field in zip(loads[1], loads[0]):
        start(*field)
    probs_copy.start()
    greet(section, t, sections, tensors, (near, cross) if chain else ())

    part_length = text_out.shape[1]
    micro, page = core, chip
    kinds = ((grad_out, layout_grad_out), (text_out, layout_out))
    pages = ((work[0].g, flipped), ys)

    def page_part(g, q, a):
        span = pl.ds(q * part_length, part_length)
        return pages[g][a].at[span] if a == 0 else pages[g][a].at[:, span]

    def each_page(g, act):
        for q in range(tensors):
            for a in range(2):
                here = (micro == g) & (t == q)

                @pl.when((section == g) & here)
                def _():
                    act(g, q, a, True)

                @pl.when((section == g) & jnp.logical_not(here))
                def _():
                    act(g, q, a, False)

    def page_copy(g, q, a):
        return remote(
            page_part(g, q, a), kinds[g][a].at[page], page_send.at[q, a], page_recv.at[g, a, page],
            {"section": micro, "tensor": q},
        )

    def page_start(g, q, a, here):
        if here:
            pltpu.make_async_copy(page_part(g, q, a), kinds[g][a].at[page], page_recv.at[g, a, page]).start()
        else:
            page_copy(g, q, a).start()

    def page_sent(g, q, a, here):
        if not here:
            page_copy(g, q, a).wait_send()

    each_page(1, page_start)

    def hop(b, n):
        part = work[b].g.at[blocks[n]]
        return remote(part, part, hop_send.at[b, n], hop_recv.at[b, n], other)

    step = ROWS
    up_first, down_first = starts[0][2], starts[0][3]
    up_count, down_count = (starts[0][3] - up_first) // step, (starts[0][4] - down_first) // step
    n_feed = up_count + down_count
    chunks = [Chunk(0, k, up_first + k * step, step) for k in range(n_feed)]
    later = [(1, 0, starts[1][MATRICES])]
    later += [(0, f, n) for f, n in pieces_of(starts[0][1], 192)]
    later += [(0, starts[0][1] + f, n) for f, n in pieces_of(starts[0][2] - starts[0][1], 64)]
    chunks += [Chunk(b, n_feed + i, f, n) for i, (b, f, n) in enumerate(later)]

    def feed_chunk(k):
        return Chunk(0, k, pl.multiple_of(up_first + k * step, 16), step)

    def span(ref, c):
        return ref.at[pl.ds(c.first, c.rows)]

    def to_sibling(c, j):
        w = work[c.b]
        return remote(
            span(w.raw.at[2 * j + 1 - core], c), span(w.from_sibling.at[j], c),
            sib_send.at[c.index, j], sib_recv.at[c.index, j], sibling,
        )

    def mine(c):
        return span(work[c.b].raw.at[t], c)

    def theirs(c):
        return span(work[c.b].raw.at[2 * (1 - chip) + core], c)

    def to_partner(c):
        return remote(
            theirs(c), span(work[c.b].from_partner, c), send.at[0, c.index], recv.at[0, c.index], partner
        )

    def from_near(c):
        return span(work[c.b].from_sibling.at[0], c)

    def from_cross(c):
        return span(work[c.b].from_sibling.at[1], c)

    def to_near(c):
        return remote(mine(c), from_near(c), send.at[1, c.index], recv.at[1, c.index], near)

    def to_cross(c):
        return remote(mine(c), from_cross(c), send.at[2, c.index], recv.at[2, c.index], cross)

    def total_to_near(c):
        return remote(
            span(work[c.b].from_partner, c), from_near(c), send.at[3, c.index], recv.at[3, c.index], near
        )

    def out_copy(c, source):
        return pltpu.make_async_copy(span(source, c), span(results[c.b], c), out_sem.at[c.index])

    def added(target, *sources):
        target[...] = sum(s[...].astype(F32) for s in sources).astype(BF)

    def send_to_sibling(c):
        for j in range(tensors // 2):
            to_sibling(c, j).start()

    def stage_sibling(c):
        w = work[c.b]
        for j in range(tensors // 2):
            to_sibling(c, j).wait_recv()
        added(theirs(c), theirs(c), span(w.from_sibling.at[1 - chip], c))
        added(mine(c), mine(c), span(w.from_sibling.at[chip], c))
        if chain:
            @pl.when(jnp.logical_not(outer))
            def _():
                for device in (near, cross):
                    pl.semaphore_signal(credit, inc=1, device_id=device, device_id_type=MESH)

    def stage_partner(c):
        to_partner(c).wait_recv()
        added(mine(c), mine(c), span(work[c.b].from_partner, c))
        if not chain:
            out_copy(c, work[c.b].raw.at[t]).start()
            return

        @pl.when(outer)
        def _():
            pl.semaphore_wait(credit, 1)
            to_near(c).start()

    def stage_near(c):
        @pl.when(jnp.logical_not(outer))
        def _():
            to_near(c).wait_recv()
            added(mine(c), mine(c), from_near(c))
            pl.semaphore_wait(credit, 1)
            to_cross(c).start()

    def stage_cross(c):
        @pl.when(jnp.logical_not(outer))
        def _():
            to_cross(c).wait_recv()
            total = work[c.b].from_partner
            added(span(total, c), mine(c), from_cross(c))
            total_to_near(c).start()
            out_copy(c, total).start()

    def stage_total(c):
        @pl.when(outer)
        def _():
            total_to_near(c).wait_recv()
            out_copy(c, work[c.b].from_sibling.at[0]).start()

    def feed_products():
        own, w = views[0], work[0]
        w.lowT[...] = own.low[...].T

        @pl.loop(0, up_count)
        def _(k):
            rows = pl.ds(pl.multiple_of(k * step, step), step)
            for q in range(tensors):
                w.raw[q, pl.ds(pl.multiple_of(up_first + k * step, 16), step), :] = dot(
                    w.lowT[rows, :], own.slope[q]
                ).astype(BF)
            send_to_sibling(feed_chunk(k))

        @pl.loop(0, down_count)
        def _(k):
            lanes = pl.ds(pl.multiple_of(k * step, step), step)
            for q in range(tensors):
                w.raw[q, pl.ds(pl.multiple_of(down_first + k * step, 16), step), :] = dot(
                    own.act[q, :, lanes].T, w.gf[...]
                ).astype(BF)
            send_to_sibling(feed_chunk(up_count + k))

    def later_product(c):
        own, w = views[c.b], work[c.b]
        for q in range(tensors):
            for i in range(MATRICES):
                first = max(c.first, starts[c.b][i])
                last = min(c.first + c.rows, starts[c.b][i + 1])
                if first >= last:
                    continue
                rows = slice(first - starts[c.b][i], last - starts[c.b][i])
                if i == 0:
                    value = dot(own.qkv[q, rows, :], own.x[...])
                elif i == 1:
                    value = dot(own.ctx[q, rows, :], w.ga[...])
                elif i == 2:
                    value = dot(w.lowT[rows, :], own.slope[q])
                else:
                    value = dot(own.act[q, :, rows].T, w.gf[...])
                w.raw[q, first:last, :] = value.astype(BF)
        send_to_sibling(c)

    @pl.when(section == 1)
    def _():
        wait(*cot_copies)
        work[1].g[...] = flipped[...].T

    for b in range(2):
        work[b].sums[...] = jnp.zeros(work[b].sums.shape, F32)
    for n, block in enumerate(blocks):
        for b in (1, 0):
            own, own_in, w, gain = views[b], loads[b], work[b], gains[b]
            if n == 0:
                wait(own_in.n2, own_in.r2)

            @pl.when(section == 0)
            def _():
                hop(b, n).wait_recv()

            for rows in small_blocks(block):
                g, normed = w.g[rows].astype(F32), own.n2[rows].astype(F32)
                low = norm_rows_back(g, normed, own.r2[rows], gain[1:2])
                w.dz[rows] = low
                w.gf[rows] = low.astype(BF)
                w.sums[1:2] += jnp.sum(g * normed, axis=0, keepdims=True)
                w.sums[3:4] += jnp.sum(g, axis=0, keepdims=True)

            if n == 0:
                wait(own_in.downward, own_in.slope, own_in.upward)

            @pl.loop(0, tensors)
            def _(q):
                d_act = dot(w.gf[block], own.downward[q], NT)
                d_pre = (d_act * own.slope[q, block].astype(F32)).astype(BF)
                own.slope[q, block] = d_pre
                w.dz[block] += dot(d_pre, own.upward[q], NT)

            if n == 0:
                wait(own_in.n1, own_in.r1, own_in.outward)
            for rows in small_blocks(block):
                g, normed = w.dz[rows], own.n1[rows].astype(F32)
                low = norm_rows_back(g, normed, own.r1[rows], gain[0:1])
                w.dz[rows] = low
                w.ga[rows] = low.astype(BF)
                w.sums[0:1] += jnp.sum(g * normed, axis=0, keepdims=True)
                w.sums[2:3] += jnp.sum(g, axis=0, keepdims=True)
            for q in range(tensors):
                w.dctx[q, :, block] = dot(own.outward[q], w.ga[block], NT).astype(BF)

    wait(loads[0].low, loads[0].act)

    @pl.when(section == 0)
    def _():
        feed_products()

    for own_in in loads:
        wait(own_in.qkv, own_in.ctx, own_in.inv)
    wait(probs_copy)
    qkv = (views[0].qkv, views[1].qkv)
    text_rows, layout_rows = slice(0, HEAD_TEXT), slice(HEAD_TEXT, HEAD_TEXT + HEAD_LAYOUT)

    ahead = 3

    def turn(k, n_known):
        fixed = isinstance(k, int)

        def at(i, stage):
            if not fixed:
                pl.when((i >= 0) & (i < n_feed))(lambda: stage(feed_chunk(i)))
            elif 0 <= i < n_known:
                stage(chunks[i])

        def sibling_and_send(c):
            stage_sibling(c)
            to_partner(c).start()

        at(k + ahead, sibling_and_send)
        at(k, stage_partner)
        if chain:
            at(k - 2, stage_near)
            at(k - 4, stage_cross)
            at(k - 6, stage_total)

    def first_copies():
        for c in chunks[:ahead]:
            stage_sibling(c)
            to_partner(c).start()

    early_turns = 6

    @pl.when(section == 0)
    def _():
        first_copies()

    @pl.loop(0, tensors)
    def _(q):
        for local in range(local_heads):
            head = q * local_heads + local

            @pl.when((section == 0) & (head % 2 == 0) & (head < 2 * early_turns))
            def _():
                turn(head // 2, n_feed)

            inv = views[0].inv[q, local : local + 1, :]
            scaled = [
                (work[s].dctx[q, local * SIZES[s] : (local + 1) * SIZES[s], :].astype(F32) * inv).astype(BF)
                for s in range(2)
            ]
            inner = [
                jnp.sum(
                    scaled[s].astype(F32)
                    * views[s].ctx[q, local * SIZES[s] : (local + 1) * SIZES[s], :].astype(F32),
                    axis=0, keepdims=True,
                )
                for s in range(2)
            ]
            rows16 = lax.broadcasted_iota(jnp.int32, (16, length), 0)
            extra = jnp.zeros((16, length), F32)
            for i, value in enumerate((inner[0] + inner[1], inner[1])):
                high = value.astype(BF).astype(F32)
                extra = jnp.where(rows16 == 2 * i, -high, extra)
                extra = jnp.where(rows16 == 2 * i + 1, high - value, extra)
            pad = jnp.zeros((128 - sum(SIZES) - 16, length), BF)
            dcT = jnp.concatenate([*scaled, extra.astype(BF), pad], axis=0)
            dc = dcT.T
            qT, kT = (head_rows(qkv, q, kind, local, SCALES if kind == 0 else None) for kind in range(2))
            v_text, v_layout = (head_part(qkv, q, 2, local, s) for s in range(2))
            one, other_one = (((rows16 // 2) == i).astype(F32).astype(BF) for i in range(2))
            low = probs_in[q, local]
            probs = low.astype(F32)
            both = dot(dc, jnp.concatenate([v_text, v_layout, one, pad], axis=0))
            ds_both = (probs * both).astype(BF)
            single = dot(dc, jnp.concatenate([jnp.zeros_like(v_text), v_layout, other_one, pad], axis=0))
            ds_layout = (probs * single).astype(BF)
            dvT = dot(dcT, low)
            put_head(qkv, q, 2, local, 0, dvT[text_rows])
            put_head(qkv, q, 2, local, 1, dvT[layout_rows])
            put_head(qkv, q, 0, local, 0, dot(kT[text_rows], ds_both, NT) * SCALES[0])
            put_head(qkv, q, 1, local, 0, dot(qT[text_rows], ds_both))
            put_head(qkv, q, 0, local, 1, dot(kT[layout_rows], ds_layout, NT) * SCALES[1])
            put_head(qkv, q, 1, local, 1, dot(qT[layout_rows], ds_layout))

    wait(loads[0].project, loads[1].project)
    page_sum = jnp.zeros((1, work[0].dz.shape[1]), F32)
    for n, block in enumerate(blocks):
        for b in (1, 0):
            down = work[b].dz[block]
            for q in range(tensors):
                down += dot(qkv[b][q, :, block].T, views[b].project[q])
            down = down.astype(BF)
            work[b].g[block] = down
            if b == 0:
                page_sum += jnp.sum(down.astype(F32), axis=0, keepdims=True)

            @pl.when(section == 1)
            def _():
                hop(b, n).start()

    wait(loads[1].low, loads[1].act)
    work[1].lowT[...] = views[1].low[...].T
    for own_in in loads:
        wait(own_in.x)
    @pl.when(section == 1)
    def _():
        feed_products()
        first_copies()

    for c in chunks[n_feed:]:
        later_product(c)

    @pl.when(section == 0)
    def _():
        flipped[...] = work[1].g[...].T
        each_page(0, page_start)

    at_page = (lax.broadcasted_iota(jnp.int32, lang_ids.shape, 0) == t % 2) & (
        lax.broadcasted_iota(jnp.int32, lang_ids.shape, 1) == t // 2
    )
    group = jnp.sum(jnp.where(at_page, lang_ids[...], 0), axis=(0, 1), keepdims=True)
    n_lang = small_out.shape[1] - 8
    chosen = (lax.broadcasted_iota(jnp.int32, (n_lang, 1), 0) == group) & (section == 0)
    small_sum[0, 0:n_lang] = jnp.where(chosen, page_sum, 0.0)
    small_sum[0, n_lang : n_lang + 4] = work[0].sums[...]
    small_sum[0, n_lang + 4 : n_lang + 8] = jnp.zeros((4, small_out.shape[2]), F32)
    small_sum[0, n_lang + 4 : n_lang + 8, : work[1].sums.shape[1]] = work[1].sums[...]

    def small_copy(i, device):
        return remote(small_sum.at[i], small_got.at[i], small_send.at[i], small_recv.at[i], device)

    if chain:
        small_copy(0, sibling).start()
    @pl.when(section == 1)
    def _():
        @pl.loop(0, early_turns)
        def _(k):
            turn(k, n_feed)

    for k in range(early_turns, len(chunks) + (6 if chain else 0)):
        turn(k, len(chunks))
        if not chain:
            continue
        if k == early_turns:
            small_copy(0, sibling).wait_recv()
            small_sum[1] = small_sum[0] + small_got[0]
            small_copy(1, partner).start()
        if k == early_turns + 1:
            small_copy(1, partner).wait_recv()
            small_sum[2] = small_sum[1] + small_got[1]
            small_copy(2, near).start()
        if k == early_turns + 2:
            small_copy(2, near).wait_recv()
            small_sum[3] = small_sum[2] + small_got[2]

            @pl.when(jnp.logical_not(outer))
            def _():
                small_copy(3, cross).start()

        if k == early_turns + 4:
            @pl.when(jnp.logical_not(outer))
            def _():
                small_copy(3, cross).wait_recv()
                small_sum[4] = small_sum[3] + small_got[3]
                small_copy(4, near).start()

        if k == early_turns + 6:
            @pl.when(outer)
            def _():
                small_copy(4, near).wait_recv()
                small_sum[4] = small_got[4]

            small_sum[5] = small_sum[4]
            small_copy(5, other).start()

    if chain:
        for i, device in enumerate((sibling, partner, near)):
            small_copy(i, device).wait_send()

        @pl.when(jnp.logical_not(outer))
        def _():
            small_copy(3, cross).wait_send()
            small_copy(4, near).wait_send()

        small_copy(5, other).wait()
        small_out[0] = small_sum[5]
        small_out[1] = small_got[5]
    else:
        small_out[0] = small_sum[0]
        small_out[1] = small_sum[0]

    @pl.when(section == 1)
    def _():
        for b in range(2):
            for n in range(len(blocks)):
                hop(b, n).wait_send()

    for c in chunks:
        for j in range(tensors // 2):
            to_sibling(c, j).wait_send()
        to_partner(c).wait_send()
        if not chain:
            out_copy(c, work[c.b].from_partner).wait()
            continue

        @pl.when(outer)
        def _():
            to_near(c).wait_send()

        @pl.when(jnp.logical_not(outer))
        def _():
            to_cross(c).wait_send()
            total_to_near(c).wait_send()

        out_copy(c, work[c.b].from_partner).wait()

    for g in range(sections):
        each_page(g, page_sent)
        for a in range(2):
            for j in range(2):
                dst = kinds[g][a].at[j]
                remote(dst, dst, page_send.at[0, a], page_recv.at[g, a, j], partner).wait_recv()
    landed = (text_out, layout_out, grad_out, layout_grad_out)
    copies = [pltpu.make_async_copy(v, h, page_out_sem.at[i]) for i, (v, h) in enumerate(zip(landed, page_outs))]
    start(*copies)
    wait(*copies)


def layer_backward(mesh, x, y, probs, kept, weights, cots, norms, lang_ids, n_lang):
    sections, dp, tensors = mesh.shape["section"], mesh.shape["dp"], mesh.shape["tensor"]
    chain = dp == 4
    needed = tuple(
        Needed(
            n2=k.n2, r2=k.r2, downward=w.downward, slope=k.slope, upward=w.upward, n1=k.n1, r1=k.r1,
            outward=w.outward, low=k.low, act=k.act, qkv=k.qkv, ctx=k.ctx, inv=k.inv, project=w.project, x=rows,
        )
        for k, w, rows in zip(kept, weights, x)
    )
    flat_in, in_tree = jax.tree.flatten((needed, probs))
    plain = [v for own in needed for name, v in own._asdict().items() if name not in Weights._fields] + [probs]
    stacks = [(matrix_starts(own)[MATRICES], rows.shape[1]) for own, rows in zip(needed, x)]
    length = x[0].shape[0]
    work = []
    for own, rows, (count, width) in zip(needed, x, stacks):
        work += Work(
            g=shape(rows.shape), gf=shape(rows.shape), ga=shape(rows.shape), dz=shape(rows.shape, F32),
            dctx=shape(own.ctx.shape), sums=shape((4, width), F32), lowT=shape((width, length)),
            raw=shape((tensors, count, width)), from_sibling=shape((tensors // 2, count, width)),
            from_partner=shape((count, width)),
        )
    small = shape((2, n_lang + 8, x[0].shape[1]), F32)
    text_page = shape((2, length // tensors, x[0].shape[1]))
    layout_page = shape((2, x[1].shape[1], length // tensors))
    summed = [shape(s) for s in stacks]
    own = needed[0]
    n_feed = (own.upward.shape[1] + own.downward.shape[1]) // ROWS
    n_chunks = n_feed + 1 + own.project.shape[1] // 192 + own.outward.shape[1] // 64
    n_blocks = len(hop_blocks(length))
    dma = pltpu.SemaphoreType.DMA
    results = pl.pallas_call(
        functools.partial(backward_kernel, sections, tensors, chain, in_tree),
        out_shape=summed + [small, text_page, layout_page, text_page, layout_page],
        in_specs=[ANY] * (len(flat_in) + 4) + [VMEM] * 3,
        out_specs=[ANY] * 2 + [VMEM] + [ANY] * 4,
        scratch_shapes=vmem_like(work) + vmem_like(plain)
        + [pltpu.VMEM(cots[1].shape, BF)] + [pltpu.VMEM((6,) + small.shape[1:], F32)] * 2
        + vmem_like([text_page, layout_page] * 2)
        + [dma((len(flat_in),)), dma((2,)), dma((2, n_blocks)), dma((2, n_blocks))]
        + [dma((n_chunks, tensors // 2))] * 2 + [dma((4, n_chunks))] * 2
        + [pltpu.SemaphoreType.REGULAR, dma((n_chunks,))]
        + [dma((6,))] * 2 + [dma((tensors, 2)), dma((sections, 2, 2)), dma((4,))],
        compiler_params=pltpu.CompilerParams(
            collective_id=1, has_side_effects=True, vmem_limit_bytes=64 << 20
        ),
        name="layer_backward",
    )(*flat_in, *cots, *y, lang_ids, norms[0][0], norms[1][0])
    totals, small, pages = results[:2], results[2], results[3:7]
    if not chain:
        totals = lax.psum(tuple(totals), "dp")
        both = lax.psum(small[0], ("dp", "tensor"))
        small = jnp.stack([both, lax.ppermute(both, "section", [(0, 1), (1, 0)])])
    return totals, small, pages


def widen_kernel(n_in, n_pages, *refs):
    n_out = 5 + n_pages + 2 * MATRICES
    hbm_in, hbm_out = refs[:n_in], refs[n_in : n_in + n_out]
    vmem_in, vmem_out = refs[n_in + n_out : 2 * n_in + n_out], refs[2 * n_in + n_out : -2]
    in_sem, out_sem = refs[-2:]
    loads = [pltpu.make_async_copy(h, v, in_sem.at[i]) for i, (h, v) in enumerate(zip(hbm_in, vmem_in))]
    sources = vmem_out[:5] + vmem_in[3:] + vmem_out[5:]
    stores = [pltpu.make_async_copy(v, h, out_sem.at[i]) for i, (v, h) in enumerate(zip(sources, hbm_out))]
    start(*loads)
    totals, small = vmem_in[0:2], vmem_in[2]
    for b in range(2):
        wait(loads[b])
        at = 0
        for i in range(b * MATRICES, (b + 1) * MATRICES):
            out = vmem_out[5 + i]
            for c in range(0, out.shape[0], 48):
                out[c : c + 48] = totals[b][at + c : at + c + 48].astype(F32)
            at += out.shape[0]
            stores[5 + n_pages + i].start()
    for i in range(n_pages):
        loads[3 + i].wait()
        stores[5 + i].start()
    loads[2].wait()
    n_lang = vmem_out[0].shape[0]
    vmem_out[0][...] = jnp.where(lax.axis_index("section") == 0, small[0, :n_lang], small[1, :n_lang])
    for i, out in enumerate(vmem_out[1:5]):
        first = n_lang + 2 * i
        out[...] = small[0, first : first + 2, : out.shape[1]]
    start(*stores[:5])
    wait(*stores)


def widen(totals, small, pages, shards, n_lang):
    widths = [total.shape[1] for total in totals]
    sums = [shape((n_lang, widths[0]), F32)] + [shape((2, w), F32) for w in widths for _ in range(2)]
    grads = [shape(m.shape, F32) for own in shards for m in own]
    inputs = (*totals, small, *pages)
    outs = sums + [shape(page.shape) for page in pages] + grads
    results = pl.pallas_call(
        functools.partial(widen_kernel, len(inputs), len(pages)), out_shape=outs,
        in_specs=[ANY] * len(inputs), out_specs=[ANY] * len(outs),
        scratch_shapes=vmem_like(inputs) + vmem_like(sums + grads)
        + [pltpu.SemaphoreType.DMA((len(inputs),)), pltpu.SemaphoreType.DMA((len(outs),))],
        compiler_params=pltpu.CompilerParams(vmem_limit_bytes=62 << 20), name="widen",
    )(*inputs)
    return results[0], results[1:5], results[5:9], results[9:13], results[13:17]


def per_device(
    mesh,
    text_input,
    layout_input,
    text_cotangent,
    layout_cotangent,
    page_counts,
    pad_mask,
    lang_ids,
    lang_table,
    text_project,
    text_outward,
    text_upward,
    text_downward,
    text_gains,
    text_biases,
    layout_project,
    layout_outward,
    layout_upward,
    layout_downward,
    layout_gains,
    layout_biases,
):
    def flat(project):
        return jnp.transpose(project[0], (1, 2, 0)).reshape(-1, project.shape[1])

    def flipped(block):
        return jnp.transpose(block[0], (0, 2, 1))

    shards = (
        Weights(flat(text_project), text_outward[0], text_upward[0], text_downward[0]),
        Weights(flat(layout_project), layout_outward[0], layout_upward[0], layout_downward[0]),
    )
    norms = ((text_gains[0], text_biases[0]), (layout_gains[0], layout_biases[0]))
    marks = (pad_mask, page_counts, lang_ids, lang_table)
    (x, y, probs, kept, weights), cots = layer_forward(
        mesh, text_input[0], flipped(layout_input), text_cotangent[0], flipped(layout_cotangent), shards, norms, marks
    )
    n_lang = lang_table.shape[0]
    totals, small, pages = layer_backward(mesh, x, y, probs, kept, weights, cots, norms, lang_ids, n_lang)
    lang_sum, norm_sums, pages, text_sums, layout_sums = widen(totals, small, pages, shards, n_lang)
    text_out, layout_out, text_grad, layout_grad = pages

    def unflat(grad, like):
        return jnp.transpose(grad.reshape(like.shape[2], like.shape[3], like.shape[1]), (2, 0, 1))[None]

    unflip = lambda block: jnp.transpose(block, (0, 2, 1))[None]
    return (
        text_out[None], unflip(layout_out), text_grad[None], unflip(layout_grad), lang_sum,
        unflat(text_sums[0], text_project), *(s[None] for s in text_sums[1:]), norm_sums[0][None], norm_sums[1][None],
        unflat(layout_sums[0], layout_project), *(s[None] for s in layout_sums[1:]),
        norm_sums[2][None], norm_sums[3][None],
    )


def solution(mesh):
    tokens = P("section", "dp", "tensor", None)
    weight_specs = (
        P("section", None, None, "tensor"), P("section", "tensor", None), P("section", None, "tensor"),
        P("section", "tensor", None), P("section", None, None), P("section", None, None),
    )
    in_specs = (tokens,) * 4 + (P(None, "dp"), P(None, "dp", None), P(None, "dp"), P()) + weight_specs * 2
    out_specs = (tokens,) * 4 + (P(),) + weight_specs * 2
    return jax.shard_map(
        functools.partial(per_device, mesh), mesh=mesh, in_specs=in_specs, out_specs=out_specs, check_vma=False
    )
```

```python
import functools
import math
import typing

import jax
import jax.numpy as jnp
from jax import lax
from jax.experimental import pallas as pl
from jax.experimental.pallas import tpu as pltpu
from jax.sharding import PartitionSpec as P

HEAD_TEXT = 64
HEAD_LAYOUT = 16
EPSILON = 1e-05
NEGATIVE = -1e30
HIGH = lax.Precision.HIGHEST
MESH = pl.DeviceIdType.MESH
BF = jnp.bfloat16
F32 = jnp.float32
ANY = pl.BlockSpec(memory_space=pl.ANY)


def remote(src, dst, send, recv, device):
    return pltpu.make_async_remote_copy(
        src_ref=src, dst_ref=dst, send_sem=send, recv_sem=recv, device_id=device, device_id_type=MESH
    )


def greet(section, tensor, sections, tensors, extra=()):
    barrier = pltpu.get_barrier_semaphore()
    for g in range(sections):
        for q in range(tensors):

            @pl.when((section != g) | (tensor != q))
            def _():
                pl.semaphore_signal(
                    barrier, inc=1, device_id={"section": g, "tensor": q}, device_id_type=MESH
                )

    for device in extra:
        pl.semaphore_signal(barrier, inc=1, device_id=device, device_id_type=MESH)
    pl.semaphore_wait(barrier, sections * tensors - 1 + len(extra))


GELU_P = 0.3275911
GELU_A = (0.254829592, -0.284496736, 1.421413741, -1.453152027, 1.061405429)
NN = (((1,), (0,)), ((), ()))
NT = (((1,), (1,)), ((), ()))
SCALES = (1.0 / math.sqrt(HEAD_TEXT), 1.0 / math.sqrt(HEAD_LAYOUT))
SIZES = (HEAD_TEXT, HEAD_LAYOUT)
ROWS = 128


class Weights(typing.NamedTuple):
    project: typing.Any
    outward: typing.Any
    upward: typing.Any
    downward: typing.Any


class Kept(typing.NamedTuple):
    qkv: typing.Any
    ctx: typing.Any
    inv: typing.Any
    n1: typing.Any
    r1: typing.Any
    low: typing.Any
    act: typing.Any
    slope: typing.Any
    n2: typing.Any
    r2: typing.Any


def dot(a, b, dims=NN):
    return lax.dot_general(a, b, dims, preferred_element_type=F32)


def gelu_pair(u):
    t = 1.0 / (1.0 + (GELU_P / math.sqrt(2.0)) * jnp.abs(u))
    e = jnp.exp(-0.5 * (u * u))
    a1, a2, a3, a4, a5 = (0.5 * a for a in GELU_A)
    tail = ((((a5 * t + a4) * t + a3) * t + a2) * t + a1) * t * e
    cdf = jnp.where(u >= 0, 1.0 - tail, tail)
    return u * cdf, cdf + u * e * (1.0 / math.sqrt(2.0 * math.pi))


def norm_rows(z, gain, offset):
    center = z - jnp.mean(z, axis=-1, keepdims=True)
    inverse = lax.rsqrt(jnp.mean(center * center, axis=-1, keepdims=True) + EPSILON)
    normed = center * inverse
    return normed * gain + offset, normed, inverse


def norm_rows_back(g, n, r, gain):
    t = g * gain
    return r * (t - jnp.mean(t, axis=-1, keepdims=True) - n * jnp.mean(t * n, axis=-1, keepdims=True))


class Staged:
    def __init__(self, tree, hbm, vmem, sem, inward):
        self.tree, self.vmem = tree, list(vmem)
        pairs = zip(hbm, vmem) if inward else zip(vmem, hbm)
        self.copies = [pltpu.make_async_copy(a, b, sem.at[i]) for i, (a, b) in enumerate(pairs)]

    def refs(self):
        return jax.tree.unflatten(self.tree, self.vmem)

    def parts(self):
        return jax.tree.unflatten(self.tree, self.copies)

    def start(self):
        for copy in self.copies:
            copy.start()

    def wait(self):
        for copy in self.copies:
            copy.wait()


def start(*copies):
    for copy in copies:
        copy.start()


def wait(*copies):
    for copy in copies:
        copy.wait()


def head_rows(stacks, slot, kind, local, scales=None, extra=None):
    rows = []
    for b in range(2):
        piece = head_part(stacks, slot, kind, local, b)
        rows.append(piece if scales is None else piece * BF(scales[b]))
    length = rows[0].shape[1]
    rows.append(jnp.zeros((16, length), BF) if extra is None else extra)
    rows.append(jnp.zeros((128 - sum(SIZES) - 16, length), BF))
    return jnp.concatenate(rows, axis=0)


def head_part(stacks, slot, kind, local, b):
    first = kind * (stacks[b].shape[1] // 3) + local * SIZES[b]
    return stacks[b][slot, first : first + SIZES[b], :]


def small_blocks(block, step=64):
    return [slice(c, c + step) for c in range(block.start, block.stop, step)]


def put_head(stacks, slot, kind, local, b, value):
    first = kind * (stacks[b].shape[1] // 3) + local * SIZES[b]
    stacks[b][slot, first : first + SIZES[b], :] = value.astype(BF)


def hop_blocks(length):
    ends = [0, length // 2, length * 3 // 4, length]
    return [slice(a, b) for a, b in zip(ends, ends[1:])]


def slot_of(u, core, chip):
    return ((chip + u // 2) % 2) * 2 + (core + u % 2) % 2


def forward_kernel(sections, tensors, shared, in_tree, out_tree, *refs):
    n_w, n_out = len(shared), out_tree.num_leaves
    sources = (refs[0:2], refs[2:4])
    shards = refs[4 : 4 + n_w]
    pad_mask, counts, lang_ids, lang_table, *norms = refs[4 + n_w : 12 + n_w]
    rest = refs[12 + n_w :]
    hbm_out, cots_out, rest = rest[:n_out], rest[n_out : n_out + 2], rest[n_out + 2 :]
    outgoing = Staged(out_tree, hbm_out, rest[:n_out], rest[n_out], False)
    rest = rest[n_out + 1 :]
    flipped, raw_x, y_narrow, *rest = rest
    nats, totals, pre, score_buffer, rest = rest[0:2], rest[2:4], rest[4:6], rest[6], rest[7:]
    page_send, page_recv, w_send, w_recv, own_sem, hop_send, hop_recv, cot_sem = rest
    x, y_pages, probs_out, kept, weights = outgoing.refs()
    y = (y_pages[0], y_narrow)
    x_out, y_out, probs_copy, kept_out, weights_out = outgoing.parts()
    section, d, t = lax.axis_index("section"), lax.axis_index("dp"), lax.axis_index("tensor")
    core, chip, half_index = t % 2, t // 2, d % 2
    sibling, partner = t + 1 - 2 * core, (t + tensors // 2) % tensors
    mate = d + 1 - 2 * half_index
    micro, page = core, chip
    part_length = sources[0][0].shape[1]
    length = x[0].shape[0]
    blocks = [slice(c, c + 2 * ROWS) for c in range(0, length, 2 * ROWS)]
    parts = hop_blocks(length)
    full = (
        weights[0].project, weights[1].project, weights[0].outward, weights[0].upward,
        weights[0].downward, weights[1].outward, weights[1].upward, weights[1].downward,
    )
    greet(section, t, sections, tensors, ({"dp": mate},) if any(shared) else ())

    def half_of(ref, i, which):
        count = shards[i].shape[0] // 2
        return ref.at[pl.ds(pl.multiple_of(which * count, 16), count)] if shared[i] else ref

    def to_partner(i):
        return remote(
            half_of(shards[i], i, half_index), half_of(full[i].at[t], i, half_index),
            w_send.at[0, i], w_recv.at[0, i], {"tensor": partner},
        )

    def to_sibling(i):
        return remote(full[i].at[t], full[i].at[t], w_send.at[1, i], w_recv.at[1, i], {"tensor": sibling})

    def to_mate(i):
        ref = half_of(full[i].at[partner], i, half_index)
        return remote(ref, ref, w_send.at[2, i], w_recv.at[2, i], {"dp": mate})

    def on_first(i):
        ref = half_of(full[i].at[partner], i, half_index)
        return remote(ref, ref, w_send.at[3, i], w_recv.at[3, i], {"tensor": sibling})

    def on_second(i):
        ref = half_of(full[i].at[partner], i, 1 - half_index)
        return remote(ref, ref, w_send.at[4, i], w_recv.at[4, i], {"tensor": sibling})

    def keep(i):
        return pltpu.make_async_copy(shards[i], full[i].at[t], own_sem.at[i])

    def relay(*which):
        for i in which:
            to_partner(i).wait_recv()
            if shared[i]:
                to_mate(i).start()
            on_first(i).start()

    def relay_second(*which):
        for i in which:
            if shared[i]:
                to_mate(i).wait_recv()
                on_second(i).start()

    def early(*which):
        for i in which:
            to_sibling(i).wait_recv()

    def late(*which):
        for i in which:
            on_first(i).wait_recv()
            if shared[i]:
                on_second(i).wait_recv()

    def token_slot(g, a, index):
        start_at = pl.multiple_of(index * part_length, part_length)
        target = (raw_x, flipped)[a]
        return target.at[pl.ds(start_at, part_length)] if a == 0 else target.at[:, pl.ds(start_at, part_length)]

    def over_pages(g, act):
        for j in range(2):
            target = 2 * j + section
            here = (section == g) & (t == target)
            for a in range(2):
                act(g, j, a, target, here)

    def page_copy(g, j, a, target):
        return remote(
            sources[g][a].at[j], token_slot(g, a, t), page_send.at[g, j, a], page_recv.at[a, t],
            {"section": g, "tensor": target},
        )

    def page_start(g, j, a, target, here):
        @pl.when(here)
        def _():
            pltpu.make_async_copy(sources[g][a].at[j], token_slot(g, a, t), page_recv.at[a, t]).start()

        @pl.when(jnp.logical_not(here))
        def _():
            page_copy(g, j, a, target).start()

    def page_sent(g, j, a, target, here):
        @pl.when(jnp.logical_not(here))
        def _():
            page_copy(g, j, a, target).wait_send()

    def pages_arrived(g):
        for a in range(2):
            for q in range(tensors):
                slot = token_slot(g, a, q)
                remote(slot, slot, page_send.at[0, 0, a], page_recv.at[a, q], {"tensor": sibling}).wait_recv()

    def hop(b, n):
        return remote(
            y[b].at[parts[n]], x[b].at[parts[n]], hop_send.at[b, n], hop_recv.at[b, n], {"section": 1 - section}
        )

    over_pages(0, page_start)
    for i in range(n_w):
        keep(i).start()
    for i in range(n_w):
        to_partner(i).start()
    over_pages(1, page_start)
    for i in range(n_w):
        keep(i).wait()
        to_sibling(i).start()

    at_page = (lax.broadcasted_iota(jnp.int32, counts.shape, 0) == micro) & (
        lax.broadcasted_iota(jnp.int32, counts.shape, 1) == page
    )

    def own_entry(ref):
        return jnp.sum(jnp.where(at_page, ref[...], 0), axis=(0, 1), keepdims=True)

    positions = lax.broadcasted_iota(jnp.int32, (1, length), 1)
    mask_row = pad_mask[micro, pl.ds(page, 1), :]
    key_mask = (positions < own_entry(counts)) & ((mask_row == 1) | (positions == 0))
    first_row = (lax.broadcasted_iota(jnp.int32, (16, length), 0) == 0).astype(F32)
    mask_row16 = (first_row * jnp.where(key_mask, 0.0, NEGATIVE)).astype(BF)
    groups = lax.broadcasted_iota(jnp.int32, (lang_table.shape[0], 1), 0)
    lang_row = jnp.sum(jnp.where(groups == own_entry(lang_ids), lang_table[...], 0.0), axis=0, keepdims=True)
    local_heads = weights[0].project.shape[1] // (3 * HEAD_TEXT)
    qkv = (kept[0].qkv, kept[1].qkv)

    @pl.when(section == 0)
    def _():
        pages_arrived(0)
        x[0][...] = (raw_x[...].astype(F32) + lang_row).astype(BF)
        x[1][...] = flipped[...].T
        early(0, 1)

    @pl.when(section == 1)
    def _():
        relay(*range(n_w))
        relay_second(*range(n_w))
        early(*range(n_w))
        late(*range(n_w))
        start(*weights_out[0], *weights_out[1])

    @pl.loop(0, 2)
    def _(half):
        @pl.when((half == 1) & (section == 0))
        def _():
            relay(0, 1)
            relay_second(0)
            late(0, 1)

        for n, block in enumerate(parts):
            @pl.when((half == 0) & (section == 1))
            def _():
                for b in range(2):
                    hop(b, n).wait_recv()

            @pl.loop(0, 2)
            def _(u):
                slot = slot_of(2 * half + u, core, chip)
                for b in range(2):
                    qkv[b][slot, :, block] = dot(weights[b].project[slot], x[b][block], NT).astype(BF)

        @pl.loop(0, 2)
        def _(u):
            slot = slot_of(2 * half + u, core, chip)
            for local in range(local_heads):
                q = head_rows(qkv, slot, 0, local, SCALES, first_row.astype(BF)).T
                kT = head_rows(qkv, slot, 1, local, None, mask_row16)
                score_buffer[local] = dot(q, kT)
                for rows in small_blocks(slice(0, length)):
                    scores = score_buffer[local, rows, :]
                    raised = jnp.exp(scores - jnp.max(scores, axis=-1, keepdims=True))
                    probs_out[slot, local, rows, :] = raised.astype(BF)
                vT = head_rows(qkv, slot, 2, local, None, first_row.astype(BF))
                ctx = dot(vT, probs_out[slot, local], NT)
                inv = 1.0 / ctx[sum(SIZES) : sum(SIZES) + 1]
                ctx = (ctx * inv).astype(BF)
                kept[0].inv[slot, local : local + 1, :] = inv
                kept[0].ctx[slot, local * HEAD_TEXT : (local + 1) * HEAD_TEXT, :] = ctx[:HEAD_TEXT]
                kept[1].ctx[slot, local * HEAD_LAYOUT : (local + 1) * HEAD_LAYOUT, :] = ctx[
                    HEAD_TEXT : HEAD_TEXT + HEAD_LAYOUT
                ]

    kept[1].inv[...] = jnp.zeros(kept[1].inv.shape, F32)
    start(probs_copy, *x_out, *(c for k in kept_out for c in (k.qkv, k.ctx, k.inv)))

    def attend(b):
        gains, biases = norms[2 * b : 2 * b + 2]
        width = x[b].shape[1]
        nats[b][...] = kept[b].ctx[...].reshape(width, length).T
        wide = weights[b].outward[...].reshape(width, width)
        for block in blocks:
            totals[b][1, block] = dot(nats[b][block], wide)
            for rows in small_blocks(block):
                h, n, r = norm_rows(x[b][rows].astype(F32) + totals[b][1, rows], gains[0:1], biases[0:1])
                totals[b][0, rows] = h
                totals[b][1, rows] = jnp.zeros(h.shape, F32)
                kept[b].n1[rows] = n.astype(BF)
                kept[b].r1[rows] = r
                kept[b].low[rows] = h.astype(BF)
        start(kept_out[b].n1, kept_out[b].r1, kept_out[b].low)

    def feed(b, first, which):
        @pl.loop(first, first + 2)
        def _(u):
            slot = slot_of(u, core, chip)
            for block in which:
                pre[b][block] = dot(kept[b].low[block], weights[b].upward[slot])
                for rows in small_blocks(block, 16):
                    act, slope = gelu_pair(pre[b][rows])
                    kept[b].act[slot, rows] = act.astype(BF)
                    kept[b].slope[slot, rows] = slope.astype(BF)
                totals[b][1, block] += dot(kept[b].act[slot, block], weights[b].downward[slot])

    def finish(b):
        gains, biases = norms[2 * b : 2 * b + 2]
        def last(block):
            feed(b, 2, [block])
            for rows in small_blocks(block):
                out, normed, r = norm_rows(totals[b][0, rows] + totals[b][1, rows], gains[1:2], biases[1:2])
                y[b][rows] = out.astype(BF)
                kept[b].n2[rows] = normed.astype(BF)
                kept[b].r2[rows] = r

        @pl.when(section == 0)
        def _():
            for n, block in enumerate(parts):
                last(block)
                hop(b, n).start()

        @pl.when(section == 1)
        def _():
            last(slice(0, length))

        if b == 1:
            y_pages[1][...] = y_narrow[...].T
        start(y_out[b], kept_out[b].act, kept_out[b].slope, kept_out[b].n2, kept_out[b].r2)

    @pl.when(section == 0)
    def _():
        relay(2, 3)
        early(2)
        late(2)

    attend(0)

    @pl.when(section == 0)
    def _():
        early(3, 4)

    feed(0, 0, [slice(0, length)])

    @pl.when(section == 0)
    def _():
        relay(4, 5, 6, 7)
        relay_second(3)
        early(5, 6, 7)
        late(5, 6, 7)

    attend(1)
    feed(1, 0, [slice(0, length)])
    finish(1)

    @pl.when(section == 0)
    def _():
        relay_second(4)
        late(3, 4)

    finish(0)

    @pl.when(section == 0)
    def _():
        start(*weights_out[0], *weights_out[1])
        for b in range(2):
            for n in range(len(parts)):
                hop(b, n).wait_send()

    for i in range(n_w):
        to_partner(i).wait_send()
        to_sibling(i).wait_send()
        on_first(i).wait_send()
        if shared[i]:
            to_mate(i).wait_send()
            on_second(i).wait_send()
    for g in range(sections):
        over_pages(g, page_sent)

    @pl.when(section == 1)
    def _():
        pages_arrived(1)
        copies = [pltpu.make_async_copy(v, h, cot_sem.at[i]) for i, (v, h) in enumerate(zip((raw_x, flipped), cots_out))]
        start(*copies)
        wait(*copies)

    outgoing.wait()


def vmem_like(tree):
    return [pltpu.VMEM(s.shape, s.dtype) for s in jax.tree.leaves(tree)]


VMEM = pl.BlockSpec(memory_space=pltpu.VMEM)


def shape(dims, dtype=BF):
    return jax.ShapeDtypeStruct(tuple(dims), dtype)


def layer_forward(mesh, text_in, layout_in, text_cot, layout_cot, shards, norms, marks):
    sections, dp, tensors = mesh.shape["section"], mesh.shape["dp"], mesh.shape["tensor"]
    length = text_in.shape[1] * tensors
    rows = (shape((length, text_in.shape[2])), shape((length, layout_in.shape[1])))
    local_heads = shards[0].project.shape[0] // (3 * HEAD_TEXT)
    kept = []
    for x, w in zip(rows, shards):
        units, column = shape((tensors, length, w.upward.shape[1])), shape((length, 1), F32)
        kept.append(Kept(
            qkv=shape((tensors, w.project.shape[0], length)), ctx=shape((tensors, w.outward.shape[0], length)),
            inv=shape((tensors, local_heads, length), F32),
            n1=shape(x.shape), r1=column, low=shape(x.shape), act=units, slope=units,
            n2=shape(x.shape), r2=column,
        ))
    weights = tuple(Weights(*(shape((tensors,) + m.shape) for m in w)) for w in shards)
    pages_out = (rows[0], shape((rows[1].shape[1], length)))
    outs = (rows, pages_out, shape((tensors, local_heads, length, length)), tuple(kept), weights)
    flat_out, out_tree = jax.tree.flatten(outs)
    (a, b) = shards
    ordered = (a.project, b.project, a.outward, a.upward, a.downward, b.outward, b.upward, b.downward)
    shared = tuple(dp % 2 == 0 and w.shape[0] >= 512 for w in ordered)
    n_w = len(ordered)
    cots = [rows[0], shape((rows[1].shape[1], length))]
    small = (*marks, *norms[0], *norms[1])
    results = pl.pallas_call(
        functools.partial(forward_kernel, sections, tensors, shared, None, out_tree),
        out_shape=flat_out + cots,
        in_specs=[ANY] * (4 + n_w) + [VMEM] * len(small),
        out_specs=[ANY] * (len(flat_out) + 2),
        scratch_shapes=vmem_like(flat_out) + [pltpu.SemaphoreType.DMA((len(flat_out),))]
        + [pltpu.VMEM(cots[1].shape, BF), pltpu.VMEM(cots[0].shape, BF), pltpu.VMEM(rows[1].shape, BF)]
        + [pltpu.VMEM(x.shape, BF) for x in rows]
        + [pltpu.VMEM((2,) + x.shape, F32) for x in rows]
        + [pltpu.VMEM((length, w.upward.shape[1]), F32) for w in shards]
        + [pltpu.VMEM((local_heads, length, length), F32)]
        + [
            pltpu.SemaphoreType.DMA((sections, 2, 2)), pltpu.SemaphoreType.DMA((2, tensors)),
            pltpu.SemaphoreType.DMA((5, n_w)), pltpu.SemaphoreType.DMA((5, n_w)), pltpu.SemaphoreType.DMA((n_w,)),
            pltpu.SemaphoreType.DMA((2, len(hop_blocks(length)))), pltpu.SemaphoreType.DMA((2, len(hop_blocks(length)))),
            pltpu.SemaphoreType.DMA((2,)),
        ],
        compiler_params=pltpu.CompilerParams(
            collective_id=0, has_side_effects=True, vmem_limit_bytes=62 << 20
        ),
        name="layer_forward",
    )(text_in, layout_in, text_cot, layout_cot, *ordered, *small)
    return jax.tree.unflatten(out_tree, results[:-2]), tuple(results[-2:])


class Needed(typing.NamedTuple):
    n2: typing.Any
    r2: typing.Any
    downward: typing.Any
    slope: typing.Any
    upward: typing.Any
    n1: typing.Any
    r1: typing.Any
    outward: typing.Any
    low: typing.Any
    act: typing.Any
    qkv: typing.Any
    ctx: typing.Any
    inv: typing.Any
    project: typing.Any
    x: typing.Any


class Work(typing.NamedTuple):
    g: typing.Any
    gf: typing.Any
    ga: typing.Any
    dz: typing.Any
    dctx: typing.Any
    sums: typing.Any
    lowT: typing.Any
    raw: typing.Any
    from_sibling: typing.Any
    from_partner: typing.Any


class Chunk(typing.NamedTuple):
    b: typing.Any
    index: typing.Any
    first: typing.Any
    rows: typing.Any


MATRICES = 4


def matrix_rows(own):
    return own.project.shape[1], own.outward.shape[1], own.upward.shape[1], own.downward.shape[1]


def matrix_starts(own):
    sizes = matrix_rows(own)
    return [sum(sizes[:i]) for i in range(MATRICES + 1)]


def pieces_of(size, step):
    return [(f, step) for f in range(0, size, step)]


def backward_kernel(sections, tensors, chain, in_tree, *refs):
    n_in = in_tree.num_leaves
    hbm_in, refs = refs[:n_in], refs[n_in:]
    (cots, ys, lang_ids, gains), refs = (refs[0:2], refs[2:4], refs[4], refs[5:7]), refs[7:]
    results, small_out, page_outs, refs = refs[0:2], refs[2], refs[3:7], refs[7:]
    n_work = len(Work._fields)
    work, refs = (Work(*refs[:n_work]), Work(*refs[n_work : 2 * n_work])), refs[2 * n_work :]
    plain, refs = refs[: n_in - 2 * MATRICES], refs[n_in - 2 * MATRICES :]
    flipped, small_got, small_sum, refs = refs[0], refs[1], refs[2], refs[3:]
    text_out, layout_out, grad_out, layout_grad_out, *refs = refs
    in_sem, cot_sem, hop_send, hop_recv, sib_send, sib_recv, send, recv, credit, out_sem, *refs = refs
    small_send, small_recv, page_send, page_recv, page_out_sem = refs
    section, d, t = lax.axis_index("section"), lax.axis_index("dp"), lax.axis_index("tensor")
    core, chip = t % 2, t // 2
    sibling = {"tensor": t + 1 - 2 * core}
    partner = {"tensor": (t + tensors // 2) % tensors}
    near, cross = {"dp": d + 1 - 2 * (d % 2)}, {"dp": 3 - d}
    outer = (d == 0) | (d == 3)
    other = {"section": 1 - section}
    hbm, probs_hbm = jax.tree.unflatten(in_tree, hbm_in)
    starts = [matrix_starts(own) for own in hbm]

    plain = list(plain)
    views = []
    for b in range(2):
        fields = {}
        for name, value in hbm[b]._asdict().items():
            if name in Weights._fields:
                i = Weights._fields.index(name)
                fields[name] = work[b].raw.at[:, pl.ds(starts[b][i], starts[b][i + 1] - starts[b][i])]
            else:
                fields[name] = plain.pop(0)
        views.append(Needed(**fields))
    probs_in = plain.pop(0)
    flat_views = jax.tree.leaves((tuple(views), probs_in))
    flat_copies = [pltpu.make_async_copy(a, v, in_sem.at[i]) for i, (a, v) in enumerate(zip(hbm_in, flat_views))]
    loads, probs_copy = jax.tree.unflatten(in_tree, flat_copies)
    length = work[0].gf.shape[0]
    local_heads = probs_in.shape[1]
    blocks = hop_blocks(length)
    cot_copies = (
        pltpu.make_async_copy(cots[0], work[0].g, cot_sem.at[0]),
        pltpu.make_async_copy(cots[1], flipped, cot_sem.at[1]),
    )

    @pl.when(section == 1)
    def _():
        start(*cot_copies)

    for field in zip(loads[1], loads[0]):
        start(*field)
    probs_copy.start()
    greet(section, t, sections, tensors, (near, cross) if chain else ())

    part_length = text_out.shape[1]
    micro, page = core, chip
    kinds = ((grad_out, layout_grad_out), (text_out, layout_out))
    pages = ((work[0].g, flipped), ys)

    def page_part(g, q, a):
        span = pl.ds(q * part_length, part_length)
        return pages[g][a].at[span] if a == 0 else pages[g][a].at[:, span]

    def each_page(g, act):
        for q in range(tensors):
            for a in range(2):
                here = (micro == g) & (t == q)

                @pl.when((section == g) & here)
                def _():
                    act(g, q, a, True)

                @pl.when((section == g) & jnp.logical_not(here))
                def _():
                    act(g, q, a, False)

    def page_copy(g, q, a):
        return remote(
            page_part(g, q, a), kinds[g][a].at[page], page_send.at[q, a], page_recv.at[g, a, page],
            {"section": micro, "tensor": q},
        )

    def page_start(g, q, a, here):
        if here:
            pltpu.make_async_copy(page_part(g, q, a), kinds[g][a].at[page], page_recv.at[g, a, page]).start()
        else:
            page_copy(g, q, a).start()

    def page_sent(g, q, a, here):
        if not here:
            page_copy(g, q, a).wait_send()

    each_page(1, page_start)

    def hop(b, n):
        part = work[b].g.at[blocks[n]]
        return remote(part, part, hop_send.at[b, n], hop_recv.at[b, n], other)

    step = ROWS
    up_first, down_first = starts[0][2], starts[0][3]
    up_count, down_count = (starts[0][3] - up_first) // step, (starts[0][4] - down_first) // step
    n_feed = up_count + down_count
    chunks = [Chunk(0, k, up_first + k * step, step) for k in range(n_feed)]
    later = [(1, 0, starts[1][MATRICES])]
    later += [(0, f, n) for f, n in pieces_of(starts[0][1], 192)]
    later += [(0, starts[0][1] + f, n) for f, n in pieces_of(starts[0][2] - starts[0][1], 64)]
    chunks += [Chunk(b, n_feed + i, f, n) for i, (b, f, n) in enumerate(later)]

    def feed_chunk(k):
        return Chunk(0, k, pl.multiple_of(up_first + k * step, 16), step)

    def span(ref, c):
        return ref.at[pl.ds(c.first, c.rows)]

    def to_sibling(c, j):
        w = work[c.b]
        return remote(
            span(w.raw.at[2 * j + 1 - core], c), span(w.from_sibling.at[j], c),
            sib_send.at[c.index, j], sib_recv.at[c.index, j], sibling,
        )

    def mine(c):
        return span(work[c.b].raw.at[t], c)

    def theirs(c):
        return span(work[c.b].raw.at[2 * (1 - chip) + core], c)

    def to_partner(c):
        return remote(
            theirs(c), span(work[c.b].from_partner, c), send.at[0, c.index], recv.at[0, c.index], partner
        )

    def from_near(c):
        return span(work[c.b].from_sibling.at[0], c)

    def from_cross(c):
        return span(work[c.b].from_sibling.at[1], c)

    def to_near(c):
        return remote(mine(c), from_near(c), send.at[1, c.index], recv.at[1, c.index], near)

    def to_cross(c):
        return remote(mine(c), from_cross(c), send.at[2, c.index], recv.at[2, c.index], cross)

    def total_to_near(c):
        return remote(
            span(work[c.b].from_partner, c), from_near(c), send.at[3, c.index], recv.at[3, c.index], near
        )

    def out_copy(c, source):
        return pltpu.make_async_copy(span(source, c), span(results[c.b], c), out_sem.at[c.index])

    def added(target, *sources):
        target[...] = sum(s[...].astype(F32) for s in sources).astype(BF)

    def send_to_sibling(c):
        for j in range(tensors // 2):
            to_sibling(c, j).start()

    def stage_sibling(c):
        w = work[c.b]
        for j in range(tensors // 2):
            to_sibling(c, j).wait_recv()
        added(theirs(c), theirs(c), span(w.from_sibling.at[1 - chip], c))
        added(mine(c), mine(c), span(w.from_sibling.at[chip], c))
        if chain:
            @pl.when(jnp.logical_not(outer))
            def _():
                for device in (near, cross):
                    pl.semaphore_signal(credit, inc=1, device_id=device, device_id_type=MESH)

    def stage_partner(c):
        to_partner(c).wait_recv()
        added(mine(c), mine(c), span(work[c.b].from_partner, c))
        if not chain:
            out_copy(c, work[c.b].raw.at[t]).start()
            return

        @pl.when(outer)
        def _():
            pl.semaphore_wait(credit, 1)
            to_near(c).start()

    def stage_near(c):
        @pl.when(jnp.logical_not(outer))
        def _():
            to_near(c).wait_recv()
            added(mine(c), mine(c), from_near(c))
            pl.semaphore_wait(credit, 1)
            to_cross(c).start()

    def stage_cross(c):
        @pl.when(jnp.logical_not(outer))
        def _():
            to_cross(c).wait_recv()
            total = work[c.b].from_partner
            added(span(total, c), mine(c), from_cross(c))
            total_to_near(c).start()
            out_copy(c, total).start()

    def stage_total(c):
        @pl.when(outer)
        def _():
            total_to_near(c).wait_recv()
            out_copy(c, work[c.b].from_sibling.at[0]).start()

    def feed_products():
        own, w = views[0], work[0]
        w.lowT[...] = own.low[...].T

        @pl.loop(0, up_count)
        def _(k):
            rows = pl.ds(pl.multiple_of(k * step, step), step)
            for q in range(tensors):
                w.raw[q, pl.ds(pl.multiple_of(up_first + k * step, 16), step), :] = dot(
                    w.lowT[rows, :], own.slope[q]
                ).astype(BF)
            send_to_sibling(feed_chunk(k))

        @pl.loop(0, down_count)
        def _(k):
            lanes = pl.ds(pl.multiple_of(k * step, step), step)
            for q in range(tensors):
                w.raw[q, pl.ds(pl.multiple_of(down_first + k * step, 16), step), :] = dot(
                    own.act[q, :, lanes].T, w.gf[...]
                ).astype(BF)
            send_to_sibling(feed_chunk(up_count + k))

    def later_product(c):
        own, w = views[c.b], work[c.b]
        for q in range(tensors):
            for i in range(MATRICES):
                first = max(c.first, starts[c.b][i])
                last = min(c.first + c.rows, starts[c.b][i + 1])
                if first >= last:
                    continue
                rows = slice(first - starts[c.b][i], last - starts[c.b][i])
                if i == 0:
                    value = dot(own.qkv[q, rows, :], own.x[...])
                elif i == 1:
                    value = dot(own.ctx[q, rows, :], w.ga[...])
                elif i == 2:
                    value = dot(w.lowT[rows, :], own.slope[q])
                else:
                    value = dot(own.act[q, :, rows].T, w.gf[...])
                w.raw[q, first:last, :] = value.astype(BF)
        send_to_sibling(c)

    @pl.when(section == 1)
    def _():
        wait(*cot_copies)
        work[1].g[...] = flipped[...].T

    for b in range(2):
        work[b].sums[...] = jnp.zeros(work[b].sums.shape, F32)
    def feed_back(n, block):
        for b in (1, 0):
            own, own_in, w, gain = views[b], loads[b], work[b], gains[b]
            if n == 0:
                wait(own_in.n2, own_in.r2)

            if block in blocks:
                hop(b, n).wait_recv()

            for rows in small_blocks(block):
                g, normed = w.g[rows].astype(F32), own.n2[rows].astype(F32)
                low = norm_rows_back(g, normed, own.r2[rows], gain[1:2])
                w.dz[rows] = low
                w.gf[rows] = low.astype(BF)
                w.sums[1:2] += jnp.sum(g * normed, axis=0, keepdims=True)
                w.sums[3:4] += jnp.sum(g, axis=0, keepdims=True)

            if n == 0:
                wait(own_in.downward, own_in.slope, own_in.upward)

            @pl.loop(0, tensors)
            def _(q):
                d_act = dot(w.gf[block], own.downward[q], NT)
                d_pre = (d_act * own.slope[q, block].astype(F32)).astype(BF)
                own.slope[q, block] = d_pre
                w.dz[block] += dot(d_pre, own.upward[q], NT)

            if n == 0:
                wait(own_in.n1, own_in.r1, own_in.outward)
            for rows in small_blocks(block):
                g, normed = w.dz[rows], own.n1[rows].astype(F32)
                low = norm_rows_back(g, normed, own.r1[rows], gain[0:1])
                w.dz[rows] = low
                w.ga[rows] = low.astype(BF)
                w.sums[0:1] += jnp.sum(g * normed, axis=0, keepdims=True)
                w.sums[2:3] += jnp.sum(g, axis=0, keepdims=True)
            for q in range(tensors):
                w.dctx[q, :, block] = dot(own.outward[q], w.ga[block], NT).astype(BF)

    @pl.when(section == 0)
    def _():
        for n, block in enumerate(blocks):
            feed_back(n, block)

    @pl.when(section == 1)
    def _():
        feed_back(0, slice(0, length))

    wait(loads[0].low, loads[0].act)

    @pl.when(section == 0)
    def _():
        feed_products()

    for own_in in loads:
        wait(own_in.qkv, own_in.ctx, own_in.inv)
    wait(probs_copy)
    qkv = (views[0].qkv, views[1].qkv)
    text_rows, layout_rows = slice(0, HEAD_TEXT), slice(HEAD_TEXT, HEAD_TEXT + HEAD_LAYOUT)

    ahead = 3

    def turn(k, n_known):
        fixed = isinstance(k, int)

        def at(i, stage):
            if not fixed:
                pl.when((i >= 0) & (i < n_feed))(lambda: stage(feed_chunk(i)))
            elif 0 <= i < n_known:
                stage(chunks[i])

        def sibling_and_send(c):
            stage_sibling(c)
            to_partner(c).start()

        at(k + ahead, sibling_and_send)
        at(k, stage_partner)
        if chain:
            at(k - 2, stage_near)
            at(k - 4, stage_cross)
            at(k - 6, stage_total)

    def first_copies():
        for c in chunks[:ahead]:
            stage_sibling(c)
            to_partner(c).start()

    early_turns = 6

    @pl.when(section == 0)
    def _():
        first_copies()

    @pl.loop(0, tensors)
    def _(q):
        for local in range(local_heads):
            head = q * local_heads + local

            @pl.when((section == 0) & (head % 2 == 0) & (head < 2 * early_turns))
            def _():
                turn(head // 2, n_feed)

            inv = views[0].inv[q, local : local + 1, :]
            scaled = [
                (work[s].dctx[q, local * SIZES[s] : (local + 1) * SIZES[s], :].astype(F32) * inv).astype(BF)
                for s in range(2)
            ]
            inner = [
                jnp.sum(
                    scaled[s].astype(F32)
                    * views[s].ctx[q, local * SIZES[s] : (local + 1) * SIZES[s], :].astype(F32),
                    axis=0, keepdims=True,
                )
                for s in range(2)
            ]
            rows16 = lax.broadcasted_iota(jnp.int32, (16, length), 0)
            extra = jnp.zeros((16, length), F32)
            for i, value in enumerate((inner[0] + inner[1], inner[1])):
                high = value.astype(BF).astype(F32)
                extra = jnp.where(rows16 == 2 * i, -high, extra)
                extra = jnp.where(rows16 == 2 * i + 1, high - value, extra)
            pad = jnp.zeros((128 - sum(SIZES) - 16, length), BF)
            dcT = jnp.concatenate([*scaled, extra.astype(BF), pad], axis=0)
            dc = dcT.T
            qT, kT = (head_rows(qkv, q, kind, local, SCALES if kind == 0 else None) for kind in range(2))
            v_text, v_layout = (head_part(qkv, q, 2, local, s) for s in range(2))
            one, other_one = (((rows16 // 2) == i).astype(F32).astype(BF) for i in range(2))
            low = probs_in[q, local]
            probs = low.astype(F32)
            both = dot(dc, jnp.concatenate([v_text, v_layout, one, pad], axis=0))
            ds_both = (probs * both).astype(BF)
            single = dot(dc, jnp.concatenate([jnp.zeros_like(v_text), v_layout, other_one, pad], axis=0))
            ds_layout = (probs * single).astype(BF)
            dvT = dot(dcT, low)
            put_head(qkv, q, 2, local, 0, dvT[text_rows])
            put_head(qkv, q, 2, local, 1, dvT[layout_rows])
            put_head(qkv, q, 0, local, 0, dot(kT[text_rows], ds_both, NT) * SCALES[0])
            put_head(qkv, q, 1, local, 0, dot(qT[text_rows], ds_both))
            put_head(qkv, q, 0, local, 1, dot(kT[layout_rows], ds_layout, NT) * SCALES[1])
            put_head(qkv, q, 1, local, 1, dot(qT[layout_rows], ds_layout))

    wait(loads[0].project, loads[1].project)
    page_sum = jnp.zeros((1, work[0].dz.shape[1]), F32)
    for n, block in enumerate(blocks):
        for b in (1, 0):
            down = work[b].dz[block]
            for q in range(tensors):
                down += dot(qkv[b][q, :, block].T, views[b].project[q])
            down = down.astype(BF)
            work[b].g[block] = down
            if b == 0:
                page_sum += jnp.sum(down.astype(F32), axis=0, keepdims=True)

            @pl.when(section == 1)
            def _():
                hop(b, n).start()

    wait(loads[1].low, loads[1].act)
    work[1].lowT[...] = views[1].low[...].T
    for own_in in loads:
        wait(own_in.x)
    @pl.when(section == 1)
    def _():
        feed_products()
        first_copies()

    for c in chunks[n_feed:]:
        later_product(c)

    @pl.when(section == 0)
    def _():
        flipped[...] = work[1].g[...].T
        each_page(0, page_start)

    at_page = (lax.broadcasted_iota(jnp.int32, lang_ids.shape, 0) == t % 2) & (
        lax.broadcasted_iota(jnp.int32, lang_ids.shape, 1) == t // 2
    )
    group = jnp.sum(jnp.where(at_page, lang_ids[...], 0), axis=(0, 1), keepdims=True)
    n_lang = small_out.shape[1] - 8
    chosen = (lax.broadcasted_iota(jnp.int32, (n_lang, 1), 0) == group) & (section == 0)
    small_sum[0, 0:n_lang] = jnp.where(chosen, page_sum, 0.0)
    small_sum[0, n_lang : n_lang + 4] = work[0].sums[...]
    small_sum[0, n_lang + 4 : n_lang + 8] = jnp.zeros((4, small_out.shape[2]), F32)
    small_sum[0, n_lang + 4 : n_lang + 8, : work[1].sums.shape[1]] = work[1].sums[...]

    def small_copy(i, device):
        return remote(small_sum.at[i], small_got.at[i], small_send.at[i], small_recv.at[i], device)

    if chain:
        small_copy(0, sibling).start()
    @pl.when(section == 1)
    def _():
        @pl.loop(0, early_turns)
        def _(k):
            turn(k, n_feed)

    for k in range(early_turns, len(chunks) + (6 if chain else 0)):
        turn(k, len(chunks))
        if not chain:
            continue
        if k == early_turns:
            small_copy(0, sibling).wait_recv()
            small_sum[1] = small_sum[0] + small_got[0]
            small_copy(1, partner).start()
        if k == early_turns + 1:
            small_copy(1, partner).wait_recv()
            small_sum[2] = small_sum[1] + small_got[1]
            small_copy(2, near).start()
        if k == early_turns + 2:
            small_copy(2, near).wait_recv()
            small_sum[3] = small_sum[2] + small_got[2]

            @pl.when(jnp.logical_not(outer))
            def _():
                small_copy(3, cross).start()

        if k == early_turns + 4:
            @pl.when(jnp.logical_not(outer))
            def _():
                small_copy(3, cross).wait_recv()
                small_sum[4] = small_sum[3] + small_got[3]
                small_copy(4, near).start()

        if k == early_turns + 6:
            @pl.when(outer)
            def _():
                small_copy(4, near).wait_recv()
                small_sum[4] = small_got[4]

            small_sum[5] = small_sum[4]
            small_copy(5, other).start()

    if chain:
        for i, device in enumerate((sibling, partner, near)):
            small_copy(i, device).wait_send()

        @pl.when(jnp.logical_not(outer))
        def _():
            small_copy(3, cross).wait_send()
            small_copy(4, near).wait_send()

        small_copy(5, other).wait()
        small_out[0] = small_sum[5]
        small_out[1] = small_got[5]
    else:
        small_out[0] = small_sum[0]
        small_out[1] = small_sum[0]

    @pl.when(section == 1)
    def _():
        for b in range(2):
            for n in range(len(blocks)):
                hop(b, n).wait_send()

    for c in chunks:
        for j in range(tensors // 2):
            to_sibling(c, j).wait_send()
        to_partner(c).wait_send()
        if not chain:
            out_copy(c, work[c.b].from_partner).wait()
            continue

        @pl.when(outer)
        def _():
            to_near(c).wait_send()

        @pl.when(jnp.logical_not(outer))
        def _():
            to_cross(c).wait_send()
            total_to_near(c).wait_send()

        out_copy(c, work[c.b].from_partner).wait()

    for g in range(sections):
        each_page(g, page_sent)
        for a in range(2):
            for j in range(2):
                dst = kinds[g][a].at[j]
                remote(dst, dst, page_send.at[0, a], page_recv.at[g, a, j], partner).wait_recv()
    landed = (text_out, layout_out, grad_out, layout_grad_out)
    copies = [pltpu.make_async_copy(v, h, page_out_sem.at[i]) for i, (v, h) in enumerate(zip(landed, page_outs))]
    start(*copies)
    wait(*copies)


def layer_backward(mesh, x, y, probs, kept, weights, cots, norms, lang_ids, n_lang):
    sections, dp, tensors = mesh.shape["section"], mesh.shape["dp"], mesh.shape["tensor"]
    chain = dp == 4
    needed = tuple(
        Needed(
            n2=k.n2, r2=k.r2, downward=w.downward, slope=k.slope, upward=w.upward, n1=k.n1, r1=k.r1,
            outward=w.outward, low=k.low, act=k.act, qkv=k.qkv, ctx=k.ctx, inv=k.inv, project=w.project, x=rows,
        )
        for k, w, rows in zip(kept, weights, x)
    )
    flat_in, in_tree = jax.tree.flatten((needed, probs))
    plain = [v for own in needed for name, v in own._asdict().items() if name not in Weights._fields] + [probs]
    stacks = [(matrix_starts(own)[MATRICES], rows.shape[1]) for own, rows in zip(needed, x)]
    length = x[0].shape[0]
    work = []
    for own, rows, (count, width) in zip(needed, x, stacks):
        work += Work(
            g=shape(rows.shape), gf=shape(rows.shape), ga=shape(rows.shape), dz=shape(rows.shape, F32),
            dctx=shape(own.ctx.shape), sums=shape((4, width), F32), lowT=shape((width, length)),
            raw=shape((tensors, count, width)), from_sibling=shape((tensors // 2, count, width)),
            from_partner=shape((count, width)),
        )
    small = shape((2, n_lang + 8, x[0].shape[1]), F32)
    text_page = shape((2, length // tensors, x[0].shape[1]))
    layout_page = shape((2, x[1].shape[1], length // tensors))
    summed = [shape(s) for s in stacks]
    own = needed[0]
    n_feed = (own.upward.shape[1] + own.downward.shape[1]) // ROWS
    n_chunks = n_feed + 1 + own.project.shape[1] // 192 + own.outward.shape[1] // 64
    n_blocks = len(hop_blocks(length))
    dma = pltpu.SemaphoreType.DMA
    results = pl.pallas_call(
        functools.partial(backward_kernel, sections, tensors, chain, in_tree),
        out_shape=summed + [small, text_page, layout_page, text_page, layout_page],
        in_specs=[ANY] * (len(flat_in) + 4) + [VMEM] * 3,
        out_specs=[ANY] * 2 + [VMEM] + [ANY] * 4,
        scratch_shapes=vmem_like(work) + vmem_like(plain)
        + [pltpu.VMEM(cots[1].shape, BF)] + [pltpu.VMEM((6,) + small.shape[1:], F32)] * 2
        + vmem_like([text_page, layout_page] * 2)
        + [dma((len(flat_in),)), dma((2,)), dma((2, n_blocks)), dma((2, n_blocks))]
        + [dma((n_chunks, tensors // 2))] * 2 + [dma((4, n_chunks))] * 2
        + [pltpu.SemaphoreType.REGULAR, dma((n_chunks,))]
        + [dma((6,))] * 2 + [dma((tensors, 2)), dma((sections, 2, 2)), dma((4,))],
        compiler_params=pltpu.CompilerParams(
            collective_id=1, has_side_effects=True, vmem_limit_bytes=64 << 20
        ),
        name="layer_backward",
    )(*flat_in, *cots, *y, lang_ids, norms[0][0], norms[1][0])
    totals, small, pages = results[:2], results[2], results[3:7]
    if not chain:
        totals = lax.psum(tuple(totals), "dp")
        both = lax.psum(small[0], ("dp", "tensor"))
        small = jnp.stack([both, lax.ppermute(both, "section", [(0, 1), (1, 0)])])
    return totals, small, pages


def widen_kernel(n_in, n_pages, *refs):
    n_out = 5 + n_pages + 2 * MATRICES
    hbm_in, hbm_out = refs[:n_in], refs[n_in : n_in + n_out]
    vmem_in, vmem_out = refs[n_in + n_out : 2 * n_in + n_out], refs[2 * n_in + n_out : -2]
    in_sem, out_sem = refs[-2:]
    loads = [pltpu.make_async_copy(h, v, in_sem.at[i]) for i, (h, v) in enumerate(zip(hbm_in, vmem_in))]
    sources = vmem_out[:5] + vmem_in[3:] + vmem_out[5:]
    stores = [pltpu.make_async_copy(v, h, out_sem.at[i]) for i, (v, h) in enumerate(zip(sources, hbm_out))]
    start(*loads)
    totals, small = vmem_in[0:2], vmem_in[2]
    for b in range(2):
        wait(loads[b])
        at = 0
        for i in range(b * MATRICES, (b + 1) * MATRICES):
            out = vmem_out[5 + i]
            for c in range(0, out.shape[0], 48):
                out[c : c + 48] = totals[b][at + c : at + c + 48].astype(F32)
            at += out.shape[0]
            stores[5 + n_pages + i].start()
    for i in range(n_pages):
        loads[3 + i].wait()
        stores[5 + i].start()
    loads[2].wait()
    n_lang = vmem_out[0].shape[0]
    vmem_out[0][...] = jnp.where(lax.axis_index("section") == 0, small[0, :n_lang], small[1, :n_lang])
    for i, out in enumerate(vmem_out[1:5]):
        first = n_lang + 2 * i
        out[...] = small[0, first : first + 2, : out.shape[1]]
    start(*stores[:5])
    wait(*stores)


def widen(totals, small, pages, shards, n_lang):
    widths = [total.shape[1] for total in totals]
    sums = [shape((n_lang, widths[0]), F32)] + [shape((2, w), F32) for w in widths for _ in range(2)]
    grads = [shape(m.shape, F32) for own in shards for m in own]
    inputs = (*totals, small, *pages)
    outs = sums + [shape(page.shape) for page in pages] + grads
    results = pl.pallas_call(
        functools.partial(widen_kernel, len(inputs), len(pages)), out_shape=outs,
        in_specs=[ANY] * len(inputs), out_specs=[ANY] * len(outs),
        scratch_shapes=vmem_like(inputs) + vmem_like(sums + grads)
        + [pltpu.SemaphoreType.DMA((len(inputs),)), pltpu.SemaphoreType.DMA((len(outs),))],
        compiler_params=pltpu.CompilerParams(vmem_limit_bytes=62 << 20), name="widen",
    )(*inputs)
    return results[0], results[1:5], results[5:9], results[9:13], results[13:17]


def per_device(
    mesh,
    text_input,
    layout_input,
    text_cotangent,
    layout_cotangent,
    page_counts,
    pad_mask,
    lang_ids,
    lang_table,
    text_project,
    text_outward,
    text_upward,
    text_downward,
    text_gains,
    text_biases,
    layout_project,
    layout_outward,
    layout_upward,
    layout_downward,
    layout_gains,
    layout_biases,
):
    def flat(project):
        return jnp.transpose(project[0], (1, 2, 0)).reshape(-1, project.shape[1])

    def flipped(block):
        return jnp.transpose(block[0], (0, 2, 1))

    shards = (
        Weights(flat(text_project), text_outward[0], text_upward[0], text_downward[0]),
        Weights(flat(layout_project), layout_outward[0], layout_upward[0], layout_downward[0]),
    )
    norms = ((text_gains[0], text_biases[0]), (layout_gains[0], layout_biases[0]))
    marks = (pad_mask, page_counts, lang_ids, lang_table)
    (x, y, probs, kept, weights), cots = layer_forward(
        mesh, text_input[0], flipped(layout_input), text_cotangent[0], flipped(layout_cotangent), shards, norms, marks
    )
    n_lang = lang_table.shape[0]
    totals, small, pages = layer_backward(mesh, x, y, probs, kept, weights, cots, norms, lang_ids, n_lang)
    lang_sum, norm_sums, pages, text_sums, layout_sums = widen(totals, small, pages, shards, n_lang)
    text_out, layout_out, text_grad, layout_grad = pages

    def unflat(grad, like):
        return jnp.transpose(grad.reshape(like.shape[2], like.shape[3], like.shape[1]), (2, 0, 1))[None]

    unflip = lambda block: jnp.transpose(block, (0, 2, 1))[None]
    return (
        text_out[None], unflip(layout_out), text_grad[None], unflip(layout_grad), lang_sum,
        unflat(text_sums[0], text_project), *(s[None] for s in text_sums[1:]), norm_sums[0][None], norm_sums[1][None],
        unflat(layout_sums[0], layout_project), *(s[None] for s in layout_sums[1:]),
        norm_sums[2][None], norm_sums[3][None],
    )


def solution(mesh):
    tokens = P("section", "dp", "tensor", None)
    weight_specs = (
        P("section", None, None, "tensor"), P("section", "tensor", None), P("section", None, "tensor"),
        P("section", "tensor", None), P("section", None, None), P("section", None, None),
    )
    in_specs = (tokens,) * 4 + (P(None, "dp"), P(None, "dp", None), P(None, "dp"), P()) + weight_specs * 2
    out_specs = (tokens,) * 4 + (P(),) + weight_specs * 2
    return jax.shard_map(
        functools.partial(per_device, mesh), mesh=mesh, in_specs=in_specs, out_specs=out_specs, check_vma=False
    )
```

```python
import functools
import math
import typing

import jax
import jax.numpy as jnp
from jax import lax
from jax.experimental import pallas as pl
from jax.experimental.pallas import tpu as pltpu
from jax.sharding import PartitionSpec as P

HEAD_TEXT = 64
HEAD_LAYOUT = 16
EPSILON = 1e-05
NEGATIVE = -1e30
HIGH = lax.Precision.HIGHEST
MESH = pl.DeviceIdType.MESH
BF = jnp.bfloat16
F32 = jnp.float32
ANY = pl.BlockSpec(memory_space=pl.ANY)


def remote(src, dst, send, recv, device):
    return pltpu.make_async_remote_copy(
        src_ref=src, dst_ref=dst, send_sem=send, recv_sem=recv, device_id=device, device_id_type=MESH
    )


def greet(section, tensor, sections, tensors, extra=()):
    barrier = pltpu.get_barrier_semaphore()
    for g in range(sections):
        for q in range(tensors):

            @pl.when((section != g) | (tensor != q))
            def _():
                pl.semaphore_signal(
                    barrier, inc=1, device_id={"section": g, "tensor": q}, device_id_type=MESH
                )

    for device in extra:
        pl.semaphore_signal(barrier, inc=1, device_id=device, device_id_type=MESH)
    pl.semaphore_wait(barrier, sections * tensors - 1 + len(extra))


GELU_P = 0.3275911
GELU_A = (0.254829592, -0.284496736, 1.421413741, -1.453152027, 1.061405429)
NN = (((1,), (0,)), ((), ()))
NT = (((1,), (1,)), ((), ()))
SCALES = (1.0 / math.sqrt(HEAD_TEXT), 1.0 / math.sqrt(HEAD_LAYOUT))
SIZES = (HEAD_TEXT, HEAD_LAYOUT)
ROWS = 128


class Weights(typing.NamedTuple):
    project: typing.Any
    outward: typing.Any
    upward: typing.Any
    downward: typing.Any


class Kept(typing.NamedTuple):
    qkv: typing.Any
    ctx: typing.Any
    inv: typing.Any
    n1: typing.Any
    r1: typing.Any
    low: typing.Any
    act: typing.Any
    slope: typing.Any
    n2: typing.Any
    r2: typing.Any


def dot(a, b, dims=NN):
    return lax.dot_general(a, b, dims, preferred_element_type=F32)


def gelu_pair(u):
    t = 1.0 / (1.0 + (GELU_P / math.sqrt(2.0)) * jnp.abs(u))
    e = jnp.exp(-0.5 * (u * u))
    a1, a2, a3, a4, a5 = (0.5 * a for a in GELU_A)
    tail = ((((a5 * t + a4) * t + a3) * t + a2) * t + a1) * t * e
    cdf = jnp.where(u >= 0, 1.0 - tail, tail)
    return u * cdf, cdf + u * e * (1.0 / math.sqrt(2.0 * math.pi))


def norm_rows(z, gain, offset):
    center = z - jnp.mean(z, axis=-1, keepdims=True)
    inverse = lax.rsqrt(jnp.mean(center * center, axis=-1, keepdims=True) + EPSILON)
    normed = center * inverse
    return normed * gain + offset, normed, inverse


def norm_rows_back(g, n, r, gain):
    t = g * gain
    return r * (t - jnp.mean(t, axis=-1, keepdims=True) - n * jnp.mean(t * n, axis=-1, keepdims=True))


class Staged:
    def __init__(self, tree, hbm, vmem, sem, inward):
        self.tree, self.vmem = tree, list(vmem)
        pairs = zip(hbm, vmem) if inward else zip(vmem, hbm)
        self.copies = [pltpu.make_async_copy(a, b, sem.at[i]) for i, (a, b) in enumerate(pairs)]

    def refs(self):
        return jax.tree.unflatten(self.tree, self.vmem)

    def parts(self):
        return jax.tree.unflatten(self.tree, self.copies)

    def start(self):
        for copy in self.copies:
            copy.start()

    def wait(self):
        for copy in self.copies:
            copy.wait()


def start(*copies):
    for copy in copies:
        copy.start()


def wait(*copies):
    for copy in copies:
        copy.wait()


def head_rows(stacks, slot, kind, local, scales=None, extra=None):
    rows = []
    for b in range(2):
        piece = head_part(stacks, slot, kind, local, b)
        rows.append(piece if scales is None else piece * BF(scales[b]))
    length = rows[0].shape[1]
    rows.append(jnp.zeros((16, length), BF) if extra is None else extra)
    rows.append(jnp.zeros((128 - sum(SIZES) - 16, length), BF))
    return jnp.concatenate(rows, axis=0)


def head_part(stacks, slot, kind, local, b):
    first = kind * (stacks[b].shape[1] // 3) + local * SIZES[b]
    return stacks[b][slot, first : first + SIZES[b], :]


def small_blocks(block, step=64):
    return [slice(c, c + step) for c in range(block.start, block.stop, step)]


def put_head(stacks, slot, kind, local, b, value):
    first = kind * (stacks[b].shape[1] // 3) + local * SIZES[b]
    stacks[b][slot, first : first + SIZES[b], :] = value.astype(BF)


def hop_blocks(length):
    ends = [0, length // 2, length * 3 // 4, length]
    return [slice(a, b) for a, b in zip(ends, ends[1:])]


def slot_of(u, core, chip):
    return ((chip + u // 2) % 2) * 2 + (core + u % 2) % 2


def forward_kernel(sections, tensors, shared, in_tree, out_tree, *refs):
    n_w, n_out = len(shared), out_tree.num_leaves
    sources = (refs[0:2], refs[2:4])
    shards = refs[4 : 4 + n_w]
    pad_mask, counts, lang_ids, lang_table, *norms = refs[4 + n_w : 12 + n_w]
    rest = refs[12 + n_w :]
    hbm_out, cots_out, rest = rest[:n_out], rest[n_out : n_out + 2], rest[n_out + 2 :]
    outgoing = Staged(out_tree, hbm_out, rest[:n_out], rest[n_out], False)
    rest = rest[n_out + 1 :]
    flipped, raw_x, y_narrow, *rest = rest
    nats, totals, pre, score_buffer, rest = rest[0:2], rest[2:4], rest[4:6], rest[6], rest[7:]
    xT, turned, turn_sem, rest = rest[0:2], (rest[2:4], rest[4:6]), rest[6], rest[7:]
    page_send, page_recv, w_send, w_recv, own_sem, hop_send, hop_recv, cot_sem = rest
    x, y_pages, probs_out, kept, weights = outgoing.refs()
    y = (y_pages[0], y_narrow)
    x_out, y_out, probs_copy, kept_out, weights_out = outgoing.parts()
    weights_hbm = jax.tree.unflatten(out_tree, list(hbm_out))[4]
    section, d, t = lax.axis_index("section"), lax.axis_index("dp"), lax.axis_index("tensor")
    core, chip, half_index = t % 2, t // 2, d % 2
    sibling, partner = t + 1 - 2 * core, (t + tensors // 2) % tensors
    mate = d + 1 - 2 * half_index
    micro, page = core, chip
    part_length = sources[0][0].shape[1]
    length = x[0].shape[0]
    blocks = [slice(c, c + 2 * ROWS) for c in range(0, length, 2 * ROWS)]
    parts = hop_blocks(length)
    full = (
        weights[0].project, weights[1].project, weights[0].outward, weights[0].upward,
        weights[0].downward, weights[1].outward, weights[1].upward, weights[1].downward,
    )
    greet(section, t, sections, tensors, ({"dp": mate},) if any(shared) else ())

    def half_of(ref, i, which):
        count = shards[i].shape[0] // 2
        return ref.at[pl.ds(pl.multiple_of(which * count, 16), count)] if shared[i] else ref

    def to_partner(i):
        return remote(
            half_of(shards[i], i, half_index), half_of(full[i].at[t], i, half_index),
            w_send.at[0, i], w_recv.at[0, i], {"tensor": partner},
        )

    def to_sibling(i):
        return remote(full[i].at[t], full[i].at[t], w_send.at[1, i], w_recv.at[1, i], {"tensor": sibling})

    def to_mate(i):
        ref = half_of(full[i].at[partner], i, half_index)
        return remote(ref, ref, w_send.at[2, i], w_recv.at[2, i], {"dp": mate})

    def on_first(i):
        ref = half_of(full[i].at[partner], i, half_index)
        return remote(ref, ref, w_send.at[3, i], w_recv.at[3, i], {"tensor": sibling})

    def on_second(i):
        ref = half_of(full[i].at[partner], i, 1 - half_index)
        return remote(ref, ref, w_send.at[4, i], w_recv.at[4, i], {"tensor": sibling})

    def keep(i):
        return pltpu.make_async_copy(shards[i], full[i].at[t], own_sem.at[i])

    def relay(*which):
        for i in which:
            to_partner(i).wait_recv()
            if shared[i]:
                to_mate(i).start()
            on_first(i).start()

    def relay_second(*which):
        for i in which:
            if shared[i]:
                to_mate(i).wait_recv()
                on_second(i).start()

    def early(*which):
        for i in which:
            to_sibling(i).wait_recv()

    def late(*which):
        for i in which:
            on_first(i).wait_recv()
            if shared[i]:
                on_second(i).wait_recv()

    def token_slot(g, a, index):
        start_at = pl.multiple_of(index * part_length, part_length)
        target = (raw_x, flipped)[a]
        return target.at[pl.ds(start_at, part_length)] if a == 0 else target.at[:, pl.ds(start_at, part_length)]

    def over_pages(g, act):
        for j in range(2):
            target = 2 * j + section
            here = (section == g) & (t == target)
            for a in range(2):
                act(g, j, a, target, here)

    def page_copy(g, j, a, target):
        return remote(
            sources[g][a].at[j], token_slot(g, a, t), page_send.at[g, j, a], page_recv.at[a, t],
            {"section": g, "tensor": target},
        )

    def page_start(g, j, a, target, here):
        @pl.when(here)
        def _():
            pltpu.make_async_copy(sources[g][a].at[j], token_slot(g, a, t), page_recv.at[a, t]).start()

        @pl.when(jnp.logical_not(here))
        def _():
            page_copy(g, j, a, target).start()

    def page_sent(g, j, a, target, here):
        @pl.when(jnp.logical_not(here))
        def _():
            page_copy(g, j, a, target).wait_send()

    def pages_arrived(g):
        for a in range(2):
            for q in range(tensors):
                slot = token_slot(g, a, q)
                remote(slot, slot, page_send.at[0, 0, a], page_recv.at[a, q], {"tensor": sibling}).wait_recv()

    def hop(b, n):
        return remote(
            y[b].at[parts[n]], x[b].at[parts[n]], hop_send.at[b, n], hop_recv.at[b, n], {"section": 1 - section}
        )

    def weights_to_hbm():
        for b in range(2):
            start(weights_out[b].project, weights_out[b].outward)
            for q in range(tensors):
                for m, name in enumerate((2, 3)):
                    copy = pltpu.make_async_copy(
                        turned[b][m].at[q % 2], weights_hbm[b][name].at[q], turn_sem.at[b, m, q % 2]
                    )
                    if q >= 2:
                        copy.wait()
                    turned[b][m][q % 2] = weights[b][name][q].T
                    copy.start()
        for b in range(2):
            for q in range(tensors - 2, tensors):
                for m, name in enumerate((2, 3)):
                    pltpu.make_async_copy(
                        turned[b][m].at[q % 2], weights_hbm[b][name].at[q], turn_sem.at[b, m, q % 2]
                    ).wait()

    over_pages(0, page_start)
    for i in range(n_w):
        keep(i).start()
    for i in range(n_w):
        to_partner(i).start()
    over_pages(1, page_start)
    for i in range(n_w):
        keep(i).wait()
        to_sibling(i).start()

    at_page = (lax.broadcasted_iota(jnp.int32, counts.shape, 0) == micro) & (
        lax.broadcasted_iota(jnp.int32, counts.shape, 1) == page
    )

    def own_entry(ref):
        return jnp.sum(jnp.where(at_page, ref[...], 0), axis=(0, 1), keepdims=True)

    positions = lax.broadcasted_iota(jnp.int32, (1, length), 1)
    mask_row = pad_mask[micro, pl.ds(page, 1), :]
    key_mask = (positions < own_entry(counts)) & ((mask_row == 1) | (positions == 0))
    first_row = (lax.broadcasted_iota(jnp.int32, (16, length), 0) == 0).astype(F32)
    mask_row16 = (first_row * jnp.where(key_mask, 0.0, NEGATIVE)).astype(BF)
    groups = lax.broadcasted_iota(jnp.int32, (lang_table.shape[0], 1), 0)
    lang_row = jnp.sum(jnp.where(groups == own_entry(lang_ids), lang_table[...], 0.0), axis=0, keepdims=True)
    local_heads = weights[0].project.shape[1] // (3 * HEAD_TEXT)
    qkv = (kept[0].qkv, kept[1].qkv)

    @pl.when(section == 0)
    def _():
        pages_arrived(0)
        x[0][...] = (raw_x[...].astype(F32) + lang_row).astype(BF)
        x[1][...] = flipped[...].T
        early(0, 1)

    @pl.when(section == 1)
    def _():
        relay(*range(n_w))
        relay_second(*range(n_w))
        early(*range(n_w))
        late(*range(n_w))
        weights_to_hbm()

    @pl.loop(0, 2)
    def _(half):
        @pl.when((half == 1) & (section == 0))
        def _():
            relay(0, 1)
            relay_second(0)
            late(0, 1)

        for n, block in enumerate(parts):
            @pl.when((half == 0) & (section == 1))
            def _():
                for b in range(2):
                    hop(b, n).wait_recv()

            @pl.when(half == 0)
            def _():
                for b in range(2):
                    xT[b][:, block] = x[b][block].T

            @pl.loop(0, 2)
            def _(u):
                slot = slot_of(2 * half + u, core, chip)
                for b in range(2):
                    qkv[b][slot, :, block] = dot(weights[b].project[slot], xT[b][:, block]).astype(BF)

        @pl.loop(0, 2)
        def _(u):
            slot = slot_of(2 * half + u, core, chip)
            for local in range(local_heads):
                q = head_rows(qkv, slot, 0, local, SCALES, first_row.astype(BF)).T
                kT = head_rows(qkv, slot, 1, local, None, mask_row16)
                score_buffer[local] = dot(q, kT)
                for rows in small_blocks(slice(0, length)):
                    scores = score_buffer[local, rows, :]
                    raised = jnp.exp(scores - jnp.max(scores, axis=-1, keepdims=True))
                    probs_out[slot, local, rows, :] = raised.astype(BF)
                vT = head_rows(qkv, slot, 2, local, None, first_row.astype(BF))
                ctx = dot(probs_out[slot, local], vT.T).T
                inv = 1.0 / ctx[sum(SIZES) : sum(SIZES) + 1]
                ctx = (ctx * inv).astype(BF)
                kept[0].inv[slot, local : local + 1, :] = inv
                kept[0].ctx[slot, local * HEAD_TEXT : (local + 1) * HEAD_TEXT, :] = ctx[:HEAD_TEXT]
                kept[1].ctx[slot, local * HEAD_LAYOUT : (local + 1) * HEAD_LAYOUT, :] = ctx[
                    HEAD_TEXT : HEAD_TEXT + HEAD_LAYOUT
                ]

    kept[1].inv[...] = jnp.zeros(kept[1].inv.shape, F32)
    start(probs_copy, *x_out, *(c for k in kept_out for c in (k.qkv, k.ctx, k.inv)))

    def attend(b):
        gains, biases = norms[2 * b : 2 * b + 2]
        width = x[b].shape[1]
        nats[b][...] = kept[b].ctx[...].reshape(width, length).T
        wide = weights[b].outward[...].reshape(width, width)
        for block in blocks:
            totals[b][1, block] = dot(nats[b][block], wide)
            for rows in small_blocks(block):
                h, n, r = norm_rows(x[b][rows].astype(F32) + totals[b][1, rows], gains[0:1], biases[0:1])
                totals[b][0, rows] = h
                totals[b][1, rows] = jnp.zeros(h.shape, F32)
                kept[b].n1[rows] = n.astype(BF)
                kept[b].r1[rows] = r
                kept[b].low[rows] = h.astype(BF)
        start(kept_out[b].n1, kept_out[b].r1, kept_out[b].low)

    def feed(b, first, which):
        @pl.loop(first, first + 2)
        def _(u):
            slot = slot_of(u, core, chip)
            for block in which:
                pre[b][block] = dot(kept[b].low[block], weights[b].upward[slot])
                for rows in small_blocks(block, 16):
                    act, slope = gelu_pair(pre[b][rows])
                    kept[b].act[slot, rows] = act.astype(BF)
                    kept[b].slope[slot, rows] = slope.astype(BF)
                totals[b][1, block] += dot(kept[b].act[slot, block], weights[b].downward[slot])

    def finish(b):
        gains, biases = norms[2 * b : 2 * b + 2]
        def last(block):
            feed(b, 2, [block])
            for rows in small_blocks(block):
                out, normed, r = norm_rows(totals[b][0, rows] + totals[b][1, rows], gains[1:2], biases[1:2])
                y[b][rows] = out.astype(BF)
                kept[b].n2[rows] = normed.astype(BF)
                kept[b].r2[rows] = r

        @pl.when(section == 0)
        def _():
            for n, block in enumerate(parts):
                last(block)
                hop(b, n).start()

        @pl.when(section == 1)
        def _():
            last(slice(0, length))

        if b == 1:
            y_pages[1][...] = y_narrow[...].T
        start(y_out[b], kept_out[b].act, kept_out[b].slope, kept_out[b].n2, kept_out[b].r2)

    @pl.when(section == 0)
    def _():
        relay(2, 3)
        early(2)
        late(2)

    attend(0)

    @pl.when(section == 0)
    def _():
        early(3, 4)

    feed(0, 0, [slice(0, length)])

    @pl.when(section == 0)
    def _():
        relay(4, 5, 6, 7)
        relay_second(3)
        early(5, 6, 7)
        late(5, 6, 7)

    attend(1)
    feed(1, 0, [slice(0, length)])
    finish(1)

    @pl.when(section == 0)
    def _():
        relay_second(4)
        late(3, 4)

    finish(0)

    @pl.when(section == 0)
    def _():
        weights_to_hbm()
        for b in range(2):
            for n in range(len(parts)):
                hop(b, n).wait_send()

    for i in range(n_w):
        to_partner(i).wait_send()
        to_sibling(i).wait_send()
        on_first(i).wait_send()
        if shared[i]:
            to_mate(i).wait_send()
            on_second(i).wait_send()
    for g in range(sections):
        over_pages(g, page_sent)

    @pl.when(section == 1)
    def _():
        pages_arrived(1)
        copies = [pltpu.make_async_copy(v, h, cot_sem.at[i]) for i, (v, h) in enumerate(zip((raw_x, flipped), cots_out))]
        start(*copies)
        wait(*copies)

    for group in (x_out, y_out, (probs_copy,), *kept_out, *(w[:2] for w in weights_out)):
        wait(*group)


def vmem_like(tree):
    return [pltpu.VMEM(s.shape, s.dtype) for s in jax.tree.leaves(tree)]


VMEM = pl.BlockSpec(memory_space=pltpu.VMEM)


def shape(dims, dtype=BF):
    return jax.ShapeDtypeStruct(tuple(dims), dtype)


def layer_forward(mesh, text_in, layout_in, text_cot, layout_cot, shards, norms, marks):
    sections, dp, tensors = mesh.shape["section"], mesh.shape["dp"], mesh.shape["tensor"]
    length = text_in.shape[1] * tensors
    rows = (shape((length, text_in.shape[2])), shape((length, layout_in.shape[1])))
    local_heads = shards[0].project.shape[0] // (3 * HEAD_TEXT)
    kept = []
    for x, w in zip(rows, shards):
        units, column = shape((tensors, length, w.upward.shape[1])), shape((length, 1), F32)
        kept.append(Kept(
            qkv=shape((tensors, w.project.shape[0], length)), ctx=shape((tensors, w.outward.shape[0], length)),
            inv=shape((tensors, local_heads, length), F32),
            n1=shape(x.shape), r1=column, low=shape(x.shape), act=units, slope=units,
            n2=shape(x.shape), r2=column,
        ))
    weights = tuple(Weights(*(shape((tensors,) + m.shape) for m in w)) for w in shards)
    pages_out = (rows[0], shape((rows[1].shape[1], length)))
    outs = (rows, pages_out, shape((tensors, local_heads, length, length)), tuple(kept), weights)
    flat_out, out_tree = jax.tree.flatten(outs)
    (a, b) = shards
    ordered = (a.project, b.project, a.outward, a.upward, a.downward, b.outward, b.upward, b.downward)
    shared = tuple(dp % 2 == 0 and w.shape[0] >= 512 for w in ordered)
    n_w = len(ordered)
    cots = [rows[0], shape((rows[1].shape[1], length))]
    small = (*marks, *norms[0], *norms[1])
    results = pl.pallas_call(
        functools.partial(forward_kernel, sections, tensors, shared, None, out_tree),
        out_shape=flat_out + cots,
        in_specs=[ANY] * (4 + n_w) + [VMEM] * len(small),
        out_specs=[ANY] * (len(flat_out) + 2),
        scratch_shapes=vmem_like(flat_out) + [pltpu.SemaphoreType.DMA((len(flat_out),))]
        + [pltpu.VMEM(cots[1].shape, BF), pltpu.VMEM(cots[0].shape, BF), pltpu.VMEM(rows[1].shape, BF)]
        + [pltpu.VMEM(x.shape, BF) for x in rows]
        + [pltpu.VMEM((2,) + x.shape, F32) for x in rows]
        + [pltpu.VMEM((length, w.upward.shape[1]), F32) for w in shards]
        + [pltpu.VMEM((local_heads, length, length), F32)]
        + [pltpu.VMEM((x.shape[1], length), BF) for x in rows]
        + [pltpu.VMEM((2,) + m.shape, BF) for w in shards for m in (w.upward, w.downward)]
        + [pltpu.SemaphoreType.DMA((2, 2, 2))]
        + [
            pltpu.SemaphoreType.DMA((sections, 2, 2)), pltpu.SemaphoreType.DMA((2, tensors)),
            pltpu.SemaphoreType.DMA((5, n_w)), pltpu.SemaphoreType.DMA((5, n_w)), pltpu.SemaphoreType.DMA((n_w,)),
            pltpu.SemaphoreType.DMA((2, len(hop_blocks(length)))), pltpu.SemaphoreType.DMA((2, len(hop_blocks(length)))),
            pltpu.SemaphoreType.DMA((2,)),
        ],
        compiler_params=pltpu.CompilerParams(
            collective_id=0, has_side_effects=True, vmem_limit_bytes=62 << 20
        ),
        name="layer_forward",
    )(text_in, layout_in, text_cot, layout_cot, *ordered, *small)
    return jax.tree.unflatten(out_tree, results[:-2]), tuple(results[-2:])


class Needed(typing.NamedTuple):
    n2: typing.Any
    r2: typing.Any
    downward: typing.Any
    slope: typing.Any
    upward: typing.Any
    n1: typing.Any
    r1: typing.Any
    outward: typing.Any
    low: typing.Any
    act: typing.Any
    qkv: typing.Any
    ctx: typing.Any
    inv: typing.Any
    project: typing.Any
    x: typing.Any


class Work(typing.NamedTuple):
    g: typing.Any
    gf: typing.Any
    ga: typing.Any
    dz: typing.Any
    dctx: typing.Any
    sums: typing.Any
    lowT: typing.Any
    raw: typing.Any
    from_sibling: typing.Any
    from_partner: typing.Any


class Chunk(typing.NamedTuple):
    b: typing.Any
    index: typing.Any
    first: typing.Any
    rows: typing.Any


MATRICES = 4


def matrix_rows(own):
    return own.project.shape[1], own.outward.shape[1], own.upward.shape[1], own.downward.shape[1]


def matrix_starts(own):
    sizes = matrix_rows(own)
    return [sum(sizes[:i]) for i in range(MATRICES + 1)]


def pieces_of(size, step):
    return [(f, step) for f in range(0, size, step)]


def backward_kernel(sections, tensors, chain, in_tree, *refs):
    n_in = in_tree.num_leaves
    hbm_in, refs = refs[:n_in], refs[n_in:]
    (cots, ys, lang_ids, gains), refs = (refs[0:2], refs[2:4], refs[4], refs[5:7]), refs[7:]
    results, small_out, page_outs, refs = refs[0:2], refs[2], refs[3:7], refs[7:]
    n_work = len(Work._fields)
    work, refs = (Work(*refs[:n_work]), Work(*refs[n_work : 2 * n_work])), refs[2 * n_work :]
    plain, refs = refs[: n_in - 2 * MATRICES], refs[n_in - 2 * MATRICES :]
    flipped, small_got, small_sum, refs = refs[0], refs[1], refs[2], refs[3:]
    text_out, layout_out, grad_out, layout_grad_out, *refs = refs
    in_sem, cot_sem, hop_send, hop_recv, sib_send, sib_recv, send, recv, credit, out_sem, *refs = refs
    small_send, small_recv, page_send, page_recv, page_out_sem = refs
    section, d, t = lax.axis_index("section"), lax.axis_index("dp"), lax.axis_index("tensor")
    core, chip = t % 2, t // 2
    sibling = {"tensor": t + 1 - 2 * core}
    partner = {"tensor": (t + tensors // 2) % tensors}
    near, cross = {"dp": d + 1 - 2 * (d % 2)}, {"dp": 3 - d}
    outer = (d == 0) | (d == 3)
    other = {"section": 1 - section}
    hbm, probs_hbm = jax.tree.unflatten(in_tree, hbm_in)
    starts = [matrix_starts(own) for own in hbm]

    plain = list(plain)
    views = []
    for b in range(2):
        fields = {}
        for name, value in hbm[b]._asdict().items():
            if name in Weights._fields:
                i = Weights._fields.index(name)
                fields[name] = work[b].raw.at[:, pl.ds(starts[b][i], starts[b][i + 1] - starts[b][i])]
            else:
                fields[name] = plain.pop(0)
        views.append(Needed(**fields))
    probs_in = plain.pop(0)
    flat_views = jax.tree.leaves((tuple(views), probs_in))
    flat_copies = [pltpu.make_async_copy(a, v, in_sem.at[i]) for i, (a, v) in enumerate(zip(hbm_in, flat_views))]
    loads, probs_copy = jax.tree.unflatten(in_tree, flat_copies)
    length = work[0].gf.shape[0]
    local_heads = probs_in.shape[1]
    blocks = hop_blocks(length)
    cot_copies = (
        pltpu.make_async_copy(cots[0], work[0].g, cot_sem.at[0]),
        pltpu.make_async_copy(cots[1], flipped, cot_sem.at[1]),
    )

    @pl.when(section == 1)
    def _():
        start(*cot_copies)

    for field in zip(loads[1], loads[0]):
        start(*field)
    probs_copy.start()
    greet(section, t, sections, tensors, (near, cross) if chain else ())

    part_length = text_out.shape[1]
    micro, page = core, chip
    kinds = ((grad_out, layout_grad_out), (text_out, layout_out))
    pages = ((work[0].g, flipped), ys)

    def page_part(g, q, a):
        span = pl.ds(q * part_length, part_length)
        return pages[g][a].at[span] if a == 0 else pages[g][a].at[:, span]

    def each_page(g, act):
        for q in range(tensors):
            for a in range(2):
                here = (micro == g) & (t == q)

                @pl.when((section == g) & here)
                def _():
                    act(g, q, a, True)

                @pl.when((section == g) & jnp.logical_not(here))
                def _():
                    act(g, q, a, False)

    def page_copy(g, q, a):
        return remote(
            page_part(g, q, a), kinds[g][a].at[page], page_send.at[q, a], page_recv.at[g, a, page],
            {"section": micro, "tensor": q},
        )

    def page_start(g, q, a, here):
        if here:
            pltpu.make_async_copy(page_part(g, q, a), kinds[g][a].at[page], page_recv.at[g, a, page]).start()
        else:
            page_copy(g, q, a).start()

    def page_sent(g, q, a, here):
        if not here:
            page_copy(g, q, a).wait_send()

    each_page(1, page_start)

    def hop(b, n):
        part = work[b].g.at[blocks[n]]
        return remote(part, part, hop_send.at[b, n], hop_recv.at[b, n], other)

    step = ROWS
    up_first, down_first = starts[0][2], starts[0][3]
    up_count, down_count = (starts[0][3] - up_first) // step, (starts[0][4] - down_first) // step
    n_feed = up_count + down_count
    chunks = [Chunk(0, k, up_first + k * step, step) for k in range(n_feed)]
    later = [(1, 0, starts[1][MATRICES])]
    later += [(0, f, n) for f, n in pieces_of(starts[0][1], 192)]
    later += [(0, starts[0][1] + f, n) for f, n in pieces_of(starts[0][2] - starts[0][1], 64)]
    chunks += [Chunk(b, n_feed + i, f, n) for i, (b, f, n) in enumerate(later)]

    def feed_chunk(k):
        return Chunk(0, k, pl.multiple_of(up_first + k * step, 16), step)

    def span(ref, c):
        return ref.at[pl.ds(c.first, c.rows)]

    def to_sibling(c, j):
        w = work[c.b]
        return remote(
            span(w.raw.at[2 * j + 1 - core], c), span(w.from_sibling.at[j], c),
            sib_send.at[c.index, j], sib_recv.at[c.index, j], sibling,
        )

    def mine(c):
        return span(work[c.b].raw.at[t], c)

    def theirs(c):
        return span(work[c.b].raw.at[2 * (1 - chip) + core], c)

    def to_partner(c):
        return remote(
            theirs(c), span(work[c.b].from_partner, c), send.at[0, c.index], recv.at[0, c.index], partner
        )

    def from_near(c):
        return span(work[c.b].from_sibling.at[0], c)

    def from_cross(c):
        return span(work[c.b].from_sibling.at[1], c)

    def to_near(c):
        return remote(mine(c), from_near(c), send.at[1, c.index], recv.at[1, c.index], near)

    def to_cross(c):
        return remote(mine(c), from_cross(c), send.at[2, c.index], recv.at[2, c.index], cross)

    def total_to_near(c):
        return remote(
            span(work[c.b].from_partner, c), from_near(c), send.at[3, c.index], recv.at[3, c.index], near
        )

    def out_copy(c, source):
        return pltpu.make_async_copy(span(source, c), span(results[c.b], c), out_sem.at[c.index])

    def added(target, *sources):
        target[...] = sum(s[...].astype(F32) for s in sources).astype(BF)

    def send_to_sibling(c):
        for j in range(tensors // 2):
            to_sibling(c, j).start()

    def stage_sibling(c):
        w = work[c.b]
        for j in range(tensors // 2):
            to_sibling(c, j).wait_recv()
        added(theirs(c), theirs(c), span(w.from_sibling.at[1 - chip], c))
        added(mine(c), mine(c), span(w.from_sibling.at[chip], c))
        if chain:
            @pl.when(jnp.logical_not(outer))
            def _():
                for device in (near, cross):
                    pl.semaphore_signal(credit, inc=1, device_id=device, device_id_type=MESH)

    def stage_partner(c):
        to_partner(c).wait_recv()
        added(mine(c), mine(c), span(work[c.b].from_partner, c))
        if not chain:
            out_copy(c, work[c.b].raw.at[t]).start()
            return

        @pl.when(outer)
        def _():
            pl.semaphore_wait(credit, 1)
            to_near(c).start()

    def stage_near(c):
        @pl.when(jnp.logical_not(outer))
        def _():
            to_near(c).wait_recv()
            added(mine(c), mine(c), from_near(c))
            pl.semaphore_wait(credit, 1)
            to_cross(c).start()

    def stage_cross(c):
        @pl.when(jnp.logical_not(outer))
        def _():
            to_cross(c).wait_recv()
            total = work[c.b].from_partner
            added(span(total, c), mine(c), from_cross(c))
            total_to_near(c).start()
            out_copy(c, total).start()

    def stage_total(c):
        @pl.when(outer)
        def _():
            total_to_near(c).wait_recv()
            out_copy(c, work[c.b].from_sibling.at[0]).start()

    def feed_products():
        own, w = views[0], work[0]
        w.lowT[...] = own.low[...].T

        @pl.loop(0, up_count)
        def _(k):
            rows = pl.ds(pl.multiple_of(k * step, step), step)
            for q in range(tensors):
                w.raw[q, pl.ds(pl.multiple_of(up_first + k * step, 16), step), :] = dot(
                    w.lowT[rows, :], own.slope[q]
                ).astype(BF)
            send_to_sibling(feed_chunk(k))

        @pl.loop(0, down_count)
        def _(k):
            lanes = pl.ds(pl.multiple_of(k * step, step), step)
            for q in range(tensors):
                w.raw[q, pl.ds(pl.multiple_of(down_first + k * step, 16), step), :] = dot(
                    own.act[q, :, lanes].T, w.gf[...]
                ).astype(BF)
            send_to_sibling(feed_chunk(up_count + k))

    def later_product(c):
        own, w = views[c.b], work[c.b]
        for q in range(tensors):
            for i in range(MATRICES):
                first = max(c.first, starts[c.b][i])
                last = min(c.first + c.rows, starts[c.b][i + 1])
                if first >= last:
                    continue
                rows = slice(first - starts[c.b][i], last - starts[c.b][i])
                if i == 0:
                    value = dot(own.qkv[q, rows, :], own.x[...])
                elif i == 1:
                    value = dot(own.ctx[q, rows, :], w.ga[...])
                elif i == 2:
                    value = dot(w.lowT[rows, :], own.slope[q])
                else:
                    value = dot(own.act[q, :, rows].T, w.gf[...])
                w.raw[q, first:last, :] = value.astype(BF)
        send_to_sibling(c)

    @pl.when(section == 1)
    def _():
        wait(*cot_copies)
        work[1].g[...] = flipped[...].T

    for b in range(2):
        work[b].sums[...] = jnp.zeros(work[b].sums.shape, F32)
    def feed_back(n, block):
        for b in (1, 0):
            own, own_in, w, gain = views[b], loads[b], work[b], gains[b]
            if n == 0:
                wait(own_in.n2, own_in.r2)

            if block in blocks:
                hop(b, n).wait_recv()

            for rows in small_blocks(block):
                g, normed = w.g[rows].astype(F32), own.n2[rows].astype(F32)
                low = norm_rows_back(g, normed, own.r2[rows], gain[1:2])
                w.dz[rows] = low
                w.gf[rows] = low.astype(BF)
                w.sums[1:2] += jnp.sum(g * normed, axis=0, keepdims=True)
                w.sums[3:4] += jnp.sum(g, axis=0, keepdims=True)

            if n == 0:
                wait(own_in.downward, own_in.slope, own_in.upward)

            @pl.loop(0, tensors)
            def _(q):
                d_act = dot(w.gf[block], own.downward[q])
                d_pre = (d_act * own.slope[q, block].astype(F32)).astype(BF)
                own.slope[q, block] = d_pre
                w.dz[block] += dot(d_pre, own.upward[q])

            if n == 0:
                wait(own_in.n1, own_in.r1, own_in.outward)
            for rows in small_blocks(block):
                g, normed = w.dz[rows], own.n1[rows].astype(F32)
                low = norm_rows_back(g, normed, own.r1[rows], gain[0:1])
                w.dz[rows] = low
                w.ga[rows] = low.astype(BF)
                w.sums[0:1] += jnp.sum(g * normed, axis=0, keepdims=True)
                w.sums[2:3] += jnp.sum(g, axis=0, keepdims=True)
            gaT = w.ga[block].T
            for q in range(tensors):
                w.dctx[q, :, block] = dot(own.outward[q], gaT).astype(BF)

    @pl.when(section == 0)
    def _():
        for n, block in enumerate(blocks):
            feed_back(n, block)

    @pl.when(section == 1)
    def _():
        feed_back(0, slice(0, length))

    wait(loads[0].low, loads[0].act)

    @pl.when(section == 0)
    def _():
        feed_products()

    for own_in in loads:
        wait(own_in.qkv, own_in.ctx, own_in.inv)
    wait(probs_copy)
    qkv = (views[0].qkv, views[1].qkv)
    text_rows, layout_rows = slice(0, HEAD_TEXT), slice(HEAD_TEXT, HEAD_TEXT + HEAD_LAYOUT)

    ahead = 3

    def turn(k, n_known):
        fixed = isinstance(k, int)

        def at(i, stage):
            if not fixed:
                pl.when((i >= 0) & (i < n_feed))(lambda: stage(feed_chunk(i)))
            elif 0 <= i < n_known:
                stage(chunks[i])

        def sibling_and_send(c):
            stage_sibling(c)
            to_partner(c).start()

        at(k + ahead, sibling_and_send)
        at(k, stage_partner)
        if chain:
            at(k - 2, stage_near)
            at(k - 4, stage_cross)
            at(k - 6, stage_total)

    def first_copies():
        for c in chunks[:ahead]:
            stage_sibling(c)
            to_partner(c).start()

    early_turns = 6

    @pl.when(section == 0)
    def _():
        first_copies()

    @pl.loop(0, tensors)
    def _(q):
        for local in range(local_heads):
            head = q * local_heads + local

            @pl.when((section == 0) & (head % 2 == 0) & (head < 2 * early_turns))
            def _():
                turn(head // 2, n_feed)

            inv = views[0].inv[q, local : local + 1, :]
            scaled = [
                (work[s].dctx[q, local * SIZES[s] : (local + 1) * SIZES[s], :].astype(F32) * inv).astype(BF)
                for s in range(2)
            ]
            inner = [
                jnp.sum(
                    scaled[s].astype(F32)
                    * views[s].ctx[q, local * SIZES[s] : (local + 1) * SIZES[s], :].astype(F32),
                    axis=0, keepdims=True,
                )
                for s in range(2)
            ]
            rows16 = lax.broadcasted_iota(jnp.int32, (16, length), 0)
            extra = jnp.zeros((16, length), F32)
            for i, value in enumerate((inner[0] + inner[1], inner[1])):
                high = value.astype(BF).astype(F32)
                extra = jnp.where(rows16 == 2 * i, -high, extra)
                extra = jnp.where(rows16 == 2 * i + 1, high - value, extra)
            pad = jnp.zeros((128 - sum(SIZES) - 16, length), BF)
            dcT = jnp.concatenate([*scaled, extra.astype(BF), pad], axis=0)
            dc = dcT.T
            qT, kT = (head_rows(qkv, q, kind, local, SCALES if kind == 0 else None) for kind in range(2))
            v_text, v_layout = (head_part(qkv, q, 2, local, s) for s in range(2))
            one, other_one = (((rows16 // 2) == i).astype(F32).astype(BF) for i in range(2))
            low = probs_in[q, local]
            probs = low.astype(F32)
            both = dot(dc, jnp.concatenate([v_text, v_layout, one, pad], axis=0))
            ds_both = (probs * both).astype(BF)
            single = dot(dc, jnp.concatenate([jnp.zeros_like(v_text), v_layout, other_one, pad], axis=0))
            ds_layout = (probs * single).astype(BF)
            dvT = dot(dcT, low)
            put_head(qkv, q, 2, local, 0, dvT[text_rows])
            put_head(qkv, q, 2, local, 1, dvT[layout_rows])
            k = kT.T
            lane = lax.broadcasted_iota(jnp.int32, (length, 128), 1)
            dq = jnp.where(lane < HEAD_TEXT, dot(ds_both, k) * SCALES[0], dot(ds_layout, k) * SCALES[1])
            dqT = dq.astype(BF).T
            put_head(qkv, q, 0, local, 0, dqT[text_rows])
            put_head(qkv, q, 0, local, 1, dqT[layout_rows])
            put_head(qkv, q, 1, local, 0, dot(qT[text_rows], ds_both))
            put_head(qkv, q, 1, local, 1, dot(qT[layout_rows], ds_layout))

    wait(loads[0].project, loads[1].project)
    page_sum = jnp.zeros((1, work[0].dz.shape[1]), F32)
    for n, block in enumerate(blocks):
        for b in (1, 0):
            down = work[b].dz[block]
            for q in range(tensors):
                down += dot(qkv[b][q, :, block].T, views[b].project[q])
            down = down.astype(BF)
            work[b].g[block] = down
            if b == 0:
                page_sum += jnp.sum(down.astype(F32), axis=0, keepdims=True)

            @pl.when(section == 1)
            def _():
                hop(b, n).start()

    wait(loads[1].low, loads[1].act)
    work[1].lowT[...] = views[1].low[...].T
    for own_in in loads:
        wait(own_in.x)
    @pl.when(section == 1)
    def _():
        feed_products()
        first_copies()

    for c in chunks[n_feed:]:
        later_product(c)

    @pl.when(section == 0)
    def _():
        flipped[...] = work[1].g[...].T
        each_page(0, page_start)

    at_page = (lax.broadcasted_iota(jnp.int32, lang_ids.shape, 0) == t % 2) & (
        lax.broadcasted_iota(jnp.int32, lang_ids.shape, 1) == t // 2
    )
    group = jnp.sum(jnp.where(at_page, lang_ids[...], 0), axis=(0, 1), keepdims=True)
    n_lang = small_out.shape[1] - 8
    chosen = (lax.broadcasted_iota(jnp.int32, (n_lang, 1), 0) == group) & (section == 0)
    small_sum[0, 0:n_lang] = jnp.where(chosen, page_sum, 0.0)
    small_sum[0, n_lang : n_lang + 4] = work[0].sums[...]
    small_sum[0, n_lang + 4 : n_lang + 8] = jnp.zeros((4, small_out.shape[2]), F32)
    small_sum[0, n_lang + 4 : n_lang + 8, : work[1].sums.shape[1]] = work[1].sums[...]

    def small_copy(i, device):
        return remote(small_sum.at[i], small_got.at[i], small_send.at[i], small_recv.at[i], device)

    if chain:
        small_copy(0, sibling).start()
    @pl.when(section == 1)
    def _():
        @pl.loop(0, early_turns)
        def _(k):
            turn(k, n_feed)

    for k in range(early_turns, len(chunks) + (6 if chain else 0)):
        turn(k, len(chunks))
        if not chain:
            continue
        if k == early_turns:
            small_copy(0, sibling).wait_recv()
            small_sum[1] = small_sum[0] + small_got[0]
            small_copy(1, partner).start()
        if k == early_turns + 1:
            small_copy(1, partner).wait_recv()
            small_sum[2] = small_sum[1] + small_got[1]
            small_copy(2, near).start()
        if k == early_turns + 2:
            small_copy(2, near).wait_recv()
            small_sum[3] = small_sum[2] + small_got[2]

            @pl.when(jnp.logical_not(outer))
            def _():
                small_copy(3, cross).start()

        if k == early_turns + 4:
            @pl.when(jnp.logical_not(outer))
            def _():
                small_copy(3, cross).wait_recv()
                small_sum[4] = small_sum[3] + small_got[3]
                small_copy(4, near).start()

        if k == early_turns + 6:
            @pl.when(outer)
            def _():
                small_copy(4, near).wait_recv()
                small_sum[4] = small_got[4]

            small_sum[5] = small_sum[4]
            small_copy(5, other).start()

    if chain:
        for i, device in enumerate((sibling, partner, near)):
            small_copy(i, device).wait_send()

        @pl.when(jnp.logical_not(outer))
        def _():
            small_copy(3, cross).wait_send()
            small_copy(4, near).wait_send()

        small_copy(5, other).wait()
        small_out[0] = small_sum[5]
        small_out[1] = small_got[5]
    else:
        small_out[0] = small_sum[0]
        small_out[1] = small_sum[0]

    @pl.when(section == 1)
    def _():
        for b in range(2):
            for n in range(len(blocks)):
                hop(b, n).wait_send()

    for c in chunks:
        for j in range(tensors // 2):
            to_sibling(c, j).wait_send()
        to_partner(c).wait_send()
        if not chain:
            out_copy(c, work[c.b].from_partner).wait()
            continue

        @pl.when(outer)
        def _():
            to_near(c).wait_send()

        @pl.when(jnp.logical_not(outer))
        def _():
            to_cross(c).wait_send()
            total_to_near(c).wait_send()

        out_copy(c, work[c.b].from_partner).wait()

    for g in range(sections):
        each_page(g, page_sent)
        for a in range(2):
            for j in range(2):
                dst = kinds[g][a].at[j]
                remote(dst, dst, page_send.at[0, a], page_recv.at[g, a, j], partner).wait_recv()
    landed = (text_out, layout_out, grad_out, layout_grad_out)
    copies = [pltpu.make_async_copy(v, h, page_out_sem.at[i]) for i, (v, h) in enumerate(zip(landed, page_outs))]
    start(*copies)
    wait(*copies)


def layer_backward(mesh, x, y, probs, kept, weights, cots, norms, lang_ids, n_lang):
    sections, dp, tensors = mesh.shape["section"], mesh.shape["dp"], mesh.shape["tensor"]
    chain = dp == 4
    needed = tuple(
        Needed(
            n2=k.n2, r2=k.r2, downward=w.downward, slope=k.slope, upward=w.upward, n1=k.n1, r1=k.r1,
            outward=w.outward, low=k.low, act=k.act, qkv=k.qkv, ctx=k.ctx, inv=k.inv, project=w.project, x=rows,
        )
        for k, w, rows in zip(kept, weights, x)
    )
    flat_in, in_tree = jax.tree.flatten((needed, probs))
    plain = [v for own in needed for name, v in own._asdict().items() if name not in Weights._fields] + [probs]
    stacks = [(matrix_starts(own)[MATRICES], rows.shape[1]) for own, rows in zip(needed, x)]
    length = x[0].shape[0]
    work = []
    for own, rows, (count, width) in zip(needed, x, stacks):
        work += Work(
            g=shape(rows.shape), gf=shape(rows.shape), ga=shape(rows.shape), dz=shape(rows.shape, F32),
            dctx=shape(own.ctx.shape), sums=shape((4, width), F32), lowT=shape((width, length)),
            raw=shape((tensors, count, width)), from_sibling=shape((tensors // 2, count, width)),
            from_partner=shape((count, width)),
        )
    small = shape((2, n_lang + 8, x[0].shape[1]), F32)
    text_page = shape((2, length // tensors, x[0].shape[1]))
    layout_page = shape((2, x[1].shape[1], length // tensors))
    summed = [shape(s) for s in stacks]
    own = needed[0]
    n_feed = (own.upward.shape[1] + own.downward.shape[1]) // ROWS
    n_chunks = n_feed + 1 + own.project.shape[1] // 192 + own.outward.shape[1] // 64
    n_blocks = len(hop_blocks(length))
    dma = pltpu.SemaphoreType.DMA
    results = pl.pallas_call(
        functools.partial(backward_kernel, sections, tensors, chain, in_tree),
        out_shape=summed + [small, text_page, layout_page, text_page, layout_page],
        in_specs=[ANY] * (len(flat_in) + 4) + [VMEM] * 3,
        out_specs=[ANY] * 2 + [VMEM] + [ANY] * 4,
        scratch_shapes=vmem_like(work) + vmem_like(plain)
        + [pltpu.VMEM(cots[1].shape, BF)] + [pltpu.VMEM((6,) + small.shape[1:], F32)] * 2
        + vmem_like([text_page, layout_page] * 2)
        + [dma((len(flat_in),)), dma((2,)), dma((2, n_blocks)), dma((2, n_blocks))]
        + [dma((n_chunks, tensors // 2))] * 2 + [dma((4, n_chunks))] * 2
        + [pltpu.SemaphoreType.REGULAR, dma((n_chunks,))]
        + [dma((6,))] * 2 + [dma((tensors, 2)), dma((sections, 2, 2)), dma((4,))],
        compiler_params=pltpu.CompilerParams(
            collective_id=1, has_side_effects=True, vmem_limit_bytes=64 << 20
        ),
        name="layer_backward",
    )(*flat_in, *cots, *y, lang_ids, norms[0][0], norms[1][0])
    totals, small, pages = results[:2], results[2], results[3:7]
    if not chain:
        totals = lax.psum(tuple(totals), "dp")
        both = lax.psum(small[0], ("dp", "tensor"))
        small = jnp.stack([both, lax.ppermute(both, "section", [(0, 1), (1, 0)])])
    return totals, small, pages


def widen_kernel(n_in, n_pages, *refs):
    n_out = 5 + n_pages + 2 * MATRICES
    hbm_in, hbm_out = refs[:n_in], refs[n_in : n_in + n_out]
    vmem_in, vmem_out = refs[n_in + n_out : 2 * n_in + n_out], refs[2 * n_in + n_out : -2]
    in_sem, out_sem = refs[-2:]
    loads = [pltpu.make_async_copy(h, v, in_sem.at[i]) for i, (h, v) in enumerate(zip(hbm_in, vmem_in))]
    sources = vmem_out[:5] + vmem_in[3:] + vmem_out[5:]
    stores = [pltpu.make_async_copy(v, h, out_sem.at[i]) for i, (v, h) in enumerate(zip(sources, hbm_out))]
    start(*loads)
    totals, small = vmem_in[0:2], vmem_in[2]
    for b in range(2):
        wait(loads[b])
        at = 0
        for i in range(b * MATRICES, (b + 1) * MATRICES):
            out = vmem_out[5 + i]
            for c in range(0, out.shape[0], 48):
                out[c : c + 48] = totals[b][at + c : at + c + 48].astype(F32)
            at += out.shape[0]
            stores[5 + n_pages + i].start()
    for i in range(n_pages):
        loads[3 + i].wait()
        stores[5 + i].start()
    loads[2].wait()
    n_lang = vmem_out[0].shape[0]
    vmem_out[0][...] = jnp.where(lax.axis_index("section") == 0, small[0, :n_lang], small[1, :n_lang])
    for i, out in enumerate(vmem_out[1:5]):
        first = n_lang + 2 * i
        out[...] = small[0, first : first + 2, : out.shape[1]]
    start(*stores[:5])
    wait(*stores)


def widen(totals, small, pages, shards, n_lang):
    widths = [total.shape[1] for total in totals]
    sums = [shape((n_lang, widths[0]), F32)] + [shape((2, w), F32) for w in widths for _ in range(2)]
    grads = [shape(m.shape, F32) for own in shards for m in own]
    inputs = (*totals, small, *pages)
    outs = sums + [shape(page.shape) for page in pages] + grads
    results = pl.pallas_call(
        functools.partial(widen_kernel, len(inputs), len(pages)), out_shape=outs,
        in_specs=[ANY] * len(inputs), out_specs=[ANY] * len(outs),
        scratch_shapes=vmem_like(inputs) + vmem_like(sums + grads)
        + [pltpu.SemaphoreType.DMA((len(inputs),)), pltpu.SemaphoreType.DMA((len(outs),))],
        compiler_params=pltpu.CompilerParams(vmem_limit_bytes=62 << 20), name="widen",
    )(*inputs)
    return results[0], results[1:5], results[5:9], results[9:13], results[13:17]


def per_device(
    mesh,
    text_input,
    layout_input,
    text_cotangent,
    layout_cotangent,
    page_counts,
    pad_mask,
    lang_ids,
    lang_table,
    text_project,
    text_outward,
    text_upward,
    text_downward,
    text_gains,
    text_biases,
    layout_project,
    layout_outward,
    layout_upward,
    layout_downward,
    layout_gains,
    layout_biases,
):
    def flat(project):
        return jnp.transpose(project[0], (1, 2, 0)).reshape(-1, project.shape[1])

    def flipped(block):
        return jnp.transpose(block[0], (0, 2, 1))

    shards = (
        Weights(flat(text_project), text_outward[0], text_upward[0], text_downward[0]),
        Weights(flat(layout_project), layout_outward[0], layout_upward[0], layout_downward[0]),
    )
    norms = ((text_gains[0], text_biases[0]), (layout_gains[0], layout_biases[0]))
    marks = (pad_mask, page_counts, lang_ids, lang_table)
    (x, y, probs, kept, weights), cots = layer_forward(
        mesh, text_input[0], flipped(layout_input), text_cotangent[0], flipped(layout_cotangent), shards, norms, marks
    )
    n_lang = lang_table.shape[0]
    totals, small, pages = layer_backward(mesh, x, y, probs, kept, weights, cots, norms, lang_ids, n_lang)
    lang_sum, norm_sums, pages, text_sums, layout_sums = widen(totals, small, pages, shards, n_lang)
    text_out, layout_out, text_grad, layout_grad = pages

    def unflat(grad, like):
        return jnp.transpose(grad.reshape(like.shape[2], like.shape[3], like.shape[1]), (2, 0, 1))[None]

    unflip = lambda block: jnp.transpose(block, (0, 2, 1))[None]
    return (
        text_out[None], unflip(layout_out), text_grad[None], unflip(layout_grad), lang_sum,
        unflat(text_sums[0], text_project), *(s[None] for s in text_sums[1:]), norm_sums[0][None], norm_sums[1][None],
        unflat(layout_sums[0], layout_project), *(s[None] for s in layout_sums[1:]),
        norm_sums[2][None], norm_sums[3][None],
    )


def solution(mesh):
    tokens = P("section", "dp", "tensor", None)
    weight_specs = (
        P("section", None, None, "tensor"), P("section", "tensor", None), P("section", None, "tensor"),
        P("section", "tensor", None), P("section", None, None), P("section", None, None),
    )
    in_specs = (tokens,) * 4 + (P(None, "dp"), P(None, "dp", None), P(None, "dp"), P()) + weight_specs * 2
    out_specs = (tokens,) * 4 + (P(),) + weight_specs * 2
    return jax.shard_map(
        functools.partial(per_device, mesh), mesh=mesh, in_specs=in_specs, out_specs=out_specs, check_vma=False
    )
```

```python
import functools
import math
import typing

import jax
import jax.numpy as jnp
from jax import lax
from jax.experimental import pallas as pl
from jax.experimental.pallas import tpu as pltpu
from jax.sharding import PartitionSpec as P

HEAD_TEXT = 64
HEAD_LAYOUT = 16
EPSILON = 1e-05
NEGATIVE = -1e30
HIGH = lax.Precision.HIGHEST
MESH = pl.DeviceIdType.MESH
BF = jnp.bfloat16
F32 = jnp.float32
ANY = pl.BlockSpec(memory_space=pl.ANY)


def remote(src, dst, send, recv, device):
    return pltpu.make_async_remote_copy(
        src_ref=src, dst_ref=dst, send_sem=send, recv_sem=recv, device_id=device, device_id_type=MESH
    )


def greet(section, tensor, sections, tensors, extra=()):
    barrier = pltpu.get_barrier_semaphore()
    for g in range(sections):
        for q in range(tensors):

            @pl.when((section != g) | (tensor != q))
            def _():
                pl.semaphore_signal(
                    barrier, inc=1, device_id={"section": g, "tensor": q}, device_id_type=MESH
                )

    for device in extra:
        pl.semaphore_signal(barrier, inc=1, device_id=device, device_id_type=MESH)
    pl.semaphore_wait(barrier, sections * tensors - 1 + len(extra))


GELU_P = 0.3275911
GELU_A = (0.254829592, -0.284496736, 1.421413741, -1.453152027, 1.061405429)
NN = (((1,), (0,)), ((), ()))
NT = (((1,), (1,)), ((), ()))
SCALES = (1.0 / math.sqrt(HEAD_TEXT), 1.0 / math.sqrt(HEAD_LAYOUT))
SIZES = (HEAD_TEXT, HEAD_LAYOUT)
ROWS = 128


class Weights(typing.NamedTuple):
    project: typing.Any
    outward: typing.Any
    upward: typing.Any
    downward: typing.Any


class Kept(typing.NamedTuple):
    qkv: typing.Any
    ctx: typing.Any
    inv: typing.Any
    n1: typing.Any
    low: typing.Any
    act: typing.Any
    slope: typing.Any
    n2: typing.Any


def dot(a, b, dims=NN):
    return lax.dot_general(a, b, dims, preferred_element_type=F32)


def gelu_pair(u):
    d = 1.0 + (GELU_P / math.sqrt(2.0)) * jnp.abs(u)
    t = pl.reciprocal(d, approx=True)
    t = t * (2.0 - d * t)
    e = jnp.exp2((u * u) * (-0.5 / math.log(2.0)))
    a1, a2, a3, a4, a5 = (0.5 * a for a in GELU_A)
    tail = ((((a5 * t + a4) * t + a3) * t + a2) * t + a1) * t * e
    cdf = jnp.where(u >= 0, 1.0 - tail, tail)
    return u * cdf, cdf + u * e * (1.0 / math.sqrt(2.0 * math.pi))


def norm_rows(z, gain, offset):
    center = z - jnp.mean(z, axis=-1, keepdims=True)
    inverse = lax.rsqrt(jnp.mean(center * center, axis=-1, keepdims=True) + EPSILON)
    normed = center * inverse
    return normed * gain + offset, normed, inverse


def norm_rows_back(g, n, r, gain):
    t = g * gain
    return r * (t - jnp.mean(t, axis=-1, keepdims=True) - n * jnp.mean(t * n, axis=-1, keepdims=True))


class Staged:
    def __init__(self, tree, hbm, vmem, sem, inward):
        self.tree, self.vmem = tree, list(vmem)
        pairs = zip(hbm, vmem) if inward else zip(vmem, hbm)
        self.copies = [pltpu.make_async_copy(a, b, sem.at[i]) for i, (a, b) in enumerate(pairs)]

    def refs(self):
        return jax.tree.unflatten(self.tree, self.vmem)

    def parts(self):
        return jax.tree.unflatten(self.tree, self.copies)

    def start(self):
        for copy in self.copies:
            copy.start()

    def wait(self):
        for copy in self.copies:
            copy.wait()


def start(*copies):
    for copy in copies:
        copy.start()


def wait(*copies):
    for copy in copies:
        copy.wait()


def head_rows(stacks, slot, kind, local, scales=None, extra=None):
    rows = []
    for b in range(2):
        piece = head_part(stacks, slot, kind, local, b)
        rows.append(piece if scales is None else piece * BF(scales[b]))
    length = rows[0].shape[1]
    rows.append(jnp.zeros((16, length), BF) if extra is None else extra)
    rows.append(jnp.zeros((128 - sum(SIZES) - 16, length), BF))
    return jnp.concatenate(rows, axis=0)


def head_part(stacks, slot, kind, local, b):
    first = kind * (stacks[b].shape[1] // 3) + local * SIZES[b]
    return stacks[b][slot, first : first + SIZES[b], :]


def small_blocks(block, step=64):
    return [slice(c, c + step) for c in range(block.start, block.stop, step)]


def put_head(stacks, slot, kind, local, b, value):
    first = kind * (stacks[b].shape[1] // 3) + local * SIZES[b]
    stacks[b][slot, first : first + SIZES[b], :] = value.astype(BF)


def hop_blocks(length):
    ends = [0, length // 2, length * 3 // 4, length]
    return [slice(a, b) for a, b in zip(ends, ends[1:])]


def slot_of(u, core, chip):
    return ((chip + u // 2) % 2) * 2 + (core + u % 2) % 2


def forward_kernel(sections, tensors, shared, in_tree, out_tree, *refs):
    n_w, n_out = len(shared), out_tree.num_leaves
    sources = (refs[0:2], refs[2:4])
    shards = refs[4 : 4 + n_w]
    pad_mask, counts, lang_ids, lang_table, *norms = refs[4 + n_w : 12 + n_w]
    rest = refs[12 + n_w :]
    hbm_out, cots_out, rest = rest[:n_out], rest[n_out : n_out + 2], rest[n_out + 2 :]
    outgoing = Staged(out_tree, hbm_out, rest[:n_out], rest[n_out], False)
    rest = rest[n_out + 1 :]
    flipped, raw_x, y_narrow, *rest = rest
    nats, totals, pre, score_buffer, rest = rest[0:2], rest[2:4], rest[4:6], rest[6], rest[7:]
    xT, turned, turn_sem, rest = rest[0:2], (rest[2:4], rest[4:6]), rest[6], rest[7:]
    page_send, page_recv, w_send, w_recv, own_sem, hop_send, hop_recv, cot_sem = rest
    x, y_pages, probs_out, roots, kept, weights = outgoing.refs()
    y = (y_pages[0], y_narrow)
    x_out, y_out, probs_copy, roots_copy, kept_out, weights_out = outgoing.parts()
    weights_hbm = jax.tree.unflatten(out_tree, list(hbm_out))[5]
    section, d, t = lax.axis_index("section"), lax.axis_index("dp"), lax.axis_index("tensor")
    core, chip, half_index = t % 2, t // 2, d % 2
    sibling, partner = t + 1 - 2 * core, (t + tensors // 2) % tensors
    mate = d + 1 - 2 * half_index
    micro, page = core, chip
    part_length = sources[0][0].shape[1]
    length = x[0].shape[0]
    blocks = [slice(c, c + 2 * ROWS) for c in range(0, length, 2 * ROWS)]
    parts = hop_blocks(length)
    full = (
        weights[0].project, weights[1].project, weights[0].outward, weights[0].upward,
        weights[0].downward, weights[1].outward, weights[1].upward, weights[1].downward,
    )
    greet(section, t, sections, tensors, ({"dp": mate},) if any(shared) else ())

    def half_of(ref, i, which):
        count = shards[i].shape[0] // 2
        return ref.at[pl.ds(pl.multiple_of(which * count, 16), count)] if shared[i] else ref

    def to_partner(i):
        return remote(
            half_of(shards[i], i, half_index), half_of(full[i].at[t], i, half_index),
            w_send.at[0, i], w_recv.at[0, i], {"tensor": partner},
        )

    def to_sibling(i):
        return remote(full[i].at[t], full[i].at[t], w_send.at[1, i], w_recv.at[1, i], {"tensor": sibling})

    def to_mate(i):
        ref = half_of(full[i].at[partner], i, half_index)
        return remote(ref, ref, w_send.at[2, i], w_recv.at[2, i], {"dp": mate})

    def on_first(i):
        ref = half_of(full[i].at[partner], i, half_index)
        return remote(ref, ref, w_send.at[3, i], w_recv.at[3, i], {"tensor": sibling})

    def on_second(i):
        ref = half_of(full[i].at[partner], i, 1 - half_index)
        return remote(ref, ref, w_send.at[4, i], w_recv.at[4, i], {"tensor": sibling})

    def keep(i):
        return pltpu.make_async_copy(shards[i], full[i].at[t], own_sem.at[i])

    def relay(*which):
        for i in which:
            to_partner(i).wait_recv()
            if shared[i]:
                to_mate(i).start()
            on_first(i).start()

    def relay_second(*which):
        for i in which:
            if shared[i]:
                to_mate(i).wait_recv()
                on_second(i).start()

    def early(*which):
        for i in which:
            to_sibling(i).wait_recv()

    def late(*which):
        for i in which:
            on_first(i).wait_recv()
            if shared[i]:
                on_second(i).wait_recv()

    def token_slot(g, a, index):
        start_at = pl.multiple_of(index * part_length, part_length)
        target = (raw_x, flipped)[a]
        return target.at[pl.ds(start_at, part_length)] if a == 0 else target.at[:, pl.ds(start_at, part_length)]

    def over_pages(g, act):
        for j in range(2):
            target = 2 * j + section
            here = (section == g) & (t == target)
            for a in range(2):
                act(g, j, a, target, here)

    def page_copy(g, j, a, target):
        return remote(
            sources[g][a].at[j], token_slot(g, a, t), page_send.at[g, j, a], page_recv.at[a, t],
            {"section": g, "tensor": target},
        )

    def page_start(g, j, a, target, here):
        @pl.when(here)
        def _():
            pltpu.make_async_copy(sources[g][a].at[j], token_slot(g, a, t), page_recv.at[a, t]).start()

        @pl.when(jnp.logical_not(here))
        def _():
            page_copy(g, j, a, target).start()

    def page_sent(g, j, a, target, here):
        @pl.when(jnp.logical_not(here))
        def _():
            page_copy(g, j, a, target).wait_send()

    def pages_arrived(g):
        for a in range(2):
            for q in range(tensors):
                slot = token_slot(g, a, q)
                remote(slot, slot, page_send.at[0, 0, a], page_recv.at[a, q], {"tensor": sibling}).wait_recv()

    def hop(b, n):
        return remote(
            y[b].at[parts[n]], x[b].at[parts[n]], hop_send.at[b, n], hop_recv.at[b, n], {"section": 1 - section}
        )

    def weights_to_hbm():
        for b in range(2):
            start(weights_out[b].project, weights_out[b].outward)
            for q in range(tensors):
                for m, name in enumerate((2, 3)):
                    copy = pltpu.make_async_copy(
                        turned[b][m].at[q % 2], weights_hbm[b][name].at[q], turn_sem.at[b, m, q % 2]
                    )
                    if q >= 2:
                        copy.wait()
                    turned[b][m][q % 2] = weights[b][name][q].T
                    copy.start()
        for b in range(2):
            for q in range(tensors - 2, tensors):
                for m, name in enumerate((2, 3)):
                    pltpu.make_async_copy(
                        turned[b][m].at[q % 2], weights_hbm[b][name].at[q], turn_sem.at[b, m, q % 2]
                    ).wait()

    over_pages(0, page_start)
    for i in range(n_w):
        keep(i).start()
    for i in range(n_w):
        to_partner(i).start()
    over_pages(1, page_start)
    for i in range(n_w):
        keep(i).wait()
        to_sibling(i).start()

    at_page = (lax.broadcasted_iota(jnp.int32, counts.shape, 0) == micro) & (
        lax.broadcasted_iota(jnp.int32, counts.shape, 1) == page
    )

    def own_entry(ref):
        return jnp.sum(jnp.where(at_page, ref[...], 0), axis=(0, 1), keepdims=True)

    positions = lax.broadcasted_iota(jnp.int32, (1, length), 1)
    mask_row = pad_mask[micro, pl.ds(page, 1), :]
    key_mask = (positions < own_entry(counts)) & ((mask_row == 1) | (positions == 0))
    first_row = (lax.broadcasted_iota(jnp.int32, (16, length), 0) == 0).astype(F32)
    mask_row16 = (first_row * jnp.where(key_mask, 0.0, NEGATIVE)).astype(BF)
    groups = lax.broadcasted_iota(jnp.int32, (lang_table.shape[0], 1), 0)
    lang_row = jnp.sum(jnp.where(groups == own_entry(lang_ids), lang_table[...], 0.0), axis=0, keepdims=True)
    local_heads = weights[0].project.shape[1] // (3 * HEAD_TEXT)
    qkv = (kept[0].qkv, kept[1].qkv)

    @pl.when(section == 0)
    def _():
        pages_arrived(0)
        x[0][...] = (raw_x[...].astype(F32) + lang_row).astype(BF)
        x[1][...] = flipped[...].T
        early(0, 1)

    @pl.when(section == 1)
    def _():
        relay(*range(n_w))
        relay_second(*range(n_w))
        early(*range(n_w))
        late(*range(n_w))
        weights_to_hbm()

    @pl.loop(0, 2)
    def _(half):
        @pl.when((half == 1) & (section == 0))
        def _():
            relay(0, 1)
            relay_second(0)
            late(0, 1)

        for n, block in enumerate(parts):
            @pl.when((half == 0) & (section == 1))
            def _():
                for b in range(2):
                    hop(b, n).wait_recv()

            @pl.when(half == 0)
            def _():
                for b in range(2):
                    xT[b][:, block] = x[b][block].T

            @pl.loop(0, 2)
            def _(u):
                slot = slot_of(2 * half + u, core, chip)
                for b in range(2):
                    qkv[b][slot, :, block] = dot(weights[b].project[slot], xT[b][:, block]).astype(BF)

        @pl.loop(0, 2)
        def _(u):
            slot = slot_of(2 * half + u, core, chip)
            for local in range(local_heads):
                q = head_rows(qkv, slot, 0, local, SCALES, first_row.astype(BF)).T
                kT = head_rows(qkv, slot, 1, local, None, mask_row16)
                score_buffer[local] = dot(q, kT)
                for rows in small_blocks(slice(0, length)):
                    scores = score_buffer[local, rows, :]
                    raised = jnp.exp(scores - jnp.max(scores, axis=-1, keepdims=True))
                    probs_out[slot, local, rows, :] = raised.astype(BF)
                vT = head_rows(qkv, slot, 2, local, None, first_row.astype(BF))
                ctx = dot(probs_out[slot, local], vT.T).T
                inv = 1.0 / ctx[sum(SIZES) : sum(SIZES) + 1]
                ctx = (ctx * inv).astype(BF)
                kept[0].inv[slot, local : local + 1, :] = inv
                kept[0].ctx[slot, local * HEAD_TEXT : (local + 1) * HEAD_TEXT, :] = ctx[:HEAD_TEXT]
                kept[1].ctx[slot, local * HEAD_LAYOUT : (local + 1) * HEAD_LAYOUT, :] = ctx[
                    HEAD_TEXT : HEAD_TEXT + HEAD_LAYOUT
                ]

    kept[1].inv[...] = jnp.zeros(kept[1].inv.shape, F32)
    start(probs_copy, *x_out, *(c for k in kept_out for c in (k.qkv, k.ctx, k.inv)))

    def attend(b):
        gains, biases = norms[2 * b : 2 * b + 2]
        width = x[b].shape[1]
        nats[b][...] = kept[b].ctx[...].reshape(width, length).T
        wide = weights[b].outward[...].reshape(width, width)
        for block in blocks:
            totals[b][1, block] = dot(nats[b][block], wide)
            for rows in small_blocks(block):
                h, n, r = norm_rows(x[b][rows].astype(F32) + totals[b][1, rows], gains[0:1], biases[0:1])
                totals[b][0, rows] = h
                totals[b][1, rows] = jnp.zeros(h.shape, F32)
                kept[b].n1[rows] = n.astype(BF)
                roots[rows, 2 * b : 2 * b + 1] = r
                kept[b].low[rows] = h.astype(BF)
        start(kept_out[b].n1, kept_out[b].low)

    def feed(b, first, which):
        @pl.loop(first, first + 2)
        def _(u):
            slot = slot_of(u, core, chip)
            for block in which:
                pre[b][block] = dot(kept[b].low[block], weights[b].upward[slot])
                for rows in small_blocks(block, 16):
                    act, slope = gelu_pair(pre[b][rows])
                    kept[b].act[slot, rows] = act.astype(BF)
                    kept[b].slope[slot, rows] = slope.astype(BF)
                totals[b][1, block] += dot(kept[b].act[slot, block], weights[b].downward[slot])

    def finish(b):
        gains, biases = norms[2 * b : 2 * b + 2]
        def last(block):
            feed(b, 2, [block])
            for rows in small_blocks(block):
                out, normed, r = norm_rows(totals[b][0, rows] + totals[b][1, rows], gains[1:2], biases[1:2])
                y[b][rows] = out.astype(BF)
                kept[b].n2[rows] = normed.astype(BF)
                roots[rows, 2 * b + 1 : 2 * b + 2] = r

        @pl.when(section == 0)
        def _():
            for n, block in enumerate(parts):
                last(block)
                hop(b, n).start()

        @pl.when(section == 1)
        def _():
            last(slice(0, length))

        if b == 1:
            y_pages[1][...] = y_narrow[...].T
        start(y_out[b], kept_out[b].act, kept_out[b].slope, kept_out[b].n2)

    @pl.when(section == 0)
    def _():
        relay(2, 3)
        early(2)
        late(2)

    attend(0)

    @pl.when(section == 0)
    def _():
        early(3, 4)

    feed(0, 0, [slice(0, length)])

    @pl.when(section == 0)
    def _():
        relay(4, 5, 6, 7)
        relay_second(3)
        early(5, 6, 7)
        late(5, 6, 7)

    attend(1)
    feed(1, 0, [slice(0, length)])
    finish(1)

    @pl.when(section == 0)
    def _():
        relay_second(4)
        late(3, 4)

    finish(0)
    start(roots_copy)

    @pl.when(section == 0)
    def _():
        weights_to_hbm()
        for b in range(2):
            for n in range(len(parts)):
                hop(b, n).wait_send()

    for i in range(n_w):
        to_partner(i).wait_send()
        to_sibling(i).wait_send()
        on_first(i).wait_send()
        if shared[i]:
            to_mate(i).wait_send()
            on_second(i).wait_send()
    for g in range(sections):
        over_pages(g, page_sent)

    @pl.when(section == 1)
    def _():
        pages_arrived(1)
        copies = [pltpu.make_async_copy(v, h, cot_sem.at[i]) for i, (v, h) in enumerate(zip((raw_x, flipped), cots_out))]
        start(*copies)
        wait(*copies)

    for group in (x_out, y_out, (probs_copy, roots_copy), *kept_out, *(w[:2] for w in weights_out)):
        wait(*group)


def vmem_like(tree):
    return [pltpu.VMEM(s.shape, s.dtype) for s in jax.tree.leaves(tree)]


VMEM = pl.BlockSpec(memory_space=pltpu.VMEM)


def shape(dims, dtype=BF):
    return jax.ShapeDtypeStruct(tuple(dims), dtype)


def layer_forward(mesh, text_in, layout_in, text_cot, layout_cot, shards, norms, marks):
    sections, dp, tensors = mesh.shape["section"], mesh.shape["dp"], mesh.shape["tensor"]
    length = text_in.shape[1] * tensors
    rows = (shape((length, text_in.shape[2])), shape((length, layout_in.shape[1])))
    local_heads = shards[0].project.shape[0] // (3 * HEAD_TEXT)
    kept = []
    for x, w in zip(rows, shards):
        units = shape((tensors, length, w.upward.shape[1]))
        kept.append(Kept(
            qkv=shape((tensors, w.project.shape[0], length)), ctx=shape((tensors, w.outward.shape[0], length)),
            inv=shape((tensors, local_heads, length), F32),
            n1=shape(x.shape), low=shape(x.shape), act=units, slope=units,
            n2=shape(x.shape),
        ))
    weights = tuple(Weights(*(shape((tensors,) + m.shape) for m in w)) for w in shards)
    pages_out = (rows[0], shape((rows[1].shape[1], length)))
    outs = (rows, pages_out, shape((tensors, local_heads, length, length)), shape((length, 4), F32), tuple(kept), weights)
    flat_out, out_tree = jax.tree.flatten(outs)
    (a, b) = shards
    ordered = (a.project, b.project, a.outward, a.upward, a.downward, b.outward, b.upward, b.downward)
    shared = tuple(dp % 2 == 0 and w.shape[0] >= 512 for w in ordered)
    n_w = len(ordered)
    cots = [rows[0], shape((rows[1].shape[1], length))]
    small = (*marks, *norms[0], *norms[1])
    results = pl.pallas_call(
        functools.partial(forward_kernel, sections, tensors, shared, None, out_tree),
        out_shape=flat_out + cots,
        in_specs=[ANY] * (4 + n_w) + [VMEM] * len(small),
        out_specs=[ANY] * (len(flat_out) + 2),
        scratch_shapes=vmem_like(flat_out) + [pltpu.SemaphoreType.DMA((len(flat_out),))]
        + [pltpu.VMEM(cots[1].shape, BF), pltpu.VMEM(cots[0].shape, BF), pltpu.VMEM(rows[1].shape, BF)]
        + [pltpu.VMEM(x.shape, BF) for x in rows]
        + [pltpu.VMEM((2,) + x.shape, F32) for x in rows]
        + [pltpu.VMEM((length, w.upward.shape[1]), F32) for w in shards]
        + [pltpu.VMEM((local_heads, length, length), F32)]
        + [pltpu.VMEM((x.shape[1], length), BF) for x in rows]
        + [pltpu.VMEM((2,) + m.shape, BF) for w in shards for m in (w.upward, w.downward)]
        + [pltpu.SemaphoreType.DMA((2, 2, 2))]
        + [
            pltpu.SemaphoreType.DMA((sections, 2, 2)), pltpu.SemaphoreType.DMA((2, tensors)),
            pltpu.SemaphoreType.DMA((5, n_w)), pltpu.SemaphoreType.DMA((5, n_w)), pltpu.SemaphoreType.DMA((n_w,)),
            pltpu.SemaphoreType.DMA((2, len(hop_blocks(length)))), pltpu.SemaphoreType.DMA((2, len(hop_blocks(length)))),
            pltpu.SemaphoreType.DMA((2,)),
        ],
        compiler_params=pltpu.CompilerParams(
            collective_id=0, has_side_effects=True, vmem_limit_bytes=62 << 20
        ),
        name="layer_forward",
    )(text_in, layout_in, text_cot, layout_cot, *ordered, *small)
    return jax.tree.unflatten(out_tree, results[:-2]), tuple(results[-2:])


class Needed(typing.NamedTuple):
    n2: typing.Any
    downward: typing.Any
    slope: typing.Any
    upward: typing.Any
    n1: typing.Any
    outward: typing.Any
    low: typing.Any
    act: typing.Any
    qkv: typing.Any
    ctx: typing.Any
    inv: typing.Any
    project: typing.Any
    x: typing.Any


class Work(typing.NamedTuple):
    g: typing.Any
    gf: typing.Any
    ga: typing.Any
    dz: typing.Any
    dctx: typing.Any
    sums: typing.Any
    lowT: typing.Any
    raw: typing.Any
    from_sibling: typing.Any
    from_partner: typing.Any


class Chunk(typing.NamedTuple):
    b: typing.Any
    index: typing.Any
    first: typing.Any
    rows: typing.Any


MATRICES = 4


def matrix_rows(own):
    return own.project.shape[1], own.outward.shape[1], own.upward.shape[1], own.downward.shape[1]


def matrix_starts(own):
    sizes = matrix_rows(own)
    return [sum(sizes[:i]) for i in range(MATRICES + 1)]


def pieces_of(size, step):
    return [(f, step) for f in range(0, size, step)]


def backward_kernel(sections, tensors, chain, in_tree, *refs):
    n_in = in_tree.num_leaves
    hbm_in, refs = refs[:n_in], refs[n_in:]
    (cots, ys, lang_ids, gains), refs = (refs[0:2], refs[2:4], refs[4], refs[5:7]), refs[7:]
    results, small_out, page_outs, refs = refs[0:2], refs[2], refs[3:7], refs[7:]
    n_work = len(Work._fields)
    work, refs = (Work(*refs[:n_work]), Work(*refs[n_work : 2 * n_work])), refs[2 * n_work :]
    plain, refs = refs[: n_in - 2 * MATRICES], refs[n_in - 2 * MATRICES :]
    flipped, small_got, small_sum, refs = refs[0], refs[1], refs[2], refs[3:]
    text_out, layout_out, grad_out, layout_grad_out, *refs = refs
    in_sem, cot_sem, hop_send, hop_recv, sib_send, sib_recv, send, recv, credit, out_sem, *refs = refs
    small_send, small_recv, page_send, page_recv, page_out_sem = refs
    section, d, t = lax.axis_index("section"), lax.axis_index("dp"), lax.axis_index("tensor")
    core, chip = t % 2, t // 2
    sibling = {"tensor": t + 1 - 2 * core}
    partner = {"tensor": (t + tensors // 2) % tensors}
    near, cross = {"dp": d + 1 - 2 * (d % 2)}, {"dp": 3 - d}
    outer = (d == 0) | (d == 3)
    other = {"section": 1 - section}
    hbm, probs_hbm, roots_hbm = jax.tree.unflatten(in_tree, hbm_in)
    starts = [matrix_starts(own) for own in hbm]

    plain = list(plain)
    views = []
    for b in range(2):
        fields = {}
        for name, value in hbm[b]._asdict().items():
            if name in Weights._fields:
                i = Weights._fields.index(name)
                fields[name] = work[b].raw.at[:, pl.ds(starts[b][i], starts[b][i + 1] - starts[b][i])]
            else:
                fields[name] = plain.pop(0)
        views.append(Needed(**fields))
    probs_in, roots = plain
    flat_views = jax.tree.leaves((tuple(views), probs_in, roots))
    flat_copies = [pltpu.make_async_copy(a, v, in_sem.at[i]) for i, (a, v) in enumerate(zip(hbm_in, flat_views))]
    loads, probs_copy, roots_copy = jax.tree.unflatten(in_tree, flat_copies)
    length = work[0].gf.shape[0]
    local_heads = probs_in.shape[1]
    blocks = hop_blocks(length)
    cot_copies = (
        pltpu.make_async_copy(cots[0], work[0].g, cot_sem.at[0]),
        pltpu.make_async_copy(cots[1], flipped, cot_sem.at[1]),
    )

    @pl.when(section == 1)
    def _():
        start(*cot_copies)

    roots_copy.start()
    for field in zip(loads[1], loads[0]):
        start(*field)
    probs_copy.start()
    greet(section, t, sections, tensors, (near, cross) if chain else ())

    part_length = text_out.shape[1]
    micro, page = core, chip
    kinds = ((grad_out, layout_grad_out), (text_out, layout_out))
    pages = ((work[0].g, flipped), ys)

    def page_part(g, q, a):
        span = pl.ds(q * part_length, part_length)
        return pages[g][a].at[span] if a == 0 else pages[g][a].at[:, span]

    def each_page(g, act):
        for q in range(tensors):
            for a in range(2):
                here = (micro == g) & (t == q)

                @pl.when((section == g) & here)
                def _():
                    act(g, q, a, True)

                @pl.when((section == g) & jnp.logical_not(here))
                def _():
                    act(g, q, a, False)

    def page_copy(g, q, a):
        return remote(
            page_part(g, q, a), kinds[g][a].at[page], page_send.at[q, a], page_recv.at[g, a, page],
            {"section": micro, "tensor": q},
        )

    def page_start(g, q, a, here):
        if here:
            pltpu.make_async_copy(page_part(g, q, a), kinds[g][a].at[page], page_recv.at[g, a, page]).start()
        else:
            page_copy(g, q, a).start()

    def page_sent(g, q, a, here):
        if not here:
            page_copy(g, q, a).wait_send()

    each_page(1, page_start)

    def hop(b, n):
        part = work[b].g.at[blocks[n]]
        return remote(part, part, hop_send.at[b, n], hop_recv.at[b, n], other)

    ahead = 3
    step = ROWS
    up_first, down_first = starts[0][2], starts[0][3]
    up_count, down_count = (starts[0][3] - up_first) // step, (starts[0][4] - down_first) // step
    n_feed = up_count + down_count
    chunks = [Chunk(0, k, up_first + k * step, step) for k in range(n_feed)]
    later = [(1, 0, starts[1][MATRICES])]
    later += [(0, f, n) for f, n in pieces_of(starts[0][1], 192)]
    later += [(0, starts[0][1] + f, n) for f, n in pieces_of(starts[0][2] - starts[0][1], 64)]
    chunks += [Chunk(b, n_feed + i, f, n) for i, (b, f, n) in enumerate(later)]

    def feed_chunk(k):
        return Chunk(0, k, pl.multiple_of(up_first + k * step, 16), step)

    def span(ref, c):
        return ref.at[pl.ds(c.first, c.rows)]

    def to_sibling(c, j):
        w = work[c.b]
        return remote(
            span(w.raw.at[2 * j + 1 - core], c), span(w.from_sibling.at[j], c),
            sib_send.at[c.index, j], sib_recv.at[c.index, j], sibling,
        )

    def mine(c):
        return span(work[c.b].raw.at[t], c)

    def theirs(c):
        return span(work[c.b].raw.at[2 * (1 - chip) + core], c)

    def to_partner(c):
        return remote(
            theirs(c), span(work[c.b].from_partner, c), send.at[0, c.index], recv.at[0, c.index], partner
        )

    def from_near(c):
        return span(work[c.b].from_sibling.at[0], c)

    def from_cross(c):
        return span(work[c.b].from_sibling.at[1], c)

    def to_near(c):
        return remote(mine(c), from_near(c), send.at[1, c.index], recv.at[1, c.index], near)

    def to_cross(c):
        return remote(mine(c), from_cross(c), send.at[2, c.index], recv.at[2, c.index], cross)

    def total_to_near(c):
        return remote(
            span(work[c.b].from_partner, c), from_near(c), send.at[3, c.index], recv.at[3, c.index], near
        )

    def out_copy(c, source):
        return pltpu.make_async_copy(span(source, c), span(results[c.b], c), out_sem.at[c.index])

    def added(target, *sources):
        target[...] = sum(s[...].astype(F32) for s in sources).astype(BF)

    def send_to_sibling(c):
        for j in range(tensors // 2):
            to_sibling(c, j).start()

    def stage_sibling(c):
        w = work[c.b]
        for j in range(tensors // 2):
            to_sibling(c, j).wait_recv()
        added(theirs(c), theirs(c), span(w.from_sibling.at[1 - chip], c))
        added(mine(c), mine(c), span(w.from_sibling.at[chip], c))
        if chain:
            @pl.when(jnp.logical_not(outer))
            def _():
                for device in (near, cross):
                    pl.semaphore_signal(credit, inc=1, device_id=device, device_id_type=MESH)

    def stage_partner(c):
        to_partner(c).wait_recv()
        added(mine(c), mine(c), span(work[c.b].from_partner, c))
        if not chain:
            out_copy(c, work[c.b].raw.at[t]).start()
            return

        @pl.when(outer)
        def _():
            pl.semaphore_wait(credit, 1)
            to_near(c).start()

    def stage_near(c):
        @pl.when(jnp.logical_not(outer))
        def _():
            to_near(c).wait_recv()
            added(mine(c), mine(c), from_near(c))
            pl.semaphore_wait(credit, 1)
            to_cross(c).start()

    def stage_cross(c):
        @pl.when(jnp.logical_not(outer))
        def _():
            to_cross(c).wait_recv()
            total = work[c.b].from_partner
            added(span(total, c), mine(c), from_cross(c))
            total_to_near(c).start()
            out_copy(c, total).start()

    def stage_total(c):
        @pl.when(outer)
        def _():
            total_to_near(c).wait_recv()
            out_copy(c, work[c.b].from_sibling.at[0]).start()

    def first_copies():
        for c in chunks[:ahead]:
            stage_sibling(c)
            to_partner(c).start()

    def turn_operands():
        wait(loads[0].low, loads[0].act)
        work[0].lowT[...] = views[0].low[...].T

    def feed_products():
        own, w = views[0], work[0]

        @pl.loop(0, up_count)
        def _(k):
            rows = pl.ds(pl.multiple_of(k * step, step), step)
            for q in range(tensors):
                w.raw[q, pl.ds(pl.multiple_of(up_first + k * step, 16), step), :] = dot(
                    w.lowT[rows, :], own.slope[q]
                ).astype(BF)
            send_to_sibling(feed_chunk(k))

        first_copies()

        @pl.loop(0, down_count)
        def _(k):
            lanes = pl.ds(pl.multiple_of(k * step, step), step)
            for q in range(tensors):
                w.raw[q, pl.ds(pl.multiple_of(down_first + k * step, 16), step), :] = dot(
                    own.act[q, :, lanes].T, w.gf[...]
                ).astype(BF)
            send_to_sibling(feed_chunk(up_count + k))

    def later_product(c):
        own, w = views[c.b], work[c.b]
        for q in range(tensors):
            for i in range(MATRICES):
                first = max(c.first, starts[c.b][i])
                last = min(c.first + c.rows, starts[c.b][i + 1])
                if first >= last:
                    continue
                rows = slice(first - starts[c.b][i], last - starts[c.b][i])
                if i == 0:
                    value = dot(own.qkv[q, rows, :], own.x[...])
                elif i == 1:
                    value = dot(own.ctx[q, rows, :], w.ga[...])
                elif i == 2:
                    value = dot(w.lowT[rows, :], own.slope[q])
                else:
                    value = dot(own.act[q, :, rows].T, w.gf[...])
                w.raw[q, first:last, :] = value.astype(BF)
        send_to_sibling(c)

    @pl.when(section == 1)
    def _():
        wait(*cot_copies)
        work[1].g[...] = flipped[...].T

    for b in range(2):
        work[b].sums[...] = jnp.zeros(work[b].sums.shape, F32)
    roots_copy.wait()

    def feed_back(n, block):
        for b in (1, 0):
            own, own_in, w, gain = views[b], loads[b], work[b], gains[b]
            if n == 0:
                wait(own_in.n2)

            if block in blocks:
                hop(b, n).wait_recv()

            for rows in small_blocks(block):
                g, normed = w.g[rows].astype(F32), own.n2[rows].astype(F32)
                low = norm_rows_back(g, normed, roots[rows, 2 * b + 1 : 2 * b + 2], gain[1:2])
                w.dz[rows] = low
                w.gf[rows] = low.astype(BF)
                w.sums[1:2] += jnp.sum(g * normed, axis=0, keepdims=True)
                w.sums[3:4] += jnp.sum(g, axis=0, keepdims=True)

            if n == 0:
                wait(own_in.downward, own_in.slope, own_in.upward)

            @pl.loop(0, tensors)
            def _(q):
                d_act = dot(w.gf[block], own.downward[q])
                d_pre = (d_act * own.slope[q, block].astype(F32)).astype(BF)
                own.slope[q, block] = d_pre
                w.dz[block] += dot(d_pre, own.upward[q])

            if n == 0:
                wait(own_in.n1, own_in.outward)
            for rows in small_blocks(block):
                g, normed = w.dz[rows], own.n1[rows].astype(F32)
                low = norm_rows_back(g, normed, roots[rows, 2 * b : 2 * b + 1], gain[0:1])
                w.dz[rows] = low
                w.ga[rows] = low.astype(BF)
                w.sums[0:1] += jnp.sum(g * normed, axis=0, keepdims=True)
                w.sums[2:3] += jnp.sum(g, axis=0, keepdims=True)
            gaT = w.ga[block].T
            for q in range(tensors):
                w.dctx[q, :, block] = dot(own.outward[q], gaT).astype(BF)

    @pl.when(section == 0)
    def _():
        turn_operands()
        for n, block in enumerate(blocks):
            feed_back(n, block)

    @pl.when(section == 1)
    def _():
        feed_back(0, slice(0, length))

    @pl.when(section == 0)
    def _():
        feed_products()

    for own_in in loads:
        wait(own_in.qkv, own_in.ctx, own_in.inv)
    wait(probs_copy)
    qkv = (views[0].qkv, views[1].qkv)
    text_rows, layout_rows = slice(0, HEAD_TEXT), slice(HEAD_TEXT, HEAD_TEXT + HEAD_LAYOUT)

    def turn(k, n_known):
        fixed = isinstance(k, int)

        def at(i, stage):
            if not fixed:
                pl.when((i >= 0) & (i < n_feed))(lambda: stage(feed_chunk(i)))
            elif 0 <= i < n_known:
                stage(chunks[i])

        def sibling_and_send(c):
            stage_sibling(c)
            to_partner(c).start()

        at(k + ahead, sibling_and_send)
        at(k, stage_partner)
        if chain:
            at(k - 2, stage_near)
            at(k - 4, stage_cross)
            at(k - 6, stage_total)

    early_turns = 6

    @pl.loop(0, tensors)
    def _(q):
        for local in range(local_heads):
            head = q * local_heads + local

            @pl.when((section == 0) & (head % 2 == 0) & (head < 2 * early_turns))
            def _():
                turn(head // 2, n_feed)

            inv = views[0].inv[q, local : local + 1, :]
            scaled = [
                (work[s].dctx[q, local * SIZES[s] : (local + 1) * SIZES[s], :].astype(F32) * inv).astype(BF)
                for s in range(2)
            ]
            inner = [
                jnp.sum(
                    scaled[s].astype(F32)
                    * views[s].ctx[q, local * SIZES[s] : (local + 1) * SIZES[s], :].astype(F32),
                    axis=0, keepdims=True,
                )
                for s in range(2)
            ]
            rows16 = lax.broadcasted_iota(jnp.int32, (16, length), 0)
            extra = jnp.zeros((16, length), F32)
            for i, value in enumerate((inner[0] + inner[1], inner[1])):
                high = value.astype(BF).astype(F32)
                extra = jnp.where(rows16 == 2 * i, -high, extra)
                extra = jnp.where(rows16 == 2 * i + 1, high - value, extra)
            pad = jnp.zeros((128 - sum(SIZES) - 16, length), BF)
            dcT = jnp.concatenate([*scaled, extra.astype(BF), pad], axis=0)
            dc = dcT.T
            qT, kT = (head_rows(qkv, q, kind, local, SCALES if kind == 0 else None) for kind in range(2))
            v_text, v_layout = (head_part(qkv, q, 2, local, s) for s in range(2))
            one, other_one = (((rows16 // 2) == i).astype(F32).astype(BF) for i in range(2))
            low = probs_in[q, local]
            probs = low.astype(F32)
            both = dot(dc, jnp.concatenate([v_text, v_layout, one, pad], axis=0))
            ds_both = (probs * both).astype(BF)
            single = dot(dc, jnp.concatenate([jnp.zeros_like(v_text), v_layout, other_one, pad], axis=0))
            ds_layout = (probs * single).astype(BF)
            dvT = dot(dcT, low)
            put_head(qkv, q, 2, local, 0, dvT[text_rows])
            put_head(qkv, q, 2, local, 1, dvT[layout_rows])
            k = kT.T
            lane = lax.broadcasted_iota(jnp.int32, (length, 128), 1)
            dq = jnp.where(lane < HEAD_TEXT, dot(ds_both, k) * SCALES[0], dot(ds_layout, k) * SCALES[1])
            dqT = dq.astype(BF).T
            put_head(qkv, q, 0, local, 0, dqT[text_rows])
            put_head(qkv, q, 0, local, 1, dqT[layout_rows])
            put_head(qkv, q, 1, local, 0, dot(qT[text_rows], ds_both))
            put_head(qkv, q, 1, local, 1, dot(qT[layout_rows], ds_layout))

    wait(loads[0].project, loads[1].project)
    page_sum = jnp.zeros((1, work[0].dz.shape[1]), F32)
    for n, block in enumerate(blocks):
        for b in (1, 0):
            down = work[b].dz[block]
            for q in range(tensors):
                down += dot(qkv[b][q, :, block].T, views[b].project[q])
            down = down.astype(BF)
            work[b].g[block] = down
            if b == 0:
                page_sum += jnp.sum(down.astype(F32), axis=0, keepdims=True)

            @pl.when(section == 1)
            def _():
                hop(b, n).start()

    wait(loads[1].low, loads[1].act)
    work[1].lowT[...] = views[1].low[...].T
    for own_in in loads:
        wait(own_in.x)
    @pl.when(section == 1)
    def _():
        turn_operands()
        feed_products()

    for c in chunks[n_feed:]:
        later_product(c)

    @pl.when(section == 0)
    def _():
        flipped[...] = work[1].g[...].T
        each_page(0, page_start)

    at_page = (lax.broadcasted_iota(jnp.int32, lang_ids.shape, 0) == t % 2) & (
        lax.broadcasted_iota(jnp.int32, lang_ids.shape, 1) == t // 2
    )
    group = jnp.sum(jnp.where(at_page, lang_ids[...], 0), axis=(0, 1), keepdims=True)
    n_lang = small_out.shape[1] - 8
    chosen = (lax.broadcasted_iota(jnp.int32, (n_lang, 1), 0) == group) & (section == 0)
    small_sum[0, 0:n_lang] = jnp.where(chosen, page_sum, 0.0)
    small_sum[0, n_lang : n_lang + 4] = work[0].sums[...]
    small_sum[0, n_lang + 4 : n_lang + 8] = jnp.zeros((4, small_out.shape[2]), F32)
    small_sum[0, n_lang + 4 : n_lang + 8, : work[1].sums.shape[1]] = work[1].sums[...]

    def small_copy(i, device):
        return remote(small_sum.at[i], small_got.at[i], small_send.at[i], small_recv.at[i], device)

    if chain:
        small_copy(0, sibling).start()
    @pl.when(section == 1)
    def _():
        @pl.loop(0, early_turns)
        def _(k):
            turn(k, n_feed)

    for k in range(early_turns, len(chunks) + (6 if chain else 0)):
        turn(k, len(chunks))
        if not chain:
            continue
        if k == early_turns:
            small_copy(0, sibling).wait_recv()
            small_sum[1] = small_sum[0] + small_got[0]
            small_copy(1, partner).start()
        if k == early_turns + 1:
            small_copy(1, partner).wait_recv()
            small_sum[2] = small_sum[1] + small_got[1]
            small_copy(2, near).start()
        if k == early_turns + 2:
            small_copy(2, near).wait_recv()
            small_sum[3] = small_sum[2] + small_got[2]

            @pl.when(jnp.logical_not(outer))
            def _():
                small_copy(3, cross).start()

        if k == early_turns + 4:
            @pl.when(jnp.logical_not(outer))
            def _():
                small_copy(3, cross).wait_recv()
                small_sum[4] = small_sum[3] + small_got[3]
                small_copy(4, near).start()

        if k == early_turns + 6:
            @pl.when(outer)
            def _():
                small_copy(4, near).wait_recv()
                small_sum[4] = small_got[4]

            small_sum[5] = small_sum[4]
            small_copy(5, other).start()

    if chain:
        for i, device in enumerate((sibling, partner, near)):
            small_copy(i, device).wait_send()

        @pl.when(jnp.logical_not(outer))
        def _():
            small_copy(3, cross).wait_send()
            small_copy(4, near).wait_send()

        small_copy(5, other).wait()
        small_out[0] = small_sum[5]
        small_out[1] = small_got[5]
    else:
        small_out[0] = small_sum[0]
        small_out[1] = small_sum[0]

    @pl.when(section == 1)
    def _():
        for b in range(2):
            for n in range(len(blocks)):
                hop(b, n).wait_send()

    for c in chunks:
        for j in range(tensors // 2):
            to_sibling(c, j).wait_send()
        to_partner(c).wait_send()
        if not chain:
            out_copy(c, work[c.b].from_partner).wait()
            continue

        @pl.when(outer)
        def _():
            to_near(c).wait_send()

        @pl.when(jnp.logical_not(outer))
        def _():
            to_cross(c).wait_send()
            total_to_near(c).wait_send()

        out_copy(c, work[c.b].from_partner).wait()

    for g in range(sections):
        each_page(g, page_sent)
        for a in range(2):
            for j in range(2):
                dst = kinds[g][a].at[j]
                remote(dst, dst, page_send.at[0, a], page_recv.at[g, a, j], partner).wait_recv()
    landed = (text_out, layout_out, grad_out, layout_grad_out)
    copies = [pltpu.make_async_copy(v, h, page_out_sem.at[i]) for i, (v, h) in enumerate(zip(landed, page_outs))]
    start(*copies)
    wait(*copies)


def layer_backward(mesh, x, y, probs, roots, kept, weights, cots, norms, lang_ids, n_lang):
    sections, dp, tensors = mesh.shape["section"], mesh.shape["dp"], mesh.shape["tensor"]
    chain = dp == 4
    needed = tuple(
        Needed(
            n2=k.n2, downward=w.downward, slope=k.slope, upward=w.upward, n1=k.n1,
            outward=w.outward, low=k.low, act=k.act, qkv=k.qkv, ctx=k.ctx, inv=k.inv, project=w.project, x=rows,
        )
        for k, w, rows in zip(kept, weights, x)
    )
    flat_in, in_tree = jax.tree.flatten((needed, probs, roots))
    plain = [v for own in needed for name, v in own._asdict().items() if name not in Weights._fields] + [probs, roots]
    stacks = [(matrix_starts(own)[MATRICES], rows.shape[1]) for own, rows in zip(needed, x)]
    length = x[0].shape[0]
    work = []
    for own, rows, (count, width) in zip(needed, x, stacks):
        work += Work(
            g=shape(rows.shape), gf=shape(rows.shape), ga=shape(rows.shape), dz=shape(rows.shape, F32),
            dctx=shape(own.ctx.shape), sums=shape((4, width), F32), lowT=shape((width, length)),
            raw=shape((tensors, count, width)), from_sibling=shape((tensors // 2, count, width)),
            from_partner=shape((count, width)),
        )
    small = shape((2, n_lang + 8, x[0].shape[1]), F32)
    text_page = shape((2, length // tensors, x[0].shape[1]))
    layout_page = shape((2, x[1].shape[1], length // tensors))
    summed = [shape(s) for s in stacks]
    own = needed[0]
    n_feed = (own.upward.shape[1] + own.downward.shape[1]) // ROWS
    n_chunks = n_feed + 1 + own.project.shape[1] // 192 + own.outward.shape[1] // 64
    n_blocks = len(hop_blocks(length))
    dma = pltpu.SemaphoreType.DMA
    results = pl.pallas_call(
        functools.partial(backward_kernel, sections, tensors, chain, in_tree),
        out_shape=summed + [small, text_page, layout_page, text_page, layout_page],
        in_specs=[ANY] * (len(flat_in) + 4) + [VMEM] * 3,
        out_specs=[ANY] * 2 + [VMEM] + [ANY] * 4,
        scratch_shapes=vmem_like(work) + vmem_like(plain)
        + [pltpu.VMEM(cots[1].shape, BF)] + [pltpu.VMEM((6,) + small.shape[1:], F32)] * 2
        + vmem_like([text_page, layout_page] * 2)
        + [dma((len(flat_in),)), dma((2,)), dma((2, n_blocks)), dma((2, n_blocks))]
        + [dma((n_chunks, tensors // 2))] * 2 + [dma((4, n_chunks))] * 2
        + [pltpu.SemaphoreType.REGULAR, dma((n_chunks,))]
        + [dma((6,))] * 2 + [dma((tensors, 2)), dma((sections, 2, 2)), dma((4,))],
        compiler_params=pltpu.CompilerParams(
            collective_id=1, has_side_effects=True, vmem_limit_bytes=64 << 20
        ),
        name="layer_backward",
    )(*flat_in, *cots, *y, lang_ids, norms[0][0], norms[1][0])
    totals, small, pages = results[:2], results[2], results[3:7]
    if not chain:
        totals = lax.psum(tuple(totals), "dp")
        both = lax.psum(small[0], ("dp", "tensor"))
        small = jnp.stack([both, lax.ppermute(both, "section", [(0, 1), (1, 0)])])
    return totals, small, pages


def widen_kernel(n_in, n_pages, *refs):
    n_out = 5 + n_pages + 2 * MATRICES
    hbm_in, hbm_out = refs[:n_in], refs[n_in : n_in + n_out]
    vmem_in, vmem_out = refs[n_in + n_out : 2 * n_in + n_out], refs[2 * n_in + n_out : -2]
    in_sem, out_sem = refs[-2:]
    loads = [pltpu.make_async_copy(h, v, in_sem.at[i]) for i, (h, v) in enumerate(zip(hbm_in, vmem_in))]
    sources = vmem_out[:5] + vmem_in[3:] + vmem_out[5:]
    stores = [pltpu.make_async_copy(v, h, out_sem.at[i]) for i, (v, h) in enumerate(zip(sources, hbm_out))]
    start(*loads)
    totals, small = vmem_in[0:2], vmem_in[2]
    for b in range(2):
        wait(loads[b])
        at = 0
        for i in range(b * MATRICES, (b + 1) * MATRICES):
            out = vmem_out[5 + i]
            for c in range(0, out.shape[0], 48):
                out[c : c + 48] = totals[b][at + c : at + c + 48].astype(F32)
            at += out.shape[0]
            stores[5 + n_pages + i].start()
    for i in range(n_pages):
        loads[3 + i].wait()
        stores[5 + i].start()
    loads[2].wait()
    n_lang = vmem_out[0].shape[0]
    vmem_out[0][...] = jnp.where(lax.axis_index("section") == 0, small[0, :n_lang], small[1, :n_lang])
    for i, out in enumerate(vmem_out[1:5]):
        first = n_lang + 2 * i
        out[...] = small[0, first : first + 2, : out.shape[1]]
    start(*stores[:5])
    wait(*stores)


def widen(totals, small, pages, shards, n_lang):
    widths = [total.shape[1] for total in totals]
    sums = [shape((n_lang, widths[0]), F32)] + [shape((2, w), F32) for w in widths for _ in range(2)]
    grads = [shape(m.shape, F32) for own in shards for m in own]
    inputs = (*totals, small, *pages)
    outs = sums + [shape(page.shape) for page in pages] + grads
    results = pl.pallas_call(
        functools.partial(widen_kernel, len(inputs), len(pages)), out_shape=outs,
        in_specs=[ANY] * len(inputs), out_specs=[ANY] * len(outs),
        scratch_shapes=vmem_like(inputs) + vmem_like(sums + grads)
        + [pltpu.SemaphoreType.DMA((len(inputs),)), pltpu.SemaphoreType.DMA((len(outs),))],
        compiler_params=pltpu.CompilerParams(vmem_limit_bytes=62 << 20), name="widen",
    )(*inputs)
    return results[0], results[1:5], results[5:9], results[9:13], results[13:17]


def per_device(
    mesh,
    text_input,
    layout_input,
    text_cotangent,
    layout_cotangent,
    page_counts,
    pad_mask,
    lang_ids,
    lang_table,
    text_project,
    text_outward,
    text_upward,
    text_downward,
    text_gains,
    text_biases,
    layout_project,
    layout_outward,
    layout_upward,
    layout_downward,
    layout_gains,
    layout_biases,
):
    def flat(project):
        return jnp.transpose(project[0], (1, 2, 0)).reshape(-1, project.shape[1])

    def flipped(block):
        return jnp.transpose(block[0], (0, 2, 1))

    shards = (
        Weights(flat(text_project), text_outward[0], text_upward[0], text_downward[0]),
        Weights(flat(layout_project), layout_outward[0], layout_upward[0], layout_downward[0]),
    )
    norms = ((text_gains[0], text_biases[0]), (layout_gains[0], layout_biases[0]))
    marks = (pad_mask, page_counts, lang_ids, lang_table)
    (x, y, probs, roots, kept, weights), cots = layer_forward(
        mesh, text_input[0], flipped(layout_input), text_cotangent[0], flipped(layout_cotangent), shards, norms, marks
    )
    n_lang = lang_table.shape[0]
    totals, small, pages = layer_backward(mesh, x, y, probs, roots, kept, weights, cots, norms, lang_ids, n_lang)
    lang_sum, norm_sums, pages, text_sums, layout_sums = widen(totals, small, pages, shards, n_lang)
    text_out, layout_out, text_grad, layout_grad = pages

    def unflat(grad, like):
        return jnp.transpose(grad.reshape(like.shape[2], like.shape[3], like.shape[1]), (2, 0, 1))[None]

    unflip = lambda block: jnp.transpose(block, (0, 2, 1))[None]
    return (
        text_out[None], unflip(layout_out), text_grad[None], unflip(layout_grad), lang_sum,
        unflat(text_sums[0], text_project), *(s[None] for s in text_sums[1:]), norm_sums[0][None], norm_sums[1][None],
        unflat(layout_sums[0], layout_project), *(s[None] for s in layout_sums[1:]),
        norm_sums[2][None], norm_sums[3][None],
    )


def solution(mesh):
    tokens = P("section", "dp", "tensor", None)
    weight_specs = (
        P("section", None, None, "tensor"), P("section", "tensor", None), P("section", None, "tensor"),
        P("section", "tensor", None), P("section", None, None), P("section", None, None),
    )
    in_specs = (tokens,) * 4 + (P(None, "dp"), P(None, "dp", None), P(None, "dp"), P()) + weight_specs * 2
    out_specs = (tokens,) * 4 + (P(),) + weight_specs * 2
    return jax.shard_map(
        functools.partial(per_device, mesh), mesh=mesh, in_specs=in_specs, out_specs=out_specs, check_vma=False
    )
```

```python
import functools
import math
import typing

import jax
import jax.numpy as jnp
from jax import lax
from jax.experimental import pallas as pl
from jax.experimental.pallas import tpu as pltpu
from jax.sharding import PartitionSpec as P

HEAD_TEXT = 64
HEAD_LAYOUT = 16
EPSILON = 1e-05
NEGATIVE = -1e30
HIGH = lax.Precision.HIGHEST
MESH = pl.DeviceIdType.MESH
BF = jnp.bfloat16
F32 = jnp.float32
ANY = pl.BlockSpec(memory_space=pl.ANY)


def remote(src, dst, send, recv, device):
    return pltpu.make_async_remote_copy(
        src_ref=src, dst_ref=dst, send_sem=send, recv_sem=recv, device_id=device, device_id_type=MESH
    )


def greet(section, tensor, sections, tensors, extra=()):
    barrier = pltpu.get_barrier_semaphore()
    for g in range(sections):
        for q in range(tensors):

            @pl.when((section != g) | (tensor != q))
            def _():
                pl.semaphore_signal(
                    barrier, inc=1, device_id={"section": g, "tensor": q}, device_id_type=MESH
                )

    for device in extra:
        pl.semaphore_signal(barrier, inc=1, device_id=device, device_id_type=MESH)
    pl.semaphore_wait(barrier, sections * tensors - 1 + len(extra))


GELU_P = 0.3275911
GELU_A = (0.254829592, -0.284496736, 1.421413741, -1.453152027, 1.061405429)
NN = (((1,), (0,)), ((), ()))
NT = (((1,), (1,)), ((), ()))
SCALES = (1.0 / math.sqrt(HEAD_TEXT), 1.0 / math.sqrt(HEAD_LAYOUT))
SIZES = (HEAD_TEXT, HEAD_LAYOUT)
ROWS = 128


class Weights(typing.NamedTuple):
    project: typing.Any
    outward: typing.Any
    upward: typing.Any
    downward: typing.Any


class Kept(typing.NamedTuple):
    qkv: typing.Any
    ctx: typing.Any
    inv: typing.Any
    n1: typing.Any
    low: typing.Any
    act: typing.Any
    slope: typing.Any
    n2: typing.Any


def dot(a, b, dims=NN):
    return lax.dot_general(a, b, dims, preferred_element_type=F32)


def gelu_pair(u):
    d = 1.0 + (GELU_P / math.sqrt(2.0)) * jnp.abs(u)
    t = pl.reciprocal(d, approx=True)
    t = t * (2.0 - d * t)
    e = jnp.exp2((u * u) * (-0.5 / math.log(2.0)))
    a1, a2, a3, a4, a5 = (0.5 * a for a in GELU_A)
    tail = ((((a5 * t + a4) * t + a3) * t + a2) * t + a1) * t * e
    cdf = jnp.where(u >= 0, 1.0 - tail, tail)
    return u * cdf, cdf + u * e * (1.0 / math.sqrt(2.0 * math.pi))


def norm_rows(z, gain, offset):
    center = z - jnp.mean(z, axis=-1, keepdims=True)
    inverse = lax.rsqrt(jnp.mean(center * center, axis=-1, keepdims=True) + EPSILON)
    normed = center * inverse
    return normed * gain + offset, normed, inverse


def norm_rows_back(g, n, r, gain):
    t = g * gain
    return r * (t - jnp.mean(t, axis=-1, keepdims=True) - n * jnp.mean(t * n, axis=-1, keepdims=True))


class Staged:
    def __init__(self, tree, hbm, vmem, sem, inward):
        self.tree, self.vmem = tree, list(vmem)
        pairs = zip(hbm, vmem) if inward else zip(vmem, hbm)
        self.copies = [pltpu.make_async_copy(a, b, sem.at[i]) for i, (a, b) in enumerate(pairs)]

    def refs(self):
        return jax.tree.unflatten(self.tree, self.vmem)

    def parts(self):
        return jax.tree.unflatten(self.tree, self.copies)

    def start(self):
        for copy in self.copies:
            copy.start()

    def wait(self):
        for copy in self.copies:
            copy.wait()


def start(*copies):
    for copy in copies:
        copy.start()


def wait(*copies):
    for copy in copies:
        copy.wait()


def head_rows(stacks, slot, kind, local, scales=None, extra=None):
    rows = []
    for b in range(2):
        piece = head_part(stacks, slot, kind, local, b)
        rows.append(piece if scales is None else piece * BF(scales[b]))
    length = rows[0].shape[1]
    rows.append(jnp.zeros((16, length), BF) if extra is None else extra)
    rows.append(jnp.zeros((128 - sum(SIZES) - 16, length), BF))
    return jnp.concatenate(rows, axis=0)


def head_part(stacks, slot, kind, local, b):
    first = kind * (stacks[b].shape[1] // 3) + local * SIZES[b]
    return stacks[b][slot, first : first + SIZES[b], :]


def small_blocks(block, step=64):
    return [slice(c, c + step) for c in range(block.start, block.stop, step)]


def put_head(stacks, slot, kind, local, b, value):
    first = kind * (stacks[b].shape[1] // 3) + local * SIZES[b]
    stacks[b][slot, first : first + SIZES[b], :] = value.astype(BF)


def hop_blocks(length):
    ends = [0, length // 2, length * 3 // 4, length]
    return [slice(a, b) for a, b in zip(ends, ends[1:])]


def slot_of(u, core, chip):
    return ((chip + u // 2) % 2) * 2 + (core + u % 2) % 2


def forward_kernel(sections, tensors, shared, in_tree, out_tree, *refs):
    n_w, n_out = len(shared), out_tree.num_leaves
    sources = (refs[0:2], refs[2:4])
    shards = refs[4 : 4 + n_w]
    pad_mask, counts, lang_ids, lang_table, *norms = refs[4 + n_w : 12 + n_w]
    rest = refs[12 + n_w :]
    hbm_out, cots_out, rest = rest[:n_out], rest[n_out : n_out + 2], rest[n_out + 2 :]
    outgoing = Staged(out_tree, hbm_out, rest[:n_out], rest[n_out], False)
    rest = rest[n_out + 1 :]
    flipped, raw_x, y_narrow, *rest = rest
    nats, totals, pre, score_buffer, rest = rest[0:2], rest[2:4], rest[4:6], rest[6], rest[7:]
    xT, turned, turn_sem, rest = rest[0:2], (rest[2:4], rest[4:6]), rest[6], rest[7:]
    page_send, page_recv, w_send, w_recv, own_sem, hop_send, hop_recv, cot_sem, act_sem = rest
    x, y_pages, probs_out, roots, kept, weights = outgoing.refs()
    y = (y_pages[0], y_narrow)
    x_out, y_out, probs_copy, roots_copy, kept_out, weights_out = outgoing.parts()
    kept_hbm, weights_hbm = jax.tree.unflatten(out_tree, list(hbm_out))[4:6]
    section, d, t = lax.axis_index("section"), lax.axis_index("dp"), lax.axis_index("tensor")
    core, chip, half_index = t % 2, t // 2, d % 2
    sibling, partner = t + 1 - 2 * core, (t + tensors // 2) % tensors
    mate = d + 1 - 2 * half_index
    micro, page = core, chip
    part_length = sources[0][0].shape[1]
    length = x[0].shape[0]
    blocks = [slice(c, c + 2 * ROWS) for c in range(0, length, 2 * ROWS)]
    parts = hop_blocks(length)
    full = (
        weights[0].project, weights[1].project, weights[0].outward, weights[0].upward,
        weights[0].downward, weights[1].outward, weights[1].upward, weights[1].downward,
    )
    greet(section, t, sections, tensors, ({"dp": mate},) if any(shared) else ())

    pieces = []
    for i in range(n_w):
        count = shards[i].shape[0] // 2
        n_parts = 2 if shared[i] and count % 64 == 0 else 1
        pieces += [(i, s * (count // n_parts), count // n_parts) for s in range(n_parts)]

    def rows_of(ref, p, which):
        i, first, count = pieces[p]
        if not shared[i]:
            return ref
        return ref.at[pl.ds(pl.multiple_of(which * (shards[i].shape[0] // 2) + first, 16), count)]

    def pieces_of_matrix(i):
        return [p for p in range(len(pieces)) if pieces[p][0] == i]

    def to_partner(p):
        i = pieces[p][0]
        return remote(
            rows_of(shards[i], p, half_index), rows_of(full[i].at[t], p, half_index),
            w_send.at[0, p], w_recv.at[0, p], {"tensor": partner},
        )

    def to_sibling(i):
        return remote(full[i].at[t], full[i].at[t], w_send.at[1, i], w_recv.at[1, i], {"tensor": sibling})

    def to_mate(p):
        ref = rows_of(full[pieces[p][0]].at[partner], p, half_index)
        return remote(ref, ref, w_send.at[2, p], w_recv.at[2, p], {"dp": mate})

    def on_first(p):
        ref = rows_of(full[pieces[p][0]].at[partner], p, half_index)
        return remote(ref, ref, w_send.at[3, p], w_recv.at[3, p], {"tensor": sibling})

    def on_second(p):
        ref = rows_of(full[pieces[p][0]].at[partner], p, 1 - half_index)
        return remote(ref, ref, w_send.at[4, p], w_recv.at[4, p], {"tensor": sibling})

    def keep(i):
        return pltpu.make_async_copy(shards[i], full[i].at[t], own_sem.at[i])

    def relay_piece(p):
        to_partner(p).wait_recv()
        if shared[pieces[p][0]]:
            to_mate(p).start()
        on_first(p).start()

    def relay(*which):
        for i in which:
            for p in pieces_of_matrix(i):
                relay_piece(p)

    def relay_second(*which):
        for i in which:
            for p in pieces_of_matrix(i):
                if shared[i]:
                    to_mate(p).wait_recv()
                    on_second(p).start()

    def early(*which):
        for i in which:
            to_sibling(i).wait_recv()

    def late(*which):
        for i in which:
            for p in pieces_of_matrix(i):
                on_first(p).wait_recv()
                if shared[i]:
                    on_second(p).wait_recv()

    def token_slot(g, a, index):
        start_at = pl.multiple_of(index * part_length, part_length)
        target = (raw_x, flipped)[a]
        return target.at[pl.ds(start_at, part_length)] if a == 0 else target.at[:, pl.ds(start_at, part_length)]

    def over_pages(g, act):
        for j in range(2):
            target = 2 * j + section
            here = (section == g) & (t == target)
            for a in range(2):
                act(g, j, a, target, here)

    def page_copy(g, j, a, target):
        return remote(
            sources[g][a].at[j], token_slot(g, a, t), page_send.at[g, j, a], page_recv.at[a, t],
            {"section": g, "tensor": target},
        )

    def page_start(g, j, a, target, here):
        @pl.when(here)
        def _():
            pltpu.make_async_copy(sources[g][a].at[j], token_slot(g, a, t), page_recv.at[a, t]).start()

        @pl.when(jnp.logical_not(here))
        def _():
            page_copy(g, j, a, target).start()

    def page_sent(g, j, a, target, here):
        @pl.when(jnp.logical_not(here))
        def _():
            page_copy(g, j, a, target).wait_send()

    def pages_arrived(g):
        for a in range(2):
            for q in range(tensors):
                slot = token_slot(g, a, q)
                remote(slot, slot, page_send.at[0, 0, a], page_recv.at[a, q], {"tensor": sibling}).wait_recv()

    def hop(b, n):
        return remote(
            y[b].at[parts[n]], x[b].at[parts[n]], hop_send.at[b, n], hop_recv.at[b, n], {"section": 1 - section}
        )

    def weights_to_hbm():
        for b in range(2):
            start(weights_out[b].project, weights_out[b].outward)
            for q in range(tensors):
                for m, name in enumerate((2, 3)):
                    copy = pltpu.make_async_copy(
                        turned[b][m].at[q % 2], weights_hbm[b][name].at[q], turn_sem.at[b, m, q % 2]
                    )
                    if q >= 2:
                        copy.wait()
                    turned[b][m][q % 2] = weights[b][name][q].T
                    copy.start()
        for b in range(2):
            for q in range(tensors - 2, tensors):
                for m, name in enumerate((2, 3)):
                    pltpu.make_async_copy(
                        turned[b][m].at[q % 2], weights_hbm[b][name].at[q], turn_sem.at[b, m, q % 2]
                    ).wait()

    over_pages(0, page_start)
    for i in range(n_w):
        keep(i).start()
    for p in range(len(pieces)):
        to_partner(p).start()
    over_pages(1, page_start)
    for i in range(n_w):
        keep(i).wait()
        to_sibling(i).start()

    at_page = (lax.broadcasted_iota(jnp.int32, counts.shape, 0) == micro) & (
        lax.broadcasted_iota(jnp.int32, counts.shape, 1) == page
    )

    def own_entry(ref):
        return jnp.sum(jnp.where(at_page, ref[...], 0), axis=(0, 1), keepdims=True)

    positions = lax.broadcasted_iota(jnp.int32, (1, length), 1)
    mask_row = pad_mask[micro, pl.ds(page, 1), :]
    key_mask = (positions < own_entry(counts)) & ((mask_row == 1) | (positions == 0))
    first_row = (lax.broadcasted_iota(jnp.int32, (16, length), 0) == 0).astype(F32)
    mask_row16 = (first_row * jnp.where(key_mask, 0.0, NEGATIVE)).astype(BF)
    groups = lax.broadcasted_iota(jnp.int32, (lang_table.shape[0], 1), 0)
    lang_row = jnp.sum(jnp.where(groups == own_entry(lang_ids), lang_table[...], 0.0), axis=0, keepdims=True)
    local_heads = weights[0].project.shape[1] // (3 * HEAD_TEXT)
    qkv = (kept[0].qkv, kept[1].qkv)

    @pl.when(section == 0)
    def _():
        pages_arrived(0)
        x[0][...] = (raw_x[...].astype(F32) + lang_row).astype(BF)
        x[1][...] = flipped[...].T
        early(0, 1)

    @pl.when(section == 1)
    def _():
        relay(*range(n_w))
        relay_second(*range(n_w))
        early(*range(n_w))
        late(*range(n_w))
        weights_to_hbm()

    @pl.loop(0, 2)
    def _(half):
        @pl.when((half == 1) & (section == 0))
        def _():
            relay(0, 1)
            relay_second(0)
            late(0, 1)

        for b in range(2):
            for n, block in enumerate(parts):
                @pl.when((half == 0) & (section == 1))
                def _():
                    hop(b, n).wait_recv()

                @pl.when(half == 0)
                def _():
                    xT[b][:, block] = x[b][block].T

                @pl.loop(0, 2)
                def _(u):
                    slot = slot_of(2 * half + u, core, chip)
                    qkv[b][slot, :, block] = dot(weights[b].project[slot], xT[b][:, block]).astype(BF)

        @pl.loop(0, 2)
        def _(u):
            @pl.when((half == 1) & (u == 1) & (section == 0))
            def _():
                relay(2)
                relay_piece(pieces_of_matrix(3)[0])

            slot = slot_of(2 * half + u, core, chip)
            for local in range(local_heads):
                q = head_rows(qkv, slot, 0, local, SCALES, first_row.astype(BF)).T
                kT = head_rows(qkv, slot, 1, local, None, mask_row16)
                score_buffer[local] = dot(q, kT)
                for rows in small_blocks(slice(0, length)):
                    scores = score_buffer[local, rows, :]
                    raised = jnp.exp(scores - jnp.max(scores, axis=-1, keepdims=True))
                    probs_out[slot, local, rows, :] = raised.astype(BF)
                vT = head_rows(qkv, slot, 2, local, None, first_row.astype(BF))
                ctx = dot(probs_out[slot, local], vT.T).T
                inv = 1.0 / ctx[sum(SIZES) : sum(SIZES) + 1]
                ctx = (ctx * inv).astype(BF)
                kept[0].inv[slot, local : local + 1, :] = inv
                kept[0].ctx[slot, local * HEAD_TEXT : (local + 1) * HEAD_TEXT, :] = ctx[:HEAD_TEXT]
                kept[1].ctx[slot, local * HEAD_LAYOUT : (local + 1) * HEAD_LAYOUT, :] = ctx[
                    HEAD_TEXT : HEAD_TEXT + HEAD_LAYOUT
                ]

    kept[1].inv[...] = jnp.zeros(kept[1].inv.shape, F32)
    start(probs_copy, *x_out, *(c for k in kept_out for c in (k.qkv, k.ctx, k.inv)))

    def attend(b):
        gains, biases = norms[2 * b : 2 * b + 2]
        width = x[b].shape[1]
        nats[b][...] = kept[b].ctx[...].reshape(width, length).T
        wide = weights[b].outward[...].reshape(width, width)
        for block in blocks:
            totals[b][1, block] = dot(nats[b][block], wide)
            for rows in small_blocks(block):
                h, n, r = norm_rows(x[b][rows].astype(F32) + totals[b][1, rows], gains[0:1], biases[0:1])
                totals[b][0, rows] = h
                totals[b][1, rows] = jnp.zeros(h.shape, F32)
                kept[b].n1[rows] = n.astype(BF)
                roots[rows, 2 * b : 2 * b + 1] = r
                kept[b].low[rows] = h.astype(BF)
        start(kept_out[b].n1, kept_out[b].low)

    def slot_copies(b, slot):
        return [
            pltpu.make_async_copy(v.at[slot], h.at[slot], act_sem.at[b, m, slot])
            for m, (v, h) in enumerate(((kept[b].act, kept_hbm[b].act), (kept[b].slope, kept_hbm[b].slope)))
        ]

    def feed(b, first, which):
        @pl.loop(first, first + 2)
        def _(u):
            slot = slot_of(u, core, chip)
            for block in which:
                pre[b][block] = dot(kept[b].low[block], weights[b].upward[slot])
                for rows in small_blocks(block, 16):
                    act, slope = gelu_pair(pre[b][rows])
                    kept[b].act[slot, rows] = act.astype(BF)
                    kept[b].slope[slot, rows] = slope.astype(BF)
                totals[b][1, block] += dot(kept[b].act[slot, block], weights[b].downward[slot])
                if block == slice(0, length):
                    start(*slot_copies(b, slot))

    def finish(b):
        gains, biases = norms[2 * b : 2 * b + 2]
        def last(block):
            feed(b, 2, [block])
            for rows in small_blocks(block):
                out, normed, r = norm_rows(totals[b][0, rows] + totals[b][1, rows], gains[1:2], biases[1:2])
                y[b][rows] = out.astype(BF)
                kept[b].n2[rows] = normed.astype(BF)
                roots[rows, 2 * b + 1 : 2 * b + 2] = r

        @pl.when(section == 0)
        def _():
            for n, block in enumerate(parts):
                last(block)
                hop(b, n).start()
            for u in range(2, 4):
                start(*slot_copies(b, slot_of(u, core, chip)))

        @pl.when(section == 1)
        def _():
            last(slice(0, length))

        if b == 1:
            y_pages[1][...] = y_narrow[...].T
        start(y_out[b], kept_out[b].n2)

    def rest_of(i):
        for p in pieces_of_matrix(i)[1:]:
            relay_piece(p)

    @pl.when(section == 0)
    def _():
        relay_second(2)
        early(2)
        late(2)

    attend(0)

    @pl.when(section == 0)
    def _():
        rest_of(3)
        early(3, 4)

    feed(0, 0, [slice(0, length)])

    @pl.when(section == 0)
    def _():
        relay(4)
        relay_second(3, 4)
        late(3, 4)

    finish(0)

    @pl.when(section == 0)
    def _():
        relay(5, 6, 7)
        relay_second(5, 6, 7)
        early(5, 6, 7)
        late(5, 6, 7)

    attend(1)
    feed(1, 0, [slice(0, length)])
    finish(1)
    start(roots_copy)

    @pl.when(section == 0)
    def _():
        weights_to_hbm()
        for b in range(2):
            for n in range(len(parts)):
                hop(b, n).wait_send()

    for i in range(n_w):
        to_sibling(i).wait_send()
        for p in pieces_of_matrix(i):
            to_partner(p).wait_send()
            on_first(p).wait_send()
            if shared[i]:
                to_mate(p).wait_send()
                on_second(p).wait_send()
    for g in range(sections):
        over_pages(g, page_sent)

    @pl.when(section == 1)
    def _():
        pages_arrived(1)
        copies = [pltpu.make_async_copy(v, h, cot_sem.at[i]) for i, (v, h) in enumerate(zip((raw_x, flipped), cots_out))]
        start(*copies)
        wait(*copies)

    for group in (x_out, y_out, (probs_copy, roots_copy), *(w[:2] for w in weights_out)):
        wait(*group)
    for b, k in enumerate(kept_out):
        wait(k.qkv, k.ctx, k.inv, k.n1, k.low, k.n2)
        for slot in range(tensors):
            wait(*slot_copies(b, slot))


def vmem_like(tree):
    return [pltpu.VMEM(s.shape, s.dtype) for s in jax.tree.leaves(tree)]


VMEM = pl.BlockSpec(memory_space=pltpu.VMEM)


def shape(dims, dtype=BF):
    return jax.ShapeDtypeStruct(tuple(dims), dtype)


def layer_forward(mesh, text_in, layout_in, text_cot, layout_cot, shards, norms, marks):
    sections, dp, tensors = mesh.shape["section"], mesh.shape["dp"], mesh.shape["tensor"]
    length = text_in.shape[1] * tensors
    rows = (shape((length, text_in.shape[2])), shape((length, layout_in.shape[1])))
    local_heads = shards[0].project.shape[0] // (3 * HEAD_TEXT)
    kept = []
    for x, w in zip(rows, shards):
        units = shape((tensors, length, w.upward.shape[1]))
        kept.append(Kept(
            qkv=shape((tensors, w.project.shape[0], length)), ctx=shape((tensors, w.outward.shape[0], length)),
            inv=shape((tensors, local_heads, length), F32),
            n1=shape(x.shape), low=shape(x.shape), act=units, slope=units,
            n2=shape(x.shape),
        ))
    weights = tuple(Weights(*(shape((tensors,) + m.shape) for m in w)) for w in shards)
    pages_out = (rows[0], shape((rows[1].shape[1], length)))
    outs = (rows, pages_out, shape((tensors, local_heads, length, length)), shape((length, 4), F32), tuple(kept), weights)
    flat_out, out_tree = jax.tree.flatten(outs)
    (a, b) = shards
    ordered = (a.project, b.project, a.outward, a.upward, a.downward, b.outward, b.upward, b.downward)
    shared = tuple(dp % 2 == 0 and w.shape[0] % 32 == 0 and w.shape[1] >= 512 for w in ordered)
    n_w, n_pieces = len(ordered), 2 * len(ordered)
    cots = [rows[0], shape((rows[1].shape[1], length))]
    small = (*marks, *norms[0], *norms[1])
    results = pl.pallas_call(
        functools.partial(forward_kernel, sections, tensors, shared, None, out_tree),
        out_shape=flat_out + cots,
        in_specs=[ANY] * (4 + n_w) + [VMEM] * len(small),
        out_specs=[ANY] * (len(flat_out) + 2),
        scratch_shapes=vmem_like(flat_out) + [pltpu.SemaphoreType.DMA((len(flat_out),))]
        + [pltpu.VMEM(cots[1].shape, BF), pltpu.VMEM(cots[0].shape, BF), pltpu.VMEM(rows[1].shape, BF)]
        + [pltpu.VMEM(x.shape, BF) for x in rows]
        + [pltpu.VMEM((2,) + x.shape, F32) for x in rows]
        + [pltpu.VMEM((length, w.upward.shape[1]), F32) for w in shards]
        + [pltpu.VMEM((local_heads, length, length), F32)]
        + [pltpu.VMEM((x.shape[1], length), BF) for x in rows]
        + [pltpu.VMEM((2,) + m.shape, BF) for w in shards for m in (w.upward, w.downward)]
        + [pltpu.SemaphoreType.DMA((2, 2, 2))]
        + [
            pltpu.SemaphoreType.DMA((sections, 2, 2)), pltpu.SemaphoreType.DMA((2, tensors)),
            pltpu.SemaphoreType.DMA((5, n_pieces)), pltpu.SemaphoreType.DMA((5, n_pieces)), pltpu.SemaphoreType.DMA((n_w,)),
            pltpu.SemaphoreType.DMA((2, len(hop_blocks(length)))), pltpu.SemaphoreType.DMA((2, len(hop_blocks(length)))),
            pltpu.SemaphoreType.DMA((2,)), pltpu.SemaphoreType.DMA((2, 2, tensors)),
        ],
        compiler_params=pltpu.CompilerParams(
            collective_id=0, has_side_effects=True, vmem_limit_bytes=62 << 20
        ),
        name="layer_forward",
    )(text_in, layout_in, text_cot, layout_cot, *ordered, *small)
    return jax.tree.unflatten(out_tree, results[:-2]), tuple(results[-2:])


class Needed(typing.NamedTuple):
    n2: typing.Any
    downward: typing.Any
    slope: typing.Any
    upward: typing.Any
    n1: typing.Any
    outward: typing.Any
    low: typing.Any
    act: typing.Any
    qkv: typing.Any
    ctx: typing.Any
    inv: typing.Any
    project: typing.Any
    x: typing.Any


class Work(typing.NamedTuple):
    g: typing.Any
    gf: typing.Any
    ga: typing.Any
    dz: typing.Any
    dctx: typing.Any
    sums: typing.Any
    lowT: typing.Any
    raw: typing.Any
    from_sibling: typing.Any
    from_partner: typing.Any


class Chunk(typing.NamedTuple):
    b: typing.Any
    index: typing.Any
    first: typing.Any
    rows: typing.Any


MATRICES = 4


def matrix_rows(own):
    return own.project.shape[1], own.outward.shape[1], own.upward.shape[1], own.downward.shape[1]


def matrix_starts(own):
    sizes = matrix_rows(own)
    return [sum(sizes[:i]) for i in range(MATRICES + 1)]


def pieces_of(size, step):
    return [(f, step) for f in range(0, size, step)]


def backward_kernel(sections, tensors, chain, in_tree, *refs):
    n_in = in_tree.num_leaves
    hbm_in, refs = refs[:n_in], refs[n_in:]
    (cots, ys, lang_ids, gains), refs = (refs[0:2], refs[2:4], refs[4], refs[5:7]), refs[7:]
    results, small_out, page_outs, refs = refs[0:2], refs[2], refs[3:7], refs[7:]
    n_work = len(Work._fields)
    work, refs = (Work(*refs[:n_work]), Work(*refs[n_work : 2 * n_work])), refs[2 * n_work :]
    plain, refs = refs[: n_in - 2 * MATRICES], refs[n_in - 2 * MATRICES :]
    flipped, small_got, small_sum, refs = refs[0], refs[1], refs[2], refs[3:]
    text_out, layout_out, grad_out, layout_grad_out, *refs = refs
    in_sem, cot_sem, hop_send, hop_recv, sib_send, sib_recv, send, recv, credit, out_sem, *refs = refs
    small_send, small_recv, page_send, page_recv, page_out_sem = refs
    section, d, t = lax.axis_index("section"), lax.axis_index("dp"), lax.axis_index("tensor")
    core, chip = t % 2, t // 2
    sibling = {"tensor": t + 1 - 2 * core}
    partner = {"tensor": (t + tensors // 2) % tensors}
    near, cross = {"dp": d + 1 - 2 * (d % 2)}, {"dp": 3 - d}
    outer = (d == 0) | (d == 3)
    other = {"section": 1 - section}
    hbm, probs_hbm, roots_hbm = jax.tree.unflatten(in_tree, hbm_in)
    starts = [matrix_starts(own) for own in hbm]

    plain = list(plain)
    views = []
    for b in range(2):
        fields = {}
        for name, value in hbm[b]._asdict().items():
            if name in Weights._fields:
                i = Weights._fields.index(name)
                fields[name] = work[b].raw.at[:, pl.ds(starts[b][i], starts[b][i + 1] - starts[b][i])]
            else:
                fields[name] = plain.pop(0)
        views.append(Needed(**fields))
    probs_in, roots = plain
    flat_views = jax.tree.leaves((tuple(views), probs_in, roots))
    flat_copies = [pltpu.make_async_copy(a, v, in_sem.at[i]) for i, (a, v) in enumerate(zip(hbm_in, flat_views))]
    loads, probs_copy, roots_copy = jax.tree.unflatten(in_tree, flat_copies)
    length = work[0].gf.shape[0]
    local_heads = probs_in.shape[1]
    blocks = hop_blocks(length)
    cot_copies = (
        pltpu.make_async_copy(cots[0], work[0].g, cot_sem.at[0]),
        pltpu.make_async_copy(cots[1], flipped, cot_sem.at[1]),
    )

    @pl.when(section == 1)
    def _():
        start(*cot_copies)

    roots_copy.start()
    for field in zip(loads[1], loads[0]):
        start(*field)
    probs_copy.start()
    greet(section, t, sections, tensors, (near, cross) if chain else ())

    part_length = text_out.shape[1]
    micro, page = core, chip
    kinds = ((grad_out, layout_grad_out), (text_out, layout_out))
    pages = ((work[0].g, flipped), ys)

    def page_part(g, q, a):
        span = pl.ds(q * part_length, part_length)
        return pages[g][a].at[span] if a == 0 else pages[g][a].at[:, span]

    def each_page(g, act):
        for q in range(tensors):
            for a in range(2):
                here = (micro == g) & (t == q)

                @pl.when((section == g) & here)
                def _():
                    act(g, q, a, True)

                @pl.when((section == g) & jnp.logical_not(here))
                def _():
                    act(g, q, a, False)

    def page_copy(g, q, a):
        return remote(
            page_part(g, q, a), kinds[g][a].at[page], page_send.at[q, a], page_recv.at[g, a, page],
            {"section": micro, "tensor": q},
        )

    def page_start(g, q, a, here):
        if here:
            pltpu.make_async_copy(page_part(g, q, a), kinds[g][a].at[page], page_recv.at[g, a, page]).start()
        else:
            page_copy(g, q, a).start()

    def page_sent(g, q, a, here):
        if not here:
            page_copy(g, q, a).wait_send()

    each_page(1, page_start)

    def hop(b, n):
        part = work[b].g.at[blocks[n]]
        return remote(part, part, hop_send.at[b, n], hop_recv.at[b, n], other)

    ahead = 3
    step = ROWS
    up_first, down_first = starts[0][2], starts[0][3]
    up_count, down_count = (starts[0][3] - up_first) // step, (starts[0][4] - down_first) // step
    n_feed = up_count + down_count
    chunks = [Chunk(0, k, up_first + k * step, step) for k in range(n_feed)]
    later = [(1, 0, starts[1][MATRICES])]
    later += [(0, f, n) for f, n in pieces_of(starts[0][1], 192)]
    later += [(0, starts[0][1] + f, n) for f, n in pieces_of(starts[0][2] - starts[0][1], 64)]
    chunks += [Chunk(b, n_feed + i, f, n) for i, (b, f, n) in enumerate(later)]

    def feed_chunk(k):
        return Chunk(0, k, pl.multiple_of(up_first + k * step, 16), step)

    def span(ref, c):
        return ref.at[pl.ds(c.first, c.rows)]

    def to_sibling(c, j):
        w = work[c.b]
        return remote(
            span(w.raw.at[2 * j + 1 - core], c), span(w.from_sibling.at[j], c),
            sib_send.at[c.index, j], sib_recv.at[c.index, j], sibling,
        )

    def mine(c):
        return span(work[c.b].raw.at[t], c)

    def theirs(c):
        return span(work[c.b].raw.at[2 * (1 - chip) + core], c)

    def to_partner(c):
        return remote(
            theirs(c), span(work[c.b].from_partner, c), send.at[0, c.index], recv.at[0, c.index], partner
        )

    def from_near(c):
        return span(work[c.b].from_sibling.at[0], c)

    def from_cross(c):
        return span(work[c.b].from_sibling.at[1], c)

    def to_near(c):
        return remote(mine(c), from_near(c), send.at[1, c.index], recv.at[1, c.index], near)

    def to_cross(c):
        return remote(mine(c), from_cross(c), send.at[2, c.index], recv.at[2, c.index], cross)

    def total_to_near(c):
        return remote(
            span(work[c.b].from_partner, c), from_near(c), send.at[3, c.index], recv.at[3, c.index], near
        )

    def out_copy(c, source):
        return pltpu.make_async_copy(span(source, c), span(results[c.b], c), out_sem.at[c.index])

    def added(target, *sources):
        target[...] = sum(s[...].astype(F32) for s in sources).astype(BF)

    def send_to_sibling(c):
        for j in range(tensors // 2):
            to_sibling(c, j).start()

    def stage_sibling(c):
        w = work[c.b]
        for j in range(tensors // 2):
            to_sibling(c, j).wait_recv()
        added(theirs(c), theirs(c), span(w.from_sibling.at[1 - chip], c))
        added(mine(c), mine(c), span(w.from_sibling.at[chip], c))
        if chain:
            @pl.when(jnp.logical_not(outer))
            def _():
                for device in (near, cross):
                    pl.semaphore_signal(credit, inc=1, device_id=device, device_id_type=MESH)

    def stage_partner(c):
        to_partner(c).wait_recv()
        added(mine(c), mine(c), span(work[c.b].from_partner, c))
        if not chain:
            out_copy(c, work[c.b].raw.at[t]).start()
            return

        @pl.when(outer)
        def _():
            pl.semaphore_wait(credit, 1)
            to_near(c).start()

    def stage_near(c):
        @pl.when(jnp.logical_not(outer))
        def _():
            to_near(c).wait_recv()
            added(mine(c), mine(c), from_near(c))
            pl.semaphore_wait(credit, 1)
            to_cross(c).start()

    def stage_cross(c):
        @pl.when(jnp.logical_not(outer))
        def _():
            to_cross(c).wait_recv()
            total = work[c.b].from_partner
            added(span(total, c), mine(c), from_cross(c))
            total_to_near(c).start()
            out_copy(c, total).start()

    def stage_total(c):
        @pl.when(outer)
        def _():
            total_to_near(c).wait_recv()
            out_copy(c, work[c.b].from_sibling.at[0]).start()

    def first_copies():
        for c in chunks[:ahead]:
            stage_sibling(c)
            to_partner(c).start()

    def turn_operands():
        wait(loads[0].low, loads[0].act)
        work[0].lowT[...] = views[0].low[...].T

    def feed_products():
        own, w = views[0], work[0]

        @pl.loop(0, up_count)
        def _(k):
            rows = pl.ds(pl.multiple_of(k * step, step), step)
            for q in range(tensors):
                w.raw[q, pl.ds(pl.multiple_of(up_first + k * step, 16), step), :] = dot(
                    w.lowT[rows, :], own.slope[q]
                ).astype(BF)
            send_to_sibling(feed_chunk(k))

        first_copies()

        @pl.loop(0, down_count)
        def _(k):
            lanes = pl.ds(pl.multiple_of(k * step, step), step)
            for q in range(tensors):
                w.raw[q, pl.ds(pl.multiple_of(down_first + k * step, 16), step), :] = dot(
                    own.act[q, :, lanes].T, w.gf[...]
                ).astype(BF)
            send_to_sibling(feed_chunk(up_count + k))

    def later_product(c):
        own, w = views[c.b], work[c.b]
        for q in range(tensors):
            for i in range(MATRICES):
                first = max(c.first, starts[c.b][i])
                last = min(c.first + c.rows, starts[c.b][i + 1])
                if first >= last:
                    continue
                rows = slice(first - starts[c.b][i], last - starts[c.b][i])
                if i == 0:
                    value = dot(own.qkv[q, rows, :], own.x[...])
                elif i == 1:
                    value = dot(own.ctx[q, rows, :], w.ga[...])
                elif i == 2:
                    value = dot(w.lowT[rows, :], own.slope[q])
                else:
                    value = dot(own.act[q, :, rows].T, w.gf[...])
                w.raw[q, first:last, :] = value.astype(BF)
        send_to_sibling(c)

    @pl.when(section == 1)
    def _():
        wait(*cot_copies)
        work[1].g[...] = flipped[...].T

    for b in range(2):
        work[b].sums[...] = jnp.zeros(work[b].sums.shape, F32)
    roots_copy.wait()

    def feed_back(n, block):
        for b in (1, 0):
            own, own_in, w, gain = views[b], loads[b], work[b], gains[b]
            if n == 0:
                wait(own_in.n2)

            if block in blocks:
                hop(b, n).wait_recv()

            for rows in small_blocks(block):
                g, normed = w.g[rows].astype(F32), own.n2[rows].astype(F32)
                low = norm_rows_back(g, normed, roots[rows, 2 * b + 1 : 2 * b + 2], gain[1:2])
                w.dz[rows] = low
                w.gf[rows] = low.astype(BF)
                w.sums[1:2] += jnp.sum(g * normed, axis=0, keepdims=True)
                w.sums[3:4] += jnp.sum(g, axis=0, keepdims=True)

            if n == 0:
                wait(own_in.downward, own_in.slope, own_in.upward)

            @pl.loop(0, tensors)
            def _(q):
                d_act = dot(w.gf[block], own.downward[q])
                d_pre = (d_act * own.slope[q, block].astype(F32)).astype(BF)
                own.slope[q, block] = d_pre
                w.dz[block] += dot(d_pre, own.upward[q])

            if n == 0:
                wait(own_in.n1, own_in.outward)
            for rows in small_blocks(block):
                g, normed = w.dz[rows], own.n1[rows].astype(F32)
                low = norm_rows_back(g, normed, roots[rows, 2 * b : 2 * b + 1], gain[0:1])
                w.dz[rows] = low
                w.ga[rows] = low.astype(BF)
                w.sums[0:1] += jnp.sum(g * normed, axis=0, keepdims=True)
                w.sums[2:3] += jnp.sum(g, axis=0, keepdims=True)
            gaT = w.ga[block].T
            for q in range(tensors):
                w.dctx[q, :, block] = dot(own.outward[q], gaT).astype(BF)

    @pl.when(section == 0)
    def _():
        turn_operands()
        for n, block in enumerate(blocks):
            feed_back(n, block)

    @pl.when(section == 1)
    def _():
        feed_back(0, slice(0, length))

    @pl.when(section == 0)
    def _():
        feed_products()

    for own_in in loads:
        wait(own_in.qkv, own_in.ctx, own_in.inv)
    wait(probs_copy)
    qkv = (views[0].qkv, views[1].qkv)
    text_rows, layout_rows = slice(0, HEAD_TEXT), slice(HEAD_TEXT, HEAD_TEXT + HEAD_LAYOUT)

    def turn(k, n_known):
        fixed = isinstance(k, int)

        def at(i, stage):
            if not fixed:
                pl.when((i >= 0) & (i < n_feed))(lambda: stage(feed_chunk(i)))
            elif 0 <= i < n_known:
                stage(chunks[i])

        def sibling_and_send(c):
            stage_sibling(c)
            to_partner(c).start()

        at(k + ahead, sibling_and_send)
        at(k, stage_partner)
        if chain:
            at(k - 2, stage_near)
            at(k - 4, stage_cross)
            at(k - 6, stage_total)

    early_turns = 6

    @pl.loop(0, tensors)
    def _(q):
        for local in range(local_heads):
            head = q * local_heads + local

            @pl.when((section == 0) & (head % 2 == 0) & (head < 2 * early_turns))
            def _():
                turn(head // 2, n_feed)

            inv = views[0].inv[q, local : local + 1, :]
            scaled = [
                (work[s].dctx[q, local * SIZES[s] : (local + 1) * SIZES[s], :].astype(F32) * inv).astype(BF)
                for s in range(2)
            ]
            inner = [
                jnp.sum(
                    scaled[s].astype(F32)
                    * views[s].ctx[q, local * SIZES[s] : (local + 1) * SIZES[s], :].astype(F32),
                    axis=0, keepdims=True,
                )
                for s in range(2)
            ]
            rows16 = lax.broadcasted_iota(jnp.int32, (16, length), 0)
            extra = jnp.zeros((16, length), F32)
            for i, value in enumerate((inner[0] + inner[1], inner[1])):
                high = value.astype(BF).astype(F32)
                extra = jnp.where(rows16 == 2 * i, -high, extra)
                extra = jnp.where(rows16 == 2 * i + 1, high - value, extra)
            pad = jnp.zeros((128 - sum(SIZES) - 16, length), BF)
            dcT = jnp.concatenate([*scaled, extra.astype(BF), pad], axis=0)
            dc = dcT.T
            qT, kT = (head_rows(qkv, q, kind, local, SCALES if kind == 0 else None) for kind in range(2))
            v_text, v_layout = (head_part(qkv, q, 2, local, s) for s in range(2))
            one, other_one = (((rows16 // 2) == i).astype(F32).astype(BF) for i in range(2))
            low = probs_in[q, local]
            probs = low.astype(F32)
            both = dot(dc, jnp.concatenate([v_text, v_layout, one, pad], axis=0))
            ds_both = (probs * both).astype(BF)
            single = dot(dc, jnp.concatenate([jnp.zeros_like(v_text), v_layout, other_one, pad], axis=0))
            ds_layout = (probs * single).astype(BF)
            dvT = dot(dcT, low)
            put_head(qkv, q, 2, local, 0, dvT[text_rows])
            put_head(qkv, q, 2, local, 1, dvT[layout_rows])
            k = kT.T
            lane = lax.broadcasted_iota(jnp.int32, (length, 128), 1)
            dq = jnp.where(lane < HEAD_TEXT, dot(ds_both, k) * SCALES[0], dot(ds_layout, k) * SCALES[1])
            dqT = dq.astype(BF).T
            put_head(qkv, q, 0, local, 0, dqT[text_rows])
            put_head(qkv, q, 0, local, 1, dqT[layout_rows])
            put_head(qkv, q, 1, local, 0, dot(qT[text_rows], ds_both))
            put_head(qkv, q, 1, local, 1, dot(qT[layout_rows], ds_layout))

    wait(loads[0].project, loads[1].project)
    page_sum = jnp.zeros((1, work[0].dz.shape[1]), F32)
    for n, block in enumerate(blocks):
        for b in (1, 0):
            down = work[b].dz[block]
            for q in range(tensors):
                down += dot(qkv[b][q, :, block].T, views[b].project[q])
            down = down.astype(BF)
            work[b].g[block] = down
            if b == 0:
                page_sum += jnp.sum(down.astype(F32), axis=0, keepdims=True)

            @pl.when(section == 1)
            def _():
                hop(b, n).start()

    wait(loads[1].low, loads[1].act)
    work[1].lowT[...] = views[1].low[...].T
    for own_in in loads:
        wait(own_in.x)
    @pl.when(section == 1)
    def _():
        turn_operands()
        feed_products()

    for c in chunks[n_feed:]:
        later_product(c)

    @pl.when(section == 0)
    def _():
        flipped[...] = work[1].g[...].T
        each_page(0, page_start)

    at_page = (lax.broadcasted_iota(jnp.int32, lang_ids.shape, 0) == t % 2) & (
        lax.broadcasted_iota(jnp.int32, lang_ids.shape, 1) == t // 2
    )
    group = jnp.sum(jnp.where(at_page, lang_ids[...], 0), axis=(0, 1), keepdims=True)
    n_lang = small_out.shape[1] - 8
    chosen = (lax.broadcasted_iota(jnp.int32, (n_lang, 1), 0) == group) & (section == 0)
    small_sum[0, 0:n_lang] = jnp.where(chosen, page_sum, 0.0)
    small_sum[0, n_lang : n_lang + 4] = work[0].sums[...]
    small_sum[0, n_lang + 4 : n_lang + 8] = jnp.zeros((4, small_out.shape[2]), F32)
    small_sum[0, n_lang + 4 : n_lang + 8, : work[1].sums.shape[1]] = work[1].sums[...]

    def small_copy(i, device):
        return remote(small_sum.at[i], small_got.at[i], small_send.at[i], small_recv.at[i], device)

    if chain:
        small_copy(0, sibling).start()
    @pl.when(section == 1)
    def _():
        @pl.loop(0, early_turns)
        def _(k):
            turn(k, n_feed)

    for k in range(early_turns, len(chunks) + (6 if chain else 0)):
        turn(k, len(chunks))
        if not chain:
            continue
        if k == early_turns:
            small_copy(0, sibling).wait_recv()
            small_sum[1] = small_sum[0] + small_got[0]
            small_copy(1, partner).start()
        if k == early_turns + 1:
            small_copy(1, partner).wait_recv()
            small_sum[2] = small_sum[1] + small_got[1]
            small_copy(2, near).start()
        if k == early_turns + 2:
            small_copy(2, near).wait_recv()
            small_sum[3] = small_sum[2] + small_got[2]

            @pl.when(jnp.logical_not(outer))
            def _():
                small_copy(3, cross).start()

        if k == early_turns + 4:
            @pl.when(jnp.logical_not(outer))
            def _():
                small_copy(3, cross).wait_recv()
                small_sum[4] = small_sum[3] + small_got[3]
                small_copy(4, near).start()

        if k == early_turns + 6:
            @pl.when(outer)
            def _():
                small_copy(4, near).wait_recv()
                small_sum[4] = small_got[4]

            small_sum[5] = small_sum[4]
            small_copy(5, other).start()

    if chain:
        for i, device in enumerate((sibling, partner, near)):
            small_copy(i, device).wait_send()

        @pl.when(jnp.logical_not(outer))
        def _():
            small_copy(3, cross).wait_send()
            small_copy(4, near).wait_send()

        small_copy(5, other).wait()
        small_out[0] = small_sum[5]
        small_out[1] = small_got[5]
    else:
        small_out[0] = small_sum[0]
        small_out[1] = small_sum[0]

    @pl.when(section == 1)
    def _():
        for b in range(2):
            for n in range(len(blocks)):
                hop(b, n).wait_send()

    for c in chunks:
        for j in range(tensors // 2):
            to_sibling(c, j).wait_send()
        to_partner(c).wait_send()
        if not chain:
            out_copy(c, work[c.b].from_partner).wait()
            continue

        @pl.when(outer)
        def _():
            to_near(c).wait_send()

        @pl.when(jnp.logical_not(outer))
        def _():
            to_cross(c).wait_send()
            total_to_near(c).wait_send()

        out_copy(c, work[c.b].from_partner).wait()

    for g in range(sections):
        each_page(g, page_sent)
        for a in range(2):
            for j in range(2):
                dst = kinds[g][a].at[j]
                remote(dst, dst, page_send.at[0, a], page_recv.at[g, a, j], partner).wait_recv()
    landed = (text_out, layout_out, grad_out, layout_grad_out)
    copies = [pltpu.make_async_copy(v, h, page_out_sem.at[i]) for i, (v, h) in enumerate(zip(landed, page_outs))]
    start(*copies)
    wait(*copies)


def layer_backward(mesh, x, y, probs, roots, kept, weights, cots, norms, lang_ids, n_lang):
    sections, dp, tensors = mesh.shape["section"], mesh.shape["dp"], mesh.shape["tensor"]
    chain = dp == 4
    needed = tuple(
        Needed(
            n2=k.n2, downward=w.downward, slope=k.slope, upward=w.upward, n1=k.n1,
            outward=w.outward, low=k.low, act=k.act, qkv=k.qkv, ctx=k.ctx, inv=k.inv, project=w.project, x=rows,
        )
        for k, w, rows in zip(kept, weights, x)
    )
    flat_in, in_tree = jax.tree.flatten((needed, probs, roots))
    plain = [v for own in needed for name, v in own._asdict().items() if name not in Weights._fields] + [probs, roots]
    stacks = [(matrix_starts(own)[MATRICES], rows.shape[1]) for own, rows in zip(needed, x)]
    length = x[0].shape[0]
    work = []
    for own, rows, (count, width) in zip(needed, x, stacks):
        work += Work(
            g=shape(rows.shape), gf=shape(rows.shape), ga=shape(rows.shape), dz=shape(rows.shape, F32),
            dctx=shape(own.ctx.shape), sums=shape((4, width), F32), lowT=shape((width, length)),
            raw=shape((tensors, count, width)), from_sibling=shape((tensors // 2, count, width)),
            from_partner=shape((count, width)),
        )
    small = shape((2, n_lang + 8, x[0].shape[1]), F32)
    text_page = shape((2, length // tensors, x[0].shape[1]))
    layout_page = shape((2, x[1].shape[1], length // tensors))
    summed = [shape(s) for s in stacks]
    own = needed[0]
    n_feed = (own.upward.shape[1] + own.downward.shape[1]) // ROWS
    n_chunks = n_feed + 1 + own.project.shape[1] // 192 + own.outward.shape[1] // 64
    n_blocks = len(hop_blocks(length))
    dma = pltpu.SemaphoreType.DMA
    results = pl.pallas_call(
        functools.partial(backward_kernel, sections, tensors, chain, in_tree),
        out_shape=summed + [small, text_page, layout_page, text_page, layout_page],
        in_specs=[ANY] * (len(flat_in) + 4) + [VMEM] * 3,
        out_specs=[ANY] * 2 + [VMEM] + [ANY] * 4,
        scratch_shapes=vmem_like(work) + vmem_like(plain)
        + [pltpu.VMEM(cots[1].shape, BF)] + [pltpu.VMEM((6,) + small.shape[1:], F32)] * 2
        + vmem_like([text_page, layout_page] * 2)
        + [dma((len(flat_in),)), dma((2,)), dma((2, n_blocks)), dma((2, n_blocks))]
        + [dma((n_chunks, tensors // 2))] * 2 + [dma((4, n_chunks))] * 2
        + [pltpu.SemaphoreType.REGULAR, dma((n_chunks,))]
        + [dma((6,))] * 2 + [dma((tensors, 2)), dma((sections, 2, 2)), dma((4,))],
        compiler_params=pltpu.CompilerParams(
            collective_id=1, has_side_effects=True, vmem_limit_bytes=64 << 20
        ),
        name="layer_backward",
    )(*flat_in, *cots, *y, lang_ids, norms[0][0], norms[1][0])
    totals, small, pages = results[:2], results[2], results[3:7]
    if not chain:
        totals = lax.psum(tuple(totals), "dp")
        both = lax.psum(small[0], ("dp", "tensor"))
        small = jnp.stack([both, lax.ppermute(both, "section", [(0, 1), (1, 0)])])
    return totals, small, pages


def widen_kernel(n_in, n_pages, *refs):
    n_out = 5 + n_pages + 2 * MATRICES
    hbm_in, hbm_out = refs[:n_in], refs[n_in : n_in + n_out]
    vmem_in, vmem_out = refs[n_in + n_out : 2 * n_in + n_out], refs[2 * n_in + n_out : -2]
    in_sem, out_sem = refs[-2:]
    loads = [pltpu.make_async_copy(h, v, in_sem.at[i]) for i, (h, v) in enumerate(zip(hbm_in, vmem_in))]
    sources = vmem_out[:5] + vmem_in[3:] + vmem_out[5:]
    stores = [pltpu.make_async_copy(v, h, out_sem.at[i]) for i, (v, h) in enumerate(zip(sources, hbm_out))]
    start(*loads)
    totals, small = vmem_in[0:2], vmem_in[2]
    for b in range(2):
        wait(loads[b])
        at = 0
        for i in range(b * MATRICES, (b + 1) * MATRICES):
            out = vmem_out[5 + i]
            for c in range(0, out.shape[0], 48):
                out[c : c + 48] = totals[b][at + c : at + c + 48].astype(F32)
            at += out.shape[0]
            stores[5 + n_pages + i].start()
    for i in range(n_pages):
        loads[3 + i].wait()
        stores[5 + i].start()
    loads[2].wait()
    n_lang = vmem_out[0].shape[0]
    vmem_out[0][...] = jnp.where(lax.axis_index("section") == 0, small[0, :n_lang], small[1, :n_lang])
    for i, out in enumerate(vmem_out[1:5]):
        first = n_lang + 2 * i
        out[...] = small[0, first : first + 2, : out.shape[1]]
    start(*stores[:5])
    wait(*stores)


def widen(totals, small, pages, shards, n_lang):
    widths = [total.shape[1] for total in totals]
    sums = [shape((n_lang, widths[0]), F32)] + [shape((2, w), F32) for w in widths for _ in range(2)]
    grads = [shape(m.shape, F32) for own in shards for m in own]
    inputs = (*totals, small, *pages)
    outs = sums + [shape(page.shape) for page in pages] + grads
    results = pl.pallas_call(
        functools.partial(widen_kernel, len(inputs), len(pages)), out_shape=outs,
        in_specs=[ANY] * len(inputs), out_specs=[ANY] * len(outs),
        scratch_shapes=vmem_like(inputs) + vmem_like(sums + grads)
        + [pltpu.SemaphoreType.DMA((len(inputs),)), pltpu.SemaphoreType.DMA((len(outs),))],
        compiler_params=pltpu.CompilerParams(vmem_limit_bytes=62 << 20), name="widen",
    )(*inputs)
    return results[0], results[1:5], results[5:9], results[9:13], results[13:17]


def per_device(
    mesh,
    text_input,
    layout_input,
    text_cotangent,
    layout_cotangent,
    page_counts,
    pad_mask,
    lang_ids,
    lang_table,
    text_project,
    text_outward,
    text_upward,
    text_downward,
    text_gains,
    text_biases,
    layout_project,
    layout_outward,
    layout_upward,
    layout_downward,
    layout_gains,
    layout_biases,
):
    def flat(project):
        return jnp.transpose(project[0], (1, 2, 0)).reshape(-1, project.shape[1])

    def flipped(block):
        return jnp.transpose(block[0], (0, 2, 1))

    shards = (
        Weights(flat(text_project), text_outward[0], text_upward[0], text_downward[0]),
        Weights(flat(layout_project), layout_outward[0], layout_upward[0], layout_downward[0]),
    )
    norms = ((text_gains[0], text_biases[0]), (layout_gains[0], layout_biases[0]))
    marks = (pad_mask, page_counts, lang_ids, lang_table)
    (x, y, probs, roots, kept, weights), cots = layer_forward(
        mesh, text_input[0], flipped(layout_input), text_cotangent[0], flipped(layout_cotangent), shards, norms, marks
    )
    n_lang = lang_table.shape[0]
    totals, small, pages = layer_backward(mesh, x, y, probs, roots, kept, weights, cots, norms, lang_ids, n_lang)
    lang_sum, norm_sums, pages, text_sums, layout_sums = widen(totals, small, pages, shards, n_lang)
    text_out, layout_out, text_grad, layout_grad = pages

    def unflat(grad, like):
        return jnp.transpose(grad.reshape(like.shape[2], like.shape[3], like.shape[1]), (2, 0, 1))[None]

    unflip = lambda block: jnp.transpose(block, (0, 2, 1))[None]
    return (
        text_out[None], unflip(layout_out), text_grad[None], unflip(layout_grad), lang_sum,
        unflat(text_sums[0], text_project), *(s[None] for s in text_sums[1:]), norm_sums[0][None], norm_sums[1][None],
        unflat(layout_sums[0], layout_project), *(s[None] for s in layout_sums[1:]),
        norm_sums[2][None], norm_sums[3][None],
    )


def solution(mesh):
    tokens = P("section", "dp", "tensor", None)
    weight_specs = (
        P("section", None, None, "tensor"), P("section", "tensor", None), P("section", None, "tensor"),
        P("section", "tensor", None), P("section", None, None), P("section", None, None),
    )
    in_specs = (tokens,) * 4 + (P(None, "dp"), P(None, "dp", None), P(None, "dp"), P()) + weight_specs * 2
    out_specs = (tokens,) * 4 + (P(),) + weight_specs * 2
    return jax.shard_map(
        functools.partial(per_device, mesh), mesh=mesh, in_specs=in_specs, out_specs=out_specs, check_vma=False
    )
```

```python
import functools
import math
import typing

import jax
import jax.numpy as jnp
from jax import lax
from jax.experimental import pallas as pl
from jax.experimental.pallas import tpu as pltpu
from jax.sharding import PartitionSpec as P

HEAD_TEXT = 64
HEAD_LAYOUT = 16
EPSILON = 1e-05
NEGATIVE = -1e30
HIGH = lax.Precision.HIGHEST
MESH = pl.DeviceIdType.MESH
BF = jnp.bfloat16
F32 = jnp.float32
ANY = pl.BlockSpec(memory_space=pl.ANY)


def remote(src, dst, send, recv, device):
    return pltpu.make_async_remote_copy(
        src_ref=src, dst_ref=dst, send_sem=send, recv_sem=recv, device_id=device, device_id_type=MESH
    )


def greet(section, tensor, sections, tensors, extra=()):
    barrier = pltpu.get_barrier_semaphore()
    for g in range(sections):
        for q in range(tensors):

            @pl.when((section != g) | (tensor != q))
            def _():
                pl.semaphore_signal(
                    barrier, inc=1, device_id={"section": g, "tensor": q}, device_id_type=MESH
                )

    for device in extra:
        pl.semaphore_signal(barrier, inc=1, device_id=device, device_id_type=MESH)
    pl.semaphore_wait(barrier, sections * tensors - 1 + len(extra))


GELU_P = 0.3275911
GELU_A = (0.254829592, -0.284496736, 1.421413741, -1.453152027, 1.061405429)
NN = (((1,), (0,)), ((), ()))
NT = (((1,), (1,)), ((), ()))
SCALES = (1.0 / math.sqrt(HEAD_TEXT), 1.0 / math.sqrt(HEAD_LAYOUT))
SIZES = (HEAD_TEXT, HEAD_LAYOUT)
ROWS = 128


class Weights(typing.NamedTuple):
    project: typing.Any
    outward: typing.Any
    upward: typing.Any
    downward: typing.Any


class Kept(typing.NamedTuple):
    qkv: typing.Any
    ctx: typing.Any
    inv: typing.Any
    n1: typing.Any
    low: typing.Any
    act: typing.Any
    slope: typing.Any
    n2: typing.Any


def dot(a, b, dims=NN):
    return lax.dot_general(a, b, dims, preferred_element_type=F32)


def gelu_pair(u):
    d = 1.0 + (GELU_P / math.sqrt(2.0)) * jnp.abs(u)
    t = pl.reciprocal(d, approx=True)
    t = t * (2.0 - d * t)
    e = jnp.exp2((u * u) * (-0.5 / math.log(2.0)))
    a1, a2, a3, a4, a5 = (0.5 * a for a in GELU_A)
    tail = ((((a5 * t + a4) * t + a3) * t + a2) * t + a1) * t * e
    cdf = jnp.where(u >= 0, 1.0 - tail, tail)
    return u * cdf, cdf + u * e * (1.0 / math.sqrt(2.0 * math.pi))


def norm_rows(z, gain, offset):
    center = z - jnp.mean(z, axis=-1, keepdims=True)
    inverse = lax.rsqrt(jnp.mean(center * center, axis=-1, keepdims=True) + EPSILON)
    normed = center * inverse
    return normed * gain + offset, normed, inverse


def norm_rows_back(g, n, r, gain):
    t = g * gain
    return r * (t - jnp.mean(t, axis=-1, keepdims=True) - n * jnp.mean(t * n, axis=-1, keepdims=True))


class Staged:
    def __init__(self, tree, hbm, vmem, sem, inward):
        self.tree, self.vmem = tree, list(vmem)
        pairs = zip(hbm, vmem) if inward else zip(vmem, hbm)
        self.copies = [pltpu.make_async_copy(a, b, sem.at[i]) for i, (a, b) in enumerate(pairs)]

    def refs(self):
        return jax.tree.unflatten(self.tree, self.vmem)

    def parts(self):
        return jax.tree.unflatten(self.tree, self.copies)

    def start(self):
        for copy in self.copies:
            copy.start()

    def wait(self):
        for copy in self.copies:
            copy.wait()


def start(*copies):
    for copy in copies:
        copy.start()


def wait(*copies):
    for copy in copies:
        copy.wait()


def head_rows(stacks, slot, kind, local, scales=None, extra=None):
    rows = []
    for b in range(2):
        piece = head_part(stacks, slot, kind, local, b)
        rows.append(piece if scales is None else piece * BF(scales[b]))
    length = rows[0].shape[1]
    rows.append(jnp.zeros((16, length), BF) if extra is None else extra)
    rows.append(jnp.zeros((128 - sum(SIZES) - 16, length), BF))
    return jnp.concatenate(rows, axis=0)


def head_part(stacks, slot, kind, local, b):
    first = kind * (stacks[b].shape[1] // 3) + local * SIZES[b]
    return stacks[b][slot, first : first + SIZES[b], :]


def small_blocks(block, step=64):
    return [slice(c, c + step) for c in range(block.start, block.stop, step)]


def put_head(stacks, slot, kind, local, b, value):
    first = kind * (stacks[b].shape[1] // 3) + local * SIZES[b]
    stacks[b][slot, first : first + SIZES[b], :] = value.astype(BF)


def hop_blocks(length):
    ends = [0, length // 2, length * 3 // 4, length]
    return [slice(a, b) for a, b in zip(ends, ends[1:])]


def slot_of(u, core, chip):
    return ((chip + u // 2) % 2) * 2 + (core + u % 2) % 2


def forward_kernel(sections, tensors, shared, in_tree, out_tree, *refs):
    n_w, n_out = len(shared), out_tree.num_leaves
    sources = (refs[0:2], refs[2:4])
    shards = refs[4 : 4 + n_w]
    pad_mask, counts, lang_ids, lang_table, *norms = refs[4 + n_w : 12 + n_w]
    rest = refs[12 + n_w :]
    hbm_out, cots_out, rest = rest[:n_out], rest[n_out : n_out + 2], rest[n_out + 2 :]
    outgoing = Staged(out_tree, hbm_out, rest[:n_out], rest[n_out], False)
    rest = rest[n_out + 1 :]
    flipped, raw_x, y_narrow, *rest = rest
    nats, totals, pre, score_buffer, rest = rest[0:2], rest[2:4], rest[4:6], rest[6], rest[7:]
    xT, turned, turn_sem, rest = rest[0:2], (rest[2:4], rest[4:6]), rest[6], rest[7:]
    page_send, page_recv, w_send, w_recv, own_sem, hop_send, hop_recv, cot_sem, act_sem = rest
    x, y_pages, probs_out, roots, kept, weights = outgoing.refs()
    y = (y_pages[0], y_narrow)
    x_out, y_out, probs_copy, roots_copy, kept_out, weights_out = outgoing.parts()
    kept_hbm, weights_hbm = jax.tree.unflatten(out_tree, list(hbm_out))[4:6]
    section, d, t = lax.axis_index("section"), lax.axis_index("dp"), lax.axis_index("tensor")
    core, chip, half_index = t % 2, t // 2, d % 2
    sibling, partner = t + 1 - 2 * core, (t + tensors // 2) % tensors
    mate = d + 1 - 2 * half_index
    micro, page = core, chip
    part_length = sources[0][0].shape[1]
    length = x[0].shape[0]
    blocks = [slice(c, c + 2 * ROWS) for c in range(0, length, 2 * ROWS)]
    parts = hop_blocks(length)
    full = (
        weights[0].project, weights[1].project, weights[0].outward, weights[0].upward,
        weights[0].downward, weights[1].outward, weights[1].upward, weights[1].downward,
    )
    greet(section, t, sections, tensors, ({"dp": mate},) if any(shared) else ())

    pieces = []
    for i in range(n_w):
        count = shards[i].shape[0] // 2
        n_parts = 2 if shared[i] and count % 64 == 0 else 1
        pieces += [(i, s * (count // n_parts), count // n_parts) for s in range(n_parts)]

    def rows_of(ref, p, which):
        i, first, count = pieces[p]
        if not shared[i]:
            return ref
        return ref.at[pl.ds(pl.multiple_of(which * (shards[i].shape[0] // 2) + first, 16), count)]

    def pieces_of_matrix(i):
        return [p for p in range(len(pieces)) if pieces[p][0] == i]

    def to_partner(p):
        i = pieces[p][0]
        return remote(
            rows_of(shards[i], p, half_index), rows_of(full[i].at[t], p, half_index),
            w_send.at[0, p], w_recv.at[0, p], {"tensor": partner},
        )

    def to_sibling(i):
        return remote(full[i].at[t], full[i].at[t], w_send.at[1, i], w_recv.at[1, i], {"tensor": sibling})

    def to_mate(p):
        ref = rows_of(full[pieces[p][0]].at[partner], p, half_index)
        return remote(ref, ref, w_send.at[2, p], w_recv.at[2, p], {"dp": mate})

    def on_first(p):
        ref = rows_of(full[pieces[p][0]].at[partner], p, half_index)
        return remote(ref, ref, w_send.at[3, p], w_recv.at[3, p], {"tensor": sibling})

    def on_second(p):
        ref = rows_of(full[pieces[p][0]].at[partner], p, 1 - half_index)
        return remote(ref, ref, w_send.at[4, p], w_recv.at[4, p], {"tensor": sibling})

    def keep(i):
        return pltpu.make_async_copy(shards[i], full[i].at[t], own_sem.at[i])

    def relay_piece(p):
        to_partner(p).wait_recv()
        if shared[pieces[p][0]]:
            to_mate(p).start()
        on_first(p).start()

    def relay(*which):
        for i in which:
            for p in pieces_of_matrix(i):
                relay_piece(p)

    def relay_second(*which):
        for i in which:
            for p in pieces_of_matrix(i):
                if shared[i]:
                    to_mate(p).wait_recv()
                    on_second(p).start()

    def early(*which):
        for i in which:
            to_sibling(i).wait_recv()

    def late(*which):
        for i in which:
            for p in pieces_of_matrix(i):
                on_first(p).wait_recv()
                if shared[i]:
                    on_second(p).wait_recv()

    def token_slot(g, a, index):
        start_at = pl.multiple_of(index * part_length, part_length)
        target = (raw_x, flipped)[a]
        return target.at[pl.ds(start_at, part_length)] if a == 0 else target.at[:, pl.ds(start_at, part_length)]

    def over_pages(g, act):
        for j in range(2):
            target = 2 * j + section
            here = (section == g) & (t == target)
            for a in range(2):
                act(g, j, a, target, here)

    def page_copy(g, j, a, target):
        return remote(
            sources[g][a].at[j], token_slot(g, a, t), page_send.at[g, j, a], page_recv.at[a, t],
            {"section": g, "tensor": target},
        )

    def page_start(g, j, a, target, here):
        @pl.when(here)
        def _():
            pltpu.make_async_copy(sources[g][a].at[j], token_slot(g, a, t), page_recv.at[a, t]).start()

        @pl.when(jnp.logical_not(here))
        def _():
            page_copy(g, j, a, target).start()

    def page_sent(g, j, a, target, here):
        @pl.when(jnp.logical_not(here))
        def _():
            page_copy(g, j, a, target).wait_send()

    def pages_arrived(g):
        for a in range(2):
            for q in range(tensors):
                slot = token_slot(g, a, q)
                remote(slot, slot, page_send.at[0, 0, a], page_recv.at[a, q], {"tensor": sibling}).wait_recv()

    def hop(b, n):
        return remote(
            y[b].at[parts[n]], x[b].at[parts[n]], hop_send.at[b, n], hop_recv.at[b, n], {"section": 1 - section}
        )

    def weights_to_hbm():
        for b in range(2):
            start(weights_out[b].project, weights_out[b].outward)
            for q in range(tensors):
                for m, name in enumerate((2, 3)):
                    copy = pltpu.make_async_copy(
                        turned[b][m].at[q % 2], weights_hbm[b][name].at[q], turn_sem.at[b, m, q % 2]
                    )
                    if q >= 2:
                        copy.wait()
                    turned[b][m][q % 2] = weights[b][name][q].T
                    copy.start()
        for b in range(2):
            for q in range(tensors - 2, tensors):
                for m, name in enumerate((2, 3)):
                    pltpu.make_async_copy(
                        turned[b][m].at[q % 2], weights_hbm[b][name].at[q], turn_sem.at[b, m, q % 2]
                    ).wait()

    over_pages(0, page_start)
    for i in range(n_w):
        keep(i).start()
    for p in range(len(pieces)):
        to_partner(p).start()

    @pl.when(section == 1)
    def _():
        over_pages(1, page_start)

    for i in range(n_w):
        keep(i).wait()
        to_sibling(i).start()

    at_page = (lax.broadcasted_iota(jnp.int32, counts.shape, 0) == micro) & (
        lax.broadcasted_iota(jnp.int32, counts.shape, 1) == page
    )

    def own_entry(ref):
        return jnp.sum(jnp.where(at_page, ref[...], 0), axis=(0, 1), keepdims=True)

    positions = lax.broadcasted_iota(jnp.int32, (1, length), 1)
    mask_row = pad_mask[micro, pl.ds(page, 1), :]
    key_mask = (positions < own_entry(counts)) & ((mask_row == 1) | (positions == 0))
    first_row = (lax.broadcasted_iota(jnp.int32, (16, length), 0) == 0).astype(F32)
    mask_row16 = (first_row * jnp.where(key_mask, 0.0, NEGATIVE)).astype(BF)
    groups = lax.broadcasted_iota(jnp.int32, (lang_table.shape[0], 1), 0)
    lang_row = jnp.sum(jnp.where(groups == own_entry(lang_ids), lang_table[...], 0.0), axis=0, keepdims=True)
    local_heads = weights[0].project.shape[1] // (3 * HEAD_TEXT)
    qkv = (kept[0].qkv, kept[1].qkv)

    @pl.when(section == 0)
    def _():
        pages_arrived(0)
        x[0][...] = (raw_x[...].astype(F32) + lang_row).astype(BF)
        x[1][...] = flipped[...].T
        early(0, 1)

    @pl.when(section == 1)
    def _():
        relay(*range(n_w))
        relay_second(*range(n_w))
        early(*range(n_w))
        late(*range(n_w))
        weights_to_hbm()

    @pl.loop(0, 2)
    def _(half):
        @pl.when((half == 1) & (section == 0))
        def _():
            relay(0, 1)
            relay_second(0)
            late(0, 1)

        for n, block in enumerate(parts):
            @pl.when((half == 0) & (section == 1))
            def _():
                for b in range(2):
                    hop(b, n).wait_recv()

            @pl.when(half == 0)
            def _():
                for b in range(2):
                    xT[b][:, block] = x[b][block].T

            @pl.loop(0, 2)
            def _(u):
                slot = slot_of(2 * half + u, core, chip)
                for b in range(2):
                    qkv[b][slot, :, block] = dot(weights[b].project[slot], xT[b][:, block]).astype(BF)

        @pl.loop(0, 2)
        def _(u):
            slot = slot_of(2 * half + u, core, chip)
            for local in range(local_heads):
                q = head_rows(qkv, slot, 0, local, SCALES, first_row.astype(BF)).T
                kT = head_rows(qkv, slot, 1, local, None, mask_row16)
                score_buffer[local] = dot(q, kT)
                for rows in small_blocks(slice(0, length)):
                    scores = score_buffer[local, rows, :]
                    raised = jnp.exp(scores - jnp.max(scores, axis=-1, keepdims=True))
                    probs_out[slot, local, rows, :] = raised.astype(BF)
                vT = head_rows(qkv, slot, 2, local, None, first_row.astype(BF))
                ctx = dot(probs_out[slot, local], vT.T).T
                inv = 1.0 / ctx[sum(SIZES) : sum(SIZES) + 1]
                ctx = (ctx * inv).astype(BF)
                kept[0].inv[slot, local : local + 1, :] = inv
                kept[0].ctx[slot, local * HEAD_TEXT : (local + 1) * HEAD_TEXT, :] = ctx[:HEAD_TEXT]
                kept[1].ctx[slot, local * HEAD_LAYOUT : (local + 1) * HEAD_LAYOUT, :] = ctx[
                    HEAD_TEXT : HEAD_TEXT + HEAD_LAYOUT
                ]

    kept[1].inv[...] = jnp.zeros(kept[1].inv.shape, F32)
    start(probs_copy, *x_out, *(c for k in kept_out for c in (k.qkv, k.ctx, k.inv)))

    def attend(b):
        gains, biases = norms[2 * b : 2 * b + 2]
        width = x[b].shape[1]
        nats[b][...] = kept[b].ctx[...].reshape(width, length).T
        wide = weights[b].outward[...].reshape(width, width)
        for block in blocks:
            totals[b][1, block] = dot(nats[b][block], wide)
            for rows in small_blocks(block):
                h, n, r = norm_rows(x[b][rows].astype(F32) + totals[b][1, rows], gains[0:1], biases[0:1])
                totals[b][0, rows] = h
                totals[b][1, rows] = jnp.zeros(h.shape, F32)
                kept[b].n1[rows] = n.astype(BF)
                roots[rows, 2 * b : 2 * b + 1] = r
                kept[b].low[rows] = h.astype(BF)
        start(kept_out[b].n1, kept_out[b].low)

    def slot_copies(b, slot):
        return [
            pltpu.make_async_copy(v.at[slot], h.at[slot], act_sem.at[b, m, slot])
            for m, (v, h) in enumerate(((kept[b].act, kept_hbm[b].act), (kept[b].slope, kept_hbm[b].slope)))
        ]

    def feed(b, first, which):
        @pl.loop(first, first + 2)
        def _(u):
            slot = slot_of(u, core, chip)
            for block in which:
                pre[b][block] = dot(kept[b].low[block], weights[b].upward[slot])
                for rows in small_blocks(block, 16):
                    act, slope = gelu_pair(pre[b][rows])
                    kept[b].act[slot, rows] = act.astype(BF)
                    kept[b].slope[slot, rows] = slope.astype(BF)
                totals[b][1, block] += dot(kept[b].act[slot, block], weights[b].downward[slot])
                if block == slice(0, length):
                    start(*slot_copies(b, slot))

    def finish(b):
        gains, biases = norms[2 * b : 2 * b + 2]
        def last(block):
            feed(b, 2, [block])
            for rows in small_blocks(block):
                out, normed, r = norm_rows(totals[b][0, rows] + totals[b][1, rows], gains[1:2], biases[1:2])
                y[b][rows] = out.astype(BF)
                kept[b].n2[rows] = normed.astype(BF)
                roots[rows, 2 * b + 1 : 2 * b + 2] = r

        @pl.when(section == 0)
        def _():
            for n, block in enumerate(parts):
                last(block)
                hop(b, n).start()
            for u in range(2, 4):
                start(*slot_copies(b, slot_of(u, core, chip)))

        @pl.when(section == 1)
        def _():
            last(slice(0, length))

        if b == 1:
            y_pages[1][...] = y_narrow[...].T
        start(y_out[b], kept_out[b].n2)

    @pl.when(section == 0)
    def _():
        relay(2)
        relay_second(2)
        early(2)
        late(2)

    attend(0)

    @pl.when(section == 0)
    def _():
        relay(3)
        early(3, 4)

    feed(0, 0, [slice(0, length)])

    @pl.when(section == 0)
    def _():
        relay(4)
        relay_second(3)
        relay(5, 6, 7)
        early(5, 6, 7)
        late(5, 6, 7)

    attend(1)
    feed(1, 0, [slice(0, length)])
    finish(1)

    @pl.when(section == 0)
    def _():
        relay_second(4)
        late(3, 4)

    finish(0)

    @pl.when(section == 0)
    def _():
        over_pages(1, page_start)

    start(roots_copy)

    @pl.when(section == 0)
    def _():
        weights_to_hbm()
        for b in range(2):
            for n in range(len(parts)):
                hop(b, n).wait_send()

    for i in range(n_w):
        to_sibling(i).wait_send()
        for p in pieces_of_matrix(i):
            to_partner(p).wait_send()
            on_first(p).wait_send()
            if shared[i]:
                to_mate(p).wait_send()
                on_second(p).wait_send()
    for g in range(sections):
        over_pages(g, page_sent)

    @pl.when(section == 1)
    def _():
        pages_arrived(1)
        copies = [pltpu.make_async_copy(v, h, cot_sem.at[i]) for i, (v, h) in enumerate(zip((raw_x, flipped), cots_out))]
        start(*copies)
        wait(*copies)

    for group in (x_out, y_out, (probs_copy, roots_copy), *(w[:2] for w in weights_out)):
        wait(*group)
    for b, k in enumerate(kept_out):
        wait(k.qkv, k.ctx, k.inv, k.n1, k.low, k.n2)
        for slot in range(tensors):
            wait(*slot_copies(b, slot))


def vmem_like(tree):
    return [pltpu.VMEM(s.shape, s.dtype) for s in jax.tree.leaves(tree)]


VMEM = pl.BlockSpec(memory_space=pltpu.VMEM)


def shape(dims, dtype=BF):
    return jax.ShapeDtypeStruct(tuple(dims), dtype)


def layer_forward(mesh, text_in, layout_in, text_cot, layout_cot, shards, norms, marks):
    sections, dp, tensors = mesh.shape["section"], mesh.shape["dp"], mesh.shape["tensor"]
    length = text_in.shape[1] * tensors
    rows = (shape((length, text_in.shape[2])), shape((length, layout_in.shape[1])))
    local_heads = shards[0].project.shape[0] // (3 * HEAD_TEXT)
    kept = []
    for x, w in zip(rows, shards):
        units = shape((tensors, length, w.upward.shape[1]))
        kept.append(Kept(
            qkv=shape((tensors, w.project.shape[0], length)), ctx=shape((tensors, w.outward.shape[0], length)),
            inv=shape((tensors, local_heads, length), F32),
            n1=shape(x.shape), low=shape(x.shape), act=units, slope=units,
            n2=shape(x.shape),
        ))
    weights = tuple(Weights(*(shape((tensors,) + m.shape) for m in w)) for w in shards)
    pages_out = (rows[0], shape((rows[1].shape[1], length)))
    outs = (rows, pages_out, shape((tensors, local_heads, length, length)), shape((length, 4), F32), tuple(kept), weights)
    flat_out, out_tree = jax.tree.flatten(outs)
    (a, b) = shards
    ordered = (a.project, b.project, a.outward, a.upward, a.downward, b.outward, b.upward, b.downward)
    shared = tuple(dp % 2 == 0 and w.shape[0] % 32 == 0 and w.shape[1] >= 512 for w in ordered)
    n_w, n_pieces = len(ordered), 2 * len(ordered)
    cots = [rows[0], shape((rows[1].shape[1], length))]
    small = (*marks, *norms[0], *norms[1])
    results = pl.pallas_call(
        functools.partial(forward_kernel, sections, tensors, shared, None, out_tree),
        out_shape=flat_out + cots,
        in_specs=[ANY] * (4 + n_w) + [VMEM] * len(small),
        out_specs=[ANY] * (len(flat_out) + 2),
        scratch_shapes=vmem_like(flat_out) + [pltpu.SemaphoreType.DMA((len(flat_out),))]
        + [pltpu.VMEM(cots[1].shape, BF), pltpu.VMEM(cots[0].shape, BF), pltpu.VMEM(rows[1].shape, BF)]
        + [pltpu.VMEM(x.shape, BF) for x in rows]
        + [pltpu.VMEM((2,) + x.shape, F32) for x in rows]
        + [pltpu.VMEM((length, w.upward.shape[1]), F32) for w in shards]
        + [pltpu.VMEM((local_heads, length, length), F32)]
        + [pltpu.VMEM((x.shape[1], length), BF) for x in rows]
        + [pltpu.VMEM((2,) + m.shape, BF) for w in shards for m in (w.upward, w.downward)]
        + [pltpu.SemaphoreType.DMA((2, 2, 2))]
        + [
            pltpu.SemaphoreType.DMA((sections, 2, 2)), pltpu.SemaphoreType.DMA((2, tensors)),
            pltpu.SemaphoreType.DMA((5, n_pieces)), pltpu.SemaphoreType.DMA((5, n_pieces)), pltpu.SemaphoreType.DMA((n_w,)),
            pltpu.SemaphoreType.DMA((2, len(hop_blocks(length)))), pltpu.SemaphoreType.DMA((2, len(hop_blocks(length)))),
            pltpu.SemaphoreType.DMA((2,)), pltpu.SemaphoreType.DMA((2, 2, tensors)),
        ],
        compiler_params=pltpu.CompilerParams(
            collective_id=0, has_side_effects=True, vmem_limit_bytes=62 << 20
        ),
        name="layer_forward",
    )(text_in, layout_in, text_cot, layout_cot, *ordered, *small)
    return jax.tree.unflatten(out_tree, results[:-2]), tuple(results[-2:])


class Needed(typing.NamedTuple):
    n2: typing.Any
    downward: typing.Any
    slope: typing.Any
    upward: typing.Any
    n1: typing.Any
    outward: typing.Any
    low: typing.Any
    act: typing.Any
    qkv: typing.Any
    ctx: typing.Any
    inv: typing.Any
    project: typing.Any
    x: typing.Any


class Work(typing.NamedTuple):
    g: typing.Any
    gf: typing.Any
    ga: typing.Any
    dz: typing.Any
    dctx: typing.Any
    sums: typing.Any
    lowT: typing.Any
    raw: typing.Any
    from_sibling: typing.Any
    from_partner: typing.Any


class Chunk(typing.NamedTuple):
    b: typing.Any
    index: typing.Any
    first: typing.Any
    rows: typing.Any


MATRICES = 4


def matrix_rows(own):
    return own.project.shape[1], own.outward.shape[1], own.upward.shape[1], own.downward.shape[1]


def matrix_starts(own):
    sizes = matrix_rows(own)
    return [sum(sizes[:i]) for i in range(MATRICES + 1)]


def pieces_of(size, step):
    return [(f, step) for f in range(0, size, step)]


def backward_kernel(sections, tensors, chain, in_tree, *refs):
    n_in = in_tree.num_leaves
    hbm_in, refs = refs[:n_in], refs[n_in:]
    (cots, ys, lang_ids, gains), refs = (refs[0:2], refs[2:4], refs[4], refs[5:7]), refs[7:]
    results, small_out, page_outs, refs = refs[0:2], refs[2], refs[3:7], refs[7:]
    n_work = len(Work._fields)
    work, refs = (Work(*refs[:n_work]), Work(*refs[n_work : 2 * n_work])), refs[2 * n_work :]
    plain, refs = refs[: n_in - 2 * MATRICES], refs[n_in - 2 * MATRICES :]
    flipped, small_got, small_sum, refs = refs[0], refs[1], refs[2], refs[3:]
    text_out, layout_out, grad_out, layout_grad_out, *refs = refs
    in_sem, cot_sem, hop_send, hop_recv, sib_send, sib_recv, send, recv, credit, out_sem, *refs = refs
    small_send, small_recv, page_send, page_recv, page_out_sem = refs
    section, d, t = lax.axis_index("section"), lax.axis_index("dp"), lax.axis_index("tensor")
    core, chip = t % 2, t // 2
    sibling = {"tensor": t + 1 - 2 * core}
    partner = {"tensor": (t + tensors // 2) % tensors}
    near, cross = {"dp": d + 1 - 2 * (d % 2)}, {"dp": 3 - d}
    outer = (d == 0) | (d == 3)
    other = {"section": 1 - section}
    hbm, probs_hbm, roots_hbm = jax.tree.unflatten(in_tree, hbm_in)
    starts = [matrix_starts(own) for own in hbm]

    plain = list(plain)
    views = []
    for b in range(2):
        fields = {}
        for name, value in hbm[b]._asdict().items():
            if name in Weights._fields:
                i = Weights._fields.index(name)
                fields[name] = work[b].raw.at[:, pl.ds(starts[b][i], starts[b][i + 1] - starts[b][i])]
            else:
                fields[name] = plain.pop(0)
        views.append(Needed(**fields))
    probs_in, roots = plain
    flat_views = jax.tree.leaves((tuple(views), probs_in, roots))
    flat_copies = [pltpu.make_async_copy(a, v, in_sem.at[i]) for i, (a, v) in enumerate(zip(hbm_in, flat_views))]
    loads, probs_copy, roots_copy = jax.tree.unflatten(in_tree, flat_copies)
    length = work[0].gf.shape[0]
    local_heads = probs_in.shape[1]
    blocks = hop_blocks(length)
    cot_copies = (
        pltpu.make_async_copy(cots[0], work[0].g, cot_sem.at[0]),
        pltpu.make_async_copy(cots[1], flipped, cot_sem.at[1]),
    )

    @pl.when(section == 1)
    def _():
        start(*cot_copies)

    roots_copy.start()
    for field in zip(loads[1], loads[0]):
        start(*field)
    probs_copy.start()
    greet(section, t, sections, tensors, (near, cross) if chain else ())

    part_length = text_out.shape[1]
    micro, page = core, chip
    kinds = ((grad_out, layout_grad_out), (text_out, layout_out))
    pages = ((work[0].g, flipped), ys)

    def page_part(g, q, a):
        span = pl.ds(q * part_length, part_length)
        return pages[g][a].at[span] if a == 0 else pages[g][a].at[:, span]

    def each_page(g, act):
        for q in range(tensors):
            for a in range(2):
                here = (micro == g) & (t == q)

                @pl.when((section == g) & here)
                def _():
                    act(g, q, a, True)

                @pl.when((section == g) & jnp.logical_not(here))
                def _():
                    act(g, q, a, False)

    def page_copy(g, q, a):
        return remote(
            page_part(g, q, a), kinds[g][a].at[page], page_send.at[q, a], page_recv.at[g, a, page],
            {"section": micro, "tensor": q},
        )

    def page_start(g, q, a, here):
        if here:
            pltpu.make_async_copy(page_part(g, q, a), kinds[g][a].at[page], page_recv.at[g, a, page]).start()
        else:
            page_copy(g, q, a).start()

    def page_sent(g, q, a, here):
        if not here:
            page_copy(g, q, a).wait_send()

    each_page(1, page_start)

    def hop(b, n):
        part = work[b].g.at[blocks[n]]
        return remote(part, part, hop_send.at[b, n], hop_recv.at[b, n], other)

    ahead = 3
    step = ROWS
    up_first, down_first = starts[0][2], starts[0][3]
    up_count, down_count = (starts[0][3] - up_first) // step, (starts[0][4] - down_first) // step
    n_feed = up_count + down_count
    chunks = [Chunk(0, k, up_first + k * step, step) for k in range(n_feed)]
    later = [(1, 0, starts[1][MATRICES])]
    later += [(0, f, n) for f, n in pieces_of(starts[0][1], 192)]
    later += [(0, starts[0][1] + f, n) for f, n in pieces_of(starts[0][2] - starts[0][1], 64)]
    chunks += [Chunk(b, n_feed + i, f, n) for i, (b, f, n) in enumerate(later)]

    def feed_chunk(k):
        return Chunk(0, k, pl.multiple_of(up_first + k * step, 16), step)

    def span(ref, c):
        return ref.at[pl.ds(c.first, c.rows)]

    def to_sibling(c, j):
        w = work[c.b]
        return remote(
            span(w.raw.at[2 * j + 1 - core], c), span(w.from_sibling.at[j], c),
            sib_send.at[c.index, j], sib_recv.at[c.index, j], sibling,
        )

    def mine(c):
        return span(work[c.b].raw.at[t], c)

    def theirs(c):
        return span(work[c.b].raw.at[2 * (1 - chip) + core], c)

    def to_partner(c):
        return remote(
            theirs(c), span(work[c.b].from_partner, c), send.at[0, c.index], recv.at[0, c.index], partner
        )

    def from_near(c):
        return span(work[c.b].from_sibling.at[0], c)

    def from_cross(c):
        return span(work[c.b].from_sibling.at[1], c)

    def to_near(c):
        return remote(mine(c), from_near(c), send.at[1, c.index], recv.at[1, c.index], near)

    def to_cross(c):
        return remote(mine(c), from_cross(c), send.at[2, c.index], recv.at[2, c.index], cross)

    def total_to_near(c):
        return remote(
            span(work[c.b].from_partner, c), from_near(c), send.at[3, c.index], recv.at[3, c.index], near
        )

    def out_copy(c, source):
        return pltpu.make_async_copy(span(source, c), span(results[c.b], c), out_sem.at[c.index])

    def added(target, *sources):
        target[...] = sum(s[...].astype(F32) for s in sources).astype(BF)

    def send_to_sibling(c):
        for j in range(tensors // 2):
            to_sibling(c, j).start()

    def stage_sibling(c):
        w = work[c.b]
        for j in range(tensors // 2):
            to_sibling(c, j).wait_recv()
        added(theirs(c), theirs(c), span(w.from_sibling.at[1 - chip], c))
        added(mine(c), mine(c), span(w.from_sibling.at[chip], c))
        if chain:
            @pl.when(jnp.logical_not(outer))
            def _():
                for device in (near, cross):
                    pl.semaphore_signal(credit, inc=1, device_id=device, device_id_type=MESH)

    def stage_partner(c):
        to_partner(c).wait_recv()
        added(mine(c), mine(c), span(work[c.b].from_partner, c))
        if not chain:
            out_copy(c, work[c.b].raw.at[t]).start()
            return

        @pl.when(outer)
        def _():
            pl.semaphore_wait(credit, 1)
            to_near(c).start()

    def stage_near(c):
        @pl.when(jnp.logical_not(outer))
        def _():
            to_near(c).wait_recv()
            added(mine(c), mine(c), from_near(c))
            pl.semaphore_wait(credit, 1)
            to_cross(c).start()

    def stage_cross(c):
        @pl.when(jnp.logical_not(outer))
        def _():
            to_cross(c).wait_recv()
            total = work[c.b].from_partner
            added(span(total, c), mine(c), from_cross(c))
            total_to_near(c).start()
            out_copy(c, total).start()

    def stage_total(c):
        @pl.when(outer)
        def _():
            total_to_near(c).wait_recv()
            out_copy(c, work[c.b].from_sibling.at[0]).start()

    def first_copies():
        for c in chunks[:ahead]:
            stage_sibling(c)
            to_partner(c).start()

    def turn_operands():
        wait(loads[0].low, loads[0].act)
        work[0].lowT[...] = views[0].low[...].T

    def feed_products():
        own, w = views[0], work[0]

        @pl.loop(0, up_count)
        def _(k):
            rows = pl.ds(pl.multiple_of(k * step, step), step)
            for q in range(tensors):
                w.raw[q, pl.ds(pl.multiple_of(up_first + k * step, 16), step), :] = dot(
                    w.lowT[rows, :], own.slope[q]
                ).astype(BF)
            send_to_sibling(feed_chunk(k))

        first_copies()

        @pl.loop(0, down_count)
        def _(k):
            lanes = pl.ds(pl.multiple_of(k * step, step), step)
            for q in range(tensors):
                w.raw[q, pl.ds(pl.multiple_of(down_first + k * step, 16), step), :] = dot(
                    own.act[q, :, lanes].T, w.gf[...]
                ).astype(BF)
            send_to_sibling(feed_chunk(up_count + k))

    def later_product(c):
        own, w = views[c.b], work[c.b]
        for q in range(tensors):
            for i in range(MATRICES):
                first = max(c.first, starts[c.b][i])
                last = min(c.first + c.rows, starts[c.b][i + 1])
                if first >= last:
                    continue
                rows = slice(first - starts[c.b][i], last - starts[c.b][i])
                if i == 0:
                    value = dot(own.qkv[q, rows, :], own.x[...])
                elif i == 1:
                    value = dot(own.ctx[q, rows, :], w.ga[...])
                elif i == 2:
                    value = dot(w.lowT[rows, :], own.slope[q])
                else:
                    value = dot(own.act[q, :, rows].T, w.gf[...])
                w.raw[q, first:last, :] = value.astype(BF)
        send_to_sibling(c)

    @pl.when(section == 1)
    def _():
        wait(*cot_copies)
        work[1].g[...] = flipped[...].T

    for b in range(2):
        work[b].sums[...] = jnp.zeros(work[b].sums.shape, F32)
    roots_copy.wait()

    def feed_back(n, block):
        for b in (1, 0):
            own, own_in, w, gain = views[b], loads[b], work[b], gains[b]
            if n == 0:
                wait(own_in.n2)

            if block in blocks:
                hop(b, n).wait_recv()

            for rows in small_blocks(block):
                g, normed = w.g[rows].astype(F32), own.n2[rows].astype(F32)
                low = norm_rows_back(g, normed, roots[rows, 2 * b + 1 : 2 * b + 2], gain[1:2])
                w.dz[rows] = low
                w.gf[rows] = low.astype(BF)
                w.sums[1:2] += jnp.sum(g * normed, axis=0, keepdims=True)
                w.sums[3:4] += jnp.sum(g, axis=0, keepdims=True)

            if n == 0:
                wait(own_in.downward, own_in.slope, own_in.upward)

            @pl.loop(0, tensors)
            def _(q):
                d_act = dot(w.gf[block], own.downward[q])
                d_pre = (d_act * own.slope[q, block].astype(F32)).astype(BF)
                own.slope[q, block] = d_pre
                w.dz[block] += dot(d_pre, own.upward[q])

            if n == 0:
                wait(own_in.n1, own_in.outward)
            for rows in small_blocks(block):
                g, normed = w.dz[rows], own.n1[rows].astype(F32)
                low = norm_rows_back(g, normed, roots[rows, 2 * b : 2 * b + 1], gain[0:1])
                w.dz[rows] = low
                w.ga[rows] = low.astype(BF)
                w.sums[0:1] += jnp.sum(g * normed, axis=0, keepdims=True)
                w.sums[2:3] += jnp.sum(g, axis=0, keepdims=True)
            gaT = w.ga[block].T
            for q in range(tensors):
                w.dctx[q, :, block] = dot(own.outward[q], gaT).astype(BF)

    @pl.when(section == 0)
    def _():
        turn_operands()
        for n, block in enumerate(blocks):
            feed_back(n, block)

    @pl.when(section == 1)
    def _():
        feed_back(0, slice(0, length))

    @pl.when(section == 0)
    def _():
        feed_products()

    for own_in in loads:
        wait(own_in.qkv, own_in.ctx, own_in.inv)
    wait(probs_copy)
    qkv = (views[0].qkv, views[1].qkv)
    text_rows, layout_rows = slice(0, HEAD_TEXT), slice(HEAD_TEXT, HEAD_TEXT + HEAD_LAYOUT)

    def turn(k, n_known):
        fixed = isinstance(k, int)

        def at(i, stage):
            if not fixed:
                pl.when((i >= 0) & (i < n_feed))(lambda: stage(feed_chunk(i)))
            elif 0 <= i < n_known:
                stage(chunks[i])

        def sibling_and_send(c):
            stage_sibling(c)
            to_partner(c).start()

        at(k + ahead, sibling_and_send)
        at(k, stage_partner)
        if chain:
            at(k - 2, stage_near)
            at(k - 4, stage_cross)
            at(k - 6, stage_total)

    early_turns = 6

    @pl.loop(0, tensors)
    def _(q):
        for local in range(local_heads):
            head = q * local_heads + local

            @pl.when((section == 0) & (head % 2 == 0) & (head < 2 * early_turns))
            def _():
                turn(head // 2, n_feed)

            inv = views[0].inv[q, local : local + 1, :]
            scaled = [
                (work[s].dctx[q, local * SIZES[s] : (local + 1) * SIZES[s], :].astype(F32) * inv).astype(BF)
                for s in range(2)
            ]
            inner = [
                jnp.sum(
                    scaled[s].astype(F32)
                    * views[s].ctx[q, local * SIZES[s] : (local + 1) * SIZES[s], :].astype(F32),
                    axis=0, keepdims=True,
                )
                for s in range(2)
            ]
            rows16 = lax.broadcasted_iota(jnp.int32, (16, length), 0)
            extra = jnp.zeros((16, length), F32)
            for i, value in enumerate((inner[0] + inner[1], inner[1])):
                high = value.astype(BF).astype(F32)
                extra = jnp.where(rows16 == 2 * i, -high, extra)
                extra = jnp.where(rows16 == 2 * i + 1, high - value, extra)
            pad = jnp.zeros((128 - sum(SIZES) - 16, length), BF)
            dcT = jnp.concatenate([*scaled, extra.astype(BF), pad], axis=0)
            dc = dcT.T
            qT, kT = (head_rows(qkv, q, kind, local, SCALES if kind == 0 else None) for kind in range(2))
            v_text, v_layout = (head_part(qkv, q, 2, local, s) for s in range(2))
            one, other_one = (((rows16 // 2) == i).astype(F32).astype(BF) for i in range(2))
            low = probs_in[q, local]
            probs = low.astype(F32)
            both = dot(dc, jnp.concatenate([v_text, v_layout, one, pad], axis=0))
            ds_both = (probs * both).astype(BF)
            single = dot(dc, jnp.concatenate([jnp.zeros_like(v_text), v_layout, other_one, pad], axis=0))
            ds_layout = (probs * single).astype(BF)
            dvT = dot(dcT, low)
            put_head(qkv, q, 2, local, 0, dvT[text_rows])
            put_head(qkv, q, 2, local, 1, dvT[layout_rows])
            k = kT.T
            lane = lax.broadcasted_iota(jnp.int32, (length, 128), 1)
            dq = jnp.where(lane < HEAD_TEXT, dot(ds_both, k) * SCALES[0], dot(ds_layout, k) * SCALES[1])
            dqT = dq.astype(BF).T
            put_head(qkv, q, 0, local, 0, dqT[text_rows])
            put_head(qkv, q, 0, local, 1, dqT[layout_rows])
            put_head(qkv, q, 1, local, 0, dot(qT[text_rows], ds_both))
            put_head(qkv, q, 1, local, 1, dot(qT[layout_rows], ds_layout))

    wait(loads[0].project, loads[1].project)
    page_sum = jnp.zeros((1, work[0].dz.shape[1]), F32)
    for n, block in enumerate(blocks):
        for b in (1, 0):
            down = work[b].dz[block]
            for q in range(tensors):
                down += dot(qkv[b][q, :, block].T, views[b].project[q])
            down = down.astype(BF)
            work[b].g[block] = down
            if b == 0:
                page_sum += jnp.sum(down.astype(F32), axis=0, keepdims=True)

            @pl.when(section == 1)
            def _():
                hop(b, n).start()

    wait(loads[1].low, loads[1].act)
    work[1].lowT[...] = views[1].low[...].T
    for own_in in loads:
        wait(own_in.x)
    @pl.when(section == 1)
    def _():
        turn_operands()
        feed_products()

    for c in chunks[n_feed:]:
        later_product(c)

    @pl.when(section == 0)
    def _():
        flipped[...] = work[1].g[...].T
        each_page(0, page_start)

    at_page = (lax.broadcasted_iota(jnp.int32, lang_ids.shape, 0) == t % 2) & (
        lax.broadcasted_iota(jnp.int32, lang_ids.shape, 1) == t // 2
    )
    group = jnp.sum(jnp.where(at_page, lang_ids[...], 0), axis=(0, 1), keepdims=True)
    n_lang = small_out.shape[1] - 8
    chosen = (lax.broadcasted_iota(jnp.int32, (n_lang, 1), 0) == group) & (section == 0)
    small_sum[0, 0:n_lang] = jnp.where(chosen, page_sum, 0.0)
    small_sum[0, n_lang : n_lang + 4] = work[0].sums[...]
    small_sum[0, n_lang + 4 : n_lang + 8] = jnp.zeros((4, small_out.shape[2]), F32)
    small_sum[0, n_lang + 4 : n_lang + 8, : work[1].sums.shape[1]] = work[1].sums[...]

    def small_copy(i, device):
        return remote(small_sum.at[i], small_got.at[i], small_send.at[i], small_recv.at[i], device)

    if chain:
        small_copy(0, sibling).start()
    @pl.when(section == 1)
    def _():
        @pl.loop(0, early_turns)
        def _(k):
            turn(k, n_feed)

    for k in range(early_turns, len(chunks) + (6 if chain else 0)):
        turn(k, len(chunks))
        if not chain:
            continue
        if k == early_turns:
            small_copy(0, sibling).wait_recv()
            small_sum[1] = small_sum[0] + small_got[0]
            small_copy(1, partner).start()
        if k == early_turns + 1:
            small_copy(1, partner).wait_recv()
            small_sum[2] = small_sum[1] + small_got[1]
            small_copy(2, near).start()
        if k == early_turns + 2:
            small_copy(2, near).wait_recv()
            small_sum[3] = small_sum[2] + small_got[2]

            @pl.when(jnp.logical_not(outer))
            def _():
                small_copy(3, cross).start()

        if k == early_turns + 4:
            @pl.when(jnp.logical_not(outer))
            def _():
                small_copy(3, cross).wait_recv()
                small_sum[4] = small_sum[3] + small_got[3]
                small_copy(4, near).start()

        if k == early_turns + 6:
            @pl.when(outer)
            def _():
                small_copy(4, near).wait_recv()
                small_sum[4] = small_got[4]

            small_sum[5] = small_sum[4]
            small_copy(5, other).start()

    if chain:
        for i, device in enumerate((sibling, partner, near)):
            small_copy(i, device).wait_send()

        @pl.when(jnp.logical_not(outer))
        def _():
            small_copy(3, cross).wait_send()
            small_copy(4, near).wait_send()

        small_copy(5, other).wait()
        small_out[0] = small_sum[5]
        small_out[1] = small_got[5]
    else:
        small_out[0] = small_sum[0]
        small_out[1] = small_sum[0]

    @pl.when(section == 1)
    def _():
        for b in range(2):
            for n in range(len(blocks)):
                hop(b, n).wait_send()

    for c in chunks:
        for j in range(tensors // 2):
            to_sibling(c, j).wait_send()
        to_partner(c).wait_send()
        if not chain:
            out_copy(c, work[c.b].from_partner).wait()
            continue

        @pl.when(outer)
        def _():
            to_near(c).wait_send()

        @pl.when(jnp.logical_not(outer))
        def _():
            to_cross(c).wait_send()
            total_to_near(c).wait_send()

        out_copy(c, work[c.b].from_partner).wait()

    for g in range(sections):
        each_page(g, page_sent)
        for a in range(2):
            for j in range(2):
                dst = kinds[g][a].at[j]
                remote(dst, dst, page_send.at[0, a], page_recv.at[g, a, j], partner).wait_recv()
    landed = (text_out, layout_out, grad_out, layout_grad_out)
    copies = [pltpu.make_async_copy(v, h, page_out_sem.at[i]) for i, (v, h) in enumerate(zip(landed, page_outs))]
    start(*copies)
    wait(*copies)


def layer_backward(mesh, x, y, probs, roots, kept, weights, cots, norms, lang_ids, n_lang):
    sections, dp, tensors = mesh.shape["section"], mesh.shape["dp"], mesh.shape["tensor"]
    chain = dp == 4
    needed = tuple(
        Needed(
            n2=k.n2, downward=w.downward, slope=k.slope, upward=w.upward, n1=k.n1,
            outward=w.outward, low=k.low, act=k.act, qkv=k.qkv, ctx=k.ctx, inv=k.inv, project=w.project, x=rows,
        )
        for k, w, rows in zip(kept, weights, x)
    )
    flat_in, in_tree = jax.tree.flatten((needed, probs, roots))
    plain = [v for own in needed for name, v in own._asdict().items() if name not in Weights._fields] + [probs, roots]
    stacks = [(matrix_starts(own)[MATRICES], rows.shape[1]) for own, rows in zip(needed, x)]
    length = x[0].shape[0]
    work = []
    for own, rows, (count, width) in zip(needed, x, stacks):
        work += Work(
            g=shape(rows.shape), gf=shape(rows.shape), ga=shape(rows.shape), dz=shape(rows.shape, F32),
            dctx=shape(own.ctx.shape), sums=shape((4, width), F32), lowT=shape((width, length)),
            raw=shape((tensors, count, width)), from_sibling=shape((tensors // 2, count, width)),
            from_partner=shape((count, width)),
        )
    small = shape((2, n_lang + 8, x[0].shape[1]), F32)
    text_page = shape((2, length // tensors, x[0].shape[1]))
    layout_page = shape((2, x[1].shape[1], length // tensors))
    summed = [shape(s) for s in stacks]
    own = needed[0]
    n_feed = (own.upward.shape[1] + own.downward.shape[1]) // ROWS
    n_chunks = n_feed + 1 + own.project.shape[1] // 192 + own.outward.shape[1] // 64
    n_blocks = len(hop_blocks(length))
    dma = pltpu.SemaphoreType.DMA
    results = pl.pallas_call(
        functools.partial(backward_kernel, sections, tensors, chain, in_tree),
        out_shape=summed + [small, text_page, layout_page, text_page, layout_page],
        in_specs=[ANY] * (len(flat_in) + 4) + [VMEM] * 3,
        out_specs=[ANY] * 2 + [VMEM] + [ANY] * 4,
        scratch_shapes=vmem_like(work) + vmem_like(plain)
        + [pltpu.VMEM(cots[1].shape, BF)] + [pltpu.VMEM((6,) + small.shape[1:], F32)] * 2
        + vmem_like([text_page, layout_page] * 2)
        + [dma((len(flat_in),)), dma((2,)), dma((2, n_blocks)), dma((2, n_blocks))]
        + [dma((n_chunks, tensors // 2))] * 2 + [dma((4, n_chunks))] * 2
        + [pltpu.SemaphoreType.REGULAR, dma((n_chunks,))]
        + [dma((6,))] * 2 + [dma((tensors, 2)), dma((sections, 2, 2)), dma((4,))],
        compiler_params=pltpu.CompilerParams(
            collective_id=1, has_side_effects=True, vmem_limit_bytes=64 << 20
        ),
        name="layer_backward",
    )(*flat_in, *cots, *y, lang_ids, norms[0][0], norms[1][0])
    totals, small, pages = results[:2], results[2], results[3:7]
    if not chain:
        totals = lax.psum(tuple(totals), "dp")
        both = lax.psum(small[0], ("dp", "tensor"))
        small = jnp.stack([both, lax.ppermute(both, "section", [(0, 1), (1, 0)])])
    return totals, small, pages


def widen_kernel(n_in, n_pages, *refs):
    n_out = 5 + n_pages + 2 * MATRICES
    hbm_in, hbm_out = refs[:n_in], refs[n_in : n_in + n_out]
    vmem_in, vmem_out = refs[n_in + n_out : 2 * n_in + n_out], refs[2 * n_in + n_out : -2]
    in_sem, out_sem = refs[-2:]
    loads = [pltpu.make_async_copy(h, v, in_sem.at[i]) for i, (h, v) in enumerate(zip(hbm_in, vmem_in))]
    sources = vmem_out[:5] + vmem_in[3:] + vmem_out[5:]
    stores = [pltpu.make_async_copy(v, h, out_sem.at[i]) for i, (v, h) in enumerate(zip(sources, hbm_out))]
    start(*loads)
    totals, small = vmem_in[0:2], vmem_in[2]
    for b in range(2):
        wait(loads[b])
        at = 0
        for i in range(b * MATRICES, (b + 1) * MATRICES):
            out = vmem_out[5 + i]
            for c in range(0, out.shape[0], 48):
                out[c : c + 48] = totals[b][at + c : at + c + 48].astype(F32)
            at += out.shape[0]
            stores[5 + n_pages + i].start()
    for i in range(n_pages):
        loads[3 + i].wait()
        stores[5 + i].start()
    loads[2].wait()
    n_lang = vmem_out[0].shape[0]
    vmem_out[0][...] = jnp.where(lax.axis_index("section") == 0, small[0, :n_lang], small[1, :n_lang])
    for i, out in enumerate(vmem_out[1:5]):
        first = n_lang + 2 * i
        out[...] = small[0, first : first + 2, : out.shape[1]]
    start(*stores[:5])
    wait(*stores)


def widen(totals, small, pages, shards, n_lang):
    widths = [total.shape[1] for total in totals]
    sums = [shape((n_lang, widths[0]), F32)] + [shape((2, w), F32) for w in widths for _ in range(2)]
    grads = [shape(m.shape, F32) for own in shards for m in own]
    inputs = (*totals, small, *pages)
    outs = sums + [shape(page.shape) for page in pages] + grads
    results = pl.pallas_call(
        functools.partial(widen_kernel, len(inputs), len(pages)), out_shape=outs,
        in_specs=[ANY] * len(inputs), out_specs=[ANY] * len(outs),
        scratch_shapes=vmem_like(inputs) + vmem_like(sums + grads)
        + [pltpu.SemaphoreType.DMA((len(inputs),)), pltpu.SemaphoreType.DMA((len(outs),))],
        compiler_params=pltpu.CompilerParams(vmem_limit_bytes=62 << 20), name="widen",
    )(*inputs)
    return results[0], results[1:5], results[5:9], results[9:13], results[13:17]


def per_device(
    mesh,
    text_input,
    layout_input,
    text_cotangent,
    layout_cotangent,
    page_counts,
    pad_mask,
    lang_ids,
    lang_table,
    text_project,
    text_outward,
    text_upward,
    text_downward,
    text_gains,
    text_biases,
    layout_project,
    layout_outward,
    layout_upward,
    layout_downward,
    layout_gains,
    layout_biases,
):
    def flat(project):
        return jnp.transpose(project[0], (1, 2, 0)).reshape(-1, project.shape[1])

    def flipped(block):
        return jnp.transpose(block[0], (0, 2, 1))

    shards = (
        Weights(flat(text_project), text_outward[0], text_upward[0], text_downward[0]),
        Weights(flat(layout_project), layout_outward[0], layout_upward[0], layout_downward[0]),
    )
    norms = ((text_gains[0], text_biases[0]), (layout_gains[0], layout_biases[0]))
    marks = (pad_mask, page_counts, lang_ids, lang_table)
    (x, y, probs, roots, kept, weights), cots = layer_forward(
        mesh, text_input[0], flipped(layout_input), text_cotangent[0], flipped(layout_cotangent), shards, norms, marks
    )
    n_lang = lang_table.shape[0]
    totals, small, pages = layer_backward(mesh, x, y, probs, roots, kept, weights, cots, norms, lang_ids, n_lang)
    lang_sum, norm_sums, pages, text_sums, layout_sums = widen(totals, small, pages, shards, n_lang)
    text_out, layout_out, text_grad, layout_grad = pages

    def unflat(grad, like):
        return jnp.transpose(grad.reshape(like.shape[2], like.shape[3], like.shape[1]), (2, 0, 1))[None]

    unflip = lambda block: jnp.transpose(block, (0, 2, 1))[None]
    return (
        text_out[None], unflip(layout_out), text_grad[None], unflip(layout_grad), lang_sum,
        unflat(text_sums[0], text_project), *(s[None] for s in text_sums[1:]), norm_sums[0][None], norm_sums[1][None],
        unflat(layout_sums[0], layout_project), *(s[None] for s in layout_sums[1:]),
        norm_sums[2][None], norm_sums[3][None],
    )


def solution(mesh):
    tokens = P("section", "dp", "tensor", None)
    weight_specs = (
        P("section", None, None, "tensor"), P("section", "tensor", None), P("section", None, "tensor"),
        P("section", "tensor", None), P("section", None, None), P("section", None, None),
    )
    in_specs = (tokens,) * 4 + (P(None, "dp"), P(None, "dp", None), P(None, "dp"), P()) + weight_specs * 2
    out_specs = (tokens,) * 4 + (P(),) + weight_specs * 2
    return jax.shard_map(
        functools.partial(per_device, mesh), mesh=mesh, in_specs=in_specs, out_specs=out_specs, check_vma=False
    )
```

```python
import functools
import math
import typing

import jax
import jax.numpy as jnp
from jax import lax
from jax.experimental import pallas as pl
from jax.experimental.pallas import tpu as pltpu
from jax.sharding import PartitionSpec as P

HEAD_TEXT = 64
HEAD_LAYOUT = 16
EPSILON = 1e-05
NEGATIVE = -1e30
HIGH = lax.Precision.HIGHEST
MESH = pl.DeviceIdType.MESH
BF = jnp.bfloat16
F32 = jnp.float32
ANY = pl.BlockSpec(memory_space=pl.ANY)


def remote(src, dst, send, recv, device):
    return pltpu.make_async_remote_copy(
        src_ref=src, dst_ref=dst, send_sem=send, recv_sem=recv, device_id=device, device_id_type=MESH
    )


def greet(section, tensor, sections, tensors, extra=()):
    barrier = pltpu.get_barrier_semaphore()
    for g in range(sections):
        for q in range(tensors):

            @pl.when((section != g) | (tensor != q))
            def _():
                pl.semaphore_signal(
                    barrier, inc=1, device_id={"section": g, "tensor": q}, device_id_type=MESH
                )

    for device in extra:
        pl.semaphore_signal(barrier, inc=1, device_id=device, device_id_type=MESH)
    pl.semaphore_wait(barrier, sections * tensors - 1 + len(extra))


GELU_P = 0.3275911
GELU_A = (0.254829592, -0.284496736, 1.421413741, -1.453152027, 1.061405429)
NN = (((1,), (0,)), ((), ()))
NT = (((1,), (1,)), ((), ()))
SCALES = (1.0 / math.sqrt(HEAD_TEXT), 1.0 / math.sqrt(HEAD_LAYOUT))
SIZES = (HEAD_TEXT, HEAD_LAYOUT)
ROWS = 128


class Weights(typing.NamedTuple):
    project: typing.Any
    outward: typing.Any
    upward: typing.Any
    downward: typing.Any


class Kept(typing.NamedTuple):
    qkv: typing.Any
    ctx: typing.Any
    inv: typing.Any
    n1: typing.Any
    low: typing.Any
    act: typing.Any
    slope: typing.Any
    n2: typing.Any


def dot(a, b, dims=NN):
    return lax.dot_general(a, b, dims, preferred_element_type=F32)


def gelu_pair(u):
    d = 1.0 + (GELU_P / math.sqrt(2.0)) * jnp.abs(u)
    t = pl.reciprocal(d, approx=True)
    t = t * (2.0 - d * t)
    e = jnp.exp2((u * u) * (-0.5 / math.log(2.0)))
    a1, a2, a3, a4, a5 = (0.5 * a for a in GELU_A)
    tail = ((((a5 * t + a4) * t + a3) * t + a2) * t + a1) * t * e
    cdf = jnp.where(u >= 0, 1.0 - tail, tail)
    return u * cdf, cdf + u * e * (1.0 / math.sqrt(2.0 * math.pi))


def norm_rows(z, gain, offset):
    center = z - jnp.mean(z, axis=-1, keepdims=True)
    inverse = lax.rsqrt(jnp.mean(center * center, axis=-1, keepdims=True) + EPSILON)
    normed = center * inverse
    return normed * gain + offset, normed, inverse


def norm_rows_back(g, n, r, gain):
    t = g * gain
    return r * (t - jnp.mean(t, axis=-1, keepdims=True) - n * jnp.mean(t * n, axis=-1, keepdims=True))


class Staged:
    def __init__(self, tree, hbm, vmem, sem, inward):
        self.tree, self.vmem = tree, list(vmem)
        pairs = zip(hbm, vmem) if inward else zip(vmem, hbm)
        self.copies = [pltpu.make_async_copy(a, b, sem.at[i]) for i, (a, b) in enumerate(pairs)]

    def refs(self):
        return jax.tree.unflatten(self.tree, self.vmem)

    def parts(self):
        return jax.tree.unflatten(self.tree, self.copies)

    def start(self):
        for copy in self.copies:
            copy.start()

    def wait(self):
        for copy in self.copies:
            copy.wait()


def start(*copies):
    for copy in copies:
        copy.start()


def wait(*copies):
    for copy in copies:
        copy.wait()


def head_rows(stacks, slot, kind, local, scales=None, extra=None):
    rows = []
    for b in range(2):
        piece = head_part(stacks, slot, kind, local, b)
        rows.append(piece if scales is None else piece * BF(scales[b]))
    length = rows[0].shape[1]
    rows.append(jnp.zeros((16, length), BF) if extra is None else extra)
    rows.append(jnp.zeros((128 - sum(SIZES) - 16, length), BF))
    return jnp.concatenate(rows, axis=0)


def head_part(stacks, slot, kind, local, b):
    first = kind * (stacks[b].shape[1] // 3) + local * SIZES[b]
    return stacks[b][slot, first : first + SIZES[b], :]


def small_blocks(block, step=64):
    return [slice(c, c + step) for c in range(block.start, block.stop, step)]


def put_head(stacks, slot, kind, local, b, value):
    first = kind * (stacks[b].shape[1] // 3) + local * SIZES[b]
    stacks[b][slot, first : first + SIZES[b], :] = value.astype(BF)


def hop_blocks(length):
    ends = [0, length // 2, length * 3 // 4, length]
    return [slice(a, b) for a, b in zip(ends, ends[1:])]


def slot_of(u, core, chip):
    return ((chip + u // 2) % 2) * 2 + (core + u % 2) % 2


def forward_kernel(sections, tensors, shared, in_tree, out_tree, *refs):
    n_w, n_out = len(shared), out_tree.num_leaves
    sources = (refs[0:2], refs[2:4])
    shards = refs[4 : 4 + n_w]
    pad_mask, counts, lang_ids, lang_table, *norms = refs[4 + n_w : 12 + n_w]
    rest = refs[12 + n_w :]
    hbm_out, cots_out, rest = rest[:n_out], rest[n_out : n_out + 2], rest[n_out + 2 :]
    outgoing = Staged(out_tree, hbm_out, rest[:n_out], rest[n_out], False)
    rest = rest[n_out + 1 :]
    flipped, raw_x, y_narrow, *rest = rest
    nats, totals, pre, score_buffer, rest = rest[0:2], rest[2:4], rest[4:6], rest[6], rest[7:]
    xT, turned, turn_sem, rest = rest[0:2], (rest[2:4], rest[4:6]), rest[6], rest[7:]
    page_send, page_recv, w_send, w_recv, own_sem, hop_send, hop_recv, cot_sem, act_sem = rest
    x, y_pages, probs_out, roots, kept, weights = outgoing.refs()
    y = (y_pages[0], y_narrow)
    x_out, y_out, probs_copy, roots_copy, kept_out, weights_out = outgoing.parts()
    kept_hbm, weights_hbm = jax.tree.unflatten(out_tree, list(hbm_out))[4:6]
    section, d, t = lax.axis_index("section"), lax.axis_index("dp"), lax.axis_index("tensor")
    core, chip, half_index = t % 2, t // 2, d % 2
    sibling, partner = t + 1 - 2 * core, (t + tensors // 2) % tensors
    mate = d + 1 - 2 * half_index
    micro, page = core, chip
    part_length = sources[0][0].shape[1]
    length = x[0].shape[0]
    blocks = [slice(c, c + 2 * ROWS) for c in range(0, length, 2 * ROWS)]
    parts = hop_blocks(length)
    full = (
        weights[0].project, weights[1].project, weights[0].outward, weights[0].upward,
        weights[0].downward, weights[1].outward, weights[1].upward, weights[1].downward,
    )
    greet(section, t, sections, tensors, ({"dp": mate},) if any(shared) else ())

    def half_of(ref, i, which):
        count = shards[i].shape[0] // 2
        return ref.at[pl.ds(pl.multiple_of(which * count, 16), count)] if shared[i] else ref

    def to_partner(i):
        return remote(
            half_of(shards[i], i, half_index), half_of(full[i].at[t], i, half_index),
            w_send.at[0, i], w_recv.at[0, i], {"tensor": partner},
        )

    def to_sibling(i):
        return remote(full[i].at[t], full[i].at[t], w_send.at[1, i], w_recv.at[1, i], {"tensor": sibling})

    def to_mate(i):
        ref = half_of(full[i].at[partner], i, half_index)
        return remote(ref, ref, w_send.at[2, i], w_recv.at[2, i], {"dp": mate})

    def on_first(i):
        ref = half_of(full[i].at[partner], i, half_index)
        return remote(ref, ref, w_send.at[3, i], w_recv.at[3, i], {"tensor": sibling})

    def on_second(i):
        ref = half_of(full[i].at[partner], i, 1 - half_index)
        return remote(ref, ref, w_send.at[4, i], w_recv.at[4, i], {"tensor": sibling})

    def keep(i):
        return pltpu.make_async_copy(shards[i], full[i].at[t], own_sem.at[i])

    def relay(*which):
        for i in which:
            to_partner(i).wait_recv()
            if shared[i]:
                to_mate(i).start()
            on_first(i).start()

    def relay_second(*which):
        for i in which:
            if shared[i]:
                to_mate(i).wait_recv()
                on_second(i).start()

    def early(*which):
        for i in which:
            to_sibling(i).wait_recv()

    def late(*which):
        for i in which:
            on_first(i).wait_recv()
            if shared[i]:
                on_second(i).wait_recv()

    def token_slot(g, a, index):
        start_at = pl.multiple_of(index * part_length, part_length)
        target = (raw_x, flipped)[a]
        return target.at[pl.ds(start_at, part_length)] if a == 0 else target.at[:, pl.ds(start_at, part_length)]

    def over_pages(g, act):
        for j in range(2):
            target = 2 * j + section
            here = (section == g) & (t == target)
            for a in range(2):
                act(g, j, a, target, here)

    def page_copy(g, j, a, target):
        return remote(
            sources[g][a].at[j], token_slot(g, a, t), page_send.at[g, j, a], page_recv.at[a, t],
            {"section": g, "tensor": target},
        )

    def page_start(g, j, a, target, here):
        @pl.when(here)
        def _():
            pltpu.make_async_copy(sources[g][a].at[j], token_slot(g, a, t), page_recv.at[a, t]).start()

        @pl.when(jnp.logical_not(here))
        def _():
            page_copy(g, j, a, target).start()

    def page_sent(g, j, a, target, here):
        @pl.when(jnp.logical_not(here))
        def _():
            page_copy(g, j, a, target).wait_send()

    def pages_arrived(g):
        for a in range(2):
            for q in range(tensors):
                slot = token_slot(g, a, q)
                remote(slot, slot, page_send.at[0, 0, a], page_recv.at[a, q], {"tensor": sibling}).wait_recv()

    def hop(b, n):
        return remote(
            y[b].at[parts[n]], x[b].at[parts[n]], hop_send.at[b, n], hop_recv.at[b, n], {"section": 1 - section}
        )

    def weights_to_hbm():
        for b in range(2):
            start(weights_out[b].project, weights_out[b].outward)
            for q in range(tensors):
                for m, name in enumerate((2, 3)):
                    copy = pltpu.make_async_copy(
                        turned[b][m].at[q % 2], weights_hbm[b][name].at[q], turn_sem.at[b, m, q % 2]
                    )
                    if q >= 2:
                        copy.wait()
                    turned[b][m][q % 2] = weights[b][name][q].T
                    copy.start()
        for b in range(2):
            for q in range(tensors - 2, tensors):
                for m, name in enumerate((2, 3)):
                    pltpu.make_async_copy(
                        turned[b][m].at[q % 2], weights_hbm[b][name].at[q], turn_sem.at[b, m, q % 2]
                    ).wait()

    over_pages(0, page_start)
    for i in range(n_w):
        keep(i).start()
    for i in range(n_w):
        to_partner(i).start()
    over_pages(1, page_start)
    for i in range(n_w):
        keep(i).wait()
        to_sibling(i).start()

    at_page = (lax.broadcasted_iota(jnp.int32, counts.shape, 0) == micro) & (
        lax.broadcasted_iota(jnp.int32, counts.shape, 1) == page
    )

    def own_entry(ref):
        return jnp.sum(jnp.where(at_page, ref[...], 0), axis=(0, 1), keepdims=True)

    positions = lax.broadcasted_iota(jnp.int32, (1, length), 1)
    mask_row = pad_mask[micro, pl.ds(page, 1), :]
    key_mask = (positions < own_entry(counts)) & ((mask_row == 1) | (positions == 0))
    first_row = (lax.broadcasted_iota(jnp.int32, (16, length), 0) == 0).astype(F32)
    mask_row16 = (first_row * jnp.where(key_mask, 0.0, NEGATIVE)).astype(BF)
    groups = lax.broadcasted_iota(jnp.int32, (lang_table.shape[0], 1), 0)
    lang_row = jnp.sum(jnp.where(groups == own_entry(lang_ids), lang_table[...], 0.0), axis=0, keepdims=True)
    local_heads = weights[0].project.shape[1] // (3 * HEAD_TEXT)
    qkv = (kept[0].qkv, kept[1].qkv)

    @pl.when(section == 0)
    def _():
        pages_arrived(0)
        x[0][...] = (raw_x[...].astype(F32) + lang_row).astype(BF)
        x[1][...] = flipped[...].T
        early(0, 1)

    @pl.when(section == 1)
    def _():
        relay(*range(n_w))
        relay_second(*range(n_w))
        early(*range(n_w))
        late(*range(n_w))
        weights_to_hbm()

    @pl.loop(0, 2)
    def _(half):
        @pl.when((half == 1) & (section == 0))
        def _():
            relay(0, 1)
            relay_second(0)
            late(0, 1)

        for n, block in enumerate(parts):
            @pl.when((half == 0) & (section == 1))
            def _():
                for b in range(2):
                    hop(b, n).wait_recv()

            @pl.when(half == 0)
            def _():
                for b in range(2):
                    xT[b][:, block] = x[b][block].T

            @pl.loop(0, 2)
            def _(u):
                slot = slot_of(2 * half + u, core, chip)
                for b in range(2):
                    qkv[b][slot, :, block] = dot(weights[b].project[slot], xT[b][:, block]).astype(BF)

        @pl.loop(0, 2)
        def _(u):
            slot = slot_of(2 * half + u, core, chip)
            for local in range(local_heads):
                q = head_rows(qkv, slot, 0, local, SCALES, first_row.astype(BF)).T
                kT = head_rows(qkv, slot, 1, local, None, mask_row16)
                score_buffer[local] = dot(q, kT)
                for rows in small_blocks(slice(0, length)):
                    scores = score_buffer[local, rows, :]
                    raised = jnp.exp(scores - jnp.max(scores, axis=-1, keepdims=True))
                    probs_out[slot, local, rows, :] = raised.astype(BF)
                vT = head_rows(qkv, slot, 2, local, None, first_row.astype(BF))
                ctx = dot(probs_out[slot, local], vT.T).T
                inv = 1.0 / ctx[sum(SIZES) : sum(SIZES) + 1]
                ctx = (ctx * inv).astype(BF)
                kept[0].inv[slot, local : local + 1, :] = inv
                kept[0].ctx[slot, local * HEAD_TEXT : (local + 1) * HEAD_TEXT, :] = ctx[:HEAD_TEXT]
                kept[1].ctx[slot, local * HEAD_LAYOUT : (local + 1) * HEAD_LAYOUT, :] = ctx[
                    HEAD_TEXT : HEAD_TEXT + HEAD_LAYOUT
                ]

    kept[1].inv[...] = jnp.zeros(kept[1].inv.shape, F32)
    start(probs_copy, *x_out, *(c for k in kept_out for c in (k.qkv, k.ctx, k.inv)))

    def attend(b):
        gains, biases = norms[2 * b : 2 * b + 2]
        width = x[b].shape[1]
        nats[b][...] = kept[b].ctx[...].reshape(width, length).T
        wide = weights[b].outward[...].reshape(width, width)
        for block in blocks:
            totals[b][1, block] = dot(nats[b][block], wide)
            for rows in small_blocks(block):
                h, n, r = norm_rows(x[b][rows].astype(F32) + totals[b][1, rows], gains[0:1], biases[0:1])
                totals[b][0, rows] = h
                totals[b][1, rows] = jnp.zeros(h.shape, F32)
                kept[b].n1[rows] = n.astype(BF)
                roots[rows, 2 * b : 2 * b + 1] = r
                kept[b].low[rows] = h.astype(BF)
        start(kept_out[b].n1, kept_out[b].low)

    def slot_copies(b, slot):
        return [
            pltpu.make_async_copy(v.at[slot], h.at[slot], act_sem.at[b, m, slot])
            for m, (v, h) in enumerate(((kept[b].act, kept_hbm[b].act), (kept[b].slope, kept_hbm[b].slope)))
        ]

    def feed(b, first, which):
        @pl.loop(first, first + 2)
        def _(u):
            slot = slot_of(u, core, chip)
            for block in which:
                pre[b][block] = dot(kept[b].low[block], weights[b].upward[slot])
                for rows in small_blocks(block, 16):
                    act, slope = gelu_pair(pre[b][rows])
                    kept[b].act[slot, rows] = act.astype(BF)
                    kept[b].slope[slot, rows] = slope.astype(BF)
                totals[b][1, block] += dot(kept[b].act[slot, block], weights[b].downward[slot])
                if block == slice(0, length):
                    start(*slot_copies(b, slot))

    def finish(b):
        gains, biases = norms[2 * b : 2 * b + 2]
        def last(block):
            feed(b, 2, [block])
            for rows in small_blocks(block):
                out, normed, r = norm_rows(totals[b][0, rows] + totals[b][1, rows], gains[1:2], biases[1:2])
                y[b][rows] = out.astype(BF)
                kept[b].n2[rows] = normed.astype(BF)
                roots[rows, 2 * b + 1 : 2 * b + 2] = r

        @pl.when(section == 0)
        def _():
            for n, block in enumerate(parts):
                last(block)
                hop(b, n).start()
            for u in range(2, 4):
                start(*slot_copies(b, slot_of(u, core, chip)))

        @pl.when(section == 1)
        def _():
            last(slice(0, length))

        if b == 1:
            y_pages[1][...] = y_narrow[...].T
        start(y_out[b], kept_out[b].n2)

    @pl.when(section == 0)
    def _():
        relay(2, 3)
        early(2)
        late(2)

    attend(0)

    @pl.when(section == 0)
    def _():
        early(3, 4)

    feed(0, 0, [slice(0, length)])

    @pl.when(section == 0)
    def _():
        relay(4, 5, 6, 7)
        relay_second(3)
        early(5, 6, 7)
        late(5, 6, 7)

    attend(1)
    feed(1, 0, [slice(0, length)])
    finish(1)

    @pl.when(section == 0)
    def _():
        relay_second(4)
        late(3, 4)

    finish(0)
    start(roots_copy)

    @pl.when(section == 0)
    def _():
        weights_to_hbm()
        for b in range(2):
            for n in range(len(parts)):
                hop(b, n).wait_send()

    for i in range(n_w):
        to_partner(i).wait_send()
        to_sibling(i).wait_send()
        on_first(i).wait_send()
        if shared[i]:
            to_mate(i).wait_send()
            on_second(i).wait_send()
    for g in range(sections):
        over_pages(g, page_sent)

    @pl.when(section == 1)
    def _():
        pages_arrived(1)
        copies = [pltpu.make_async_copy(v, h, cot_sem.at[i]) for i, (v, h) in enumerate(zip((raw_x, flipped), cots_out))]
        start(*copies)
        wait(*copies)

    for group in (x_out, y_out, (probs_copy, roots_copy), *(w[:2] for w in weights_out)):
        wait(*group)
    for b, k in enumerate(kept_out):
        wait(k.qkv, k.ctx, k.inv, k.n1, k.low, k.n2)
        for slot in range(tensors):
            wait(*slot_copies(b, slot))


def vmem_like(tree):
    return [pltpu.VMEM(s.shape, s.dtype) for s in jax.tree.leaves(tree)]


VMEM = pl.BlockSpec(memory_space=pltpu.VMEM)


def shape(dims, dtype=BF):
    return jax.ShapeDtypeStruct(tuple(dims), dtype)


def layer_forward(mesh, text_in, layout_in, text_cot, layout_cot, shards, norms, marks):
    sections, dp, tensors = mesh.shape["section"], mesh.shape["dp"], mesh.shape["tensor"]
    length = text_in.shape[1] * tensors
    rows = (shape((length, text_in.shape[2])), shape((length, layout_in.shape[1])))
    local_heads = shards[0].project.shape[0] // (3 * HEAD_TEXT)
    kept = []
    for x, w in zip(rows, shards):
        units = shape((tensors, length, w.upward.shape[1]))
        kept.append(Kept(
            qkv=shape((tensors, w.project.shape[0], length)), ctx=shape((tensors, w.outward.shape[0], length)),
            inv=shape((tensors, local_heads, length), F32),
            n1=shape(x.shape), low=shape(x.shape), act=units, slope=units,
            n2=shape(x.shape),
        ))
    weights = tuple(Weights(*(shape((tensors,) + m.shape) for m in w)) for w in shards)
    pages_out = (rows[0], shape((rows[1].shape[1], length)))
    outs = (rows, pages_out, shape((tensors, local_heads, length, length)), shape((length, 4), F32), tuple(kept), weights)
    flat_out, out_tree = jax.tree.flatten(outs)
    (a, b) = shards
    ordered = (a.project, b.project, a.outward, a.upward, a.downward, b.outward, b.upward, b.downward)
    shared = tuple(dp % 2 == 0 and w.shape[0] >= 512 for w in ordered)
    n_w = len(ordered)
    cots = [rows[0], shape((rows[1].shape[1], length))]
    small = (*marks, *norms[0], *norms[1])
    results = pl.pallas_call(
        functools.partial(forward_kernel, sections, tensors, shared, None, out_tree),
        out_shape=flat_out + cots,
        in_specs=[ANY] * (4 + n_w) + [VMEM] * len(small),
        out_specs=[ANY] * (len(flat_out) + 2),
        scratch_shapes=vmem_like(flat_out) + [pltpu.SemaphoreType.DMA((len(flat_out),))]
        + [pltpu.VMEM(cots[1].shape, BF), pltpu.VMEM(cots[0].shape, BF), pltpu.VMEM(rows[1].shape, BF)]
        + [pltpu.VMEM(x.shape, BF) for x in rows]
        + [pltpu.VMEM((2,) + x.shape, F32) for x in rows]
        + [pltpu.VMEM((length, w.upward.shape[1]), F32) for w in shards]
        + [pltpu.VMEM((local_heads, length, length), F32)]
        + [pltpu.VMEM((x.shape[1], length), BF) for x in rows]
        + [pltpu.VMEM((2,) + m.shape, BF) for w in shards for m in (w.upward, w.downward)]
        + [pltpu.SemaphoreType.DMA((2, 2, 2))]
        + [
            pltpu.SemaphoreType.DMA((sections, 2, 2)), pltpu.SemaphoreType.DMA((2, tensors)),
            pltpu.SemaphoreType.DMA((5, n_w)), pltpu.SemaphoreType.DMA((5, n_w)), pltpu.SemaphoreType.DMA((n_w,)),
            pltpu.SemaphoreType.DMA((2, len(hop_blocks(length)))), pltpu.SemaphoreType.DMA((2, len(hop_blocks(length)))),
            pltpu.SemaphoreType.DMA((2,)), pltpu.SemaphoreType.DMA((2, 2, tensors)),
        ],
        compiler_params=pltpu.CompilerParams(
            collective_id=0, has_side_effects=True, vmem_limit_bytes=62 << 20
        ),
        name="layer_forward",
    )(text_in, layout_in, text_cot, layout_cot, *ordered, *small)
    return jax.tree.unflatten(out_tree, results[:-2]), tuple(results[-2:])


class Needed(typing.NamedTuple):
    n2: typing.Any
    downward: typing.Any
    slope: typing.Any
    upward: typing.Any
    n1: typing.Any
    outward: typing.Any
    low: typing.Any
    act: typing.Any
    qkv: typing.Any
    ctx: typing.Any
    inv: typing.Any
    project: typing.Any
    x: typing.Any


class Work(typing.NamedTuple):
    g: typing.Any
    gf: typing.Any
    ga: typing.Any
    dz: typing.Any
    dctx: typing.Any
    sums: typing.Any
    lowT: typing.Any
    raw: typing.Any
    from_sibling: typing.Any
    from_partner: typing.Any


class Chunk(typing.NamedTuple):
    b: typing.Any
    index: typing.Any
    first: typing.Any
    rows: typing.Any


MATRICES = 4


def matrix_rows(own):
    return own.project.shape[-2], own.outward.shape[-2], own.upward.shape[-2], own.downward.shape[-2]


def matrix_starts(own):
    sizes = matrix_rows(own)
    return [sum(sizes[:i]) for i in range(MATRICES + 1)]


def pieces_of(size, step):
    return [(f, step) for f in range(0, size, step)]


def backward_kernel(sections, tensors, chain, in_tree, *refs):
    n_in = in_tree.num_leaves
    hbm_in, refs = refs[:n_in], refs[n_in:]
    (cots, ys, lang_ids, gains), refs = (refs[0:2], refs[2:4], refs[4], refs[5:7]), refs[7:]
    results, small_out, page_outs, refs = refs[0:2], refs[2], refs[3:7], refs[7:]
    n_work = len(Work._fields)
    work, refs = (Work(*refs[:n_work]), Work(*refs[n_work : 2 * n_work])), refs[2 * n_work :]
    plain, refs = refs[: n_in - 2 * MATRICES], refs[n_in - 2 * MATRICES :]
    flipped, small_got, small_sum, refs = refs[0], refs[1], refs[2], refs[3:]
    text_out, layout_out, grad_out, layout_grad_out, *refs = refs
    in_sem, cot_sem, hop_send, hop_recv, sib_send, sib_recv, send, recv, credit, out_sem, *refs = refs
    small_send, small_recv, page_send, page_recv, page_out_sem = refs
    section, d, t = lax.axis_index("section"), lax.axis_index("dp"), lax.axis_index("tensor")
    core, chip = t % 2, t // 2
    sibling = {"tensor": t + 1 - 2 * core}
    partner = {"tensor": (t + tensors // 2) % tensors}
    near, cross = {"dp": d + 1 - 2 * (d % 2)}, {"dp": 3 - d}
    outer = (d == 0) | (d == 3)
    other = {"section": 1 - section}
    hbm, probs_hbm, roots_hbm = jax.tree.unflatten(in_tree, hbm_in)
    starts = [matrix_starts(own) for own in hbm]

    plain = list(plain)
    views = []
    for b in range(2):
        fields = {}
        for name, value in hbm[b]._asdict().items():
            if name in Weights._fields:
                i = Weights._fields.index(name)
                fields[name] = work[b].raw.at[:, :, pl.ds(starts[b][i], starts[b][i + 1] - starts[b][i])]
            else:
                fields[name] = plain.pop(0)
        views.append(Needed(**fields))
    probs_in, roots = plain
    flat_views = jax.tree.leaves((tuple(views), probs_in, roots))
    flat_copies = [pltpu.make_async_copy(a, v, in_sem.at[i]) for i, (a, v) in enumerate(zip(hbm_in, flat_views))]
    loads, probs_copy, roots_copy = jax.tree.unflatten(in_tree, flat_copies)
    length = work[0].gf.shape[0]
    local_heads = probs_in.shape[1]
    blocks = hop_blocks(length)
    cot_copies = (
        pltpu.make_async_copy(cots[0], work[0].g, cot_sem.at[0]),
        pltpu.make_async_copy(cots[1], flipped, cot_sem.at[1]),
    )

    @pl.when(section == 1)
    def _():
        start(*cot_copies)

    roots_copy.start()
    for field in zip(loads[1], loads[0]):
        start(*field)
    probs_copy.start()
    greet(section, t, sections, tensors, (near, cross) if chain else ())

    part_length = text_out.shape[1]
    micro, page = core, chip
    kinds = ((grad_out, layout_grad_out), (text_out, layout_out))
    pages = ((work[0].g, flipped), ys)

    def page_part(g, q, a):
        span = pl.ds(q * part_length, part_length)
        return pages[g][a].at[span] if a == 0 else pages[g][a].at[:, span]

    def each_page(g, act):
        for q in range(tensors):
            for a in range(2):
                here = (micro == g) & (t == q)

                @pl.when((section == g) & here)
                def _():
                    act(g, q, a, True)

                @pl.when((section == g) & jnp.logical_not(here))
                def _():
                    act(g, q, a, False)

    def page_copy(g, q, a):
        return remote(
            page_part(g, q, a), kinds[g][a].at[page], page_send.at[q, a], page_recv.at[g, a, page],
            {"section": micro, "tensor": q},
        )

    def page_start(g, q, a, here):
        if here:
            pltpu.make_async_copy(page_part(g, q, a), kinds[g][a].at[page], page_recv.at[g, a, page]).start()
        else:
            page_copy(g, q, a).start()

    def page_sent(g, q, a, here):
        if not here:
            page_copy(g, q, a).wait_send()

    each_page(1, page_start)

    def hop(b, n):
        part = work[b].g.at[blocks[n]]
        return remote(part, part, hop_send.at[b, n], hop_recv.at[b, n], other)

    ahead = 2
    step = 2 * ROWS
    up_first, down_first = starts[0][2], starts[0][3]
    up_count, down_count = (starts[0][3] - up_first) // step, (starts[0][4] - down_first) // step
    n_feed = up_count + down_count
    chunks = [Chunk(0, k, up_first + k * step, step) for k in range(n_feed)]
    later = [(1, 0, starts[1][MATRICES])]
    later += [(0, f, n) for f, n in pieces_of(starts[0][1], starts[0][1] // 2)]
    later += [(0, starts[0][1] + f, n) for f, n in pieces_of(starts[0][2] - starts[0][1], starts[0][2] - starts[0][1])]
    chunks += [Chunk(b, n_feed + i, f, n) for i, (b, f, n) in enumerate(later)]

    def feed_chunk(k):
        return Chunk(0, k, pl.multiple_of(up_first + k * step, 16), step)

    def span(ref, c):
        return ref.at[pl.ds(c.first, c.rows)]

    def to_sibling(c):
        w, rows = work[c.b], pl.ds(c.first, c.rows)
        return remote(
            w.raw.at[:, 1 - core, rows], w.from_sibling.at[:, rows], sib_send.at[c.index], sib_recv.at[c.index], sibling
        )

    def mine(c):
        return span(work[c.b].raw.at[chip, core], c)

    def theirs(c):
        return span(work[c.b].raw.at[1 - chip, core], c)

    def to_partner(c):
        return remote(
            theirs(c), span(work[c.b].from_partner, c), send.at[0, c.index], recv.at[0, c.index], partner
        )

    def from_near(c):
        return span(work[c.b].from_sibling.at[0], c)

    def from_cross(c):
        return span(work[c.b].from_sibling.at[1], c)

    def to_near(c):
        return remote(mine(c), from_near(c), send.at[1, c.index], recv.at[1, c.index], near)

    def to_cross(c):
        return remote(mine(c), from_cross(c), send.at[2, c.index], recv.at[2, c.index], cross)

    def total_to_near(c):
        return remote(
            span(work[c.b].from_partner, c), from_near(c), send.at[3, c.index], recv.at[3, c.index], near
        )

    def out_copy(c, source):
        return pltpu.make_async_copy(span(source, c), span(results[c.b], c), out_sem.at[c.index])

    def added(target, *sources):
        target[...] = sum(s[...].astype(F32) for s in sources).astype(BF)

    def send_to_sibling(c):
        to_sibling(c).start()

    def stage_sibling(c):
        w = work[c.b]
        to_sibling(c).wait_recv()
        added(theirs(c), theirs(c), span(w.from_sibling.at[1 - chip], c))
        added(mine(c), mine(c), span(w.from_sibling.at[chip], c))
        if chain:
            @pl.when(jnp.logical_not(outer))
            def _():
                for device in (near, cross):
                    pl.semaphore_signal(credit, inc=1, device_id=device, device_id_type=MESH)

    def stage_partner(c):
        to_partner(c).wait_recv()
        added(mine(c), mine(c), span(work[c.b].from_partner, c))
        if not chain:
            out_copy(c, work[c.b].raw.at[chip, core]).start()
            return

        @pl.when(outer)
        def _():
            pl.semaphore_wait(credit, 1)
            to_near(c).start()

    def stage_near(c):
        @pl.when(jnp.logical_not(outer))
        def _():
            to_near(c).wait_recv()
            added(mine(c), mine(c), from_near(c))
            pl.semaphore_wait(credit, 1)
            to_cross(c).start()

    def stage_cross(c):
        @pl.when(jnp.logical_not(outer))
        def _():
            to_cross(c).wait_recv()
            total = work[c.b].from_partner
            added(span(total, c), mine(c), from_cross(c))
            total_to_near(c).start()
            out_copy(c, total).start()

    def stage_total(c):
        @pl.when(outer)
        def _():
            total_to_near(c).wait_recv()
            out_copy(c, work[c.b].from_sibling.at[0]).start()

    def first_copies():
        for c in chunks[:ahead]:
            stage_sibling(c)
            to_partner(c).start()

    def turn_operands():
        wait(loads[0].low, loads[0].act)
        work[0].lowT[...] = views[0].low[...].T

    def feed_products():
        own, w = views[0], work[0]

        @pl.loop(0, up_count)
        def _(k):
            rows = pl.ds(pl.multiple_of(k * step, step), step)
            for q in range(tensors):
                w.raw[q // 2, q % 2, pl.ds(pl.multiple_of(up_first + k * step, 16), step), :] = dot(
                    w.lowT[rows, :], own.slope[q]
                ).astype(BF)
            send_to_sibling(feed_chunk(k))

        first_copies()

        @pl.loop(0, down_count)
        def _(k):
            lanes = pl.ds(pl.multiple_of(k * step, step), step)
            for q in range(tensors):
                w.raw[q // 2, q % 2, pl.ds(pl.multiple_of(down_first + k * step, 16), step), :] = dot(
                    own.act[q, :, lanes].T, w.gf[...]
                ).astype(BF)
            send_to_sibling(feed_chunk(up_count + k))

    def later_product(c):
        own, w = views[c.b], work[c.b]
        for q in range(tensors):
            for i in range(MATRICES):
                first = max(c.first, starts[c.b][i])
                last = min(c.first + c.rows, starts[c.b][i + 1])
                if first >= last:
                    continue
                rows = slice(first - starts[c.b][i], last - starts[c.b][i])
                if i == 0:
                    value = dot(own.qkv[q, rows, :], own.x[...])
                elif i == 1:
                    value = dot(own.ctx[q, rows, :], w.ga[...])
                elif i == 2:
                    value = dot(w.lowT[rows, :], own.slope[q])
                else:
                    value = dot(own.act[q, :, rows].T, w.gf[...])
                w.raw[q // 2, q % 2, first:last, :] = value.astype(BF)
        send_to_sibling(c)

    @pl.when(section == 1)
    def _():
        wait(*cot_copies)
        work[1].g[...] = flipped[...].T

    for b in range(2):
        work[b].sums[...] = jnp.zeros(work[b].sums.shape, F32)
    roots_copy.wait()

    def feed_back(n, block):
        for b in (1, 0):
            own, own_in, w, gain = views[b], loads[b], work[b], gains[b]
            if n == 0:
                wait(own_in.n2)

            if block in blocks:
                hop(b, n).wait_recv()

            for rows in small_blocks(block):
                g, normed = w.g[rows].astype(F32), own.n2[rows].astype(F32)
                low = norm_rows_back(g, normed, roots[rows, 2 * b + 1 : 2 * b + 2], gain[1:2])
                w.dz[rows] = low
                w.gf[rows] = low.astype(BF)
                w.sums[1:2] += jnp.sum(g * normed, axis=0, keepdims=True)
                w.sums[3:4] += jnp.sum(g, axis=0, keepdims=True)

            if n == 0:
                wait(own_in.downward, own_in.slope, own_in.upward)

            @pl.loop(0, tensors)
            def _(q):
                d_act = dot(w.gf[block], own.downward[q // 2, q % 2])
                d_pre = (d_act * own.slope[q, block].astype(F32)).astype(BF)
                own.slope[q, block] = d_pre
                w.dz[block] += dot(d_pre, own.upward[q // 2, q % 2])

            if n == 0:
                wait(own_in.n1, own_in.outward)
            for rows in small_blocks(block):
                g, normed = w.dz[rows], own.n1[rows].astype(F32)
                low = norm_rows_back(g, normed, roots[rows, 2 * b : 2 * b + 1], gain[0:1])
                w.dz[rows] = low
                w.ga[rows] = low.astype(BF)
                w.sums[0:1] += jnp.sum(g * normed, axis=0, keepdims=True)
                w.sums[2:3] += jnp.sum(g, axis=0, keepdims=True)
            gaT = w.ga[block].T
            for q in range(tensors):
                w.dctx[q, :, block] = dot(own.outward[q // 2, q % 2], gaT).astype(BF)

    @pl.when(section == 0)
    def _():
        turn_operands()
        for n, block in enumerate(blocks):
            feed_back(n, block)

    @pl.when(section == 1)
    def _():
        feed_back(0, slice(0, length))

    @pl.when(section == 0)
    def _():
        feed_products()

    for own_in in loads:
        wait(own_in.qkv, own_in.ctx, own_in.inv)
    wait(probs_copy)
    qkv = (views[0].qkv, views[1].qkv)
    text_rows, layout_rows = slice(0, HEAD_TEXT), slice(HEAD_TEXT, HEAD_TEXT + HEAD_LAYOUT)

    def turn(k, n_known):
        fixed = isinstance(k, int)

        def at(i, stage):
            if not fixed:
                pl.when((i >= 0) & (i < n_feed))(lambda: stage(feed_chunk(i)))
            elif 0 <= i < n_known:
                stage(chunks[i])

        def sibling_and_send(c):
            stage_sibling(c)
            to_partner(c).start()

        at(k + ahead, sibling_and_send)
        at(k, stage_partner)
        if chain:
            at(k - 1, stage_near)
            at(k - 2, stage_cross)
            at(k - 3, stage_total)

    early_turns = 3

    @pl.loop(0, tensors)
    def _(q):
        for local in range(local_heads):
            head = q * local_heads + local

            @pl.when((section == 0) & (head % 4 == 0) & (head < 4 * early_turns))
            def _():
                turn(head // 4, n_feed)

            inv = views[0].inv[q, local : local + 1, :]
            scaled = [
                (work[s].dctx[q, local * SIZES[s] : (local + 1) * SIZES[s], :].astype(F32) * inv).astype(BF)
                for s in range(2)
            ]
            inner = [
                jnp.sum(
                    scaled[s].astype(F32)
                    * views[s].ctx[q, local * SIZES[s] : (local + 1) * SIZES[s], :].astype(F32),
                    axis=0, keepdims=True,
                )
                for s in range(2)
            ]
            rows16 = lax.broadcasted_iota(jnp.int32, (16, length), 0)
            extra = jnp.zeros((16, length), F32)
            for i, value in enumerate((inner[0] + inner[1], inner[1])):
                high = value.astype(BF).astype(F32)
                extra = jnp.where(rows16 == 2 * i, -high, extra)
                extra = jnp.where(rows16 == 2 * i + 1, high - value, extra)
            pad = jnp.zeros((128 - sum(SIZES) - 16, length), BF)
            dcT = jnp.concatenate([*scaled, extra.astype(BF), pad], axis=0)
            dc = dcT.T
            qT, kT = (head_rows(qkv, q, kind, local, SCALES if kind == 0 else None) for kind in range(2))
            v_text, v_layout = (head_part(qkv, q, 2, local, s) for s in range(2))
            one, other_one = (((rows16 // 2) == i).astype(F32).astype(BF) for i in range(2))
            low = probs_in[q, local]
            probs = low.astype(F32)
            both = dot(dc, jnp.concatenate([v_text, v_layout, one, pad], axis=0))
            ds_both = (probs * both).astype(BF)
            single = dot(dc, jnp.concatenate([jnp.zeros_like(v_text), v_layout, other_one, pad], axis=0))
            ds_layout = (probs * single).astype(BF)
            dvT = dot(dcT, low)
            put_head(qkv, q, 2, local, 0, dvT[text_rows])
            put_head(qkv, q, 2, local, 1, dvT[layout_rows])
            k = kT.T
            lane = lax.broadcasted_iota(jnp.int32, (length, 128), 1)
            dq = jnp.where(lane < HEAD_TEXT, dot(ds_both, k) * SCALES[0], dot(ds_layout, k) * SCALES[1])
            dqT = dq.astype(BF).T
            put_head(qkv, q, 0, local, 0, dqT[text_rows])
            put_head(qkv, q, 0, local, 1, dqT[layout_rows])
            put_head(qkv, q, 1, local, 0, dot(qT[text_rows], ds_both))
            put_head(qkv, q, 1, local, 1, dot(qT[layout_rows], ds_layout))

    wait(loads[0].project, loads[1].project)
    page_sum = jnp.zeros((1, work[0].dz.shape[1]), F32)
    for n, block in enumerate(blocks):
        for b in (1, 0):
            down = work[b].dz[block]
            for q in range(tensors):
                down += dot(qkv[b][q, :, block].T, views[b].project[q // 2, q % 2])
            down = down.astype(BF)
            work[b].g[block] = down
            if b == 0:
                page_sum += jnp.sum(down.astype(F32), axis=0, keepdims=True)

            @pl.when(section == 1)
            def _():
                hop(b, n).start()

    wait(loads[1].low, loads[1].act)
    work[1].lowT[...] = views[1].low[...].T
    for own_in in loads:
        wait(own_in.x)
    @pl.when(section == 1)
    def _():
        turn_operands()
        feed_products()

    for c in chunks[n_feed:]:
        later_product(c)

    @pl.when(section == 0)
    def _():
        flipped[...] = work[1].g[...].T
        each_page(0, page_start)

    at_page = (lax.broadcasted_iota(jnp.int32, lang_ids.shape, 0) == t % 2) & (
        lax.broadcasted_iota(jnp.int32, lang_ids.shape, 1) == t // 2
    )
    group = jnp.sum(jnp.where(at_page, lang_ids[...], 0), axis=(0, 1), keepdims=True)
    n_lang = small_out.shape[1] - 8
    chosen = (lax.broadcasted_iota(jnp.int32, (n_lang, 1), 0) == group) & (section == 0)
    small_sum[0, 0:n_lang] = jnp.where(chosen, page_sum, 0.0)
    small_sum[0, n_lang : n_lang + 4] = work[0].sums[...]
    small_sum[0, n_lang + 4 : n_lang + 8] = jnp.zeros((4, small_out.shape[2]), F32)
    small_sum[0, n_lang + 4 : n_lang + 8, : work[1].sums.shape[1]] = work[1].sums[...]

    def small_copy(i, device):
        return remote(small_sum.at[i], small_got.at[i], small_send.at[i], small_recv.at[i], device)

    if chain:
        small_copy(0, sibling).start()
    @pl.when(section == 1)
    def _():
        @pl.loop(0, early_turns)
        def _(k):
            turn(k, n_feed)

    for k in range(early_turns, len(chunks) + (3 if chain else 0)):
        turn(k, len(chunks))
        if not chain:
            continue
        if k == early_turns:
            small_copy(0, sibling).wait_recv()
            small_sum[1] = small_sum[0] + small_got[0]
            small_copy(1, partner).start()
        if k == early_turns + 1:
            small_copy(1, partner).wait_recv()
            small_sum[2] = small_sum[1] + small_got[1]
            small_copy(2, near).start()
        if k == early_turns + 2:
            small_copy(2, near).wait_recv()
            small_sum[3] = small_sum[2] + small_got[2]

            @pl.when(jnp.logical_not(outer))
            def _():
                small_copy(3, cross).start()

        if k == early_turns + 3:
            @pl.when(jnp.logical_not(outer))
            def _():
                small_copy(3, cross).wait_recv()
                small_sum[4] = small_sum[3] + small_got[3]
                small_copy(4, near).start()

        if k == early_turns + 4:
            @pl.when(outer)
            def _():
                small_copy(4, near).wait_recv()
                small_sum[4] = small_got[4]

            small_sum[5] = small_sum[4]
            small_copy(5, other).start()

    if chain:
        for i, device in enumerate((sibling, partner, near)):
            small_copy(i, device).wait_send()

        @pl.when(jnp.logical_not(outer))
        def _():
            small_copy(3, cross).wait_send()
            small_copy(4, near).wait_send()

        small_copy(5, other).wait()
        small_out[0] = small_sum[5]
        small_out[1] = small_got[5]
    else:
        small_out[0] = small_sum[0]
        small_out[1] = small_sum[0]

    @pl.when(section == 1)
    def _():
        for b in range(2):
            for n in range(len(blocks)):
                hop(b, n).wait_send()

    for c in chunks:
        to_sibling(c).wait_send()
        to_partner(c).wait_send()
        if not chain:
            out_copy(c, work[c.b].from_partner).wait()
            continue

        @pl.when(outer)
        def _():
            to_near(c).wait_send()

        @pl.when(jnp.logical_not(outer))
        def _():
            to_cross(c).wait_send()
            total_to_near(c).wait_send()

        out_copy(c, work[c.b].from_partner).wait()

    for g in range(sections):
        each_page(g, page_sent)
        for a in range(2):
            for j in range(2):
                dst = kinds[g][a].at[j]
                remote(dst, dst, page_send.at[0, a], page_recv.at[g, a, j], partner).wait_recv()
    landed = (text_out, layout_out, grad_out, layout_grad_out)
    copies = [pltpu.make_async_copy(v, h, page_out_sem.at[i]) for i, (v, h) in enumerate(zip(landed, page_outs))]
    start(*copies)
    wait(*copies)


def layer_backward(mesh, x, y, probs, roots, kept, weights, cots, norms, lang_ids, n_lang):
    sections, dp, tensors = mesh.shape["section"], mesh.shape["dp"], mesh.shape["tensor"]
    chain = dp == 4
    weights = tuple(Weights(*(m.reshape((tensors // 2, 2) + m.shape[1:]) for m in w)) for w in weights)
    needed = tuple(
        Needed(
            n2=k.n2, downward=w.downward, slope=k.slope, upward=w.upward, n1=k.n1,
            outward=w.outward, low=k.low, act=k.act, qkv=k.qkv, ctx=k.ctx, inv=k.inv, project=w.project, x=rows,
        )
        for k, w, rows in zip(kept, weights, x)
    )
    flat_in, in_tree = jax.tree.flatten((needed, probs, roots))
    plain = [v for own in needed for name, v in own._asdict().items() if name not in Weights._fields] + [probs, roots]
    stacks = [(matrix_starts(own)[MATRICES], rows.shape[1]) for own, rows in zip(needed, x)]
    length = x[0].shape[0]
    work = []
    for own, rows, (count, width) in zip(needed, x, stacks):
        work += Work(
            g=shape(rows.shape), gf=shape(rows.shape), ga=shape(rows.shape), dz=shape(rows.shape, F32),
            dctx=shape(own.ctx.shape), sums=shape((4, width), F32), lowT=shape((width, length)),
            raw=shape((tensors // 2, 2, count, width)), from_sibling=shape((tensors // 2, count, width)),
            from_partner=shape((count, width)),
        )
    small = shape((2, n_lang + 8, x[0].shape[1]), F32)
    text_page = shape((2, length // tensors, x[0].shape[1]))
    layout_page = shape((2, x[1].shape[1], length // tensors))
    summed = [shape(s) for s in stacks]
    own = needed[0]
    n_chunks = (own.upward.shape[-2] + own.downward.shape[-2]) // (2 * ROWS) + 4
    n_blocks = len(hop_blocks(length))
    dma = pltpu.SemaphoreType.DMA
    results = pl.pallas_call(
        functools.partial(backward_kernel, sections, tensors, chain, in_tree),
        out_shape=summed + [small, text_page, layout_page, text_page, layout_page],
        in_specs=[ANY] * (len(flat_in) + 4) + [VMEM] * 3,
        out_specs=[ANY] * 2 + [VMEM] + [ANY] * 4,
        scratch_shapes=vmem_like(work) + vmem_like(plain)
        + [pltpu.VMEM(cots[1].shape, BF)] + [pltpu.VMEM((6,) + small.shape[1:], F32)] * 2
        + vmem_like([text_page, layout_page] * 2)
        + [dma((len(flat_in),)), dma((2,)), dma((2, n_blocks)), dma((2, n_blocks))]
        + [dma((n_chunks,))] * 2 + [dma((4, n_chunks))] * 2
        + [pltpu.SemaphoreType.REGULAR, dma((n_chunks,))]
        + [dma((6,))] * 2 + [dma((tensors, 2)), dma((sections, 2, 2)), dma((4,))],
        compiler_params=pltpu.CompilerParams(
            collective_id=1, has_side_effects=True, vmem_limit_bytes=64 << 20
        ),
        name="layer_backward",
    )(*flat_in, *cots, *y, lang_ids, norms[0][0], norms[1][0])
    totals, small, pages = results[:2], results[2], results[3:7]
    if not chain:
        totals = lax.psum(tuple(totals), "dp")
        both = lax.psum(small[0], ("dp", "tensor"))
        small = jnp.stack([both, lax.ppermute(both, "section", [(0, 1), (1, 0)])])
    return totals, small, pages


def widen_kernel(n_in, n_pages, *refs):
    n_out = 5 + n_pages + 2 * MATRICES
    hbm_in, hbm_out = refs[:n_in], refs[n_in : n_in + n_out]
    vmem_in, vmem_out = refs[n_in + n_out : 2 * n_in + n_out], refs[2 * n_in + n_out : -2]
    in_sem, out_sem = refs[-2:]
    loads = [pltpu.make_async_copy(h, v, in_sem.at[i]) for i, (h, v) in enumerate(zip(hbm_in, vmem_in))]
    sources = vmem_out[:5] + vmem_in[3:] + vmem_out[5:]
    stores = [pltpu.make_async_copy(v, h, out_sem.at[i]) for i, (v, h) in enumerate(zip(sources, hbm_out))]
    start(*loads)
    totals, small = vmem_in[0:2], vmem_in[2]
    for b in range(2):
        wait(loads[b])
        at = 0
        for i in range(b * MATRICES, (b + 1) * MATRICES):
            out = vmem_out[5 + i]
            for c in range(0, out.shape[0], 48):
                out[c : c + 48] = totals[b][at + c : at + c + 48].astype(F32)
            at += out.shape[0]
            stores[5 + n_pages + i].start()
    for i in range(n_pages):
        loads[3 + i].wait()
        stores[5 + i].start()
    loads[2].wait()
    n_lang = vmem_out[0].shape[0]
    vmem_out[0][...] = jnp.where(lax.axis_index("section") == 0, small[0, :n_lang], small[1, :n_lang])
    for i, out in enumerate(vmem_out[1:5]):
        first = n_lang + 2 * i
        out[...] = small[0, first : first + 2, : out.shape[1]]
    start(*stores[:5])
    wait(*stores)


def widen(totals, small, pages, shards, n_lang):
    widths = [total.shape[1] for total in totals]
    sums = [shape((n_lang, widths[0]), F32)] + [shape((2, w), F32) for w in widths for _ in range(2)]
    grads = [shape(m.shape, F32) for own in shards for m in own]
    inputs = (*totals, small, *pages)
    outs = sums + [shape(page.shape) for page in pages] + grads
    results = pl.pallas_call(
        functools.partial(widen_kernel, len(inputs), len(pages)), out_shape=outs,
        in_specs=[ANY] * len(inputs), out_specs=[ANY] * len(outs),
        scratch_shapes=vmem_like(inputs) + vmem_like(sums + grads)
        + [pltpu.SemaphoreType.DMA((len(inputs),)), pltpu.SemaphoreType.DMA((len(outs),))],
        compiler_params=pltpu.CompilerParams(vmem_limit_bytes=62 << 20), name="widen",
    )(*inputs)
    return results[0], results[1:5], results[5:9], results[9:13], results[13:17]


def per_device(
    mesh,
    text_input,
    layout_input,
    text_cotangent,
    layout_cotangent,
    page_counts,
    pad_mask,
    lang_ids,
    lang_table,
    text_project,
    text_outward,
    text_upward,
    text_downward,
    text_gains,
    text_biases,
    layout_project,
    layout_outward,
    layout_upward,
    layout_downward,
    layout_gains,
    layout_biases,
):
    def flat(project):
        return jnp.transpose(project[0], (1, 2, 0)).reshape(-1, project.shape[1])

    def flipped(block):
        return jnp.transpose(block[0], (0, 2, 1))

    shards = (
        Weights(flat(text_project), text_outward[0], text_upward[0], text_downward[0]),
        Weights(flat(layout_project), layout_outward[0], layout_upward[0], layout_downward[0]),
    )
    norms = ((text_gains[0], text_biases[0]), (layout_gains[0], layout_biases[0]))
    marks = (pad_mask, page_counts, lang_ids, lang_table)
    (x, y, probs, roots, kept, weights), cots = layer_forward(
        mesh, text_input[0], flipped(layout_input), text_cotangent[0], flipped(layout_cotangent), shards, norms, marks
    )
    n_lang = lang_table.shape[0]
    totals, small, pages = layer_backward(mesh, x, y, probs, roots, kept, weights, cots, norms, lang_ids, n_lang)
    lang_sum, norm_sums, pages, text_sums, layout_sums = widen(totals, small, pages, shards, n_lang)
    text_out, layout_out, text_grad, layout_grad = pages

    def unflat(grad, like):
        return jnp.transpose(grad.reshape(like.shape[2], like.shape[3], like.shape[1]), (2, 0, 1))[None]

    unflip = lambda block: jnp.transpose(block, (0, 2, 1))[None]
    return (
        text_out[None], unflip(layout_out), text_grad[None], unflip(layout_grad), lang_sum,
        unflat(text_sums[0], text_project), *(s[None] for s in text_sums[1:]), norm_sums[0][None], norm_sums[1][None],
        unflat(layout_sums[0], layout_project), *(s[None] for s in layout_sums[1:]),
        norm_sums[2][None], norm_sums[3][None],
    )


def solution(mesh):
    tokens = P("section", "dp", "tensor", None)
    weight_specs = (
        P("section", None, None, "tensor"), P("section", "tensor", None), P("section", None, "tensor"),
        P("section", "tensor", None), P("section", None, None), P("section", None, None),
    )
    in_specs = (tokens,) * 4 + (P(None, "dp"), P(None, "dp", None), P(None, "dp"), P()) + weight_specs * 2
    out_specs = (tokens,) * 4 + (P(),) + weight_specs * 2
    return jax.shard_map(
        functools.partial(per_device, mesh), mesh=mesh, in_specs=in_specs, out_specs=out_specs, check_vma=False
    )
```

```python
import functools
import math
import typing

import jax
import jax.numpy as jnp
from jax import lax
from jax.experimental import pallas as pl
from jax.experimental.pallas import tpu as pltpu
from jax.sharding import PartitionSpec as P

HEAD_TEXT = 64
HEAD_LAYOUT = 16
EPSILON = 1e-05
NEGATIVE = -1e30
HIGH = lax.Precision.HIGHEST
MESH = pl.DeviceIdType.MESH
BF = jnp.bfloat16
F32 = jnp.float32
ANY = pl.BlockSpec(memory_space=pl.ANY)


def remote(src, dst, send, recv, device):
    return pltpu.make_async_remote_copy(
        src_ref=src, dst_ref=dst, send_sem=send, recv_sem=recv, device_id=device, device_id_type=MESH
    )


def greet(section, tensor, sections, tensors, extra=()):
    barrier = pltpu.get_barrier_semaphore()
    for g in range(sections):
        for q in range(tensors):

            @pl.when((section != g) | (tensor != q))
            def _():
                pl.semaphore_signal(
                    barrier, inc=1, device_id={"section": g, "tensor": q}, device_id_type=MESH
                )

    for device in extra:
        pl.semaphore_signal(barrier, inc=1, device_id=device, device_id_type=MESH)
    pl.semaphore_wait(barrier, sections * tensors - 1 + len(extra))


GELU_P = 0.3275911
GELU_A = (0.254829592, -0.284496736, 1.421413741, -1.453152027, 1.061405429)
NN = (((1,), (0,)), ((), ()))
NT = (((1,), (1,)), ((), ()))
SCALES = (1.0 / math.sqrt(HEAD_TEXT), 1.0 / math.sqrt(HEAD_LAYOUT))
SIZES = (HEAD_TEXT, HEAD_LAYOUT)
ROWS = 128


class Weights(typing.NamedTuple):
    project: typing.Any
    outward: typing.Any
    upward: typing.Any
    downward: typing.Any


class Kept(typing.NamedTuple):
    qkv: typing.Any
    ctx: typing.Any
    inv: typing.Any
    n1: typing.Any
    low: typing.Any
    act: typing.Any
    slope: typing.Any
    n2: typing.Any


def dot(a, b, dims=NN):
    return lax.dot_general(a, b, dims, preferred_element_type=F32)


def gelu_pair(u):
    d = 1.0 + (GELU_P / math.sqrt(2.0)) * jnp.abs(u)
    t = pl.reciprocal(d, approx=True)
    t = t * (2.0 - d * t)
    e = jnp.exp2((u * u) * (-0.5 / math.log(2.0)))
    a1, a2, a3, a4, a5 = (0.5 * a for a in GELU_A)
    tail = ((((a5 * t + a4) * t + a3) * t + a2) * t + a1) * t * e
    cdf = jnp.where(u >= 0, 1.0 - tail, tail)
    return u * cdf, cdf + u * e * (1.0 / math.sqrt(2.0 * math.pi))


def norm_rows(z, gain, offset):
    center = z - jnp.mean(z, axis=-1, keepdims=True)
    inverse = lax.rsqrt(jnp.mean(center * center, axis=-1, keepdims=True) + EPSILON)
    normed = center * inverse
    return normed * gain + offset, normed, inverse


def norm_rows_back(g, n, r, gain):
    t = g * gain
    return r * (t - jnp.mean(t, axis=-1, keepdims=True) - n * jnp.mean(t * n, axis=-1, keepdims=True))


class Staged:
    def __init__(self, tree, hbm, vmem, sem, inward):
        self.tree, self.vmem = tree, list(vmem)
        pairs = zip(hbm, vmem) if inward else zip(vmem, hbm)
        self.copies = [pltpu.make_async_copy(a, b, sem.at[i]) for i, (a, b) in enumerate(pairs)]

    def refs(self):
        return jax.tree.unflatten(self.tree, self.vmem)

    def parts(self):
        return jax.tree.unflatten(self.tree, self.copies)

    def start(self):
        for copy in self.copies:
            copy.start()

    def wait(self):
        for copy in self.copies:
            copy.wait()


def start(*copies):
    for copy in copies:
        copy.start()


def wait(*copies):
    for copy in copies:
        copy.wait()


def head_rows(stacks, slot, kind, local, scales=None, extra=None):
    rows = []
    for b in range(2):
        piece = head_part(stacks, slot, kind, local, b)
        rows.append(piece if scales is None else piece * BF(scales[b]))
    length = rows[0].shape[1]
    rows.append(jnp.zeros((16, length), BF) if extra is None else extra)
    rows.append(jnp.zeros((128 - sum(SIZES) - 16, length), BF))
    return jnp.concatenate(rows, axis=0)


def head_part(stacks, slot, kind, local, b):
    first = kind * (stacks[b].shape[1] // 3) + local * SIZES[b]
    return stacks[b][slot, first : first + SIZES[b], :]


def small_blocks(block, step=64):
    return [slice(c, c + step) for c in range(block.start, block.stop, step)]


def put_head(stacks, slot, kind, local, b, value):
    first = kind * (stacks[b].shape[1] // 3) + local * SIZES[b]
    stacks[b][slot, first : first + SIZES[b], :] = value.astype(BF)


def hop_blocks(length):
    ends = [0, length // 2, length * 3 // 4, length]
    return [slice(a, b) for a, b in zip(ends, ends[1:])]


def slot_of(u, core, chip):
    return ((chip + u // 2) % 2) * 2 + (core + u % 2) % 2


def forward_kernel(sections, tensors, shared, in_tree, out_tree, *refs):
    n_w, n_out, n_shards = len(shared), out_tree.num_leaves, 2 * MATRICES
    sources = (refs[0:2], refs[2:4])
    matrices = refs[4 : 4 + n_shards]
    pad_mask, counts, lang_ids, lang_table, *norms = refs[4 + n_shards : 12 + n_shards]
    rest = refs[12 + n_shards :]
    hbm_out, cots_out, rest = rest[:n_out], rest[n_out : n_out + 2], rest[n_out + 2 :]
    outgoing = Staged(out_tree, hbm_out, rest[:n_out], rest[n_out], False)
    rest = rest[n_out + 1 :]
    flipped, raw_x, y_narrow, *rest = rest
    nats, totals, pre, score_buffer, rest = rest[0:2], rest[2:4], rest[4:6], rest[6], rest[7:]
    xT, turned, turn_sem, rest = rest[0:2], (rest[2:4], rest[4:6]), rest[6], rest[7:]
    page_send, page_recv, w_send, w_recv, own_sem, hop_send, hop_recv, cot_sem, act_sem, stack, stack_sem = rest
    x, y_pages, probs_out, roots, kept, weights = outgoing.refs()
    y = (y_pages[0], y_narrow)
    x_out, y_out, probs_copy, roots_copy, kept_out, weights_out = outgoing.parts()
    kept_hbm, weights_hbm = jax.tree.unflatten(out_tree, list(hbm_out))[4:6]
    section, d, t = lax.axis_index("section"), lax.axis_index("dp"), lax.axis_index("tensor")
    core, chip, half_index = t % 2, t // 2, d % 2
    sibling, partner = t + 1 - 2 * core, (t + tensors // 2) % tensors
    mate = d + 1 - 2 * half_index
    micro, page = core, chip
    part_length = sources[0][0].shape[1]
    length = x[0].shape[0]
    blocks = [slice(c, c + 2 * ROWS) for c in range(0, length, 2 * ROWS)]
    parts = hop_blocks(length)
    sizes = [m.shape[0] for m in matrices[MATRICES:]]
    firsts = [sum(sizes[:i]) for i in range(MATRICES)]
    weights = (weights[0], Weights(*(stack.at[:, pl.ds(f, n)] for f, n in zip(firsts, sizes))))
    full = (weights[0].project, stack, weights[0].outward, weights[0].upward, weights[0].downward)
    shards = (matrices[0], stack.at[t], matrices[1], matrices[2], matrices[3])
    greet(section, t, sections, tensors, ({"dp": mate},) if any(shared) else ())

    def half_of(ref, i, which):
        count = shards[i].shape[0] // 2
        return ref.at[pl.ds(pl.multiple_of(which * count, 16), count)] if shared[i] else ref

    def to_partner(i):
        return remote(
            half_of(shards[i], i, half_index), half_of(full[i].at[t], i, half_index),
            w_send.at[0, i], w_recv.at[0, i], {"tensor": partner},
        )

    def to_sibling(i):
        return remote(full[i].at[t], full[i].at[t], w_send.at[1, i], w_recv.at[1, i], {"tensor": sibling})

    def to_mate(i):
        ref = half_of(full[i].at[partner], i, half_index)
        return remote(ref, ref, w_send.at[2, i], w_recv.at[2, i], {"dp": mate})

    def on_first(i):
        ref = half_of(full[i].at[partner], i, half_index)
        return remote(ref, ref, w_send.at[3, i], w_recv.at[3, i], {"tensor": sibling})

    def on_second(i):
        ref = half_of(full[i].at[partner], i, 1 - half_index)
        return remote(ref, ref, w_send.at[4, i], w_recv.at[4, i], {"tensor": sibling})

    def keep(i):
        if i != 1:
            return [pltpu.make_async_copy(shards[i], full[i].at[t], own_sem.at[i])]
        return [
            pltpu.make_async_copy(m, weights[1][j].at[t], own_sem.at[n_w + j])
            for j, m in enumerate(matrices[MATRICES:])
        ]

    def relay(*which):
        for i in which:
            to_partner(i).wait_recv()
            if shared[i]:
                to_mate(i).start()
            on_first(i).start()

    def relay_second(*which):
        for i in which:
            if shared[i]:
                to_mate(i).wait_recv()
                on_second(i).start()

    def early(*which):
        for i in which:
            to_sibling(i).wait_recv()

    def late(*which):
        for i in which:
            on_first(i).wait_recv()
            if shared[i]:
                on_second(i).wait_recv()

    def token_slot(g, a, index):
        start_at = pl.multiple_of(index * part_length, part_length)
        target = (raw_x, flipped)[a]
        return target.at[pl.ds(start_at, part_length)] if a == 0 else target.at[:, pl.ds(start_at, part_length)]

    def over_pages(g, act):
        for j in range(2):
            target = 2 * j + section
            here = (section == g) & (t == target)
            for a in range(2):
                act(g, j, a, target, here)

    def page_copy(g, j, a, target):
        return remote(
            sources[g][a].at[j], token_slot(g, a, t), page_send.at[g, j, a], page_recv.at[a, t],
            {"section": g, "tensor": target},
        )

    def page_start(g, j, a, target, here):
        @pl.when(here)
        def _():
            pltpu.make_async_copy(sources[g][a].at[j], token_slot(g, a, t), page_recv.at[a, t]).start()

        @pl.when(jnp.logical_not(here))
        def _():
            page_copy(g, j, a, target).start()

    def page_sent(g, j, a, target, here):
        @pl.when(jnp.logical_not(here))
        def _():
            page_copy(g, j, a, target).wait_send()

    def pages_arrived(g):
        for a in range(2):
            for q in range(tensors):
                slot = token_slot(g, a, q)
                remote(slot, slot, page_send.at[0, 0, a], page_recv.at[a, q], {"tensor": sibling}).wait_recv()

    def hop(b, n):
        return remote(
            y[b].at[parts[n]], x[b].at[parts[n]], hop_send.at[b, n], hop_recv.at[b, n], {"section": 1 - section}
        )

    stack_copies = [
        pltpu.make_async_copy(weights[1][m], weights_hbm[1][m], stack_sem.at[m]) for m in range(2)
    ]

    def weights_to_hbm():
        for b in range(2):
            if b == 0:
                start(weights_out[0].project, weights_out[0].outward)
            else:
                start(*stack_copies)
            for q in range(tensors):
                for m, name in enumerate((2, 3)):
                    copy = pltpu.make_async_copy(
                        turned[b][m].at[q % 2], weights_hbm[b][name].at[q], turn_sem.at[b, m, q % 2]
                    )
                    if q >= 2:
                        copy.wait()
                    turned[b][m][q % 2] = weights[b][name][q].T
                    copy.start()
        for b in range(2):
            for q in range(tensors - 2, tensors):
                for m, name in enumerate((2, 3)):
                    pltpu.make_async_copy(
                        turned[b][m].at[q % 2], weights_hbm[b][name].at[q], turn_sem.at[b, m, q % 2]
                    ).wait()

    over_pages(0, page_start)
    for i in range(n_w):
        start(*keep(i))
    to_partner(0).start()
    wait(*keep(1))
    for i in range(1, n_w):
        to_partner(i).start()
    over_pages(1, page_start)
    for i in range(n_w):
        if i != 1:
            wait(*keep(i))
        to_sibling(i).start()

    at_page = (lax.broadcasted_iota(jnp.int32, counts.shape, 0) == micro) & (
        lax.broadcasted_iota(jnp.int32, counts.shape, 1) == page
    )

    def own_entry(ref):
        return jnp.sum(jnp.where(at_page, ref[...], 0), axis=(0, 1), keepdims=True)

    positions = lax.broadcasted_iota(jnp.int32, (1, length), 1)
    mask_row = pad_mask[micro, pl.ds(page, 1), :]
    key_mask = (positions < own_entry(counts)) & ((mask_row == 1) | (positions == 0))
    first_row = (lax.broadcasted_iota(jnp.int32, (16, length), 0) == 0).astype(F32)
    mask_row16 = (first_row * jnp.where(key_mask, 0.0, NEGATIVE)).astype(BF)
    groups = lax.broadcasted_iota(jnp.int32, (lang_table.shape[0], 1), 0)
    lang_row = jnp.sum(jnp.where(groups == own_entry(lang_ids), lang_table[...], 0.0), axis=0, keepdims=True)
    local_heads = weights[0].project.shape[1] // (3 * HEAD_TEXT)
    qkv = (kept[0].qkv, kept[1].qkv)

    @pl.when(section == 0)
    def _():
        pages_arrived(0)
        x[0][...] = (raw_x[...].astype(F32) + lang_row).astype(BF)
        x[1][...] = flipped[...].T
        early(0, 1)

    @pl.when(section == 1)
    def _():
        relay(*range(n_w))
        relay_second(*range(n_w))
        early(*range(n_w))
        late(*range(n_w))
        weights_to_hbm()

    @pl.loop(0, 2)
    def _(half):
        @pl.when((half == 1) & (section == 0))
        def _():
            relay(0, 1)
            relay_second(0)
            late(0, 1)

        for n, block in enumerate(parts):
            @pl.when((half == 0) & (section == 1))
            def _():
                for b in range(2):
                    hop(b, n).wait_recv()

            @pl.when(half == 0)
            def _():
                for b in range(2):
                    xT[b][:, block] = x[b][block].T

            @pl.loop(0, 2)
            def _(u):
                slot = slot_of(2 * half + u, core, chip)
                for b in range(2):
                    qkv[b][slot, :, block] = dot(weights[b].project[slot], xT[b][:, block]).astype(BF)

        @pl.loop(0, 2)
        def _(u):
            slot = slot_of(2 * half + u, core, chip)
            for local in range(local_heads):
                q = head_rows(qkv, slot, 0, local, SCALES, first_row.astype(BF)).T
                kT = head_rows(qkv, slot, 1, local, None, mask_row16)
                score_buffer[local] = dot(q, kT)
                for rows in small_blocks(slice(0, length)):
                    scores = score_buffer[local, rows, :]
                    raised = jnp.exp(scores - jnp.max(scores, axis=-1, keepdims=True))
                    probs_out[slot, local, rows, :] = raised.astype(BF)
                vT = head_rows(qkv, slot, 2, local, None, first_row.astype(BF))
                ctx = dot(probs_out[slot, local], vT.T).T
                inv = 1.0 / ctx[sum(SIZES) : sum(SIZES) + 1]
                ctx = (ctx * inv).astype(BF)
                kept[0].inv[slot, local : local + 1, :] = inv
                kept[0].ctx[slot, local * HEAD_TEXT : (local + 1) * HEAD_TEXT, :] = ctx[:HEAD_TEXT]
                kept[1].ctx[slot, local * HEAD_LAYOUT : (local + 1) * HEAD_LAYOUT, :] = ctx[
                    HEAD_TEXT : HEAD_TEXT + HEAD_LAYOUT
                ]

    kept[1].inv[...] = jnp.zeros(kept[1].inv.shape, F32)
    start(probs_copy, *x_out, *(c for k in kept_out for c in (k.qkv, k.ctx, k.inv)))

    def attend(b):
        gains, biases = norms[2 * b : 2 * b + 2]
        width = x[b].shape[1]
        nats[b][...] = kept[b].ctx[...].reshape(width, length).T
        wide = weights[b].outward[...].reshape(width, width)
        for block in blocks:
            totals[b][1, block] = dot(nats[b][block], wide)
            for rows in small_blocks(block):
                h, n, r = norm_rows(x[b][rows].astype(F32) + totals[b][1, rows], gains[0:1], biases[0:1])
                totals[b][0, rows] = h
                totals[b][1, rows] = jnp.zeros(h.shape, F32)
                kept[b].n1[rows] = n.astype(BF)
                roots[rows, 2 * b : 2 * b + 1] = r
                kept[b].low[rows] = h.astype(BF)
        start(kept_out[b].n1, kept_out[b].low)

    def slot_copies(b, slot):
        return [
            pltpu.make_async_copy(v.at[slot], h.at[slot], act_sem.at[b, m, slot])
            for m, (v, h) in enumerate(((kept[b].act, kept_hbm[b].act), (kept[b].slope, kept_hbm[b].slope)))
        ]

    def feed(b, first, which):
        @pl.loop(first, first + 2)
        def _(u):
            slot = slot_of(u, core, chip)
            for block in which:
                pre[b][block] = dot(kept[b].low[block], weights[b].upward[slot])
                for rows in small_blocks(block, 16):
                    act, slope = gelu_pair(pre[b][rows])
                    kept[b].act[slot, rows] = act.astype(BF)
                    kept[b].slope[slot, rows] = slope.astype(BF)
                totals[b][1, block] += dot(kept[b].act[slot, block], weights[b].downward[slot])
                if block == slice(0, length):
                    start(*slot_copies(b, slot))

    def finish(b):
        gains, biases = norms[2 * b : 2 * b + 2]
        def last(block):
            feed(b, 2, [block])
            for rows in small_blocks(block):
                out, normed, r = norm_rows(totals[b][0, rows] + totals[b][1, rows], gains[1:2], biases[1:2])
                y[b][rows] = out.astype(BF)
                kept[b].n2[rows] = normed.astype(BF)
                roots[rows, 2 * b + 1 : 2 * b + 2] = r

        @pl.when(section == 0)
        def _():
            for n, block in enumerate(parts):
                last(block)
                hop(b, n).start()
            for u in range(2, 4):
                start(*slot_copies(b, slot_of(u, core, chip)))

        @pl.when(section == 1)
        def _():
            last(slice(0, length))

        if b == 1:
            y_pages[1][...] = y_narrow[...].T
        start(y_out[b], kept_out[b].n2)

    @pl.when(section == 0)
    def _():
        relay(2, 3)
        early(2)
        late(2)

    attend(0)

    @pl.when(section == 0)
    def _():
        early(3, 4)

    feed(0, 0, [slice(0, length)])

    @pl.when(section == 0)
    def _():
        relay(4)
        relay_second(3)

    attend(1)
    feed(1, 0, [slice(0, length)])
    finish(1)

    @pl.when(section == 0)
    def _():
        relay_second(4)
        late(3, 4)

    finish(0)
    start(roots_copy)

    @pl.when(section == 0)
    def _():
        weights_to_hbm()
        for b in range(2):
            for n in range(len(parts)):
                hop(b, n).wait_send()

    for i in range(n_w):
        to_partner(i).wait_send()
        to_sibling(i).wait_send()
        on_first(i).wait_send()
        if shared[i]:
            to_mate(i).wait_send()
            on_second(i).wait_send()
    for g in range(sections):
        over_pages(g, page_sent)

    @pl.when(section == 1)
    def _():
        pages_arrived(1)
        copies = [pltpu.make_async_copy(v, h, cot_sem.at[i]) for i, (v, h) in enumerate(zip((raw_x, flipped), cots_out))]
        start(*copies)
        wait(*copies)

    for group in (x_out, y_out, (probs_copy, roots_copy), weights_out[0][:2], stack_copies):
        wait(*group)
    for b, k in enumerate(kept_out):
        wait(k.qkv, k.ctx, k.inv, k.n1, k.low, k.n2)
        for slot in range(tensors):
            wait(*slot_copies(b, slot))


def vmem_like(tree):
    return [pltpu.VMEM(s.shape, s.dtype) for s in jax.tree.leaves(tree)]


VMEM = pl.BlockSpec(memory_space=pltpu.VMEM)


def shape(dims, dtype=BF):
    return jax.ShapeDtypeStruct(tuple(dims), dtype)


def layer_forward(mesh, text_in, layout_in, text_cot, layout_cot, shards, norms, marks):
    sections, dp, tensors = mesh.shape["section"], mesh.shape["dp"], mesh.shape["tensor"]
    length = text_in.shape[1] * tensors
    rows = (shape((length, text_in.shape[2])), shape((length, layout_in.shape[1])))
    local_heads = shards[0].project.shape[0] // (3 * HEAD_TEXT)
    kept = []
    for x, w in zip(rows, shards):
        units = shape((tensors, length, w.upward.shape[1]))
        kept.append(Kept(
            qkv=shape((tensors, w.project.shape[0], length)), ctx=shape((tensors, w.outward.shape[0], length)),
            inv=shape((tensors, local_heads, length), F32),
            n1=shape(x.shape), low=shape(x.shape), act=units, slope=units,
            n2=shape(x.shape),
        ))
    weights = tuple(Weights(*(shape((tensors,) + m.shape) for m in w)) for w in shards)
    pages_out = (rows[0], shape((rows[1].shape[1], length)))
    outs = (rows, pages_out, shape((tensors, local_heads, length, length)), shape((length, 4), F32), tuple(kept), weights)
    flat_out, out_tree = jax.tree.flatten(outs)
    (a, b) = shards
    ordered = (*a, *b)
    stack = shape((tensors, sum(m.shape[0] for m in b), b.project.shape[1]))
    sent = (a.project, stack, a.outward, a.upward, a.downward)
    shared = tuple(dp % 2 == 0 and len(w.shape) == 2 and w.shape[0] >= 512 for w in sent)
    n_w = len(sent)
    cots = [rows[0], shape((rows[1].shape[1], length))]
    small = (*marks, *norms[0], *norms[1])
    results = pl.pallas_call(
        functools.partial(forward_kernel, sections, tensors, shared, None, out_tree),
        out_shape=flat_out + cots,
        in_specs=[ANY] * (4 + len(ordered)) + [VMEM] * len(small),
        out_specs=[ANY] * (len(flat_out) + 2),
        scratch_shapes=vmem_like(flat_out) + [pltpu.SemaphoreType.DMA((len(flat_out),))]
        + [pltpu.VMEM(cots[1].shape, BF), pltpu.VMEM(cots[0].shape, BF), pltpu.VMEM(rows[1].shape, BF)]
        + [pltpu.VMEM(x.shape, BF) for x in rows]
        + [pltpu.VMEM((2,) + x.shape, F32) for x in rows]
        + [pltpu.VMEM((length, w.upward.shape[1]), F32) for w in shards]
        + [pltpu.VMEM((local_heads, length, length), F32)]
        + [pltpu.VMEM((x.shape[1], length), BF) for x in rows]
        + [pltpu.VMEM((2,) + m.shape, BF) for w in shards for m in (w.upward, w.downward)]
        + [pltpu.SemaphoreType.DMA((2, 2, 2))]
        + [
            pltpu.SemaphoreType.DMA((sections, 2, 2)), pltpu.SemaphoreType.DMA((2, tensors)),
            pltpu.SemaphoreType.DMA((5, n_w)), pltpu.SemaphoreType.DMA((5, n_w)), pltpu.SemaphoreType.DMA((n_w + MATRICES,)),
            pltpu.SemaphoreType.DMA((2, len(hop_blocks(length)))), pltpu.SemaphoreType.DMA((2, len(hop_blocks(length)))),
            pltpu.SemaphoreType.DMA((2,)), pltpu.SemaphoreType.DMA((2, 2, tensors)),
            pltpu.VMEM(stack.shape, BF), pltpu.SemaphoreType.DMA((2,)),
        ],
        compiler_params=pltpu.CompilerParams(
            collective_id=0, has_side_effects=True, vmem_limit_bytes=62 << 20
        ),
        name="layer_forward",
    )(text_in, layout_in, text_cot, layout_cot, *ordered, *small)
    return jax.tree.unflatten(out_tree, results[:-2]), tuple(results[-2:])


class Needed(typing.NamedTuple):
    n2: typing.Any
    downward: typing.Any
    slope: typing.Any
    upward: typing.Any
    n1: typing.Any
    outward: typing.Any
    low: typing.Any
    act: typing.Any
    qkv: typing.Any
    ctx: typing.Any
    inv: typing.Any
    project: typing.Any
    x: typing.Any


class Work(typing.NamedTuple):
    g: typing.Any
    gf: typing.Any
    ga: typing.Any
    dz: typing.Any
    dctx: typing.Any
    sums: typing.Any
    lowT: typing.Any
    raw: typing.Any
    from_sibling: typing.Any
    from_partner: typing.Any


class Chunk(typing.NamedTuple):
    b: typing.Any
    index: typing.Any
    first: typing.Any
    rows: typing.Any


MATRICES = 4


def matrix_rows(own):
    return own.project.shape[-2], own.outward.shape[-2], own.upward.shape[-2], own.downward.shape[-2]


def matrix_starts(own):
    sizes = matrix_rows(own)
    return [sum(sizes[:i]) for i in range(MATRICES + 1)]


def pieces_of(size, step):
    return [(f, step) for f in range(0, size, step)]


def backward_kernel(sections, tensors, chain, in_tree, *refs):
    n_in = in_tree.num_leaves
    hbm_in, refs = refs[:n_in], refs[n_in:]
    (cots, ys, lang_ids, gains), refs = (refs[0:2], refs[2:4], refs[4], refs[5:7]), refs[7:]
    results, small_out, page_outs, refs = refs[0:2], refs[2], refs[3:7], refs[7:]
    n_work = len(Work._fields)
    work, refs = (Work(*refs[:n_work]), Work(*refs[n_work : 2 * n_work])), refs[2 * n_work :]
    plain, refs = refs[: n_in - 2 * MATRICES], refs[n_in - 2 * MATRICES :]
    flipped, small_got, small_sum, refs = refs[0], refs[1], refs[2], refs[3:]
    text_out, layout_out, grad_out, layout_grad_out, *refs = refs
    in_sem, cot_sem, hop_send, hop_recv, sib_send, sib_recv, send, recv, credit, out_sem, *refs = refs
    small_send, small_recv, page_send, page_recv, page_out_sem = refs
    section, d, t = lax.axis_index("section"), lax.axis_index("dp"), lax.axis_index("tensor")
    core, chip = t % 2, t // 2
    sibling = {"tensor": t + 1 - 2 * core}
    partner = {"tensor": (t + tensors // 2) % tensors}
    near, cross = {"dp": d + 1 - 2 * (d % 2)}, {"dp": 3 - d}
    outer = (d == 0) | (d == 3)
    other = {"section": 1 - section}
    hbm, probs_hbm, roots_hbm = jax.tree.unflatten(in_tree, hbm_in)
    starts = [matrix_starts(own) for own in hbm]

    plain = list(plain)
    views = []
    for b in range(2):
        fields = {}
        for name, value in hbm[b]._asdict().items():
            if name in Weights._fields:
                i = Weights._fields.index(name)
                fields[name] = work[b].raw.at[:, :, pl.ds(starts[b][i], starts[b][i + 1] - starts[b][i])]
            else:
                fields[name] = plain.pop(0)
        views.append(Needed(**fields))
    probs_in, roots = plain
    flat_views = jax.tree.leaves((tuple(views), probs_in, roots))
    flat_copies = [pltpu.make_async_copy(a, v, in_sem.at[i]) for i, (a, v) in enumerate(zip(hbm_in, flat_views))]
    loads, probs_copy, roots_copy = jax.tree.unflatten(in_tree, flat_copies)
    length = work[0].gf.shape[0]
    local_heads = probs_in.shape[1]
    blocks = hop_blocks(length)
    cot_copies = (
        pltpu.make_async_copy(cots[0], work[0].g, cot_sem.at[0]),
        pltpu.make_async_copy(cots[1], flipped, cot_sem.at[1]),
    )

    @pl.when(section == 1)
    def _():
        start(*cot_copies)

    roots_copy.start()
    for field in zip(loads[1], loads[0]):
        start(*field)
    probs_copy.start()
    greet(section, t, sections, tensors, (near, cross) if chain else ())

    part_length = text_out.shape[1]
    micro, page = core, chip
    kinds = ((grad_out, layout_grad_out), (text_out, layout_out))
    pages = ((work[0].g, flipped), ys)

    def page_part(g, q, a):
        span = pl.ds(q * part_length, part_length)
        return pages[g][a].at[span] if a == 0 else pages[g][a].at[:, span]

    def each_page(g, act):
        for q in range(tensors):
            for a in range(2):
                here = (micro == g) & (t == q)

                @pl.when((section == g) & here)
                def _():
                    act(g, q, a, True)

                @pl.when((section == g) & jnp.logical_not(here))
                def _():
                    act(g, q, a, False)

    def page_copy(g, q, a):
        return remote(
            page_part(g, q, a), kinds[g][a].at[page], page_send.at[q, a], page_recv.at[g, a, page],
            {"section": micro, "tensor": q},
        )

    def page_start(g, q, a, here):
        if here:
            pltpu.make_async_copy(page_part(g, q, a), kinds[g][a].at[page], page_recv.at[g, a, page]).start()
        else:
            page_copy(g, q, a).start()

    def page_sent(g, q, a, here):
        if not here:
            page_copy(g, q, a).wait_send()

    each_page(1, page_start)

    def hop(b, n):
        part = work[b].g.at[blocks[n]]
        return remote(part, part, hop_send.at[b, n], hop_recv.at[b, n], other)

    ahead = 2
    step = 2 * ROWS
    up_first, down_first = starts[0][2], starts[0][3]
    up_count, down_count = (starts[0][3] - up_first) // step, (starts[0][4] - down_first) // step
    n_feed = up_count + down_count
    chunks = [Chunk(0, k, up_first + k * step, step) for k in range(n_feed)]
    later = [(1, 0, starts[1][MATRICES])]
    later += [(0, f, n) for f, n in pieces_of(starts[0][1], starts[0][1] // 2)]
    later += [(0, starts[0][1] + f, n) for f, n in pieces_of(starts[0][2] - starts[0][1], starts[0][2] - starts[0][1])]
    chunks += [Chunk(b, n_feed + i, f, n) for i, (b, f, n) in enumerate(later)]

    def feed_chunk(k):
        return Chunk(0, k, pl.multiple_of(up_first + k * step, 16), step)

    def span(ref, c):
        return ref.at[pl.ds(c.first, c.rows)]

    def to_sibling(c):
        w, rows = work[c.b], pl.ds(c.first, c.rows)
        return remote(
            w.raw.at[:, 1 - core, rows], w.from_sibling.at[:, rows], sib_send.at[c.index], sib_recv.at[c.index], sibling
        )

    def mine(c):
        return span(work[c.b].raw.at[chip, core], c)

    def theirs(c):
        return span(work[c.b].raw.at[1 - chip, core], c)

    def to_partner(c):
        return remote(
            theirs(c), span(work[c.b].from_partner, c), send.at[0, c.index], recv.at[0, c.index], partner
        )

    def from_near(c):
        return span(work[c.b].from_sibling.at[0], c)

    def from_cross(c):
        return span(work[c.b].from_sibling.at[1], c)

    def to_near(c):
        return remote(mine(c), from_near(c), send.at[1, c.index], recv.at[1, c.index], near)

    def to_cross(c):
        return remote(mine(c), from_cross(c), send.at[2, c.index], recv.at[2, c.index], cross)

    def total_to_near(c):
        return remote(
            span(work[c.b].from_partner, c), from_near(c), send.at[3, c.index], recv.at[3, c.index], near
        )

    def out_copy(c, source):
        return pltpu.make_async_copy(span(source, c), span(results[c.b], c), out_sem.at[c.index])

    def added(target, *sources):
        target[...] = sum(s[...].astype(F32) for s in sources).astype(BF)

    def send_to_sibling(c):
        to_sibling(c).start()

    def stage_sibling(c):
        w = work[c.b]
        to_sibling(c).wait_recv()
        added(theirs(c), theirs(c), span(w.from_sibling.at[1 - chip], c))
        added(mine(c), mine(c), span(w.from_sibling.at[chip], c))
        if chain:
            @pl.when(jnp.logical_not(outer))
            def _():
                for device in (near, cross):
                    pl.semaphore_signal(credit, inc=1, device_id=device, device_id_type=MESH)

    def stage_partner(c):
        to_partner(c).wait_recv()
        added(mine(c), mine(c), span(work[c.b].from_partner, c))
        if not chain:
            out_copy(c, work[c.b].raw.at[chip, core]).start()
            return

        @pl.when(outer)
        def _():
            pl.semaphore_wait(credit, 1)
            to_near(c).start()

    def stage_near(c):
        @pl.when(jnp.logical_not(outer))
        def _():
            to_near(c).wait_recv()
            added(mine(c), mine(c), from_near(c))
            pl.semaphore_wait(credit, 1)
            to_cross(c).start()

    def stage_cross(c):
        @pl.when(jnp.logical_not(outer))
        def _():
            to_cross(c).wait_recv()
            total = work[c.b].from_partner
            added(span(total, c), mine(c), from_cross(c))
            total_to_near(c).start()
            out_copy(c, total).start()

    def stage_total(c):
        @pl.when(outer)
        def _():
            total_to_near(c).wait_recv()
            out_copy(c, work[c.b].from_sibling.at[0]).start()

    def turn_operands():
        wait(loads[0].low, loads[0].act)
        work[0].lowT[...] = views[0].low[...].T

    def feed_products():
        own, w = views[0], work[0]

        @pl.loop(0, up_count)
        def _(k):
            rows = pl.ds(pl.multiple_of(k * step, step), step)
            for q in range(tensors):
                w.raw[q // 2, q % 2, pl.ds(pl.multiple_of(up_first + k * step, 16), step), :] = dot(
                    w.lowT[rows, :], own.slope[q]
                ).astype(BF)
            send_to_sibling(feed_chunk(k))

            @pl.when((k >= 1) & (k <= ahead))
            def _():
                stage_sibling(feed_chunk(k - 1))
                to_partner(feed_chunk(k - 1)).start()

        @pl.loop(0, down_count)
        def _(k):
            lanes = pl.ds(pl.multiple_of(k * step, step), step)
            for q in range(tensors):
                w.raw[q // 2, q % 2, pl.ds(pl.multiple_of(down_first + k * step, 16), step), :] = dot(
                    own.act[q, :, lanes].T, w.gf[...]
                ).astype(BF)
            send_to_sibling(feed_chunk(up_count + k))

    def later_product(c):
        own, w = views[c.b], work[c.b]
        for q in range(tensors):
            for i in range(MATRICES):
                first = max(c.first, starts[c.b][i])
                last = min(c.first + c.rows, starts[c.b][i + 1])
                if first >= last:
                    continue
                rows = slice(first - starts[c.b][i], last - starts[c.b][i])
                if i == 0:
                    value = dot(own.qkv[q, rows, :], own.x[...])
                elif i == 1:
                    value = dot(own.ctx[q, rows, :], w.ga[...])
                elif i == 2:
                    value = dot(w.lowT[rows, :], own.slope[q])
                else:
                    value = dot(own.act[q, :, rows].T, w.gf[...])
                w.raw[q // 2, q % 2, first:last, :] = value.astype(BF)
        send_to_sibling(c)

    @pl.when(section == 1)
    def _():
        wait(*cot_copies)
        work[1].g[...] = flipped[...].T

    for b in range(2):
        work[b].sums[...] = jnp.zeros(work[b].sums.shape, F32)
    roots_copy.wait()

    def feed_back(n, block):
        for b in (1, 0):
            own, own_in, w, gain = views[b], loads[b], work[b], gains[b]
            if n == 0:
                wait(own_in.n2)

            if block in blocks:
                hop(b, n).wait_recv()

            for rows in small_blocks(block):
                g, normed = w.g[rows].astype(F32), own.n2[rows].astype(F32)
                low = norm_rows_back(g, normed, roots[rows, 2 * b + 1 : 2 * b + 2], gain[1:2])
                w.dz[rows] = low
                w.gf[rows] = low.astype(BF)
                w.sums[1:2] += jnp.sum(g * normed, axis=0, keepdims=True)
                w.sums[3:4] += jnp.sum(g, axis=0, keepdims=True)

            if n == 0:
                wait(own_in.downward, own_in.slope, own_in.upward)

            @pl.loop(0, tensors)
            def _(q):
                d_act = dot(w.gf[block], own.downward[q // 2, q % 2])
                d_pre = (d_act * own.slope[q, block].astype(F32)).astype(BF)
                own.slope[q, block] = d_pre
                w.dz[block] += dot(d_pre, own.upward[q // 2, q % 2])

            if n == 0:
                wait(own_in.n1, own_in.outward)
            for rows in small_blocks(block):
                g, normed = w.dz[rows], own.n1[rows].astype(F32)
                low = norm_rows_back(g, normed, roots[rows, 2 * b : 2 * b + 1], gain[0:1])
                w.dz[rows] = low
                w.ga[rows] = low.astype(BF)
                w.sums[0:1] += jnp.sum(g * normed, axis=0, keepdims=True)
                w.sums[2:3] += jnp.sum(g, axis=0, keepdims=True)
            gaT = w.ga[block].T
            for q in range(tensors):
                w.dctx[q, :, block] = dot(own.outward[q // 2, q % 2], gaT).astype(BF)

    @pl.when(section == 0)
    def _():
        turn_operands()
        for n, block in enumerate(blocks):
            feed_back(n, block)

    @pl.when(section == 1)
    def _():
        feed_back(0, slice(0, length))

    @pl.when(section == 0)
    def _():
        feed_products()

    for own_in in loads:
        wait(own_in.qkv, own_in.ctx, own_in.inv)
    wait(probs_copy)
    qkv = (views[0].qkv, views[1].qkv)
    text_rows, layout_rows = slice(0, HEAD_TEXT), slice(HEAD_TEXT, HEAD_TEXT + HEAD_LAYOUT)

    def turn(k, n_known):
        fixed = isinstance(k, int)

        def at(i, stage):
            if not fixed:
                pl.when((i >= 0) & (i < n_feed))(lambda: stage(feed_chunk(i)))
            elif 0 <= i < n_known:
                stage(chunks[i])

        def sibling_and_send(c):
            stage_sibling(c)
            to_partner(c).start()

        at(k + ahead, sibling_and_send)
        at(k, stage_partner)
        if chain:
            at(k - 1, stage_near)
            at(k - 2, stage_cross)
            at(k - 3, stage_total)

    early_turns = 4

    @pl.loop(0, tensors)
    def _(q):
        for local in range(local_heads):
            head = q * local_heads + local

            @pl.when((section == 0) & (head % 4 == 0) & (head < 4 * (early_turns - 1)))
            def _():
                turn(head // 4, n_feed)

            inv = views[0].inv[q, local : local + 1, :]
            scaled = [
                (work[s].dctx[q, local * SIZES[s] : (local + 1) * SIZES[s], :].astype(F32) * inv).astype(BF)
                for s in range(2)
            ]
            inner = [
                jnp.sum(
                    scaled[s].astype(F32)
                    * views[s].ctx[q, local * SIZES[s] : (local + 1) * SIZES[s], :].astype(F32),
                    axis=0, keepdims=True,
                )
                for s in range(2)
            ]
            rows16 = lax.broadcasted_iota(jnp.int32, (16, length), 0)
            extra = jnp.zeros((16, length), F32)
            for i, value in enumerate((inner[0] + inner[1], inner[1])):
                high = value.astype(BF).astype(F32)
                extra = jnp.where(rows16 == 2 * i, -high, extra)
                extra = jnp.where(rows16 == 2 * i + 1, high - value, extra)
            pad = jnp.zeros((128 - sum(SIZES) - 16, length), BF)
            dcT = jnp.concatenate([*scaled, extra.astype(BF), pad], axis=0)
            dc = dcT.T
            qT, kT = (head_rows(qkv, q, kind, local, SCALES if kind == 0 else None) for kind in range(2))
            v_text, v_layout = (head_part(qkv, q, 2, local, s) for s in range(2))
            one, other_one = (((rows16 // 2) == i).astype(F32).astype(BF) for i in range(2))
            low = probs_in[q, local]
            probs = low.astype(F32)
            both = dot(dc, jnp.concatenate([v_text, v_layout, one, pad], axis=0))
            ds_both = (probs * both).astype(BF)
            single = dot(dc, jnp.concatenate([jnp.zeros_like(v_text), v_layout, other_one, pad], axis=0))
            ds_layout = (probs * single).astype(BF)
            dvT = dot(dcT, low)
            put_head(qkv, q, 2, local, 0, dvT[text_rows])
            put_head(qkv, q, 2, local, 1, dvT[layout_rows])
            k = kT.T
            lane = lax.broadcasted_iota(jnp.int32, (length, 128), 1)
            dq = jnp.where(lane < HEAD_TEXT, dot(ds_both, k) * SCALES[0], dot(ds_layout, k) * SCALES[1])
            dqT = dq.astype(BF).T
            put_head(qkv, q, 0, local, 0, dqT[text_rows])
            put_head(qkv, q, 0, local, 1, dqT[layout_rows])
            put_head(qkv, q, 1, local, 0, dot(qT[text_rows], ds_both))
            put_head(qkv, q, 1, local, 1, dot(qT[layout_rows], ds_layout))

    @pl.when(section == 0)
    def _():
        turn(early_turns - 1, n_feed)

    wait(loads[0].project, loads[1].project)
    page_sum = jnp.zeros((1, work[0].dz.shape[1]), F32)
    for n, block in enumerate(blocks):
        for b in (1, 0):
            down = work[b].dz[block]
            for q in range(tensors):
                down += dot(qkv[b][q, :, block].T, views[b].project[q // 2, q % 2])
            down = down.astype(BF)
            work[b].g[block] = down
            if b == 0:
                page_sum += jnp.sum(down.astype(F32), axis=0, keepdims=True)

            @pl.when(section == 1)
            def _():
                hop(b, n).start()

    wait(loads[1].low, loads[1].act)
    work[1].lowT[...] = views[1].low[...].T
    for own_in in loads:
        wait(own_in.x)
    @pl.when(section == 1)
    def _():
        turn_operands()
        feed_products()

    for c in chunks[n_feed:]:
        later_product(c)

    @pl.when(section == 0)
    def _():
        flipped[...] = work[1].g[...].T
        each_page(0, page_start)

    at_page = (lax.broadcasted_iota(jnp.int32, lang_ids.shape, 0) == t % 2) & (
        lax.broadcasted_iota(jnp.int32, lang_ids.shape, 1) == t // 2
    )
    group = jnp.sum(jnp.where(at_page, lang_ids[...], 0), axis=(0, 1), keepdims=True)
    n_lang = small_out.shape[1] - 8
    chosen = (lax.broadcasted_iota(jnp.int32, (n_lang, 1), 0) == group) & (section == 0)
    small_sum[0, 0:n_lang] = jnp.where(chosen, page_sum, 0.0)
    small_sum[0, n_lang : n_lang + 4] = work[0].sums[...]
    small_sum[0, n_lang + 4 : n_lang + 8] = jnp.zeros((4, small_out.shape[2]), F32)
    small_sum[0, n_lang + 4 : n_lang + 8, : work[1].sums.shape[1]] = work[1].sums[...]

    def small_copy(i, device):
        return remote(small_sum.at[i], small_got.at[i], small_send.at[i], small_recv.at[i], device)

    if chain:
        small_copy(0, sibling).start()
    @pl.when(section == 1)
    def _():
        @pl.loop(0, early_turns)
        def _(k):
            turn(k, n_feed)

    for k in range(early_turns, len(chunks) + (3 if chain else 0)):
        turn(k, len(chunks))
        if not chain:
            continue
        if k == early_turns:
            small_copy(0, sibling).wait_recv()
            small_sum[1] = small_sum[0] + small_got[0]
            small_copy(1, partner).start()
        if k == early_turns + 1:
            small_copy(1, partner).wait_recv()
            small_sum[2] = small_sum[1] + small_got[1]
            small_copy(2, near).start()
        if k == early_turns + 2:
            small_copy(2, near).wait_recv()
            small_sum[3] = small_sum[2] + small_got[2]

            @pl.when(jnp.logical_not(outer))
            def _():
                small_copy(3, cross).start()

        if k == early_turns + 3:
            @pl.when(jnp.logical_not(outer))
            def _():
                small_copy(3, cross).wait_recv()
                small_sum[4] = small_sum[3] + small_got[3]
                small_copy(4, near).start()

        if k == early_turns + 4:
            @pl.when(outer)
            def _():
                small_copy(4, near).wait_recv()
                small_sum[4] = small_got[4]

            small_sum[5] = small_sum[4]
            small_copy(5, other).start()

    if chain:
        for i, device in enumerate((sibling, partner, near)):
            small_copy(i, device).wait_send()

        @pl.when(jnp.logical_not(outer))
        def _():
            small_copy(3, cross).wait_send()
            small_copy(4, near).wait_send()

        small_copy(5, other).wait()
        small_out[0] = small_sum[5]
        small_out[1] = small_got[5]
    else:
        small_out[0] = small_sum[0]
        small_out[1] = small_sum[0]

    @pl.when(section == 1)
    def _():
        for b in range(2):
            for n in range(len(blocks)):
                hop(b, n).wait_send()

    for c in chunks:
        to_sibling(c).wait_send()
        to_partner(c).wait_send()
        if not chain:
            out_copy(c, work[c.b].from_partner).wait()
            continue

        @pl.when(outer)
        def _():
            to_near(c).wait_send()

        @pl.when(jnp.logical_not(outer))
        def _():
            to_cross(c).wait_send()
            total_to_near(c).wait_send()

        out_copy(c, work[c.b].from_partner).wait()

    for g in range(sections):
        each_page(g, page_sent)
        for a in range(2):
            for j in range(2):
                dst = kinds[g][a].at[j]
                remote(dst, dst, page_send.at[0, a], page_recv.at[g, a, j], partner).wait_recv()
    landed = (text_out, layout_out, grad_out, layout_grad_out)
    copies = [pltpu.make_async_copy(v, h, page_out_sem.at[i]) for i, (v, h) in enumerate(zip(landed, page_outs))]
    start(*copies)
    wait(*copies)


def layer_backward(mesh, x, y, probs, roots, kept, weights, cots, norms, lang_ids, n_lang):
    sections, dp, tensors = mesh.shape["section"], mesh.shape["dp"], mesh.shape["tensor"]
    chain = dp == 4
    weights = tuple(Weights(*(m.reshape((tensors // 2, 2) + m.shape[1:]) for m in w)) for w in weights)
    needed = tuple(
        Needed(
            n2=k.n2, downward=w.downward, slope=k.slope, upward=w.upward, n1=k.n1,
            outward=w.outward, low=k.low, act=k.act, qkv=k.qkv, ctx=k.ctx, inv=k.inv, project=w.project, x=rows,
        )
        for k, w, rows in zip(kept, weights, x)
    )
    flat_in, in_tree = jax.tree.flatten((needed, probs, roots))
    plain = [v for own in needed for name, v in own._asdict().items() if name not in Weights._fields] + [probs, roots]
    stacks = [(matrix_starts(own)[MATRICES], rows.shape[1]) for own, rows in zip(needed, x)]
    length = x[0].shape[0]
    work = []
    for own, rows, (count, width) in zip(needed, x, stacks):
        work += Work(
            g=shape(rows.shape), gf=shape(rows.shape), ga=shape(rows.shape), dz=shape(rows.shape, F32),
            dctx=shape(own.ctx.shape), sums=shape((4, width), F32), lowT=shape((width, length)),
            raw=shape((tensors // 2, 2, count, width)), from_sibling=shape((tensors // 2, count, width)),
            from_partner=shape((count, width)),
        )
    small = shape((2, n_lang + 8, x[0].shape[1]), F32)
    text_page = shape((2, length // tensors, x[0].shape[1]))
    layout_page = shape((2, x[1].shape[1], length // tensors))
    summed = [shape(s) for s in stacks]
    own = needed[0]
    n_chunks = (own.upward.shape[-2] + own.downward.shape[-2]) // (2 * ROWS) + 4
    n_blocks = len(hop_blocks(length))
    dma = pltpu.SemaphoreType.DMA
    results = pl.pallas_call(
        functools.partial(backward_kernel, sections, tensors, chain, in_tree),
        out_shape=summed + [small, text_page, layout_page, text_page, layout_page],
        in_specs=[ANY] * (len(flat_in) + 4) + [VMEM] * 3,
        out_specs=[ANY] * 2 + [VMEM] + [ANY] * 4,
        scratch_shapes=vmem_like(work) + vmem_like(plain)
        + [pltpu.VMEM(cots[1].shape, BF)] + [pltpu.VMEM((6,) + small.shape[1:], F32)] * 2
        + vmem_like([text_page, layout_page] * 2)
        + [dma((len(flat_in),)), dma((2,)), dma((2, n_blocks)), dma((2, n_blocks))]
        + [dma((n_chunks,))] * 2 + [dma((4, n_chunks))] * 2
        + [pltpu.SemaphoreType.REGULAR, dma((n_chunks,))]
        + [dma((6,))] * 2 + [dma((tensors, 2)), dma((sections, 2, 2)), dma((4,))],
        compiler_params=pltpu.CompilerParams(
            collective_id=1, has_side_effects=True, vmem_limit_bytes=64 << 20
        ),
        name="layer_backward",
    )(*flat_in, *cots, *y, lang_ids, norms[0][0], norms[1][0])
    totals, small, pages = results[:2], results[2], results[3:7]
    if not chain:
        totals = lax.psum(tuple(totals), "dp")
        both = lax.psum(small[0], ("dp", "tensor"))
        small = jnp.stack([both, lax.ppermute(both, "section", [(0, 1), (1, 0)])])
    return totals, small, pages


def widen_kernel(n_in, n_pages, *refs):
    n_out = 5 + n_pages + 2 * MATRICES
    hbm_in, hbm_out = refs[:n_in], refs[n_in : n_in + n_out]
    vmem_in, vmem_out = refs[n_in + n_out : 2 * n_in + n_out], refs[2 * n_in + n_out : -2]
    in_sem, out_sem = refs[-2:]
    loads = [pltpu.make_async_copy(h, v, in_sem.at[i]) for i, (h, v) in enumerate(zip(hbm_in, vmem_in))]
    sources = vmem_out[:5] + vmem_in[3:] + vmem_out[5:]
    stores = [pltpu.make_async_copy(v, h, out_sem.at[i]) for i, (v, h) in enumerate(zip(sources, hbm_out))]
    start(*loads)
    totals, small = vmem_in[0:2], vmem_in[2]
    for b in range(2):
        wait(loads[b])
        at = 0
        for i in range(b * MATRICES, (b + 1) * MATRICES):
            out = vmem_out[5 + i]
            for c in range(0, out.shape[0], 48):
                out[c : c + 48] = totals[b][at + c : at + c + 48].astype(F32)
            at += out.shape[0]
            stores[5 + n_pages + i].start()
    for i in range(n_pages):
        loads[3 + i].wait()
        stores[5 + i].start()
    loads[2].wait()
    n_lang = vmem_out[0].shape[0]
    vmem_out[0][...] = jnp.where(lax.axis_index("section") == 0, small[0, :n_lang], small[1, :n_lang])
    for i, out in enumerate(vmem_out[1:5]):
        first = n_lang + 2 * i
        out[...] = small[0, first : first + 2, : out.shape[1]]
    start(*stores[:5])
    wait(*stores)


def widen(totals, small, pages, shards, n_lang):
    widths = [total.shape[1] for total in totals]
    sums = [shape((n_lang, widths[0]), F32)] + [shape((2, w), F32) for w in widths for _ in range(2)]
    grads = [shape(m.shape, F32) for own in shards for m in own]
    inputs = (*totals, small, *pages)
    outs = sums + [shape(page.shape) for page in pages] + grads
    results = pl.pallas_call(
        functools.partial(widen_kernel, len(inputs), len(pages)), out_shape=outs,
        in_specs=[ANY] * len(inputs), out_specs=[ANY] * len(outs),
        scratch_shapes=vmem_like(inputs) + vmem_like(sums + grads)
        + [pltpu.SemaphoreType.DMA((len(inputs),)), pltpu.SemaphoreType.DMA((len(outs),))],
        compiler_params=pltpu.CompilerParams(vmem_limit_bytes=62 << 20), name="widen",
    )(*inputs)
    return results[0], results[1:5], results[5:9], results[9:13], results[13:17]


def per_device(
    mesh,
    text_input,
    layout_input,
    text_cotangent,
    layout_cotangent,
    page_counts,
    pad_mask,
    lang_ids,
    lang_table,
    text_project,
    text_outward,
    text_upward,
    text_downward,
    text_gains,
    text_biases,
    layout_project,
    layout_outward,
    layout_upward,
    layout_downward,
    layout_gains,
    layout_biases,
):
    def flat(project):
        return jnp.transpose(project[0], (1, 2, 0)).reshape(-1, project.shape[1])

    def flipped(block):
        return jnp.transpose(block[0], (0, 2, 1))

    shards = (
        Weights(flat(text_project), text_outward[0], text_upward[0], text_downward[0]),
        Weights(flat(layout_project), layout_outward[0], layout_upward[0], layout_downward[0]),
    )
    norms = ((text_gains[0], text_biases[0]), (layout_gains[0], layout_biases[0]))
    marks = (pad_mask, page_counts, lang_ids, lang_table)
    (x, y, probs, roots, kept, weights), cots = layer_forward(
        mesh, text_input[0], flipped(layout_input), text_cotangent[0], flipped(layout_cotangent), shards, norms, marks
    )
    n_lang = lang_table.shape[0]
    totals, small, pages = layer_backward(mesh, x, y, probs, roots, kept, weights, cots, norms, lang_ids, n_lang)
    lang_sum, norm_sums, pages, text_sums, layout_sums = widen(totals, small, pages, shards, n_lang)
    text_out, layout_out, text_grad, layout_grad = pages

    def unflat(grad, like):
        return jnp.transpose(grad.reshape(like.shape[2], like.shape[3], like.shape[1]), (2, 0, 1))[None]

    unflip = lambda block: jnp.transpose(block, (0, 2, 1))[None]
    return (
        text_out[None], unflip(layout_out), text_grad[None], unflip(layout_grad), lang_sum,
        unflat(text_sums[0], text_project), *(s[None] for s in text_sums[1:]), norm_sums[0][None], norm_sums[1][None],
        unflat(layout_sums[0], layout_project), *(s[None] for s in layout_sums[1:]),
        norm_sums[2][None], norm_sums[3][None],
    )


def solution(mesh):
    tokens = P("section", "dp", "tensor", None)
    weight_specs = (
        P("section", None, None, "tensor"), P("section", "tensor", None), P("section", None, "tensor"),
        P("section", "tensor", None), P("section", None, None), P("section", None, None),
    )
    in_specs = (tokens,) * 4 + (P(None, "dp"), P(None, "dp", None), P(None, "dp"), P()) + weight_specs * 2
    out_specs = (tokens,) * 4 + (P(),) + weight_specs * 2
    return jax.shard_map(
        functools.partial(per_device, mesh), mesh=mesh, in_specs=in_specs, out_specs=out_specs, check_vma=False
    )
```

```python
import functools
import math
import typing

import jax
import jax.numpy as jnp
from jax import lax
from jax.experimental import pallas as pl
from jax.experimental.pallas import tpu as pltpu
from jax.sharding import PartitionSpec as P

HEAD_TEXT = 64
HEAD_LAYOUT = 16
EPSILON = 1e-05
NEGATIVE = -1e30
HIGH = lax.Precision.HIGHEST
MESH = pl.DeviceIdType.MESH
BF = jnp.bfloat16
F32 = jnp.float32
ANY = pl.BlockSpec(memory_space=pl.ANY)


def remote(src, dst, send, recv, device):
    return pltpu.make_async_remote_copy(
        src_ref=src, dst_ref=dst, send_sem=send, recv_sem=recv, device_id=device, device_id_type=MESH
    )


def greet(section, tensor, sections, tensors, extra=()):
    barrier = pltpu.get_barrier_semaphore()
    for g in range(sections):
        for q in range(tensors):

            @pl.when((section != g) | (tensor != q))
            def _():
                pl.semaphore_signal(
                    barrier, inc=1, device_id={"section": g, "tensor": q}, device_id_type=MESH
                )

    for device in extra:
        pl.semaphore_signal(barrier, inc=1, device_id=device, device_id_type=MESH)
    pl.semaphore_wait(barrier, sections * tensors - 1 + len(extra))


GELU_P = 0.3275911
GELU_A = (0.254829592, -0.284496736, 1.421413741, -1.453152027, 1.061405429)
NN = (((1,), (0,)), ((), ()))
NT = (((1,), (1,)), ((), ()))
SCALES = (1.0 / math.sqrt(HEAD_TEXT), 1.0 / math.sqrt(HEAD_LAYOUT))
SIZES = (HEAD_TEXT, HEAD_LAYOUT)
ROWS = 128


class Weights(typing.NamedTuple):
    project: typing.Any
    outward: typing.Any
    upward: typing.Any
    downward: typing.Any


class Kept(typing.NamedTuple):
    qkv: typing.Any
    ctx: typing.Any
    inv: typing.Any
    n1: typing.Any
    low: typing.Any
    act: typing.Any
    slope: typing.Any
    n2: typing.Any


def dot(a, b, dims=NN):
    return lax.dot_general(a, b, dims, preferred_element_type=F32)


def gelu_pair(u):
    d = 1.0 + (GELU_P / math.sqrt(2.0)) * jnp.abs(u)
    t = pl.reciprocal(d, approx=True)
    t = t * (2.0 - d * t)
    e = jnp.exp2((u * u) * (-0.5 / math.log(2.0)))
    a1, a2, a3, a4, a5 = (0.5 * a for a in GELU_A)
    tail = ((((a5 * t + a4) * t + a3) * t + a2) * t + a1) * t * e
    cdf = jnp.where(u >= 0, 1.0 - tail, tail)
    return u * cdf, cdf + u * e * (1.0 / math.sqrt(2.0 * math.pi))


def norm_rows(z, gain, offset):
    center = z - jnp.mean(z, axis=-1, keepdims=True)
    inverse = lax.rsqrt(jnp.mean(center * center, axis=-1, keepdims=True) + EPSILON)
    normed = center * inverse
    return normed * gain + offset, normed, inverse


def norm_rows_back(g, n, r, gain):
    t = g * gain
    return r * (t - jnp.mean(t, axis=-1, keepdims=True) - n * jnp.mean(t * n, axis=-1, keepdims=True))


class Staged:
    def __init__(self, tree, hbm, vmem, sem, inward):
        self.tree, self.vmem = tree, list(vmem)
        pairs = zip(hbm, vmem) if inward else zip(vmem, hbm)
        self.copies = [pltpu.make_async_copy(a, b, sem.at[i]) for i, (a, b) in enumerate(pairs)]

    def refs(self):
        return jax.tree.unflatten(self.tree, self.vmem)

    def parts(self):
        return jax.tree.unflatten(self.tree, self.copies)

    def start(self):
        for copy in self.copies:
            copy.start()

    def wait(self):
        for copy in self.copies:
            copy.wait()


def start(*copies):
    for copy in copies:
        copy.start()


def wait(*copies):
    for copy in copies:
        copy.wait()


def head_rows(stacks, slot, kind, local, scales=None, extra=None):
    rows = []
    for b in range(2):
        piece = head_part(stacks, slot, kind, local, b)
        rows.append(piece if scales is None else piece * BF(scales[b]))
    length = rows[0].shape[1]
    rows.append(jnp.zeros((16, length), BF) if extra is None else extra)
    rows.append(jnp.zeros((128 - sum(SIZES) - 16, length), BF))
    return jnp.concatenate(rows, axis=0)


def head_part(stacks, slot, kind, local, b):
    first = kind * (stacks[b].shape[1] // 3) + local * SIZES[b]
    return stacks[b][slot, first : first + SIZES[b], :]


def small_blocks(block, step=64):
    return [slice(c, c + step) for c in range(block.start, block.stop, step)]


def put_head(stacks, slot, kind, local, b, value):
    first = kind * (stacks[b].shape[1] // 3) + local * SIZES[b]
    stacks[b][slot, first : first + SIZES[b], :] = value.astype(BF)


def hop_blocks(length):
    ends = [0, length // 2, length * 3 // 4, length]
    return [slice(a, b) for a, b in zip(ends, ends[1:])]


def slot_of(u, core, chip):
    return ((chip + u // 2) % 2) * 2 + (core + u % 2) % 2


def forward_kernel(sections, tensors, shared, in_tree, out_tree, *refs):
    n_w, n_out = len(shared), out_tree.num_leaves
    sources = (refs[0:2], refs[2:4])
    shards = refs[4 : 4 + n_w]
    pad_mask, counts, lang_ids, lang_table, *norms = refs[4 + n_w : 12 + n_w]
    rest = refs[12 + n_w :]
    hbm_out, cots_out, rest = rest[:n_out], rest[n_out : n_out + 2], rest[n_out + 2 :]
    outgoing = Staged(out_tree, hbm_out, rest[:n_out], rest[n_out], False)
    rest = rest[n_out + 1 :]
    flipped, raw_x, y_narrow, *rest = rest
    nats, totals, pre, score_buffer, rest = rest[0:2], rest[2:4], rest[4:6], rest[6], rest[7:]
    xT, turned, turn_sem, rest = rest[0:2], (rest[2:4], rest[4:6]), rest[6], rest[7:]
    page_send, page_recv, w_send, w_recv, own_sem, hop_send, hop_recv, cot_sem, act_sem = rest
    x, y_pages, probs_out, roots, kept, weights = outgoing.refs()
    y = (y_pages[0], y_narrow)
    x_out, y_out, probs_copy, roots_copy, kept_out, weights_out = outgoing.parts()
    kept_hbm, weights_hbm = jax.tree.unflatten(out_tree, list(hbm_out))[4:6]
    section, d, t = lax.axis_index("section"), lax.axis_index("dp"), lax.axis_index("tensor")
    core, chip, half_index = t % 2, t // 2, d % 2
    sibling, partner = t + 1 - 2 * core, (t + tensors // 2) % tensors
    mate = d + 1 - 2 * half_index
    micro, page = core, chip
    part_length = sources[0][0].shape[1]
    length = x[0].shape[0]
    blocks = [slice(c, c + 2 * ROWS) for c in range(0, length, 2 * ROWS)]
    parts = hop_blocks(length)
    full = (
        weights[0].project, weights[1].project, weights[0].outward, weights[0].upward,
        weights[0].downward, weights[1].outward, weights[1].upward, weights[1].downward,
    )
    greet(section, t, sections, tensors, ({"dp": mate},) if any(shared) else ())

    def half_of(ref, i, which):
        count = shards[i].shape[0] // 2
        return ref.at[pl.ds(pl.multiple_of(which * count, 16), count)] if shared[i] else ref

    def to_partner(i):
        return remote(
            half_of(shards[i], i, half_index), half_of(full[i].at[t], i, half_index),
            w_send.at[0, i], w_recv.at[0, i], {"tensor": partner},
        )

    def to_sibling(i):
        return remote(full[i].at[t], full[i].at[t], w_send.at[1, i], w_recv.at[1, i], {"tensor": sibling})

    def to_mate(i):
        ref = half_of(full[i].at[partner], i, half_index)
        return remote(ref, ref, w_send.at[2, i], w_recv.at[2, i], {"dp": mate})

    def on_first(i):
        ref = half_of(full[i].at[partner], i, half_index)
        return remote(ref, ref, w_send.at[3, i], w_recv.at[3, i], {"tensor": sibling})

    def on_second(i):
        ref = half_of(full[i].at[partner], i, 1 - half_index)
        return remote(ref, ref, w_send.at[4, i], w_recv.at[4, i], {"tensor": sibling})

    def keep(i):
        return pltpu.make_async_copy(shards[i], full[i].at[t], own_sem.at[i])

    def relay(*which):
        for i in which:
            to_partner(i).wait_recv()
            if shared[i]:
                to_mate(i).start()
            on_first(i).start()

    def relay_second(*which):
        for i in which:
            if shared[i]:
                to_mate(i).wait_recv()
                on_second(i).start()

    def early(*which):
        for i in which:
            to_sibling(i).wait_recv()

    def late(*which):
        for i in which:
            on_first(i).wait_recv()
            if shared[i]:
                on_second(i).wait_recv()

    def token_slot(g, a, index):
        start_at = pl.multiple_of(index * part_length, part_length)
        target = (raw_x, flipped)[a]
        return target.at[pl.ds(start_at, part_length)] if a == 0 else target.at[:, pl.ds(start_at, part_length)]

    def over_pages(g, act):
        for j in range(2):
            target = 2 * j + section
            here = (section == g) & (t == target)
            for a in range(2):
                act(g, j, a, target, here)

    def page_copy(g, j, a, target):
        return remote(
            sources[g][a].at[j], token_slot(g, a, t), page_send.at[g, j, a], page_recv.at[a, t],
            {"section": g, "tensor": target},
        )

    def page_start(g, j, a, target, here):
        @pl.when(here)
        def _():
            pltpu.make_async_copy(sources[g][a].at[j], token_slot(g, a, t), page_recv.at[a, t]).start()

        @pl.when(jnp.logical_not(here))
        def _():
            page_copy(g, j, a, target).start()

    def page_sent(g, j, a, target, here):
        @pl.when(jnp.logical_not(here))
        def _():
            page_copy(g, j, a, target).wait_send()

    def pages_arrived(g):
        for a in range(2):
            for q in range(tensors):
                slot = token_slot(g, a, q)
                remote(slot, slot, page_send.at[0, 0, a], page_recv.at[a, q], {"tensor": sibling}).wait_recv()

    def parts_of(b):
        return parts if b == 0 else [slice(0, length)]

    def hop(b, n):
        part = parts_of(b)[n]
        return remote(
            y[b].at[part], x[b].at[part], hop_send.at[b, n], hop_recv.at[b, n], {"section": 1 - section}
        )

    def weights_to_hbm():
        for b in range(2):
            start(weights_out[b].project, weights_out[b].outward)
            for q in range(tensors):
                for m, name in enumerate((2, 3)):
                    copy = pltpu.make_async_copy(
                        turned[b][m].at[q % 2], weights_hbm[b][name].at[q], turn_sem.at[b, m, q % 2]
                    )
                    if q >= 2:
                        copy.wait()
                    turned[b][m][q % 2] = weights[b][name][q].T
                    copy.start()
        for b in range(2):
            for q in range(tensors - 2, tensors):
                for m, name in enumerate((2, 3)):
                    pltpu.make_async_copy(
                        turned[b][m].at[q % 2], weights_hbm[b][name].at[q], turn_sem.at[b, m, q % 2]
                    ).wait()

    over_pages(0, page_start)
    for i in range(n_w):
        keep(i).start()
    for i in range(n_w):
        to_partner(i).start()
    over_pages(1, page_start)
    for i in range(n_w):
        keep(i).wait()
        to_sibling(i).start()

    at_page = (lax.broadcasted_iota(jnp.int32, counts.shape, 0) == micro) & (
        lax.broadcasted_iota(jnp.int32, counts.shape, 1) == page
    )

    def own_entry(ref):
        return jnp.sum(jnp.where(at_page, ref[...], 0), axis=(0, 1), keepdims=True)

    positions = lax.broadcasted_iota(jnp.int32, (1, length), 1)
    mask_row = pad_mask[micro, pl.ds(page, 1), :]
    key_mask = (positions < own_entry(counts)) & ((mask_row == 1) | (positions == 0))
    first_row = (lax.broadcasted_iota(jnp.int32, (16, length), 0) == 0).astype(F32)
    mask_row16 = (first_row * jnp.where(key_mask, 0.0, NEGATIVE)).astype(BF)
    groups = lax.broadcasted_iota(jnp.int32, (lang_table.shape[0], 1), 0)
    lang_row = jnp.sum(jnp.where(groups == own_entry(lang_ids), lang_table[...], 0.0), axis=0, keepdims=True)
    local_heads = weights[0].project.shape[1] // (3 * HEAD_TEXT)
    qkv = (kept[0].qkv, kept[1].qkv)

    @pl.when(section == 0)
    def _():
        pages_arrived(0)
        x[0][...] = (raw_x[...].astype(F32) + lang_row).astype(BF)
        x[1][...] = flipped[...].T
        early(0, 1)

    @pl.when(section == 1)
    def _():
        relay(*range(n_w))
        relay_second(*range(n_w))
        early(*range(n_w))
        late(*range(n_w))
        weights_to_hbm()

    @pl.loop(0, 2)
    def _(half):
        @pl.when((half == 1) & (section == 0))
        def _():
            relay(0, 1)
            relay_second(0)
            late(0, 1)

        for n, block in enumerate(parts):
            @pl.when((half == 0) & (section == 1))
            def _():
                for b in range(2):
                    if n < len(parts_of(b)):
                        hop(b, n).wait_recv()

            @pl.when(half == 0)
            def _():
                for b in range(2):
                    xT[b][:, block] = x[b][block].T

            @pl.loop(0, 2)
            def _(u):
                slot = slot_of(2 * half + u, core, chip)
                for b in range(2):
                    qkv[b][slot, :, block] = dot(weights[b].project[slot], xT[b][:, block]).astype(BF)

        @pl.loop(0, 2)
        def _(u):
            slot = slot_of(2 * half + u, core, chip)
            for local in range(local_heads):
                q = head_rows(qkv, slot, 0, local, SCALES, first_row.astype(BF)).T
                kT = head_rows(qkv, slot, 1, local, None, mask_row16)
                score_buffer[local] = dot(q, kT)
                for rows in small_blocks(slice(0, length)):
                    scores = score_buffer[local, rows, :]
                    raised = jnp.exp(scores - jnp.max(scores, axis=-1, keepdims=True))
                    probs_out[slot, local, rows, :] = raised.astype(BF)
                vT = head_rows(qkv, slot, 2, local, None, first_row.astype(BF))
                ctx = dot(probs_out[slot, local], vT.T).T
                inv = 1.0 / ctx[sum(SIZES) : sum(SIZES) + 1]
                ctx = (ctx * inv).astype(BF)
                kept[0].inv[slot, local : local + 1, :] = inv
                kept[0].ctx[slot, local * HEAD_TEXT : (local + 1) * HEAD_TEXT, :] = ctx[:HEAD_TEXT]
                kept[1].ctx[slot, local * HEAD_LAYOUT : (local + 1) * HEAD_LAYOUT, :] = ctx[
                    HEAD_TEXT : HEAD_TEXT + HEAD_LAYOUT
                ]

    kept[1].inv[...] = jnp.zeros(kept[1].inv.shape, F32)
    start(probs_copy, *x_out, *(c for k in kept_out for c in (k.qkv, k.ctx, k.inv)))

    def attend(b):
        gains, biases = norms[2 * b : 2 * b + 2]
        width = x[b].shape[1]
        nats[b][...] = kept[b].ctx[...].reshape(width, length).T
        wide = weights[b].outward[...].reshape(width, width)
        for block in blocks:
            totals[b][1, block] = dot(nats[b][block], wide)
            for rows in small_blocks(block):
                h, n, r = norm_rows(x[b][rows].astype(F32) + totals[b][1, rows], gains[0:1], biases[0:1])
                totals[b][0, rows] = h
                totals[b][1, rows] = jnp.zeros(h.shape, F32)
                kept[b].n1[rows] = n.astype(BF)
                roots[rows, 2 * b : 2 * b + 1] = r
                kept[b].low[rows] = h.astype(BF)
        start(kept_out[b].n1, kept_out[b].low)

    def slot_copies(b, slot):
        return [
            pltpu.make_async_copy(v.at[slot], h.at[slot], act_sem.at[b, m, slot])
            for m, (v, h) in enumerate(((kept[b].act, kept_hbm[b].act), (kept[b].slope, kept_hbm[b].slope)))
        ]

    def feed(b, first, which):
        @pl.loop(first, first + 2)
        def _(u):
            slot = slot_of(u, core, chip)
            for block in which:
                pre[b][block] = dot(kept[b].low[block], weights[b].upward[slot])
                for rows in small_blocks(block, 16):
                    act, slope = gelu_pair(pre[b][rows])
                    kept[b].act[slot, rows] = act.astype(BF)
                    kept[b].slope[slot, rows] = slope.astype(BF)
                totals[b][1, block] += dot(kept[b].act[slot, block], weights[b].downward[slot])
                if block == slice(0, length):
                    start(*slot_copies(b, slot))

    def finish(b):
        gains, biases = norms[2 * b : 2 * b + 2]
        def last(block):
            feed(b, 2, [block])
            for rows in small_blocks(block):
                out, normed, r = norm_rows(totals[b][0, rows] + totals[b][1, rows], gains[1:2], biases[1:2])
                y[b][rows] = out.astype(BF)
                kept[b].n2[rows] = normed.astype(BF)
                roots[rows, 2 * b + 1 : 2 * b + 2] = r

        @pl.when(section == 0)
        def _():
            for n, block in enumerate(parts_of(b)):
                last(block)
                hop(b, n).start()
            if b == 0:
                for u in range(2, 4):
                    start(*slot_copies(b, slot_of(u, core, chip)))

        @pl.when(section == 1)
        def _():
            last(slice(0, length))

        if b == 1:
            y_pages[1][...] = y_narrow[...].T
        start(y_out[b], kept_out[b].n2)

    @pl.when(section == 0)
    def _():
        relay(2, 3)
        early(2)
        late(2)

    attend(0)

    @pl.when(section == 0)
    def _():
        early(3, 4)

    feed(0, 0, [slice(0, length)])

    @pl.when(section == 0)
    def _():
        relay(4, 5, 6, 7)
        relay_second(3)
        early(5, 6, 7)
        late(5, 6, 7)

    attend(1)
    feed(1, 0, [slice(0, length)])
    finish(1)

    @pl.when(section == 0)
    def _():
        relay_second(4)
        late(3, 4)

    finish(0)
    start(roots_copy)

    @pl.when(section == 0)
    def _():
        weights_to_hbm()
        for b in range(2):
            for n in range(len(parts_of(b))):
                hop(b, n).wait_send()

    for i in range(n_w):
        to_partner(i).wait_send()
        to_sibling(i).wait_send()
        on_first(i).wait_send()
        if shared[i]:
            to_mate(i).wait_send()
            on_second(i).wait_send()
    for g in range(sections):
        over_pages(g, page_sent)

    @pl.when(section == 1)
    def _():
        pages_arrived(1)
        copies = [pltpu.make_async_copy(v, h, cot_sem.at[i]) for i, (v, h) in enumerate(zip((raw_x, flipped), cots_out))]
        start(*copies)
        wait(*copies)

    for group in (x_out, y_out, (probs_copy, roots_copy), *(w[:2] for w in weights_out)):
        wait(*group)
    for b, k in enumerate(kept_out):
        wait(k.qkv, k.ctx, k.inv, k.n1, k.low, k.n2)
        for slot in range(tensors):
            wait(*slot_copies(b, slot))


def vmem_like(tree):
    return [pltpu.VMEM(s.shape, s.dtype) for s in jax.tree.leaves(tree)]


VMEM = pl.BlockSpec(memory_space=pltpu.VMEM)


def shape(dims, dtype=BF):
    return jax.ShapeDtypeStruct(tuple(dims), dtype)


def layer_forward(mesh, text_in, layout_in, text_cot, layout_cot, shards, norms, marks):
    sections, dp, tensors = mesh.shape["section"], mesh.shape["dp"], mesh.shape["tensor"]
    length = text_in.shape[1] * tensors
    rows = (shape((length, text_in.shape[2])), shape((length, layout_in.shape[1])))
    local_heads = shards[0].project.shape[0] // (3 * HEAD_TEXT)
    kept = []
    for x, w in zip(rows, shards):
        units = shape((tensors, length, w.upward.shape[1]))
        kept.append(Kept(
            qkv=shape((tensors, w.project.shape[0], length)), ctx=shape((tensors, w.outward.shape[0], length)),
            inv=shape((tensors, local_heads, length), F32),
            n1=shape(x.shape), low=shape(x.shape), act=units, slope=units,
            n2=shape(x.shape),
        ))
    weights = tuple(Weights(*(shape((tensors,) + m.shape) for m in w)) for w in shards)
    pages_out = (rows[0], shape((rows[1].shape[1], length)))
    outs = (rows, pages_out, shape((tensors, local_heads, length, length)), shape((length, 4), F32), tuple(kept), weights)
    flat_out, out_tree = jax.tree.flatten(outs)
    (a, b) = shards
    ordered = (a.project, b.project, a.outward, a.upward, a.downward, b.outward, b.upward, b.downward)
    shared = tuple(dp % 2 == 0 and w.shape[0] >= 512 for w in ordered)
    n_w = len(ordered)
    cots = [rows[0], shape((rows[1].shape[1], length))]
    small = (*marks, *norms[0], *norms[1])
    results = pl.pallas_call(
        functools.partial(forward_kernel, sections, tensors, shared, None, out_tree),
        out_shape=flat_out + cots,
        in_specs=[ANY] * (4 + n_w) + [VMEM] * len(small),
        out_specs=[ANY] * (len(flat_out) + 2),
        scratch_shapes=vmem_like(flat_out) + [pltpu.SemaphoreType.DMA((len(flat_out),))]
        + [pltpu.VMEM(cots[1].shape, BF), pltpu.VMEM(cots[0].shape, BF), pltpu.VMEM(rows[1].shape, BF)]
        + [pltpu.VMEM(x.shape, BF) for x in rows]
        + [pltpu.VMEM((2,) + x.shape, F32) for x in rows]
        + [pltpu.VMEM((length, w.upward.shape[1]), F32) for w in shards]
        + [pltpu.VMEM((local_heads, length, length), F32)]
        + [pltpu.VMEM((x.shape[1], length), BF) for x in rows]
        + [pltpu.VMEM((2,) + m.shape, BF) for w in shards for m in (w.upward, w.downward)]
        + [pltpu.SemaphoreType.DMA((2, 2, 2))]
        + [
            pltpu.SemaphoreType.DMA((sections, 2, 2)), pltpu.SemaphoreType.DMA((2, tensors)),
            pltpu.SemaphoreType.DMA((5, n_w)), pltpu.SemaphoreType.DMA((5, n_w)), pltpu.SemaphoreType.DMA((n_w,)),
            pltpu.SemaphoreType.DMA((2, len(hop_blocks(length)))), pltpu.SemaphoreType.DMA((2, len(hop_blocks(length)))),
            pltpu.SemaphoreType.DMA((2,)), pltpu.SemaphoreType.DMA((2, 2, tensors)),
        ],
        compiler_params=pltpu.CompilerParams(
            collective_id=0, has_side_effects=True, vmem_limit_bytes=62 << 20
        ),
        name="layer_forward",
    )(text_in, layout_in, text_cot, layout_cot, *ordered, *small)
    return jax.tree.unflatten(out_tree, results[:-2]), tuple(results[-2:])


class Needed(typing.NamedTuple):
    n2: typing.Any
    downward: typing.Any
    slope: typing.Any
    upward: typing.Any
    n1: typing.Any
    outward: typing.Any
    low: typing.Any
    act: typing.Any
    qkv: typing.Any
    ctx: typing.Any
    inv: typing.Any
    project: typing.Any
    x: typing.Any


class Work(typing.NamedTuple):
    g: typing.Any
    gf: typing.Any
    ga: typing.Any
    dz: typing.Any
    dctx: typing.Any
    sums: typing.Any
    lowT: typing.Any
    raw: typing.Any
    from_sibling: typing.Any
    from_partner: typing.Any


class Chunk(typing.NamedTuple):
    b: typing.Any
    index: typing.Any
    first: typing.Any
    rows: typing.Any


MATRICES = 4


def matrix_rows(own):
    return own.project.shape[-2], own.outward.shape[-2], own.upward.shape[-2], own.downward.shape[-2]


def matrix_starts(own):
    sizes = matrix_rows(own)
    return [sum(sizes[:i]) for i in range(MATRICES + 1)]


def pieces_of(size, step):
    return [(f, step) for f in range(0, size, step)]


def backward_kernel(sections, tensors, chain, in_tree, *refs):
    n_in = in_tree.num_leaves
    hbm_in, refs = refs[:n_in], refs[n_in:]
    (cots, ys, lang_ids, gains), refs = (refs[0:2], refs[2:4], refs[4], refs[5:7]), refs[7:]
    results, small_out, page_outs, refs = refs[0:2], refs[2], refs[3:7], refs[7:]
    n_work = len(Work._fields)
    work, refs = (Work(*refs[:n_work]), Work(*refs[n_work : 2 * n_work])), refs[2 * n_work :]
    plain, refs = refs[: n_in - 2 * MATRICES], refs[n_in - 2 * MATRICES :]
    flipped, small_got, small_sum, refs = refs[0], refs[1], refs[2], refs[3:]
    text_out, layout_out, grad_out, layout_grad_out, *refs = refs
    in_sem, cot_sem, hop_send, hop_recv, sib_send, sib_recv, send, recv, credit, out_sem, *refs = refs
    small_send, small_recv, page_send, page_recv, page_out_sem = refs
    section, d, t = lax.axis_index("section"), lax.axis_index("dp"), lax.axis_index("tensor")
    core, chip = t % 2, t // 2
    sibling = {"tensor": t + 1 - 2 * core}
    partner = {"tensor": (t + tensors // 2) % tensors}
    near, cross = {"dp": d + 1 - 2 * (d % 2)}, {"dp": 3 - d}
    outer = (d == 0) | (d == 3)
    other = {"section": 1 - section}
    hbm, probs_hbm, roots_hbm = jax.tree.unflatten(in_tree, hbm_in)
    starts = [matrix_starts(own) for own in hbm]

    plain = list(plain)
    views = []
    for b in range(2):
        fields = {}
        for name, value in hbm[b]._asdict().items():
            if name in Weights._fields:
                i = Weights._fields.index(name)
                fields[name] = work[b].raw.at[:, :, pl.ds(starts[b][i], starts[b][i + 1] - starts[b][i])]
            else:
                fields[name] = plain.pop(0)
        views.append(Needed(**fields))
    probs_in, roots = plain
    flat_views = jax.tree.leaves((tuple(views), probs_in, roots))
    flat_copies = [pltpu.make_async_copy(a, v, in_sem.at[i]) for i, (a, v) in enumerate(zip(hbm_in, flat_views))]
    loads, probs_copy, roots_copy = jax.tree.unflatten(in_tree, flat_copies)
    length = work[0].gf.shape[0]
    local_heads = probs_in.shape[1]
    blocks = hop_blocks(length)
    cot_copies = (
        pltpu.make_async_copy(cots[0], work[0].g, cot_sem.at[0]),
        pltpu.make_async_copy(cots[1], flipped, cot_sem.at[1]),
    )

    @pl.when(section == 1)
    def _():
        start(*cot_copies)

    roots_copy.start()
    for field in zip(loads[1], loads[0]):
        start(*field)
    probs_copy.start()
    greet(section, t, sections, tensors, (near, cross) if chain else ())

    part_length = text_out.shape[1]
    micro, page = core, chip
    kinds = ((grad_out, layout_grad_out), (text_out, layout_out))
    pages = ((work[0].g, flipped), ys)

    def page_part(g, q, a):
        span = pl.ds(q * part_length, part_length)
        return pages[g][a].at[span] if a == 0 else pages[g][a].at[:, span]

    def each_page(g, act):
        for q in range(tensors):
            for a in range(2):
                here = (micro == g) & (t == q)

                @pl.when((section == g) & here)
                def _():
                    act(g, q, a, True)

                @pl.when((section == g) & jnp.logical_not(here))
                def _():
                    act(g, q, a, False)

    def page_copy(g, q, a):
        return remote(
            page_part(g, q, a), kinds[g][a].at[page], page_send.at[q, a], page_recv.at[g, a, page],
            {"section": micro, "tensor": q},
        )

    def page_start(g, q, a, here):
        if here:
            pltpu.make_async_copy(page_part(g, q, a), kinds[g][a].at[page], page_recv.at[g, a, page]).start()
        else:
            page_copy(g, q, a).start()

    def page_sent(g, q, a, here):
        if not here:
            page_copy(g, q, a).wait_send()

    each_page(1, page_start)

    def blocks_of(b):
        return blocks if b == 0 else [slice(0, length)]

    def hop(b, n):
        part = work[b].g.at[blocks_of(b)[n]]
        return remote(part, part, hop_send.at[b, n], hop_recv.at[b, n], other)

    ahead = 2
    step = 2 * ROWS
    up_first, down_first = starts[0][2], starts[0][3]
    up_count, down_count = (starts[0][3] - up_first) // step, (starts[0][4] - down_first) // step
    n_feed = up_count + down_count
    chunks = [Chunk(0, k, up_first + k * step, step) for k in range(n_feed)]
    later = [(1, 0, starts[1][MATRICES])]
    later += [(0, f, n) for f, n in pieces_of(starts[0][1], starts[0][1] // 2)]
    later += [(0, starts[0][1] + f, n) for f, n in pieces_of(starts[0][2] - starts[0][1], starts[0][2] - starts[0][1])]
    chunks += [Chunk(b, n_feed + i, f, n) for i, (b, f, n) in enumerate(later)]

    def feed_chunk(k):
        return Chunk(0, k, pl.multiple_of(up_first + k * step, 16), step)

    def span(ref, c):
        return ref.at[pl.ds(c.first, c.rows)]

    def to_sibling(c):
        w, rows = work[c.b], pl.ds(c.first, c.rows)
        return remote(
            w.raw.at[:, 1 - core, rows], w.from_sibling.at[:, rows], sib_send.at[c.index], sib_recv.at[c.index], sibling
        )

    def mine(c):
        return span(work[c.b].raw.at[chip, core], c)

    def theirs(c):
        return span(work[c.b].raw.at[1 - chip, core], c)

    def to_partner(c):
        return remote(
            theirs(c), span(work[c.b].from_partner, c), send.at[0, c.index], recv.at[0, c.index], partner
        )

    def from_near(c):
        return span(work[c.b].from_sibling.at[0], c)

    def from_cross(c):
        return span(work[c.b].from_sibling.at[1], c)

    def to_near(c):
        return remote(mine(c), from_near(c), send.at[1, c.index], recv.at[1, c.index], near)

    def to_cross(c):
        return remote(mine(c), from_cross(c), send.at[2, c.index], recv.at[2, c.index], cross)

    def total_to_near(c):
        return remote(
            span(work[c.b].from_partner, c), from_near(c), send.at[3, c.index], recv.at[3, c.index], near
        )

    def out_copy(c, source):
        return pltpu.make_async_copy(span(source, c), span(results[c.b], c), out_sem.at[c.index])

    def added(target, *sources):
        target[...] = sum(s[...].astype(F32) for s in sources).astype(BF)

    def send_to_sibling(c):
        to_sibling(c).start()

    def stage_sibling(c):
        w = work[c.b]
        to_sibling(c).wait_recv()
        added(theirs(c), theirs(c), span(w.from_sibling.at[1 - chip], c))
        added(mine(c), mine(c), span(w.from_sibling.at[chip], c))
        if chain:
            @pl.when(jnp.logical_not(outer))
            def _():
                for device in (near, cross):
                    pl.semaphore_signal(credit, inc=1, device_id=device, device_id_type=MESH)

    def stage_partner(c):
        to_partner(c).wait_recv()
        added(mine(c), mine(c), span(work[c.b].from_partner, c))
        if not chain:
            out_copy(c, work[c.b].raw.at[chip, core]).start()
            return

        @pl.when(outer)
        def _():
            pl.semaphore_wait(credit, 1)
            to_near(c).start()

    def stage_near(c):
        @pl.when(jnp.logical_not(outer))
        def _():
            to_near(c).wait_recv()
            added(mine(c), mine(c), from_near(c))
            pl.semaphore_wait(credit, 1)
            to_cross(c).start()

    def stage_cross(c):
        @pl.when(jnp.logical_not(outer))
        def _():
            to_cross(c).wait_recv()
            total = work[c.b].from_partner
            added(span(total, c), mine(c), from_cross(c))
            total_to_near(c).start()
            out_copy(c, total).start()

    def stage_total(c):
        @pl.when(outer)
        def _():
            total_to_near(c).wait_recv()
            out_copy(c, work[c.b].from_sibling.at[0]).start()

    def turn_operands():
        wait(loads[0].low, loads[0].act)
        work[0].lowT[...] = views[0].low[...].T

    def feed_products():
        own, w = views[0], work[0]

        @pl.loop(0, up_count)
        def _(k):
            rows = pl.ds(pl.multiple_of(k * step, step), step)
            for q in range(tensors):
                w.raw[q // 2, q % 2, pl.ds(pl.multiple_of(up_first + k * step, 16), step), :] = dot(
                    w.lowT[rows, :], own.slope[q]
                ).astype(BF)
            send_to_sibling(feed_chunk(k))

            @pl.when((k >= 1) & (k <= ahead))
            def _():
                stage_sibling(feed_chunk(k - 1))
                to_partner(feed_chunk(k - 1)).start()

        @pl.loop(0, down_count)
        def _(k):
            lanes = pl.ds(pl.multiple_of(k * step, step), step)
            for q in range(tensors):
                w.raw[q // 2, q % 2, pl.ds(pl.multiple_of(down_first + k * step, 16), step), :] = dot(
                    own.act[q, :, lanes].T, w.gf[...]
                ).astype(BF)
            send_to_sibling(feed_chunk(up_count + k))

    def later_product(c):
        own, w = views[c.b], work[c.b]
        for q in range(tensors):
            for i in range(MATRICES):
                first = max(c.first, starts[c.b][i])
                last = min(c.first + c.rows, starts[c.b][i + 1])
                if first >= last:
                    continue
                rows = slice(first - starts[c.b][i], last - starts[c.b][i])
                if i == 0:
                    value = dot(own.qkv[q, rows, :], own.x[...])
                elif i == 1:
                    value = dot(own.ctx[q, rows, :], w.ga[...])
                elif i == 2:
                    value = dot(w.lowT[rows, :], own.slope[q])
                else:
                    value = dot(own.act[q, :, rows].T, w.gf[...])
                w.raw[q // 2, q % 2, first:last, :] = value.astype(BF)
        send_to_sibling(c)

    @pl.when(section == 1)
    def _():
        wait(*cot_copies)
        work[1].g[...] = flipped[...].T

    for b in range(2):
        work[b].sums[...] = jnp.zeros(work[b].sums.shape, F32)
    roots_copy.wait()

    def feed_back(b, n, block, hopped):
        own, own_in, w, gain = views[b], loads[b], work[b], gains[b]
        if n == 0:
            wait(own_in.n2)

        if hopped:
            hop(b, n).wait_recv()

        for rows in small_blocks(block):
            g, normed = w.g[rows].astype(F32), own.n2[rows].astype(F32)
            low = norm_rows_back(g, normed, roots[rows, 2 * b + 1 : 2 * b + 2], gain[1:2])
            w.dz[rows] = low
            w.gf[rows] = low.astype(BF)
            w.sums[1:2] += jnp.sum(g * normed, axis=0, keepdims=True)
            w.sums[3:4] += jnp.sum(g, axis=0, keepdims=True)

        if n == 0:
            wait(own_in.downward, own_in.slope, own_in.upward)

        @pl.loop(0, tensors)
        def _(q):
            d_act = dot(w.gf[block], own.downward[q // 2, q % 2])
            d_pre = (d_act * own.slope[q, block].astype(F32)).astype(BF)
            own.slope[q, block] = d_pre
            w.dz[block] += dot(d_pre, own.upward[q // 2, q % 2])

        if n == 0:
            wait(own_in.n1, own_in.outward)
        for rows in small_blocks(block):
            g, normed = w.dz[rows], own.n1[rows].astype(F32)
            low = norm_rows_back(g, normed, roots[rows, 2 * b : 2 * b + 1], gain[0:1])
            w.dz[rows] = low
            w.ga[rows] = low.astype(BF)
            w.sums[0:1] += jnp.sum(g * normed, axis=0, keepdims=True)
            w.sums[2:3] += jnp.sum(g, axis=0, keepdims=True)
        gaT = w.ga[block].T
        for q in range(tensors):
            w.dctx[q, :, block] = dot(own.outward[q // 2, q % 2], gaT).astype(BF)

    @pl.when(section == 0)
    def _():
        turn_operands()
        for s in (1, 0):
            for n, block in enumerate(blocks_of(s)):
                feed_back(s, n, block, True)

    @pl.when(section == 1)
    def _():
        for s in (1, 0):
            feed_back(s, 0, slice(0, length), False)

    @pl.when(section == 0)
    def _():
        feed_products()

    for own_in in loads:
        wait(own_in.qkv, own_in.ctx, own_in.inv)
    wait(probs_copy)
    qkv = (views[0].qkv, views[1].qkv)
    text_rows, layout_rows = slice(0, HEAD_TEXT), slice(HEAD_TEXT, HEAD_TEXT + HEAD_LAYOUT)

    def turn(k, n_known):
        fixed = isinstance(k, int)

        def at(i, stage):
            if not fixed:
                pl.when((i >= 0) & (i < n_feed))(lambda: stage(feed_chunk(i)))
            elif 0 <= i < n_known:
                stage(chunks[i])

        def sibling_and_send(c):
            stage_sibling(c)
            to_partner(c).start()

        at(k + ahead, sibling_and_send)
        at(k, stage_partner)
        if chain:
            at(k - 1, stage_near)
            at(k - 2, stage_cross)
            at(k - 3, stage_total)

    early_turns = 4

    @pl.loop(0, tensors)
    def _(q):
        for local in range(local_heads):
            head = q * local_heads + local

            @pl.when((section == 0) & (head % 4 == 0) & (head < 4 * (early_turns - 1)))
            def _():
                turn(head // 4, n_feed)

            inv = views[0].inv[q, local : local + 1, :]
            scaled = [
                (work[s].dctx[q, local * SIZES[s] : (local + 1) * SIZES[s], :].astype(F32) * inv).astype(BF)
                for s in range(2)
            ]
            inner = [
                jnp.sum(
                    scaled[s].astype(F32)
                    * views[s].ctx[q, local * SIZES[s] : (local + 1) * SIZES[s], :].astype(F32),
                    axis=0, keepdims=True,
                )
                for s in range(2)
            ]
            rows16 = lax.broadcasted_iota(jnp.int32, (16, length), 0)
            extra = jnp.zeros((16, length), F32)
            for i, value in enumerate((inner[0] + inner[1], inner[1])):
                high = value.astype(BF).astype(F32)
                extra = jnp.where(rows16 == 2 * i, -high, extra)
                extra = jnp.where(rows16 == 2 * i + 1, high - value, extra)
            pad = jnp.zeros((128 - sum(SIZES) - 16, length), BF)
            dcT = jnp.concatenate([*scaled, extra.astype(BF), pad], axis=0)
            dc = dcT.T
            qT, kT = (head_rows(qkv, q, kind, local, SCALES if kind == 0 else None) for kind in range(2))
            v_text, v_layout = (head_part(qkv, q, 2, local, s) for s in range(2))
            one, other_one = (((rows16 // 2) == i).astype(F32).astype(BF) for i in range(2))
            low = probs_in[q, local]
            probs = low.astype(F32)
            both = dot(dc, jnp.concatenate([v_text, v_layout, one, pad], axis=0))
            ds_both = (probs * both).astype(BF)
            single = dot(dc, jnp.concatenate([jnp.zeros_like(v_text), v_layout, other_one, pad], axis=0))
            ds_layout = (probs * single).astype(BF)
            dvT = dot(dcT, low)
            put_head(qkv, q, 2, local, 0, dvT[text_rows])
            put_head(qkv, q, 2, local, 1, dvT[layout_rows])
            k = kT.T
            lane = lax.broadcasted_iota(jnp.int32, (length, 128), 1)
            dq = jnp.where(lane < HEAD_TEXT, dot(ds_both, k) * SCALES[0], dot(ds_layout, k) * SCALES[1])
            dqT = dq.astype(BF).T
            put_head(qkv, q, 0, local, 0, dqT[text_rows])
            put_head(qkv, q, 0, local, 1, dqT[layout_rows])
            put_head(qkv, q, 1, local, 0, dot(qT[text_rows], ds_both))
            put_head(qkv, q, 1, local, 1, dot(qT[layout_rows], ds_layout))

    @pl.when(section == 0)
    def _():
        turn(early_turns - 1, n_feed)

    wait(loads[0].project, loads[1].project)
    page_sum = jnp.zeros((1, work[0].dz.shape[1]), F32)
    for b in (1, 0):
        for n, block in enumerate(blocks_of(b)):
            down = work[b].dz[block]
            for q in range(tensors):
                down += dot(qkv[b][q, :, block].T, views[b].project[q // 2, q % 2])
            down = down.astype(BF)
            work[b].g[block] = down
            if b == 0:
                page_sum += jnp.sum(down.astype(F32), axis=0, keepdims=True)

            @pl.when(section == 1)
            def _():
                hop(b, n).start()

    wait(loads[1].low, loads[1].act)
    work[1].lowT[...] = views[1].low[...].T
    for own_in in loads:
        wait(own_in.x)
    @pl.when(section == 1)
    def _():
        turn_operands()
        feed_products()

    for c in chunks[n_feed:]:
        later_product(c)

    @pl.when(section == 0)
    def _():
        flipped[...] = work[1].g[...].T
        each_page(0, page_start)

    at_page = (lax.broadcasted_iota(jnp.int32, lang_ids.shape, 0) == t % 2) & (
        lax.broadcasted_iota(jnp.int32, lang_ids.shape, 1) == t // 2
    )
    group = jnp.sum(jnp.where(at_page, lang_ids[...], 0), axis=(0, 1), keepdims=True)
    n_lang = small_out.shape[1] - 8
    chosen = (lax.broadcasted_iota(jnp.int32, (n_lang, 1), 0) == group) & (section == 0)
    small_sum[0, 0:n_lang] = jnp.where(chosen, page_sum, 0.0)
    small_sum[0, n_lang : n_lang + 4] = work[0].sums[...]
    small_sum[0, n_lang + 4 : n_lang + 8] = jnp.zeros((4, small_out.shape[2]), F32)
    small_sum[0, n_lang + 4 : n_lang + 8, : work[1].sums.shape[1]] = work[1].sums[...]

    def small_copy(i, device):
        return remote(small_sum.at[i], small_got.at[i], small_send.at[i], small_recv.at[i], device)

    if chain:
        small_copy(0, sibling).start()
    @pl.when(section == 1)
    def _():
        @pl.loop(0, early_turns)
        def _(k):
            turn(k, n_feed)

    for k in range(early_turns, len(chunks) + (3 if chain else 0)):
        turn(k, len(chunks))
        if not chain:
            continue
        if k == early_turns:
            small_copy(0, sibling).wait_recv()
            small_sum[1] = small_sum[0] + small_got[0]
            small_copy(1, partner).start()
        if k == early_turns + 1:
            small_copy(1, partner).wait_recv()
            small_sum[2] = small_sum[1] + small_got[1]
            small_copy(2, near).start()
        if k == early_turns + 2:
            small_copy(2, near).wait_recv()
            small_sum[3] = small_sum[2] + small_got[2]

            @pl.when(jnp.logical_not(outer))
            def _():
                small_copy(3, cross).start()

        if k == early_turns + 3:
            @pl.when(jnp.logical_not(outer))
            def _():
                small_copy(3, cross).wait_recv()
                small_sum[4] = small_sum[3] + small_got[3]
                small_copy(4, near).start()

        if k == early_turns + 4:
            @pl.when(outer)
            def _():
                small_copy(4, near).wait_recv()
                small_sum[4] = small_got[4]

            small_sum[5] = small_sum[4]
            small_copy(5, other).start()

    if chain:
        for i, device in enumerate((sibling, partner, near)):
            small_copy(i, device).wait_send()

        @pl.when(jnp.logical_not(outer))
        def _():
            small_copy(3, cross).wait_send()
            small_copy(4, near).wait_send()

        small_copy(5, other).wait()
        small_out[0] = small_sum[5]
        small_out[1] = small_got[5]
    else:
        small_out[0] = small_sum[0]
        small_out[1] = small_sum[0]

    @pl.when(section == 1)
    def _():
        for b in range(2):
            for n in range(len(blocks_of(b))):
                hop(b, n).wait_send()

    for c in chunks:
        to_sibling(c).wait_send()
        to_partner(c).wait_send()
        if not chain:
            out_copy(c, work[c.b].from_partner).wait()
            continue

        @pl.when(outer)
        def _():
            to_near(c).wait_send()

        @pl.when(jnp.logical_not(outer))
        def _():
            to_cross(c).wait_send()
            total_to_near(c).wait_send()

        out_copy(c, work[c.b].from_partner).wait()

    for g in range(sections):
        each_page(g, page_sent)
        for a in range(2):
            for j in range(2):
                dst = kinds[g][a].at[j]
                remote(dst, dst, page_send.at[0, a], page_recv.at[g, a, j], partner).wait_recv()
    landed = (text_out, layout_out, grad_out, layout_grad_out)
    copies = [pltpu.make_async_copy(v, h, page_out_sem.at[i]) for i, (v, h) in enumerate(zip(landed, page_outs))]
    start(*copies)
    wait(*copies)


def layer_backward(mesh, x, y, probs, roots, kept, weights, cots, norms, lang_ids, n_lang):
    sections, dp, tensors = mesh.shape["section"], mesh.shape["dp"], mesh.shape["tensor"]
    chain = dp == 4
    weights = tuple(Weights(*(m.reshape((tensors // 2, 2) + m.shape[1:]) for m in w)) for w in weights)
    needed = tuple(
        Needed(
            n2=k.n2, downward=w.downward, slope=k.slope, upward=w.upward, n1=k.n1,
            outward=w.outward, low=k.low, act=k.act, qkv=k.qkv, ctx=k.ctx, inv=k.inv, project=w.project, x=rows,
        )
        for k, w, rows in zip(kept, weights, x)
    )
    flat_in, in_tree = jax.tree.flatten((needed, probs, roots))
    plain = [v for own in needed for name, v in own._asdict().items() if name not in Weights._fields] + [probs, roots]
    stacks = [(matrix_starts(own)[MATRICES], rows.shape[1]) for own, rows in zip(needed, x)]
    length = x[0].shape[0]
    work = []
    for own, rows, (count, width) in zip(needed, x, stacks):
        work += Work(
            g=shape(rows.shape), gf=shape(rows.shape), ga=shape(rows.shape), dz=shape(rows.shape, F32),
            dctx=shape(own.ctx.shape), sums=shape((4, width), F32), lowT=shape((width, length)),
            raw=shape((tensors // 2, 2, count, width)), from_sibling=shape((tensors // 2, count, width)),
            from_partner=shape((count, width)),
        )
    small = shape((2, n_lang + 8, x[0].shape[1]), F32)
    text_page = shape((2, length // tensors, x[0].shape[1]))
    layout_page = shape((2, x[1].shape[1], length // tensors))
    summed = [shape(s) for s in stacks]
    own = needed[0]
    n_chunks = (own.upward.shape[-2] + own.downward.shape[-2]) // (2 * ROWS) + 4
    n_blocks = len(hop_blocks(length))
    dma = pltpu.SemaphoreType.DMA
    results = pl.pallas_call(
        functools.partial(backward_kernel, sections, tensors, chain, in_tree),
        out_shape=summed + [small, text_page, layout_page, text_page, layout_page],
        in_specs=[ANY] * (len(flat_in) + 4) + [VMEM] * 3,
        out_specs=[ANY] * 2 + [VMEM] + [ANY] * 4,
        scratch_shapes=vmem_like(work) + vmem_like(plain)
        + [pltpu.VMEM(cots[1].shape, BF)] + [pltpu.VMEM((6,) + small.shape[1:], F32)] * 2
        + vmem_like([text_page, layout_page] * 2)
        + [dma((len(flat_in),)), dma((2,)), dma((2, n_blocks)), dma((2, n_blocks))]
        + [dma((n_chunks,))] * 2 + [dma((4, n_chunks))] * 2
        + [pltpu.SemaphoreType.REGULAR, dma((n_chunks,))]
        + [dma((6,))] * 2 + [dma((tensors, 2)), dma((sections, 2, 2)), dma((4,))],
        compiler_params=pltpu.CompilerParams(
            collective_id=1, has_side_effects=True, vmem_limit_bytes=64 << 20
        ),
        name="layer_backward",
    )(*flat_in, *cots, *y, lang_ids, norms[0][0], norms[1][0])
    totals, small, pages = results[:2], results[2], results[3:7]
    if not chain:
        totals = lax.psum(tuple(totals), "dp")
        both = lax.psum(small[0], ("dp", "tensor"))
        small = jnp.stack([both, lax.ppermute(both, "section", [(0, 1), (1, 0)])])
    return totals, small, pages


def widen_kernel(n_in, n_pages, *refs):
    n_out = 5 + n_pages + 2 * MATRICES
    hbm_in, hbm_out = refs[:n_in], refs[n_in : n_in + n_out]
    vmem_in, vmem_out = refs[n_in + n_out : 2 * n_in + n_out], refs[2 * n_in + n_out : -2]
    in_sem, out_sem = refs[-2:]
    loads = [pltpu.make_async_copy(h, v, in_sem.at[i]) for i, (h, v) in enumerate(zip(hbm_in, vmem_in))]
    sources = vmem_out[:5] + vmem_in[3:] + vmem_out[5:]
    stores = [pltpu.make_async_copy(v, h, out_sem.at[i]) for i, (v, h) in enumerate(zip(sources, hbm_out))]
    start(*loads)
    totals, small = vmem_in[0:2], vmem_in[2]
    for b in range(2):
        wait(loads[b])
        at = 0
        for i in range(b * MATRICES, (b + 1) * MATRICES):
            out = vmem_out[5 + i]
            for c in range(0, out.shape[0], 48):
                out[c : c + 48] = totals[b][at + c : at + c + 48].astype(F32)
            at += out.shape[0]
            stores[5 + n_pages + i].start()
    for i in range(n_pages):
        loads[3 + i].wait()
        stores[5 + i].start()
    loads[2].wait()
    n_lang = vmem_out[0].shape[0]
    vmem_out[0][...] = jnp.where(lax.axis_index("section") == 0, small[0, :n_lang], small[1, :n_lang])
    for i, out in enumerate(vmem_out[1:5]):
        first = n_lang + 2 * i
        out[...] = small[0, first : first + 2, : out.shape[1]]
    start(*stores[:5])
    wait(*stores)


def widen(totals, small, pages, shards, n_lang):
    widths = [total.shape[1] for total in totals]
    sums = [shape((n_lang, widths[0]), F32)] + [shape((2, w), F32) for w in widths for _ in range(2)]
    grads = [shape(m.shape, F32) for own in shards for m in own]
    inputs = (*totals, small, *pages)
    outs = sums + [shape(page.shape) for page in pages] + grads
    results = pl.pallas_call(
        functools.partial(widen_kernel, len(inputs), len(pages)), out_shape=outs,
        in_specs=[ANY] * len(inputs), out_specs=[ANY] * len(outs),
        scratch_shapes=vmem_like(inputs) + vmem_like(sums + grads)
        + [pltpu.SemaphoreType.DMA((len(inputs),)), pltpu.SemaphoreType.DMA((len(outs),))],
        compiler_params=pltpu.CompilerParams(vmem_limit_bytes=62 << 20), name="widen",
    )(*inputs)
    return results[0], results[1:5], results[5:9], results[9:13], results[13:17]


def per_device(
    mesh,
    text_input,
    layout_input,
    text_cotangent,
    layout_cotangent,
    page_counts,
    pad_mask,
    lang_ids,
    lang_table,
    text_project,
    text_outward,
    text_upward,
    text_downward,
    text_gains,
    text_biases,
    layout_project,
    layout_outward,
    layout_upward,
    layout_downward,
    layout_gains,
    layout_biases,
):
    def flat(project):
        return jnp.transpose(project[0], (1, 2, 0)).reshape(-1, project.shape[1])

    def flipped(block):
        return jnp.transpose(block[0], (0, 2, 1))

    shards = (
        Weights(flat(text_project), text_outward[0], text_upward[0], text_downward[0]),
        Weights(flat(layout_project), layout_outward[0], layout_upward[0], layout_downward[0]),
    )
    norms = ((text_gains[0], text_biases[0]), (layout_gains[0], layout_biases[0]))
    marks = (pad_mask, page_counts, lang_ids, lang_table)
    (x, y, probs, roots, kept, weights), cots = layer_forward(
        mesh, text_input[0], flipped(layout_input), text_cotangent[0], flipped(layout_cotangent), shards, norms, marks
    )
    n_lang = lang_table.shape[0]
    totals, small, pages = layer_backward(mesh, x, y, probs, roots, kept, weights, cots, norms, lang_ids, n_lang)
    lang_sum, norm_sums, pages, text_sums, layout_sums = widen(totals, small, pages, shards, n_lang)
    text_out, layout_out, text_grad, layout_grad = pages

    def unflat(grad, like):
        return jnp.transpose(grad.reshape(like.shape[2], like.shape[3], like.shape[1]), (2, 0, 1))[None]

    unflip = lambda block: jnp.transpose(block, (0, 2, 1))[None]
    return (
        text_out[None], unflip(layout_out), text_grad[None], unflip(layout_grad), lang_sum,
        unflat(text_sums[0], text_project), *(s[None] for s in text_sums[1:]), norm_sums[0][None], norm_sums[1][None],
        unflat(layout_sums[0], layout_project), *(s[None] for s in layout_sums[1:]),
        norm_sums[2][None], norm_sums[3][None],
    )


def solution(mesh):
    tokens = P("section", "dp", "tensor", None)
    weight_specs = (
        P("section", None, None, "tensor"), P("section", "tensor", None), P("section", None, "tensor"),
        P("section", "tensor", None), P("section", None, None), P("section", None, None),
    )
    in_specs = (tokens,) * 4 + (P(None, "dp"), P(None, "dp", None), P(None, "dp"), P()) + weight_specs * 2
    out_specs = (tokens,) * 4 + (P(),) + weight_specs * 2
    return jax.shard_map(
        functools.partial(per_device, mesh), mesh=mesh, in_specs=in_specs, out_specs=out_specs, check_vma=False
    )
```

```python
import functools
import math
import typing

import jax
import jax.numpy as jnp
from jax import lax
from jax.experimental import pallas as pl
from jax.experimental.pallas import tpu as pltpu
from jax.sharding import PartitionSpec as P

HEAD_TEXT = 64
HEAD_LAYOUT = 16
EPSILON = 1e-05
NEGATIVE = -1e30
HIGH = lax.Precision.HIGHEST
MESH = pl.DeviceIdType.MESH
BF = jnp.bfloat16
F32 = jnp.float32
ANY = pl.BlockSpec(memory_space=pl.ANY)


def remote(src, dst, send, recv, device):
    return pltpu.make_async_remote_copy(
        src_ref=src, dst_ref=dst, send_sem=send, recv_sem=recv, device_id=device, device_id_type=MESH
    )


def greet(section, tensor, sections, tensors, extra=()):
    barrier = pltpu.get_barrier_semaphore()
    for g in range(sections):
        for q in range(tensors):

            @pl.when((section != g) | (tensor != q))
            def _():
                pl.semaphore_signal(
                    barrier, inc=1, device_id={"section": g, "tensor": q}, device_id_type=MESH
                )

    for device in extra:
        pl.semaphore_signal(barrier, inc=1, device_id=device, device_id_type=MESH)
    pl.semaphore_wait(barrier, sections * tensors - 1 + len(extra))


GELU_P = 0.3275911
GELU_A = (0.254829592, -0.284496736, 1.421413741, -1.453152027, 1.061405429)
NN = (((1,), (0,)), ((), ()))
NT = (((1,), (1,)), ((), ()))
SCALES = (1.0 / math.sqrt(HEAD_TEXT), 1.0 / math.sqrt(HEAD_LAYOUT))
SIZES = (HEAD_TEXT, HEAD_LAYOUT)
ROWS = 128


class Weights(typing.NamedTuple):
    project: typing.Any
    outward: typing.Any
    upward: typing.Any
    downward: typing.Any


class Kept(typing.NamedTuple):
    qkv: typing.Any
    ctx: typing.Any
    inv: typing.Any
    n1: typing.Any
    low: typing.Any
    act: typing.Any
    slope: typing.Any
    n2: typing.Any


def dot(a, b, dims=NN):
    return lax.dot_general(a, b, dims, preferred_element_type=F32)


def gelu_pair(u):
    d = 1.0 + (GELU_P / math.sqrt(2.0)) * jnp.abs(u)
    t = pl.reciprocal(d, approx=True)
    t = t * (2.0 - d * t)
    e = jnp.exp2((u * u) * (-0.5 / math.log(2.0)))
    a1, a2, a3, a4, a5 = (0.5 * a for a in GELU_A)
    tail = ((((a5 * t + a4) * t + a3) * t + a2) * t + a1) * t * e
    cdf = jnp.where(u >= 0, 1.0 - tail, tail)
    return u * cdf, cdf + u * e * (1.0 / math.sqrt(2.0 * math.pi))


def norm_rows(z, gain, offset):
    center = z - jnp.mean(z, axis=-1, keepdims=True)
    inverse = lax.rsqrt(jnp.mean(center * center, axis=-1, keepdims=True) + EPSILON)
    normed = center * inverse
    return normed * gain + offset, normed, inverse


def norm_rows_back(g, n, r, gain):
    t = g * gain
    return r * (t - jnp.mean(t, axis=-1, keepdims=True) - n * jnp.mean(t * n, axis=-1, keepdims=True))


class Staged:
    def __init__(self, tree, hbm, vmem, sem, inward):
        self.tree, self.vmem = tree, list(vmem)
        pairs = zip(hbm, vmem) if inward else zip(vmem, hbm)
        self.copies = [pltpu.make_async_copy(a, b, sem.at[i]) for i, (a, b) in enumerate(pairs)]

    def refs(self):
        return jax.tree.unflatten(self.tree, self.vmem)

    def parts(self):
        return jax.tree.unflatten(self.tree, self.copies)

    def start(self):
        for copy in self.copies:
            copy.start()

    def wait(self):
        for copy in self.copies:
            copy.wait()


def start(*copies):
    for copy in copies:
        copy.start()


def wait(*copies):
    for copy in copies:
        copy.wait()


def head_rows(stacks, slot, kind, local, scales=None, extra=None):
    rows = []
    for b in range(2):
        piece = head_part(stacks, slot, kind, local, b)
        rows.append(piece if scales is None else piece * BF(scales[b]))
    length = rows[0].shape[1]
    rows.append(jnp.zeros((16, length), BF) if extra is None else extra)
    rows.append(jnp.zeros((128 - sum(SIZES) - 16, length), BF))
    return jnp.concatenate(rows, axis=0)


def head_part(stacks, slot, kind, local, b):
    first = kind * (stacks[b].shape[1] // 3) + local * SIZES[b]
    return stacks[b][slot, first : first + SIZES[b], :]


def small_blocks(block, step=64):
    return [slice(c, c + step) for c in range(block.start, block.stop, step)]


def put_head(stacks, slot, kind, local, b, value):
    first = kind * (stacks[b].shape[1] // 3) + local * SIZES[b]
    stacks[b][slot, first : first + SIZES[b], :] = value.astype(BF)


def hop_blocks(length):
    ends = [0, length // 2, length * 3 // 4, length]
    return [slice(a, b) for a, b in zip(ends, ends[1:])]


def slot_of(u, core, chip):
    return ((chip + u // 2) % 2) * 2 + (core + u % 2) % 2


def forward_kernel(sections, tensors, shared, in_tree, out_tree, *refs):
    n_w, n_out = len(shared), out_tree.num_leaves
    sources = (refs[0:2], refs[2:4])
    shards = refs[4 : 4 + n_w]
    pad_mask, counts, lang_ids, lang_table, *norms = refs[4 + n_w : 12 + n_w]
    rest = refs[12 + n_w :]
    hbm_out, cots_out, rest = rest[:n_out], rest[n_out : n_out + 2], rest[n_out + 2 :]
    outgoing = Staged(out_tree, hbm_out, rest[:n_out], rest[n_out], False)
    rest = rest[n_out + 1 :]
    flipped, raw_x, y_narrow, *rest = rest
    nats, totals, pre, score_buffer, rest = rest[0:2], rest[2:4], rest[4:6], rest[6], rest[7:]
    xT, turned, turn_sem, rest = rest[0:2], (rest[2:4], rest[4:6]), rest[6], rest[7:]
    page_send, page_recv, w_send, w_recv, own_sem, hop_send, hop_recv, cot_sem, act_sem = rest
    x, y_pages, probs_out, roots, kept, weights = outgoing.refs()
    y = (y_pages[0], y_narrow)
    x_out, y_out, probs_copy, roots_copy, kept_out, weights_out = outgoing.parts()
    kept_hbm, weights_hbm = jax.tree.unflatten(out_tree, list(hbm_out))[4:6]
    section, d, t = lax.axis_index("section"), lax.axis_index("dp"), lax.axis_index("tensor")
    core, chip, half_index = t % 2, t // 2, d % 2
    sibling, partner = t + 1 - 2 * core, (t + tensors // 2) % tensors
    mate = d + 1 - 2 * half_index
    micro, page = core, chip
    part_length = sources[0][0].shape[1]
    length = x[0].shape[0]
    blocks = [slice(c, c + 2 * ROWS) for c in range(0, length, 2 * ROWS)]
    parts = hop_blocks(length)
    full = (
        weights[0].project, weights[1].project, weights[0].outward, weights[0].upward,
        weights[0].downward, weights[1].outward, weights[1].upward, weights[1].downward,
    )
    greet(section, t, sections, tensors, ({"dp": mate},) if any(shared) else ())

    def half_of(ref, i, which):
        count = shards[i].shape[0] // 2
        return ref.at[pl.ds(pl.multiple_of(which * count, 16), count)] if shared[i] else ref

    def to_partner(i):
        return remote(
            half_of(shards[i], i, half_index), half_of(full[i].at[t], i, half_index),
            w_send.at[0, i], w_recv.at[0, i], {"tensor": partner},
        )

    def to_sibling(i):
        return remote(full[i].at[t], full[i].at[t], w_send.at[1, i], w_recv.at[1, i], {"tensor": sibling})

    def to_mate(i):
        ref = half_of(full[i].at[partner], i, half_index)
        return remote(ref, ref, w_send.at[2, i], w_recv.at[2, i], {"dp": mate})

    def on_first(i):
        ref = half_of(full[i].at[partner], i, half_index)
        return remote(ref, ref, w_send.at[3, i], w_recv.at[3, i], {"tensor": sibling})

    def on_second(i):
        ref = half_of(full[i].at[partner], i, 1 - half_index)
        return remote(ref, ref, w_send.at[4, i], w_recv.at[4, i], {"tensor": sibling})

    def keep(i):
        return pltpu.make_async_copy(shards[i], full[i].at[t], own_sem.at[i])

    def relay(*which):
        for i in which:
            to_partner(i).wait_recv()
            if shared[i]:
                to_mate(i).start()
            on_first(i).start()

    def relay_second(*which):
        for i in which:
            if shared[i]:
                to_mate(i).wait_recv()
                on_second(i).start()

    def early(*which):
        for i in which:
            to_sibling(i).wait_recv()

    def late(*which):
        for i in which:
            on_first(i).wait_recv()
            if shared[i]:
                on_second(i).wait_recv()

    def token_slot(g, a, index):
        start_at = pl.multiple_of(index * part_length, part_length)
        target = (raw_x, flipped)[a]
        return target.at[pl.ds(start_at, part_length)] if a == 0 else target.at[:, pl.ds(start_at, part_length)]

    def over_pages(g, act):
        for j in range(2):
            target = 2 * j + section
            here = (section == g) & (t == target)
            for a in range(2):
                act(g, j, a, target, here)

    def page_copy(g, j, a, target):
        return remote(
            sources[g][a].at[j], token_slot(g, a, t), page_send.at[g, j, a], page_recv.at[a, t],
            {"section": g, "tensor": target},
        )

    def page_start(g, j, a, target, here):
        @pl.when(here)
        def _():
            pltpu.make_async_copy(sources[g][a].at[j], token_slot(g, a, t), page_recv.at[a, t]).start()

        @pl.when(jnp.logical_not(here))
        def _():
            page_copy(g, j, a, target).start()

    def page_sent(g, j, a, target, here):
        @pl.when(jnp.logical_not(here))
        def _():
            page_copy(g, j, a, target).wait_send()

    def pages_arrived(g):
        for a in range(2):
            for q in range(tensors):
                slot = token_slot(g, a, q)
                remote(slot, slot, page_send.at[0, 0, a], page_recv.at[a, q], {"tensor": sibling}).wait_recv()

    def parts_of(b):
        return parts if b == 0 else [slice(0, length)]

    def hop(b, n):
        part = parts_of(b)[n]
        return remote(
            y[b].at[part], x[b].at[part], hop_send.at[b, n], hop_recv.at[b, n], {"section": 1 - section}
        )

    def weights_to_hbm():
        for b in range(2):
            start(weights_out[b].project, weights_out[b].outward)
            for q in range(tensors):
                for m, name in enumerate((2, 3)):
                    copy = pltpu.make_async_copy(
                        turned[b][m].at[q % 2], weights_hbm[b][name].at[q], turn_sem.at[b, m, q % 2]
                    )
                    if q >= 2:
                        copy.wait()
                    turned[b][m][q % 2] = weights[b][name][q].T
                    copy.start()
        for b in range(2):
            for q in range(tensors - 2, tensors):
                for m, name in enumerate((2, 3)):
                    pltpu.make_async_copy(
                        turned[b][m].at[q % 2], weights_hbm[b][name].at[q], turn_sem.at[b, m, q % 2]
                    ).wait()

    over_pages(0, page_start)
    for i in range(n_w):
        keep(i).start()
    for i in range(n_w):
        to_partner(i).start()
    over_pages(1, page_start)
    for i in range(n_w):
        keep(i).wait()
        to_sibling(i).start()

    at_page = (lax.broadcasted_iota(jnp.int32, counts.shape, 0) == micro) & (
        lax.broadcasted_iota(jnp.int32, counts.shape, 1) == page
    )

    def own_entry(ref):
        return jnp.sum(jnp.where(at_page, ref[...], 0), axis=(0, 1), keepdims=True)

    positions = lax.broadcasted_iota(jnp.int32, (1, length), 1)
    mask_row = pad_mask[micro, pl.ds(page, 1), :]
    key_mask = (positions < own_entry(counts)) & ((mask_row == 1) | (positions == 0))
    first_row = (lax.broadcasted_iota(jnp.int32, (16, length), 0) == 0).astype(F32)
    mask_row16 = (first_row * jnp.where(key_mask, 0.0, NEGATIVE)).astype(BF)
    groups = lax.broadcasted_iota(jnp.int32, (lang_table.shape[0], 1), 0)
    lang_row = jnp.sum(jnp.where(groups == own_entry(lang_ids), lang_table[...], 0.0), axis=0, keepdims=True)
    local_heads = weights[0].project.shape[1] // (3 * HEAD_TEXT)
    qkv = (kept[0].qkv, kept[1].qkv)

    @pl.when(section == 0)
    def _():
        pages_arrived(0)
        x[0][...] = (raw_x[...].astype(F32) + lang_row).astype(BF)
        x[1][...] = flipped[...].T
        early(0, 1)

    @pl.when(section == 1)
    def _():
        relay(*range(n_w))
        relay_second(*range(n_w))
        early(*range(n_w))
        late(*range(n_w))
        weights_to_hbm()

    @pl.loop(0, 2)
    def _(half):
        @pl.when((half == 1) & (section == 0))
        def _():
            relay(0, 1)
            relay_second(0)
            late(0, 1)

        for n, block in enumerate(parts):
            @pl.when((half == 0) & (section == 1))
            def _():
                for b in range(2):
                    if n < len(parts_of(b)):
                        hop(b, n).wait_recv()

            @pl.when(half == 0)
            def _():
                for b in range(2):
                    xT[b][:, block] = x[b][block].T

            @pl.loop(0, 2)
            def _(u):
                slot = slot_of(2 * half + u, core, chip)
                for b in range(2):
                    qkv[b][slot, :, block] = dot(weights[b].project[slot], xT[b][:, block]).astype(BF)

        @pl.loop(0, 2)
        def _(u):
            slot = slot_of(2 * half + u, core, chip)
            for local in range(local_heads):
                q = head_rows(qkv, slot, 0, local, SCALES, first_row.astype(BF)).T
                kT = head_rows(qkv, slot, 1, local, None, mask_row16)
                score_buffer[local] = dot(q, kT)
                for rows in small_blocks(slice(0, length)):
                    scores = score_buffer[local, rows, :]
                    raised = jnp.exp(scores - jnp.max(scores, axis=-1, keepdims=True))
                    probs_out[slot, local, rows, :] = raised.astype(BF)
                vT = head_rows(qkv, slot, 2, local, None, first_row.astype(BF))
                ctx = dot(probs_out[slot, local], vT.T).T
                inv = 1.0 / ctx[sum(SIZES) : sum(SIZES) + 1]
                ctx = (ctx * inv).astype(BF)
                kept[0].inv[slot, local : local + 1, :] = inv
                kept[0].ctx[slot, local * HEAD_TEXT : (local + 1) * HEAD_TEXT, :] = ctx[:HEAD_TEXT]
                kept[1].ctx[slot, local * HEAD_LAYOUT : (local + 1) * HEAD_LAYOUT, :] = ctx[
                    HEAD_TEXT : HEAD_TEXT + HEAD_LAYOUT
                ]

    kept[1].inv[...] = jnp.zeros(kept[1].inv.shape, F32)
    start(probs_copy, *x_out, *(c for k in kept_out for c in (k.qkv, k.ctx, k.inv)))

    def attend(b):
        gains, biases = norms[2 * b : 2 * b + 2]
        width = x[b].shape[1]
        nats[b][...] = kept[b].ctx[...].reshape(width, length).T
        wide = weights[b].outward[...].reshape(width, width)
        for block in blocks:
            totals[b][1, block] = dot(nats[b][block], wide)
            for rows in small_blocks(block):
                h, n, r = norm_rows(x[b][rows].astype(F32) + totals[b][1, rows], gains[0:1], biases[0:1])
                totals[b][0, rows] = h
                totals[b][1, rows] = jnp.zeros(h.shape, F32)
                kept[b].n1[rows] = n.astype(BF)
                roots[rows, 2 * b : 2 * b + 1] = r
                kept[b].low[rows] = h.astype(BF)
        start(kept_out[b].n1, kept_out[b].low)

    def slot_copies(b, slot):
        return [
            pltpu.make_async_copy(v.at[slot], h.at[slot], act_sem.at[b, m, slot])
            for m, (v, h) in enumerate(((kept[b].act, kept_hbm[b].act), (kept[b].slope, kept_hbm[b].slope)))
        ]

    def feed(b, first, which):
        @pl.loop(first, first + 2)
        def _(u):
            slot = slot_of(u, core, chip)
            for block in which:
                pre[b][block] = dot(kept[b].low[block], weights[b].upward[slot])
                for rows in small_blocks(block, 16):
                    act, slope = gelu_pair(pre[b][rows])
                    kept[b].act[slot, rows] = act.astype(BF)
                    kept[b].slope[slot, rows] = slope.astype(BF)
                totals[b][1, block] += dot(kept[b].act[slot, block], weights[b].downward[slot])
                if block == slice(0, length):
                    start(*slot_copies(b, slot))

    def finish(b):
        gains, biases = norms[2 * b : 2 * b + 2]
        def last(block):
            feed(b, 2, [block])
            for rows in small_blocks(block):
                out, normed, r = norm_rows(totals[b][0, rows] + totals[b][1, rows], gains[1:2], biases[1:2])
                y[b][rows] = out.astype(BF)
                kept[b].n2[rows] = normed.astype(BF)
                roots[rows, 2 * b + 1 : 2 * b + 2] = r

        @pl.when(section == 0)
        def _():
            for n, block in enumerate(parts_of(b)):
                last(block)
                hop(b, n).start()
            if b == 0:
                for u in range(2, 4):
                    start(*slot_copies(b, slot_of(u, core, chip)))

        @pl.when(section == 1)
        def _():
            last(slice(0, length))

        if b == 1:
            y_pages[1][...] = y_narrow[...].T
        start(y_out[b], kept_out[b].n2)

    @pl.when(section == 0)
    def _():
        relay(2, 3)
        early(2)
        late(2)

    attend(0)

    @pl.when(section == 0)
    def _():
        early(3, 4)

    feed(0, 0, [slice(0, length)])

    @pl.when(section == 0)
    def _():
        relay(4, 5, 6, 7)
        relay_second(3)
        early(5, 6, 7)
        late(5, 6, 7)

    attend(1)
    feed(1, 0, [slice(0, length)])
    finish(1)

    @pl.when(section == 0)
    def _():
        relay_second(4)
        late(3, 4)

    finish(0)
    start(roots_copy)

    @pl.when(section == 0)
    def _():
        weights_to_hbm()
        for b in range(2):
            for n in range(len(parts_of(b))):
                hop(b, n).wait_send()

    for i in range(n_w):
        to_partner(i).wait_send()
        to_sibling(i).wait_send()
        on_first(i).wait_send()
        if shared[i]:
            to_mate(i).wait_send()
            on_second(i).wait_send()
    for g in range(sections):
        over_pages(g, page_sent)

    @pl.when(section == 1)
    def _():
        pages_arrived(1)
        copies = [pltpu.make_async_copy(v, h, cot_sem.at[i]) for i, (v, h) in enumerate(zip((raw_x, flipped), cots_out))]
        start(*copies)
        wait(*copies)

    for group in (x_out, y_out, (probs_copy, roots_copy), *(w[:2] for w in weights_out)):
        wait(*group)
    for b, k in enumerate(kept_out):
        wait(k.qkv, k.ctx, k.inv, k.n1, k.low, k.n2)
        for slot in range(tensors):
            wait(*slot_copies(b, slot))


def vmem_like(tree):
    return [pltpu.VMEM(s.shape, s.dtype) for s in jax.tree.leaves(tree)]


VMEM = pl.BlockSpec(memory_space=pltpu.VMEM)


def shape(dims, dtype=BF):
    return jax.ShapeDtypeStruct(tuple(dims), dtype)


def layer_forward(mesh, text_in, layout_in, text_cot, layout_cot, shards, norms, marks):
    sections, dp, tensors = mesh.shape["section"], mesh.shape["dp"], mesh.shape["tensor"]
    length = text_in.shape[1] * tensors
    rows = (shape((length, text_in.shape[2])), shape((length, layout_in.shape[1])))
    local_heads = shards[0].project.shape[0] // (3 * HEAD_TEXT)
    kept = []
    for x, w in zip(rows, shards):
        units = shape((tensors, length, w.upward.shape[1]))
        kept.append(Kept(
            qkv=shape((tensors, w.project.shape[0], length)), ctx=shape((tensors, w.outward.shape[0], length)),
            inv=shape((tensors, local_heads, length), F32),
            n1=shape(x.shape), low=shape(x.shape), act=units, slope=units,
            n2=shape(x.shape),
        ))
    weights = tuple(Weights(*(shape((tensors,) + m.shape) for m in w)) for w in shards)
    pages_out = (rows[0], shape((rows[1].shape[1], length)))
    outs = (rows, pages_out, shape((tensors, local_heads, length, length)), shape((length, 4), F32), tuple(kept), weights)
    flat_out, out_tree = jax.tree.flatten(outs)
    (a, b) = shards
    ordered = (a.project, b.project, a.outward, a.upward, a.downward, b.outward, b.upward, b.downward)
    shared = tuple(dp % 2 == 0 and w.shape[0] >= 512 for w in ordered)
    n_w = len(ordered)
    cots = [rows[0], shape((rows[1].shape[1], length))]
    small = (*marks, *norms[0], *norms[1])
    results = pl.pallas_call(
        functools.partial(forward_kernel, sections, tensors, shared, None, out_tree),
        out_shape=flat_out + cots,
        in_specs=[ANY] * (4 + n_w) + [VMEM] * len(small),
        out_specs=[ANY] * (len(flat_out) + 2),
        scratch_shapes=vmem_like(flat_out) + [pltpu.SemaphoreType.DMA((len(flat_out),))]
        + [pltpu.VMEM(cots[1].shape, BF), pltpu.VMEM(cots[0].shape, BF), pltpu.VMEM(rows[1].shape, BF)]
        + [pltpu.VMEM(x.shape, BF) for x in rows]
        + [pltpu.VMEM((2,) + x.shape, F32) for x in rows]
        + [pltpu.VMEM((length, w.upward.shape[1]), F32) for w in shards]
        + [pltpu.VMEM((local_heads, length, length), F32)]
        + [pltpu.VMEM((x.shape[1], length), BF) for x in rows]
        + [pltpu.VMEM((2,) + m.shape, BF) for w in shards for m in (w.upward, w.downward)]
        + [pltpu.SemaphoreType.DMA((2, 2, 2))]
        + [
            pltpu.SemaphoreType.DMA((sections, 2, 2)), pltpu.SemaphoreType.DMA((2, tensors)),
            pltpu.SemaphoreType.DMA((5, n_w)), pltpu.SemaphoreType.DMA((5, n_w)), pltpu.SemaphoreType.DMA((n_w,)),
            pltpu.SemaphoreType.DMA((2, len(hop_blocks(length)))), pltpu.SemaphoreType.DMA((2, len(hop_blocks(length)))),
            pltpu.SemaphoreType.DMA((2,)), pltpu.SemaphoreType.DMA((2, 2, tensors)),
        ],
        compiler_params=pltpu.CompilerParams(
            collective_id=0, has_side_effects=True, vmem_limit_bytes=62 << 20
        ),
        name="layer_forward",
    )(text_in, layout_in, text_cot, layout_cot, *ordered, *small)
    return jax.tree.unflatten(out_tree, results[:-2]), tuple(results[-2:])


class Needed(typing.NamedTuple):
    n2: typing.Any
    downward: typing.Any
    slope: typing.Any
    upward: typing.Any
    n1: typing.Any
    outward: typing.Any
    low: typing.Any
    act: typing.Any
    qkv: typing.Any
    ctx: typing.Any
    inv: typing.Any
    project: typing.Any
    x: typing.Any


class Work(typing.NamedTuple):
    g: typing.Any
    gf: typing.Any
    ga: typing.Any
    dz: typing.Any
    dctx: typing.Any
    sums: typing.Any
    lowT: typing.Any
    raw: typing.Any
    from_sibling: typing.Any
    from_partner: typing.Any


class Chunk(typing.NamedTuple):
    b: typing.Any
    index: typing.Any
    first: typing.Any
    rows: typing.Any


MATRICES = 4


def matrix_rows(own):
    return own.project.shape[-2], own.outward.shape[-2], own.upward.shape[-2], own.downward.shape[-2]


def matrix_starts(own):
    sizes = matrix_rows(own)
    return [sum(sizes[:i]) for i in range(MATRICES + 1)]


def pieces_of(size, step):
    return [(f, step) for f in range(0, size, step)]


def backward_kernel(sections, tensors, chain, in_tree, *refs):
    n_in = in_tree.num_leaves
    hbm_in, refs = refs[:n_in], refs[n_in:]
    (cots, ys, lang_ids, gains), refs = (refs[0:2], refs[2:4], refs[4], refs[5:7]), refs[7:]
    results, small_out, page_outs, refs = refs[0:2], refs[2], refs[3:7], refs[7:]
    n_work = len(Work._fields)
    work, refs = (Work(*refs[:n_work]), Work(*refs[n_work : 2 * n_work])), refs[2 * n_work :]
    plain, refs = refs[: n_in - 2 * MATRICES], refs[n_in - 2 * MATRICES :]
    flipped, small_got, small_sum, refs = refs[0], refs[1], refs[2], refs[3:]
    text_out, layout_out, grad_out, layout_grad_out, *refs = refs
    in_sem, cot_sem, hop_send, hop_recv, sib_send, sib_recv, send, recv, credit, out_sem, *refs = refs
    small_send, small_recv, page_send, page_recv, page_out_sem = refs
    section, d, t = lax.axis_index("section"), lax.axis_index("dp"), lax.axis_index("tensor")
    core, chip = t % 2, t // 2
    sibling = {"tensor": t + 1 - 2 * core}
    partner = {"tensor": (t + tensors // 2) % tensors}
    near, cross = {"dp": d + 1 - 2 * (d % 2)}, {"dp": 3 - d}
    outer = (d == 0) | (d == 3)
    other = {"section": 1 - section}
    hbm, probs_hbm, roots_hbm = jax.tree.unflatten(in_tree, hbm_in)
    starts = [matrix_starts(own) for own in hbm]

    plain = list(plain)
    views = []
    for b in range(2):
        fields = {}
        for name, value in hbm[b]._asdict().items():
            if name in Weights._fields:
                i = Weights._fields.index(name)
                fields[name] = work[b].raw.at[:, :, pl.ds(starts[b][i], starts[b][i + 1] - starts[b][i])]
            else:
                fields[name] = plain.pop(0)
        views.append(Needed(**fields))
    probs_in, roots = plain
    flat_views = jax.tree.leaves((tuple(views), probs_in, roots))
    flat_copies = [pltpu.make_async_copy(a, v, in_sem.at[i]) for i, (a, v) in enumerate(zip(hbm_in, flat_views))]
    loads, probs_copy, roots_copy = jax.tree.unflatten(in_tree, flat_copies)
    length = work[0].gf.shape[0]
    local_heads = probs_in.shape[1]
    blocks = hop_blocks(length)
    cot_copies = (
        pltpu.make_async_copy(cots[0], work[0].g, cot_sem.at[0]),
        pltpu.make_async_copy(cots[1], flipped, cot_sem.at[1]),
    )

    @pl.when(section == 1)
    def _():
        start(*cot_copies)

    roots_copy.start()
    for field in zip(loads[1], loads[0]):
        start(*field)
    probs_copy.start()
    greet(section, t, sections, tensors, (near, cross) if chain else ())

    part_length = text_out.shape[1]
    micro, page = core, chip
    kinds = ((grad_out, layout_grad_out), (text_out, layout_out))
    pages = ((work[0].g, flipped), ys)

    def page_part(g, q, a):
        span = pl.ds(q * part_length, part_length)
        return pages[g][a].at[span] if a == 0 else pages[g][a].at[:, span]

    def each_page(g, act):
        for q in range(tensors):
            for a in range(2):
                here = (micro == g) & (t == q)

                @pl.when((section == g) & here)
                def _():
                    act(g, q, a, True)

                @pl.when((section == g) & jnp.logical_not(here))
                def _():
                    act(g, q, a, False)

    def page_copy(g, q, a):
        return remote(
            page_part(g, q, a), kinds[g][a].at[page], page_send.at[q, a], page_recv.at[g, a, page],
            {"section": micro, "tensor": q},
        )

    def page_start(g, q, a, here):
        if here:
            pltpu.make_async_copy(page_part(g, q, a), kinds[g][a].at[page], page_recv.at[g, a, page]).start()
        else:
            page_copy(g, q, a).start()

    def page_sent(g, q, a, here):
        if not here:
            page_copy(g, q, a).wait_send()

    each_page(1, page_start)

    def blocks_of(b):
        return blocks if b == 0 else [slice(0, length)]

    def hop(b, n):
        part = work[b].g.at[blocks_of(b)[n]]
        return remote(part, part, hop_send.at[b, n], hop_recv.at[b, n], other)

    ahead = 2
    step = 2 * ROWS
    up_first, down_first = starts[0][2], starts[0][3]
    up_count, down_count = (starts[0][3] - up_first) // step, (starts[0][4] - down_first) // step
    n_feed = up_count + down_count
    chunks = [Chunk(0, k, up_first + k * step, step) for k in range(n_feed)]
    later = [(1, 0, starts[1][MATRICES])]
    later += [(0, f, n) for f, n in pieces_of(starts[0][1], starts[0][1] // 2)]
    later += [(0, starts[0][1] + f, n) for f, n in pieces_of(starts[0][2] - starts[0][1], starts[0][2] - starts[0][1])]
    chunks += [Chunk(b, n_feed + i, f, n) for i, (b, f, n) in enumerate(later)]

    def feed_chunk(k):
        return Chunk(0, k, pl.multiple_of(up_first + k * step, 16), step)

    def span(ref, c):
        return ref.at[pl.ds(c.first, c.rows)]

    def to_sibling(c):
        w, rows = work[c.b], pl.ds(c.first, c.rows)
        return remote(
            w.raw.at[:, 1 - core, rows], w.from_sibling.at[:, rows], sib_send.at[c.index], sib_recv.at[c.index], sibling
        )

    def mine(c):
        return span(work[c.b].raw.at[chip, core], c)

    def theirs(c):
        return span(work[c.b].raw.at[1 - chip, core], c)

    def to_partner(c):
        return remote(
            theirs(c), span(work[c.b].from_partner, c), send.at[0, c.index], recv.at[0, c.index], partner
        )

    def from_near(c):
        return span(work[c.b].from_sibling.at[0], c)

    def from_cross(c):
        return span(work[c.b].from_sibling.at[1], c)

    def to_near(c):
        return remote(mine(c), from_near(c), send.at[1, c.index], recv.at[1, c.index], near)

    def to_cross(c):
        return remote(mine(c), from_cross(c), send.at[2, c.index], recv.at[2, c.index], cross)

    def total_to_near(c):
        return remote(
            span(work[c.b].from_partner, c), from_near(c), send.at[3, c.index], recv.at[3, c.index], near
        )

    def out_copy(c, source):
        return pltpu.make_async_copy(span(source, c), span(results[c.b], c), out_sem.at[c.index])

    def added(target, *sources):
        target[...] = sum(s[...].astype(F32) for s in sources).astype(BF)

    def send_to_sibling(c):
        to_sibling(c).start()

    def stage_sibling(c):
        w = work[c.b]
        to_sibling(c).wait_recv()
        added(theirs(c), theirs(c), span(w.from_sibling.at[1 - chip], c))
        added(mine(c), mine(c), span(w.from_sibling.at[chip], c))
        if chain:
            @pl.when(jnp.logical_not(outer))
            def _():
                for device in (near, cross):
                    pl.semaphore_signal(credit, inc=1, device_id=device, device_id_type=MESH)

    def stage_partner(c):
        to_partner(c).wait_recv()
        added(mine(c), mine(c), span(work[c.b].from_partner, c))
        if not chain:
            out_copy(c, work[c.b].raw.at[chip, core]).start()
            return

        @pl.when(outer)
        def _():
            pl.semaphore_wait(credit, 1)
            to_near(c).start()

    def stage_near(c):
        @pl.when(jnp.logical_not(outer))
        def _():
            to_near(c).wait_recv()
            added(mine(c), mine(c), from_near(c))
            pl.semaphore_wait(credit, 1)
            to_cross(c).start()

    def stage_cross(c):
        @pl.when(jnp.logical_not(outer))
        def _():
            to_cross(c).wait_recv()
            total = work[c.b].from_partner
            added(span(total, c), mine(c), from_cross(c))
            total_to_near(c).start()
            out_copy(c, total).start()

    def stage_total(c):
        @pl.when(outer)
        def _():
            total_to_near(c).wait_recv()
            out_copy(c, work[c.b].from_sibling.at[0]).start()

    def turn_operands():
        wait(loads[0].low, loads[0].act)
        work[0].lowT[...] = views[0].low[...].T

    def feed_products():
        own, w = views[0], work[0]

        @pl.loop(0, up_count)
        def _(k):
            rows = pl.ds(pl.multiple_of(k * step, step), step)
            for q in range(tensors):
                w.raw[q // 2, q % 2, pl.ds(pl.multiple_of(up_first + k * step, 16), step), :] = dot(
                    w.lowT[rows, :], own.slope[q]
                ).astype(BF)
            send_to_sibling(feed_chunk(k))

            @pl.when((k >= 1) & (k <= ahead))
            def _():
                stage_sibling(feed_chunk(k - 1))
                to_partner(feed_chunk(k - 1)).start()

        @pl.loop(0, down_count)
        def _(k):
            lanes = pl.ds(pl.multiple_of(k * step, step), step)
            for q in range(tensors):
                w.raw[q // 2, q % 2, pl.ds(pl.multiple_of(down_first + k * step, 16), step), :] = dot(
                    own.act[q, :, lanes].T, w.gf[...]
                ).astype(BF)
            send_to_sibling(feed_chunk(up_count + k))

    def later_product(c):
        own, w = views[c.b], work[c.b]
        for q in range(tensors):
            for i in range(MATRICES):
                first = max(c.first, starts[c.b][i])
                last = min(c.first + c.rows, starts[c.b][i + 1])
                if first >= last:
                    continue
                rows = slice(first - starts[c.b][i], last - starts[c.b][i])
                if i == 0:
                    value = dot(own.qkv[q, rows, :], own.x[...])
                elif i == 1:
                    value = dot(own.ctx[q, rows, :], w.ga[...])
                elif i == 2:
                    value = dot(w.lowT[rows, :], own.slope[q])
                else:
                    value = dot(own.act[q, :, rows].T, w.gf[...])
                w.raw[q // 2, q % 2, first:last, :] = value.astype(BF)
        send_to_sibling(c)

    @pl.when(section == 1)
    def _():
        wait(*cot_copies)
        work[1].g[...] = flipped[...].T

    for b in range(2):
        work[b].sums[...] = jnp.zeros(work[b].sums.shape, F32)
    roots_copy.wait()

    def feed_back(b, n, block, hopped):
        own, own_in, w, gain = views[b], loads[b], work[b], gains[b]
        if n == 0:
            wait(own_in.n2)

        if hopped:
            hop(b, n).wait_recv()

        for rows in small_blocks(block):
            g, normed = w.g[rows].astype(F32), own.n2[rows].astype(F32)
            low = norm_rows_back(g, normed, roots[rows, 2 * b + 1 : 2 * b + 2], gain[1:2])
            w.dz[rows] = low
            w.gf[rows] = low.astype(BF)
            w.sums[1:2] += jnp.sum(g * normed, axis=0, keepdims=True)
            w.sums[3:4] += jnp.sum(g, axis=0, keepdims=True)

        if n == 0:
            wait(own_in.downward, own_in.slope, own_in.upward)

        @pl.loop(0, tensors)
        def _(q):
            d_act = dot(w.gf[block], own.downward[q // 2, q % 2])
            d_pre = (d_act * own.slope[q, block].astype(F32)).astype(BF)
            own.slope[q, block] = d_pre
            w.dz[block] += dot(d_pre, own.upward[q // 2, q % 2])

        if n == 0:
            wait(own_in.n1, own_in.outward)
        for rows in small_blocks(block):
            g, normed = w.dz[rows], own.n1[rows].astype(F32)
            low = norm_rows_back(g, normed, roots[rows, 2 * b : 2 * b + 1], gain[0:1])
            w.dz[rows] = low
            w.ga[rows] = low.astype(BF)
            w.sums[0:1] += jnp.sum(g * normed, axis=0, keepdims=True)
            w.sums[2:3] += jnp.sum(g, axis=0, keepdims=True)
        gaT = w.ga[block].T
        for q in range(tensors):
            w.dctx[q, :, block] = dot(own.outward[q // 2, q % 2], gaT).astype(BF)

    @pl.when(section == 0)
    def _():
        turn_operands()
        for s in (1, 0):
            for n, block in enumerate(blocks_of(s)):
                feed_back(s, n, block, True)

    @pl.when(section == 1)
    def _():
        for s in (1, 0):
            feed_back(s, 0, slice(0, length), False)

    @pl.when(section == 0)
    def _():
        feed_products()

    for own_in in loads:
        wait(own_in.qkv, own_in.ctx, own_in.inv)
    wait(probs_copy)
    qkv = (views[0].qkv, views[1].qkv)
    text_rows, layout_rows = slice(0, HEAD_TEXT), slice(HEAD_TEXT, HEAD_TEXT + HEAD_LAYOUT)

    def turn(k, n_known):
        fixed = isinstance(k, int)

        def at(i, stage):
            if not fixed:
                pl.when((i >= 0) & (i < n_feed))(lambda: stage(feed_chunk(i)))
            elif 0 <= i < n_known:
                stage(chunks[i])

        def sibling_and_send(c):
            stage_sibling(c)
            to_partner(c).start()

        at(k + ahead, sibling_and_send)
        at(k, stage_partner)
        if chain:
            at(k - 1, stage_near)
            at(k - 2, stage_cross)
            at(k - 3, stage_total)

    early_turns = 4

    @pl.loop(0, tensors)
    def _(q):
        for local in range(local_heads):
            head = q * local_heads + local

            @pl.when((section == 0) & (head % 4 == 0) & (head < 4 * (early_turns - 1)))
            def _():
                turn(head // 4, n_feed)

            inv = views[0].inv[q, local : local + 1, :]
            scaled = [
                (work[s].dctx[q, local * SIZES[s] : (local + 1) * SIZES[s], :].astype(F32) * inv).astype(BF)
                for s in range(2)
            ]
            inner = [
                jnp.sum(
                    scaled[s].astype(F32)
                    * views[s].ctx[q, local * SIZES[s] : (local + 1) * SIZES[s], :].astype(F32),
                    axis=0, keepdims=True,
                )
                for s in range(2)
            ]
            rows16 = lax.broadcasted_iota(jnp.int32, (16, length), 0)
            extra = jnp.zeros((16, length), F32)
            for i, value in enumerate((inner[0] + inner[1], inner[1])):
                high = value.astype(BF).astype(F32)
                extra = jnp.where(rows16 == 2 * i, -high, extra)
                extra = jnp.where(rows16 == 2 * i + 1, high - value, extra)
            pad = jnp.zeros((128 - sum(SIZES) - 16, length), BF)
            dcT = jnp.concatenate([*scaled, extra.astype(BF), pad], axis=0)
            dc = dcT.T
            qT, kT = (head_rows(qkv, q, kind, local, SCALES if kind == 0 else None) for kind in range(2))
            v_text, v_layout = (head_part(qkv, q, 2, local, s) for s in range(2))
            one, other_one = (((rows16 // 2) == i).astype(F32).astype(BF) for i in range(2))
            low = probs_in[q, local]
            probs = low.astype(F32)
            both = dot(dc, jnp.concatenate([v_text, v_layout, one, pad], axis=0))
            ds_both = (probs * both).astype(BF)
            single = dot(dc, jnp.concatenate([jnp.zeros_like(v_text), v_layout, other_one, pad], axis=0))
            ds_layout = (probs * single).astype(BF)
            dvT = dot(dcT, low)
            put_head(qkv, q, 2, local, 0, dvT[text_rows])
            put_head(qkv, q, 2, local, 1, dvT[layout_rows])
            k = kT.T
            lane = lax.broadcasted_iota(jnp.int32, (length, 128), 1)
            dq = jnp.where(lane < HEAD_TEXT, dot(ds_both, k) * SCALES[0], dot(ds_layout, k) * SCALES[1])
            dqT = dq.astype(BF).T
            put_head(qkv, q, 0, local, 0, dqT[text_rows])
            put_head(qkv, q, 0, local, 1, dqT[layout_rows])
            put_head(qkv, q, 1, local, 0, dot(qT[text_rows], ds_both))
            put_head(qkv, q, 1, local, 1, dot(qT[layout_rows], ds_layout))

    @pl.when(section == 0)
    def _():
        turn(early_turns - 1, n_feed)

    wait(loads[0].project, loads[1].project)
    page_sum = jnp.zeros((1, work[0].dz.shape[1]), F32)
    for b in (1, 0):
        for n, block in enumerate(blocks_of(b)):
            down = work[b].dz[block]
            for q in range(tensors):
                down += dot(qkv[b][q, :, block].T, views[b].project[q // 2, q % 2])
            down = down.astype(BF)
            work[b].g[block] = down
            if b == 0:
                page_sum += jnp.sum(down.astype(F32), axis=0, keepdims=True)

            @pl.when(section == 1)
            def _():
                hop(b, n).start()

    wait(loads[1].low, loads[1].act)
    work[1].lowT[...] = views[1].low[...].T
    for own_in in loads:
        wait(own_in.x)
    @pl.when(section == 1)
    def _():
        turn_operands()
        feed_products()

    for c in chunks[n_feed:]:
        later_product(c)

    @pl.when(section == 0)
    def _():
        flipped[...] = work[1].g[...].T

    at_page = (lax.broadcasted_iota(jnp.int32, lang_ids.shape, 0) == t % 2) & (
        lax.broadcasted_iota(jnp.int32, lang_ids.shape, 1) == t // 2
    )
    group = jnp.sum(jnp.where(at_page, lang_ids[...], 0), axis=(0, 1), keepdims=True)
    n_lang = small_out.shape[1] - 8
    chosen = (lax.broadcasted_iota(jnp.int32, (n_lang, 1), 0) == group) & (section == 0)
    small_sum[0, 0:n_lang] = jnp.where(chosen, page_sum, 0.0)
    small_sum[0, n_lang : n_lang + 4] = work[0].sums[...]
    small_sum[0, n_lang + 4 : n_lang + 8] = jnp.zeros((4, small_out.shape[2]), F32)
    small_sum[0, n_lang + 4 : n_lang + 8, : work[1].sums.shape[1]] = work[1].sums[...]

    def small_copy(i, device):
        return remote(small_sum.at[i], small_got.at[i], small_send.at[i], small_recv.at[i], device)

    if chain:
        small_copy(0, sibling).start()
    @pl.when(section == 1)
    def _():
        @pl.loop(0, early_turns)
        def _(k):
            turn(k, n_feed)

    for k in range(early_turns, len(chunks) + (3 if chain else 0)):
        turn(k, len(chunks))
        if k == len(chunks) - 1:
            each_page(0, page_start)
        if not chain:
            continue
        if k == early_turns:
            small_copy(0, sibling).wait_recv()
            small_sum[1] = small_sum[0] + small_got[0]
            small_copy(1, partner).start()
        if k == early_turns + 1:
            small_copy(1, partner).wait_recv()
            small_sum[2] = small_sum[1] + small_got[1]
            small_copy(2, near).start()
        if k == early_turns + 2:
            small_copy(2, near).wait_recv()
            small_sum[3] = small_sum[2] + small_got[2]

            @pl.when(jnp.logical_not(outer))
            def _():
                small_copy(3, cross).start()

        if k == early_turns + 3:
            @pl.when(jnp.logical_not(outer))
            def _():
                small_copy(3, cross).wait_recv()
                small_sum[4] = small_sum[3] + small_got[3]
                small_copy(4, near).start()

        if k == early_turns + 4:
            @pl.when(outer)
            def _():
                small_copy(4, near).wait_recv()
                small_sum[4] = small_got[4]

            small_sum[5] = small_sum[4]
            small_copy(5, other).start()

    if chain:
        for i, device in enumerate((sibling, partner, near)):
            small_copy(i, device).wait_send()

        @pl.when(jnp.logical_not(outer))
        def _():
            small_copy(3, cross).wait_send()
            small_copy(4, near).wait_send()

        small_copy(5, other).wait()
        small_out[0] = small_sum[5]
        small_out[1] = small_got[5]
    else:
        small_out[0] = small_sum[0]
        small_out[1] = small_sum[0]

    @pl.when(section == 1)
    def _():
        for b in range(2):
            for n in range(len(blocks_of(b))):
                hop(b, n).wait_send()

    for c in chunks:
        to_sibling(c).wait_send()
        to_partner(c).wait_send()
        if not chain:
            out_copy(c, work[c.b].from_partner).wait()
            continue

        @pl.when(outer)
        def _():
            to_near(c).wait_send()

        @pl.when(jnp.logical_not(outer))
        def _():
            to_cross(c).wait_send()
            total_to_near(c).wait_send()

        out_copy(c, work[c.b].from_partner).wait()

    for g in range(sections):
        each_page(g, page_sent)
        for a in range(2):
            for j in range(2):
                dst = kinds[g][a].at[j]
                remote(dst, dst, page_send.at[0, a], page_recv.at[g, a, j], partner).wait_recv()
    landed = (text_out, layout_out, grad_out, layout_grad_out)
    copies = [pltpu.make_async_copy(v, h, page_out_sem.at[i]) for i, (v, h) in enumerate(zip(landed, page_outs))]
    start(*copies)
    wait(*copies)


def layer_backward(mesh, x, y, probs, roots, kept, weights, cots, norms, lang_ids, n_lang):
    sections, dp, tensors = mesh.shape["section"], mesh.shape["dp"], mesh.shape["tensor"]
    chain = dp == 4
    weights = tuple(Weights(*(m.reshape((tensors // 2, 2) + m.shape[1:]) for m in w)) for w in weights)
    needed = tuple(
        Needed(
            n2=k.n2, downward=w.downward, slope=k.slope, upward=w.upward, n1=k.n1,
            outward=w.outward, low=k.low, act=k.act, qkv=k.qkv, ctx=k.ctx, inv=k.inv, project=w.project, x=rows,
        )
        for k, w, rows in zip(kept, weights, x)
    )
    flat_in, in_tree = jax.tree.flatten((needed, probs, roots))
    plain = [v for own in needed for name, v in own._asdict().items() if name not in Weights._fields] + [probs, roots]
    stacks = [(matrix_starts(own)[MATRICES], rows.shape[1]) for own, rows in zip(needed, x)]
    length = x[0].shape[0]
    work = []
    for own, rows, (count, width) in zip(needed, x, stacks):
        work += Work(
            g=shape(rows.shape), gf=shape(rows.shape), ga=shape(rows.shape), dz=shape(rows.shape, F32),
            dctx=shape(own.ctx.shape), sums=shape((4, width), F32), lowT=shape((width, length)),
            raw=shape((tensors // 2, 2, count, width)), from_sibling=shape((tensors // 2, count, width)),
            from_partner=shape((count, width)),
        )
    small = shape((2, n_lang + 8, x[0].shape[1]), F32)
    text_page = shape((2, length // tensors, x[0].shape[1]))
    layout_page = shape((2, x[1].shape[1], length // tensors))
    summed = [shape(s) for s in stacks]
    own = needed[0]
    n_chunks = (own.upward.shape[-2] + own.downward.shape[-2]) // (2 * ROWS) + 4
    n_blocks = len(hop_blocks(length))
    dma = pltpu.SemaphoreType.DMA
    results = pl.pallas_call(
        functools.partial(backward_kernel, sections, tensors, chain, in_tree),
        out_shape=summed + [small, text_page, layout_page, text_page, layout_page],
        in_specs=[ANY] * (len(flat_in) + 4) + [VMEM] * 3,
        out_specs=[ANY] * 2 + [VMEM] + [ANY] * 4,
        scratch_shapes=vmem_like(work) + vmem_like(plain)
        + [pltpu.VMEM(cots[1].shape, BF)] + [pltpu.VMEM((6,) + small.shape[1:], F32)] * 2
        + vmem_like([text_page, layout_page] * 2)
        + [dma((len(flat_in),)), dma((2,)), dma((2, n_blocks)), dma((2, n_blocks))]
        + [dma((n_chunks,))] * 2 + [dma((4, n_chunks))] * 2
        + [pltpu.SemaphoreType.REGULAR, dma((n_chunks,))]
        + [dma((6,))] * 2 + [dma((tensors, 2)), dma((sections, 2, 2)), dma((4,))],
        compiler_params=pltpu.CompilerParams(
            collective_id=1, has_side_effects=True, vmem_limit_bytes=64 << 20
        ),
        name="layer_backward",
    )(*flat_in, *cots, *y, lang_ids, norms[0][0], norms[1][0])
    totals, small, pages = results[:2], results[2], results[3:7]
    if not chain:
        totals = lax.psum(tuple(totals), "dp")
        both = lax.psum(small[0], ("dp", "tensor"))
        small = jnp.stack([both, lax.ppermute(both, "section", [(0, 1), (1, 0)])])
    return totals, small, pages


def widen_kernel(n_in, n_pages, *refs):
    n_out = 5 + n_pages + 2 * MATRICES
    hbm_in, hbm_out = refs[:n_in], refs[n_in : n_in + n_out]
    vmem_in, vmem_out = refs[n_in + n_out : 2 * n_in + n_out], refs[2 * n_in + n_out : -2]
    in_sem, out_sem = refs[-2:]
    loads = [pltpu.make_async_copy(h, v, in_sem.at[i]) for i, (h, v) in enumerate(zip(hbm_in, vmem_in))]
    sources = vmem_out[:5] + vmem_in[3:] + vmem_out[5:]
    stores = [pltpu.make_async_copy(v, h, out_sem.at[i]) for i, (v, h) in enumerate(zip(sources, hbm_out))]
    start(*loads)
    totals, small = vmem_in[0:2], vmem_in[2]
    for b in range(2):
        wait(loads[b])
        at = 0
        for i in range(b * MATRICES, (b + 1) * MATRICES):
            out = vmem_out[5 + i]
            for c in range(0, out.shape[0], 48):
                out[c : c + 48] = totals[b][at + c : at + c + 48].astype(F32)
            at += out.shape[0]
            stores[5 + n_pages + i].start()
    for i in range(n_pages):
        loads[3 + i].wait()
        stores[5 + i].start()
    loads[2].wait()
    n_lang = vmem_out[0].shape[0]
    vmem_out[0][...] = jnp.where(lax.axis_index("section") == 0, small[0, :n_lang], small[1, :n_lang])
    for i, out in enumerate(vmem_out[1:5]):
        first = n_lang + 2 * i
        out[...] = small[0, first : first + 2, : out.shape[1]]
    start(*stores[:5])
    wait(*stores)


def widen(totals, small, pages, shards, n_lang):
    widths = [total.shape[1] for total in totals]
    sums = [shape((n_lang, widths[0]), F32)] + [shape((2, w), F32) for w in widths for _ in range(2)]
    grads = [shape(m.shape, F32) for own in shards for m in own]
    inputs = (*totals, small, *pages)
    outs = sums + [shape(page.shape) for page in pages] + grads
    results = pl.pallas_call(
        functools.partial(widen_kernel, len(inputs), len(pages)), out_shape=outs,
        in_specs=[ANY] * len(inputs), out_specs=[ANY] * len(outs),
        scratch_shapes=vmem_like(inputs) + vmem_like(sums + grads)
        + [pltpu.SemaphoreType.DMA((len(inputs),)), pltpu.SemaphoreType.DMA((len(outs),))],
        compiler_params=pltpu.CompilerParams(vmem_limit_bytes=62 << 20), name="widen",
    )(*inputs)
    return results[0], results[1:5], results[5:9], results[9:13], results[13:17]


def per_device(
    mesh,
    text_input,
    layout_input,
    text_cotangent,
    layout_cotangent,
    page_counts,
    pad_mask,
    lang_ids,
    lang_table,
    text_project,
    text_outward,
    text_upward,
    text_downward,
    text_gains,
    text_biases,
    layout_project,
    layout_outward,
    layout_upward,
    layout_downward,
    layout_gains,
    layout_biases,
):
    def flat(project):
        return jnp.transpose(project[0], (1, 2, 0)).reshape(-1, project.shape[1])

    def flipped(block):
        return jnp.transpose(block[0], (0, 2, 1))

    shards = (
        Weights(flat(text_project), text_outward[0], text_upward[0], text_downward[0]),
        Weights(flat(layout_project), layout_outward[0], layout_upward[0], layout_downward[0]),
    )
    norms = ((text_gains[0], text_biases[0]), (layout_gains[0], layout_biases[0]))
    marks = (pad_mask, page_counts, lang_ids, lang_table)
    (x, y, probs, roots, kept, weights), cots = layer_forward(
        mesh, text_input[0], flipped(layout_input), text_cotangent[0], flipped(layout_cotangent), shards, norms, marks
    )
    n_lang = lang_table.shape[0]
    totals, small, pages = layer_backward(mesh, x, y, probs, roots, kept, weights, cots, norms, lang_ids, n_lang)
    lang_sum, norm_sums, pages, text_sums, layout_sums = widen(totals, small, pages, shards, n_lang)
    text_out, layout_out, text_grad, layout_grad = pages

    def unflat(grad, like):
        return jnp.transpose(grad.reshape(like.shape[2], like.shape[3], like.shape[1]), (2, 0, 1))[None]

    unflip = lambda block: jnp.transpose(block, (0, 2, 1))[None]
    return (
        text_out[None], unflip(layout_out), text_grad[None], unflip(layout_grad), lang_sum,
        unflat(text_sums[0], text_project), *(s[None] for s in text_sums[1:]), norm_sums[0][None], norm_sums[1][None],
        unflat(layout_sums[0], layout_project), *(s[None] for s in layout_sums[1:]),
        norm_sums[2][None], norm_sums[3][None],
    )


def solution(mesh):
    tokens = P("section", "dp", "tensor", None)
    weight_specs = (
        P("section", None, None, "tensor"), P("section", "tensor", None), P("section", None, "tensor"),
        P("section", "tensor", None), P("section", None, None), P("section", None, None),
    )
    in_specs = (tokens,) * 4 + (P(None, "dp"), P(None, "dp", None), P(None, "dp"), P()) + weight_specs * 2
    out_specs = (tokens,) * 4 + (P(),) + weight_specs * 2
    return jax.shard_map(
        functools.partial(per_device, mesh), mesh=mesh, in_specs=in_specs, out_specs=out_specs, check_vma=False
    )
```

```python
import functools
import math
import typing

import jax
import jax.numpy as jnp
from jax import lax
from jax.experimental import pallas as pl
from jax.experimental.pallas import tpu as pltpu
from jax.sharding import PartitionSpec as P

HEAD_TEXT = 64
HEAD_LAYOUT = 16
EPSILON = 1e-05
NEGATIVE = -1e30
HIGH = lax.Precision.HIGHEST
MESH = pl.DeviceIdType.MESH
BF = jnp.bfloat16
F32 = jnp.float32
ANY = pl.BlockSpec(memory_space=pl.ANY)


def remote(src, dst, send, recv, device):
    return pltpu.make_async_remote_copy(
        src_ref=src, dst_ref=dst, send_sem=send, recv_sem=recv, device_id=device, device_id_type=MESH
    )


def greet(section, tensor, sections, tensors, extra=()):
    barrier = pltpu.get_barrier_semaphore()
    for g in range(sections):
        for q in range(tensors):

            @pl.when((section != g) | (tensor != q))
            def _():
                pl.semaphore_signal(
                    barrier, inc=1, device_id={"section": g, "tensor": q}, device_id_type=MESH
                )

    for device in extra:
        pl.semaphore_signal(barrier, inc=1, device_id=device, device_id_type=MESH)
    pl.semaphore_wait(barrier, sections * tensors - 1 + len(extra))


GELU_P = 0.3275911
GELU_A = (0.254829592, -0.284496736, 1.421413741, -1.453152027, 1.061405429)
NN = (((1,), (0,)), ((), ()))
NT = (((1,), (1,)), ((), ()))
SCALES = (1.0 / math.sqrt(HEAD_TEXT), 1.0 / math.sqrt(HEAD_LAYOUT))
SIZES = (HEAD_TEXT, HEAD_LAYOUT)
ROWS = 128


class Weights(typing.NamedTuple):
    project: typing.Any
    outward: typing.Any
    upward: typing.Any
    downward: typing.Any


class Kept(typing.NamedTuple):
    qkv: typing.Any
    ctx: typing.Any
    inv: typing.Any
    n1: typing.Any
    low: typing.Any
    act: typing.Any
    slope: typing.Any
    n2: typing.Any


def dot(a, b, dims=NN):
    return lax.dot_general(a, b, dims, preferred_element_type=F32)


def gelu_pair(u):
    d = 1.0 + (GELU_P / math.sqrt(2.0)) * jnp.abs(u)
    t = pl.reciprocal(d, approx=True)
    t = t * (2.0 - d * t)
    e = jnp.exp2((u * u) * (-0.5 / math.log(2.0)))
    a1, a2, a3, a4, a5 = (0.5 * a for a in GELU_A)
    tail = ((((a5 * t + a4) * t + a3) * t + a2) * t + a1) * t * e
    cdf = jnp.where(u >= 0, 1.0 - tail, tail)
    return u * cdf, cdf + u * e * (1.0 / math.sqrt(2.0 * math.pi))


def norm_rows(z, gain, offset):
    center = z - jnp.mean(z, axis=-1, keepdims=True)
    inverse = lax.rsqrt(jnp.mean(center * center, axis=-1, keepdims=True) + EPSILON)
    normed = center * inverse
    return normed * gain + offset, normed, inverse


def norm_rows_back(g, n, r, gain):
    t = g * gain
    return r * (t - jnp.mean(t, axis=-1, keepdims=True) - n * jnp.mean(t * n, axis=-1, keepdims=True))


class Staged:
    def __init__(self, tree, hbm, vmem, sem, inward):
        self.tree, self.vmem = tree, list(vmem)
        pairs = zip(hbm, vmem) if inward else zip(vmem, hbm)
        self.copies = [pltpu.make_async_copy(a, b, sem.at[i]) for i, (a, b) in enumerate(pairs)]

    def refs(self):
        return jax.tree.unflatten(self.tree, self.vmem)

    def parts(self):
        return jax.tree.unflatten(self.tree, self.copies)

    def start(self):
        for copy in self.copies:
            copy.start()

    def wait(self):
        for copy in self.copies:
            copy.wait()


def start(*copies):
    for copy in copies:
        copy.start()


def wait(*copies):
    for copy in copies:
        copy.wait()


def head_rows(stacks, slot, kind, local, scales=None, extra=None):
    rows = []
    for b in range(2):
        piece = head_part(stacks, slot, kind, local, b)
        rows.append(piece if scales is None else piece * BF(scales[b]))
    length = rows[0].shape[1]
    rows.append(jnp.zeros((16, length), BF) if extra is None else extra)
    rows.append(jnp.zeros((128 - sum(SIZES) - 16, length), BF))
    return jnp.concatenate(rows, axis=0)


def head_part(stacks, slot, kind, local, b):
    first = kind * (stacks[b].shape[1] // 3) + local * SIZES[b]
    return stacks[b][slot, first : first + SIZES[b], :]


def small_blocks(block, step=64):
    return [slice(c, c + step) for c in range(block.start, block.stop, step)]


def put_head(stacks, slot, kind, local, b, value):
    first = kind * (stacks[b].shape[1] // 3) + local * SIZES[b]
    stacks[b][slot, first : first + SIZES[b], :] = value.astype(BF)


def hop_blocks(length):
    ends = [0, length // 2, length * 3 // 4, length]
    return [slice(a, b) for a, b in zip(ends, ends[1:])]


def slot_of(u, core, chip):
    return ((chip + u // 2) % 2) * 2 + (core + u % 2) % 2


def forward_kernel(sections, tensors, shared, in_tree, out_tree, *refs):
    n_w, n_out = len(shared), out_tree.num_leaves
    sources = (refs[0:2], refs[2:4])
    shards = refs[4 : 4 + n_w]
    pad_mask, counts, lang_ids, lang_table, *norms = refs[4 + n_w : 12 + n_w]
    rest = refs[12 + n_w :]
    hbm_out, cots_out, rest = rest[:n_out], rest[n_out : n_out + 2], rest[n_out + 2 :]
    outgoing = Staged(out_tree, hbm_out, rest[:n_out], rest[n_out], False)
    rest = rest[n_out + 1 :]
    flipped, raw_x, y_narrow, *rest = rest
    nats, totals, pre, score_buffer, rest = rest[0:2], rest[2:4], rest[4:6], rest[6], rest[7:]
    xT, turned, turn_sem, rest = rest[0:2], (rest[2:4], rest[4:6]), rest[6], rest[7:]
    page_send, page_recv, w_send, w_recv, own_sem, hop_send, hop_recv, cot_sem, act_sem = rest
    x, y_pages, probs_out, roots, kept, weights = outgoing.refs()
    y = (y_pages[0], y_narrow)
    x_out, y_out, probs_copy, roots_copy, kept_out, weights_out = outgoing.parts()
    kept_hbm, weights_hbm = jax.tree.unflatten(out_tree, list(hbm_out))[4:6]
    section, d, t = lax.axis_index("section"), lax.axis_index("dp"), lax.axis_index("tensor")
    core, chip, half_index = t % 2, t // 2, d % 2
    sibling, partner = t + 1 - 2 * core, (t + tensors // 2) % tensors
    mate = d + 1 - 2 * half_index
    micro, page = core, chip
    part_length = sources[0][0].shape[1]
    length = x[0].shape[0]
    blocks = [slice(c, c + 2 * ROWS) for c in range(0, length, 2 * ROWS)]
    parts = hop_blocks(length)
    full = (
        weights[0].project, weights[1].project, weights[0].outward, weights[0].upward,
        weights[0].downward, weights[1].outward, weights[1].upward, weights[1].downward,
    )
    greet(section, t, sections, tensors, ({"dp": mate},) if any(shared) else ())

    def half_of(ref, i, which):
        count = shards[i].shape[0] // 2
        return ref.at[pl.ds(pl.multiple_of(which * count, 16), count)] if shared[i] else ref

    def to_partner(i):
        return remote(
            half_of(shards[i], i, half_index), half_of(full[i].at[t], i, half_index),
            w_send.at[0, i], w_recv.at[0, i], {"tensor": partner},
        )

    def to_sibling(i):
        return remote(full[i].at[t], full[i].at[t], w_send.at[1, i], w_recv.at[1, i], {"tensor": sibling})

    def to_mate(i):
        ref = half_of(full[i].at[partner], i, half_index)
        return remote(ref, ref, w_send.at[2, i], w_recv.at[2, i], {"dp": mate})

    def on_first(i):
        ref = half_of(full[i].at[partner], i, half_index)
        return remote(ref, ref, w_send.at[3, i], w_recv.at[3, i], {"tensor": sibling})

    def on_second(i):
        ref = half_of(full[i].at[partner], i, 1 - half_index)
        return remote(ref, ref, w_send.at[4, i], w_recv.at[4, i], {"tensor": sibling})

    def keep(i):
        return pltpu.make_async_copy(shards[i], full[i].at[t], own_sem.at[i])

    def relay(*which):
        for i in which:
            to_partner(i).wait_recv()
            if shared[i]:
                to_mate(i).start()
            on_first(i).start()

    def relay_second(*which):
        for i in which:
            if shared[i]:
                to_mate(i).wait_recv()
                on_second(i).start()

    def early(*which):
        for i in which:
            to_sibling(i).wait_recv()

    def late(*which):
        for i in which:
            on_first(i).wait_recv()
            if shared[i]:
                on_second(i).wait_recv()

    def token_slot(g, a, index):
        start_at = pl.multiple_of(index * part_length, part_length)
        target = (raw_x, flipped)[a]
        return target.at[pl.ds(start_at, part_length)] if a == 0 else target.at[:, pl.ds(start_at, part_length)]

    def over_pages(g, act):
        for j in range(2):
            target = 2 * j + section
            here = (section == g) & (t == target)
            for a in range(2):
                act(g, j, a, target, here)

    def page_copy(g, j, a, target):
        return remote(
            sources[g][a].at[j], token_slot(g, a, t), page_send.at[g, j, a], page_recv.at[a, t],
            {"section": g, "tensor": target},
        )

    def page_start(g, j, a, target, here):
        @pl.when(here)
        def _():
            pltpu.make_async_copy(sources[g][a].at[j], token_slot(g, a, t), page_recv.at[a, t]).start()

        @pl.when(jnp.logical_not(here))
        def _():
            page_copy(g, j, a, target).start()

    def page_sent(g, j, a, target, here):
        @pl.when(jnp.logical_not(here))
        def _():
            page_copy(g, j, a, target).wait_send()

    def pages_arrived(g):
        for a in range(2):
            for q in range(tensors):
                slot = token_slot(g, a, q)
                remote(slot, slot, page_send.at[0, 0, a], page_recv.at[a, q], {"tensor": sibling}).wait_recv()

    def parts_of(b):
        return parts if b == 0 else [slice(0, length)]

    def hop(b, n):
        part = parts_of(b)[n]
        return remote(
            y[b].at[part], x[b].at[part], hop_send.at[b, n], hop_recv.at[b, n], {"section": 1 - section}
        )

    def weights_to_hbm():
        for b in range(2):
            start(weights_out[b].project, weights_out[b].outward)
            for q in range(tensors):
                for m, name in enumerate((2, 3)):
                    copy = pltpu.make_async_copy(
                        turned[b][m].at[q % 2], weights_hbm[b][name].at[q], turn_sem.at[b, m, q % 2]
                    )
                    if q >= 2:
                        copy.wait()
                    turned[b][m][q % 2] = weights[b][name][q].T
                    copy.start()
        for b in range(2):
            for q in range(tensors - 2, tensors):
                for m, name in enumerate((2, 3)):
                    pltpu.make_async_copy(
                        turned[b][m].at[q % 2], weights_hbm[b][name].at[q], turn_sem.at[b, m, q % 2]
                    ).wait()

    over_pages(0, page_start)
    for i in range(n_w):
        keep(i).start()
    for i in range(n_w):
        to_partner(i).start()

    @pl.when(section == 1)
    def _():
        over_pages(1, page_start)

    for i in range(n_w):
        keep(i).wait()
        to_sibling(i).start()

    at_page = (lax.broadcasted_iota(jnp.int32, counts.shape, 0) == micro) & (
        lax.broadcasted_iota(jnp.int32, counts.shape, 1) == page
    )

    def own_entry(ref):
        return jnp.sum(jnp.where(at_page, ref[...], 0), axis=(0, 1), keepdims=True)

    positions = lax.broadcasted_iota(jnp.int32, (1, length), 1)
    mask_row = pad_mask[micro, pl.ds(page, 1), :]
    key_mask = (positions < own_entry(counts)) & ((mask_row == 1) | (positions == 0))
    first_row = (lax.broadcasted_iota(jnp.int32, (16, length), 0) == 0).astype(F32)
    mask_row16 = (first_row * jnp.where(key_mask, 0.0, NEGATIVE)).astype(BF)
    groups = lax.broadcasted_iota(jnp.int32, (lang_table.shape[0], 1), 0)
    lang_row = jnp.sum(jnp.where(groups == own_entry(lang_ids), lang_table[...], 0.0), axis=0, keepdims=True)
    local_heads = weights[0].project.shape[1] // (3 * HEAD_TEXT)
    qkv = (kept[0].qkv, kept[1].qkv)

    @pl.when(section == 0)
    def _():
        pages_arrived(0)
        x[0][...] = (raw_x[...].astype(F32) + lang_row).astype(BF)
        x[1][...] = flipped[...].T
        early(0, 1)

    @pl.when(section == 1)
    def _():
        relay(*range(n_w))
        relay_second(*range(n_w))
        early(*range(n_w))
        late(*range(n_w))
        weights_to_hbm()

    @pl.loop(0, 2)
    def _(half):
        @pl.when((half == 1) & (section == 0))
        def _():
            relay(0, 1)
            relay_second(0)
            late(0, 1)

        for n, block in enumerate(parts):
            @pl.when((half == 0) & (section == 1))
            def _():
                for b in range(2):
                    if n < len(parts_of(b)):
                        hop(b, n).wait_recv()

            @pl.when(half == 0)
            def _():
                for b in range(2):
                    xT[b][:, block] = x[b][block].T

            @pl.loop(0, 2)
            def _(u):
                slot = slot_of(2 * half + u, core, chip)
                for b in range(2):
                    qkv[b][slot, :, block] = dot(weights[b].project[slot], xT[b][:, block]).astype(BF)

        @pl.loop(0, 2)
        def _(u):
            slot = slot_of(2 * half + u, core, chip)
            for local in range(local_heads):
                q = head_rows(qkv, slot, 0, local, SCALES, first_row.astype(BF)).T
                kT = head_rows(qkv, slot, 1, local, None, mask_row16)
                score_buffer[local] = dot(q, kT)
                for rows in small_blocks(slice(0, length)):
                    scores = score_buffer[local, rows, :]
                    raised = jnp.exp(scores - jnp.max(scores, axis=-1, keepdims=True))
                    probs_out[slot, local, rows, :] = raised.astype(BF)
                vT = head_rows(qkv, slot, 2, local, None, first_row.astype(BF))
                ctx = dot(probs_out[slot, local], vT.T).T
                inv = 1.0 / ctx[sum(SIZES) : sum(SIZES) + 1]
                ctx = (ctx * inv).astype(BF)
                kept[0].inv[slot, local : local + 1, :] = inv
                kept[0].ctx[slot, local * HEAD_TEXT : (local + 1) * HEAD_TEXT, :] = ctx[:HEAD_TEXT]
                kept[1].ctx[slot, local * HEAD_LAYOUT : (local + 1) * HEAD_LAYOUT, :] = ctx[
                    HEAD_TEXT : HEAD_TEXT + HEAD_LAYOUT
                ]

    kept[1].inv[...] = jnp.zeros(kept[1].inv.shape, F32)
    start(probs_copy, *x_out, *(c for k in kept_out for c in (k.qkv, k.ctx, k.inv)))

    def attend(b):
        gains, biases = norms[2 * b : 2 * b + 2]
        width = x[b].shape[1]
        nats[b][...] = kept[b].ctx[...].reshape(width, length).T
        wide = weights[b].outward[...].reshape(width, width)
        for block in blocks:
            totals[b][1, block] = dot(nats[b][block], wide)
            for rows in small_blocks(block):
                h, n, r = norm_rows(x[b][rows].astype(F32) + totals[b][1, rows], gains[0:1], biases[0:1])
                totals[b][0, rows] = h
                totals[b][1, rows] = jnp.zeros(h.shape, F32)
                kept[b].n1[rows] = n.astype(BF)
                roots[rows, 2 * b : 2 * b + 1] = r
                kept[b].low[rows] = h.astype(BF)
        start(kept_out[b].n1, kept_out[b].low)

    def slot_copies(b, slot):
        return [
            pltpu.make_async_copy(v.at[slot], h.at[slot], act_sem.at[b, m, slot])
            for m, (v, h) in enumerate(((kept[b].act, kept_hbm[b].act), (kept[b].slope, kept_hbm[b].slope)))
        ]

    def feed(b, first, which):
        @pl.loop(first, first + 2)
        def _(u):
            slot = slot_of(u, core, chip)
            for block in which:
                pre[b][block] = dot(kept[b].low[block], weights[b].upward[slot])
                for rows in small_blocks(block, 16):
                    act, slope = gelu_pair(pre[b][rows])
                    kept[b].act[slot, rows] = act.astype(BF)
                    kept[b].slope[slot, rows] = slope.astype(BF)
                totals[b][1, block] += dot(kept[b].act[slot, block], weights[b].downward[slot])
                if block == slice(0, length):
                    start(*slot_copies(b, slot))

    def finish(b):
        gains, biases = norms[2 * b : 2 * b + 2]
        def last(block):
            feed(b, 2, [block])
            for rows in small_blocks(block):
                out, normed, r = norm_rows(totals[b][0, rows] + totals[b][1, rows], gains[1:2], biases[1:2])
                y[b][rows] = out.astype(BF)
                kept[b].n2[rows] = normed.astype(BF)
                roots[rows, 2 * b + 1 : 2 * b + 2] = r

        @pl.when(section == 0)
        def _():
            for n, block in enumerate(parts_of(b)):
                last(block)
                hop(b, n).start()
            if b == 0:
                for u in range(2, 4):
                    start(*slot_copies(b, slot_of(u, core, chip)))

        @pl.when(section == 1)
        def _():
            last(slice(0, length))

        if b == 1:
            y_pages[1][...] = y_narrow[...].T
        start(y_out[b], kept_out[b].n2)

    @pl.when(section == 0)
    def _():
        relay(2, 3)
        early(2)
        late(2)

    attend(0)

    @pl.when(section == 0)
    def _():
        early(3, 4)

    feed(0, 0, [slice(0, length)])

    @pl.when(section == 0)
    def _():
        relay(4, 5, 6, 7)
        relay_second(3)
        early(5, 6, 7)
        late(5, 6, 7)

    attend(1)
    feed(1, 0, [slice(0, length)])
    finish(1)

    @pl.when(section == 0)
    def _():
        relay_second(4)
        late(3, 4)

    finish(0)
    start(roots_copy)

    @pl.when(section == 0)
    def _():
        over_pages(1, page_start)


    @pl.when(section == 0)
    def _():
        weights_to_hbm()
        for b in range(2):
            for n in range(len(parts_of(b))):
                hop(b, n).wait_send()

    for i in range(n_w):
        to_partner(i).wait_send()
        to_sibling(i).wait_send()
        on_first(i).wait_send()
        if shared[i]:
            to_mate(i).wait_send()
            on_second(i).wait_send()
    for g in range(sections):
        over_pages(g, page_sent)

    @pl.when(section == 1)
    def _():
        pages_arrived(1)
        copies = [pltpu.make_async_copy(v, h, cot_sem.at[i]) for i, (v, h) in enumerate(zip((raw_x, flipped), cots_out))]
        start(*copies)
        wait(*copies)

    for group in (x_out, y_out, (probs_copy, roots_copy), *(w[:2] for w in weights_out)):
        wait(*group)
    for b, k in enumerate(kept_out):
        wait(k.qkv, k.ctx, k.inv, k.n1, k.low, k.n2)
        for slot in range(tensors):
            wait(*slot_copies(b, slot))


def vmem_like(tree):
    return [pltpu.VMEM(s.shape, s.dtype) for s in jax.tree.leaves(tree)]


VMEM = pl.BlockSpec(memory_space=pltpu.VMEM)


def shape(dims, dtype=BF):
    return jax.ShapeDtypeStruct(tuple(dims), dtype)


def layer_forward(mesh, text_in, layout_in, text_cot, layout_cot, shards, norms, marks):
    sections, dp, tensors = mesh.shape["section"], mesh.shape["dp"], mesh.shape["tensor"]
    length = text_in.shape[1] * tensors
    rows = (shape((length, text_in.shape[2])), shape((length, layout_in.shape[1])))
    local_heads = shards[0].project.shape[0] // (3 * HEAD_TEXT)
    kept = []
    for x, w in zip(rows, shards):
        units = shape((tensors, length, w.upward.shape[1]))
        kept.append(Kept(
            qkv=shape((tensors, w.project.shape[0], length)), ctx=shape((tensors, w.outward.shape[0], length)),
            inv=shape((tensors, local_heads, length), F32),
            n1=shape(x.shape), low=shape(x.shape), act=units, slope=units,
            n2=shape(x.shape),
        ))
    weights = tuple(Weights(*(shape((tensors,) + m.shape) for m in w)) for w in shards)
    pages_out = (rows[0], shape((rows[1].shape[1], length)))
    outs = (rows, pages_out, shape((tensors, local_heads, length, length)), shape((length, 4), F32), tuple(kept), weights)
    flat_out, out_tree = jax.tree.flatten(outs)
    (a, b) = shards
    ordered = (a.project, b.project, a.outward, a.upward, a.downward, b.outward, b.upward, b.downward)
    shared = tuple(dp % 2 == 0 and w.shape[0] >= 512 for w in ordered)
    n_w = len(ordered)
    cots = [rows[0], shape((rows[1].shape[1], length))]
    small = (*marks, *norms[0], *norms[1])
    results = pl.pallas_call(
        functools.partial(forward_kernel, sections, tensors, shared, None, out_tree),
        out_shape=flat_out + cots,
        in_specs=[ANY] * (4 + n_w) + [VMEM] * len(small),
        out_specs=[ANY] * (len(flat_out) + 2),
        scratch_shapes=vmem_like(flat_out) + [pltpu.SemaphoreType.DMA((len(flat_out),))]
        + [pltpu.VMEM(cots[1].shape, BF), pltpu.VMEM(cots[0].shape, BF), pltpu.VMEM(rows[1].shape, BF)]
        + [pltpu.VMEM(x.shape, BF) for x in rows]
        + [pltpu.VMEM((2,) + x.shape, F32) for x in rows]
        + [pltpu.VMEM((length, w.upward.shape[1]), F32) for w in shards]
        + [pltpu.VMEM((local_heads, length, length), F32)]
        + [pltpu.VMEM((x.shape[1], length), BF) for x in rows]
        + [pltpu.VMEM((2,) + m.shape, BF) for w in shards for m in (w.upward, w.downward)]
        + [pltpu.SemaphoreType.DMA((2, 2, 2))]
        + [
            pltpu.SemaphoreType.DMA((sections, 2, 2)), pltpu.SemaphoreType.DMA((2, tensors)),
            pltpu.SemaphoreType.DMA((5, n_w)), pltpu.SemaphoreType.DMA((5, n_w)), pltpu.SemaphoreType.DMA((n_w,)),
            pltpu.SemaphoreType.DMA((2, len(hop_blocks(length)))), pltpu.SemaphoreType.DMA((2, len(hop_blocks(length)))),
            pltpu.SemaphoreType.DMA((2,)), pltpu.SemaphoreType.DMA((2, 2, tensors)),
        ],
        compiler_params=pltpu.CompilerParams(
            collective_id=0, has_side_effects=True, vmem_limit_bytes=62 << 20
        ),
        name="layer_forward",
    )(text_in, layout_in, text_cot, layout_cot, *ordered, *small)
    return jax.tree.unflatten(out_tree, results[:-2]), tuple(results[-2:])


class Needed(typing.NamedTuple):
    n2: typing.Any
    downward: typing.Any
    slope: typing.Any
    upward: typing.Any
    n1: typing.Any
    outward: typing.Any
    low: typing.Any
    act: typing.Any
    qkv: typing.Any
    ctx: typing.Any
    inv: typing.Any
    project: typing.Any
    x: typing.Any


class Work(typing.NamedTuple):
    g: typing.Any
    gf: typing.Any
    ga: typing.Any
    dz: typing.Any
    dctx: typing.Any
    sums: typing.Any
    lowT: typing.Any
    raw: typing.Any
    from_sibling: typing.Any
    from_partner: typing.Any


class Chunk(typing.NamedTuple):
    b: typing.Any
    index: typing.Any
    first: typing.Any
    rows: typing.Any


MATRICES = 4


def matrix_rows(own):
    return own.project.shape[-2], own.outward.shape[-2], own.upward.shape[-2], own.downward.shape[-2]


def matrix_starts(own):
    sizes = matrix_rows(own)
    return [sum(sizes[:i]) for i in range(MATRICES + 1)]


def pieces_of(size, step):
    return [(f, step) for f in range(0, size, step)]


def backward_kernel(sections, tensors, chain, in_tree, *refs):
    n_in = in_tree.num_leaves
    hbm_in, refs = refs[:n_in], refs[n_in:]
    (cots, ys, lang_ids, gains), refs = (refs[0:2], refs[2:4], refs[4], refs[5:7]), refs[7:]
    results, small_out, page_outs, refs = refs[0:2], refs[2], refs[3:7], refs[7:]
    n_work = len(Work._fields)
    work, refs = (Work(*refs[:n_work]), Work(*refs[n_work : 2 * n_work])), refs[2 * n_work :]
    plain, refs = refs[: n_in - 2 * MATRICES], refs[n_in - 2 * MATRICES :]
    flipped, small_got, small_sum, refs = refs[0], refs[1], refs[2], refs[3:]
    text_out, layout_out, grad_out, layout_grad_out, *refs = refs
    in_sem, cot_sem, hop_send, hop_recv, sib_send, sib_recv, send, recv, credit, out_sem, *refs = refs
    small_send, small_recv, page_send, page_recv, page_out_sem = refs
    section, d, t = lax.axis_index("section"), lax.axis_index("dp"), lax.axis_index("tensor")
    core, chip = t % 2, t // 2
    sibling = {"tensor": t + 1 - 2 * core}
    partner = {"tensor": (t + tensors // 2) % tensors}
    near, cross = {"dp": d + 1 - 2 * (d % 2)}, {"dp": 3 - d}
    outer = (d == 0) | (d == 3)
    other = {"section": 1 - section}
    hbm, probs_hbm, roots_hbm = jax.tree.unflatten(in_tree, hbm_in)
    starts = [matrix_starts(own) for own in hbm]

    plain = list(plain)
    views = []
    for b in range(2):
        fields = {}
        for name, value in hbm[b]._asdict().items():
            if name in Weights._fields:
                i = Weights._fields.index(name)
                fields[name] = work[b].raw.at[:, :, pl.ds(starts[b][i], starts[b][i + 1] - starts[b][i])]
            else:
                fields[name] = plain.pop(0)
        views.append(Needed(**fields))
    probs_in, roots = plain
    flat_views = jax.tree.leaves((tuple(views), probs_in, roots))
    flat_copies = [pltpu.make_async_copy(a, v, in_sem.at[i]) for i, (a, v) in enumerate(zip(hbm_in, flat_views))]
    loads, probs_copy, roots_copy = jax.tree.unflatten(in_tree, flat_copies)
    length = work[0].gf.shape[0]
    local_heads = probs_in.shape[1]
    blocks = hop_blocks(length)
    cot_copies = (
        pltpu.make_async_copy(cots[0], work[0].g, cot_sem.at[0]),
        pltpu.make_async_copy(cots[1], flipped, cot_sem.at[1]),
    )

    @pl.when(section == 1)
    def _():
        start(*cot_copies)

    roots_copy.start()
    for field in zip(loads[1], loads[0]):
        start(*field)
    probs_copy.start()
    greet(section, t, sections, tensors, (near, cross) if chain else ())

    part_length = text_out.shape[1]
    micro, page = core, chip
    kinds = ((grad_out, layout_grad_out), (text_out, layout_out))
    pages = ((work[0].g, flipped), ys)

    def page_part(g, q, a):
        span = pl.ds(q * part_length, part_length)
        return pages[g][a].at[span] if a == 0 else pages[g][a].at[:, span]

    def each_page(g, act):
        for q in range(tensors):
            for a in range(2):
                here = (micro == g) & (t == q)

                @pl.when((section == g) & here)
                def _():
                    act(g, q, a, True)

                @pl.when((section == g) & jnp.logical_not(here))
                def _():
                    act(g, q, a, False)

    def page_copy(g, q, a):
        return remote(
            page_part(g, q, a), kinds[g][a].at[page], page_send.at[q, a], page_recv.at[g, a, page],
            {"section": micro, "tensor": q},
        )

    def page_start(g, q, a, here):
        if here:
            pltpu.make_async_copy(page_part(g, q, a), kinds[g][a].at[page], page_recv.at[g, a, page]).start()
        else:
            page_copy(g, q, a).start()

    def page_sent(g, q, a, here):
        if not here:
            page_copy(g, q, a).wait_send()

    each_page(1, page_start)

    def blocks_of(b):
        return blocks if b == 0 else [slice(0, length)]

    def hop(b, n):
        part = work[b].g.at[blocks_of(b)[n]]
        return remote(part, part, hop_send.at[b, n], hop_recv.at[b, n], other)

    ahead = 2
    step = 2 * ROWS
    up_first, down_first = starts[0][2], starts[0][3]
    up_count, down_count = (starts[0][3] - up_first) // step, (starts[0][4] - down_first) // step
    n_feed = up_count + down_count
    chunks = [Chunk(0, k, up_first + k * step, step) for k in range(n_feed)]
    later = [(1, 0, starts[1][MATRICES])]
    later += [(0, f, n) for f, n in pieces_of(starts[0][1], starts[0][1] // 2)]
    later += [(0, starts[0][1] + f, n) for f, n in pieces_of(starts[0][2] - starts[0][1], starts[0][2] - starts[0][1])]
    chunks += [Chunk(b, n_feed + i, f, n) for i, (b, f, n) in enumerate(later)]

    def feed_chunk(k):
        return Chunk(0, k, pl.multiple_of(up_first + k * step, 16), step)

    def span(ref, c):
        return ref.at[pl.ds(c.first, c.rows)]

    def to_sibling(c):
        w, rows = work[c.b], pl.ds(c.first, c.rows)
        return remote(
            w.raw.at[:, 1 - core, rows], w.from_sibling.at[:, rows], sib_send.at[c.index], sib_recv.at[c.index], sibling
        )

    def mine(c):
        return span(work[c.b].raw.at[chip, core], c)

    def theirs(c):
        return span(work[c.b].raw.at[1 - chip, core], c)

    def to_partner(c):
        return remote(
            theirs(c), span(work[c.b].from_partner, c), send.at[0, c.index], recv.at[0, c.index], partner
        )

    def from_near(c):
        return span(work[c.b].from_sibling.at[0], c)

    def from_cross(c):
        return span(work[c.b].from_sibling.at[1], c)

    def to_near(c):
        return remote(mine(c), from_near(c), send.at[1, c.index], recv.at[1, c.index], near)

    def to_cross(c):
        return remote(mine(c), from_cross(c), send.at[2, c.index], recv.at[2, c.index], cross)

    def total_to_near(c):
        return remote(
            span(work[c.b].from_partner, c), from_near(c), send.at[3, c.index], recv.at[3, c.index], near
        )

    def out_copy(c, source):
        return pltpu.make_async_copy(span(source, c), span(results[c.b], c), out_sem.at[c.index])

    def added(target, *sources):
        target[...] = sum(s[...].astype(F32) for s in sources).astype(BF)

    def send_to_sibling(c):
        to_sibling(c).start()

    def stage_sibling(c):
        w = work[c.b]
        to_sibling(c).wait_recv()
        added(theirs(c), theirs(c), span(w.from_sibling.at[1 - chip], c))
        added(mine(c), mine(c), span(w.from_sibling.at[chip], c))
        if chain:
            @pl.when(jnp.logical_not(outer))
            def _():
                for device in (near, cross):
                    pl.semaphore_signal(credit, inc=1, device_id=device, device_id_type=MESH)

    def stage_partner(c):
        to_partner(c).wait_recv()
        added(mine(c), mine(c), span(work[c.b].from_partner, c))
        if not chain:
            out_copy(c, work[c.b].raw.at[chip, core]).start()
            return

        @pl.when(outer)
        def _():
            pl.semaphore_wait(credit, 1)
            to_near(c).start()

    def stage_near(c):
        @pl.when(jnp.logical_not(outer))
        def _():
            to_near(c).wait_recv()
            added(mine(c), mine(c), from_near(c))
            pl.semaphore_wait(credit, 1)
            to_cross(c).start()

    def stage_cross(c):
        @pl.when(jnp.logical_not(outer))
        def _():
            to_cross(c).wait_recv()
            total = work[c.b].from_partner
            added(span(total, c), mine(c), from_cross(c))
            total_to_near(c).start()
            out_copy(c, total).start()

    def stage_total(c):
        @pl.when(outer)
        def _():
            total_to_near(c).wait_recv()
            out_copy(c, work[c.b].from_sibling.at[0]).start()

    def turn_operands():
        wait(loads[0].low, loads[0].act)
        work[0].lowT[...] = views[0].low[...].T

    def feed_products():
        own, w = views[0], work[0]

        @pl.loop(0, up_count)
        def _(k):
            rows = pl.ds(pl.multiple_of(k * step, step), step)
            for q in range(tensors):
                w.raw[q // 2, q % 2, pl.ds(pl.multiple_of(up_first + k * step, 16), step), :] = dot(
                    w.lowT[rows, :], own.slope[q]
                ).astype(BF)
            send_to_sibling(feed_chunk(k))

            @pl.when((k >= 1) & (k <= ahead))
            def _():
                stage_sibling(feed_chunk(k - 1))
                to_partner(feed_chunk(k - 1)).start()

        @pl.loop(0, down_count)
        def _(k):
            lanes = pl.ds(pl.multiple_of(k * step, step), step)
            for q in range(tensors):
                w.raw[q // 2, q % 2, pl.ds(pl.multiple_of(down_first + k * step, 16), step), :] = dot(
                    own.act[q, :, lanes].T, w.gf[...]
                ).astype(BF)
            send_to_sibling(feed_chunk(up_count + k))

    def later_product(c):
        own, w = views[c.b], work[c.b]
        for q in range(tensors):
            for i in range(MATRICES):
                first = max(c.first, starts[c.b][i])
                last = min(c.first + c.rows, starts[c.b][i + 1])
                if first >= last:
                    continue
                rows = slice(first - starts[c.b][i], last - starts[c.b][i])
                if i == 0:
                    value = dot(own.qkv[q, rows, :], own.x[...])
                elif i == 1:
                    value = dot(own.ctx[q, rows, :], w.ga[...])
                elif i == 2:
                    value = dot(w.lowT[rows, :], own.slope[q])
                else:
                    value = dot(own.act[q, :, rows].T, w.gf[...])
                w.raw[q // 2, q % 2, first:last, :] = value.astype(BF)
        send_to_sibling(c)

    @pl.when(section == 1)
    def _():
        wait(*cot_copies)
        work[1].g[...] = flipped[...].T

    for b in range(2):
        work[b].sums[...] = jnp.zeros(work[b].sums.shape, F32)
    roots_copy.wait()

    def feed_back(b, n, block, hopped):
        own, own_in, w, gain = views[b], loads[b], work[b], gains[b]
        if n == 0:
            wait(own_in.n2)

        if hopped:
            hop(b, n).wait_recv()

        for rows in small_blocks(block):
            g, normed = w.g[rows].astype(F32), own.n2[rows].astype(F32)
            low = norm_rows_back(g, normed, roots[rows, 2 * b + 1 : 2 * b + 2], gain[1:2])
            w.dz[rows] = low
            w.gf[rows] = low.astype(BF)
            w.sums[1:2] += jnp.sum(g * normed, axis=0, keepdims=True)
            w.sums[3:4] += jnp.sum(g, axis=0, keepdims=True)

        if n == 0:
            wait(own_in.downward, own_in.slope, own_in.upward)

        @pl.loop(0, tensors)
        def _(q):
            d_act = dot(w.gf[block], own.downward[q // 2, q % 2])
            d_pre = (d_act * own.slope[q, block].astype(F32)).astype(BF)
            own.slope[q, block] = d_pre
            w.dz[block] += dot(d_pre, own.upward[q // 2, q % 2])

        if n == 0:
            wait(own_in.n1, own_in.outward)
        for rows in small_blocks(block):
            g, normed = w.dz[rows], own.n1[rows].astype(F32)
            low = norm_rows_back(g, normed, roots[rows, 2 * b : 2 * b + 1], gain[0:1])
            w.dz[rows] = low
            w.ga[rows] = low.astype(BF)
            w.sums[0:1] += jnp.sum(g * normed, axis=0, keepdims=True)
            w.sums[2:3] += jnp.sum(g, axis=0, keepdims=True)
        gaT = w.ga[block].T
        for q in range(tensors):
            w.dctx[q, :, block] = dot(own.outward[q // 2, q % 2], gaT).astype(BF)

    @pl.when(section == 0)
    def _():
        turn_operands()
        for s in (1, 0):
            for n, block in enumerate(blocks_of(s)):
                feed_back(s, n, block, True)

    @pl.when(section == 1)
    def _():
        for s in (1, 0):
            feed_back(s, 0, slice(0, length), False)

    @pl.when(section == 0)
    def _():
        feed_products()

    for own_in in loads:
        wait(own_in.qkv, own_in.ctx, own_in.inv)
    wait(probs_copy)
    qkv = (views[0].qkv, views[1].qkv)
    text_rows, layout_rows = slice(0, HEAD_TEXT), slice(HEAD_TEXT, HEAD_TEXT + HEAD_LAYOUT)

    def turn(k, n_known):
        fixed = isinstance(k, int)

        def at(i, stage):
            if not fixed:
                pl.when((i >= 0) & (i < n_feed))(lambda: stage(feed_chunk(i)))
            elif 0 <= i < n_known:
                stage(chunks[i])

        def sibling_and_send(c):
            stage_sibling(c)
            to_partner(c).start()

        at(k + ahead, sibling_and_send)
        at(k, stage_partner)
        if chain:
            at(k - 1, stage_near)
            at(k - 2, stage_cross)
            at(k - 3, stage_total)

    early_turns = 4

    @pl.loop(0, tensors)
    def _(q):
        for local in range(local_heads):
            head = q * local_heads + local

            @pl.when((section == 0) & (head % 4 == 0) & (head < 4 * (early_turns - 1)))
            def _():
                turn(head // 4, n_feed)

            inv = views[0].inv[q, local : local + 1, :]
            scaled = [
                (work[s].dctx[q, local * SIZES[s] : (local + 1) * SIZES[s], :].astype(F32) * inv).astype(BF)
                for s in range(2)
            ]
            inner = [
                jnp.sum(
                    scaled[s].astype(F32)
                    * views[s].ctx[q, local * SIZES[s] : (local + 1) * SIZES[s], :].astype(F32),
                    axis=0, keepdims=True,
                )
                for s in range(2)
            ]
            rows16 = lax.broadcasted_iota(jnp.int32, (16, length), 0)
            extra = jnp.zeros((16, length), F32)
            for i, value in enumerate((inner[0] + inner[1], inner[1])):
                high = value.astype(BF).astype(F32)
                extra = jnp.where(rows16 == 2 * i, -high, extra)
                extra = jnp.where(rows16 == 2 * i + 1, high - value, extra)
            pad = jnp.zeros((128 - sum(SIZES) - 16, length), BF)
            dcT = jnp.concatenate([*scaled, extra.astype(BF), pad], axis=0)
            dc = dcT.T
            qT, kT = (head_rows(qkv, q, kind, local, SCALES if kind == 0 else None) for kind in range(2))
            v_text, v_layout = (head_part(qkv, q, 2, local, s) for s in range(2))
            one, other_one = (((rows16 // 2) == i).astype(F32).astype(BF) for i in range(2))
            low = probs_in[q, local]
            probs = low.astype(F32)
            both = dot(dc, jnp.concatenate([v_text, v_layout, one, pad], axis=0))
            ds_both = (probs * both).astype(BF)
            single = dot(dc, jnp.concatenate([jnp.zeros_like(v_text), v_layout, other_one, pad], axis=0))
            ds_layout = (probs * single).astype(BF)
            dvT = dot(dcT, low)
            put_head(qkv, q, 2, local, 0, dvT[text_rows])
            put_head(qkv, q, 2, local, 1, dvT[layout_rows])
            k = kT.T
            lane = lax.broadcasted_iota(jnp.int32, (length, 128), 1)
            dq = jnp.where(lane < HEAD_TEXT, dot(ds_both, k) * SCALES[0], dot(ds_layout, k) * SCALES[1])
            dqT = dq.astype(BF).T
            put_head(qkv, q, 0, local, 0, dqT[text_rows])
            put_head(qkv, q, 0, local, 1, dqT[layout_rows])
            put_head(qkv, q, 1, local, 0, dot(qT[text_rows], ds_both))
            put_head(qkv, q, 1, local, 1, dot(qT[layout_rows], ds_layout))

    @pl.when(section == 0)
    def _():
        turn(early_turns - 1, n_feed)

    wait(loads[0].project, loads[1].project)
    page_sum = jnp.zeros((1, work[0].dz.shape[1]), F32)
    for b in (1, 0):
        for n, block in enumerate(blocks_of(b)):
            down = work[b].dz[block]
            for q in range(tensors):
                down += dot(qkv[b][q, :, block].T, views[b].project[q // 2, q % 2])
            down = down.astype(BF)
            work[b].g[block] = down
            if b == 0:
                page_sum += jnp.sum(down.astype(F32), axis=0, keepdims=True)

            @pl.when(section == 1)
            def _():
                hop(b, n).start()

    wait(loads[1].low, loads[1].act)
    work[1].lowT[...] = views[1].low[...].T
    for own_in in loads:
        wait(own_in.x)
    @pl.when(section == 1)
    def _():
        turn_operands()
        feed_products()

    for c in chunks[n_feed:]:
        later_product(c)

    @pl.when(section == 0)
    def _():
        flipped[...] = work[1].g[...].T

    at_page = (lax.broadcasted_iota(jnp.int32, lang_ids.shape, 0) == t % 2) & (
        lax.broadcasted_iota(jnp.int32, lang_ids.shape, 1) == t // 2
    )
    group = jnp.sum(jnp.where(at_page, lang_ids[...], 0), axis=(0, 1), keepdims=True)
    n_lang = small_out.shape[1] - 8
    chosen = (lax.broadcasted_iota(jnp.int32, (n_lang, 1), 0) == group) & (section == 0)
    small_sum[0, 0:n_lang] = jnp.where(chosen, page_sum, 0.0)
    small_sum[0, n_lang : n_lang + 4] = work[0].sums[...]
    small_sum[0, n_lang + 4 : n_lang + 8] = jnp.zeros((4, small_out.shape[2]), F32)
    small_sum[0, n_lang + 4 : n_lang + 8, : work[1].sums.shape[1]] = work[1].sums[...]

    def small_copy(i, device):
        return remote(small_sum.at[i], small_got.at[i], small_send.at[i], small_recv.at[i], device)

    if chain:
        small_copy(0, sibling).start()
    @pl.when(section == 1)
    def _():
        @pl.loop(0, early_turns)
        def _(k):
            turn(k, n_feed)

    for k in range(early_turns, len(chunks) + (3 if chain else 0)):
        turn(k, len(chunks))
        if k == len(chunks) - 1:
            each_page(0, page_start)
        if not chain:
            continue
        if k == early_turns:
            small_copy(0, sibling).wait_recv()
            small_sum[1] = small_sum[0] + small_got[0]
            small_copy(1, partner).start()
        if k == early_turns + 1:
            small_copy(1, partner).wait_recv()
            small_sum[2] = small_sum[1] + small_got[1]
            small_copy(2, near).start()
        if k == early_turns + 2:
            small_copy(2, near).wait_recv()
            small_sum[3] = small_sum[2] + small_got[2]

            @pl.when(jnp.logical_not(outer))
            def _():
                small_copy(3, cross).start()

        if k == early_turns + 3:
            @pl.when(jnp.logical_not(outer))
            def _():
                small_copy(3, cross).wait_recv()
                small_sum[4] = small_sum[3] + small_got[3]
                small_copy(4, near).start()

        if k == early_turns + 4:
            @pl.when(outer)
            def _():
                small_copy(4, near).wait_recv()
                small_sum[4] = small_got[4]

            small_sum[5] = small_sum[4]
            small_copy(5, other).start()

    if chain:
        for i, device in enumerate((sibling, partner, near)):
            small_copy(i, device).wait_send()

        @pl.when(jnp.logical_not(outer))
        def _():
            small_copy(3, cross).wait_send()
            small_copy(4, near).wait_send()

        small_copy(5, other).wait()
        small_out[0] = small_sum[5]
        small_out[1] = small_got[5]
    else:
        small_out[0] = small_sum[0]
        small_out[1] = small_sum[0]

    @pl.when(section == 1)
    def _():
        for b in range(2):
            for n in range(len(blocks_of(b))):
                hop(b, n).wait_send()

    for c in chunks:
        to_sibling(c).wait_send()
        to_partner(c).wait_send()
        if not chain:
            out_copy(c, work[c.b].from_partner).wait()
            continue

        @pl.when(outer)
        def _():
            to_near(c).wait_send()

        @pl.when(jnp.logical_not(outer))
        def _():
            to_cross(c).wait_send()
            total_to_near(c).wait_send()

        out_copy(c, work[c.b].from_partner).wait()

    for g in range(sections):
        each_page(g, page_sent)
        for a in range(2):
            for j in range(2):
                dst = kinds[g][a].at[j]
                remote(dst, dst, page_send.at[0, a], page_recv.at[g, a, j], partner).wait_recv()
    landed = (text_out, layout_out, grad_out, layout_grad_out)
    copies = [pltpu.make_async_copy(v, h, page_out_sem.at[i]) for i, (v, h) in enumerate(zip(landed, page_outs))]
    start(*copies)
    wait(*copies)


def layer_backward(mesh, x, y, probs, roots, kept, weights, cots, norms, lang_ids, n_lang):
    sections, dp, tensors = mesh.shape["section"], mesh.shape["dp"], mesh.shape["tensor"]
    chain = dp == 4
    weights = tuple(Weights(*(m.reshape((tensors // 2, 2) + m.shape[1:]) for m in w)) for w in weights)
    needed = tuple(
        Needed(
            n2=k.n2, downward=w.downward, slope=k.slope, upward=w.upward, n1=k.n1,
            outward=w.outward, low=k.low, act=k.act, qkv=k.qkv, ctx=k.ctx, inv=k.inv, project=w.project, x=rows,
        )
        for k, w, rows in zip(kept, weights, x)
    )
    flat_in, in_tree = jax.tree.flatten((needed, probs, roots))
    plain = [v for own in needed for name, v in own._asdict().items() if name not in Weights._fields] + [probs, roots]
    stacks = [(matrix_starts(own)[MATRICES], rows.shape[1]) for own, rows in zip(needed, x)]
    length = x[0].shape[0]
    work = []
    for own, rows, (count, width) in zip(needed, x, stacks):
        work += Work(
            g=shape(rows.shape), gf=shape(rows.shape), ga=shape(rows.shape), dz=shape(rows.shape, F32),
            dctx=shape(own.ctx.shape), sums=shape((4, width), F32), lowT=shape((width, length)),
            raw=shape((tensors // 2, 2, count, width)), from_sibling=shape((tensors // 2, count, width)),
            from_partner=shape((count, width)),
        )
    small = shape((2, n_lang + 8, x[0].shape[1]), F32)
    text_page = shape((2, length // tensors, x[0].shape[1]))
    layout_page = shape((2, x[1].shape[1], length // tensors))
    summed = [shape(s) for s in stacks]
    own = needed[0]
    n_chunks = (own.upward.shape[-2] + own.downward.shape[-2]) // (2 * ROWS) + 4
    n_blocks = len(hop_blocks(length))
    dma = pltpu.SemaphoreType.DMA
    results = pl.pallas_call(
        functools.partial(backward_kernel, sections, tensors, chain, in_tree),
        out_shape=summed + [small, text_page, layout_page, text_page, layout_page],
        in_specs=[ANY] * (len(flat_in) + 4) + [VMEM] * 3,
        out_specs=[ANY] * 2 + [VMEM] + [ANY] * 4,
        scratch_shapes=vmem_like(work) + vmem_like(plain)
        + [pltpu.VMEM(cots[1].shape, BF)] + [pltpu.VMEM((6,) + small.shape[1:], F32)] * 2
        + vmem_like([text_page, layout_page] * 2)
        + [dma((len(flat_in),)), dma((2,)), dma((2, n_blocks)), dma((2, n_blocks))]
        + [dma((n_chunks,))] * 2 + [dma((4, n_chunks))] * 2
        + [pltpu.SemaphoreType.REGULAR, dma((n_chunks,))]
        + [dma((6,))] * 2 + [dma((tensors, 2)), dma((sections, 2, 2)), dma((4,))],
        compiler_params=pltpu.CompilerParams(
            collective_id=1, has_side_effects=True, vmem_limit_bytes=64 << 20
        ),
        name="layer_backward",
    )(*flat_in, *cots, *y, lang_ids, norms[0][0], norms[1][0])
    totals, small, pages = results[:2], results[2], results[3:7]
    if not chain:
        totals = lax.psum(tuple(totals), "dp")
        both = lax.psum(small[0], ("dp", "tensor"))
        small = jnp.stack([both, lax.ppermute(both, "section", [(0, 1), (1, 0)])])
    return totals, small, pages


def widen_kernel(n_in, n_pages, *refs):
    n_out = 5 + n_pages + 2 * MATRICES
    hbm_in, hbm_out = refs[:n_in], refs[n_in : n_in + n_out]
    vmem_in, vmem_out = refs[n_in + n_out : 2 * n_in + n_out], refs[2 * n_in + n_out : -2]
    in_sem, out_sem = refs[-2:]
    loads = [pltpu.make_async_copy(h, v, in_sem.at[i]) for i, (h, v) in enumerate(zip(hbm_in, vmem_in))]
    sources = vmem_out[:5] + vmem_in[3:] + vmem_out[5:]
    stores = [pltpu.make_async_copy(v, h, out_sem.at[i]) for i, (v, h) in enumerate(zip(sources, hbm_out))]
    start(*loads)
    totals, small = vmem_in[0:2], vmem_in[2]
    for b in range(2):
        wait(loads[b])
        at = 0
        for i in range(b * MATRICES, (b + 1) * MATRICES):
            out = vmem_out[5 + i]
            for c in range(0, out.shape[0], 48):
                out[c : c + 48] = totals[b][at + c : at + c + 48].astype(F32)
            at += out.shape[0]
            stores[5 + n_pages + i].start()
    for i in range(n_pages):
        loads[3 + i].wait()
        stores[5 + i].start()
    loads[2].wait()
    n_lang = vmem_out[0].shape[0]
    vmem_out[0][...] = jnp.where(lax.axis_index("section") == 0, small[0, :n_lang], small[1, :n_lang])
    for i, out in enumerate(vmem_out[1:5]):
        first = n_lang + 2 * i
        out[...] = small[0, first : first + 2, : out.shape[1]]
    start(*stores[:5])
    wait(*stores)


def widen(totals, small, pages, shards, n_lang):
    widths = [total.shape[1] for total in totals]
    sums = [shape((n_lang, widths[0]), F32)] + [shape((2, w), F32) for w in widths for _ in range(2)]
    grads = [shape(m.shape, F32) for own in shards for m in own]
    inputs = (*totals, small, *pages)
    outs = sums + [shape(page.shape) for page in pages] + grads
    results = pl.pallas_call(
        functools.partial(widen_kernel, len(inputs), len(pages)), out_shape=outs,
        in_specs=[ANY] * len(inputs), out_specs=[ANY] * len(outs),
        scratch_shapes=vmem_like(inputs) + vmem_like(sums + grads)
        + [pltpu.SemaphoreType.DMA((len(inputs),)), pltpu.SemaphoreType.DMA((len(outs),))],
        compiler_params=pltpu.CompilerParams(vmem_limit_bytes=62 << 20), name="widen",
    )(*inputs)
    return results[0], results[1:5], results[5:9], results[9:13], results[13:17]


def per_device(
    mesh,
    text_input,
    layout_input,
    text_cotangent,
    layout_cotangent,
    page_counts,
    pad_mask,
    lang_ids,
    lang_table,
    text_project,
    text_outward,
    text_upward,
    text_downward,
    text_gains,
    text_biases,
    layout_project,
    layout_outward,
    layout_upward,
    layout_downward,
    layout_gains,
    layout_biases,
):
    def flat(project):
        return jnp.transpose(project[0], (1, 2, 0)).reshape(-1, project.shape[1])

    def flipped(block):
        return jnp.transpose(block[0], (0, 2, 1))

    shards = (
        Weights(flat(text_project), text_outward[0], text_upward[0], text_downward[0]),
        Weights(flat(layout_project), layout_outward[0], layout_upward[0], layout_downward[0]),
    )
    norms = ((text_gains[0], text_biases[0]), (layout_gains[0], layout_biases[0]))
    marks = (pad_mask, page_counts, lang_ids, lang_table)
    (x, y, probs, roots, kept, weights), cots = layer_forward(
        mesh, text_input[0], flipped(layout_input), text_cotangent[0], flipped(layout_cotangent), shards, norms, marks
    )
    n_lang = lang_table.shape[0]
    totals, small, pages = layer_backward(mesh, x, y, probs, roots, kept, weights, cots, norms, lang_ids, n_lang)
    lang_sum, norm_sums, pages, text_sums, layout_sums = widen(totals, small, pages, shards, n_lang)
    text_out, layout_out, text_grad, layout_grad = pages

    def unflat(grad, like):
        return jnp.transpose(grad.reshape(like.shape[2], like.shape[3], like.shape[1]), (2, 0, 1))[None]

    unflip = lambda block: jnp.transpose(block, (0, 2, 1))[None]
    return (
        text_out[None], unflip(layout_out), text_grad[None], unflip(layout_grad), lang_sum,
        unflat(text_sums[0], text_project), *(s[None] for s in text_sums[1:]), norm_sums[0][None], norm_sums[1][None],
        unflat(layout_sums[0], layout_project), *(s[None] for s in layout_sums[1:]),
        norm_sums[2][None], norm_sums[3][None],
    )


def solution(mesh):
    tokens = P("section", "dp", "tensor", None)
    weight_specs = (
        P("section", None, None, "tensor"), P("section", "tensor", None), P("section", None, "tensor"),
        P("section", "tensor", None), P("section", None, None), P("section", None, None),
    )
    in_specs = (tokens,) * 4 + (P(None, "dp"), P(None, "dp", None), P(None, "dp"), P()) + weight_specs * 2
    out_specs = (tokens,) * 4 + (P(),) + weight_specs * 2
    return jax.shard_map(
        functools.partial(per_device, mesh), mesh=mesh, in_specs=in_specs, out_specs=out_specs, check_vma=False
    )
```
